32 devices in a mesh: rows: 8 (over z, x), ch: 4 (over y, core).
Axes of the slice: x: 2, y: 2, z: 4, core: 2. Of those that a mesh axis runs over, the one named last changes fastest.
Arguments:
- inputs: float32 [8, 32, 64, 2048], P('ch', 'rows'), may hold values from -6 to 6
- heights: int32 [8], replicated, may hold values from 16 to 32, as said below
- displacements: int32 [18, 8, 32, 64], P(None, 'ch', 'rows'), may hold values from -5 to 5
- reduce_one: float32 [512, 2048], P('ch'), may hold values from -0.125 to 0.125
- reduce_gain_one: float32 [512], replicated, may hold values from 0.1 to 1.9
- reduce_bias_one: float32 [512], replicated, may hold values from -3 to 3
- offset_weight: float32 [18, 4608], replicated, may hold values from -0.25 to 0.25
- deform_weight: float32 [512, 4608], P('ch'), may hold values from -0.09375 to 0.09375
- deform_gain: float32 [512], replicated, may hold values from 0.1 to 1.9
- deform_bias: float32 [512], replicated, may hold values from -3 to 3
- expand_one: float32 [2048, 512], P('ch'), may hold values from -0.25 to 0.25
- expand_gain_one: float32 [2048], replicated, may hold values from 0.1 to 1.9
- expand_bias_one: float32 [2048], replicated, may hold values from -3 to 3
- reduce_two: float32 [512, 2048], P('ch'), may hold values from -0.125 to 0.125
- reduce_gain_two: float32 [512], replicated, may hold values from 0.1 to 1.9
- reduce_bias_two: float32 [512], replicated, may hold values from -3 to 3
- conv_weight: float32 [512, 4608], P('ch'), may hold values from -0.09375 to 0.09375
- conv_gain: float32 [512], replicated, may hold values from 0.1 to 1.9
- conv_bias: float32 [512], replicated, may hold values from -3 to 3
- expand_two: float32 [2048, 512], P('ch'), may hold values from -0.25 to 0.25
- expand_gain_two: float32 [2048], replicated, may hold values from 0.1 to 1.9
- expand_bias_two: float32 [2048], replicated, may hold values from -3 to 3
- cotangent: float32 [8, 32, 64, 2048], P('ch', 'rows'), may hold values from -6 to 6
Outputs:
- output: float32 [8, 32, 64, 2048], P('ch', 'rows')
- input_grad: float32 [8, 32, 64, 2048], P('ch', 'rows')
- reduce_one_grad: float32 [512, 2048], P('ch')
- reduce_gain_one_grad: float32 [512], P('ch')
- reduce_bias_one_grad: float32 [512], P('ch')
- offset_weight_grad: float32 [18, 4608], replicated
- deform_weight_grad: float32 [512, 4608], P('ch')
- deform_gain_grad: float32 [512], P('ch')
- deform_bias_grad: float32 [512], P('ch')
- expand_one_grad: float32 [2048, 512], P('ch')
- expand_gain_one_grad: float32 [2048], P('ch')
- expand_bias_one_grad: float32 [2048], P('ch')
- reduce_two_grad: float32 [512, 2048], P('ch')
- reduce_gain_two_grad: float32 [512], P('ch')
- reduce_bias_two_grad: float32 [512], P('ch')
- conv_weight_grad: float32 [512, 4608], P('ch')
- conv_gain_grad: float32 [512], P('ch')
- conv_bias_grad: float32 [512], P('ch')
- expand_two_grad: float32 [2048, 512], P('ch')
- expand_gain_two_grad: float32 [2048], P('ch')
- expand_bias_two_grad: float32 [2048], P('ch')
The draws below stay inside these ranges and needn't reach their ends.
Inputs may be any that keep to these rules, and one draw needn't show every extreme that they name: `heights`: at least one image is 32 rows tall; rows at or beyond an image's height are padding and are masked. `displacements`: entry 2k is a row displacement and entry 2k + 1 a column displacement of tap k.
All inputs are finite; a program needn't handle non-finite values.
Results may differ from the reference program's by a relative error of at most 0.025.
The reference program's roundings to bfloat16 on the way count: a program that leaves them out, or rounds other values in their place, can miss the bound.
Values may be sent and summed in bfloat16 or wider, within the bound.
No kernel may reach another device: no remote copies, remote signals or barrier semaphores. Data moves between devices by JAX's collectives and lax.ppermute only.
A program may use at most 256 MiB of HBM per device.

```python
import jax
import jax.numpy as jnp
from jax import lax

C_IN = 2048
C_MID = 512
OFFS = 18
W = 64
TILES = 2
H_DEV = 4
B = 8
H = 32


def draw_heights(key, part):
    key = jax.random.fold_in(key, 7)
    first_key, second_key = jax.random.split(key)
    drawn = jax.random.randint(first_key, (B,), H // 2, H + 1)
    chosen = jax.random.randint(second_key, (), 0, B)
    return jnp.where(jnp.arange(B) == chosen, H, drawn).astype(jnp.int32)


def with_ends(array, rng, low, largest):
    spot = [jax.random.randint(jax.random.fold_in(rng, axis), (), 0, length) for axis, length in enumerate(array.shape)]
    widest = array.shape.index(max(array.shape))
    neighbour = spot[:widest] + [(spot[widest] + 1) % array.shape[widest]] + spot[widest + 1:]
    return array.at[tuple(spot)].set(low).at[tuple(neighbour)].set(largest)


def steps_of(own_key, extent, shards, low, high):
    level = 1.0
    for axis_at, blocks in shards:
        steps = jax.random.uniform(jax.random.fold_in(jax.random.fold_in(own_key, 6), axis_at), (blocks,), jnp.float32, low / len(shards), high / len(shards))
        level = level * jnp.repeat(jnp.exp(steps), extent[axis_at] // blocks).reshape((-1,) + (1,) * (len(extent) - 1 - axis_at))
    return level


def scatter_about(rng, shape, scale, most, cuts=(), held_as=jnp.bfloat16):
    entries = jax.random.normal(rng, shape, jnp.float32) * scale
    if len(cuts) > 0:
        entries = steps_of(rng, shape, cuts, -0.22, 0.18) * entries
    return jnp.clip(entries, min=-most, max=most).astype(held_as)


def setup_inputs(seed: int = 0) -> dict:
    key_list = jax.random.split(jax.random.key(seed), 24)
    inputs = scatter_about(key_list[0], (B, H, W, C_IN), 1.0, 6.0, ((0, 4), (1, 8)), jnp.float32)
    heights = draw_heights(jax.random.fold_in(key_list[23], 71), 0)
    displacements = with_ends(jax.random.randint(key_list[2], (OFFS, B, H, W), 3 - TILES * H_DEV, TILES * H_DEV - 2), jax.random.fold_in(key_list[2], 1), 3 - TILES * H_DEV, (TILES * H_DEV - 2) - 1).astype(jnp.int32)
    reduce_one = scatter_about(key_list[3], (C_MID, C_IN), C_IN ** -0.5, 0.125, ((0, 4),), jnp.float32)
    reduce_gain_one = jnp.clip(1.0 + 0.18 * jax.random.normal(key_list[4], (C_MID,), jnp.float32), 0.1, 1.9)
    reduce_bias_one = scatter_about(key_list[5], (C_MID,), 0.5, 3.0, (), jnp.float32)
    offset_weight = scatter_about(key_list[6], (OFFS, 9 * C_MID), C_MID ** -0.5, 0.25, (), jnp.float32)
    deform_weight = scatter_about(key_list[7], (C_MID, 9 * C_MID), (9 * C_MID) ** -0.5, 0.09375, ((0, 4),), jnp.float32)
    deform_gain = jnp.clip(1.0 + 0.18 * jax.random.normal(key_list[8], (C_MID,), jnp.float32), 0.1, 1.9)
    deform_bias = scatter_about(key_list[9], (C_MID,), 0.5, 3.0, (), jnp.float32)
    expand_one = scatter_about(key_list[10], (C_IN, C_MID), C_MID ** -0.5, 0.25, ((0, 4),), jnp.float32)
    expand_gain_one = jnp.clip(1.0 + 0.18 * jax.random.normal(key_list[11], (C_IN,), jnp.float32), 0.1, 1.9)
    expand_bias_one = scatter_about(key_list[12], (C_IN,), 0.5, 3.0, (), jnp.float32)
    reduce_two = scatter_about(key_list[13], (C_MID, C_IN), C_IN ** -0.5, 0.125, ((0, 4),), jnp.float32)
    reduce_gain_two = jnp.clip(1.0 + 0.18 * jax.random.normal(key_list[14], (C_MID,), jnp.float32), 0.1, 1.9)
    reduce_bias_two = scatter_about(key_list[15], (C_MID,), 0.5, 3.0, (), jnp.float32)
    conv_weight = scatter_about(key_list[16], (C_MID, 9 * C_MID), (9 * C_MID) ** -0.5, 0.09375, ((0, 4),), jnp.float32)
    conv_gain = jnp.clip(1.0 + 0.18 * jax.random.normal(key_list[17], (C_MID,), jnp.float32), 0.1, 1.9)
    conv_bias = scatter_about(key_list[18], (C_MID,), 0.5, 3.0, (), jnp.float32)
    expand_two = scatter_about(key_list[19], (C_IN, C_MID), C_MID ** -0.5, 0.25, ((0, 4),), jnp.float32)
    expand_gain_two = jnp.clip(1.0 + 0.18 * jax.random.normal(key_list[20], (C_IN,), jnp.float32), 0.1, 1.9)
    expand_bias_two = scatter_about(key_list[21], (C_IN,), 0.5, 3.0, (), jnp.float32)
    cotangent = scatter_about(key_list[22], (B, H, W, C_IN), 1.0, 6.0, ((0, 4), (1, 8)), jnp.float32)
    return {"inputs": inputs, "heights": heights, "displacements": displacements, "reduce_one": reduce_one, "reduce_gain_one": reduce_gain_one, "reduce_bias_one": reduce_bias_one, "offset_weight": offset_weight, "deform_weight": deform_weight, "deform_gain": deform_gain, "deform_bias": deform_bias, "expand_one": expand_one, "expand_gain_one": expand_gain_one, "expand_bias_one": expand_bias_one, "reduce_two": reduce_two, "reduce_gain_two": reduce_gain_two, "reduce_bias_two": reduce_bias_two, "conv_weight": conv_weight, "conv_gain": conv_gain, "conv_bias": conv_bias, "expand_two": expand_two, "expand_gain_two": expand_gain_two, "expand_bias_two": expand_bias_two, "cotangent": cotangent}


@jax.custom_vjp
def low(v):
    return lax.optimization_barrier(v.astype(jnp.bfloat16)).astype(jnp.float32)

@jax.custom_vjp
def low_back(v):
    return v

def low_keep(v):
    return (low(v), None)

def low_pass(kept, grad):
    return (grad,)

def back_keep(v):
    return (v, None)

def back_low(kept, grad):
    return (low(grad),)
low.defvjp(low_keep, low_pass)
low_back.defvjp(back_keep, back_low)
EPSILON = 1e-05
HIGHEST = lax.Precision.HIGHEST

def gelu_tanh(v):
    return jax.nn.gelu(v, approximate=True)

def project(acts, weight):
    return jnp.einsum('bhwc,oc->bhwo', acts, weight, precision=HIGHEST)

def batch_norm(values, gain, shift, mask_full, count):
    masked = values * mask_full
    mean_val = lax.optimization_barrier(jnp.sum(masked, axis=(0, 1, 2))) / count
    square = lax.optimization_barrier(jnp.sum(masked * values, axis=(0, 1, 2))) / count
    scale = lax.rsqrt(square - mean_val * mean_val + EPSILON)
    return (values - mean_val) * scale * gain + shift

def patches_of(acts):
    rows_all, width = (acts.shape[1], acts.shape[2])
    padded = jnp.pad(acts, ((0, 0), (2, 2), (2, 2), (0, 0)))
    return jnp.concatenate([padded[:, 2 * i:2 * i + rows_all, 2 * j:2 * j + width, :] for i in range(3) for j in range(3)], axis=3)

def sample(acts, fraction, displacements):
    batch, rows_all, width, channels = acts.shape
    flat = acts.reshape(batch * rows_all * width, channels)
    image = jnp.arange(batch, dtype=jnp.int32)[:, None, None]
    row = jnp.arange(rows_all, dtype=jnp.int32)[None, :, None]
    column = jnp.arange(width, dtype=jnp.int32)[None, None, :]
    pieces = []
    for k in range(9):
        i, j = (k // 3 - 1, k % 3 - 1)
        top = row + 2 * i + displacements[2 * k]
        left = column + 2 * j + displacements[2 * k + 1]
        frac_y = fraction[..., 2 * k][..., None]
        frac_x = fraction[..., 2 * k + 1][..., None]

        def corner(r, c):
            valid = ((r >= 0) & (r < rows_all) & (c >= 0) & (c < width)).astype(jnp.float32)
            index = (image * rows_all + jnp.clip(r, 0, rows_all - 1)) * width + jnp.clip(c, 0, width - 1)
            return jnp.take(flat, index.astype(jnp.int32), axis=0) * valid[..., None]
        upper = (1.0 - frac_x) * corner(top, left) + frac_x * corner(top, left + 1)
        lower = (1.0 - frac_x) * corner(top + 1, left) + frac_x * corner(top + 1, left + 1)
        pieces.append((1.0 - frac_y) * upper + frac_y * lower)
    return jnp.concatenate(pieces, axis=3)

def front(inputs, reduce_weight, gain, shift, mask_full, count):
    reduced = low_back(project(low(inputs), low(reduce_weight)))
    return low(gelu_tanh(batch_norm(reduced, gain, shift, mask_full, count)) * mask_full)

def finish(columns, mid_weight, mid_gain, mid_bias, expand_weight, expand_gain, expand_bias, residual, mask_full, count):
    mixed = low_back(project(columns, low(mid_weight)))
    middle = low(gelu_tanh(batch_norm(mixed, mid_gain, mid_bias, mask_full, count)) * mask_full)
    expanded = low_back(project(middle, low(expand_weight)))
    return gelu_tanh(batch_norm(expanded, expand_gain, expand_bias, mask_full, count) + residual) * mask_full

def reference(inputs, heights, displacements, reduce_one, reduce_gain_one, reduce_bias_one, offset_weight, deform_weight, deform_gain, deform_bias, expand_one, expand_gain_one, expand_bias_one, reduce_two, reduce_gain_two, reduce_bias_two, conv_weight, conv_gain, conv_bias, expand_two, expand_gain_two, expand_bias_two, cotangent):
    mask = (jnp.arange(H, dtype=jnp.int32)[None, :] < heights[:, None]).astype(jnp.float32)
    mask_full = mask[:, :, None, None]
    count = jnp.sum(heights).astype(jnp.float32) * W

    def sampled(acts, fraction):
        return sample(acts, fraction, displacements)

    def forward(inputs, reduce_one, reduce_gain_one, reduce_bias_one, offset_weight, deform_weight, deform_gain, deform_bias, expand_one, expand_gain_one, expand_bias_one, reduce_two, reduce_gain_two, reduce_bias_two, conv_weight, conv_gain, conv_bias, expand_two, expand_gain_two, expand_bias_two):
        hidden = front(inputs, reduce_one, reduce_gain_one, reduce_bias_one, mask_full, count)
        offsets = low_back(jnp.einsum('bhwk,ok->bhwo', patches_of(hidden), low(offset_weight), precision=HIGHEST))
        columns = low(jax.checkpoint(sampled)(hidden, jax.nn.sigmoid(offsets)))
        first = finish(columns, deform_weight, deform_gain, deform_bias, expand_one, expand_gain_one, expand_bias_one, inputs, mask_full, count)
        hidden_two = front(first, reduce_two, reduce_gain_two, reduce_bias_two, mask_full, count)
        return finish(patches_of(hidden_two), conv_weight, conv_gain, conv_bias, expand_two, expand_gain_two, expand_bias_two, first, mask_full, count)
    output, pullback = jax.vjp(forward, inputs, reduce_one, reduce_gain_one, reduce_bias_one, offset_weight, deform_weight, deform_gain, deform_bias, expand_one, expand_gain_one, expand_bias_one, reduce_two, reduce_gain_two, reduce_bias_two, conv_weight, conv_gain, conv_bias, expand_two, expand_gain_two, expand_bias_two)
    grads = pullback(cotangent)
    return (output, grads[0], grads[1], grads[2], grads[3], grads[4], grads[5], grads[6], grads[7], grads[8], grads[9], grads[10], grads[11], grads[12], grads[13], grads[14], grads[15], grads[16], grads[17], grads[18], grads[19])
```

```python
import jax
import jax.numpy as jnp
from jax import lax
from jax.sharding import PartitionSpec as P

TILES = 2


EPSILON = 1e-05
HIGHEST = lax.Precision.HIGHEST


def from_behind(block, axis, distance):
    devices = range(lax.axis_size(axis))
    route = [(i - distance, i) for i in devices if i - distance in devices]
    return lax.ppermute(block, axis, route)


def extended_2(block, sides, width):
    for axis, dim in sides:
        count = lax.axis_size(axis)
        forward = [(i, i + 1) for i in range(count - 1)]
        backward = [(target, source) for source, target in forward]
        low = lax.ppermute(
            lax.slice_in_dim(block, block.shape[dim] - width, None, axis=dim), axis, forward
        )
        high = lax.ppermute(lax.slice_in_dim(block, 0, width, axis=dim), axis, backward)
        block = jnp.concatenate([low, block, high], axis=dim)
    return block


def gelu_tanh(v):
    return jax.nn.gelu(v, approximate=True)


def gelu_back(pre, upstream):
    _, pullback = jax.vjp(gelu_tanh, pre)
    return pullback(upstream)[0]


def product(left, right):
    return lax.dot_general(
        left, right, (((left.ndim - 1,), (1,)), ((), ())), preferred_element_type=jnp.float32
    )


def product_back(upstream, right):
    return lax.dot_general(
        upstream,
        right,
        (((upstream.ndim - 1,), (0,)), ((), ())),
        preferred_element_type=jnp.float32,
    )


def flat_rows(values):
    return values.reshape(-1, values.shape[-1])


def outer_term(upstream, acts):
    return lax.dot_general(
        flat_rows(upstream),
        flat_rows(acts),
        (((0,), (0,)), ((), ())),
        preferred_element_type=jnp.float32,
    )


def rows_term(upstream_flat, acts_flat):
    return lax.dot_general(
        upstream_flat, acts_flat, (((0,), (0,)), ((), ())), preferred_element_type=jnp.float32
    )


def ladder_sum(values):
    for axis in ("ch", "rows"):
        count, step = lax.axis_size(axis), 1
        while step < count:
            values = values + lax.ppermute(values, axis, [(i, i ^ step) for i in range(count)])
            step *= 2
    return values


def own_slice(full):
    size = full.shape[0] // lax.axis_size("ch")
    return lax.dynamic_slice_in_dim(full, lax.axis_index("ch") * size, size)


def gather_block(reduce_weight, mid_weight, expand_weight):
    return (
        lax.all_gather(reduce_weight.astype(jnp.bfloat16), "ch", axis=0, tiled=True),
        lax.all_gather(mid_weight.astype(jnp.bfloat16), "ch", axis=0, tiled=True),
        lax.all_gather(expand_weight.astype(jnp.bfloat16), "ch", axis=0, tiled=True),
    )


def to_everyone(values, axes, groups, size):
    spread = jnp.broadcast_to(values[None], (size,) + values.shape)
    return lax.all_to_all(spread, axes, 0, 0, axis_index_groups=groups, tiled=True)


def totals_of(first, second):
    rows, ch = lax.axis_size("rows"), lax.axis_size("ch")
    channels = first.shape[0]
    if channels < 2048:
        block = jnp.concatenate([first, second]).reshape(-1, 128)
        block = jnp.sum(to_everyone(block, ("rows", "ch"), None, rows * ch), axis=0)
        return block.reshape(2, channels)
    core = lax.axis_index("ch") % 2
    swap = [(i, i ^ 1) for i in range(ch)]
    own = jnp.where(core == 0, first, second).reshape(-1, 128)
    other = jnp.where(core == 0, second, first).reshape(-1, 128)
    half = own + lax.ppermute(other, "ch", swap)
    groups = [[i * 2 + k for i in range(rows * ch // 2)] for k in range(2)]
    half = jnp.sum(to_everyone(half, ("rows", "ch"), groups, rows * ch // 2), axis=0)
    other = lax.ppermute(half, "ch", swap)
    return (
        jnp.where(core == 0, half, other).reshape(channels),
        jnp.where(core == 0, other, half).reshape(channels),
    )


def norm_forward(values, gain, shift, mask_full, count):
    masked = values * mask_full
    totals = totals_of(jnp.sum(masked, axis=(0, 1, 2)), jnp.sum(masked * values, axis=(0, 1, 2)))
    mean_val = totals[0] / count
    scale = lax.rsqrt(totals[1] / count - mean_val * mean_val + EPSILON)
    normal = (values - mean_val) * scale
    return (normal * gain + shift, (normal, scale))


def norm_backward(upstream, kept, gain, mask_full, count):
    normal, scale = kept
    totals = totals_of(jnp.sum(upstream, axis=(0, 1, 2)), jnp.sum(upstream * normal, axis=(0, 1, 2)))
    shift_sum, gain_sum = totals
    values_grad = scale * (
        upstream * gain - mask_full * (gain * shift_sum + normal * (gain * gain_sum)) / count
    )
    return (values_grad, own_slice(gain_sum), own_slice(shift_sum))


def deep_rows(tile):

    def neighbour(by):
        return from_behind(tile, "rows", by)

    above = [neighbour(k) for k in range(TILES, 0, -1)]
    below = [neighbour(-k) for k in range(1, TILES + 1)]
    return jnp.concatenate(above + [tile] + below, axis=1)


def deep_return(extended_grad, rows_dev):

    def send_back(piece, by):
        return from_behind(piece.astype(jnp.bfloat16), "rows", by).astype(piece.dtype)

    own = extended_grad[:, TILES * rows_dev : (TILES + 1) * rows_dev]
    for k in range(1, TILES + 1):
        own = own + send_back(
            extended_grad[:, (TILES - k) * rows_dev : (TILES - k + 1) * rows_dev], -k
        )
        own = own + send_back(
            extended_grad[:, (TILES + k) * rows_dev : (TILES + k + 1) * rows_dev], k
        )
    return own


def near_return(extended_grad, rows_dev):

    def send_rim(piece, by):
        return from_behind(piece.astype(jnp.bfloat16), "rows", by).astype(piece.dtype)

    own = extended_grad[:, 2 : rows_dev + 2]
    own = own.at[:, rows_dev - 2 :].add(send_rim(extended_grad[:, :2], -1))
    own = own.at[:, :2].add(send_rim(extended_grad[:, rows_dev + 2 :], 1))
    return own


def patches_from(extended, base, rows_dev):
    width = extended.shape[2]
    padded = jnp.pad(extended, ((0, 0), (0, 0), (2, 2), (0, 0)))
    return jnp.concatenate(
        [
            padded[:, base + 2 * i : base + 2 * i + rows_dev, 2 * j : 2 * j + width, :]
            for i in range(3)
            for j in range(3)
        ],
        axis=3,
    )


def patches_back(patch_grad, ext_rows, base, mid_width):
    batch, rows_dev, width, _ = patch_grad.shape
    total = jnp.zeros((batch, ext_rows, width + 4, mid_width), jnp.float32)
    for i in range(3):
        for j in range(3):
            k = i * 3 + j
            total = total.at[
                :, base + 2 * i : base + 2 * i + rows_dev, 2 * j : 2 * j + width, :
            ].add(patch_grad[..., k * mid_width : (k + 1) * mid_width])
    return total[:, :, 2 : 2 + width, :]


def window_rows_of(rows_dev):
    return rows_dev + 2 * TILES * rows_dev - 5


def tap_targets(displacements, k, rows_dev, width):
    batch = displacements.shape[1]
    i, j = (k // 3 - 1, k % 3 - 1)
    first_row = 2 * i + 3
    row = jnp.arange(rows_dev, dtype=jnp.int32)[None, :, None]
    column = jnp.arange(width, dtype=jnp.int32)[None, None, :]
    top = TILES * rows_dev + row + 2 * i + displacements[2 * k] - first_row
    left = column + 2 * j + displacements[2 * k + 1]
    targets = []
    for down in (0, 1):
        for right in (0, 1):
            place = left + right
            valid = (place >= 0) & (place < width)
            targets.append(jnp.where(valid, (top + down) * width + place, -1))
    return (first_row, jnp.stack(targets, axis=1).reshape(batch, 4, rows_dev * width))


def sample_columns(extended, displacements, fraction):
    batch, ext_rows, width, mid_width = extended.shape
    rows_dev = fraction.shape[1]
    window_rows = window_rows_of(rows_dev)
    sources = jnp.arange(window_rows * width, dtype=jnp.int32)
    pieces = []
    corner_keep = []
    for k in range(9):
        first_row, targets = tap_targets(displacements, k, rows_dev, width)
        window = extended[:, first_row : first_row + window_rows].reshape(
            batch, window_rows * width, mid_width
        )
        onehot = (targets[..., None] == sources).astype(jnp.bfloat16)
        picked = lax.dot_general(
            onehot, window, (((3,), (1,)), ((0,), (0,))), preferred_element_type=jnp.float32
        )
        corner_keep.append(picked.astype(jnp.bfloat16))
        values = [picked[:, n].reshape(batch, rows_dev, width, mid_width) for n in range(4)]
        frac_y = fraction[..., 2 * k][..., None]
        frac_x = fraction[..., 2 * k + 1][..., None]
        upper = (1.0 - frac_x) * values[0] + frac_x * values[1]
        lower = (1.0 - frac_x) * values[2] + frac_x * values[3]
        pieces.append((1.0 - frac_y) * upper + frac_y * lower)
    return (jnp.concatenate(pieces, axis=3).astype(jnp.bfloat16), corner_keep)


def sample_back(corner_keep, displacements, fraction, column_grad, ext_rows):
    batch, rows_dev, width = (fraction.shape[0], fraction.shape[1], fraction.shape[2])
    mid_width = column_grad.shape[3] // 9
    window_rows = window_rows_of(rows_dev)
    sources = jnp.arange(window_rows * width, dtype=jnp.int32)
    total = jnp.zeros((batch, ext_rows, width, mid_width), jnp.float32)
    frac_grads = []
    for k in range(9):
        first_row, targets = tap_targets(displacements, k, rows_dev, width)
        picked = corner_keep[k].astype(jnp.float32)
        values = [picked[:, n].reshape(batch, rows_dev, width, mid_width) for n in range(4)]
        frac_y = fraction[..., 2 * k][..., None]
        frac_x = fraction[..., 2 * k + 1][..., None]
        tap_grad = column_grad[..., k * mid_width : (k + 1) * mid_width]
        frac_grads.append(
            jnp.sum(
                tap_grad
                * ((1.0 - frac_x) * (values[2] - values[0]) + frac_x * (values[3] - values[1])),
                axis=3,
            )
        )
        frac_grads.append(
            jnp.sum(
                tap_grad
                * ((1.0 - frac_y) * (values[1] - values[0]) + frac_y * (values[3] - values[2])),
                axis=3,
            )
        )
        shares = [
            (1.0 - frac_y) * (1.0 - frac_x),
            (1.0 - frac_y) * frac_x,
            frac_y * (1.0 - frac_x),
            frac_y * frac_x,
        ]
        spread = jnp.zeros((batch, rows_dev * width, window_rows * width), jnp.float32)
        for n in range(4):
            spread = spread + jnp.where(
                targets[:, n, :, None] == sources,
                shares[n].reshape(batch, rows_dev * width)[..., None],
                0.0,
            )
        returned = lax.dot_general(
            spread,
            tap_grad.reshape(batch, rows_dev * width, mid_width),
            (((1,), (1,)), ((0,), (0,))),
            precision=HIGHEST,
            preferred_element_type=jnp.float32,
        )
        total = total.at[:, first_row : first_row + window_rows].add(
            returned.reshape(batch, window_rows, width, mid_width)
        )
    return (total, jnp.stack(frac_grads, axis=3))


def block_grads(reduce_pair, mid_pair, expand_pair):

    def owned(pair):
        upstream_flat, acts_flat = (flat_rows(pair[0]), flat_rows(pair[1]))
        return lax.psum_scatter(
            rows_term(upstream_flat, acts_flat).astype(jnp.bfloat16),
            "ch",
            scatter_dimension=0,
            tiled=True,
        ).astype(jnp.float32)

    first_part, second_part, third_part = (owned(reduce_pair), owned(mid_pair), owned(expand_pair))
    return (
        lax.psum(first_part.astype(jnp.bfloat16), "rows").astype(jnp.float32),
        lax.psum(second_part.astype(jnp.bfloat16), "rows").astype(jnp.float32),
        lax.psum(third_part.astype(jnp.bfloat16), "rows").astype(jnp.float32),
    )


def end_forward(
    columns,
    mid_full,
    mid_gain,
    mid_bias,
    expand_full,
    expand_gain,
    expand_bias,
    residual,
    mask_full,
    count,
):
    mixed, mixed_keep = norm_forward(
        product(columns, mid_full), mid_gain, mid_bias, mask_full, count
    )
    middle = (gelu_tanh(mixed) * mask_full).astype(jnp.bfloat16)
    expanded, expanded_keep = norm_forward(
        product(middle, expand_full), expand_gain, expand_bias, mask_full, count
    )
    pre_out = expanded + residual
    return (gelu_tanh(pre_out) * mask_full, (mixed, mixed_keep, middle, expanded_keep, pre_out))


def end_backward(upstream, kept, mid_full, mid_gain, expand_full, expand_gain, mask_full, count):
    mixed, mixed_keep, middle, expanded_keep, pre_out = kept
    pre_grad = gelu_back(pre_out, upstream * mask_full)
    expanded_grad, expand_gain_grad, expand_bias_grad = norm_backward(
        pre_grad, expanded_keep, expand_gain, mask_full, count
    )
    expanded_low = expanded_grad.astype(jnp.bfloat16)
    middle_grad = product_back(expanded_low, expand_full)
    mixed_pre = gelu_back(mixed, middle_grad * mask_full)
    mixed_grad, mid_gain_grad, mid_bias_grad = norm_backward(
        mixed_pre, mixed_keep, mid_gain, mask_full, count
    )
    mixed_low = mixed_grad.astype(jnp.bfloat16)
    column_grad = product_back(mixed_low, mid_full)
    return (
        pre_grad,
        column_grad,
        (mixed_low, expanded_low, middle),
        (mid_gain_grad, mid_bias_grad, expand_gain_grad, expand_bias_grad),
    )


def front_backward(
    hidden_grad, reduced, reduced_keep, reduce_gain, reduce_full, pre_grad, mask_full, count
):
    reduced_pre = gelu_back(reduced, hidden_grad * mask_full)
    reduced_grad, gain_grad, bias_grad = norm_backward(
        reduced_pre, reduced_keep, reduce_gain, mask_full, count
    )
    reduced_low = reduced_grad.astype(jnp.bfloat16)
    input_grad = pre_grad + product_back(reduced_low, reduce_full)
    return (input_grad, reduced_low, gain_grad, bias_grad)


def per_device(
    inputs,
    heights,
    displacements,
    reduce_one,
    reduce_gain_one,
    reduce_bias_one,
    offset_weight,
    deform_weight,
    deform_gain,
    deform_bias,
    expand_one,
    expand_gain_one,
    expand_bias_one,
    reduce_two,
    reduce_gain_two,
    reduce_bias_two,
    conv_weight,
    conv_gain,
    conv_bias,
    expand_two,
    expand_gain_two,
    expand_bias_two,
    cotangent,
):
    batch, rows_dev, width, channels = inputs.shape
    mid_width = deform_weight.shape[1] // 9
    own_heights = lax.dynamic_slice_in_dim(heights, lax.axis_index("ch") * batch, batch)
    rows_here = lax.axis_index("rows") * rows_dev + jnp.arange(rows_dev, dtype=jnp.int32)
    mask_full = (rows_here[None, :] < own_heights[:, None]).astype(jnp.float32)[:, :, None, None]
    count = jnp.sum(heights).astype(jnp.float32) * width
    deep_base = TILES * rows_dev
    deep_height = (2 * TILES + 1) * rows_dev
    offset_low = offset_weight.astype(jnp.bfloat16)
    first_weights = gather_block(reduce_one, deform_weight, expand_one)
    second_weights = gather_block(reduce_two, conv_weight, expand_two)
    input_low = inputs.astype(jnp.bfloat16)
    reduced_one, reduced_keep_one = norm_forward(
        product(input_low, first_weights[0]), reduce_gain_one, reduce_bias_one, mask_full, count
    )
    hidden = (gelu_tanh(reduced_one) * mask_full).astype(jnp.bfloat16)
    extended = deep_rows(hidden)
    offset_patches = patches_from(extended, deep_base - 2, rows_dev)
    fraction = jax.nn.sigmoid(product(offset_patches, offset_low))
    columns, corner_keep = sample_columns(extended, displacements, fraction)
    first, first_kept = end_forward(
        columns,
        first_weights[1],
        deform_gain,
        deform_bias,
        first_weights[2],
        expand_gain_one,
        expand_bias_one,
        inputs,
        mask_full,
        count,
    )
    first_low = first.astype(jnp.bfloat16)
    reduced_two, reduced_keep_two = norm_forward(
        product(first_low, second_weights[0]), reduce_gain_two, reduce_bias_two, mask_full, count
    )
    hidden_two = (gelu_tanh(reduced_two) * mask_full).astype(jnp.bfloat16)
    rimmed = extended_2(hidden_two, (("rows", 1),), 2)
    conv_patches = patches_from(rimmed, 0, rows_dev)
    output, second_kept = end_forward(
        conv_patches,
        second_weights[1],
        conv_gain,
        conv_bias,
        second_weights[2],
        expand_gain_two,
        expand_bias_two,
        first,
        mask_full,
        count,
    )
    pre_grad, column_grad, pairs_two, gains_two = end_backward(
        cotangent,
        second_kept,
        second_weights[1],
        conv_gain,
        second_weights[2],
        expand_gain_two,
        mask_full,
        count,
    )
    hidden_two_grad = near_return(patches_back(column_grad, rows_dev + 4, 0, mid_width), rows_dev)
    first_grad, reduced_low_two, reduce_gain_two_grad, reduce_bias_two_grad = front_backward(
        hidden_two_grad,
        reduced_two,
        reduced_keep_two,
        reduce_gain_two,
        second_weights[0],
        pre_grad,
        mask_full,
        count,
    )
    reduce_two_grad, conv_weight_grad, expand_two_grad = block_grads(
        (reduced_low_two, first_low), (pairs_two[0], conv_patches), (pairs_two[1], pairs_two[2])
    )
    pre_grad_one, deform_column_grad, pairs_one, gains_one = end_backward(
        first_grad,
        first_kept,
        first_weights[1],
        deform_gain,
        first_weights[2],
        expand_gain_one,
        mask_full,
        count,
    )
    extended_grad, fraction_grad = sample_back(
        corner_keep, displacements, fraction, deform_column_grad, deep_height
    )
    offsets_low = (fraction_grad * fraction * (1.0 - fraction)).astype(jnp.bfloat16)
    offset_weight_grad = ladder_sum(outer_term(offsets_low, offset_patches))
    extended_grad = extended_grad + patches_back(
        product_back(offsets_low, offset_low), deep_height, deep_base - 2, mid_width
    )
    hidden_grad = deep_return(extended_grad, rows_dev)
    input_grad, reduced_low_one, reduce_gain_one_grad, reduce_bias_one_grad = front_backward(
        hidden_grad,
        reduced_one,
        reduced_keep_one,
        reduce_gain_one,
        first_weights[0],
        pre_grad_one,
        mask_full,
        count,
    )
    reduce_one_grad, deform_weight_grad, expand_one_grad = block_grads(
        (reduced_low_one, input_low), (pairs_one[0], columns), (pairs_one[1], pairs_one[2])
    )
    return (
        output,
        input_grad,
        reduce_one_grad,
        reduce_gain_one_grad,
        reduce_bias_one_grad,
        offset_weight_grad,
        deform_weight_grad,
        gains_one[0],
        gains_one[1],
        expand_one_grad,
        gains_one[2],
        gains_one[3],
        reduce_two_grad,
        reduce_gain_two_grad,
        reduce_bias_two_grad,
        conv_weight_grad,
        gains_two[0],
        gains_two[1],
        expand_two_grad,
        gains_two[2],
        gains_two[3],
    )


def solution(mesh):
    placed = (
        P("ch", "rows", None, None),
        P(),
        P(None, "ch", "rows", None),
        P("ch", None),
        P(),
        P(),
        P(),
        P("ch", None),
        P(),
        P(),
        P("ch", None),
        P(),
        P(),
        P("ch", None),
        P(),
        P(),
        P("ch", None),
        P(),
        P(),
        P("ch", None),
        P(),
        P(),
        P("ch", "rows", None, None),
    )
    return jax.shard_map(
        per_device,
        mesh=mesh,
        in_specs=placed,
        out_specs=(
            P("ch", "rows", None, None),
            P("ch", "rows", None, None),
            P("ch", None),
            P("ch"),
            P("ch"),
            P(),
            P("ch", None),
            P("ch"),
            P("ch"),
            P("ch", None),
            P("ch"),
            P("ch"),
            P("ch", None),
            P("ch"),
            P("ch"),
            P("ch", None),
            P("ch"),
            P("ch"),
            P("ch", None),
            P("ch"),
            P("ch"),
        ),
        check_vma=False,
    )
```

```python
import functools
import jax
import jax.numpy as jnp
from jax import lax
from jax.experimental import pallas as pl
from jax.experimental.pallas import tpu as pltpu
from jax.sharding import PartitionSpec as P

bf16 = jnp.bfloat16
f32 = jnp.float32
VMEM = pltpu.VMEM
MID = 512
NT = (((1,), (1,)), ((), ()))
NN = (((1,), (0,)), ((), ()))


def dot(a, b, dims=NN):
    return lax.dot_general(a, b, dims, preferred_element_type=f32)


def call(body, outs, scratch=(), limit=56):
    return pl.pallas_call(
        body,
        out_shape=outs,
        scratch_shapes=list(scratch),
        compiler_params=pltpu.CompilerParams(vmem_limit_bytes=limit * 2**20),
    )


def shift_lanes(values, by, width):
    place = lax.broadcasted_iota(jnp.int32, values.shape, values.ndim - 1) % width
    moved = pltpu.roll(values, by % values.shape[-1], values.ndim - 1)
    return jnp.where((place >= by) & (place < width + by), moved, 0.0)


def shift_rows(values, by, width):
    place = lax.broadcasted_iota(jnp.int32, values.shape, 0) % width
    moved = pltpu.roll(values, by % values.shape[0], 0)
    return jnp.where((place >= by) & (place < width + by), moved, 0.0)


def offset_fraction(ext_ref, ow_ref, b, base, pixels, width):
    u = None
    for i in range(3):
        start = (base + 2 * i) * width
        term = dot(ow_ref[i], ext_ref[b, start : start + pixels, :], NT)
        u = term if u is None else u + term
    total = u[32:64]
    total = total + shift_lanes(u[0:32], 2, width) + shift_lanes(u[64:96], -2, width)
    return 1.0 / (1.0 + jnp.exp(-total))


def deform_forward_body(
    ext_ref, ow_ref, disp_ref, m_ref, mask_ref,
    cols_ref, y_ref, frac_ref, stat_ref,
    par_ref, s_ref, *, batch, rows, width, deep
):
    pixels = rows * width
    lane = lax.broadcasted_iota(jnp.int32, (32, 128), 1)
    column = lane % width
    upper = lane // width

    def image(b, carry):
        frac = offset_fraction(ext_ref, ow_ref, b, deep - 2, pixels, width)
        for i in range(4):
            frac_ref[b, i] = frac[i * 8 : i * 8 + 8]
        pix = lax.broadcasted_iota(jnp.int32, (1, pixels), 1)
        row_at, col_at = pix // width, pix % width
        tops, lefts, ys, xs = [], [], [], []
        for k in range(9):
            i, j = k // 3, k % 3
            tops.append(row_at + disp_ref[b, i, 2 * j : 2 * j + 1, :] + (deep - 2))
            lefts.append(col_at + 2 * (j - 1) + disp_ref[b, i, 2 * j + 1 : 2 * j + 2, :])
            at = i * 8 + 2 * j
            ys.append(frac[at : at + 1])
            xs.append(frac[at + 1 : at + 2])
        blank = jnp.zeros((23, pixels), f32)
        par = jnp.concatenate(
            [jnp.concatenate(g, axis=0).astype(f32) if g is not None else blank
             for g in (tops, None, lefts, None, ys, None, xs, None)], axis=0)
        par_ref[...] = par.T

        def row_of_taps(i, carry):
            for j in range(3):
                k = i * 3 + j
                for c in range(pixels // 32):
                    p = pltpu.roll(par_ref[c * 32 : c * 32 + 32, :], 128 - k, 1)
                    wide = (32, 128)
                    top = jnp.broadcast_to(p[:, 0:1], wide).astype(jnp.int32) - upper
                    left = jnp.broadcast_to(p[:, 32:33], wide).astype(jnp.int32)
                    fy = jnp.broadcast_to(p[:, 64:65], wide)
                    fx = jnp.broadcast_to(p[:, 96:97], wide)
                    cw = jnp.where(column == left, 1.0 - fx, jnp.where(column == left + 1, fx, 0.0))
                    ca, cb = (1.0 - fy) * cw, fy * cw
                    for q in range(8):
                        s = jnp.where(top == 2 * q, ca, jnp.where(top == 2 * q - 1, cb, 0.0))
                        s_ref[j * pixels + c * 32 : j * pixels + c * 32 + 32, q * 128 : q * 128 + 128] = s.astype(bf16)
            start = pl.multiple_of(i * 2 * width, 128)
            window = ext_ref[b, pl.ds(start, 16 * width), :]
            for j in range(3):
                got = dot(s_ref[j * pixels : (j + 1) * pixels, :], window).astype(bf16)
                cols_ref[pl.ds(pl.multiple_of(b * pixels, pixels), pixels), pl.ds(pl.multiple_of((i * 3 + j) * MID, MID), MID)] = got
            return carry

        return lax.fori_loop(0, 3, row_of_taps, carry)

    lax.fori_loop(0, batch, image, 0)
    y = dot(cols_ref[...], m_ref[...], NT)
    y_ref[...] = y
    write_stats(stat_ref, y * mask_ref[:, 0:1], y)


def write_stats(stat_ref, weighted, values):
    channels = weighted.shape[1]
    n = channels // 128
    first = jnp.sum(weighted, axis=0, keepdims=True)
    second = jnp.sum(weighted * values, axis=0, keepdims=True)
    for c in range(n):
        stat_ref[c : c + 1, :] = first[:, c * 128 : c * 128 + 128]
        stat_ref[n + c : n + c + 1, :] = second[:, c * 128 : c * 128 + 128]


def deform_forward(ext, offset_rows, disp, weight, mask_wide, rows, width):
    batch = ext.shape[0]
    pixels = rows * width
    n = batch * pixels
    return call(
        functools.partial(deform_forward_body, batch=batch, rows=rows, width=width, deep=2 * rows),
        (
            jax.ShapeDtypeStruct((n, 9 * MID), bf16),
            jax.ShapeDtypeStruct((n, MID), f32),
            jax.ShapeDtypeStruct((batch, 4, 8, pixels), f32),
            jax.ShapeDtypeStruct((8, 128), f32),
        ),
        [VMEM((pixels, 128), f32), VMEM((3 * pixels, 16 * width), bf16)],
    )(ext, offset_rows, disp, weight, mask_wide)


def deform_backward_body(
    ext_ref, ow_ref, disp_ref, frac_ref, m_ref, dy_ref,
    far_up_ref, up_ref, own_ref, down_ref, far_down_ref, dow_ref,
    dext_ref, dc_ref, g_ref, st_ref, df_ref, *, batch, rows, width, deep
):
    pixels = rows * width
    window = 16 * width
    dow_ref[...] = jnp.zeros_like(dow_ref)
    dext_ref[...] = jnp.zeros_like(dext_ref)

    def image(b, carry):
        at = pl.multiple_of(b * pixels, pixels)

        def row_of_taps(i, carry):
            dy = dy_ref[pl.ds(at, pixels), :]
            for j in range(3):
                m = m_ref[:, pl.ds(pl.multiple_of((i * 3 + j) * MID, MID), MID)]
                dc_ref[j * pixels : (j + 1) * pixels, :] = dot(dy, m).astype(bf16)
            start = pl.multiple_of(i * 2 * width, 128)
            g_ref[...] = dot(ext_ref[b, pl.ds(start, window), :], dc_ref[...], NT)
            place = lax.broadcasted_iota(jnp.int32, (width, 128), 0)
            for j in range(3):
                for h in range(pixels // 128):
                    lanes = slice(h * 128, h * 128 + 128)
                    at_l = slice(j * pixels + h * 128, j * pixels + h * 128 + 128)
                    pix = lax.broadcasted_iota(jnp.int32, (1, 128), 1) + h * 128
                    by_y, by_x = slice(2 * j, 2 * j + 1), slice(2 * j + 1, 2 * j + 2)
                    top = pix // width + disp_ref[b, i, by_y, lanes] + (deep - 2)
                    left = pix % width + 2 * (j - 1) + disp_ref[b, i, by_x, lanes]
                    fy = frac_ref[b, i, by_y, lanes]
                    fx = frac_ref[b, i, by_x, lanes]
                    here, after = place == left, place == left + 1
                    cw = jnp.where(here, 1.0 - fx, jnp.where(after, fx, 0.0))
                    ca, cb = (1.0 - fy) * cw, fy * cw
                    low_sum = jnp.zeros((width, 128), f32)
                    high_sum = jnp.zeros((width, 128), f32)
                    for r in range(16):
                        part = slice(r * width, r * width + width)
                        g = g_ref[part, at_l]
                        m0, m1 = top == r, top == r - 1
                        low_sum = low_sum + jnp.where(m0, g, 0.0)
                        high_sum = high_sum + jnp.where(m1, g, 0.0)
                        st_ref[part, at_l] = jnp.where(m0, ca, jnp.where(m1, cb, 0.0)).astype(bf16)
                    d_fy = jnp.sum((high_sum - low_sum) * cw, axis=0, keepdims=True)
                    mixed = (1.0 - fy) * low_sum + fy * high_sum
                    d_fx = jnp.sum(
                        jnp.where(after, mixed, 0.0) - jnp.where(here, mixed, 0.0), axis=0, keepdims=True)
                    df_ref[i, by_y, lanes] = d_fy * fy * (1.0 - fy)
                    df_ref[i, by_x, lanes] = d_fx * fx * (1.0 - fx)
            dext_ref[b, pl.ds(start, window), :] += dot(st_ref[...], dc_ref[...])
            return carry

        df_ref[...] = jnp.zeros_like(df_ref)
        carry = lax.fori_loop(0, 3, row_of_taps, carry)
        d_off = df_ref[...].reshape(32, pixels).astype(bf16).astype(f32)
        stacked = jnp.concatenate(
            [shift_lanes(d_off, -2, width), d_off, shift_lanes(d_off, 2, width)], axis=0)
        across = jnp.concatenate([stacked, jnp.zeros((32, pixels), f32)], axis=0).T.astype(bf16)
        stacked = stacked.astype(bf16)
        for i in range(3):
            first = (deep - 2 + 2 * i) * width
            part = slice(first, first + pixels)
            dow_ref[i] += dot(stacked, ext_ref[b, part, :])
            dext_ref[b, part, :] += dot(across[:, :96], ow_ref[i])
        tiles = (far_up_ref, up_ref, own_ref, down_ref, far_down_ref)
        for t, ref in enumerate(tiles):
            ref[b] = dext_ref[b, t * pixels : (t + 1) * pixels, :].astype(ref.dtype)
        return carry

    lax.fori_loop(0, batch, image, 0)


def deform_backward(ext, offset_rows, disp, frac, weight, dy, rows, width):
    batch = ext.shape[0]
    pixels = rows * width
    return call(
        functools.partial(deform_backward_body, batch=batch, rows=rows, width=width, deep=2 * rows),
        tuple(jax.ShapeDtypeStruct((batch, pixels, MID), f32 if t == 2 else bf16) for t in range(5))
        + (jax.ShapeDtypeStruct((3, 96, MID), f32),),
        [
            VMEM(ext.shape, f32),
            VMEM((3 * pixels, MID), bf16),
            VMEM((16 * width, 3 * pixels), f32),
            VMEM((16 * width, 3 * pixels), bf16),
            VMEM((4, 8, pixels), f32),
        ],
    )(ext, offset_rows, disp, frac, weight, dy)


def conv_forward_body(rim_ref, m_ref, mask_ref, y_ref, stat_ref, *, batch, rows, width):
    pixels = rows * width
    for b in range(batch):
        total = None
        for j in range(3):
            u = None
            for i in range(3):
                k = i * 3 + j
                start = 2 * i * width
                term = dot(rim_ref[b, start : start + pixels, :], m_ref[:, k * MID : (k + 1) * MID], NT)
                u = term if u is None else u + term
            u = shift_rows(u, -2 * (j - 1), width) if j != 1 else u
            total = u if total is None else total + u
        y_ref[b * pixels : (b + 1) * pixels, :] = total
    y = y_ref[...]
    write_stats(stat_ref, y * mask_ref[:, 0:1], y)


def conv_forward(rim, weight, mask_wide, rows, width):
    batch = rim.shape[0]
    n = batch * rows * width
    return call(
        functools.partial(conv_forward_body, batch=batch, rows=rows, width=width),
        (jax.ShapeDtypeStruct((n, MID), f32), jax.ShapeDtypeStruct((8, 128), f32)),
    )(rim, weight, mask_wide)


def conv_backward_body(rim_ref, m_ref, dh_ref, *, batch, rows, width):
    pixels = rows * width
    for b in range(batch):
        total = None
        for j in range(3):
            u = None
            for i in range(3):
                k = i * 3 + j
                start = (4 - 2 * i) * width
                term = dot(rim_ref[b, start : start + pixels, :], m_ref[:, k * MID : (k + 1) * MID])
                u = term if u is None else u + term
            u = shift_rows(u, 2 * (j - 1), width) if j != 1 else u
            total = u if total is None else total + u
        dh_ref[b * pixels : (b + 1) * pixels, :] = total


def conv_backward(rim, weight, rows, width):
    batch = rim.shape[0]
    n = batch * rows * width
    return call(
        functools.partial(conv_backward_body, batch=batch, rows=rows, width=width),
        jax.ShapeDtypeStruct((n, MID), f32),
    )(rim, weight)


def conv_weight_body(dy_ref, rim_ref, out_ref, dyt_ref, *, batch, rows, width):
    pixels = rows * width
    n = batch * pixels
    dy = dy_ref[...].astype(f32)
    for j in range(3):
        moved = shift_rows(dy, 2 * (j - 1), width) if j != 1 else dy
        dyt_ref[j] = moved.T.astype(bf16)
    for j in range(3):
        for i in range(3):
            k = i * 3 + j
            start = 2 * i * width
            total = None
            for b in range(batch):
                term = dot(dyt_ref[j, :, b * pixels : (b + 1) * pixels], rim_ref[b, start : start + pixels, :])
                total = term if total is None else total + term
            out_ref[:, k * MID : (k + 1) * MID] = total.astype(bf16)


def conv_weight_gradient(dy, rim, rows, width):
    batch = rim.shape[0]
    return call(
        functools.partial(conv_weight_body, batch=batch, rows=rows, width=width),
        jax.ShapeDtypeStruct((MID, 9 * MID), bf16),
        [VMEM((3, MID, batch * rows * width), bf16)],
    )(dy, rim)


TILES = 2
EPSILON = 1e-05


def gelu_tanh(v):
    return jax.nn.gelu(v, approximate=True)


def gelu_back(pre, upstream):
    _, pullback = jax.vjp(gelu_tanh, pre)
    return pullback(upstream)[0]


def swap_with(values, axis, step):
    return lax.ppermute(values, axis, [(i, i ^ step) for i in range(lax.axis_size(axis))])


def from_behind(block, axis, distance):
    devices = range(lax.axis_size(axis))
    route = [(i - distance, i) for i in devices if i - distance in devices]
    return lax.ppermute(block, axis, route)


def ladder_sum(values):
    for axis in ("ch", "rows"):
        step = 1
        while step < lax.axis_size(axis):
            values = values + swap_with(values, axis, step)
            step *= 2
    return values


def to_everyone(values, groups, size):
    spread = jnp.broadcast_to(values[None], (size,) + values.shape)
    return lax.all_to_all(spread, ("rows", "ch"), 0, 0, axis_index_groups=groups, tiled=True)


def total_of(block):
    devices = lax.axis_size("rows") * lax.axis_size("ch")
    if block.shape[0] < 32:
        block = jnp.sum(to_everyone(block, None, devices), axis=0)
        return block.reshape(2, -1)
    core = lax.axis_index("ch") % 2
    first, second = block.reshape(2, -1, 128)
    own = jnp.where(core == 0, first, second)
    other = jnp.where(core == 0, second, first)
    half = own + swap_with(other, "ch", 1)
    groups = [[i * 2 + k for i in range(devices // 2)] for k in range(2)]
    half = jnp.sum(to_everyone(half, groups, devices // 2), axis=0)
    other = swap_with(half, "ch", 1)
    first = jnp.where(core == 0, half, other)
    second = jnp.where(core == 0, other, half)
    return jnp.stack([first.reshape(-1), second.reshape(-1)])


def sums_block(first, second):
    return jnp.concatenate([jnp.sum(first, axis=0), jnp.sum(second, axis=0)]).reshape(-1, 128)


def own_slice(full):
    size = full.shape[0] // lax.axis_size("ch")
    return lax.dynamic_slice_in_dim(full, lax.axis_index("ch") * size, size)


def gather_weight(weight):
    return lax.all_gather(weight.astype(bf16), "ch", axis=0, tiled=True)


class Norm:
    def __init__(self, values, block, gain, shift, mask, count):
        sums = total_of(block)
        self.mean = sums[0] / count
        self.scale = lax.rsqrt(sums[1] / count - self.mean * self.mean + EPSILON)
        self.values, self.gain, self.shift, self.mask, self.count = values, gain, shift, mask, count

    def normal(self):
        return (self.values - self.mean) * self.scale

    def out(self):
        return self.normal() * self.gain + self.shift

    def back(self, upstream):
        shift_sum, gain_sum = total_of(sums_block(upstream, upstream * self.normal()))
        values_grad = self.scale * (
            upstream * self.gain
            - self.mask * (self.gain * shift_sum + self.normal() * (self.gain * gain_sum)) / self.count
        )
        return values_grad.astype(bf16), own_slice(gain_sum), own_slice(shift_sum)


def forward_block(values, mask):
    masked = values * mask
    return sums_block(masked, masked * values)


def pick(values, bit):
    return lax.dynamic_index_in_dim(values, bit, 1, keepdims=False)


def halve(values, axis, step, bit):
    pairs = values.reshape((values.shape[0] // 2, 2) + values.shape[1:])
    got = swap_with(pick(pairs, 1 - bit), axis, step)
    return (pick(pairs, bit).astype(f32) + got.astype(f32)).astype(bf16)


def reduce_gradient(upstream, acts):
    ch, rows = lax.axis_size("ch"), lax.axis_size("rows")
    out, inner = upstream.shape[1], acts.shape[1]
    core = lax.axis_index("ch") % 2

    def part(bit):
        split = upstream.reshape(upstream.shape[0], ch // 2, 2, out // ch)
        chosen = lax.dynamic_index_in_dim(split, bit, 2, keepdims=False)
        chosen = chosen.reshape(upstream.shape[0], out // 2)
        return dot(chosen, acts, (((0,), (0,)), ((), ()))).astype(bf16)

    got = swap_with(part(1 - core), "ch", 1)
    total = (part(core).astype(f32) + got.astype(f32)).astype(bf16)
    return finish_reduction(total, ch, rows, out, inner)


def reduce_whole(gradient):
    ch, rows = lax.axis_size("ch"), lax.axis_size("rows")
    out, inner = gradient.shape
    total = halve(gradient.reshape(ch, out // ch, inner), "ch", 1, lax.axis_index("ch") % 2)
    return finish_reduction(total, ch, rows, out, inner)


def finish_reduction(total, ch, rows, out, inner):
    total = total.reshape(ch // 2, out // ch, inner)
    step = 2
    while step < ch:
        total = halve(total, "ch", step, lax.axis_index("ch") // step % 2)
        step *= 2
    total = total.reshape(rows, out // ch // rows, inner)
    step = 1
    while step < rows:
        total = halve(total, "rows", step, lax.axis_index("rows") // step % 2)
        step *= 2
    while step > 1:
        step //= 2
        bit = lax.axis_index("rows") // step % 2
        got = swap_with(total, "rows", step)
        first = jnp.where(bit == 0, total, got)
        second = jnp.where(bit == 0, got, total)
        total = jnp.stack([first, second], axis=1).reshape((-1,) + total.shape[1:])
    return total.reshape(out // ch, inner).astype(f32)


def deep_rows(tile):
    above = [from_behind(tile, "rows", k) for k in range(TILES, 0, -1)]
    below = [from_behind(tile, "rows", -k) for k in range(1, TILES + 1)]
    return jnp.concatenate(above + [tile] + below, axis=1)


def deep_return(tiles):
    far_up, up, own, down, far_down = tiles
    own = own + from_behind(far_up, "rows", -2).astype(f32)
    own = own + from_behind(up, "rows", -1).astype(f32)
    own = own + from_behind(down, "rows", 1).astype(f32)
    return own + from_behind(far_down, "rows", 2).astype(f32)


def near_rows(tile, width):
    size = 2 * width
    above = from_behind(tile[:, -size:], "rows", 1)
    below = from_behind(tile[:, :size], "rows", -1)
    return jnp.concatenate([above, tile, below], axis=1)


def per_device(
    inputs,
    heights,
    displacements,
    reduce_one,
    reduce_gain_one,
    reduce_bias_one,
    offset_weight,
    deform_weight,
    deform_gain,
    deform_bias,
    expand_one,
    expand_gain_one,
    expand_bias_one,
    reduce_two,
    reduce_gain_two,
    reduce_bias_two,
    conv_weight,
    conv_gain,
    conv_bias,
    expand_two,
    expand_gain_two,
    expand_bias_two,
    cotangent,
):
    batch, rows, width, channels = inputs.shape
    pixels = rows * width
    n = batch * pixels
    own_heights = lax.dynamic_slice_in_dim(heights, lax.axis_index("ch") * batch, batch)
    rows_here = lax.axis_index("rows") * rows + jnp.arange(rows, dtype=jnp.int32)
    mask = (rows_here[None, :] < own_heights[:, None]).astype(f32)
    mask = jnp.broadcast_to(mask[:, :, None], (batch, rows, width)).reshape(n, 1)
    mask_wide = jnp.broadcast_to(mask, (n, 128))
    count = jnp.sum(heights).astype(f32) * width

    offset_rows = offset_weight.astype(bf16).reshape(3, 6, 3, 3, MID).transpose(2, 3, 0, 1, 4)
    offset_rows = jnp.pad(offset_rows, ((0, 0), (0, 0), (0, 1), (0, 2), (0, 0))).reshape(3, 96, MID)
    disp = jnp.pad(displacements.reshape(3, 6, batch, pixels), ((0, 0), (0, 2), (0, 0), (0, 0)))
    disp = disp.transpose(2, 0, 1, 3)

    reduce_full, deform_full, expand_full, reduce_full_two, conv_full, expand_full_two = [
        gather_weight(w)
        for w in (reduce_one, deform_weight, expand_one, reduce_two, conv_weight, expand_two)
    ]

    acts = inputs.reshape(n, channels)
    acts_low = acts.astype(bf16)
    reduced = dot(acts_low, reduce_full, NT)
    norm_a = Norm(reduced, forward_block(reduced, mask), reduce_gain_one, reduce_bias_one, mask, count)
    hidden = (gelu_tanh(norm_a.out()) * mask).astype(bf16)
    extended = deep_rows(hidden.reshape(batch, pixels, MID))
    columns, mixed, fraction, block = deform_forward(
        extended, offset_rows, disp, deform_full, mask_wide, rows, width
    )
    norm_b = Norm(mixed, block, deform_gain, deform_bias, mask, count)
    middle = (gelu_tanh(norm_b.out()) * mask).astype(bf16)
    expanded = dot(middle, expand_full, NT)
    norm_c = Norm(expanded, forward_block(expanded, mask), expand_gain_one, expand_bias_one, mask, count)
    pre_out = norm_c.out() + acts
    first = gelu_tanh(pre_out) * mask

    first_low = first.astype(bf16)
    reduced_two = dot(first_low, reduce_full_two, NT)
    norm_d = Norm(
        reduced_two, forward_block(reduced_two, mask), reduce_gain_two, reduce_bias_two, mask, count
    )
    hidden_two = (gelu_tanh(norm_d.out()) * mask).astype(bf16)
    rimmed = near_rows(hidden_two.reshape(batch, pixels, MID), width)
    mixed_two, block = conv_forward(rimmed, conv_full, mask_wide, rows, width)
    norm_e = Norm(mixed_two, block, conv_gain, conv_bias, mask, count)
    middle_two = (gelu_tanh(norm_e.out()) * mask).astype(bf16)
    expanded_two = dot(middle_two, expand_full_two, NT)
    norm_f = Norm(
        expanded_two, forward_block(expanded_two, mask), expand_gain_two, expand_bias_two, mask, count
    )
    pre_out_two = norm_f.out() + first
    output = gelu_tanh(pre_out_two) * mask

    pre_grad_two = gelu_back(pre_out_two, cotangent.reshape(n, channels) * mask)
    expanded_grad_two, expand_gain_two_grad, expand_bias_two_grad = norm_f.back(pre_grad_two)
    middle_grad_two = dot(expanded_grad_two, expand_full_two)
    mixed_grad_two, conv_gain_grad, conv_bias_grad = norm_e.back(
        gelu_back(norm_e.out(), middle_grad_two * mask)
    )
    expand_two_grad = reduce_gradient(expanded_grad_two, middle_two)
    mixed_rim = near_rows(mixed_grad_two.reshape(batch, pixels, MID), width)
    conv_weight_grad = reduce_whole(conv_weight_gradient(mixed_grad_two, rimmed, rows, width))
    hidden_grad_two = conv_backward(mixed_rim, conv_full, rows, width)
    reduced_grad_two, reduce_gain_two_grad, reduce_bias_two_grad = norm_d.back(
        gelu_back(norm_d.out(), hidden_grad_two * mask)
    )
    reduce_two_grad = reduce_gradient(reduced_grad_two, first_low)
    first_grad = pre_grad_two + dot(reduced_grad_two, reduce_full_two)

    pre_grad = gelu_back(pre_out, first_grad * mask)
    expanded_grad, expand_gain_one_grad, expand_bias_one_grad = norm_c.back(pre_grad)
    middle_grad = dot(expanded_grad, expand_full)
    mixed_grad, deform_gain_grad, deform_bias_grad = norm_b.back(
        gelu_back(norm_b.out(), middle_grad * mask)
    )
    expand_one_grad = reduce_gradient(expanded_grad, middle)
    *tiles, offset_grad = deform_backward(
        extended, offset_rows, disp, fraction, deform_full, mixed_grad, rows, width
    )
    deform_weight_grad = reduce_gradient(mixed_grad, columns)
    offset_grad = offset_grad.reshape(3, 3, 4, 8, MID)[:, :, :3, :6]
    offset_grad = offset_grad.transpose(2, 3, 0, 1, 4).reshape(18, 9 * MID)
    offset_weight_grad = ladder_sum(offset_grad)
    hidden_grad = deep_return(tiles).reshape(n, MID)
    reduced_grad, reduce_gain_one_grad, reduce_bias_one_grad = norm_a.back(
        gelu_back(norm_a.out(), hidden_grad * mask)
    )
    reduce_one_grad = reduce_gradient(reduced_grad, acts_low)
    input_grad = pre_grad + dot(reduced_grad, reduce_full)
    return (
        output.reshape(inputs.shape),
        input_grad.reshape(inputs.shape),
        reduce_one_grad,
        reduce_gain_one_grad,
        reduce_bias_one_grad,
        offset_weight_grad,
        deform_weight_grad,
        deform_gain_grad,
        deform_bias_grad,
        expand_one_grad,
        expand_gain_one_grad,
        expand_bias_one_grad,
        reduce_two_grad,
        reduce_gain_two_grad,
        reduce_bias_two_grad,
        conv_weight_grad,
        conv_gain_grad,
        conv_bias_grad,
        expand_two_grad,
        expand_gain_two_grad,
        expand_bias_two_grad,
    )


def solution(mesh):
    tiles = P("ch", "rows", None, None)
    owned = P("ch", None)
    block = (owned, P(), P())
    placed = (tiles, P(), P(None, "ch", "rows", None)) + block + (P(),) + 2 * block + 3 * block + (tiles,)
    grads = (owned, P("ch"), P("ch"))
    return jax.shard_map(
        per_device,
        mesh=mesh,
        in_specs=placed,
        out_specs=(tiles, tiles) + grads + (P(),) + 2 * grads + 3 * grads,
        check_vma=False,
    )
```

```python
import functools
import jax
import jax.numpy as jnp
from jax import lax
from jax.experimental import pallas as pl
from jax.experimental.pallas import tpu as pltpu
from jax.sharding import PartitionSpec as P

bf16 = jnp.bfloat16
f32 = jnp.float32
VMEM = pltpu.VMEM
MID = 512
NT = (((1,), (1,)), ((), ()))
TN = (((0,), (0,)), ((), ()))
NN = (((1,), (0,)), ((), ()))


def dot(a, b, dims=NN):
    return lax.dot_general(a, b, dims, preferred_element_type=f32)


def call(body, outs, scratch=(), limit=56):
    return pl.pallas_call(
        body,
        out_shape=outs,
        scratch_shapes=list(scratch),
        compiler_params=pltpu.CompilerParams(vmem_limit_bytes=limit * 2**20),
    )


def shift_lanes(values, by, width):
    place = lax.broadcasted_iota(jnp.int32, values.shape, values.ndim - 1) % width
    moved = pltpu.roll(values, by % values.shape[-1], values.ndim - 1)
    return jnp.where((place >= by) & (place < width + by), moved, 0.0)


def shift_rows(values, by, width):
    place = lax.broadcasted_iota(jnp.int32, values.shape, 0) % width
    moved = pltpu.roll(values, by % values.shape[0], 0)
    return jnp.where((place >= by) & (place < width + by), moved, 0.0)


def offset_fraction(ext_ref, ow_ref, b, base, pixels, width):
    u = None
    for i in range(3):
        start = (base + 2 * i) * width
        term = dot(ow_ref[i], ext_ref[b, start : start + pixels, :], NT)
        u = term if u is None else u + term
    total = u[32:64]
    total = total + shift_lanes(u[0:32], 2, width) + shift_lanes(u[64:96], -2, width)
    return 1.0 / (1.0 + jnp.exp(-total))


def join_tiles(tiles, ext_ref, pixels):
    for t, ref in enumerate(tiles):
        ext_ref[:, t * pixels : (t + 1) * pixels, :] = ref[...]


def deform_forward_body(
    t0_ref, t1_ref, t2_ref, t3_ref, t4_ref, ow_ref, disp_ref, m_ref, mask_ref,
    cols_ref, y_ref, frac_ref, stat_ref,
    ext_ref, par_ref, s_ref, *, batch, rows, width, deep
):
    pixels = rows * width
    join_tiles((t0_ref, t1_ref, t2_ref, t3_ref, t4_ref), ext_ref, pixels)
    lane = lax.broadcasted_iota(jnp.int32, (32, 128), 1)
    column = lane % width
    upper = lane // width

    def image(b, carry):
        frac = offset_fraction(ext_ref, ow_ref, b, deep - 2, pixels, width)
        for i in range(4):
            frac_ref[b, i] = frac[i * 8 : i * 8 + 8]
        pix = lax.broadcasted_iota(jnp.int32, (1, pixels), 1)
        row_at, col_at = pix // width, pix % width
        tops, lefts, ys, xs = [], [], [], []
        for k in range(9):
            i, j = k // 3, k % 3
            tops.append(row_at + disp_ref[b, i, 2 * j : 2 * j + 1, :] + (deep - 2))
            lefts.append(col_at + 2 * (j - 1) + disp_ref[b, i, 2 * j + 1 : 2 * j + 2, :])
            at = i * 8 + 2 * j
            ys.append(frac[at : at + 1])
            xs.append(frac[at + 1 : at + 2])
        blank = jnp.zeros((23, pixels), f32)
        par = jnp.concatenate(
            [jnp.concatenate(g, axis=0).astype(f32) if g is not None else blank
             for g in (tops, None, lefts, None, ys, None, xs, None)], axis=0)
        par_ref[...] = par.T

        def row_of_taps(i, carry):
            for j in range(3):
                k = i * 3 + j
                for c in range(pixels // 32):
                    p = pltpu.roll(par_ref[c * 32 : c * 32 + 32, :], 128 - k, 1)
                    wide = (32, 128)
                    top = jnp.broadcast_to(p[:, 0:1], wide).astype(jnp.int32) - upper
                    left = jnp.broadcast_to(p[:, 32:33], wide).astype(jnp.int32)
                    fy = jnp.broadcast_to(p[:, 64:65], wide)
                    fx = jnp.broadcast_to(p[:, 96:97], wide)
                    cw = jnp.where(column == left, 1.0 - fx, jnp.where(column == left + 1, fx, 0.0))
                    ca, cb = (1.0 - fy) * cw, fy * cw
                    for q in range(8):
                        s = jnp.where(top == 2 * q, ca, jnp.where(top == 2 * q - 1, cb, 0.0))
                        s_ref[j * pixels + c * 32 : j * pixels + c * 32 + 32, q * 128 : q * 128 + 128] = s.astype(bf16)
            start = pl.multiple_of(i * 2 * width, 128)
            window = ext_ref[b, pl.ds(start, 16 * width), :]
            for j in range(3):
                got = dot(s_ref[j * pixels : (j + 1) * pixels, :], window).astype(bf16)
                cols_ref[pl.ds(pl.multiple_of(b * pixels, pixels), pixels), pl.ds(pl.multiple_of((i * 3 + j) * MID, MID), MID)] = got
            return carry

        return lax.fori_loop(0, 3, row_of_taps, carry)

    lax.fori_loop(0, batch, image, 0)
    y = dot(cols_ref[...], m_ref[...], NT)
    y_ref[...] = y
    write_stats(stat_ref, y * mask_ref[:, 0:1], y)


def write_stats(stat_ref, weighted, values):
    channels = weighted.shape[1]
    n = channels // 128
    first = jnp.sum(weighted, axis=0, keepdims=True)
    second = jnp.sum(weighted * values, axis=0, keepdims=True)
    for c in range(n):
        stat_ref[c : c + 1, :] = first[:, c * 128 : c * 128 + 128]
        stat_ref[n + c : n + c + 1, :] = second[:, c * 128 : c * 128 + 128]


def deform_forward(tiles, offset_rows, disp, weight, mask_wide, rows, width):
    batch = tiles[0].shape[0]
    pixels = rows * width
    n = batch * pixels
    return call(
        functools.partial(deform_forward_body, batch=batch, rows=rows, width=width, deep=2 * rows),
        (
            jax.ShapeDtypeStruct((n, 9 * MID), bf16),
            jax.ShapeDtypeStruct((n, MID), f32),
            jax.ShapeDtypeStruct((batch, 4, 8, pixels), f32),
            jax.ShapeDtypeStruct((8, 128), f32),
        ),
        [
            VMEM((batch, 5 * pixels, MID), bf16),
            VMEM((pixels, 128), f32),
            VMEM((3 * pixels, 16 * width), bf16),
        ],
    )(*tiles, offset_rows, disp, weight, mask_wide)


def deform_backward_body(
    t0_ref, t1_ref, t2_ref, t3_ref, t4_ref, ow_ref, disp_ref, frac_ref, m_ref, dy_ref,
    far_up_ref, up_ref, own_ref, down_ref, far_down_ref, dow_ref,
    ext_ref, dext_ref, dc_ref, g_ref, st_ref, df_ref, *, batch, rows, width, deep
):
    pixels = rows * width
    join_tiles((t0_ref, t1_ref, t2_ref, t3_ref, t4_ref), ext_ref, pixels)
    window = 16 * width
    dow_ref[...] = jnp.zeros_like(dow_ref)
    dext_ref[...] = jnp.zeros_like(dext_ref)

    def image(b, carry):
        at = pl.multiple_of(b * pixels, pixels)

        def row_of_taps(i, carry):
            dy = dy_ref[pl.ds(at, pixels), :]
            for j in range(3):
                m = m_ref[:, pl.ds(pl.multiple_of((i * 3 + j) * MID, MID), MID)]
                dc_ref[j * pixels : (j + 1) * pixels, :] = dot(dy, m).astype(bf16)
            start = pl.multiple_of(i * 2 * width, 128)
            g_ref[...] = dot(ext_ref[b, pl.ds(start, window), :], dc_ref[...], NT)
            place = lax.broadcasted_iota(jnp.int32, (width, 128), 0)
            for j in range(3):
                for h in range(pixels // 128):
                    lanes = slice(h * 128, h * 128 + 128)
                    at_l = slice(j * pixels + h * 128, j * pixels + h * 128 + 128)
                    pix = lax.broadcasted_iota(jnp.int32, (1, 128), 1) + h * 128
                    by_y, by_x = slice(2 * j, 2 * j + 1), slice(2 * j + 1, 2 * j + 2)
                    top = pix // width + disp_ref[b, i, by_y, lanes] + (deep - 2)
                    left = pix % width + 2 * (j - 1) + disp_ref[b, i, by_x, lanes]
                    fy = frac_ref[b, i, by_y, lanes]
                    fx = frac_ref[b, i, by_x, lanes]
                    here, after = place == left, place == left + 1
                    cw = jnp.where(here, 1.0 - fx, jnp.where(after, fx, 0.0))
                    ca, cb = (1.0 - fy) * cw, fy * cw
                    low_sum = jnp.zeros((width, 128), f32)
                    high_sum = jnp.zeros((width, 128), f32)
                    for r in range(16):
                        part = slice(r * width, r * width + width)
                        g = g_ref[part, at_l]
                        m0, m1 = top == r, top == r - 1
                        low_sum = low_sum + jnp.where(m0, g, 0.0)
                        high_sum = high_sum + jnp.where(m1, g, 0.0)
                        st_ref[part, at_l] = jnp.where(m0, ca, jnp.where(m1, cb, 0.0)).astype(bf16)
                    d_fy = jnp.sum((high_sum - low_sum) * cw, axis=0, keepdims=True)
                    mixed = (1.0 - fy) * low_sum + fy * high_sum
                    d_fx = jnp.sum(
                        jnp.where(after, mixed, 0.0) - jnp.where(here, mixed, 0.0), axis=0, keepdims=True)
                    df_ref[i, by_y, lanes] = d_fy * fy * (1.0 - fy)
                    df_ref[i, by_x, lanes] = d_fx * fx * (1.0 - fx)
            dext_ref[b, pl.ds(start, window), :] += dot(st_ref[...], dc_ref[...])
            return carry

        df_ref[...] = jnp.zeros_like(df_ref)
        carry = lax.fori_loop(0, 3, row_of_taps, carry)
        d_off = df_ref[...].reshape(32, pixels).astype(bf16).astype(f32)
        stacked = jnp.concatenate(
            [shift_lanes(d_off, -2, width), d_off, shift_lanes(d_off, 2, width)], axis=0)
        across = jnp.concatenate([stacked, jnp.zeros((32, pixels), f32)], axis=0).T.astype(bf16)
        stacked = stacked.astype(bf16)
        for i in range(3):
            first = (deep - 2 + 2 * i) * width
            part = slice(first, first + pixels)
            dow_ref[i] += dot(stacked, ext_ref[b, part, :])
            dext_ref[b, part, :] += dot(across[:, :96], ow_ref[i])
        tiles = (far_up_ref, up_ref, own_ref, down_ref, far_down_ref)
        for t, ref in enumerate(tiles):
            ref[b] = dext_ref[b, t * pixels : (t + 1) * pixels, :].astype(ref.dtype)
        return carry

    lax.fori_loop(0, batch, image, 0)


def deform_backward(tiles, offset_rows, disp, frac, weight, dy, rows, width):
    batch = tiles[0].shape[0]
    pixels = rows * width
    return call(
        functools.partial(deform_backward_body, batch=batch, rows=rows, width=width, deep=2 * rows),
        tuple(jax.ShapeDtypeStruct((batch, pixels, MID), f32 if t == 2 else bf16) for t in range(5))
        + (jax.ShapeDtypeStruct((3, 96, MID), f32),),
        [
            VMEM((batch, 5 * pixels, MID), bf16),
            VMEM((batch, 5 * pixels, MID), f32),
            VMEM((3 * pixels, MID), bf16),
            VMEM((16 * width, 3 * pixels), f32),
            VMEM((16 * width, 3 * pixels), bf16),
            VMEM((4, 8, pixels), f32),
        ],
    )(*tiles, offset_rows, disp, frac, weight, dy)


def conv_forward_body(rim_ref, m_ref, mask_ref, y_ref, stat_ref, *, batch, rows, width):
    pixels = rows * width
    for b in range(batch):
        total = None
        for j in range(3):
            u = None
            for i in range(3):
                k = i * 3 + j
                start = 2 * i * width
                term = dot(rim_ref[b, start : start + pixels, :], m_ref[:, k * MID : (k + 1) * MID], NT)
                u = term if u is None else u + term
            u = shift_rows(u, -2 * (j - 1), width) if j != 1 else u
            total = u if total is None else total + u
        y_ref[b * pixels : (b + 1) * pixels, :] = total
    y = y_ref[...]
    write_stats(stat_ref, y * mask_ref[:, 0:1], y)


def conv_forward(rim, weight, mask_wide, rows, width):
    batch = rim.shape[0]
    n = batch * rows * width
    return call(
        functools.partial(conv_forward_body, batch=batch, rows=rows, width=width),
        (jax.ShapeDtypeStruct((n, MID), f32), jax.ShapeDtypeStruct((8, 128), f32)),
    )(rim, weight, mask_wide)


def conv_backward_body(rim_ref, m_ref, dh_ref, *, batch, rows, width):
    pixels = rows * width
    for b in range(batch):
        total = None
        for j in range(3):
            u = None
            for i in range(3):
                k = i * 3 + j
                start = (4 - 2 * i) * width
                term = dot(rim_ref[b, start : start + pixels, :], m_ref[:, k * MID : (k + 1) * MID])
                u = term if u is None else u + term
            u = shift_rows(u, 2 * (j - 1), width) if j != 1 else u
            total = u if total is None else total + u
        dh_ref[b * pixels : (b + 1) * pixels, :] = total


def conv_backward(rim, weight, rows, width):
    batch = rim.shape[0]
    n = batch * rows * width
    return call(
        functools.partial(conv_backward_body, batch=batch, rows=rows, width=width),
        jax.ShapeDtypeStruct((n, MID), f32),
    )(rim, weight)


def conv_weight_body(dy_ref, rim_ref, out_ref, dyt_ref, *, batch, rows, width):
    pixels = rows * width
    n = batch * pixels
    dy = dy_ref[...].astype(f32)
    for j in range(3):
        moved = shift_rows(dy, 2 * (j - 1), width) if j != 1 else dy
        dyt_ref[j] = moved.T.astype(bf16)
    for j in range(3):
        for i in range(3):
            k = i * 3 + j
            start = 2 * i * width
            total = None
            for b in range(batch):
                term = dot(dyt_ref[j, :, b * pixels : (b + 1) * pixels], rim_ref[b, start : start + pixels, :])
                total = term if total is None else total + term
            out_ref[:, k * MID : (k + 1) * MID] = total.astype(bf16)


def conv_weight_gradient(dy, rim, rows, width):
    batch = rim.shape[0]
    return call(
        functools.partial(conv_weight_body, batch=batch, rows=rows, width=width),
        jax.ShapeDtypeStruct((MID, 9 * MID), bf16),
        [VMEM((3, MID, batch * rows * width), bf16)],
    )(dy, rim)


def columns_weight_body(dy_ref, cols_ref, out_ref, dyt_ref):
    dyt_ref[...] = dy_ref[...].astype(f32).T.astype(bf16)
    for k in range(9):
        part = slice(k * MID, (k + 1) * MID)
        out_ref[:, part] = dot(dyt_ref[...], cols_ref[:, part]).astype(bf16)


def columns_weight_gradient(dy, cols):
    return call(
        columns_weight_body,
        jax.ShapeDtypeStruct((MID, 9 * MID), bf16),
        [VMEM((MID, dy.shape[0]), bf16)],
    )(dy, cols)


TILES = 2
EPSILON = 1e-05


def gelu_tanh(v):
    return jax.nn.gelu(v, approximate=True)


def gelu_back(pre, upstream):
    _, pullback = jax.vjp(gelu_tanh, pre)
    return pullback(upstream)[0]


def swap_with(values, axis, step):
    return lax.ppermute(values, axis, [(i, i ^ step) for i in range(lax.axis_size(axis))])


def from_behind(block, axis, distance):
    devices = range(lax.axis_size(axis))
    route = [(i - distance, i) for i in devices if i - distance in devices]
    return lax.ppermute(block, axis, route)


def ladder_sum(values, axis):
    step = 1
    while step < lax.axis_size(axis):
        got = swap_with(values.astype(bf16), axis, step)
        values = values + got.astype(f32)
        step *= 2
    return values


def to_everyone(values, groups, size):
    spread = jnp.broadcast_to(values[None], (size,) + values.shape)
    return lax.all_to_all(spread, ("rows", "ch"), 0, 0, axis_index_groups=groups, tiled=True)


def total_of(block):
    devices = lax.axis_size("rows") * lax.axis_size("ch")
    if block.shape[0] < 32:
        block = jnp.sum(to_everyone(block, None, devices), axis=0)
        return block.reshape(2, -1)
    core = lax.axis_index("ch") % 2
    first, second = block.reshape(2, -1, 128)
    own = jnp.where(core == 0, first, second)
    other = jnp.where(core == 0, second, first)
    half = own + swap_with(other, "ch", 1)
    groups = [[i * 2 + k for i in range(devices // 2)] for k in range(2)]
    half = jnp.sum(to_everyone(half, groups, devices // 2), axis=0)
    other = swap_with(half, "ch", 1)
    first = jnp.where(core == 0, half, other)
    second = jnp.where(core == 0, other, half)
    return jnp.stack([first.reshape(-1), second.reshape(-1)])


def sums_block(first, second):
    return jnp.concatenate([jnp.sum(first, axis=0), jnp.sum(second, axis=0)]).reshape(-1, 128)


def own_slice(full):
    size = full.shape[0] // lax.axis_size("ch")
    return lax.dynamic_slice_in_dim(full, lax.axis_index("ch") * size, size)


def gather_weight(weight):
    return lax.all_gather(weight.astype(bf16), "ch", axis=0, tiled=True)


def gather_by_swaps(weight):
    ch = lax.axis_size("ch")
    held = weight.astype(bf16)[None]
    step = ch // 2
    while step >= 1:
        got = swap_with(held, "ch", step)
        odd = lax.axis_index("ch") // step % 2 == 1
        held = jnp.stack([jnp.where(odd, got, held), jnp.where(odd, held, got)], axis=1)
        held = held.reshape((-1,) + held.shape[2:])
        step //= 2
    return held.reshape((-1,) + weight.shape[1:])


class Norm:
    def __init__(self, values, block, gain, shift, mask, count):
        sums = total_of(block)
        self.mean = sums[0] / count
        self.scale = lax.rsqrt(sums[1] / count - self.mean * self.mean + EPSILON)
        self.values, self.gain, self.shift, self.mask, self.count = values, gain, shift, mask, count

    def normal(self):
        return (self.values - self.mean) * self.scale

    def out(self):
        return self.normal() * self.gain + self.shift

    def back(self, upstream):
        shift_sum, gain_sum = total_of(sums_block(upstream, upstream * self.normal()))
        values_grad = self.scale * (
            upstream * self.gain
            - self.mask * (self.gain * shift_sum + self.normal() * (self.gain * gain_sum)) / self.count
        )
        return values_grad.astype(bf16), own_slice(gain_sum), own_slice(shift_sum)


def forward_block(values, mask):
    masked = values * mask
    return sums_block(masked, masked * values)


def pick(values, bit):
    return lax.dynamic_index_in_dim(values, bit, 1, keepdims=False)


def halve(values, axis, step):
    bit = lax.axis_index(axis) // step % 2
    pairs = values.reshape((values.shape[0] // 2, 2) + values.shape[1:])
    got = swap_with(pick(pairs, 1 - bit), axis, step)
    return (pick(pairs, bit).astype(f32) + got.astype(f32)).astype(bf16)


def scatter_ch(gradient):
    return lax.psum_scatter(gradient, "ch", scatter_dimension=0, tiled=True)


def halve_ch(gradient):
    ch = lax.axis_size("ch")
    total = gradient.reshape((ch, gradient.shape[0] // ch) + gradient.shape[1:])
    step = 1
    while step < ch:
        total = halve(total, "ch", step)
        step *= 2
    return total[0]


def blocks_to_lanes(values, base):
    return jnp.concatenate([values[r : r + base] for r in range(0, values.shape[0], base)], axis=1)


def lanes_to_blocks(values, wide):
    return jnp.concatenate(
        [values[:, c : c + wide] for c in range(0, values.shape[1], wide)], axis=0
    )


def sum_over_rows(parts):
    rows = lax.axis_size("rows")
    total = jnp.concatenate(parts, axis=1)
    base, wide = total.shape
    groups = [[x + 2 * k for k in range(rows // 2)] for x in range(2)]
    total = halve(total.reshape(rows, base // rows, wide), "rows", 1)
    total = lax.all_to_all(total, "rows", 0, 0, axis_index_groups=groups, tiled=True)
    total = jnp.sum(total.astype(f32), axis=0).astype(bf16)
    total = jnp.broadcast_to(total[None], (rows // 2,) + total.shape)
    total = lax.all_to_all(total, "rows", 0, 0, axis_index_groups=groups, tiled=True)
    got = swap_with(total, "rows", 1)
    odd = lax.axis_index("rows") % 2 == 1
    total = jnp.stack([jnp.where(odd, got, total), jnp.where(odd, total, got)], axis=1)
    total = total.reshape(base, wide).astype(f32)
    ends, at = [], 0
    for part in parts:
        ends.append(total[:, at : at + part.shape[1]])
        at += part.shape[1]
    return ends


def deep_rows(tile):
    odd = lax.axis_index("rows") % 2 == 1
    far_up = from_behind(tile, "rows", 2)
    far_down = from_behind(tile, "rows", -2)
    partner = swap_with(tile, "rows", 1)
    passed = swap_with(jnp.where(odd, far_up, far_down), "rows", 1)
    up = jnp.where(odd, partner, passed)
    down = jnp.where(odd, passed, partner)
    return far_up, up, tile, down, far_down


def deep_return(tiles):
    far_up, up, own, down, far_down = tiles
    odd = lax.axis_index("rows") % 2 == 1
    passed = swap_with(jnp.where(odd, down, up), "rows", 1)
    partner = swap_with(jnp.where(odd, up, down), "rows", 1)
    added = (jnp.where(odd, far_up, far_down).astype(f32) + passed.astype(f32)).astype(bf16)
    own = own + partner.astype(f32)
    own = own + from_behind(jnp.where(odd, added, far_up), "rows", -2).astype(f32)
    return own + from_behind(jnp.where(odd, far_down, added), "rows", 2).astype(f32)


def near_rows(tile, width):
    size = 2 * width
    above = from_behind(tile[:, -size:], "rows", 1)
    below = from_behind(tile[:, :size], "rows", -1)
    return jnp.concatenate([above, tile, below], axis=1)


def per_device(
    inputs,
    heights,
    displacements,
    reduce_one,
    reduce_gain_one,
    reduce_bias_one,
    offset_weight,
    deform_weight,
    deform_gain,
    deform_bias,
    expand_one,
    expand_gain_one,
    expand_bias_one,
    reduce_two,
    reduce_gain_two,
    reduce_bias_two,
    conv_weight,
    conv_gain,
    conv_bias,
    expand_two,
    expand_gain_two,
    expand_bias_two,
    cotangent,
):
    batch, rows, width, channels = inputs.shape
    pixels = rows * width
    n = batch * pixels
    own_heights = lax.dynamic_slice_in_dim(heights, lax.axis_index("ch") * batch, batch)
    rows_here = lax.axis_index("rows") * rows + jnp.arange(rows, dtype=jnp.int32)
    mask = (rows_here[None, :] < own_heights[:, None]).astype(f32)
    mask = jnp.broadcast_to(mask[:, :, None], (batch, rows, width)).reshape(n, 1)
    mask_wide = jnp.broadcast_to(mask, (n, 128))
    count = jnp.sum(heights).astype(f32) * width

    offset_rows = offset_weight.astype(bf16).reshape(3, 6, 3, 3, MID).transpose(2, 3, 0, 1, 4)
    offset_rows = jnp.pad(offset_rows, ((0, 0), (0, 0), (0, 1), (0, 2), (0, 0))).reshape(3, 96, MID)
    disp = jnp.pad(displacements.reshape(3, 6, batch, pixels), ((0, 0), (0, 2), (0, 0), (0, 0)))
    disp = disp.transpose(2, 0, 1, 3)

    reduce_full = gather_by_swaps(reduce_one)
    deform_full, expand_full, reduce_full_two, conv_full, expand_full_two = [
        gather_weight(w) for w in (deform_weight, expand_one, reduce_two, conv_weight, expand_two)
    ]

    acts = inputs.reshape(n, channels)
    acts_low = acts.astype(bf16)
    reduced = dot(acts_low, reduce_full, NT)
    norm_a = Norm(reduced, forward_block(reduced, mask), reduce_gain_one, reduce_bias_one, mask, count)
    hidden = (gelu_tanh(norm_a.out()) * mask).astype(bf16)
    near_tiles = deep_rows(hidden.reshape(batch, pixels, MID))
    columns, mixed, fraction, block = deform_forward(
        near_tiles, offset_rows, disp, deform_full, mask_wide, rows, width
    )
    norm_b = Norm(mixed, block, deform_gain, deform_bias, mask, count)
    middle = (gelu_tanh(norm_b.out()) * mask).astype(bf16)
    expanded = dot(middle, expand_full, NT)
    norm_c = Norm(expanded, forward_block(expanded, mask), expand_gain_one, expand_bias_one, mask, count)
    pre_out = norm_c.out() + acts
    first = gelu_tanh(pre_out) * mask

    first_low = first.astype(bf16)
    reduced_two = dot(first_low, reduce_full_two, NT)
    norm_d = Norm(
        reduced_two, forward_block(reduced_two, mask), reduce_gain_two, reduce_bias_two, mask, count
    )
    hidden_two = (gelu_tanh(norm_d.out()) * mask).astype(bf16)
    rimmed = near_rows(hidden_two.reshape(batch, pixels, MID), width)
    mixed_two, block = conv_forward(rimmed, conv_full, mask_wide, rows, width)
    norm_e = Norm(mixed_two, block, conv_gain, conv_bias, mask, count)
    middle_two = (gelu_tanh(norm_e.out()) * mask).astype(bf16)
    expanded_two = dot(middle_two, expand_full_two, NT)
    norm_f = Norm(
        expanded_two, forward_block(expanded_two, mask), expand_gain_two, expand_bias_two, mask, count
    )
    pre_out_two = norm_f.out() + first
    output = gelu_tanh(pre_out_two) * mask

    pre_grad_two = gelu_back(pre_out_two, cotangent.reshape(n, channels) * mask)
    expanded_grad_two, expand_gain_two_grad, expand_bias_two_grad = norm_f.back(pre_grad_two)
    middle_grad_two = dot(expanded_grad_two, expand_full_two)
    mixed_grad_two, conv_gain_grad, conv_bias_grad = norm_e.back(
        gelu_back(norm_e.out(), middle_grad_two * mask)
    )
    expand_two_part = scatter_ch(dot(expanded_grad_two, middle_two, TN).astype(bf16))
    mixed_rim = near_rows(mixed_grad_two.reshape(batch, pixels, MID), width)
    conv_part = scatter_ch(conv_weight_gradient(mixed_grad_two, rimmed, rows, width))
    hidden_grad_two = conv_backward(mixed_rim, conv_full, rows, width)
    reduced_grad_two, reduce_gain_two_grad, reduce_bias_two_grad = norm_d.back(
        gelu_back(norm_d.out(), hidden_grad_two * mask)
    )
    reduce_two_part = scatter_ch(dot(reduced_grad_two, first_low, TN).astype(bf16))
    base = conv_part.shape[0]
    conv_weight_grad, reduce_two_grad, expand_two_grad = sum_over_rows(
        [conv_part, reduce_two_part, blocks_to_lanes(expand_two_part, base)]
    )
    expand_two_grad = lanes_to_blocks(expand_two_grad, MID)
    first_grad = pre_grad_two + dot(reduced_grad_two, reduce_full_two)

    pre_grad = gelu_back(pre_out, first_grad * mask)
    expanded_grad, expand_gain_one_grad, expand_bias_one_grad = norm_c.back(pre_grad)
    middle_grad = dot(expanded_grad, expand_full)
    mixed_grad, deform_gain_grad, deform_bias_grad = norm_b.back(
        gelu_back(norm_b.out(), middle_grad * mask)
    )
    expand_one_part = scatter_ch(dot(expanded_grad, middle, TN).astype(bf16))
    *tiles, offset_grad = deform_backward(
        near_tiles, offset_rows, disp, fraction, deform_full, mixed_grad, rows, width
    )
    deform_part = scatter_ch(columns_weight_gradient(mixed_grad, columns))
    deform_weight_grad, expand_one_grad = sum_over_rows(
        [deform_part, blocks_to_lanes(expand_one_part, base)]
    )
    expand_one_grad = lanes_to_blocks(expand_one_grad, MID)
    offset_part = ladder_sum(offset_grad.reshape(-1, MID), "ch").astype(bf16)
    offset_part = jnp.pad(offset_part, ((0, -offset_part.shape[0] % base), (0, 0)))
    hidden_grad = deep_return(tiles).reshape(n, MID)
    reduced_grad, reduce_gain_one_grad, reduce_bias_one_grad = norm_a.back(
        gelu_back(norm_a.out(), hidden_grad * mask)
    )
    reduce_one_grad, offset_grad = sum_over_rows(
        [halve_ch(dot(reduced_grad, acts_low, TN).astype(bf16)), blocks_to_lanes(offset_part, base)]
    )
    offset_grad = lanes_to_blocks(offset_grad, MID)[:288].reshape(3, 3, 4, 8, MID)[:, :, :3, :6]
    offset_weight_grad = offset_grad.transpose(2, 3, 0, 1, 4).reshape(18, 9 * MID)
    input_grad = pre_grad + dot(reduced_grad, reduce_full)
    return (
        output.reshape(inputs.shape),
        input_grad.reshape(inputs.shape),
        reduce_one_grad,
        reduce_gain_one_grad,
        reduce_bias_one_grad,
        offset_weight_grad,
        deform_weight_grad,
        deform_gain_grad,
        deform_bias_grad,
        expand_one_grad,
        expand_gain_one_grad,
        expand_bias_one_grad,
        reduce_two_grad,
        reduce_gain_two_grad,
        reduce_bias_two_grad,
        conv_weight_grad,
        conv_gain_grad,
        conv_bias_grad,
        expand_two_grad,
        expand_gain_two_grad,
        expand_bias_two_grad,
    )


def solution(mesh):
    tiles = P("ch", "rows", None, None)
    owned = P("ch", None)
    block = (owned, P(), P())
    placed = (tiles, P(), P(None, "ch", "rows", None)) + block + (P(),) + 2 * block + 3 * block + (tiles,)
    grads = (owned, P("ch"), P("ch"))
    return jax.shard_map(
        per_device,
        mesh=mesh,
        in_specs=placed,
        out_specs=(tiles, tiles) + grads + (P(),) + 2 * grads + 3 * grads,
        check_vma=False,
    )
```

```python
import functools
import jax
import jax.numpy as jnp
from jax import lax
from jax.experimental import pallas as pl
from jax.experimental.pallas import tpu as pltpu
from jax.sharding import PartitionSpec as P

bf16 = jnp.bfloat16
f32 = jnp.float32
VMEM = pltpu.VMEM
MID = 512
NT = (((1,), (1,)), ((), ()))
TN = (((0,), (0,)), ((), ()))
NN = (((1,), (0,)), ((), ()))


def dot(a, b, dims=NN):
    return lax.dot_general(a, b, dims, preferred_element_type=f32)


def without(body, count, extra):
    return lambda *refs: body(*refs[:count], *refs[count + extra :])


def call(body, operands, outs, scratch=(), after=()):
    whole = pl.BlockSpec(memory_space=VMEM)
    many = isinstance(outs, tuple)
    return pl.pallas_call(
        without(body, len(operands), len(after)),
        in_specs=[whole] * len(operands) + [pl.BlockSpec(memory_space=pl.ANY)] * len(after),
        out_specs=tuple(whole for _ in outs) if many else whole,
        out_shape=outs,
        scratch_shapes=list(scratch),
        compiler_params=pltpu.CompilerParams(vmem_limit_bytes=56 * 2**20),
    )(*operands, *after)


GELU_A = 0.7978845608028654
GELU_B = 0.044715
STEP = 512


def gelu(v):
    return 0.5 * v * (1.0 + jnp.tanh(GELU_A * (v + GELU_B * v * v * v)))


def gelu_slope(v):
    t = jnp.tanh(GELU_A * (v + GELU_B * v * v * v))
    return 0.5 * (1.0 + t) + 0.5 * v * (1.0 - t * t) * (GELU_A * (1.0 + 3.0 * GELU_B * v * v))


def staged(body, operands, tiled, outs, out_tiled, scratch=(), after=()):
    def spec(shape, dim):
        if dim is None:
            return pl.BlockSpec(shape, lambda s: (0,) * len(shape))
        block = tuple(STEP if d == dim else size for d, size in enumerate(shape))
        if dim == "stat":
            return pl.BlockSpec((8, 128), lambda s: (s, 0))
        return pl.BlockSpec(block, lambda s: tuple(s if d == dim else 0 for d in range(len(shape))))

    steps = [a.shape[d] // STEP for a, d in zip(operands, tiled) if d is not None][0]
    return pl.pallas_call(
        without(body, len(operands), len(after)),
        grid=(steps,),
        in_specs=[spec(a.shape, d) for a, d in zip(operands, tiled)]
        + [pl.BlockSpec(memory_space=pl.ANY)] * len(after),
        out_specs=tuple(spec(o.shape, d) for o, d in zip(outs, out_tiled)),
        out_shape=tuple(outs),
        scratch_shapes=list(scratch),
        compiler_params=pltpu.CompilerParams(vmem_limit_bytes=56 * 2**20),
    )(*operands, *after)


def shaped(*shape, dtype=f32):
    return jax.ShapeDtypeStruct(shape, dtype)


def normed(values, par_ref):
    return values * par_ref[0:1, :] + par_ref[1:2, :]


def norm_gradient(upstream, values, par_ref, back_ref, mask):
    normal = values * par_ref[2:3, :] + par_ref[3:4, :]
    return upstream * back_ref[0:1, :] - mask * (back_ref[1:2, :] + normal * back_ref[2:3, :])


def expand_forward_body(y_ref, par_ref, mask_ref, e_ref, mid_ref, out_ref, stat_ref):
    mask = mask_ref[:, 0:1]

    @pl.when(pl.program_id(0) == 0)
    def _():
        mid_ref[...] = (gelu(normed(y_ref[...], par_ref)) * mask).astype(bf16)

    out = dot(mid_ref[...], e_ref[...], NT)
    out_ref[...] = out
    write_stats(stat_ref, out * mask, out)


def expand_forward(y, par, mask_wide, weight):
    n, wide = y.shape[0], weight.shape[0]
    return staged(
        expand_forward_body,
        (y, par, mask_wide, weight),
        (None, None, None, 0),
        (shaped(n, MID, dtype=bf16), shaped(n, wide), shaped(wide // 64, 128)),
        (None, 1, "stat"),
    )


def first_forward_body(y_ref, par_ref, x_ref, mask_ref, w_ref, first_ref, low_ref, out_ref, stat_ref):
    s = pl.program_id(0)
    mask = mask_ref[:, 0:1]
    first = gelu(normed(y_ref[...], par_ref) + x_ref[...]) * mask
    first_ref[...] = first
    low = first.astype(bf16)
    low_ref[...] = low
    term = dot(low, w_ref[...], NT)

    @pl.when(s == 0)
    def _():
        out_ref[...] = term

    @pl.when(s > 0)
    def _():
        out_ref[...] += term

    @pl.when(s == pl.num_programs(0) - 1)
    def _():
        out = out_ref[...]
        write_stats(stat_ref, out * mask, out)


def first_forward(y, par, x, mask_wide, weight, devices):
    n, wide = y.shape
    return staged(
        first_forward_body,
        (y, par, x, mask_wide, weight),
        (1, 1, 1, None, 1),
        (shaped(n, wide), shaped(n, wide, dtype=bf16), shaped(n, MID), shaped(devices, 8, 128)),
        (1, 1, None, None),
    )


def output_stage_body(y_ref, par_ref, first_ref, cot_ref, mask_ref, out_ref, dt_ref, stat_ref):
    mask = mask_ref[:, 0:1]
    y = y_ref[...]
    pre = normed(y, par_ref) + first_ref[...]
    t = jnp.tanh(GELU_A * (pre + GELU_B * pre * pre * pre))
    out_ref[...] = 0.5 * pre * (1.0 + t) * mask
    slope = 0.5 * (1.0 + t) + 0.5 * pre * (1.0 - t * t) * (GELU_A * (1.0 + 3.0 * GELU_B * pre * pre))
    dt = slope * (cot_ref[...] * mask)
    dt_ref[...] = dt
    write_stats(stat_ref, dt, y * par_ref[2:3, :] + par_ref[3:4, :])


def output_stage(y, par, first, cot, mask_wide):
    n, wide = y.shape
    return staged(
        output_stage_body,
        (y, par, first, cot, mask_wide),
        (1, 1, 1, 1, None),
        (shaped(n, wide), shaped(n, wide), shaped(wide // 64, 128)),
        (1, 1, "stat"),
    )


def expand_backward_body(
    dt_ref, y_ref, par_ref, back_ref, mask_ref, e_ref, mid_y_ref, mid_par_ref,
    dy_ref, mid_dt_ref, stat_ref, acc_ref
):
    s = pl.program_id(0)
    mask = mask_ref[:, 0:1]
    dy = norm_gradient(dt_ref[...], y_ref[...], par_ref, back_ref, mask).astype(bf16)
    dy_ref[...] = dy
    term = dot(dy, e_ref[...])

    @pl.when(s == 0)
    def _():
        acc_ref[...] = term

    @pl.when(s > 0)
    def _():
        acc_ref[...] += term

    @pl.when(s == pl.num_programs(0) - 1)
    def _():
        y = mid_y_ref[...]
        dt = gelu_slope(normed(y, mid_par_ref)) * (acc_ref[...] * mask)
        mid_dt_ref[...] = dt
        write_stats(stat_ref, dt, y * mid_par_ref[2:3, :] + mid_par_ref[3:4, :])


def expand_backward(dt, y, par, back, mask_wide, weight, mid_y, mid_par, devices, after=()):
    n, wide = y.shape
    return staged(
        expand_backward_body,
        (dt, y, par, back, mask_wide, weight, mid_y, mid_par),
        (1, 1, 1, 1, None, 0, None, None),
        (shaped(n, wide, dtype=bf16), shaped(n, MID), shaped(devices, 8, 128)),
        (1, None, None),
        [VMEM((n, MID), f32)],
        after,
    )


def residual_backward_body(
    dt_ref, y_ref, par_ref, back_ref, mask_ref, w_ref, add_ref, wide_y_ref, wide_par_ref, x_ref,
    dy_ref, out_ref, stat_ref
):
    mask = mask_ref[:, 0:1]

    @pl.when(pl.program_id(0) == 0)
    def _():
        dy_ref[...] = norm_gradient(dt_ref[...], y_ref[...], par_ref, back_ref, mask).astype(bf16)

    grad = add_ref[...] + dot(dy_ref[...], w_ref[...])
    y = wide_y_ref[...]
    dt = gelu_slope(normed(y, wide_par_ref) + x_ref[...]) * (grad * mask)
    out_ref[...] = dt
    write_stats(stat_ref, dt, y * wide_par_ref[2:3, :] + wide_par_ref[3:4, :])


def residual_backward(dt, y, par, back, mask_wide, weight, add, wide_y, wide_par, x):
    n, wide = x.shape
    return staged(
        residual_backward_body,
        (dt, y, par, back, mask_wide, weight, add, wide_y, wide_par, x),
        (None, None, None, None, None, 1, 1, 1, 1, 1),
        (shaped(n, MID, dtype=bf16), shaped(n, wide), shaped(wide // 64, 128)),
        (None, 1, "stat"),
    )


def input_backward_body(dy_ref, w_ref, add_ref, out_ref):
    out_ref[...] = add_ref[...] + dot(dy_ref[...], w_ref[...])


def input_backward(dy, weight, add):
    n, wide = add.shape
    return staged(
        input_backward_body,
        (dy, weight, add),
        (None, 1, 1),
        (shaped(n, wide),),
        (1,),
    )[0]


def shift_lanes(values, by, width):
    place = lax.broadcasted_iota(jnp.int32, values.shape, values.ndim - 1) % width
    moved = pltpu.roll(values, by % values.shape[-1], values.ndim - 1)
    return jnp.where((place >= by) & (place < width + by), moved, 0.0)


def shift_rows(values, by, width):
    place = lax.broadcasted_iota(jnp.int32, values.shape, 0) % width
    moved = pltpu.roll(values, by % values.shape[0], 0)
    return jnp.where((place >= by) & (place < width + by), moved, 0.0)


def offset_fraction(ext_ref, ow_ref, b, base, pixels, width):
    u = None
    for i in range(3):
        start = (base + 2 * i) * width
        term = dot(ow_ref[i], ext_ref[b, start : start + pixels, :], NT)
        u = term if u is None else u + term
    total = u[32:64]
    total = total + shift_lanes(u[0:32], 2, width) + shift_lanes(u[64:96], -2, width)
    return 1.0 / (1.0 + jnp.exp(-total))


def join_tiles(tiles, ext_ref, pixels):
    for t, ref in enumerate(tiles):
        ext_ref[:, t * pixels : (t + 1) * pixels, :] = ref[...]


def deform_forward_body(
    t0_ref, t1_ref, t2_ref, t3_ref, t4_ref, ow_ref, disp_ref, m_ref, mask_ref,
    cols_ref, y_ref, frac_ref, stat_ref,
    ext_ref, par_ref, s_ref, *, batch, rows, width, deep
):
    pixels = rows * width
    join_tiles((t0_ref, t1_ref, t2_ref, t3_ref, t4_ref), ext_ref, pixels)
    lane = lax.broadcasted_iota(jnp.int32, (32, 128), 1)
    column = lane % width
    upper = lane // width

    def image(b, carry):
        frac = offset_fraction(ext_ref, ow_ref, b, deep - 2, pixels, width)
        for i in range(4):
            frac_ref[b, i] = frac[i * 8 : i * 8 + 8]
        pix = lax.broadcasted_iota(jnp.int32, (1, pixels), 1)
        row_at, col_at = pix // width, pix % width
        tops, lefts, ys, xs = [], [], [], []
        for k in range(9):
            i, j = k // 3, k % 3
            tops.append(row_at + disp_ref[b, i, 2 * j : 2 * j + 1, :] + (deep - 2))
            lefts.append(col_at + 2 * (j - 1) + disp_ref[b, i, 2 * j + 1 : 2 * j + 2, :])
            at = i * 8 + 2 * j
            ys.append(frac[at : at + 1])
            xs.append(frac[at + 1 : at + 2])
        blank = jnp.zeros((23, pixels), f32)
        par = jnp.concatenate(
            [jnp.concatenate(g, axis=0).astype(f32) if g is not None else blank
             for g in (tops, None, lefts, None, ys, None, xs, None)], axis=0)
        par_ref[...] = par.T

        def row_of_taps(i, carry):
            for j in range(3):
                k = i * 3 + j
                for c in range(pixels // 32):
                    p = pltpu.roll(par_ref[c * 32 : c * 32 + 32, :], 128 - k, 1)
                    wide = (32, 128)
                    top = jnp.broadcast_to(p[:, 0:1], wide).astype(jnp.int32) - upper
                    left = jnp.broadcast_to(p[:, 32:33], wide).astype(jnp.int32)
                    fy = jnp.broadcast_to(p[:, 64:65], wide)
                    fx = jnp.broadcast_to(p[:, 96:97], wide)
                    cw = jnp.where(column == left, 1.0 - fx, jnp.where(column == left + 1, fx, 0.0))
                    ca, cb = (1.0 - fy) * cw, fy * cw
                    for q in range(8):
                        s = jnp.where(top == 2 * q, ca, jnp.where(top == 2 * q - 1, cb, 0.0))
                        s_ref[j * pixels + c * 32 : j * pixels + c * 32 + 32, q * 128 : q * 128 + 128] = s.astype(bf16)
            start = pl.multiple_of(i * 2 * width, 128)
            window = ext_ref[b, pl.ds(start, 16 * width), :]
            for j in range(3):
                got = dot(s_ref[j * pixels : (j + 1) * pixels, :], window).astype(bf16)
                cols_ref[pl.ds(pl.multiple_of(b * pixels, pixels), pixels), pl.ds(pl.multiple_of((i * 3 + j) * MID, MID), MID)] = got
            return carry

        return lax.fori_loop(0, 3, row_of_taps, carry)

    lax.fori_loop(0, batch, image, 0)
    y = dot(cols_ref[...], m_ref[...], NT)
    y_ref[...] = y
    write_stats(stat_ref, y * mask_ref[:, 0:1], y)


def write_stats(stat_ref, weighted, values):
    n = weighted.shape[1] // 128
    sums = (
        jnp.sum(weighted, axis=0, keepdims=True),
        jnp.sum(weighted * values, axis=0, keepdims=True),
    )
    block = jnp.concatenate([v[:, c * 128 : c * 128 + 128] for v in sums for c in range(n)], axis=0)
    stat_ref[...] = jnp.broadcast_to(block[None], stat_ref.shape) if len(stat_ref.shape) == 3 else block


def deform_forward(tiles, offset_rows, disp, weight, mask_wide, rows, width, devices):
    batch = tiles[0].shape[0]
    pixels = rows * width
    n = batch * pixels
    return call(
        functools.partial(deform_forward_body, batch=batch, rows=rows, width=width, deep=2 * rows),
        (*tiles, offset_rows, disp, weight, mask_wide),
        (
            jax.ShapeDtypeStruct((n, 9 * MID), bf16),
            jax.ShapeDtypeStruct((n, MID), f32),
            jax.ShapeDtypeStruct((batch, 4, 8, pixels), f32),
            jax.ShapeDtypeStruct((devices, 8, 128), f32),
        ),
        [
            VMEM((batch, 5 * pixels, MID), bf16),
            VMEM((pixels, 128), f32),
            VMEM((3 * pixels, 16 * width), bf16),
        ],
    )


def deform_backward_body(
    t0_ref, t1_ref, t2_ref, t3_ref, t4_ref, ow_ref, disp_ref, frac_ref, m_ref, dy_ref,
    far_up_ref, up_ref, own_ref, down_ref, far_down_ref, dow_ref,
    ext_ref, dext_ref, dc_ref, g_ref, st_ref, df_ref, *, batch, rows, width, deep
):
    pixels = rows * width
    join_tiles((t0_ref, t1_ref, t2_ref, t3_ref, t4_ref), ext_ref, pixels)
    window = 16 * width
    dow_ref[...] = jnp.zeros_like(dow_ref)
    dext_ref[...] = jnp.zeros_like(dext_ref)

    def image(b, carry):
        at = pl.multiple_of(b * pixels, pixels)

        def row_of_taps(i, carry):
            dy = dy_ref[pl.ds(at, pixels), :]
            for j in range(3):
                m = m_ref[:, pl.ds(pl.multiple_of((i * 3 + j) * MID, MID), MID)]
                dc_ref[j * pixels : (j + 1) * pixels, :] = dot(dy, m).astype(bf16)
            start = pl.multiple_of(i * 2 * width, 128)
            g_ref[...] = dot(ext_ref[b, pl.ds(start, window), :], dc_ref[...], NT)
            place = lax.broadcasted_iota(jnp.int32, (width, 128), 0)
            for j in range(3):
                for h in range(pixels // 128):
                    lanes = slice(h * 128, h * 128 + 128)
                    at_l = slice(j * pixels + h * 128, j * pixels + h * 128 + 128)
                    pix = lax.broadcasted_iota(jnp.int32, (1, 128), 1) + h * 128
                    by_y, by_x = slice(2 * j, 2 * j + 1), slice(2 * j + 1, 2 * j + 2)
                    top = pix // width + disp_ref[b, i, by_y, lanes] + (deep - 2)
                    left = pix % width + 2 * (j - 1) + disp_ref[b, i, by_x, lanes]
                    fy = frac_ref[b, i, by_y, lanes]
                    fx = frac_ref[b, i, by_x, lanes]
                    here, after = place == left, place == left + 1
                    cw = jnp.where(here, 1.0 - fx, jnp.where(after, fx, 0.0))
                    ca, cb = (1.0 - fy) * cw, fy * cw
                    low_sum = jnp.zeros((width, 128), f32)
                    high_sum = jnp.zeros((width, 128), f32)
                    for r in range(16):
                        part = slice(r * width, r * width + width)
                        g = g_ref[part, at_l]
                        m0, m1 = top == r, top == r - 1
                        low_sum = low_sum + jnp.where(m0, g, 0.0)
                        high_sum = high_sum + jnp.where(m1, g, 0.0)
                        st_ref[part, at_l] = jnp.where(m0, ca, jnp.where(m1, cb, 0.0)).astype(bf16)
                    d_fy = jnp.sum((high_sum - low_sum) * cw, axis=0, keepdims=True)
                    mixed = (1.0 - fy) * low_sum + fy * high_sum
                    d_fx = jnp.sum(
                        jnp.where(after, mixed, 0.0) - jnp.where(here, mixed, 0.0), axis=0, keepdims=True)
                    df_ref[i, by_y, lanes] = d_fy * fy * (1.0 - fy)
                    df_ref[i, by_x, lanes] = d_fx * fx * (1.0 - fx)
            dext_ref[b, pl.ds(start, window), :] += dot(st_ref[...], dc_ref[...])
            return carry

        df_ref[...] = jnp.zeros_like(df_ref)
        carry = lax.fori_loop(0, 3, row_of_taps, carry)
        d_off = df_ref[...].reshape(32, pixels).astype(bf16).astype(f32)
        stacked = jnp.concatenate(
            [shift_lanes(d_off, -2, width), d_off, shift_lanes(d_off, 2, width)], axis=0)
        across = jnp.concatenate([stacked, jnp.zeros((32, pixels), f32)], axis=0).T.astype(bf16)
        stacked = stacked.astype(bf16)
        for i in range(3):
            first = (deep - 2 + 2 * i) * width
            part = slice(first, first + pixels)
            dow_ref[i] += dot(stacked, ext_ref[b, part, :])
            dext_ref[b, part, :] += dot(across[:, :96], ow_ref[i])
        tiles = (far_up_ref, up_ref, own_ref, down_ref, far_down_ref)
        for t, ref in enumerate(tiles):
            ref[b] = dext_ref[b, t * pixels : (t + 1) * pixels, :].astype(ref.dtype)
        return carry

    lax.fori_loop(0, batch, image, 0)


def deform_backward(tiles, offset_rows, disp, frac, weight, dy, rows, width, after):
    batch = tiles[0].shape[0]
    pixels = rows * width
    return call(
        functools.partial(deform_backward_body, batch=batch, rows=rows, width=width, deep=2 * rows),
        (*tiles, offset_rows, disp, frac, weight, dy),
        tuple(jax.ShapeDtypeStruct((batch, pixels, MID), f32 if t == 2 else bf16) for t in range(5))
        + (jax.ShapeDtypeStruct((3, 96, MID), f32),),
        [
            VMEM((batch, 5 * pixels, MID), bf16),
            VMEM((batch, 5 * pixels, MID), f32),
            VMEM((3 * pixels, MID), bf16),
            VMEM((16 * width, 3 * pixels), f32),
            VMEM((16 * width, 3 * pixels), bf16),
            VMEM((4, 8, pixels), f32),
        ],
        after,
    )


def conv_forward_body(rim_ref, m_ref, mask_ref, y_ref, stat_ref, *, batch, rows, width):
    pixels = rows * width
    for b in range(batch):
        total = None
        for j in range(3):
            u = None
            for i in range(3):
                k = i * 3 + j
                start = 2 * i * width
                term = dot(rim_ref[b, start : start + pixels, :], m_ref[:, k * MID : (k + 1) * MID], NT)
                u = term if u is None else u + term
            u = shift_rows(u, -2 * (j - 1), width) if j != 1 else u
            total = u if total is None else total + u
        y_ref[b * pixels : (b + 1) * pixels, :] = total
    y = y_ref[...]
    write_stats(stat_ref, y * mask_ref[:, 0:1], y)


def conv_forward(rim, weight, mask_wide, rows, width, devices):
    batch = rim.shape[0]
    n = batch * rows * width
    return call(
        functools.partial(conv_forward_body, batch=batch, rows=rows, width=width),
        (rim, weight, mask_wide),
        (jax.ShapeDtypeStruct((n, MID), f32), jax.ShapeDtypeStruct((devices, 8, 128), f32)),
    )


def conv_backward_body(
    rim_ref, m_ref, y_ref, par_ref, mask_ref, dt_ref, stat_ref, *, batch, rows, width
):
    pixels = rows * width
    for b in range(batch):
        total = None
        for j in range(3):
            u = None
            for i in range(3):
                k = i * 3 + j
                start = (4 - 2 * i) * width
                term = dot(rim_ref[b, start : start + pixels, :], m_ref[:, k * MID : (k + 1) * MID])
                u = term if u is None else u + term
            u = shift_rows(u, 2 * (j - 1), width) if j != 1 else u
            total = u if total is None else total + u
        dt_ref[b * pixels : (b + 1) * pixels, :] = total
    y = y_ref[...]
    dt = gelu_slope(normed(y, par_ref)) * (dt_ref[...] * mask_ref[:, 0:1])
    dt_ref[...] = dt
    write_stats(stat_ref, dt, y * par_ref[2:3, :] + par_ref[3:4, :])


def conv_backward(rim, weight, y, par, mask_wide, rows, width, devices, after):
    batch = rim.shape[0]
    n = batch * rows * width
    return call(
        functools.partial(conv_backward_body, batch=batch, rows=rows, width=width),
        (rim, weight, y, par, mask_wide),
        (jax.ShapeDtypeStruct((n, MID), f32), jax.ShapeDtypeStruct((devices, 8, 128), f32)),
        after=after,
    )


def conv_weight_body(dy_ref, rim_ref, out_ref, dyt_ref, *, batch, rows, width):
    pixels = rows * width
    n = batch * pixels
    dy = dy_ref[...].astype(f32)
    for j in range(3):
        moved = shift_rows(dy, 2 * (j - 1), width) if j != 1 else dy
        dyt_ref[j] = moved.T.astype(bf16)
    for j in range(3):
        for i in range(3):
            k = i * 3 + j
            start = 2 * i * width
            total = None
            for b in range(batch):
                term = dot(dyt_ref[j, :, b * pixels : (b + 1) * pixels], rim_ref[b, start : start + pixels, :])
                total = term if total is None else total + term
            out_ref[:, k * MID : (k + 1) * MID] = total.astype(bf16)


def conv_weight_gradient(dy, rim, rows, width, after):
    batch = rim.shape[0]
    return call(
        functools.partial(conv_weight_body, batch=batch, rows=rows, width=width),
        (dy, rim),
        jax.ShapeDtypeStruct((MID, 9 * MID), bf16),
        [VMEM((3, MID, batch * rows * width), bf16)],
        after,
    )


def columns_weight_body(dy_ref, cols_ref, out_ref, dyt_ref):
    dyt_ref[...] = dy_ref[...].astype(f32).T.astype(bf16)
    for k in range(9):
        part = slice(k * MID, (k + 1) * MID)
        out_ref[:, part] = dot(dyt_ref[...], cols_ref[:, part]).astype(bf16)


def columns_weight_gradient(dy, cols):
    return call(
        columns_weight_body,
        (dy, cols),
        jax.ShapeDtypeStruct((MID, 9 * MID), bf16),
        [VMEM((MID, dy.shape[0]), bf16)],
    )


TILES = 2
EPSILON = 1e-05


def swap_with(values, axis, step):
    return lax.ppermute(values, axis, [(i, i ^ step) for i in range(lax.axis_size(axis))])


def from_behind(block, axis, distance):
    devices = range(lax.axis_size(axis))
    route = [(i - distance, i) for i in devices if i - distance in devices]
    return lax.ppermute(block, axis, route)


def ladder_sum(values, axis):
    step = 1
    while step < lax.axis_size(axis):
        got = swap_with(values.astype(bf16), axis, step)
        values = values + got.astype(f32)
        step *= 2
    return values


def to_everyone(spread, groups=None):
    return lax.all_to_all(spread, ("rows", "ch"), 0, 0, axis_index_groups=groups, tiled=True)


def small_total(spread):
    return jnp.sum(to_everyone(spread), axis=0).reshape(2, -1)


def wide_total(block):
    devices = lax.axis_size("rows") * lax.axis_size("ch")
    core = lax.axis_index("ch") % 2
    above, below = block.reshape(2, -1, 128)
    half = jnp.where(core == 0, above, below) + swap_with(jnp.where(core == 0, below, above), "ch", 1)
    groups = [[i * 2 + k for i in range(devices // 2)] for k in range(2)]
    half = jnp.broadcast_to(half[None], (devices // 2,) + half.shape)
    half = jnp.sum(to_everyone(half, groups), axis=0)
    other = swap_with(half, "ch", 1)
    whole = jnp.stack([jnp.where(core == 0, half, other), jnp.where(core == 0, other, half)])
    whole = whole.reshape(-1, 2, STEP)
    return whole[:, 0].reshape(-1), whole[:, 1].reshape(-1)


def sums_spread(first, second, devices):
    block = jnp.concatenate([jnp.sum(first, axis=0), jnp.sum(second, axis=0)]).reshape(-1, 128)
    return jnp.broadcast_to(block[None], (devices,) + block.shape)


def forward_rows(sums, gain, shift, count):
    mean = sums[0] / count
    scale = lax.rsqrt(sums[1] / count - mean * mean + EPSILON)
    return jnp.stack([scale * gain, shift - mean * scale * gain, scale, -mean * scale])


def backward_rows(sums, par, count):
    rows = jnp.stack([par[0], par[0] * sums[0] / count, par[0] * sums[1] / count])
    return rows, own_slice(sums[1]), own_slice(sums[0])


def own_slice(full):
    size = full.shape[0] // lax.axis_size("ch")
    return lax.dynamic_slice_in_dim(full, lax.axis_index("ch") * size, size)


def gather_weight(weight):
    return lax.all_gather(weight.astype(bf16), "ch", axis=0, tiled=True)


def gather_by_swaps(weight):
    ch = lax.axis_size("ch")
    held = weight.astype(bf16)[None]
    step = ch // 2
    while step >= 1:
        got = swap_with(held, "ch", step)
        odd = lax.axis_index("ch") // step % 2 == 1
        held = jnp.stack([jnp.where(odd, got, held), jnp.where(odd, held, got)], axis=1)
        held = held.reshape((-1,) + held.shape[2:])
        step //= 2
    return held.reshape((-1,) + weight.shape[1:])


def pick(values, bit):
    return lax.dynamic_index_in_dim(values, bit, 1, keepdims=False)


def halve(values, axis, step):
    bit = lax.axis_index(axis) // step % 2
    pairs = values.reshape((values.shape[0] // 2, 2) + values.shape[1:])
    got = swap_with(pick(pairs, 1 - bit), axis, step)
    return (pick(pairs, bit).astype(f32) + got.astype(f32)).astype(bf16)


def scatter_ch(gradient):
    return lax.psum_scatter(gradient, "ch", scatter_dimension=0, tiled=True)


def halve_ch(gradient):
    ch = lax.axis_size("ch")
    total = gradient.reshape((ch, gradient.shape[0] // ch) + gradient.shape[1:])
    step = 1
    while step < ch:
        total = halve(total, "ch", step)
        step *= 2
    return total[0]


def blocks_to_lanes(values, base):
    return jnp.concatenate([values[r : r + base] for r in range(0, values.shape[0], base)], axis=1)


def lanes_to_blocks(values, wide):
    return jnp.concatenate(
        [values[:, c : c + wide] for c in range(0, values.shape[1], wide)], axis=0
    )


def rows_scatter(parts):
    rows = lax.axis_size("rows")
    total = jnp.concatenate(parts, axis=1)
    base, wide = total.shape
    total = lax.all_to_all(total.reshape(rows, base // rows, wide), "rows", 0, 0, tiled=True)
    return jnp.sum(total.astype(f32), axis=0).astype(bf16)


def rows_gather(share, widths):
    rows = lax.axis_size("rows")
    total = jnp.broadcast_to(share[None], (rows,) + share.shape)
    total = lax.all_to_all(total, "rows", 0, 0, tiled=True)
    total = total.reshape(-1, share.shape[1]).astype(f32)
    ends, at = [], 0
    for width in widths:
        ends.append(total[:, at : at + width])
        at += width
    return ends


def deep_rows(tile):
    odd = lax.axis_index("rows") % 2 == 1
    far_up = from_behind(tile, "rows", 2)
    far_down = from_behind(tile, "rows", -2)
    partner = swap_with(tile, "rows", 1)
    passed = swap_with(jnp.where(odd, far_up, far_down), "rows", 1)
    up = jnp.where(odd, partner, passed)
    down = jnp.where(odd, passed, partner)
    return far_up, up, tile, down, far_down


def deep_return(tiles):
    far_up, up, own, down, far_down = tiles
    odd = lax.axis_index("rows") % 2 == 1
    passed = swap_with(jnp.where(odd, down, up), "rows", 1)
    partner = swap_with(jnp.where(odd, up, down), "rows", 1)
    added = (jnp.where(odd, far_up, far_down).astype(f32) + passed.astype(f32)).astype(bf16)
    own = own + partner.astype(f32)
    own = own + from_behind(jnp.where(odd, added, far_up), "rows", -2).astype(f32)
    return own + from_behind(jnp.where(odd, far_down, added), "rows", 2).astype(f32)


def near_rows(tile, width):
    size = 2 * width
    above = from_behind(tile[:, -size:], "rows", 1)
    below = from_behind(tile[:, :size], "rows", -1)
    return jnp.concatenate([above, tile, below], axis=1)


def per_device(
    inputs,
    heights,
    displacements,
    reduce_one,
    reduce_gain_one,
    reduce_bias_one,
    offset_weight,
    deform_weight,
    deform_gain,
    deform_bias,
    expand_one,
    expand_gain_one,
    expand_bias_one,
    reduce_two,
    reduce_gain_two,
    reduce_bias_two,
    conv_weight,
    conv_gain,
    conv_bias,
    expand_two,
    expand_gain_two,
    expand_bias_two,
    cotangent,
):
    batch, rows, width, channels = inputs.shape
    pixels = rows * width
    n = batch * pixels
    own_heights = lax.dynamic_slice_in_dim(heights, lax.axis_index("ch") * batch, batch)
    rows_here = lax.axis_index("rows") * rows + jnp.arange(rows, dtype=jnp.int32)
    mask = (rows_here[None, :] < own_heights[:, None]).astype(f32)
    mask = jnp.broadcast_to(mask[:, :, None], (batch, rows, width)).reshape(n, 1)
    mask_wide = jnp.broadcast_to(mask, (n, 128))
    count = jnp.sum(heights).astype(f32) * width

    offset_rows = offset_weight.astype(bf16).reshape(3, 6, 3, 3, MID).transpose(2, 3, 0, 1, 4)
    offset_rows = jnp.pad(offset_rows, ((0, 0), (0, 0), (0, 1), (0, 2), (0, 0))).reshape(3, 96, MID)
    disp = jnp.pad(displacements.reshape(3, 6, batch, pixels), ((0, 0), (0, 2), (0, 0), (0, 0)))
    disp = disp.transpose(2, 0, 1, 3)

    reduce_full = gather_by_swaps(reduce_one)
    deform_full, expand_full, reduce_full_two, conv_full, expand_full_two = [
        gather_weight(w) for w in (deform_weight, expand_one, reduce_two, conv_weight, expand_two)
    ]

    devices = lax.axis_size("rows") * lax.axis_size("ch")
    acts = inputs.reshape(n, channels)
    acts_low = acts.astype(bf16)
    y_a = dot(acts_low, reduce_full, NT)
    masked = y_a * mask
    par_a = forward_rows(
        small_total(sums_spread(masked, masked * y_a, devices)), reduce_gain_one, reduce_bias_one, count
    )
    hidden = (gelu(y_a * par_a[0] + par_a[1]) * mask).astype(bf16)
    near_tiles = deep_rows(hidden.reshape(batch, pixels, MID))
    columns, y_b, fraction, spread = deform_forward(
        near_tiles, offset_rows, disp, deform_full, mask_wide, rows, width, devices
    )
    par_b = forward_rows(small_total(spread), deform_gain, deform_bias, count)
    middle, y_c, block = expand_forward(y_b, par_b, mask_wide, expand_full)
    par_c = forward_rows(wide_total(block), expand_gain_one, expand_bias_one, count)

    first, first_low, y_d, spread = first_forward(y_c, par_c, acts, mask_wide, reduce_full_two, devices)
    par_d = forward_rows(small_total(spread), reduce_gain_two, reduce_bias_two, count)
    hidden_two = (gelu(y_d * par_d[0] + par_d[1]) * mask).astype(bf16)
    rimmed = near_rows(hidden_two.reshape(batch, pixels, MID), width)
    y_e, spread = conv_forward(rimmed, conv_full, mask_wide, rows, width, devices)
    par_e = forward_rows(small_total(spread), conv_gain, conv_bias, count)
    middle_two, y_f, block = expand_forward(y_e, par_e, mask_wide, expand_full_two)
    par_f = forward_rows(wide_total(block), expand_gain_two, expand_bias_two, count)

    output, dt_f, block = output_stage(y_f, par_f, first, cotangent.reshape(n, channels), mask_wide)
    back_f, expand_gain_two_grad, expand_bias_two_grad = backward_rows(wide_total(block), par_f, count)
    dy_f, dt_e, spread = expand_backward(
        dt_f, y_f, par_f, back_f, mask_wide, expand_full_two, y_e, par_e, devices
    )
    expand_two_local = dot(dy_f, middle_two, TN).astype(bf16)
    expand_two_part = scatter_ch(expand_two_local)
    back_e, conv_gain_grad, conv_bias_grad = backward_rows(small_total(spread), par_e, count)
    dy_e = norm_gradient(dt_e, y_e, par_e, back_e, mask).astype(bf16)
    dy_e_rim = near_rows(dy_e.reshape(batch, pixels, MID), width)
    conv_local = conv_weight_gradient(dy_e, rimmed, rows, width, (expand_two_local,))
    conv_part = scatter_ch(conv_local)
    dt_d, spread = conv_backward(
        dy_e_rim, conv_full, y_d, par_d, mask_wide, rows, width, devices, (conv_local,)
    )
    base = conv_part.shape[0]
    conv_weight_grad, expand_two_grad = lax.psum(
        (conv_part, blocks_to_lanes(expand_two_part, base)), "rows"
    )
    conv_weight_grad = conv_weight_grad.astype(f32)
    expand_two_grad = lanes_to_blocks(expand_two_grad, MID).astype(f32)
    back_d, reduce_gain_two_grad, reduce_bias_two_grad = backward_rows(small_total(spread), par_d, count)
    dy_d, dt_c, block = residual_backward(
        dt_d, y_d, par_d, back_d, mask_wide, reduce_full_two, dt_f, y_c, par_c, acts
    )
    reduce_two_local = dot(dy_d, first_low, TN).astype(bf16)
    reduce_two_part = halve_ch(reduce_two_local)

    back_c, expand_gain_one_grad, expand_bias_one_grad = backward_rows(wide_total(block), par_c, count)
    dy_c, dt_b, spread = expand_backward(
        dt_c, y_c, par_c, back_c, mask_wide, expand_full, y_b, par_b, devices, (reduce_two_local,)
    )
    expand_one_local = dot(dy_c, middle, TN).astype(bf16)
    expand_one_part = halve_ch(expand_one_local)
    back_b, deform_gain_grad, deform_bias_grad = backward_rows(small_total(spread), par_b, count)
    dy_b = norm_gradient(dt_b, y_b, par_b, back_b, mask).astype(bf16)
    deform_local = columns_weight_gradient(dy_b, columns)
    deform_part = halve_ch(deform_local)
    *tiles, offset_local = deform_backward(
        near_tiles, offset_rows, disp, fraction, deform_full, dy_b, rows, width,
        (deform_local, expand_one_local, reduce_two_part),
    )
    share = rows_scatter([reduce_two_part, blocks_to_lanes(expand_one_part, base)])
    reduce_two_grad, expand_one_grad = rows_gather(share, (channels, channels))
    expand_one_grad = lanes_to_blocks(expand_one_grad, MID)
    hidden_grad = deep_return(tiles).reshape(n, MID)
    dt_a = gelu_slope(y_a * par_a[0] + par_a[1]) * (hidden_grad * mask)
    sums = small_total(sums_spread(dt_a, dt_a * (y_a * par_a[2] + par_a[3]), devices))
    back_a, reduce_gain_one_grad, reduce_bias_one_grad = backward_rows(sums, par_a, count)
    dy_a = norm_gradient(dt_a, y_a, par_a, back_a, mask).astype(bf16)
    (deform_weight_grad,) = rows_gather(rows_scatter([deform_part]), (9 * MID,))
    offset_part = ladder_sum(offset_local.reshape(-1, MID), "ch").astype(bf16)
    offset_part = jnp.pad(offset_part, ((0, -offset_part.shape[0] % base), (0, 0)))
    offset_part = blocks_to_lanes(offset_part, base)
    reduce_one_part = halve_ch(dot(dy_a, acts_low, TN).astype(bf16))
    reduce_one_grad, offset_grad = rows_gather(
        rows_scatter([reduce_one_part, offset_part]), (channels, offset_part.shape[1])
    )
    offset_grad = lanes_to_blocks(offset_grad, MID)[:288].reshape(3, 3, 4, 8, MID)[:, :, :3, :6]
    offset_weight_grad = offset_grad.transpose(2, 3, 0, 1, 4).reshape(18, 9 * MID)
    input_grad = input_backward(dy_a, reduce_full, dt_c)
    return (
        output.reshape(inputs.shape),
        input_grad.reshape(inputs.shape),
        reduce_one_grad,
        reduce_gain_one_grad,
        reduce_bias_one_grad,
        offset_weight_grad,
        deform_weight_grad,
        deform_gain_grad,
        deform_bias_grad,
        expand_one_grad,
        expand_gain_one_grad,
        expand_bias_one_grad,
        reduce_two_grad,
        reduce_gain_two_grad,
        reduce_bias_two_grad,
        conv_weight_grad,
        conv_gain_grad,
        conv_bias_grad,
        expand_two_grad,
        expand_gain_two_grad,
        expand_bias_two_grad,
    )


def solution(mesh):
    tiles = P("ch", "rows", None, None)
    owned = P("ch", None)
    block = (owned, P(), P())
    placed = (tiles, P(), P(None, "ch", "rows", None)) + block + (P(),) + 2 * block + 3 * block + (tiles,)
    grads = (owned, P("ch"), P("ch"))
    return jax.shard_map(
        per_device,
        mesh=mesh,
        in_specs=placed,
        out_specs=(tiles, tiles) + grads + (P(),) + 2 * grads + 3 * grads,
        check_vma=False,
    )
```

```python
import functools
import jax
import jax.numpy as jnp
from jax import lax
from jax.experimental import pallas as pl
from jax.experimental.pallas import tpu as pltpu
from jax.sharding import PartitionSpec as P

bf16 = jnp.bfloat16
f32 = jnp.float32
VMEM = pltpu.VMEM
MID = 512
NT = (((1,), (1,)), ((), ()))
TN = (((0,), (0,)), ((), ()))
NN = (((1,), (0,)), ((), ()))


def dot(a, b, dims=NN):
    return lax.dot_general(a, b, dims, preferred_element_type=f32)


def without(body, n_in, n_after, n_out, n_through):
    first = n_in + n_after + n_through
    return lambda *refs: body(
        *refs[:n_in], *refs[first : first + n_out], *refs[first + n_out + n_through :]
    )


def ordered(body, operands, in_specs, outs, out_specs, after, through, **options):
    anywhere = pl.BlockSpec(memory_space=pl.ANY)
    n_in, n_out = len(operands), len(outs)
    results = pl.pallas_call(
        without(body, n_in, len(after), n_out, len(through)),
        in_specs=list(in_specs) + [anywhere] * (len(after) + len(through)),
        out_specs=tuple(out_specs) + (anywhere,) * len(through),
        out_shape=tuple(outs) + tuple(jax.ShapeDtypeStruct(v.shape, v.dtype) for v in through),
        input_output_aliases={n_in + len(after) + t: n_out + t for t in range(len(through))},
        **options,
    )(*operands, *after, *through)
    return results


def cost(us):
    return pl.CostEstimate(flops=int(us * 1.1e9), bytes_accessed=int(us * 2.2e6), transcendentals=0)


def call(body, operands, outs, us, limit, scratch=(), after=(), through=()):
    whole = pl.BlockSpec(memory_space=VMEM)
    return ordered(
        body,
        operands,
        [whole] * len(operands),
        outs,
        [whole] * len(outs),
        after,
        through,
        scratch_shapes=list(scratch),
        compiler_params=pltpu.CompilerParams(vmem_limit_bytes=limit * 2**20),
        cost_estimate=cost(us),
    )


GELU_A = 0.7978845608028654
GELU_B = 0.044715
STEP = 512


def gelu(v):
    return 0.5 * v * (1.0 + jnp.tanh(GELU_A * (v + GELU_B * v * v * v)))


def gelu_slope(v):
    t = jnp.tanh(GELU_A * (v + GELU_B * v * v * v))
    return 0.5 * (1.0 + t) + 0.5 * v * (1.0 - t * t) * (GELU_A * (1.0 + 3.0 * GELU_B * v * v))


def staged(body, operands, tiled, outs, out_tiled, us, scratch=(), after=(), through=()):
    def spec(shape, dim):
        if dim is None:
            return pl.BlockSpec(shape, lambda s: (0,) * len(shape))
        block = tuple(STEP if d == dim else size for d, size in enumerate(shape))
        if dim == "stat":
            return pl.BlockSpec((8, 128), lambda s: (s, 0))
        return pl.BlockSpec(block, lambda s: tuple(s if d == dim else 0 for d in range(len(shape))))

    steps = [a.shape[d] // STEP for a, d in zip(operands, tiled) if d is not None][0]
    return ordered(
        body,
        operands,
        [spec(a.shape, d) for a, d in zip(operands, tiled)],
        outs,
        [spec(o.shape, d) for o, d in zip(outs, out_tiled)],
        after,
        through,
        grid=(steps,),
        scratch_shapes=list(scratch),
        compiler_params=pltpu.CompilerParams(vmem_limit_bytes=24 * 2**20),
        cost_estimate=cost(us),
    )


def shaped(*shape, dtype=f32):
    return jax.ShapeDtypeStruct(shape, dtype)


def normed(values, par_ref):
    return values * par_ref[0:1, :] + par_ref[1:2, :]


def norm_gradient(upstream, values, par_ref, back_ref, mask):
    normal = values * par_ref[2:3, :] + par_ref[3:4, :]
    return upstream * back_ref[0:1, :] - mask * (back_ref[1:2, :] + normal * back_ref[2:3, :])


def product_forward_body(x_ref, mask_ref, w_ref, low_ref, out_ref, stat_ref):
    s = pl.program_id(0)
    low = x_ref[...].astype(bf16)
    low_ref[...] = low
    term = dot(low, w_ref[...], NT)

    @pl.when(s == 0)
    def _():
        out_ref[...] = term

    @pl.when(s > 0)
    def _():
        out_ref[...] += term

    @pl.when(s == pl.num_programs(0) - 1)
    def _():
        out = out_ref[...]
        write_stats(stat_ref, out * mask_ref[:, 0:1], out)


def product_forward(x, mask_wide, weight, devices):
    n, wide = x.shape
    return staged(
        product_forward_body,
        (x, mask_wide, weight),
        (1, None, 1),
        (shaped(n, wide, dtype=bf16), shaped(n, MID), shaped(devices, 8, 128)),
        (1, None, None),
        5,
    )


def expand_forward_body(y_ref, par_ref, mask_ref, e_ref, mid_ref, out_ref, stat_ref):
    mask = mask_ref[:, 0:1]

    @pl.when(pl.program_id(0) == 0)
    def _():
        mid_ref[...] = (gelu(normed(y_ref[...], par_ref)) * mask).astype(bf16)

    out = dot(mid_ref[...], e_ref[...], NT)
    out_ref[...] = out
    write_stats(stat_ref, out * mask, out)


def expand_forward(y, par, mask_wide, weight):
    n, wide = y.shape[0], weight.shape[0]
    return staged(
        expand_forward_body,
        (y, par, mask_wide, weight),
        (None, None, None, 0),
        (shaped(n, MID, dtype=bf16), shaped(n, wide), shaped(wide // 64, 128)),
        (None, 1, "stat"),
        5,
    )


def first_forward_body(y_ref, par_ref, x_ref, mask_ref, w_ref, first_ref, low_ref, out_ref, stat_ref):
    s = pl.program_id(0)
    mask = mask_ref[:, 0:1]
    first = gelu(normed(y_ref[...], par_ref) + x_ref[...]) * mask
    first_ref[...] = first
    low = first.astype(bf16)
    low_ref[...] = low
    term = dot(low, w_ref[...], NT)

    @pl.when(s == 0)
    def _():
        out_ref[...] = term

    @pl.when(s > 0)
    def _():
        out_ref[...] += term

    @pl.when(s == pl.num_programs(0) - 1)
    def _():
        out = out_ref[...]
        write_stats(stat_ref, out * mask, out)


def first_forward(y, par, x, mask_wide, weight, devices):
    n, wide = y.shape
    return staged(
        first_forward_body,
        (y, par, x, mask_wide, weight),
        (1, 1, 1, None, 1),
        (shaped(n, wide), shaped(n, wide, dtype=bf16), shaped(n, MID), shaped(devices, 8, 128)),
        (1, 1, None, None),
        8,
    )


def output_stage_body(y_ref, par_ref, first_ref, cot_ref, mask_ref, out_ref, dt_ref, stat_ref):
    mask = mask_ref[:, 0:1]
    y = y_ref[...]
    pre = normed(y, par_ref) + first_ref[...]
    t = jnp.tanh(GELU_A * (pre + GELU_B * pre * pre * pre))
    out_ref[...] = 0.5 * pre * (1.0 + t) * mask
    slope = 0.5 * (1.0 + t) + 0.5 * pre * (1.0 - t * t) * (GELU_A * (1.0 + 3.0 * GELU_B * pre * pre))
    dt = slope * (cot_ref[...] * mask)
    dt_ref[...] = dt
    write_stats(stat_ref, dt, y * par_ref[2:3, :] + par_ref[3:4, :])


def output_stage(y, par, first, cot, mask_wide):
    n, wide = y.shape
    return staged(
        output_stage_body,
        (y, par, first, cot, mask_wide),
        (1, 1, 1, 1, None),
        (shaped(n, wide), shaped(n, wide), shaped(wide // 64, 128)),
        (1, 1, "stat"),
        10,
    )


def expand_backward_body(
    dt_ref, y_ref, par_ref, back_ref, mask_ref, e_ref, mid_y_ref, mid_par_ref,
    dy_ref, mid_dt_ref, stat_ref, acc_ref
):
    s = pl.program_id(0)
    mask = mask_ref[:, 0:1]
    dy = norm_gradient(dt_ref[...], y_ref[...], par_ref, back_ref, mask).astype(bf16)
    dy_ref[...] = dy
    term = dot(dy, e_ref[...])

    @pl.when(s == 0)
    def _():
        acc_ref[...] = term

    @pl.when(s > 0)
    def _():
        acc_ref[...] += term

    @pl.when(s == pl.num_programs(0) - 1)
    def _():
        y = mid_y_ref[...]
        dt = gelu_slope(normed(y, mid_par_ref)) * (acc_ref[...] * mask)
        mid_dt_ref[...] = dt
        write_stats(stat_ref, dt, y * mid_par_ref[2:3, :] + mid_par_ref[3:4, :])


def expand_backward(dt, y, par, back, mask_wide, weight, mid_y, mid_par, devices, through=()):
    n, wide = y.shape
    return staged(
        expand_backward_body,
        (dt, y, par, back, mask_wide, weight, mid_y, mid_par),
        (1, 1, 1, 1, None, 0, None, None),
        (shaped(n, wide, dtype=bf16), shaped(n, MID), shaped(devices, 8, 128)),
        (1, None, None),
        8,
        [VMEM((n, MID), f32)],
        through=through,
    )


def residual_backward_body(
    dt_ref, y_ref, par_ref, back_ref, mask_ref, w_ref, add_ref, wide_y_ref, wide_par_ref, x_ref,
    dy_ref, out_ref, stat_ref
):
    mask = mask_ref[:, 0:1]

    @pl.when(pl.program_id(0) == 0)
    def _():
        dy_ref[...] = norm_gradient(dt_ref[...], y_ref[...], par_ref, back_ref, mask).astype(bf16)

    grad = add_ref[...] + dot(dy_ref[...], w_ref[...])
    y = wide_y_ref[...]
    dt = gelu_slope(normed(y, wide_par_ref) + x_ref[...]) * (grad * mask)
    out_ref[...] = dt
    write_stats(stat_ref, dt, y * wide_par_ref[2:3, :] + wide_par_ref[3:4, :])


def residual_backward(dt, y, par, back, mask_wide, weight, add, wide_y, wide_par, x):
    n, wide = x.shape
    return staged(
        residual_backward_body,
        (dt, y, par, back, mask_wide, weight, add, wide_y, wide_par, x),
        (None, None, None, None, None, 1, 1, 1, 1, 1),
        (shaped(n, MID, dtype=bf16), shaped(n, wide), shaped(wide // 64, 128)),
        (None, 1, "stat"),
        10,
    )


def input_backward_body(dy_ref, w_ref, add_ref, out_ref):
    out_ref[...] = add_ref[...] + dot(dy_ref[...], w_ref[...])


def input_backward(dy, weight, add, after):
    n, wide = add.shape
    return staged(
        input_backward_body,
        (dy, weight, add),
        (None, 1, 1),
        (shaped(n, wide),),
        (1,),
        6,
        after=after,
    )[0]


def hidden_backward_body(
    own_ref, near_ref, up_ref, down_ref, y_ref, par_ref, mask_ref, dt_ref, stat_ref
):
    grad = own_ref[...] + near_ref[...].astype(f32) + up_ref[...].astype(f32) + down_ref[...].astype(f32)
    y = y_ref[...]
    dt = gelu_slope(normed(y, par_ref)) * (grad * mask_ref[:, 0:1])
    dt_ref[...] = dt
    write_stats(stat_ref, dt, y * par_ref[2:3, :] + par_ref[3:4, :])


def hidden_backward(pieces, y, par, mask_wide, devices, after):
    n = y.shape[0]
    return call(
        hidden_backward_body,
        (*[p.reshape(n, MID) for p in pieces], y, par, mask_wide),
        (shaped(n, MID), shaped(devices, 8, 128)),
        3,
        16,
        after=after,
    )


def cast_body(v_ref, out_ref):
    out_ref[...] = v_ref[...].astype(bf16)


def cast_after(values, *after):
    return call(cast_body, (values,), (shaped(*values.shape, dtype=bf16),), 2, 12, after=after)[0]


def shift_lanes(values, by, width):
    place = lax.broadcasted_iota(jnp.int32, values.shape, values.ndim - 1) % width
    moved = pltpu.roll(values, by % values.shape[-1], values.ndim - 1)
    return jnp.where((place >= by) & (place < width + by), moved, 0.0)


def shift_rows(values, by, width):
    place = lax.broadcasted_iota(jnp.int32, values.shape, 0) % width
    moved = pltpu.roll(values, by % values.shape[0], 0)
    return jnp.where((place >= by) & (place < width + by), moved, 0.0)


def offset_fraction(ext_ref, ow_ref, b, base, pixels, width):
    u = None
    for i in range(3):
        start = (base + 2 * i) * width
        term = dot(ow_ref[i], ext_ref[b, start : start + pixels, :], NT)
        u = term if u is None else u + term
    total = u[32:64]
    total = total + shift_lanes(u[0:32], 2, width) + shift_lanes(u[64:96], -2, width)
    return 1.0 / (1.0 + jnp.exp(-total))


def join_tiles(tiles, ext_ref, pixels):
    for t, ref in enumerate(tiles):
        ext_ref[:, t * pixels : (t + 1) * pixels, :] = ref[...]


def deform_forward_body(
    t0_ref, t1_ref, t2_ref, t3_ref, t4_ref, ow_ref, disp_ref, m_ref, mask_ref,
    cols_ref, y_ref, frac_ref, stat_ref,
    ext_ref, par_ref, s_ref, *, batch, rows, width, deep
):
    pixels = rows * width
    join_tiles((t0_ref, t1_ref, t2_ref, t3_ref, t4_ref), ext_ref, pixels)
    lane = lax.broadcasted_iota(jnp.int32, (32, 128), 1)
    column = lane % width
    upper = lane // width

    def image(b, carry):
        frac = offset_fraction(ext_ref, ow_ref, b, deep - 2, pixels, width)
        for i in range(4):
            frac_ref[b, i] = frac[i * 8 : i * 8 + 8]
        pix = lax.broadcasted_iota(jnp.int32, (1, pixels), 1)
        row_at, col_at = pix // width, pix % width
        tops, lefts, ys, xs = [], [], [], []
        for k in range(9):
            i, j = k // 3, k % 3
            tops.append(row_at + disp_ref[b, i, 2 * j : 2 * j + 1, :] + (deep - 2))
            lefts.append(col_at + 2 * (j - 1) + disp_ref[b, i, 2 * j + 1 : 2 * j + 2, :])
            at = i * 8 + 2 * j
            ys.append(frac[at : at + 1])
            xs.append(frac[at + 1 : at + 2])
        blank = jnp.zeros((23, pixels), f32)
        par = jnp.concatenate(
            [jnp.concatenate(g, axis=0).astype(f32) if g is not None else blank
             for g in (tops, None, lefts, None, ys, None, xs, None)], axis=0)
        par_ref[...] = par.T

        def row_of_taps(i, carry):
            for j in range(3):
                k = i * 3 + j
                for c in range(pixels // 32):
                    p = pltpu.roll(par_ref[c * 32 : c * 32 + 32, :], 128 - k, 1)
                    wide = (32, 128)
                    top = jnp.broadcast_to(p[:, 0:1], wide).astype(jnp.int32) - upper
                    left = jnp.broadcast_to(p[:, 32:33], wide).astype(jnp.int32)
                    fy = jnp.broadcast_to(p[:, 64:65], wide)
                    fx = jnp.broadcast_to(p[:, 96:97], wide)
                    cw = jnp.where(column == left, 1.0 - fx, jnp.where(column == left + 1, fx, 0.0))
                    ca, cb = (1.0 - fy) * cw, fy * cw
                    for q in range(8):
                        s = jnp.where(top == 2 * q, ca, jnp.where(top == 2 * q - 1, cb, 0.0))
                        s_ref[j * pixels + c * 32 : j * pixels + c * 32 + 32, q * 128 : q * 128 + 128] = s.astype(bf16)
            start = pl.multiple_of(i * 2 * width, 128)
            window = ext_ref[b, pl.ds(start, 16 * width), :]
            for j in range(3):
                got = dot(s_ref[j * pixels : (j + 1) * pixels, :], window).astype(bf16)
                cols_ref[pl.ds(pl.multiple_of(b * pixels, pixels), pixels), pl.ds(pl.multiple_of((i * 3 + j) * MID, MID), MID)] = got
            return carry

        return lax.fori_loop(0, 3, row_of_taps, carry)

    lax.fori_loop(0, batch, image, 0)
    y = dot(cols_ref[...], m_ref[...], NT)
    y_ref[...] = y
    write_stats(stat_ref, y * mask_ref[:, 0:1], y)


def write_stats(stat_ref, weighted, values):
    n = weighted.shape[1] // 128
    sums = (
        jnp.sum(weighted, axis=0, keepdims=True),
        jnp.sum(weighted * values, axis=0, keepdims=True),
    )
    block = jnp.concatenate([v[:, c * 128 : c * 128 + 128] for v in sums for c in range(n)], axis=0)
    stat_ref[...] = jnp.broadcast_to(block[None], stat_ref.shape) if len(stat_ref.shape) == 3 else block


def deform_forward(tiles, offset_rows, disp, weight, mask_wide, rows, width, devices):
    batch = tiles[0].shape[0]
    pixels = rows * width
    n = batch * pixels
    return call(
        functools.partial(deform_forward_body, batch=batch, rows=rows, width=width, deep=2 * rows),
        (*tiles, offset_rows, disp, weight, mask_wide),
        (
            jax.ShapeDtypeStruct((n, 9 * MID), bf16),
            jax.ShapeDtypeStruct((n, MID), f32),
            jax.ShapeDtypeStruct((batch, 4, 8, pixels), f32),
            jax.ShapeDtypeStruct((devices, 8, 128), f32),
        ),
        17,
        30,
        [
            VMEM((batch, 5 * pixels, MID), bf16),
            VMEM((pixels, 128), f32),
            VMEM((3 * pixels, 16 * width), bf16),
        ],
    )


def deform_backward_body(
    t0_ref, t1_ref, t2_ref, t3_ref, t4_ref, ow_ref, disp_ref, frac_ref, m_ref, dy_ref,
    far_up_ref, up_ref, own_ref, down_ref, far_down_ref, dow_ref,
    ext_ref, dext_ref, dc_ref, g_ref, st_ref, df_ref, *, batch, rows, width, deep
):
    pixels = rows * width
    join_tiles((t0_ref, t1_ref, t2_ref, t3_ref, t4_ref), ext_ref, pixels)
    window = 16 * width
    dow_ref[...] = jnp.zeros_like(dow_ref)
    dext_ref[...] = jnp.zeros_like(dext_ref)

    def image(b, carry):
        at = pl.multiple_of(b * pixels, pixels)

        def row_of_taps(i, carry):
            dy = dy_ref[pl.ds(at, pixels), :]
            for j in range(3):
                m = m_ref[:, pl.ds(pl.multiple_of((i * 3 + j) * MID, MID), MID)]
                dc_ref[j * pixels : (j + 1) * pixels, :] = dot(dy, m).astype(bf16)
            start = pl.multiple_of(i * 2 * width, 128)
            g_ref[...] = dot(ext_ref[b, pl.ds(start, window), :], dc_ref[...], NT)
            place = lax.broadcasted_iota(jnp.int32, (width, 128), 0)
            for j in range(3):
                for h in range(pixels // 128):
                    lanes = slice(h * 128, h * 128 + 128)
                    at_l = slice(j * pixels + h * 128, j * pixels + h * 128 + 128)
                    pix = lax.broadcasted_iota(jnp.int32, (1, 128), 1) + h * 128
                    by_y, by_x = slice(2 * j, 2 * j + 1), slice(2 * j + 1, 2 * j + 2)
                    top = pix // width + disp_ref[b, i, by_y, lanes] + (deep - 2)
                    left = pix % width + 2 * (j - 1) + disp_ref[b, i, by_x, lanes]
                    fy = frac_ref[b, i, by_y, lanes]
                    fx = frac_ref[b, i, by_x, lanes]
                    here, after = place == left, place == left + 1
                    cw = jnp.where(here, 1.0 - fx, jnp.where(after, fx, 0.0))
                    ca, cb = (1.0 - fy) * cw, fy * cw
                    low_sum = jnp.zeros((width, 128), f32)
                    high_sum = jnp.zeros((width, 128), f32)
                    for r in range(16):
                        part = slice(r * width, r * width + width)
                        g = g_ref[part, at_l]
                        m0, m1 = top == r, top == r - 1
                        low_sum = low_sum + jnp.where(m0, g, 0.0)
                        high_sum = high_sum + jnp.where(m1, g, 0.0)
                        st_ref[part, at_l] = jnp.where(m0, ca, jnp.where(m1, cb, 0.0)).astype(bf16)
                    d_fy = jnp.sum((high_sum - low_sum) * cw, axis=0, keepdims=True)
                    mixed = (1.0 - fy) * low_sum + fy * high_sum
                    d_fx = jnp.sum(
                        jnp.where(after, mixed, 0.0) - jnp.where(here, mixed, 0.0), axis=0, keepdims=True)
                    df_ref[i, by_y, lanes] = d_fy * fy * (1.0 - fy)
                    df_ref[i, by_x, lanes] = d_fx * fx * (1.0 - fx)
            dext_ref[b, pl.ds(start, window), :] += dot(st_ref[...], dc_ref[...])
            return carry

        df_ref[...] = jnp.zeros_like(df_ref)
        carry = lax.fori_loop(0, 3, row_of_taps, carry)
        d_off = df_ref[...].reshape(32, pixels).astype(bf16).astype(f32)
        stacked = jnp.concatenate(
            [shift_lanes(d_off, -2, width), d_off, shift_lanes(d_off, 2, width)], axis=0)
        across = jnp.concatenate([stacked, jnp.zeros((32, pixels), f32)], axis=0).T.astype(bf16)
        stacked = stacked.astype(bf16)
        for i in range(3):
            first = (deep - 2 + 2 * i) * width
            part = slice(first, first + pixels)
            dow_ref[i] += dot(stacked, ext_ref[b, part, :])
            dext_ref[b, part, :] += dot(across[:, :96], ow_ref[i])
        tiles = (far_up_ref, up_ref, own_ref, down_ref, far_down_ref)
        for t, ref in enumerate(tiles):
            ref[b] = dext_ref[b, t * pixels : (t + 1) * pixels, :].astype(ref.dtype)
        return carry

    lax.fori_loop(0, batch, image, 0)


def deform_backward(tiles, offset_rows, disp, frac, weight, dy, rows, width, after, through):
    batch = tiles[0].shape[0]
    pixels = rows * width
    return call(
        functools.partial(deform_backward_body, batch=batch, rows=rows, width=width, deep=2 * rows),
        (*tiles, offset_rows, disp, frac, weight, dy),
        tuple(jax.ShapeDtypeStruct((batch, pixels, MID), f32 if t == 2 else bf16) for t in range(5))
        + (jax.ShapeDtypeStruct((3, 96, MID), f32),),
        22,
        36,
        [
            VMEM((batch, 5 * pixels, MID), bf16),
            VMEM((batch, 5 * pixels, MID), f32),
            VMEM((3 * pixels, MID), bf16),
            VMEM((16 * width, 3 * pixels), f32),
            VMEM((16 * width, 3 * pixels), bf16),
            VMEM((4, 8, pixels), f32),
        ],
        after,
        through,
    )


def conv_forward_body(rim_ref, m_ref, mask_ref, y_ref, stat_ref, *, batch, rows, width):
    pixels = rows * width
    for b in range(batch):
        total = None
        for j in range(3):
            u = None
            for i in range(3):
                k = i * 3 + j
                start = 2 * i * width
                term = dot(rim_ref[b, start : start + pixels, :], m_ref[:, k * MID : (k + 1) * MID], NT)
                u = term if u is None else u + term
            u = shift_rows(u, -2 * (j - 1), width) if j != 1 else u
            total = u if total is None else total + u
        y_ref[b * pixels : (b + 1) * pixels, :] = total
    y = y_ref[...]
    write_stats(stat_ref, y * mask_ref[:, 0:1], y)


def conv_forward(rim, weight, mask_wide, rows, width, devices):
    batch = rim.shape[0]
    n = batch * rows * width
    return call(
        functools.partial(conv_forward_body, batch=batch, rows=rows, width=width),
        (rim, weight, mask_wide),
        (jax.ShapeDtypeStruct((n, MID), f32), jax.ShapeDtypeStruct((devices, 8, 128), f32)),
        6,
        20,
    )


def conv_backward_body(
    rim_ref, m_ref, y_ref, par_ref, mask_ref, dt_ref, stat_ref, *, batch, rows, width
):
    pixels = rows * width
    for b in range(batch):
        total = None
        for j in range(3):
            u = None
            for i in range(3):
                k = i * 3 + j
                start = (4 - 2 * i) * width
                term = dot(rim_ref[b, start : start + pixels, :], m_ref[:, k * MID : (k + 1) * MID])
                u = term if u is None else u + term
            u = shift_rows(u, 2 * (j - 1), width) if j != 1 else u
            total = u if total is None else total + u
        dt_ref[b * pixels : (b + 1) * pixels, :] = total
    y = y_ref[...]
    dt = gelu_slope(normed(y, par_ref)) * (dt_ref[...] * mask_ref[:, 0:1])
    dt_ref[...] = dt
    write_stats(stat_ref, dt, y * par_ref[2:3, :] + par_ref[3:4, :])


def conv_backward(rim, weight, y, par, mask_wide, rows, width, devices, after):
    batch = rim.shape[0]
    n = batch * rows * width
    return call(
        functools.partial(conv_backward_body, batch=batch, rows=rows, width=width),
        (rim, weight, y, par, mask_wide),
        (jax.ShapeDtypeStruct((n, MID), f32), jax.ShapeDtypeStruct((devices, 8, 128), f32)),
        7,
        20,
        after=after,
    )


def conv_weight_body(dy_ref, rim_ref, out_ref, dyt_ref, *, batch, rows, width):
    pixels = rows * width
    n = batch * pixels
    dy = dy_ref[...].astype(f32)
    for j in range(3):
        moved = shift_rows(dy, 2 * (j - 1), width) if j != 1 else dy
        dyt_ref[j] = moved.T.astype(bf16)
    for j in range(3):
        for i in range(3):
            k = i * 3 + j
            start = 2 * i * width
            total = None
            for b in range(batch):
                term = dot(dyt_ref[j, :, b * pixels : (b + 1) * pixels], rim_ref[b, start : start + pixels, :])
                total = term if total is None else total + term
            out_ref[:, k * MID : (k + 1) * MID] = total.astype(bf16)


def conv_weight_gradient(dy, rim, rows, width, after):
    batch = rim.shape[0]
    return call(
        functools.partial(conv_weight_body, batch=batch, rows=rows, width=width),
        (dy, rim),
        (jax.ShapeDtypeStruct((MID, 9 * MID), bf16),),
        6,
        20,
        [VMEM((3, MID, batch * rows * width), bf16)],
        after,
    )[0]


def columns_weight_body(dy_ref, cols_ref, out_ref, dyt_ref):
    dyt_ref[...] = dy_ref[...].astype(f32).T.astype(bf16)
    for k in range(9):
        part = slice(k * MID, (k + 1) * MID)
        out_ref[:, part] = dot(dyt_ref[...], cols_ref[:, part]).astype(bf16)


def columns_weight_gradient(dy, cols, through):
    return call(
        columns_weight_body,
        (dy, cols),
        (jax.ShapeDtypeStruct((MID, 9 * MID), bf16),),
        7,
        20,
        [VMEM((MID, dy.shape[0]), bf16)],
        through=through,
    )


TILES = 2
EPSILON = 1e-05


def swap_with(values, axis, step):
    return lax.ppermute(values, axis, [(i, i ^ step) for i in range(lax.axis_size(axis))])


def from_behind(block, axis, distance):
    devices = range(lax.axis_size(axis))
    route = [(i - distance, i) for i in devices if i - distance in devices]
    return lax.ppermute(block, axis, route)


def ladder_sum(values, axis):
    step = 1
    while step < lax.axis_size(axis):
        got = swap_with(values.astype(bf16), axis, step)
        values = values + got.astype(f32)
        step *= 2
    return values


def to_everyone(spread, groups=None):
    return lax.all_to_all(spread, ("rows", "ch"), 0, 0, axis_index_groups=groups, tiled=True)


def small_total(spread):
    return jnp.sum(to_everyone(spread), axis=0).reshape(2, -1)


def wide_total(block):
    devices = lax.axis_size("rows") * lax.axis_size("ch")
    core = lax.axis_index("ch") % 2
    above, below = block.reshape(2, -1, 128)
    half = jnp.where(core == 0, above, below) + swap_with(jnp.where(core == 0, below, above), "ch", 1)
    groups = [[i * 2 + k for i in range(devices // 2)] for k in range(2)]
    half = jnp.broadcast_to(half[None], (devices // 2,) + half.shape)
    half = jnp.sum(to_everyone(half, groups), axis=0)
    other = swap_with(half, "ch", 1)
    whole = jnp.stack([jnp.where(core == 0, half, other), jnp.where(core == 0, other, half)])
    whole = whole.reshape(-1, 2, STEP)
    return whole[:, 0].reshape(-1), whole[:, 1].reshape(-1)


def forward_rows(sums, gain, shift, count):
    mean = sums[0] / count
    scale = lax.rsqrt(sums[1] / count - mean * mean + EPSILON)
    return jnp.stack([scale * gain, shift - mean * scale * gain, scale, -mean * scale])


def backward_rows(sums, par, count):
    rows = jnp.stack([par[0], par[0] * sums[0] / count, par[0] * sums[1] / count])
    return rows, own_slice(sums[1]), own_slice(sums[0])


def own_slice(full):
    size = full.shape[0] // lax.axis_size("ch")
    return lax.dynamic_slice_in_dim(full, lax.axis_index("ch") * size, size)


def gather_weight(weight):
    return lax.all_gather(weight.astype(bf16), "ch", axis=0, tiled=True)


def gather_weight_after(weight, *after):
    return lax.all_gather(cast_after(weight, *after), "ch", axis=0, tiled=True)


def gather_by_swaps(weight):
    ch = lax.axis_size("ch")
    came = None
    held = weight.astype(bf16)[None]
    step = ch // 2
    while step >= 1:
        got = swap_with(held, "ch", step)
        came = got if came is None else came
        odd = lax.axis_index("ch") // step % 2 == 1
        held = jnp.stack([jnp.where(odd, got, held), jnp.where(odd, held, got)], axis=1)
        held = held.reshape((-1,) + held.shape[2:])
        step //= 2
    return held.reshape((-1,) + weight.shape[1:]), came


def pick(values, bit):
    return lax.dynamic_index_in_dim(values, bit, 1, keepdims=False)


def scatter_ch(gradient):
    return lax.psum_scatter(gradient, "ch", scatter_dimension=0, tiled=True)


def split_ch(total, step):
    bit = lax.axis_index("ch") // step % 2
    pairs = total.reshape((total.shape[0] // 2, 2) + total.shape[1:])
    return swap_with(pick(pairs, 1 - bit), "ch", step), pick(pairs, bit)


def added(got, kept):
    return (got.astype(f32) + kept.astype(f32)).astype(bf16)


def by_owner(gradient):
    ch = lax.axis_size("ch")
    return gradient.reshape((ch, gradient.shape[0] // ch) + gradient.shape[1:])


def rest_of_ch(total, step):
    while step < lax.axis_size("ch"):
        total = added(*split_ch(total, step))
        step *= 2
    return total


def blocks_to_lanes(values, base):
    return jnp.concatenate([values[r : r + base] for r in range(0, values.shape[0], base)], axis=1)


def lanes_to_blocks(values, wide):
    return jnp.concatenate(
        [values[:, c : c + wide] for c in range(0, values.shape[1], wide)], axis=0
    )


def rows_scatter(parts):
    rows = lax.axis_size("rows")
    total = jnp.concatenate(parts, axis=1)
    base, wide = total.shape
    total = lax.all_to_all(total.reshape(rows, base // rows, wide), "rows", 0, 0, tiled=True)
    return jnp.sum(total.astype(f32), axis=0).astype(bf16)


def rows_gather(share, widths):
    rows = lax.axis_size("rows")
    total = jnp.broadcast_to(share[None], (rows,) + share.shape)
    total = lax.all_to_all(total, "rows", 0, 0, tiled=True)
    total = total.reshape(-1, share.shape[1]).astype(f32)
    ends, at = [], 0
    for width in widths:
        ends.append(total[:, at : at + width])
        at += width
    return ends


def deep_rows(tile):
    odd = lax.axis_index("rows") % 2 == 1
    far_up = from_behind(tile, "rows", 2)
    far_down = from_behind(tile, "rows", -2)
    partner = swap_with(tile, "rows", 1)
    passed = swap_with(jnp.where(odd, far_up, far_down), "rows", 1)
    up = jnp.where(odd, partner, passed)
    down = jnp.where(odd, passed, partner)
    return far_up, up, tile, down, far_down


def deep_return(tiles):
    far_up, up, own, down, far_down = tiles
    odd = lax.axis_index("rows") % 2 == 1
    passed = swap_with(jnp.where(odd, down, up), "rows", 1)
    partner = swap_with(jnp.where(odd, up, down), "rows", 1)
    added = (jnp.where(odd, far_up, far_down).astype(f32) + passed.astype(f32)).astype(bf16)
    below = from_behind(jnp.where(odd, added, far_up), "rows", -2)
    above = from_behind(jnp.where(odd, far_down, added), "rows", 2)
    return own, partner, below, above


def near_rows(tile, width):
    size = 2 * width
    above = from_behind(tile[:, -size:], "rows", 1)
    below = from_behind(tile[:, :size], "rows", -1)
    return jnp.concatenate([above, tile, below], axis=1)


def per_device(
    inputs,
    heights,
    displacements,
    reduce_one,
    reduce_gain_one,
    reduce_bias_one,
    offset_weight,
    deform_weight,
    deform_gain,
    deform_bias,
    expand_one,
    expand_gain_one,
    expand_bias_one,
    reduce_two,
    reduce_gain_two,
    reduce_bias_two,
    conv_weight,
    conv_gain,
    conv_bias,
    expand_two,
    expand_gain_two,
    expand_bias_two,
    cotangent,
):
    batch, rows, width, channels = inputs.shape
    pixels = rows * width
    n = batch * pixels
    own_heights = lax.dynamic_slice_in_dim(heights, lax.axis_index("ch") * batch, batch)
    rows_here = lax.axis_index("rows") * rows + jnp.arange(rows, dtype=jnp.int32)
    mask = (rows_here[None, :] < own_heights[:, None]).astype(f32)
    mask = jnp.broadcast_to(mask[:, :, None], (batch, rows, width)).reshape(n, 1)
    mask_wide = jnp.broadcast_to(mask, (n, 128))
    count = jnp.sum(heights).astype(f32) * width

    offset_rows = offset_weight.astype(bf16).reshape(3, 6, 3, 3, MID).transpose(2, 3, 0, 1, 4)
    offset_rows = jnp.pad(offset_rows, ((0, 0), (0, 0), (0, 1), (0, 2), (0, 0))).reshape(3, 96, MID)
    disp = jnp.pad(displacements.reshape(3, 6, batch, pixels), ((0, 0), (0, 2), (0, 0), (0, 0)))
    disp = disp.transpose(2, 0, 1, 3)

    reduce_full, came = gather_by_swaps(reduce_one)
    deform_full = gather_weight_after(deform_weight, came)
    expand_full, reduce_full_two, conv_full, expand_full_two = [
        gather_weight(w) for w in (expand_one, reduce_two, conv_weight, expand_two)
    ]

    devices = lax.axis_size("rows") * lax.axis_size("ch")
    acts = inputs.reshape(n, channels)
    acts_low, y_a, spread = product_forward(acts, mask_wide, reduce_full, devices)
    par_a = forward_rows(small_total(spread), reduce_gain_one, reduce_bias_one, count)
    hidden = (gelu(y_a * par_a[0] + par_a[1]) * mask).astype(bf16)
    near_tiles = deep_rows(hidden.reshape(batch, pixels, MID))
    columns, y_b, fraction, spread = deform_forward(
        near_tiles, offset_rows, disp, deform_full, mask_wide, rows, width, devices
    )
    par_b = forward_rows(small_total(spread), deform_gain, deform_bias, count)
    middle, y_c, block = expand_forward(y_b, par_b, mask_wide, expand_full)
    par_c = forward_rows(wide_total(block), expand_gain_one, expand_bias_one, count)

    first, first_low, y_d, spread = first_forward(y_c, par_c, acts, mask_wide, reduce_full_two, devices)
    par_d = forward_rows(small_total(spread), reduce_gain_two, reduce_bias_two, count)
    hidden_two = (gelu(y_d * par_d[0] + par_d[1]) * mask).astype(bf16)
    rimmed = near_rows(hidden_two.reshape(batch, pixels, MID), width)
    y_e, spread = conv_forward(rimmed, conv_full, mask_wide, rows, width, devices)
    par_e = forward_rows(small_total(spread), conv_gain, conv_bias, count)
    middle_two, y_f, block = expand_forward(y_e, par_e, mask_wide, expand_full_two)
    par_f = forward_rows(wide_total(block), expand_gain_two, expand_bias_two, count)

    output, dt_f, block = output_stage(y_f, par_f, first, cotangent.reshape(n, channels), mask_wide)
    back_f, expand_gain_two_grad, expand_bias_two_grad = backward_rows(wide_total(block), par_f, count)
    dy_f, dt_e, spread = expand_backward(
        dt_f, y_f, par_f, back_f, mask_wide, expand_full_two, y_e, par_e, devices
    )
    expand_two_local = dot(dy_f, middle_two, TN).astype(bf16)
    expand_two_part = scatter_ch(expand_two_local)
    back_e, conv_gain_grad, conv_bias_grad = backward_rows(small_total(spread), par_e, count)
    dy_e = norm_gradient(dt_e, y_e, par_e, back_e, mask).astype(bf16)
    dy_e_rim = near_rows(dy_e.reshape(batch, pixels, MID), width)
    conv_local = conv_weight_gradient(dy_e, rimmed, rows, width, (expand_two_local,))
    conv_part = scatter_ch(conv_local)
    dt_d, spread = conv_backward(
        dy_e_rim, conv_full, y_d, par_d, mask_wide, rows, width, devices, (conv_local,)
    )
    base = conv_part.shape[0]
    expand_two_part = blocks_to_lanes(expand_two_part, base)
    conv_weight_sum, expand_two_sum = lax.psum((conv_part, expand_two_part), "rows")
    conv_weight_grad = conv_weight_sum.astype(f32)
    expand_two_grad = lanes_to_blocks(expand_two_sum, MID).astype(f32)
    back_d, reduce_gain_two_grad, reduce_bias_two_grad = backward_rows(small_total(spread), par_d, count)
    dy_d, dt_c, block = residual_backward(
        dt_d, y_d, par_d, back_d, mask_wide, reduce_full_two, dt_f, y_c, par_c, acts
    )
    reduce_two_local = dot(dy_d, first_low, TN).astype(bf16)
    reduce_two_got, reduce_two_kept = split_ch(by_owner(reduce_two_local), 1)

    back_c, expand_gain_one_grad, expand_bias_one_grad = backward_rows(wide_total(block), par_c, count)
    dy_c, dt_b, spread, reduce_two_kept = expand_backward(
        dt_c, y_c, par_c, back_c, mask_wide, expand_full, y_b, par_b, devices, (reduce_two_kept,)
    )
    reduce_two_got, reduce_two_kept = split_ch(added(reduce_two_got, reduce_two_kept), 2)
    expand_one_local = dot(dy_c, middle, TN).astype(bf16)
    expand_one_got, expand_one_kept = split_ch(by_owner(expand_one_local), 1)
    back_b, deform_gain_grad, deform_bias_grad = backward_rows(small_total(spread), par_b, count)
    dy_b = norm_gradient(dt_b, y_b, par_b, back_b, mask).astype(bf16)
    deform_local, reduce_two_kept, expand_one_kept = columns_weight_gradient(
        dy_b, columns, (reduce_two_kept, expand_one_kept)
    )
    reduce_two_part = rest_of_ch(added(reduce_two_got, reduce_two_kept), 4)[0]
    expand_one_got, expand_one_kept = split_ch(added(expand_one_got, expand_one_kept), 2)
    deform_got, deform_kept = split_ch(by_owner(deform_local), 1)
    *tiles, offset_local, reduce_two_part, expand_one_kept, deform_kept = deform_backward(
        near_tiles, offset_rows, disp, fraction, deform_full, dy_b, rows, width,
        (conv_part, expand_two_part), (reduce_two_part, expand_one_kept, deform_kept),
    )
    expand_one_part = rest_of_ch(added(expand_one_got, expand_one_kept), 4)[0]
    deform_part = rest_of_ch(added(deform_got, deform_kept), 2)[0]
    share = rows_scatter([reduce_two_part, blocks_to_lanes(expand_one_part, base)])
    dt_a, spread = hidden_backward(
        deep_return(tiles), y_a, par_a, mask_wide, devices, (share,)
    )
    reduce_two_grad, expand_one_grad = rows_gather(share, (channels, channels))
    expand_one_grad = lanes_to_blocks(expand_one_grad, MID)
    sums = small_total(spread)
    back_a, reduce_gain_one_grad, reduce_bias_one_grad = backward_rows(sums, par_a, count)
    dy_a = norm_gradient(dt_a, y_a, par_a, back_a, mask).astype(bf16)
    deform_share = rows_scatter([deform_part])
    (deform_weight_grad,) = rows_gather(deform_share, (9 * MID,))
    offset_part = ladder_sum(offset_local.reshape(-1, MID), "ch").astype(bf16)
    offset_part = jnp.pad(offset_part, ((0, -offset_part.shape[0] % base), (0, 0)))
    offset_part = blocks_to_lanes(offset_part, base)
    reduce_one_local = dot(dy_a, acts_low, TN).astype(bf16)
    reduce_one_part = rest_of_ch(by_owner(reduce_one_local), 1)[0]
    reduce_one_grad, offset_grad = rows_gather(
        rows_scatter([reduce_one_part, offset_part]), (channels, offset_part.shape[1])
    )
    offset_grad = lanes_to_blocks(offset_grad, MID)[:288].reshape(3, 3, 4, 8, MID)[:, :, :3, :6]
    offset_weight_grad = offset_grad.transpose(2, 3, 0, 1, 4).reshape(18, 9 * MID)
    input_grad = input_backward(
        dy_a, reduce_full, dt_c, (deform_share, reduce_two_grad, conv_weight_sum, reduce_one_local)
    )
    return (
        output.reshape(inputs.shape),
        input_grad.reshape(inputs.shape),
        reduce_one_grad,
        reduce_gain_one_grad,
        reduce_bias_one_grad,
        offset_weight_grad,
        deform_weight_grad,
        deform_gain_grad,
        deform_bias_grad,
        expand_one_grad,
        expand_gain_one_grad,
        expand_bias_one_grad,
        reduce_two_grad,
        reduce_gain_two_grad,
        reduce_bias_two_grad,
        conv_weight_grad,
        conv_gain_grad,
        conv_bias_grad,
        expand_two_grad,
        expand_gain_two_grad,
        expand_bias_two_grad,
    )


def solution(mesh):
    tiles = P("ch", "rows", None, None)
    owned = P("ch", None)
    block = (owned, P(), P())
    placed = (tiles, P(), P(None, "ch", "rows", None)) + block + (P(),) + 2 * block + 3 * block + (tiles,)
    grads = (owned, P("ch"), P("ch"))
    return jax.shard_map(
        per_device,
        mesh=mesh,
        in_specs=placed,
        out_specs=(tiles, tiles) + grads + (P(),) + 2 * grads + 3 * grads,
        check_vma=False,
    )
```

```python
import functools

import jax
import jax.numpy as jnp
from jax import lax
from jax.experimental import pallas as pl
from jax.experimental.pallas import tpu as pltpu
from jax.sharding import PartitionSpec as P

bf16 = jnp.bfloat16
f32 = jnp.float32
VMEM = pltpu.VMEM
HBM = pltpu.HBM
DMA = pltpu.SemaphoreType.DMA
MID = 512
STEP = 512
NT = (((1,), (1,)), ((), ()))
TN = (((0,), (0,)), ((), ()))
NN = (((1,), (0,)), ((), ()))
GELU_A = 0.7978845608028654
GELU_B = 0.044715


def dot(a, b, dims=NN):
    return lax.dot_general(a, b, dims, preferred_element_type=f32)


def shaped(*shape, dtype=f32):
    return jax.ShapeDtypeStruct(shape, dtype)


def without(body, n_in, n_after, n_out, n_through):
    first = n_in + n_after + n_through
    return lambda *refs: body(
        *refs[:n_in], *refs[first : first + n_out], *refs[first + n_out + n_through :]
    )


def cost(us):
    return pl.CostEstimate(flops=int(us * 1.1e9), bytes_accessed=int(us * 2.2e6), transcendentals=0)


def call(body, operands, places, outs, out_places, us, limit, scratch=(), after=(), through=()):
    def spec(place):
        return pl.BlockSpec(memory_space=HBM if place == "h" else VMEM)

    def pinned(value, place):
        if place == "v":
            return value
        return pltpu.with_memory_space_constraint(value, HBM if place == "h" else VMEM)

    def result(out, place):
        if place == "v":
            return out
        return (HBM if place == "h" else VMEM)(out.shape, out.dtype)

    n_in, n_out, n_after = len(operands), len(outs), len(after)
    kept = [pltpu.with_memory_space_constraint(v, HBM) for v in (*after, *through)]
    return pl.pallas_call(
        without(body, n_in, n_after, n_out, len(through)),
        in_specs=[spec(p) for p in places] + [spec("h")] * len(kept),
        out_specs=tuple(spec(p) for p in out_places) + (spec("h"),) * len(through),
        out_shape=tuple(result(o, p) for o, p in zip(outs, out_places))
        + tuple(HBM(v.shape, v.dtype) for v in through),
        input_output_aliases={n_in + n_after + t: n_out + t for t in range(len(through))},
        scratch_shapes=list(scratch),
        compiler_params=pltpu.CompilerParams(vmem_limit_bytes=limit * 2**20),
        cost_estimate=cost(us),
    )(*[pinned(v, p) for v, p in zip(operands, places)], *kept)


def moving(source, target, sem):
    copy = pltpu.make_async_copy(source, target, sem)
    copy.start()
    return copy


def columns_moving(source, target, sems, wide=STEP):
    return [
        moving(source.at[:, s * wide : (s + 1) * wide], target.at[:, s * wide : (s + 1) * wide], sems.at[s])
        for s in range(source.shape[1] // wide)
    ]


def rows_moving(source, target, sems, tall=STEP):
    return [
        moving(source.at[s * tall : (s + 1) * tall], target.at[s * tall : (s + 1) * tall], sems.at[s])
        for s in range(source.shape[0] // tall)
    ]


def blocks(wide):
    return [(s, slice(s * STEP, (s + 1) * STEP)) for s in range(wide // STEP)]


def gelu(v):
    return 0.5 * v * (1.0 + jnp.tanh(GELU_A * (v + GELU_B * v * v * v)))


def gelu_slope(v):
    t = jnp.tanh(GELU_A * (v + GELU_B * v * v * v))
    return 0.5 * (1.0 + t) + 0.5 * v * (1.0 - t * t) * (GELU_A * (1.0 + 3.0 * GELU_B * v * v))


def normed(values, par_ref, part=slice(None)):
    return values * par_ref[0:1, part] + par_ref[1:2, part]


def normal_of(values, par_ref, part=slice(None)):
    return values * par_ref[2:3, part] + par_ref[3:4, part]


def norm_gradient(upstream, values, par_ref, back_ref, mask, part=slice(None)):
    normal = normal_of(values, par_ref, part)
    return upstream * back_ref[0:1, part] - mask * (back_ref[1:2, part] + normal * back_ref[2:3, part])


def sums_block(weighted, values):
    n = weighted.shape[1] // 128
    sums = (
        jnp.sum(weighted, axis=0, keepdims=True),
        jnp.sum(weighted * values, axis=0, keepdims=True),
    )
    return jnp.concatenate([v[:, c * 128 : c * 128 + 128] for v in sums for c in range(n)], axis=0)


def write_stats(stat_ref, weighted, values):
    stat_ref[...] = jnp.broadcast_to(sums_block(weighted, values)[None], stat_ref.shape)


def product_forward_body(x_ref, mask_ref, w_ref, low_ref, out_ref, stat_ref, x_buf, low_buf, sems):
    wide = x_ref.shape[1]
    coming = columns_moving(x_ref, x_buf, sems.at[0])
    total, going = None, []
    for s, part in blocks(wide):
        coming[s].wait()
        low_buf[:, part] = x_buf[:, part].astype(bf16)
        going.append(moving(low_buf.at[:, part], low_ref.at[:, part], sems.at[1, s]))
        term = dot(low_buf[:, part], w_ref[:, part], NT)
        total = term if total is None else total + term
    out_ref[...] = total
    write_stats(stat_ref, total * mask_ref[:, 0:1], total)
    for copy in going:
        copy.wait()


def product_forward(x, mask_wide, weight, devices):
    n, wide = x.shape
    return call(
        product_forward_body,
        (x, mask_wide, weight),
        "hvv",
        (shaped(n, wide, dtype=bf16), shaped(n, MID), shaped(devices, 8, 128)),
        "hvv",
        5,
        20,
        [VMEM((n, wide), f32), VMEM((n, wide), bf16), DMA((2, wide // STEP))],
    )


def expand_forward_body(y_ref, par_ref, mask_ref, e_ref, mid_ref, out_ref, stat_ref, e_buf, sems):
    coming = rows_moving(e_ref, e_buf, sems)
    mask = mask_ref[:, 0:1]
    mid_ref[...] = (gelu(normed(y_ref[...], par_ref)) * mask).astype(bf16)
    for s, part in blocks(e_ref.shape[0]):
        coming[s].wait()
        out = dot(mid_ref[...], e_buf[part, :], NT)
        out_ref[:, part] = out
        stat_ref[s * 8 : s * 8 + 8, :] = sums_block(out * mask, out)


def expand_forward(y, par, mask_wide, weight):
    n, wide = y.shape[0], weight.shape[0]
    return call(
        expand_forward_body,
        (y, par, mask_wide, weight),
        "vvvh",
        (shaped(n, MID, dtype=bf16), shaped(n, wide), shaped(wide // 64, 128)),
        "vVv",
        3,
        16,
        [VMEM(weight.shape, bf16), DMA((wide // STEP,))],
    )


def first_forward_body(
    y_ref, par_ref, x_ref, mask_ref, w_ref, first_ref, low_ref, out_ref, stat_ref,
    x_buf, w_buf, low_buf, sems
):
    wide = x_ref.shape[1]
    coming_x = columns_moving(x_ref, x_buf, sems.at[0])
    coming_w = columns_moving(w_ref, w_buf, sems.at[1])
    mask = mask_ref[:, 0:1]
    total, going = None, []
    for s, part in blocks(wide):
        coming_x[s].wait()
        first = gelu(normed(y_ref[:, part], par_ref, part) + x_buf[:, part]) * mask
        first_ref[:, part] = first
        low_buf[:, part] = first.astype(bf16)
        going.append(moving(low_buf.at[:, part], low_ref.at[:, part], sems.at[2, s]))
        coming_w[s].wait()
        term = dot(low_buf[:, part], w_buf[:, part], NT)
        total = term if total is None else total + term
    out_ref[...] = total
    write_stats(stat_ref, total * mask, total)
    for copy in going:
        copy.wait()


def first_forward(y, par, x, mask_wide, weight, devices):
    n, wide = y.shape
    return call(
        first_forward_body,
        (y, par, x, mask_wide, weight),
        "Vvhvh",
        (shaped(n, wide), shaped(n, wide, dtype=bf16), shaped(n, MID), shaped(devices, 8, 128)),
        "Vhvv",
        5,
        20,
        [VMEM((n, wide), f32), VMEM(weight.shape, bf16), VMEM((n, wide), bf16), DMA((3, wide // STEP))],
    )


def output_stage_body(
    y_ref, par_ref, first_ref, cot_ref, mask_ref, out_ref, dt_ref, stat_ref, cot_buf, out_buf, sems
):
    wide = y_ref.shape[1]
    coming = columns_moving(cot_ref, cot_buf, sems.at[0])
    mask = mask_ref[:, 0:1]
    going = []
    for s, part in blocks(wide):
        y = y_ref[:, part]
        pre = normed(y, par_ref, part) + first_ref[:, part]
        t = jnp.tanh(GELU_A * (pre + GELU_B * pre * pre * pre))
        out_buf[:, part] = 0.5 * pre * (1.0 + t) * mask
        going.append(moving(out_buf.at[:, part], out_ref.at[:, part], sems.at[1, s]))
        slope = 0.5 * (1.0 + t) + 0.5 * pre * (1.0 - t * t) * (GELU_A * (1.0 + 3.0 * GELU_B * pre * pre))
        coming[s].wait()
        dt = slope * (cot_buf[:, part] * mask)
        dt_ref[:, part] = dt
        stat_ref[s * 8 : s * 8 + 8, :] = sums_block(dt, normal_of(y, par_ref, part))
    for copy in going:
        copy.wait()


def output_stage(y, par, first, cot, mask_wide):
    n, wide = y.shape
    return call(
        output_stage_body,
        (y, par, first, cot, mask_wide),
        "VvVhv",
        (shaped(n, wide), shaped(n, wide), shaped(wide // 64, 128)),
        "hVv",
        6,
        20,
        [VMEM((n, wide), f32), VMEM((n, wide), f32), DMA((2, wide // STEP))],
    )


def expand_backward_body(
    dt_ref, y_ref, par_ref, back_ref, mask_ref, e_ref, mid_y_ref, mid_par_ref,
    dy_ref, mid_dt_ref, stat_ref, e_buf, dy_buf, sems
):
    wide = dt_ref.shape[1]
    coming = rows_moving(e_ref, e_buf, sems.at[0])
    mask = mask_ref[:, 0:1]
    total, going = None, []
    for s, part in blocks(wide):
        dy = norm_gradient(dt_ref[:, part], y_ref[:, part], par_ref, back_ref, mask, part).astype(bf16)
        dy_buf[:, part] = dy
        going.append(moving(dy_buf.at[:, part], dy_ref.at[:, part], sems.at[1, s]))
        coming[s].wait()
        term = dot(dy, e_buf[part, :])
        total = term if total is None else total + term
    y = mid_y_ref[...]
    dt = gelu_slope(normed(y, mid_par_ref)) * (total * mask)
    mid_dt_ref[...] = dt
    write_stats(stat_ref, dt, normal_of(y, mid_par_ref))
    for copy in going:
        copy.wait()


def expand_backward(dt, y, par, back, mask_wide, weight, mid_y, mid_par, devices, through=()):
    n, wide = y.shape
    return call(
        expand_backward_body,
        (dt, y, par, back, mask_wide, weight, mid_y, mid_par),
        "VVvvvhvv",
        (shaped(n, wide, dtype=bf16), shaped(n, MID), shaped(devices, 8, 128)),
        "hvv",
        4,
        20,
        [VMEM(weight.shape, bf16), VMEM((n, wide), bf16), DMA((2, wide // STEP))],
        through=through,
    )


def residual_backward_body(
    dt_ref, y_ref, par_ref, back_ref, mask_ref, w_ref, add_ref, wide_y_ref, wide_par_ref, x_ref,
    dy_ref, out_ref, stat_ref, w_buf, x_buf, sems
):
    wide = x_ref.shape[1]
    coming_w = columns_moving(w_ref, w_buf, sems.at[0])
    coming_x = columns_moving(x_ref, x_buf, sems.at[1])
    mask = mask_ref[:, 0:1]
    dy_ref[...] = norm_gradient(dt_ref[...], y_ref[...], par_ref, back_ref, mask).astype(bf16)
    for s, part in blocks(wide):
        coming_w[s].wait()
        grad = add_ref[:, part] + dot(dy_ref[...], w_buf[:, part])
        coming_x[s].wait()
        y = wide_y_ref[:, part]
        dt = gelu_slope(normed(y, wide_par_ref, part) + x_buf[:, part]) * (grad * mask)
        out_ref[:, part] = dt
        stat_ref[s * 8 : s * 8 + 8, :] = sums_block(dt, normal_of(y, wide_par_ref, part))


def residual_backward(dt, y, par, back, mask_wide, weight, add, wide_y, wide_par, x):
    n, wide = x.shape
    return call(
        residual_backward_body,
        (dt, y, par, back, mask_wide, weight, add, wide_y, wide_par, x),
        "vvvvvhVVvh",
        (shaped(n, MID, dtype=bf16), shaped(n, wide), shaped(wide // 64, 128)),
        "vVv",
        6,
        20,
        [VMEM(weight.shape, bf16), VMEM((n, wide), f32), DMA((2, wide // STEP))],
    )


def input_backward_body(dy_ref, w_ref, add_ref, out_ref, w_buf, out_buf, sems):
    coming = columns_moving(w_ref, w_buf, sems.at[0])
    going = []
    for s, part in blocks(w_ref.shape[1]):
        coming[s].wait()
        out_buf[:, part] = add_ref[:, part] + dot(dy_ref[...], w_buf[:, part])
        going.append(moving(out_buf.at[:, part], out_ref.at[:, part], sems.at[1, s]))
    for copy in going:
        copy.wait()


def input_backward(dy, weight, add, after):
    n, wide = add.shape
    return call(
        input_backward_body,
        (dy, weight, add),
        "vhV",
        (shaped(n, wide),),
        "h",
        4,
        16,
        [VMEM(weight.shape, bf16), VMEM((n, wide), f32), DMA((2, wide // STEP))],
        after=after,
    )[0]


def hidden_backward_body(
    own_ref, near_ref, up_ref, down_ref, y_ref, par_ref, mask_ref, dt_ref, stat_ref
):
    grad = own_ref[...] + near_ref[...].astype(f32) + up_ref[...].astype(f32) + down_ref[...].astype(f32)
    y = y_ref[...]
    dt = gelu_slope(normed(y, par_ref)) * (grad * mask_ref[:, 0:1])
    dt_ref[...] = dt
    write_stats(stat_ref, dt, normal_of(y, par_ref))


def hidden_backward(pieces, y, par, mask_wide, devices, after, through):
    n = y.shape[0]
    return call(
        hidden_backward_body,
        (*[p.reshape(n, MID) for p in pieces], y, par, mask_wide),
        "vvvvvvv",
        (shaped(n, MID), shaped(devices, 8, 128)),
        "vv",
        3,
        16,
        after=after,
        through=through,
    )


def mid_gradient_body(dt_ref, y_ref, par_ref, back_ref, mask_ref, dy_ref):
    dy = norm_gradient(dt_ref[...], y_ref[...], par_ref, back_ref, mask_ref[:, 0:1])
    dy_ref[...] = dy.astype(bf16)


def mid_gradient(dt, y, par, back, mask_wide, after):
    return call(
        mid_gradient_body,
        (dt, y, par, back, mask_wide),
        "vvvvv",
        (shaped(*y.shape, dtype=bf16),),
        "v",
        2,
        12,
        after=after,
    )[0]


def cast_body(v_ref, out_ref):
    out_ref[...] = v_ref[...].astype(bf16)


def cast_after(values, *after):
    return call(cast_body, (values,), "v", (shaped(*values.shape, dtype=bf16),), "v", 2, 12, after=after)[0]


def shift_lanes(values, by, width):
    place = lax.broadcasted_iota(jnp.int32, values.shape, values.ndim - 1) % width
    moved = pltpu.roll(values, by % values.shape[-1], values.ndim - 1)
    return jnp.where((place >= by) & (place < width + by), moved, 0.0)


def shift_rows(values, by, width):
    place = lax.broadcasted_iota(jnp.int32, values.shape, 0) % width
    moved = pltpu.roll(values, by % values.shape[0], 0)
    return jnp.where((place >= by) & (place < width + by), moved, 0.0)


def offset_fraction(ext_ref, ow_ref, b, base, pixels, width):
    u = None
    for i in range(3):
        start = (base + 2 * i) * width
        term = dot(ow_ref[i], ext_ref[b, start : start + pixels, :], NT)
        u = term if u is None else u + term
    total = u[32:64]
    total = total + shift_lanes(u[0:32], 2, width) + shift_lanes(u[64:96], -2, width)
    return 1.0 / (1.0 + jnp.exp(-total))


def tiles_moving(tiles, ext_ref, pixels, sems):
    return [
        moving(ref, ext_ref.at[:, t * pixels : (t + 1) * pixels, :], sems.at[t])
        for t, ref in enumerate(tiles)
    ]


def deform_forward_body(
    t0_ref, t1_ref, t2_ref, t3_ref, t4_ref, ow_ref, disp_ref, m_ref, mask_ref,
    cols_out_ref, y_ref, frac_ref, stat_ref,
    ext_ref, par_ref, s_ref, cols_ref, m_buf, tile_sems, sems, *, batch, rows, width, deep
):
    pixels = rows * width
    coming = tiles_moving((t0_ref, t1_ref, t2_ref, t3_ref, t4_ref), ext_ref, pixels, tile_sems)
    coming_m = moving(m_ref, m_buf, sems.at[0])
    for copy in coming:
        copy.wait()
    lane = lax.broadcasted_iota(jnp.int32, (32, 128), 1)
    column = lane % width
    upper = lane // width

    def image(b, carry):
        frac = offset_fraction(ext_ref, ow_ref, b, deep - 2, pixels, width)
        for i in range(4):
            frac_ref[b, i] = frac[i * 8 : i * 8 + 8]
        pix = lax.broadcasted_iota(jnp.int32, (1, pixels), 1)
        row_at, col_at = pix // width, pix % width
        tops, lefts, ys, xs = [], [], [], []
        for k in range(9):
            i, j = k // 3, k % 3
            tops.append(row_at + disp_ref[b, i, 2 * j : 2 * j + 1, :] + (deep - 2))
            lefts.append(col_at + 2 * (j - 1) + disp_ref[b, i, 2 * j + 1 : 2 * j + 2, :])
            at = i * 8 + 2 * j
            ys.append(frac[at : at + 1])
            xs.append(frac[at + 1 : at + 2])
        blank = jnp.zeros((23, pixels), f32)
        par = jnp.concatenate(
            [jnp.concatenate(g, axis=0).astype(f32) if g is not None else blank
             for g in (tops, None, lefts, None, ys, None, xs, None)], axis=0)
        par_ref[...] = par.T

        def row_of_taps(i, carry):
            for j in range(3):
                k = i * 3 + j
                for c in range(pixels // 32):
                    p = pltpu.roll(par_ref[c * 32 : c * 32 + 32, :], 128 - k, 1)
                    wide = (32, 128)
                    top = jnp.broadcast_to(p[:, 0:1], wide).astype(jnp.int32) - upper
                    left = jnp.broadcast_to(p[:, 32:33], wide).astype(jnp.int32)
                    fy = jnp.broadcast_to(p[:, 64:65], wide)
                    fx = jnp.broadcast_to(p[:, 96:97], wide)
                    cw = jnp.where(column == left, 1.0 - fx, jnp.where(column == left + 1, fx, 0.0))
                    ca, cb = (1.0 - fy) * cw, fy * cw
                    for q in range(8):
                        s = jnp.where(top == 2 * q, ca, jnp.where(top == 2 * q - 1, cb, 0.0))
                        s_ref[j * pixels + c * 32 : j * pixels + c * 32 + 32, q * 128 : q * 128 + 128] = s.astype(bf16)
            start = pl.multiple_of(i * 2 * width, 128)
            window = ext_ref[b, pl.ds(start, 16 * width), :]
            for j in range(3):
                got = dot(s_ref[j * pixels : (j + 1) * pixels, :], window).astype(bf16)
                cols_ref[pl.ds(pl.multiple_of(b * pixels, pixels), pixels), pl.ds(pl.multiple_of((i * 3 + j) * MID, MID), MID)] = got
            return carry

        return lax.fori_loop(0, 3, row_of_taps, carry)

    lax.fori_loop(0, batch, image, 0)
    going = moving(cols_ref, cols_out_ref, sems.at[1])
    coming_m.wait()
    y = dot(cols_ref[...], m_buf[...], NT)
    y_ref[...] = y
    write_stats(stat_ref, y * mask_ref[:, 0:1], y)
    going.wait()


def deform_forward(tiles, offset_rows, disp, weight, mask_wide, rows, width, devices):
    batch = tiles[0].shape[0]
    pixels = rows * width
    n = batch * pixels
    return call(
        functools.partial(deform_forward_body, batch=batch, rows=rows, width=width, deep=2 * rows),
        (*tiles, offset_rows, disp, weight, mask_wide),
        "hhhhhvvhv",
        (
            shaped(n, 9 * MID, dtype=bf16),
            shaped(n, MID),
            shaped(batch, 4, 8, pixels),
            shaped(devices, 8, 128),
        ),
        "hvvv",
        15,
        30,
        [
            VMEM((batch, 5 * pixels, MID), bf16),
            VMEM((pixels, 128), f32),
            VMEM((3 * pixels, 16 * width), bf16),
            VMEM((n, 9 * MID), bf16),
            VMEM(weight.shape, bf16),
            DMA((5,)),
            DMA((2,)),
        ],
    )


def deform_backward_body(
    t0_ref, t1_ref, t2_ref, t3_ref, t4_ref, ow_ref, disp_ref, frac_ref, m_ref, dy_ref,
    far_up_ref, up_ref, own_ref, down_ref, far_down_ref, dow_ref,
    ext_ref, dext_ref, dc_ref, g_ref, st_ref, df_ref, m_buf, tile_sems, m_sem,
    *, batch, rows, width, deep
):
    pixels = rows * width
    coming = tiles_moving((t0_ref, t1_ref, t2_ref, t3_ref, t4_ref), ext_ref, pixels, tile_sems)
    coming_m = moving(m_ref, m_buf, m_sem)
    window = 16 * width
    dow_ref[...] = jnp.zeros_like(dow_ref)
    dext_ref[...] = jnp.zeros_like(dext_ref)
    for copy in coming:
        copy.wait()
    coming_m.wait()

    def image(b, carry):
        at = pl.multiple_of(b * pixels, pixels)

        def row_of_taps(i, carry):
            dy = dy_ref[pl.ds(at, pixels), :]
            for j in range(3):
                m = m_buf[:, pl.ds(pl.multiple_of((i * 3 + j) * MID, MID), MID)]
                dc_ref[j * pixels : (j + 1) * pixels, :] = dot(dy, m).astype(bf16)
            start = pl.multiple_of(i * 2 * width, 128)
            g_ref[...] = dot(ext_ref[b, pl.ds(start, window), :], dc_ref[...], NT)
            place = lax.broadcasted_iota(jnp.int32, (width, 128), 0)
            for j in range(3):
                for h in range(pixels // 128):
                    lanes = slice(h * 128, h * 128 + 128)
                    at_l = slice(j * pixels + h * 128, j * pixels + h * 128 + 128)
                    pix = lax.broadcasted_iota(jnp.int32, (1, 128), 1) + h * 128
                    by_y, by_x = slice(2 * j, 2 * j + 1), slice(2 * j + 1, 2 * j + 2)
                    top = pix // width + disp_ref[b, i, by_y, lanes] + (deep - 2)
                    left = pix % width + 2 * (j - 1) + disp_ref[b, i, by_x, lanes]
                    fy = frac_ref[b, i, by_y, lanes]
                    fx = frac_ref[b, i, by_x, lanes]
                    here, after = place == left, place == left + 1
                    cw = jnp.where(here, 1.0 - fx, jnp.where(after, fx, 0.0))
                    ca, cb = (1.0 - fy) * cw, fy * cw
                    low_sum = jnp.zeros((width, 128), f32)
                    high_sum = jnp.zeros((width, 128), f32)
                    for r in range(16):
                        part = slice(r * width, r * width + width)
                        g = g_ref[part, at_l]
                        m0, m1 = top == r, top == r - 1
                        low_sum = low_sum + jnp.where(m0, g, 0.0)
                        high_sum = high_sum + jnp.where(m1, g, 0.0)
                        st_ref[part, at_l] = jnp.where(m0, ca, jnp.where(m1, cb, 0.0)).astype(bf16)
                    d_fy = jnp.sum((high_sum - low_sum) * cw, axis=0, keepdims=True)
                    mixed = (1.0 - fy) * low_sum + fy * high_sum
                    d_fx = jnp.sum(
                        jnp.where(after, mixed, 0.0) - jnp.where(here, mixed, 0.0), axis=0, keepdims=True)
                    df_ref[i, by_y, lanes] = d_fy * fy * (1.0 - fy)
                    df_ref[i, by_x, lanes] = d_fx * fx * (1.0 - fx)
            dext_ref[b, pl.ds(start, window), :] += dot(st_ref[...], dc_ref[...])
            return carry

        df_ref[...] = jnp.zeros_like(df_ref)
        carry = lax.fori_loop(0, 3, row_of_taps, carry)
        d_off = df_ref[...].reshape(32, pixels).astype(bf16).astype(f32)
        stacked = jnp.concatenate(
            [shift_lanes(d_off, -2, width), d_off, shift_lanes(d_off, 2, width)], axis=0)
        across = jnp.concatenate([stacked, jnp.zeros((32, pixels), f32)], axis=0).T.astype(bf16)
        stacked = stacked.astype(bf16)
        for i in range(3):
            first = (deep - 2 + 2 * i) * width
            part = slice(first, first + pixels)
            dow_ref[i] += dot(stacked, ext_ref[b, part, :])
            dext_ref[b, part, :] += dot(across[:, :96], ow_ref[i])
        tiles = (far_up_ref, up_ref, own_ref, down_ref, far_down_ref)
        for t, ref in enumerate(tiles):
            ref[b] = dext_ref[b, t * pixels : (t + 1) * pixels, :].astype(ref.dtype)
        return carry

    lax.fori_loop(0, batch, image, 0)


def deform_backward(tiles, offset_rows, disp, frac, weight, dy, rows, width, after, through):
    batch = tiles[0].shape[0]
    pixels = rows * width
    return call(
        functools.partial(deform_backward_body, batch=batch, rows=rows, width=width, deep=2 * rows),
        (*tiles, offset_rows, disp, frac, weight, dy),
        "hhhhhvvvhv",
        tuple(shaped(batch, pixels, MID, dtype=f32 if t == 2 else bf16) for t in range(5))
        + (shaped(3, 96, MID),),
        "vvvvvv",
        20,
        36,
        [
            VMEM((batch, 5 * pixels, MID), bf16),
            VMEM((batch, 5 * pixels, MID), f32),
            VMEM((3 * pixels, MID), bf16),
            VMEM((16 * width, 3 * pixels), f32),
            VMEM((16 * width, 3 * pixels), bf16),
            VMEM((4, 8, pixels), f32),
            VMEM(weight.shape, bf16),
            DMA((5,)),
            DMA,
        ],
        after,
        through,
    )


def taps_moving(m_ref, m_buf, sems):
    wide = 3 * MID
    return columns_moving(m_ref, m_buf, sems, wide)


def conv_forward_body(rim_ref, m_ref, mask_ref, y_ref, stat_ref, m_buf, sems, *, batch, rows, width):
    pixels = rows * width
    coming = taps_moving(m_ref, m_buf, sems)
    sums = [[None] * 3 for _ in range(batch)]
    for i in range(3):
        coming[i].wait()
        for b in range(batch):
            for j in range(3):
                k = i * 3 + j
                start = 2 * i * width
                term = dot(rim_ref[b, start : start + pixels, :], m_buf[:, k * MID : (k + 1) * MID], NT)
                sums[b][j] = term if i == 0 else sums[b][j] + term
    for b in range(batch):
        total = sums[b][1] + shift_rows(sums[b][0], 2, width) + shift_rows(sums[b][2], -2, width)
        y_ref[b * pixels : (b + 1) * pixels, :] = total
    y = y_ref[...]
    write_stats(stat_ref, y * mask_ref[:, 0:1], y)


def conv_forward(rim, weight, mask_wide, rows, width, devices):
    batch = rim.shape[0]
    n = batch * rows * width
    return call(
        functools.partial(conv_forward_body, batch=batch, rows=rows, width=width),
        (rim, weight, mask_wide),
        "vhv",
        (shaped(n, MID), shaped(devices, 8, 128)),
        "vv",
        5,
        24,
        [VMEM(weight.shape, bf16), DMA((3,))],
    )


def conv_backward_body(
    rim_ref, m_ref, y_ref, par_ref, mask_ref, dt_ref, stat_ref, m_buf, sems, *, batch, rows, width
):
    pixels = rows * width
    coming = taps_moving(m_ref, m_buf, sems)
    sums = [[None] * 3 for _ in range(batch)]
    for i in range(3):
        coming[i].wait()
        for b in range(batch):
            for j in range(3):
                k = i * 3 + j
                start = (4 - 2 * i) * width
                term = dot(rim_ref[b, start : start + pixels, :], m_buf[:, k * MID : (k + 1) * MID])
                sums[b][j] = term if i == 0 else sums[b][j] + term
    for b in range(batch):
        total = sums[b][1] + shift_rows(sums[b][0], -2, width) + shift_rows(sums[b][2], 2, width)
        dt_ref[b * pixels : (b + 1) * pixels, :] = total
    y = y_ref[...]
    dt = gelu_slope(normed(y, par_ref)) * (dt_ref[...] * mask_ref[:, 0:1])
    dt_ref[...] = dt
    write_stats(stat_ref, dt, normal_of(y, par_ref))


def conv_backward(rim, weight, y, par, mask_wide, rows, width, devices, after):
    batch = rim.shape[0]
    n = batch * rows * width
    return call(
        functools.partial(conv_backward_body, batch=batch, rows=rows, width=width),
        (rim, weight, y, par, mask_wide),
        "vhvvv",
        (shaped(n, MID), shaped(devices, 8, 128)),
        "vv",
        6,
        24,
        [VMEM(weight.shape, bf16), DMA((3,))],
        after,
    )


def conv_weight_body(dy_ref, rim_ref, out_ref, dyt_ref, out_buf, sems, *, batch, rows, width):
    pixels = rows * width
    dy = dy_ref[...].astype(f32)
    going = []
    for j in range(3):
        moved = shift_rows(dy, 2 * (j - 1), width) if j != 1 else dy
        dyt_ref[j] = moved.T.astype(bf16)
        for i in range(3):
            part = slice((i * 3 + j) * MID, (i * 3 + j + 1) * MID)
            start = 2 * i * width
            total = None
            for b in range(batch):
                term = dot(dyt_ref[j, :, b * pixels : (b + 1) * pixels], rim_ref[b, start : start + pixels, :])
                total = term if total is None else total + term
            out_buf[:, part] = total.astype(bf16)
            going.append(moving(out_buf.at[:, part], out_ref.at[:, part], sems.at[i * 3 + j]))
    for copy in going:
        copy.wait()


def conv_weight_gradient(dy, rim, rows, width, after):
    batch = rim.shape[0]
    return call(
        functools.partial(conv_weight_body, batch=batch, rows=rows, width=width),
        (dy, rim),
        "vv",
        (shaped(MID, 9 * MID, dtype=bf16),),
        "h",
        6,
        20,
        [VMEM((3, MID, batch * rows * width), bf16), VMEM((MID, 9 * MID), bf16), DMA((9,))],
        after,
    )[0]


def columns_weight_body(dy_ref, cols_ref, out_ref, dyt_ref, cols_buf, out_buf, sems):
    coming = columns_moving(cols_ref, cols_buf, sems.at[0])
    dyt_ref[...] = dy_ref[...].astype(f32).T.astype(bf16)
    going = []
    for s, part in blocks(cols_ref.shape[1]):
        coming[s].wait()
        out_buf[:, part] = dot(dyt_ref[...], cols_buf[:, part]).astype(bf16)
        going.append(moving(out_buf.at[:, part], out_ref.at[:, part], sems.at[1, s]))
    for copy in going:
        copy.wait()


def columns_weight_gradient(dy, cols, through):
    n, wide = cols.shape
    return call(
        columns_weight_body,
        (dy, cols),
        "vh",
        (shaped(MID, wide, dtype=bf16),),
        "h",
        6,
        20,
        [VMEM((MID, n), bf16), VMEM((n, wide), bf16), VMEM((MID, wide), bf16), DMA((2, wide // STEP))],
        through=through,
    )


TILES = 2
EPSILON = 1e-05


def swap_with(values, axis, step):
    return lax.ppermute(values, axis, [(i, i ^ step) for i in range(lax.axis_size(axis))])


def from_behind(block, axis, distance):
    devices = range(lax.axis_size(axis))
    route = [(i - distance, i) for i in devices if i - distance in devices]
    return lax.ppermute(block, axis, route)


def ladder_sum(values, axis):
    step = 1
    while step < lax.axis_size(axis):
        got = swap_with(values.astype(bf16), axis, step)
        values = values + got.astype(f32)
        step *= 2
    return values


def to_everyone(spread, groups=None):
    return lax.all_to_all(spread, ("rows", "ch"), 0, 0, axis_index_groups=groups, tiled=True)


def small_total(spread):
    return jnp.sum(to_everyone(spread), axis=0).reshape(2, -1)


def wide_total(block):
    devices = lax.axis_size("rows") * lax.axis_size("ch")
    core = lax.axis_index("ch") % 2
    above, below = block.reshape(2, -1, 128)
    half = jnp.where(core == 0, above, below) + swap_with(jnp.where(core == 0, below, above), "ch", 1)
    groups = [[i * 2 + k for i in range(devices // 2)] for k in range(2)]
    half = jnp.broadcast_to(half[None], (devices // 2,) + half.shape)
    half = jnp.sum(to_everyone(half, groups), axis=0)
    other = swap_with(half, "ch", 1)
    whole = jnp.stack([jnp.where(core == 0, half, other), jnp.where(core == 0, other, half)])
    whole = whole.reshape(-1, 2, STEP)
    return whole[:, 0].reshape(-1), whole[:, 1].reshape(-1)


def forward_rows(sums, gain, shift, count):
    mean = sums[0] / count
    scale = lax.rsqrt(sums[1] / count - mean * mean + EPSILON)
    return jnp.stack([scale * gain, shift - mean * scale * gain, scale, -mean * scale])


def backward_rows(sums, par, count):
    rows = jnp.stack([par[0], par[0] * sums[0] / count, par[0] * sums[1] / count])
    return rows, own_slice(sums[1]), own_slice(sums[0])


def own_slice(full):
    size = full.shape[0] // lax.axis_size("ch")
    return lax.dynamic_slice_in_dim(full, lax.axis_index("ch") * size, size)


def gather_weight(weight):
    return lax.all_gather(weight.astype(bf16), "ch", axis=0, tiled=True)


def gather_weight_after(weight, *after):
    return lax.all_gather(cast_after(weight, *after), "ch", axis=0, tiled=True)


def gather_by_swaps(weight):
    ch = lax.axis_size("ch")
    came = None
    held = weight.astype(bf16)[None]
    step = ch // 2
    while step >= 1:
        got = swap_with(held, "ch", step)
        came = got if came is None else came
        odd = lax.axis_index("ch") // step % 2 == 1
        held = jnp.stack([jnp.where(odd, got, held), jnp.where(odd, held, got)], axis=1)
        held = held.reshape((-1,) + held.shape[2:])
        step //= 2
    return held.reshape((-1,) + weight.shape[1:]), came


def pick(values, bit):
    return lax.dynamic_index_in_dim(values, bit, 1, keepdims=False)


def scatter_ch(gradient):
    return lax.psum_scatter(gradient, "ch", scatter_dimension=0, tiled=True)


def split_ch(total, step):
    bit = lax.axis_index("ch") // step % 2
    pairs = total.reshape((total.shape[0] // 2, 2) + total.shape[1:])
    return swap_with(pick(pairs, 1 - bit), "ch", step), pick(pairs, bit)


def added(got, kept):
    return (got.astype(f32) + kept.astype(f32)).astype(bf16)


def by_owner(gradient):
    ch = lax.axis_size("ch")
    return gradient.reshape((ch, gradient.shape[0] // ch) + gradient.shape[1:])


def rest_of_ch(total, step):
    while step < lax.axis_size("ch"):
        total = added(*split_ch(total, step))
        step *= 2
    return total


def blocks_to_lanes(values, base):
    return jnp.concatenate([values[r : r + base] for r in range(0, values.shape[0], base)], axis=1)


def lanes_to_blocks(values, wide):
    return jnp.concatenate(
        [values[:, c : c + wide] for c in range(0, values.shape[1], wide)], axis=0
    )


def rows_scatter(parts):
    rows = lax.axis_size("rows")
    total = jnp.concatenate(parts, axis=1)
    base, wide = total.shape
    total = lax.all_to_all(total.reshape(rows, base // rows, wide), "rows", 0, 0, tiled=True)
    return jnp.sum(total.astype(f32), axis=0).astype(bf16)


def rows_gather(share, widths):
    rows = lax.axis_size("rows")
    total = jnp.broadcast_to(share[None], (rows,) + share.shape)
    came = lax.all_to_all(total, "rows", 0, 0, tiled=True)
    total = came.reshape(-1, share.shape[1]).astype(f32)
    ends, at = [], 0
    for width in widths:
        ends.append(total[:, at : at + width])
        at += width
    return ends, came


def deep_rows(tile):
    odd = lax.axis_index("rows") % 2 == 1
    far_up = from_behind(tile, "rows", 2)
    far_down = from_behind(tile, "rows", -2)
    partner = swap_with(tile, "rows", 1)
    passed = swap_with(jnp.where(odd, far_up, far_down), "rows", 1)
    up = jnp.where(odd, partner, passed)
    down = jnp.where(odd, passed, partner)
    return far_up, up, tile, down, far_down


def deep_return(tiles):
    far_up, up, own, down, far_down = tiles
    odd = lax.axis_index("rows") % 2 == 1
    passed = swap_with(jnp.where(odd, down, up), "rows", 1)
    partner = swap_with(jnp.where(odd, up, down), "rows", 1)
    added = (jnp.where(odd, far_up, far_down).astype(f32) + passed.astype(f32)).astype(bf16)
    below = from_behind(jnp.where(odd, added, far_up), "rows", -2)
    above = from_behind(jnp.where(odd, far_down, added), "rows", 2)
    return own, partner, below, above


def near_rows(tile, width):
    size = 2 * width
    above = from_behind(tile[:, -size:], "rows", 1)
    below = from_behind(tile[:, :size], "rows", -1)
    return jnp.concatenate([above, tile, below], axis=1)


def per_device(
    inputs,
    heights,
    displacements,
    reduce_one,
    reduce_gain_one,
    reduce_bias_one,
    offset_weight,
    deform_weight,
    deform_gain,
    deform_bias,
    expand_one,
    expand_gain_one,
    expand_bias_one,
    reduce_two,
    reduce_gain_two,
    reduce_bias_two,
    conv_weight,
    conv_gain,
    conv_bias,
    expand_two,
    expand_gain_two,
    expand_bias_two,
    cotangent,
):
    batch, rows, width, channels = inputs.shape
    pixels = rows * width
    n = batch * pixels
    own_heights = lax.dynamic_slice_in_dim(heights, lax.axis_index("ch") * batch, batch)
    rows_here = lax.axis_index("rows") * rows + jnp.arange(rows, dtype=jnp.int32)
    mask = (rows_here[None, :] < own_heights[:, None]).astype(f32)
    mask = jnp.broadcast_to(mask[:, :, None], (batch, rows, width)).reshape(n, 1)
    mask_wide = jnp.broadcast_to(mask, (n, 128))
    count = jnp.sum(heights).astype(f32) * width

    offset_rows = offset_weight.astype(bf16).reshape(3, 6, 3, 3, MID).transpose(2, 3, 0, 1, 4)
    offset_rows = jnp.pad(offset_rows, ((0, 0), (0, 0), (0, 1), (0, 2), (0, 0))).reshape(3, 96, MID)
    disp = jnp.pad(displacements.reshape(3, 6, batch, pixels), ((0, 0), (0, 2), (0, 0), (0, 0)))
    disp = disp.transpose(2, 0, 1, 3)

    reduce_full, came = gather_by_swaps(reduce_one)
    deform_full = gather_weight_after(deform_weight, came)
    expand_full, reduce_full_two, conv_full, expand_full_two = [
        gather_weight(w) for w in (expand_one, reduce_two, conv_weight, expand_two)
    ]

    devices = lax.axis_size("rows") * lax.axis_size("ch")
    acts = inputs.reshape(n, channels)
    acts_low, y_a, spread = product_forward(acts, mask_wide, reduce_full, devices)
    par_a = forward_rows(small_total(spread), reduce_gain_one, reduce_bias_one, count)
    hidden = (gelu(y_a * par_a[0] + par_a[1]) * mask).astype(bf16)
    near_tiles = deep_rows(hidden.reshape(batch, pixels, MID))
    columns, y_b, fraction, spread = deform_forward(
        near_tiles, offset_rows, disp, deform_full, mask_wide, rows, width, devices
    )
    par_b = forward_rows(small_total(spread), deform_gain, deform_bias, count)
    middle, y_c, block = expand_forward(y_b, par_b, mask_wide, expand_full)
    par_c = forward_rows(wide_total(block), expand_gain_one, expand_bias_one, count)

    first, first_low, y_d, spread = first_forward(y_c, par_c, acts, mask_wide, reduce_full_two, devices)
    par_d = forward_rows(small_total(spread), reduce_gain_two, reduce_bias_two, count)
    hidden_two = (gelu(y_d * par_d[0] + par_d[1]) * mask).astype(bf16)
    rimmed = near_rows(hidden_two.reshape(batch, pixels, MID), width)
    y_e, spread = conv_forward(rimmed, conv_full, mask_wide, rows, width, devices)
    par_e = forward_rows(small_total(spread), conv_gain, conv_bias, count)
    middle_two, y_f, block = expand_forward(y_e, par_e, mask_wide, expand_full_two)
    par_f = forward_rows(wide_total(block), expand_gain_two, expand_bias_two, count)

    output, dt_f, block = output_stage(y_f, par_f, first, cotangent.reshape(n, channels), mask_wide)
    back_f, expand_gain_two_grad, expand_bias_two_grad = backward_rows(wide_total(block), par_f, count)
    dy_f, dt_e, spread = expand_backward(
        dt_f, y_f, par_f, back_f, mask_wide, expand_full_two, y_e, par_e, devices
    )
    expand_two_local = dot(dy_f, middle_two, TN).astype(bf16)
    expand_two_part = scatter_ch(expand_two_local)
    back_e, conv_gain_grad, conv_bias_grad = backward_rows(small_total(spread), par_e, count)
    dy_e = norm_gradient(dt_e, y_e, par_e, back_e, mask).astype(bf16)
    dy_e_rim = near_rows(dy_e.reshape(batch, pixels, MID), width)
    conv_local = conv_weight_gradient(dy_e, rimmed, rows, width, (expand_two_local,))
    conv_part = scatter_ch(conv_local)
    dt_d, spread = conv_backward(
        dy_e_rim, conv_full, y_d, par_d, mask_wide, rows, width, devices, (conv_local,)
    )
    base = conv_part.shape[0]
    expand_two_part = blocks_to_lanes(expand_two_part, base)
    conv_weight_sum, expand_two_sum = lax.psum((conv_part, expand_two_part), "rows")
    conv_weight_grad = conv_weight_sum.astype(f32)
    expand_two_grad = lanes_to_blocks(expand_two_sum, MID).astype(f32)
    back_d, reduce_gain_two_grad, reduce_bias_two_grad = backward_rows(small_total(spread), par_d, count)
    dy_d, dt_c, block = residual_backward(
        dt_d, y_d, par_d, back_d, mask_wide, reduce_full_two, dt_f, y_c, par_c, acts
    )
    reduce_two_local = dot(dy_d, first_low, TN).astype(bf16)
    reduce_two_got, reduce_two_kept = split_ch(by_owner(reduce_two_local), 1)

    back_c, expand_gain_one_grad, expand_bias_one_grad = backward_rows(wide_total(block), par_c, count)
    dy_c, dt_b, spread, reduce_two_kept = expand_backward(
        dt_c, y_c, par_c, back_c, mask_wide, expand_full, y_b, par_b, devices, (reduce_two_kept,)
    )
    reduce_two_got, reduce_two_kept = split_ch(added(reduce_two_got, reduce_two_kept), 2)
    expand_one_local = dot(dy_c, middle, TN).astype(bf16)
    expand_one_got, expand_one_kept = split_ch(by_owner(expand_one_local), 1)
    back_b, deform_gain_grad, deform_bias_grad = backward_rows(small_total(spread), par_b, count)
    dy_b = norm_gradient(dt_b, y_b, par_b, back_b, mask).astype(bf16)
    deform_local, reduce_two_kept, expand_one_kept = columns_weight_gradient(
        dy_b, columns, (reduce_two_kept, expand_one_kept)
    )
    reduce_two_part = rest_of_ch(added(reduce_two_got, reduce_two_kept), 4)[0]
    expand_one_got, expand_one_kept = split_ch(added(expand_one_got, expand_one_kept), 2)
    deform_got, deform_kept = split_ch(by_owner(deform_local), 1)
    *tiles, offset_local, reduce_two_part, expand_one_kept, deform_kept = deform_backward(
        near_tiles, offset_rows, disp, fraction, deform_full, dy_b, rows, width,
        (conv_part, expand_two_part), (reduce_two_part, expand_one_kept, deform_kept),
    )
    expand_one_part = rest_of_ch(added(expand_one_got, expand_one_kept), 4)[0]
    deform_got, deform_kept = split_ch(added(deform_got, deform_kept), 2)
    share = rows_scatter([reduce_two_part, blocks_to_lanes(expand_one_part, base)])
    dt_a, spread, deform_kept = hidden_backward(
        deep_return(tiles), y_a, par_a, mask_wide, devices, (share,), (deform_kept,)
    )
    deform_part = rest_of_ch(added(deform_got, deform_kept), 4)[0]
    deform_share = rows_scatter([deform_part])
    (reduce_two_grad, expand_one_grad), came = rows_gather(share, (channels, channels))
    expand_one_grad = lanes_to_blocks(expand_one_grad, MID)
    back_a, reduce_gain_one_grad, reduce_bias_one_grad = backward_rows(small_total(spread), par_a, count)
    dy_a = mid_gradient(dt_a, y_a, par_a, back_a, mask_wide, (conv_weight_sum, came))
    (deform_weight_grad,), _ = rows_gather(deform_share, (9 * MID,))
    offset_part = ladder_sum(offset_local.reshape(-1, MID), "ch").astype(bf16)
    offset_part = jnp.pad(offset_part, ((0, -offset_part.shape[0] % base), (0, 0)))
    offset_part = blocks_to_lanes(offset_part, base)
    reduce_one_local = dot(dy_a, acts_low, TN).astype(bf16)
    reduce_one_part = rest_of_ch(by_owner(reduce_one_local), 1)[0]
    (reduce_one_grad, offset_grad), _ = rows_gather(
        rows_scatter([reduce_one_part, offset_part]), (channels, offset_part.shape[1])
    )
    offset_grad = lanes_to_blocks(offset_grad, MID)[:288].reshape(3, 3, 4, 8, MID)[:, :, :3, :6]
    offset_weight_grad = offset_grad.transpose(2, 3, 0, 1, 4).reshape(18, 9 * MID)
    input_grad = input_backward(dy_a, reduce_full, dt_c, (reduce_one_local,))
    return (
        output.reshape(inputs.shape),
        input_grad.reshape(inputs.shape),
        reduce_one_grad,
        reduce_gain_one_grad,
        reduce_bias_one_grad,
        offset_weight_grad,
        deform_weight_grad,
        deform_gain_grad,
        deform_bias_grad,
        expand_one_grad,
        expand_gain_one_grad,
        expand_bias_one_grad,
        reduce_two_grad,
        reduce_gain_two_grad,
        reduce_bias_two_grad,
        conv_weight_grad,
        conv_gain_grad,
        conv_bias_grad,
        expand_two_grad,
        expand_gain_two_grad,
        expand_bias_two_grad,
    )


def solution(mesh):
    tiles = P("ch", "rows", None, None)
    owned = P("ch", None)
    block = (owned, P(), P())
    placed = (tiles, P(), P(None, "ch", "rows", None)) + block + (P(),) + 2 * block + 3 * block + (tiles,)
    grads = (owned, P("ch"), P("ch"))
    return jax.shard_map(
        per_device,
        mesh=mesh,
        in_specs=placed,
        out_specs=(tiles, tiles) + grads + (P(),) + 2 * grads + 3 * grads,
        check_vma=False,
    )
```

```python
import functools

import jax
import jax.numpy as jnp
from jax import lax
from jax.experimental import pallas as pl
from jax.experimental.pallas import tpu as pltpu
from jax.sharding import PartitionSpec as P

bf16 = jnp.bfloat16
f32 = jnp.float32
VMEM = pltpu.VMEM
HBM = pltpu.HBM
DMA = pltpu.SemaphoreType.DMA
MID = 512
STEP = 512
NT = (((1,), (1,)), ((), ()))
TN = (((0,), (0,)), ((), ()))
NN = (((1,), (0,)), ((), ()))
GELU_A = 0.7978845608028654
GELU_B = 0.044715


def dot(a, b, dims=NN):
    return lax.dot_general(a, b, dims, preferred_element_type=f32)


def shaped(*shape, dtype=f32):
    return jax.ShapeDtypeStruct(shape, dtype)


def without(body, n_in, n_after, n_out, n_through):
    first = n_in + n_after + n_through
    return lambda *refs: body(
        *refs[:n_in], *refs[first : first + n_out], *refs[first + n_out + n_through :]
    )


def cost(us):
    return pl.CostEstimate(flops=int(us * 1.1e9), bytes_accessed=int(us * 2.2e6), transcendentals=0)


def call(body, operands, places, outs, out_places, us, limit, scratch=(), after=(), through=()):
    def spec(place):
        return pl.BlockSpec(memory_space=HBM if place == "h" else VMEM)

    def pinned(value, place):
        if place == "v":
            return value
        return pltpu.with_memory_space_constraint(value, HBM if place == "h" else VMEM)

    def result(out, place):
        if place == "v":
            return out
        return (HBM if place == "h" else VMEM)(out.shape, out.dtype)

    n_in, n_out, n_after = len(operands), len(outs), len(after)
    kept = [pltpu.with_memory_space_constraint(v, HBM) for v in (*after, *through)]
    return pl.pallas_call(
        without(body, n_in, n_after, n_out, len(through)),
        in_specs=[spec(p) for p in places] + [spec("h")] * len(kept),
        out_specs=tuple(spec(p) for p in out_places) + (spec("h"),) * len(through),
        out_shape=tuple(result(o, p) for o, p in zip(outs, out_places))
        + tuple(HBM(v.shape, v.dtype) for v in through),
        input_output_aliases={n_in + n_after + t: n_out + t for t in range(len(through))},
        scratch_shapes=list(scratch),
        compiler_params=pltpu.CompilerParams(vmem_limit_bytes=limit * 2**20),
        cost_estimate=cost(us),
    )(*[pinned(v, p) for v, p in zip(operands, places)], *kept)


def moving(source, target, sem):
    copy = pltpu.make_async_copy(source, target, sem)
    copy.start()
    return copy


def columns_moving(source, target, sems, wide=STEP):
    return [
        moving(source.at[:, s * wide : (s + 1) * wide], target.at[:, s * wide : (s + 1) * wide], sems.at[s])
        for s in range(source.shape[1] // wide)
    ]


def rows_moving(source, target, sems, tall=STEP):
    return [
        moving(source.at[s * tall : (s + 1) * tall], target.at[s * tall : (s + 1) * tall], sems.at[s])
        for s in range(source.shape[0] // tall)
    ]


def blocks(wide):
    return [(s, slice(s * STEP, (s + 1) * STEP)) for s in range(wide // STEP)]


def gelu(v):
    return 0.5 * v * (1.0 + jnp.tanh(GELU_A * (v + GELU_B * v * v * v)))


def gelu_slope(v):
    t = jnp.tanh(GELU_A * (v + GELU_B * v * v * v))
    return 0.5 * (1.0 + t) + 0.5 * v * (1.0 - t * t) * (GELU_A * (1.0 + 3.0 * GELU_B * v * v))


def normed(values, par_ref, part=slice(None)):
    return values * par_ref[0:1, part] + par_ref[1:2, part]


def normal_of(values, par_ref, part=slice(None)):
    return values * par_ref[2:3, part] + par_ref[3:4, part]


def norm_gradient(upstream, values, par_ref, back_ref, mask, part=slice(None)):
    normal = normal_of(values, par_ref, part)
    return upstream * back_ref[0:1, part] - mask * (back_ref[1:2, part] + normal * back_ref[2:3, part])


def sums_block(weighted, values):
    n = weighted.shape[1] // 128
    sums = (
        jnp.sum(weighted, axis=0, keepdims=True),
        jnp.sum(weighted * values, axis=0, keepdims=True),
    )
    return jnp.concatenate([v[:, c * 128 : c * 128 + 128] for v in sums for c in range(n)], axis=0)


def write_stats(stat_ref, weighted, values):
    stat_ref[...] = jnp.broadcast_to(sums_block(weighted, values)[None], stat_ref.shape)


def product_forward_body(x_ref, mask_ref, w_ref, low_ref, out_ref, stat_ref, x_buf, low_buf, sems):
    wide = x_ref.shape[1]
    coming = columns_moving(x_ref, x_buf, sems.at[0])
    total, going = None, []
    for s, part in blocks(wide):
        coming[s].wait()
        low_buf[:, part] = x_buf[:, part].astype(bf16)
        going.append(moving(low_buf.at[:, part], low_ref.at[:, part], sems.at[1, s]))
        term = dot(low_buf[:, part], w_ref[:, part], NT)
        total = term if total is None else total + term
    out_ref[...] = total
    write_stats(stat_ref, total * mask_ref[:, 0:1], total)
    for copy in going:
        copy.wait()


def product_forward(x, mask_wide, weight, devices):
    n, wide = x.shape
    return call(
        product_forward_body,
        (x, mask_wide, weight),
        "hvv",
        (shaped(n, wide, dtype=bf16), shaped(n, MID), shaped(devices, 8, 128)),
        "hvv",
        5,
        20,
        [VMEM((n, wide), f32), VMEM((n, wide), bf16), DMA((2, wide // STEP))],
    )


def expand_forward_body(
    y_ref, par_ref, mask_ref, e_ref, mid_ref, out_ref, stat_ref, e_buf, out_buf, sems
):
    coming = rows_moving(e_ref, e_buf, sems.at[0])
    mask = mask_ref[:, 0:1]
    mid_ref[...] = (gelu(normed(y_ref[...], par_ref)) * mask).astype(bf16)
    going = []
    for s, part in blocks(e_ref.shape[0]):
        coming[s].wait()
        out = dot(mid_ref[...], e_buf[part, :], NT)
        out_buf[:, part] = out.astype(bf16)
        going.append(moving(out_buf.at[:, part], out_ref.at[:, part], sems.at[1, s]))
        stat_ref[s * 8 : s * 8 + 8, :] = sums_block(out * mask, out)
    for copy in going:
        copy.wait()


def expand_forward(y, par, mask_wide, weight):
    n, wide = y.shape[0], weight.shape[0]
    return call(
        expand_forward_body,
        (y, par, mask_wide, weight),
        "vvvh",
        (shaped(n, MID, dtype=bf16), shaped(n, wide, dtype=bf16), shaped(wide // 64, 128)),
        "vhv",
        4,
        16,
        [VMEM(weight.shape, bf16), VMEM((n, wide), bf16), DMA((2, wide // STEP))],
    )


def first_forward_body(
    y_ref, par_ref, x_ref, mask_ref, w_ref, low_ref, out_ref, stat_ref,
    y_buf, x_buf, w_buf, low_buf, sems
):
    wide = x_ref.shape[1]
    coming_y = columns_moving(y_ref, y_buf, sems.at[0])
    coming_x = columns_moving(x_ref, x_buf, sems.at[1])
    coming_w = columns_moving(w_ref, w_buf, sems.at[2])
    mask = mask_ref[:, 0:1]
    total, going = None, []
    for s, part in blocks(wide):
        coming_y[s].wait()
        coming_x[s].wait()
        first = gelu(normed(y_buf[:, part].astype(f32), par_ref, part) + x_buf[:, part]) * mask
        low_buf[:, part] = first.astype(bf16)
        going.append(moving(low_buf.at[:, part], low_ref.at[:, part], sems.at[3, s]))
        coming_w[s].wait()
        term = dot(low_buf[:, part], w_buf[:, part], NT)
        total = term if total is None else total + term
    out_ref[...] = total
    write_stats(stat_ref, total * mask, total)
    for copy in going:
        copy.wait()


def first_forward(y, par, x, mask_wide, weight, devices):
    n, wide = y.shape
    return call(
        first_forward_body,
        (y, par, x, mask_wide, weight),
        "hvhvh",
        (shaped(n, wide, dtype=bf16), shaped(n, MID), shaped(devices, 8, 128)),
        "hvv",
        6,
        24,
        [
            VMEM((n, wide), bf16),
            VMEM((n, wide), f32),
            VMEM(weight.shape, bf16),
            VMEM((n, wide), bf16),
            DMA((4, wide // STEP)),
        ],
    )


def output_stage_body(
    y_ref, par_ref, first_ref, cot_ref, mask_ref, out_ref, dt_ref, stat_ref,
    y_buf, first_buf, cot_buf, out_buf, dt_buf, sems
):
    wide = y_ref.shape[1]
    coming_y = columns_moving(y_ref, y_buf, sems.at[0])
    coming_f = columns_moving(first_ref, first_buf, sems.at[1])
    coming_c = columns_moving(cot_ref, cot_buf, sems.at[2])
    mask = mask_ref[:, 0:1]
    going = []
    for s, part in blocks(wide):
        coming_y[s].wait()
        coming_f[s].wait()
        y = y_buf[:, part].astype(f32)
        pre = normed(y, par_ref, part) + first_buf[:, part].astype(f32)
        t = jnp.tanh(GELU_A * (pre + GELU_B * pre * pre * pre))
        out_buf[:, part] = 0.5 * pre * (1.0 + t) * mask
        going.append(moving(out_buf.at[:, part], out_ref.at[:, part], sems.at[3, s]))
        slope = 0.5 * (1.0 + t) + 0.5 * pre * (1.0 - t * t) * (GELU_A * (1.0 + 3.0 * GELU_B * pre * pre))
        coming_c[s].wait()
        dt = slope * (cot_buf[:, part] * mask)
        dt_buf[:, part] = dt.astype(bf16)
        going.append(moving(dt_buf.at[:, part], dt_ref.at[:, part], sems.at[4, s]))
        stat_ref[s * 8 : s * 8 + 8, :] = sums_block(dt, normal_of(y, par_ref, part))
    for copy in going:
        copy.wait()


def output_stage(y, par, first, cot, mask_wide):
    n, wide = y.shape
    return call(
        output_stage_body,
        (y, par, first, cot, mask_wide),
        "hvhhv",
        (shaped(n, wide), shaped(n, wide, dtype=bf16), shaped(wide // 64, 128)),
        "hhv",
        8,
        28,
        [
            VMEM((n, wide), bf16),
            VMEM((n, wide), bf16),
            VMEM((n, wide), f32),
            VMEM((n, wide), f32),
            VMEM((n, wide), bf16),
            DMA((5, wide // STEP)),
        ],
    )


def expand_backward_body(
    dt_ref, y_ref, par_ref, back_ref, mask_ref, e_ref, mid_y_ref, mid_par_ref,
    dy_ref, mid_dt_ref, stat_ref, dt_buf, y_buf, e_buf, dy_buf, sems
):
    wide = dt_ref.shape[1]
    coming_dt = columns_moving(dt_ref, dt_buf, sems.at[0])
    coming_y = columns_moving(y_ref, y_buf, sems.at[1])
    coming_e = rows_moving(e_ref, e_buf, sems.at[2])
    mask = mask_ref[:, 0:1]
    total, going = None, []
    for s, part in blocks(wide):
        coming_dt[s].wait()
        coming_y[s].wait()
        dt, y = dt_buf[:, part].astype(f32), y_buf[:, part].astype(f32)
        dy = norm_gradient(dt, y, par_ref, back_ref, mask, part).astype(bf16)
        dy_buf[:, part] = dy
        going.append(moving(dy_buf.at[:, part], dy_ref.at[:, part], sems.at[3, s]))
        coming_e[s].wait()
        term = dot(dy, e_buf[part, :])
        total = term if total is None else total + term
    y = mid_y_ref[...]
    dt = gelu_slope(normed(y, mid_par_ref)) * (total * mask)
    mid_dt_ref[...] = dt
    write_stats(stat_ref, dt, normal_of(y, mid_par_ref))
    for copy in going:
        copy.wait()


def expand_backward(dt, y, par, back, mask_wide, weight, mid_y, mid_par, devices, through=()):
    n, wide = y.shape
    return call(
        expand_backward_body,
        (dt, y, par, back, mask_wide, weight, mid_y, mid_par),
        "hhvvvhvv",
        (shaped(n, wide, dtype=bf16), shaped(n, MID), shaped(devices, 8, 128)),
        "hvv",
        5,
        24,
        [
            VMEM((n, wide), bf16),
            VMEM((n, wide), bf16),
            VMEM(weight.shape, bf16),
            VMEM((n, wide), bf16),
            DMA((4, wide // STEP)),
        ],
        through=through,
    )


def residual_backward_body(
    dt_ref, y_ref, par_ref, back_ref, mask_ref, w_ref, add_ref, wide_y_ref, wide_par_ref, x_ref,
    dy_ref, out_ref, stat_ref, w_buf, add_buf, y_buf, x_buf, out_buf, sems
):
    wide = x_ref.shape[1]
    coming = [
        columns_moving(source, target, sems.at[t])
        for t, (source, target) in enumerate(
            ((w_ref, w_buf), (add_ref, add_buf), (wide_y_ref, y_buf), (x_ref, x_buf))
        )
    ]
    mask = mask_ref[:, 0:1]
    dy_ref[...] = norm_gradient(dt_ref[...], y_ref[...], par_ref, back_ref, mask).astype(bf16)
    going = []
    for s, part in blocks(wide):
        for copies in coming:
            copies[s].wait()
        grad = add_buf[:, part].astype(f32) + dot(dy_ref[...], w_buf[:, part])
        y = y_buf[:, part].astype(f32)
        pre = normed(y, wide_par_ref, part) + x_buf[:, part].astype(f32)
        dt = gelu_slope(pre) * (grad * mask)
        out_buf[:, part] = dt.astype(bf16)
        going.append(moving(out_buf.at[:, part], out_ref.at[:, part], sems.at[4, s]))
        stat_ref[s * 8 : s * 8 + 8, :] = sums_block(dt, normal_of(y, wide_par_ref, part))
    for copy in going:
        copy.wait()


def residual_backward(dt, y, par, back, mask_wide, weight, add, wide_y, wide_par, x):
    n, wide = x.shape
    return call(
        residual_backward_body,
        (dt, y, par, back, mask_wide, weight, add, wide_y, wide_par, x),
        "vvvvvhhhvh",
        (shaped(n, MID, dtype=bf16), shaped(n, wide, dtype=bf16), shaped(wide // 64, 128)),
        "vhv",
        6,
        24,
        [VMEM(weight.shape, bf16)] + [VMEM((n, wide), bf16)] * 4 + [DMA((5, wide // STEP))],
    )


def input_backward_body(dy_ref, w_ref, add_ref, out_ref, w_buf, add_buf, out_buf, sems):
    coming_w = columns_moving(w_ref, w_buf, sems.at[0])
    coming_a = columns_moving(add_ref, add_buf, sems.at[1])
    going = []
    for s, part in blocks(w_ref.shape[1]):
        coming_w[s].wait()
        coming_a[s].wait()
        out_buf[:, part] = add_buf[:, part].astype(f32) + dot(dy_ref[...], w_buf[:, part])
        going.append(moving(out_buf.at[:, part], out_ref.at[:, part], sems.at[2, s]))
    for copy in going:
        copy.wait()


def input_backward(dy, weight, add, through):
    n, wide = add.shape
    return call(
        input_backward_body,
        (dy, weight, add),
        "vhh",
        (shaped(n, wide),),
        "h",
        5,
        20,
        [VMEM(weight.shape, bf16), VMEM((n, wide), bf16), VMEM((n, wide), f32), DMA((3, wide // STEP))],
        through=through,
    )


def hidden_backward_body(*refs):
    *piece_refs, y_ref, par_ref, mask_ref, dt_ref, stat_ref = refs
    batch = len(piece_refs) // 4
    pixels = y_ref.shape[0] // batch
    for b in range(batch):
        own, near, up, down = [ref[...].astype(f32) for ref in piece_refs[4 * b : 4 * b + 4]]
        dt_ref[b * pixels : (b + 1) * pixels, :] = own + near + up + down
    grad = dt_ref[...]
    y = y_ref[...]
    dt = gelu_slope(normed(y, par_ref)) * (grad * mask_ref[:, 0:1])
    dt_ref[...] = dt
    write_stats(stat_ref, dt, normal_of(y, par_ref))


def hidden_backward(pieces, y, par, mask_wide, devices, through):
    n = y.shape[0]
    return call(
        hidden_backward_body,
        (*pieces, y, par, mask_wide),
        "v" * (len(pieces) + 3),
        (shaped(n, MID), shaped(devices, 8, 128)),
        "vv",
        3,
        16,
        through=through,
    )


def mid_gradient_body(dt_ref, y_ref, par_ref, back_ref, mask_ref, dy_ref):
    dy = norm_gradient(dt_ref[...], y_ref[...], par_ref, back_ref, mask_ref[:, 0:1])
    dy_ref[...] = dy.astype(bf16)


def mid_gradient(dt, y, par, back, mask_wide, through):
    return call(
        mid_gradient_body,
        (dt, y, par, back, mask_wide),
        "vvvvv",
        (shaped(*y.shape, dtype=bf16),),
        "v",
        2,
        12,
        through=through,
    )


def cast_body(v_ref, out_ref):
    out_ref[...] = v_ref[...].astype(bf16)


def cast_after(values, *after):
    return call(cast_body, (values,), "v", (shaped(*values.shape, dtype=bf16),), "v", 2, 12, after=after)[0]


def shift_lanes(values, by, width):
    place = lax.broadcasted_iota(jnp.int32, values.shape, values.ndim - 1) % width
    moved = pltpu.roll(values, by % values.shape[-1], values.ndim - 1)
    return jnp.where((place >= by) & (place < width + by), moved, 0.0)


def shift_rows(values, by, width):
    place = lax.broadcasted_iota(jnp.int32, values.shape, 0) % width
    moved = pltpu.roll(values, by % values.shape[0], 0)
    return jnp.where((place >= by) & (place < width + by), moved, 0.0)


def offset_fraction(ext_ref, ow_ref, b, base, pixels, width):
    u = None
    for i in range(3):
        start = (base + 2 * i) * width
        term = dot(ow_ref[i], ext_ref[b, start : start + pixels, :], NT)
        u = term if u is None else u + term
    total = u[32:64]
    total = total + shift_lanes(u[0:32], 2, width) + shift_lanes(u[64:96], -2, width)
    return 1.0 / (1.0 + jnp.exp(-total))


def tiles_moving(tiles, ext_ref, pixels, sems):
    return [
        moving(ref, ext_ref.at[t // 5, t % 5 * pixels : (t % 5 + 1) * pixels, :], sems.at[t])
        for t, ref in enumerate(tiles)
    ]


def deform_forward_body(*refs, batch, rows, width, deep):
    tile_refs, refs = refs[: 5 * batch], refs[5 * batch :]
    ow_ref, disp_ref, m_ref, mask_ref, cols_out_ref, y_ref, frac_ref, stat_ref = refs[:8]
    ext_ref, par_ref, s_ref, cols_ref, m_buf, tile_sems, sems = refs[8:]
    pixels = rows * width
    coming = tiles_moving(tile_refs, ext_ref, pixels, tile_sems)
    coming_m = moving(m_ref, m_buf, sems.at[0])
    for copy in coming:
        copy.wait()
    lane = lax.broadcasted_iota(jnp.int32, (32, 128), 1)
    column = lane % width
    upper = lane // width

    def image(b, carry):
        frac = offset_fraction(ext_ref, ow_ref, b, deep - 2, pixels, width)
        for i in range(4):
            frac_ref[b, i] = frac[i * 8 : i * 8 + 8]
        pix = lax.broadcasted_iota(jnp.int32, (1, pixels), 1)
        row_at, col_at = pix // width, pix % width
        tops, lefts, ys, xs = [], [], [], []
        for k in range(9):
            i, j = k // 3, k % 3
            tops.append(row_at + disp_ref[b, i, 2 * j : 2 * j + 1, :] + (deep - 2))
            lefts.append(col_at + 2 * (j - 1) + disp_ref[b, i, 2 * j + 1 : 2 * j + 2, :])
            at = i * 8 + 2 * j
            ys.append(frac[at : at + 1])
            xs.append(frac[at + 1 : at + 2])
        blank = jnp.zeros((23, pixels), f32)
        par = jnp.concatenate(
            [jnp.concatenate(g, axis=0).astype(f32) if g is not None else blank
             for g in (tops, None, lefts, None, ys, None, xs, None)], axis=0)
        par_ref[...] = par.T

        def row_of_taps(i, carry):
            for j in range(3):
                k = i * 3 + j
                for c in range(pixels // 32):
                    p = pltpu.roll(par_ref[c * 32 : c * 32 + 32, :], 128 - k, 1)
                    wide = (32, 128)
                    top = jnp.broadcast_to(p[:, 0:1], wide).astype(jnp.int32) - upper
                    left = jnp.broadcast_to(p[:, 32:33], wide).astype(jnp.int32)
                    fy = jnp.broadcast_to(p[:, 64:65], wide)
                    fx = jnp.broadcast_to(p[:, 96:97], wide)
                    cw = jnp.where(column == left, 1.0 - fx, jnp.where(column == left + 1, fx, 0.0))
                    ca, cb = (1.0 - fy) * cw, fy * cw
                    for q in range(8):
                        s = jnp.where(top == 2 * q, ca, jnp.where(top == 2 * q - 1, cb, 0.0))
                        s_ref[j * pixels + c * 32 : j * pixels + c * 32 + 32, q * 128 : q * 128 + 128] = s.astype(bf16)
            start = pl.multiple_of(i * 2 * width, 128)
            window = ext_ref[b, pl.ds(start, 16 * width), :]
            for j in range(3):
                got = dot(s_ref[j * pixels : (j + 1) * pixels, :], window).astype(bf16)
                cols_ref[pl.ds(pl.multiple_of(b * pixels, pixels), pixels), pl.ds(pl.multiple_of((i * 3 + j) * MID, MID), MID)] = got
            return carry

        return lax.fori_loop(0, 3, row_of_taps, carry)

    lax.fori_loop(0, batch, image, 0)
    going = moving(cols_ref, cols_out_ref, sems.at[1])
    coming_m.wait()
    y = dot(cols_ref[...], m_buf[...], NT)
    y_ref[...] = y
    write_stats(stat_ref, y * mask_ref[:, 0:1], y)
    going.wait()


def deform_forward(tiles, offset_rows, disp, weight, mask_wide, rows, width, devices):
    batch = len(tiles) // 5
    pixels = rows * width
    n = batch * pixels
    return call(
        functools.partial(deform_forward_body, batch=batch, rows=rows, width=width, deep=2 * rows),
        (*tiles, offset_rows, disp, weight, mask_wide),
        "h" * (5 * batch) + "vvhv",
        (
            shaped(n, 9 * MID, dtype=bf16),
            shaped(n, MID),
            shaped(batch, 4, 8, pixels),
            shaped(devices, 8, 128),
        ),
        "hvvv",
        15,
        30,
        [
            VMEM((batch, 5 * pixels, MID), bf16),
            VMEM((pixels, 128), f32),
            VMEM((3 * pixels, 16 * width), bf16),
            VMEM((n, 9 * MID), bf16),
            VMEM(weight.shape, bf16),
            DMA((5 * batch,)),
            DMA((2,)),
        ],
    )


def deform_backward_body(*refs, batch, rows, width, deep):
    tile_refs, refs = refs[: 5 * batch], refs[5 * batch :]
    (ow_ref, disp_ref, frac_ref, m_ref, dy_ref), refs = refs[:5], refs[5:]
    out_refs, refs = refs[: 5 * batch], refs[5 * batch :]
    dow_ref, ext_ref, dext_ref, dc_ref, g_ref, st_ref, df_ref, m_buf, tile_sems, m_sem = refs
    pixels = rows * width
    coming = tiles_moving(tile_refs, ext_ref, pixels, tile_sems)
    coming_m = moving(m_ref, m_buf, m_sem)
    window = 16 * width
    dow_ref[...] = jnp.zeros_like(dow_ref)
    dext_ref[...] = jnp.zeros_like(dext_ref)
    for copy in coming:
        copy.wait()
    coming_m.wait()

    def image(b, carry):
        at = pl.multiple_of(b * pixels, pixels)

        def row_of_taps(i, carry):
            dy = dy_ref[pl.ds(at, pixels), :]
            for j in range(3):
                m = m_buf[:, pl.ds(pl.multiple_of((i * 3 + j) * MID, MID), MID)]
                dc_ref[j * pixels : (j + 1) * pixels, :] = dot(dy, m).astype(bf16)
            start = pl.multiple_of(i * 2 * width, 128)
            g_ref[...] = dot(ext_ref[b, pl.ds(start, window), :], dc_ref[...], NT)
            place = lax.broadcasted_iota(jnp.int32, (width, 128), 0)
            for j in range(3):
                for h in range(pixels // 128):
                    lanes = slice(h * 128, h * 128 + 128)
                    at_l = slice(j * pixels + h * 128, j * pixels + h * 128 + 128)
                    pix = lax.broadcasted_iota(jnp.int32, (1, 128), 1) + h * 128
                    by_y, by_x = slice(2 * j, 2 * j + 1), slice(2 * j + 1, 2 * j + 2)
                    top = pix // width + disp_ref[b, i, by_y, lanes] + (deep - 2)
                    left = pix % width + 2 * (j - 1) + disp_ref[b, i, by_x, lanes]
                    fy = frac_ref[b, i, by_y, lanes]
                    fx = frac_ref[b, i, by_x, lanes]
                    here, after = place == left, place == left + 1
                    cw = jnp.where(here, 1.0 - fx, jnp.where(after, fx, 0.0))
                    ca, cb = (1.0 - fy) * cw, fy * cw
                    low_sum = jnp.zeros((width, 128), f32)
                    high_sum = jnp.zeros((width, 128), f32)
                    for r in range(16):
                        part = slice(r * width, r * width + width)
                        g = g_ref[part, at_l]
                        m0, m1 = top == r, top == r - 1
                        low_sum = low_sum + jnp.where(m0, g, 0.0)
                        high_sum = high_sum + jnp.where(m1, g, 0.0)
                        st_ref[part, at_l] = jnp.where(m0, ca, jnp.where(m1, cb, 0.0)).astype(bf16)
                    d_fy = jnp.sum((high_sum - low_sum) * cw, axis=0, keepdims=True)
                    mixed = (1.0 - fy) * low_sum + fy * high_sum
                    d_fx = jnp.sum(
                        jnp.where(after, mixed, 0.0) - jnp.where(here, mixed, 0.0), axis=0, keepdims=True)
                    df_ref[i, by_y, lanes] = d_fy * fy * (1.0 - fy)
                    df_ref[i, by_x, lanes] = d_fx * fx * (1.0 - fx)
            dext_ref[b, pl.ds(start, window), :] += dot(st_ref[...], dc_ref[...])
            return carry

        df_ref[...] = jnp.zeros_like(df_ref)
        carry = lax.fori_loop(0, 3, row_of_taps, carry)
        d_off = df_ref[...].reshape(32, pixels).astype(bf16).astype(f32)
        stacked = jnp.concatenate(
            [shift_lanes(d_off, -2, width), d_off, shift_lanes(d_off, 2, width)], axis=0)
        across = jnp.concatenate([stacked, jnp.zeros((32, pixels), f32)], axis=0).T.astype(bf16)
        stacked = stacked.astype(bf16)
        for i in range(3):
            first = (deep - 2 + 2 * i) * width
            part = slice(first, first + pixels)
            dow_ref[i] += dot(stacked, ext_ref[b, part, :])
            dext_ref[b, part, :] += dot(across[:, :96], ow_ref[i])
        return carry

    lax.fori_loop(0, batch, image, 0)
    for t, ref in enumerate(out_refs):
        ref[...] = dext_ref[t // 5, t % 5 * pixels : (t % 5 + 1) * pixels, :].astype(ref.dtype)


def deform_backward(tiles, offset_rows, disp, frac, weight, dy, rows, width, after, through):
    batch = len(tiles) // 5
    pixels = rows * width
    return call(
        functools.partial(deform_backward_body, batch=batch, rows=rows, width=width, deep=2 * rows),
        (*tiles, offset_rows, disp, frac, weight, dy),
        "h" * (5 * batch) + "vvvhv",
        tuple(shaped(pixels, MID, dtype=f32 if t == 2 else bf16) for _ in range(batch) for t in range(5))
        + (shaped(3, 96, MID),),
        "v" * (5 * batch + 1),
        20,
        36,
        [
            VMEM((batch, 5 * pixels, MID), bf16),
            VMEM((batch, 5 * pixels, MID), f32),
            VMEM((3 * pixels, MID), bf16),
            VMEM((16 * width, 3 * pixels), f32),
            VMEM((16 * width, 3 * pixels), bf16),
            VMEM((4, 8, pixels), f32),
            VMEM(weight.shape, bf16),
            DMA((5 * batch,)),
            DMA,
        ],
        after,
        through,
    )


def taps_moving(m_ref, m_buf, sems):
    wide = 3 * MID
    return columns_moving(m_ref, m_buf, sems, wide)


def conv_forward_body(rim_ref, m_ref, mask_ref, y_ref, stat_ref, m_buf, sems, *, batch, rows, width):
    pixels = rows * width
    coming = taps_moving(m_ref, m_buf, sems)
    sums = [[None] * 3 for _ in range(batch)]
    for i in range(3):
        coming[i].wait()
        for b in range(batch):
            for j in range(3):
                k = i * 3 + j
                start = 2 * i * width
                term = dot(rim_ref[b, start : start + pixels, :], m_buf[:, k * MID : (k + 1) * MID], NT)
                sums[b][j] = term if i == 0 else sums[b][j] + term
    for b in range(batch):
        total = sums[b][1] + shift_rows(sums[b][0], 2, width) + shift_rows(sums[b][2], -2, width)
        y_ref[b * pixels : (b + 1) * pixels, :] = total
    y = y_ref[...]
    write_stats(stat_ref, y * mask_ref[:, 0:1], y)


def conv_forward(rim, weight, mask_wide, rows, width, devices):
    batch = rim.shape[0]
    n = batch * rows * width
    return call(
        functools.partial(conv_forward_body, batch=batch, rows=rows, width=width),
        (rim, weight, mask_wide),
        "vhv",
        (shaped(n, MID), shaped(devices, 8, 128)),
        "vv",
        5,
        24,
        [VMEM(weight.shape, bf16), DMA((3,))],
    )


def conv_backward_body(
    rim_ref, m_ref, y_ref, par_ref, mask_ref, dt_ref, stat_ref, m_buf, sems, *, batch, rows, width
):
    pixels = rows * width
    coming = taps_moving(m_ref, m_buf, sems)
    sums = [[None] * 3 for _ in range(batch)]
    for i in range(3):
        coming[i].wait()
        for b in range(batch):
            for j in range(3):
                k = i * 3 + j
                start = (4 - 2 * i) * width
                term = dot(rim_ref[b, start : start + pixels, :], m_buf[:, k * MID : (k + 1) * MID])
                sums[b][j] = term if i == 0 else sums[b][j] + term
    for b in range(batch):
        total = sums[b][1] + shift_rows(sums[b][0], -2, width) + shift_rows(sums[b][2], 2, width)
        dt_ref[b * pixels : (b + 1) * pixels, :] = total
    y = y_ref[...]
    dt = gelu_slope(normed(y, par_ref)) * (dt_ref[...] * mask_ref[:, 0:1])
    dt_ref[...] = dt
    write_stats(stat_ref, dt, normal_of(y, par_ref))


def conv_backward(rim, weight, y, par, mask_wide, rows, width, devices, after):
    batch = rim.shape[0]
    n = batch * rows * width
    return call(
        functools.partial(conv_backward_body, batch=batch, rows=rows, width=width),
        (rim, weight, y, par, mask_wide),
        "vhvvv",
        (shaped(n, MID), shaped(devices, 8, 128)),
        "vv",
        6,
        24,
        [VMEM(weight.shape, bf16), DMA((3,))],
        after,
    )


def conv_weight_body(dy_ref, rim_ref, out_ref, dyt_ref, out_buf, sems, *, batch, rows, width):
    pixels = rows * width
    dy = dy_ref[...].astype(f32)
    going = []
    for j in range(3):
        moved = shift_rows(dy, 2 * (j - 1), width) if j != 1 else dy
        dyt_ref[j] = moved.T.astype(bf16)
        for i in range(3):
            part = slice((i * 3 + j) * MID, (i * 3 + j + 1) * MID)
            start = 2 * i * width
            total = None
            for b in range(batch):
                term = dot(dyt_ref[j, :, b * pixels : (b + 1) * pixels], rim_ref[b, start : start + pixels, :])
                total = term if total is None else total + term
            out_buf[:, part] = total.astype(bf16)
            going.append(moving(out_buf.at[:, part], out_ref.at[:, part], sems.at[i * 3 + j]))
    for copy in going:
        copy.wait()


def conv_weight_gradient(dy, rim, rows, width, after):
    batch = rim.shape[0]
    return call(
        functools.partial(conv_weight_body, batch=batch, rows=rows, width=width),
        (dy, rim),
        "vv",
        (shaped(MID, 9 * MID, dtype=bf16),),
        "h",
        6,
        20,
        [VMEM((3, MID, batch * rows * width), bf16), VMEM((MID, 9 * MID), bf16), DMA((9,))],
        after,
    )[0]


def columns_weight_body(dy_ref, cols_ref, out_ref, dyt_ref, cols_buf, out_buf, sems):
    coming = columns_moving(cols_ref, cols_buf, sems.at[0])
    dyt_ref[...] = dy_ref[...].astype(f32).T.astype(bf16)
    going = []
    for s, part in blocks(cols_ref.shape[1]):
        coming[s].wait()
        out_buf[:, part] = dot(dyt_ref[...], cols_buf[:, part]).astype(bf16)
        going.append(moving(out_buf.at[:, part], out_ref.at[:, part], sems.at[1, s]))
    for copy in going:
        copy.wait()


def columns_weight_gradient(dy, cols, through):
    n, wide = cols.shape
    return call(
        columns_weight_body,
        (dy, cols),
        "vh",
        (shaped(MID, wide, dtype=bf16),),
        "h",
        6,
        20,
        [VMEM((MID, n), bf16), VMEM((n, wide), bf16), VMEM((MID, wide), bf16), DMA((2, wide // STEP))],
        through=through,
    )


TILES = 2
EPSILON = 1e-05


def swap_with(values, axis, step):
    return lax.ppermute(values, axis, [(i, i ^ step) for i in range(lax.axis_size(axis))])


def from_behind(block, axis, distance):
    devices = range(lax.axis_size(axis))
    route = [(i - distance, i) for i in devices if i - distance in devices]
    return lax.ppermute(block, axis, route)


def ladder_sum(values, axis):
    step = 1
    while step < lax.axis_size(axis):
        got = swap_with(values.astype(bf16), axis, step)
        values = values + got.astype(f32)
        step *= 2
    return values


def to_everyone(spread, groups=None):
    return lax.all_to_all(spread, ("rows", "ch"), 0, 0, axis_index_groups=groups, tiled=True)


def small_total(spread):
    return jnp.sum(to_everyone(spread), axis=0).reshape(2, -1)


def wide_total(block):
    devices = lax.axis_size("rows") * lax.axis_size("ch")
    core = lax.axis_index("ch") % 2
    above, below = block.reshape(2, -1, 128)
    half = jnp.where(core == 0, above, below) + swap_with(jnp.where(core == 0, below, above), "ch", 1)
    groups = [[i * 2 + k for i in range(devices // 2)] for k in range(2)]
    half = jnp.broadcast_to(half[None], (devices // 2,) + half.shape)
    half = jnp.sum(to_everyone(half, groups), axis=0)
    other = swap_with(half, "ch", 1)
    whole = jnp.stack([jnp.where(core == 0, half, other), jnp.where(core == 0, other, half)])
    whole = whole.reshape(-1, 2, STEP)
    return whole[:, 0].reshape(-1), whole[:, 1].reshape(-1)


def forward_rows(sums, gain, shift, count):
    mean = sums[0] / count
    scale = lax.rsqrt(sums[1] / count - mean * mean + EPSILON)
    return jnp.stack([scale * gain, shift - mean * scale * gain, scale, -mean * scale])


def backward_rows(sums, par, count):
    rows = jnp.stack([par[0], par[0] * sums[0] / count, par[0] * sums[1] / count])
    return rows, own_slice(sums[1]), own_slice(sums[0])


def own_slice(full):
    size = full.shape[0] // lax.axis_size("ch")
    return lax.dynamic_slice_in_dim(full, lax.axis_index("ch") * size, size)


def gather_weight(weight):
    return lax.all_gather(weight.astype(bf16), "ch", axis=0, tiled=True)


def gather_weight_after(weight, *after):
    return lax.all_gather(cast_after(weight, *after), "ch", axis=0, tiled=True)


def gather_by_swaps(weight):
    ch = lax.axis_size("ch")
    came = None
    held = weight.astype(bf16)[None]
    step = ch // 2
    while step >= 1:
        got = swap_with(held, "ch", step)
        came = got if came is None else came
        odd = lax.axis_index("ch") // step % 2 == 1
        held = jnp.stack([jnp.where(odd, got, held), jnp.where(odd, held, got)], axis=1)
        held = held.reshape((-1,) + held.shape[2:])
        step //= 2
    return held.reshape((-1,) + weight.shape[1:]), came


def pick(values, bit):
    return lax.dynamic_index_in_dim(values, bit, 1, keepdims=False)


def scatter_ch(gradient):
    return lax.psum_scatter(gradient, "ch", scatter_dimension=0, tiled=True)


def split(total, axis, step):
    bit = lax.axis_index(axis) // step % 2
    pairs = total.reshape((total.shape[0] // 2, 2) + total.shape[1:])
    return swap_with(pick(pairs, 1 - bit), axis, step), pick(pairs, bit)


def added(pair):
    got, kept = pair
    return (got.astype(f32) + kept.astype(f32)).astype(bf16)


def rest_of(total, axis, step=1):
    while step < lax.axis_size(axis):
        total = added(split(total, axis, step))
        step *= 2
    return total


def by_owner(gradient, axis="ch"):
    count = lax.axis_size(axis)
    return gradient.reshape((count, gradient.shape[0] // count) + gradient.shape[1:])


def by_row_tile(parts):
    return by_owner(jnp.concatenate(parts, axis=1), "rows")


def rows_gather(total, widths):
    step = lax.axis_size("rows")
    while step > 1:
        step //= 2
        odd = lax.axis_index("rows") // step % 2 == 1
        got = swap_with(total, "rows", step)
        total = jnp.stack([jnp.where(odd, got, total), jnp.where(odd, total, got)], axis=1)
        total = total.reshape((-1,) + total.shape[2:])
    total = total.reshape(-1, total.shape[2]).astype(f32)
    ends, at = [], 0
    for width in widths:
        ends.append(total[:, at : at + width])
        at += width
    return ends


def blocks_to_lanes(values, base):
    return jnp.concatenate([values[r : r + base] for r in range(0, values.shape[0], base)], axis=1)


def lanes_to_blocks(values, wide):
    return jnp.concatenate(
        [values[:, c : c + wide] for c in range(0, values.shape[1], wide)], axis=0
    )


def deep_rows(tile):
    odd = lax.axis_index("rows") % 2 == 1
    images = [tile[b] for b in range(tile.shape[0])]
    far = [(from_behind(own, "rows", 2), from_behind(own, "rows", -2)) for own in images]
    partner = [swap_with(own, "rows", 1) for own in images]
    passed = [swap_with(jnp.where(odd, up, down), "rows", 1) for up, down in far]
    tiles = []
    for own, (far_up, far_down), near, other in zip(images, far, partner, passed):
        tiles += [far_up, jnp.where(odd, near, other), own, jnp.where(odd, other, near), far_down]
    return tiles


def deep_return(tiles):
    odd = lax.axis_index("rows") % 2 == 1
    images = [tiles[t : t + 5] for t in range(0, len(tiles), 5)]
    passed = [swap_with(jnp.where(odd, down, up), "rows", 1) for _, up, _, down, _ in images]
    partner = [swap_with(jnp.where(odd, up, down), "rows", 1) for _, up, _, down, _ in images]
    pieces = []
    for (far_up, _, own, _, far_down), got, near in zip(images, passed, partner):
        total = added((jnp.where(odd, far_up, far_down), got))
        below = from_behind(jnp.where(odd, total, far_up), "rows", -2)
        above = from_behind(jnp.where(odd, far_down, total), "rows", 2)
        pieces += [own, near, below, above]
    return pieces


def near_rows(tile, width):
    size = 2 * width
    above = from_behind(tile[:, -size:], "rows", 1)
    below = from_behind(tile[:, :size], "rows", -1)
    return jnp.concatenate([above, tile, below], axis=1)


def per_device(
    inputs,
    heights,
    displacements,
    reduce_one,
    reduce_gain_one,
    reduce_bias_one,
    offset_weight,
    deform_weight,
    deform_gain,
    deform_bias,
    expand_one,
    expand_gain_one,
    expand_bias_one,
    reduce_two,
    reduce_gain_two,
    reduce_bias_two,
    conv_weight,
    conv_gain,
    conv_bias,
    expand_two,
    expand_gain_two,
    expand_bias_two,
    cotangent,
):
    batch, rows, width, channels = inputs.shape
    pixels = rows * width
    n = batch * pixels
    own_heights = lax.dynamic_slice_in_dim(heights, lax.axis_index("ch") * batch, batch)
    rows_here = lax.axis_index("rows") * rows + jnp.arange(rows, dtype=jnp.int32)
    mask = (rows_here[None, :] < own_heights[:, None]).astype(f32)
    mask = jnp.broadcast_to(mask[:, :, None], (batch, rows, width)).reshape(n, 1)
    mask_wide = jnp.broadcast_to(mask, (n, 128))
    count = jnp.sum(heights).astype(f32) * width

    offset_rows = offset_weight.astype(bf16).reshape(3, 6, 3, 3, MID).transpose(2, 3, 0, 1, 4)
    offset_rows = jnp.pad(offset_rows, ((0, 0), (0, 0), (0, 1), (0, 2), (0, 0))).reshape(3, 96, MID)
    disp = jnp.pad(displacements.reshape(3, 6, batch, pixels), ((0, 0), (0, 2), (0, 0), (0, 0)))
    disp = disp.transpose(2, 0, 1, 3)

    reduce_full, came = gather_by_swaps(reduce_one)
    deform_full = gather_weight_after(deform_weight, came)
    expand_full, reduce_full_two, conv_full, expand_full_two = [
        gather_weight(w) for w in (expand_one, reduce_two, conv_weight, expand_two)
    ]

    devices = lax.axis_size("rows") * lax.axis_size("ch")
    acts = inputs.reshape(n, channels)
    acts_low, y_a, spread = product_forward(acts, mask_wide, reduce_full, devices)
    par_a = forward_rows(small_total(spread), reduce_gain_one, reduce_bias_one, count)
    hidden = (gelu(y_a * par_a[0] + par_a[1]) * mask).astype(bf16)
    near_tiles = deep_rows(hidden.reshape(batch, pixels, MID))
    columns, y_b, fraction, spread = deform_forward(
        near_tiles, offset_rows, disp, deform_full, mask_wide, rows, width, devices
    )
    par_b = forward_rows(small_total(spread), deform_gain, deform_bias, count)
    middle, y_c, block = expand_forward(y_b, par_b, mask_wide, expand_full)
    par_c = forward_rows(wide_total(block), expand_gain_one, expand_bias_one, count)

    first_low, y_d, spread = first_forward(y_c, par_c, acts, mask_wide, reduce_full_two, devices)
    par_d = forward_rows(small_total(spread), reduce_gain_two, reduce_bias_two, count)
    hidden_two = (gelu(y_d * par_d[0] + par_d[1]) * mask).astype(bf16)
    rimmed = near_rows(hidden_two.reshape(batch, pixels, MID), width)
    y_e, spread = conv_forward(rimmed, conv_full, mask_wide, rows, width, devices)
    par_e = forward_rows(small_total(spread), conv_gain, conv_bias, count)
    middle_two, y_f, block = expand_forward(y_e, par_e, mask_wide, expand_full_two)
    par_f = forward_rows(wide_total(block), expand_gain_two, expand_bias_two, count)

    output, dt_f, block = output_stage(y_f, par_f, first_low, cotangent.reshape(n, channels), mask_wide)
    back_f, expand_gain_two_grad, expand_bias_two_grad = backward_rows(wide_total(block), par_f, count)
    dy_f, dt_e, spread = expand_backward(
        dt_f, y_f, par_f, back_f, mask_wide, expand_full_two, y_e, par_e, devices
    )
    expand_two_local = dot(dy_f, middle_two, TN).astype(bf16)
    expand_two_part = scatter_ch(expand_two_local)
    back_e, conv_gain_grad, conv_bias_grad = backward_rows(small_total(spread), par_e, count)
    dy_e = norm_gradient(dt_e, y_e, par_e, back_e, mask).astype(bf16)
    dy_e_rim = near_rows(dy_e.reshape(batch, pixels, MID), width)
    conv_local = conv_weight_gradient(dy_e, rimmed, rows, width, (expand_two_local,))
    conv_part = scatter_ch(conv_local)
    dt_d, spread = conv_backward(
        dy_e_rim, conv_full, y_d, par_d, mask_wide, rows, width, devices, (conv_local,)
    )
    base = conv_part.shape[0]
    expand_two_part = blocks_to_lanes(expand_two_part, base)
    back_d, reduce_gain_two_grad, reduce_bias_two_grad = backward_rows(small_total(spread), par_d, count)
    dy_d, dt_c, block = residual_backward(
        dt_d, y_d, par_d, back_d, mask_wide, reduce_full_two, dt_f, y_c, par_c, acts_low
    )
    reduce_two_local = dot(dy_d, first_low, TN).astype(bf16)
    red_two = split(by_owner(reduce_two_local), "ch", 1)

    back_c, expand_gain_one_grad, expand_bias_one_grad = backward_rows(wide_total(block), par_c, count)
    dy_c, dt_b, spread, kept = expand_backward(
        dt_c, y_c, par_c, back_c, mask_wide, expand_full, y_b, par_b, devices, (red_two[1],)
    )
    red_two = split(added((red_two[0], kept)), "ch", 2)
    expand_one_local = dot(dy_c, middle, TN).astype(bf16)
    exp_one = split(by_owner(expand_one_local), "ch", 1)
    back_b, deform_gain_grad, deform_bias_grad = backward_rows(small_total(spread), par_b, count)
    dy_b = norm_gradient(dt_b, y_b, par_b, back_b, mask).astype(bf16)
    deform_local, *kept = columns_weight_gradient(dy_b, columns, (red_two[1], exp_one[1]))
    deform_part = scatter_ch(deform_local)
    reduce_two_part = rest_of(added((red_two[0], kept[0])), "ch", 4)[0]
    exp_one = split(added((exp_one[0], kept[1])), "ch", 2)
    batch_p = split(by_row_tile([conv_part, expand_two_part]), "rows", 1)
    *tiles, offset_local, reduce_two_part, kept_one, kept_p = deform_backward(
        near_tiles, offset_rows, disp, fraction, deform_full, dy_b, rows, width,
        (), (reduce_two_part, exp_one[1], batch_p[1]),
    )
    batch_p = split(added((batch_p[0], kept_p)), "rows", 2)
    expand_one_part = rest_of(added((exp_one[0], kept_one)), "ch", 4)[0]
    batch_q = by_row_tile([reduce_two_part, blocks_to_lanes(expand_one_part, base)])
    dt_a, spread, kept_p, batch_q = hidden_backward(
        deep_return(tiles), y_a, par_a, mask_wide, devices, (batch_p[1], batch_q)
    )
    batch_p = split(added((batch_p[0], kept_p)), "rows", 4)
    batch_q = split(batch_q, "rows", 1)
    back_a, reduce_gain_one_grad, reduce_bias_one_grad = backward_rows(small_total(spread), par_a, count)
    dy_a, kept_p, kept_q = mid_gradient(dt_a, y_a, par_a, back_a, mask_wide, (batch_p[1], batch_q[1]))
    reduce_one_local = dot(dy_a, acts_low, TN).astype(bf16)
    red_one = split(by_owner(reduce_one_local), "ch", 1)
    input_grad, kept = input_backward(dy_a, reduce_full, dt_c, (red_one[1],))
    reduce_one_part = rest_of(added((red_one[0], kept)), "ch", 2)[0]
    offset_part = ladder_sum(offset_local.reshape(-1, MID), "ch").astype(bf16)
    offset_part = jnp.pad(offset_part, ((0, -offset_part.shape[0] % base), (0, 0)))
    offset_part = blocks_to_lanes(offset_part, base)
    conv_weight_grad, expand_two_grad = rows_gather(
        rest_of(added((batch_p[0], kept_p)), "rows", 8), (9 * MID, channels)
    )
    reduce_two_grad, expand_one_grad = rows_gather(
        rest_of(added((batch_q[0], kept_q)), "rows", 2), (channels, channels)
    )
    (deform_weight_grad,) = rows_gather(rest_of(by_row_tile([deform_part]), "rows"), (9 * MID,))
    reduce_one_grad, offset_grad = rows_gather(
        rest_of(by_row_tile([reduce_one_part, offset_part]), "rows"), (channels, offset_part.shape[1])
    )
    expand_two_grad = lanes_to_blocks(expand_two_grad, MID)
    expand_one_grad = lanes_to_blocks(expand_one_grad, MID)
    offset_grad = lanes_to_blocks(offset_grad, MID)[:288].reshape(3, 3, 4, 8, MID)[:, :, :3, :6]
    offset_weight_grad = offset_grad.transpose(2, 3, 0, 1, 4).reshape(18, 9 * MID)
    return (
        output.reshape(inputs.shape),
        input_grad.reshape(inputs.shape),
        reduce_one_grad,
        reduce_gain_one_grad,
        reduce_bias_one_grad,
        offset_weight_grad,
        deform_weight_grad,
        deform_gain_grad,
        deform_bias_grad,
        expand_one_grad,
        expand_gain_one_grad,
        expand_bias_one_grad,
        reduce_two_grad,
        reduce_gain_two_grad,
        reduce_bias_two_grad,
        conv_weight_grad,
        conv_gain_grad,
        conv_bias_grad,
        expand_two_grad,
        expand_gain_two_grad,
        expand_bias_two_grad,
    )


def solution(mesh):
    tiles = P("ch", "rows", None, None)
    owned = P("ch", None)
    block = (owned, P(), P())
    placed = (tiles, P(), P(None, "ch", "rows", None)) + block + (P(),) + 2 * block + 3 * block + (tiles,)
    grads = (owned, P("ch"), P("ch"))
    return jax.shard_map(
        per_device,
        mesh=mesh,
        in_specs=placed,
        out_specs=(tiles, tiles) + grads + (P(),) + 2 * grads + 3 * grads,
        check_vma=False,
    )
```

```python
import functools

import jax
import jax.numpy as jnp
from jax import lax
from jax.experimental import pallas as pl
from jax.experimental.pallas import tpu as pltpu
from jax.sharding import PartitionSpec as P

bf16 = jnp.bfloat16
f32 = jnp.float32
VMEM = pltpu.VMEM
HBM = pltpu.HBM
DMA = pltpu.SemaphoreType.DMA
MID = 512
STEP = 512
NT = (((1,), (1,)), ((), ()))
TN = (((0,), (0,)), ((), ()))
NN = (((1,), (0,)), ((), ()))
GELU_A = 0.7978845608028654
GELU_B = 0.044715


def dot(a, b, dims=NN):
    return lax.dot_general(a, b, dims, preferred_element_type=f32)


def shaped(*shape, dtype=f32):
    return jax.ShapeDtypeStruct(shape, dtype)


def without(body, n_in, n_after, n_out, n_through):
    first = n_in + n_after + n_through
    return lambda *refs: body(
        *refs[:n_in], *refs[first : first + n_out], *refs[first + n_out + n_through :]
    )


def cost(us):
    return pl.CostEstimate(flops=int(us * 0.4e9), bytes_accessed=int(us * 0.8e6), transcendentals=0)


def call(body, operands, places, outs, out_places, us, limit, scratch=(), after=(), through=()):
    def spec(place):
        return pl.BlockSpec(memory_space=HBM if place == "h" else VMEM)

    def pinned(value, place):
        if place == "v":
            return value
        return pltpu.with_memory_space_constraint(value, HBM if place == "h" else VMEM)

    def result(out, place):
        if place == "v":
            return out
        return (HBM if place == "h" else VMEM)(out.shape, out.dtype)

    n_in, n_out, n_after = len(operands), len(outs), len(after)
    kept = [pltpu.with_memory_space_constraint(v, HBM) for v in (*after, *through)]
    return pl.pallas_call(
        without(body, n_in, n_after, n_out, len(through)),
        in_specs=[spec(p) for p in places] + [spec("h")] * len(kept),
        out_specs=tuple(spec(p) for p in out_places) + (spec("h"),) * len(through),
        out_shape=tuple(result(o, p) for o, p in zip(outs, out_places))
        + tuple(HBM(v.shape, v.dtype) for v in through),
        input_output_aliases={n_in + n_after + t: n_out + t for t in range(len(through))},
        scratch_shapes=list(scratch),
        compiler_params=pltpu.CompilerParams(vmem_limit_bytes=limit * 2**20),
        cost_estimate=cost(us),
    )(*[pinned(v, p) for v, p in zip(operands, places)], *kept)


def moving(source, target, sem):
    copy = pltpu.make_async_copy(source, target, sem)
    copy.start()
    return copy


def columns_moving(source, target, sems, wide=STEP):
    return [
        moving(source.at[:, s * wide : (s + 1) * wide], target.at[:, s * wide : (s + 1) * wide], sems.at[s])
        for s in range(source.shape[1] // wide)
    ]


def rows_moving(source, target, sems, tall=STEP):
    return [
        moving(source.at[s * tall : (s + 1) * tall], target.at[s * tall : (s + 1) * tall], sems.at[s])
        for s in range(source.shape[0] // tall)
    ]


def blocks(wide):
    return [(s, slice(s * STEP, (s + 1) * STEP)) for s in range(wide // STEP)]


def gelu(v):
    return 0.5 * v * (1.0 + jnp.tanh(GELU_A * (v + GELU_B * v * v * v)))


def gelu_slope(v):
    t = jnp.tanh(GELU_A * (v + GELU_B * v * v * v))
    return 0.5 * (1.0 + t) + 0.5 * v * (1.0 - t * t) * (GELU_A * (1.0 + 3.0 * GELU_B * v * v))


def normed(values, par_ref, part=slice(None)):
    return values * par_ref[0:1, part] + par_ref[1:2, part]


def normal_of(values, par_ref, part=slice(None)):
    return values * par_ref[2:3, part] + par_ref[3:4, part]


def norm_gradient(upstream, values, par_ref, back_ref, mask, part=slice(None)):
    normal = normal_of(values, par_ref, part)
    return upstream * back_ref[0:1, part] - mask * (back_ref[1:2, part] + normal * back_ref[2:3, part])


def sums_block(weighted, values):
    n = weighted.shape[1] // 128
    sums = (
        jnp.sum(weighted, axis=0, keepdims=True),
        jnp.sum(weighted * values, axis=0, keepdims=True),
    )
    return jnp.concatenate([v[:, c * 128 : c * 128 + 128] for v in sums for c in range(n)], axis=0)


def write_stats(stat_ref, weighted, values):
    stat_ref[...] = jnp.broadcast_to(sums_block(weighted, values)[None], stat_ref.shape)


def product_forward_body(x_ref, mask_ref, w_ref, low_ref, out_ref, stat_ref, x_buf, low_buf, sems):
    wide = x_ref.shape[1]
    coming = columns_moving(x_ref, x_buf, sems.at[0])
    total, going = None, []
    for s, part in blocks(wide):
        coming[s].wait()
        low_buf[:, part] = x_buf[:, part].astype(bf16)
        going.append(moving(low_buf.at[:, part], low_ref.at[:, part], sems.at[1, s]))
        term = dot(low_buf[:, part], w_ref[:, part], NT)
        total = term if total is None else total + term
    out_ref[...] = total
    write_stats(stat_ref, total * mask_ref[:, 0:1], total)
    for copy in going:
        copy.wait()


def product_forward(x, mask_wide, weight, devices):
    n, wide = x.shape
    return call(
        product_forward_body,
        (x, mask_wide, weight),
        "hvv",
        (shaped(n, wide, dtype=bf16), shaped(n, MID), shaped(devices, 8, 128)),
        "hvv",
        5,
        20,
        [VMEM((n, wide), f32), VMEM((n, wide), bf16), DMA((2, wide // STEP))],
    )


def expand_forward_body(*refs):
    *y_refs, par_ref, mask_ref, e_ref, mid_ref, out_ref, stat_ref, e_buf, out_buf, sems = refs
    coming = rows_moving(e_ref, e_buf, sems.at[0])
    mask = mask_ref[:, 0:1]
    at = 0
    for y_ref in y_refs:
        part = slice(at, at + y_ref.shape[0])
        mid_ref[part, :] = (gelu(normed(y_ref[...], par_ref)) * mask_ref[part, 0:1]).astype(bf16)
        at += y_ref.shape[0]
    going = []
    for s, part in blocks(e_ref.shape[0]):
        coming[s].wait()
        out = dot(mid_ref[...], e_buf[part, :], NT)
        out_buf[:, part] = out.astype(bf16)
        going.append(moving(out_buf.at[:, part], out_ref.at[:, part], sems.at[1, s]))
        stat_ref[s * 8 : s * 8 + 8, :] = sums_block(out * mask, out)
    for copy in going:
        copy.wait()


def expand_forward(y_parts, par, mask_wide, weight):
    n, wide = mask_wide.shape[0], weight.shape[0]
    return call(
        expand_forward_body,
        (*y_parts, par, mask_wide, weight),
        "v" * (len(y_parts) + 2) + "h",
        (shaped(n, MID, dtype=bf16), shaped(n, wide, dtype=bf16), shaped(wide // 64, 128)),
        "vhv",
        4,
        16,
        [VMEM(weight.shape, bf16), VMEM((n, wide), bf16), DMA((2, wide // STEP))],
    )


def first_forward_body(
    y_ref, par_ref, x_ref, mask_ref, w_ref, low_ref, out_ref, stat_ref,
    y_buf, x_buf, w_buf, low_buf, sems
):
    wide = x_ref.shape[1]
    coming_y = columns_moving(y_ref, y_buf, sems.at[0])
    coming_x = columns_moving(x_ref, x_buf, sems.at[1])
    coming_w = columns_moving(w_ref, w_buf, sems.at[2])
    mask = mask_ref[:, 0:1]
    total, going = None, []
    for s, part in blocks(wide):
        coming_y[s].wait()
        coming_x[s].wait()
        first = gelu(normed(y_buf[:, part].astype(f32), par_ref, part) + x_buf[:, part]) * mask
        low_buf[:, part] = first.astype(bf16)
        going.append(moving(low_buf.at[:, part], low_ref.at[:, part], sems.at[3, s]))
        coming_w[s].wait()
        term = dot(low_buf[:, part], w_buf[:, part], NT)
        total = term if total is None else total + term
    out_ref[...] = total
    write_stats(stat_ref, total * mask, total)
    for copy in going:
        copy.wait()


def first_forward(y, par, x, mask_wide, weight, devices):
    n, wide = y.shape
    return call(
        first_forward_body,
        (y, par, x, mask_wide, weight),
        "hvhvh",
        (shaped(n, wide, dtype=bf16), shaped(n, MID), shaped(devices, 8, 128)),
        "hvv",
        6,
        24,
        [
            VMEM((n, wide), bf16),
            VMEM((n, wide), f32),
            VMEM(weight.shape, bf16),
            VMEM((n, wide), bf16),
            DMA((4, wide // STEP)),
        ],
    )


def output_stage_body(
    y_ref, par_ref, first_ref, cot_ref, mask_ref, out_ref, dt_ref, stat_ref,
    y_buf, first_buf, cot_buf, out_buf, dt_buf, sems
):
    wide = y_ref.shape[1]
    coming_y = columns_moving(y_ref, y_buf, sems.at[0])
    coming_f = columns_moving(first_ref, first_buf, sems.at[1])
    coming_c = columns_moving(cot_ref, cot_buf, sems.at[2])
    mask = mask_ref[:, 0:1]
    going = []
    for s, part in blocks(wide):
        coming_y[s].wait()
        coming_f[s].wait()
        y = y_buf[:, part].astype(f32)
        pre = normed(y, par_ref, part) + first_buf[:, part].astype(f32)
        t = jnp.tanh(GELU_A * (pre + GELU_B * pre * pre * pre))
        out_buf[:, part] = 0.5 * pre * (1.0 + t) * mask
        going.append(moving(out_buf.at[:, part], out_ref.at[:, part], sems.at[3, s]))
        slope = 0.5 * (1.0 + t) + 0.5 * pre * (1.0 - t * t) * (GELU_A * (1.0 + 3.0 * GELU_B * pre * pre))
        coming_c[s].wait()
        dt = slope * (cot_buf[:, part] * mask)
        dt_buf[:, part] = dt.astype(bf16)
        going.append(moving(dt_buf.at[:, part], dt_ref.at[:, part], sems.at[4, s]))
        stat_ref[s * 8 : s * 8 + 8, :] = sums_block(dt, normal_of(y, par_ref, part))
    for copy in going:
        copy.wait()


def output_stage(y, par, first, cot, mask_wide):
    n, wide = y.shape
    return call(
        output_stage_body,
        (y, par, first, cot, mask_wide),
        "hvhhv",
        (shaped(n, wide), shaped(n, wide, dtype=bf16), shaped(wide // 64, 128)),
        "hhv",
        8,
        28,
        [
            VMEM((n, wide), bf16),
            VMEM((n, wide), bf16),
            VMEM((n, wide), f32),
            VMEM((n, wide), f32),
            VMEM((n, wide), bf16),
            DMA((5, wide // STEP)),
        ],
    )


def expand_backward_body(
    dt_ref, y_ref, par_ref, back_ref, mask_ref, e_ref, mid_y_ref, mid_par_ref,
    dy_ref, mid_dt_ref, stat_ref, dt_buf, y_buf, e_buf, dy_buf, sems
):
    wide = dt_ref.shape[1]
    coming_dt = columns_moving(dt_ref, dt_buf, sems.at[0])
    coming_y = columns_moving(y_ref, y_buf, sems.at[1])
    coming_e = rows_moving(e_ref, e_buf, sems.at[2])
    mask = mask_ref[:, 0:1]
    total, going = None, []
    for s, part in blocks(wide):
        coming_dt[s].wait()
        coming_y[s].wait()
        dt, y = dt_buf[:, part].astype(f32), y_buf[:, part].astype(f32)
        dy = norm_gradient(dt, y, par_ref, back_ref, mask, part).astype(bf16)
        dy_buf[:, part] = dy
        going.append(moving(dy_buf.at[:, part], dy_ref.at[:, part], sems.at[3, s]))
        coming_e[s].wait()
        term = dot(dy, e_buf[part, :])
        total = term if total is None else total + term
    y = mid_y_ref[...]
    dt = gelu_slope(normed(y, mid_par_ref)) * (total * mask)
    mid_dt_ref[...] = dt
    write_stats(stat_ref, dt, normal_of(y, mid_par_ref))
    for copy in going:
        copy.wait()


def expand_backward(dt, y, par, back, mask_wide, weight, mid_y, mid_par, devices, through=()):
    n, wide = y.shape
    return call(
        expand_backward_body,
        (dt, y, par, back, mask_wide, weight, mid_y, mid_par),
        "hhvvvhvv",
        (shaped(n, wide, dtype=bf16), shaped(n, MID), shaped(devices, 8, 128)),
        "hvv",
        5,
        24,
        [
            VMEM((n, wide), bf16),
            VMEM((n, wide), bf16),
            VMEM(weight.shape, bf16),
            VMEM((n, wide), bf16),
            DMA((4, wide // STEP)),
        ],
        through=through,
    )


def residual_backward_body(
    dt_ref, y_ref, par_ref, back_ref, mask_ref, w_ref, add_ref, wide_y_ref, wide_par_ref, x_ref,
    dy_ref, out_ref, stat_ref, w_buf, add_buf, y_buf, x_buf, out_buf, sems
):
    wide = x_ref.shape[1]
    coming = [
        columns_moving(source, target, sems.at[t])
        for t, (source, target) in enumerate(
            ((w_ref, w_buf), (add_ref, add_buf), (wide_y_ref, y_buf), (x_ref, x_buf))
        )
    ]
    mask = mask_ref[:, 0:1]
    dy_ref[...] = norm_gradient(dt_ref[...], y_ref[...], par_ref, back_ref, mask).astype(bf16)
    going = []
    for s, part in blocks(wide):
        for copies in coming:
            copies[s].wait()
        grad = add_buf[:, part].astype(f32) + dot(dy_ref[...], w_buf[:, part])
        y = y_buf[:, part].astype(f32)
        pre = normed(y, wide_par_ref, part) + x_buf[:, part].astype(f32)
        dt = gelu_slope(pre) * (grad * mask)
        out_buf[:, part] = dt.astype(bf16)
        going.append(moving(out_buf.at[:, part], out_ref.at[:, part], sems.at[4, s]))
        stat_ref[s * 8 : s * 8 + 8, :] = sums_block(dt, normal_of(y, wide_par_ref, part))
    for copy in going:
        copy.wait()


def residual_backward(dt, y, par, back, mask_wide, weight, add, wide_y, wide_par, x):
    n, wide = x.shape
    return call(
        residual_backward_body,
        (dt, y, par, back, mask_wide, weight, add, wide_y, wide_par, x),
        "vvvvvhhhvh",
        (shaped(n, MID, dtype=bf16), shaped(n, wide, dtype=bf16), shaped(wide // 64, 128)),
        "vhv",
        6,
        24,
        [VMEM(weight.shape, bf16)] + [VMEM((n, wide), bf16)] * 4 + [DMA((5, wide // STEP))],
    )


def input_backward_body(dy_ref, w_ref, add_ref, out_ref, w_buf, add_buf, out_buf, sems):
    coming_w = columns_moving(w_ref, w_buf, sems.at[0])
    coming_a = columns_moving(add_ref, add_buf, sems.at[1])
    going = []
    for s, part in blocks(w_ref.shape[1]):
        coming_w[s].wait()
        coming_a[s].wait()
        out_buf[:, part] = add_buf[:, part].astype(f32) + dot(dy_ref[...], w_buf[:, part])
        going.append(moving(out_buf.at[:, part], out_ref.at[:, part], sems.at[2, s]))
    for copy in going:
        copy.wait()


def input_backward(dy, weight, add, through):
    n, wide = add.shape
    return call(
        input_backward_body,
        (dy, weight, add),
        "vhh",
        (shaped(n, wide),),
        "h",
        5,
        20,
        [VMEM(weight.shape, bf16), VMEM((n, wide), bf16), VMEM((n, wide), f32), DMA((3, wide // STEP))],
        through=through,
    )


def hidden_backward_body(*refs):
    *piece_refs, y_ref, par_ref, mask_ref, dt_ref, stat_ref = refs
    batch = len(piece_refs) // 4
    pixels = y_ref.shape[0] // batch
    for b in range(batch):
        own, near, up, down = [ref[...].astype(f32) for ref in piece_refs[4 * b : 4 * b + 4]]
        dt_ref[b * pixels : (b + 1) * pixels, :] = own + near + up + down
    grad = dt_ref[...]
    y = y_ref[...]
    dt = gelu_slope(normed(y, par_ref)) * (grad * mask_ref[:, 0:1])
    dt_ref[...] = dt
    write_stats(stat_ref, dt, normal_of(y, par_ref))


def hidden_backward(pieces, y, par, mask_wide, devices, through):
    n = y.shape[0]
    return call(
        hidden_backward_body,
        (*pieces, y, par, mask_wide),
        "v" * (len(pieces) + 3),
        (shaped(n, MID), shaped(devices, 8, 128)),
        "vv",
        3,
        16,
        through=through,
    )


def mid_gradient_body(dt_ref, y_ref, par_ref, back_ref, mask_ref, dy_ref):
    dy = norm_gradient(dt_ref[...], y_ref[...], par_ref, back_ref, mask_ref[:, 0:1])
    dy_ref[...] = dy.astype(bf16)


def mid_gradient(dt, y, par, back, mask_wide, through):
    return call(
        mid_gradient_body,
        (dt, y, par, back, mask_wide),
        "vvvvv",
        (shaped(*y.shape, dtype=bf16),),
        "v",
        2,
        12,
        through=through,
    )


def cast_body(v_ref, out_ref):
    out_ref[...] = v_ref[...].astype(bf16)


def cast_after(values, *after):
    return call(cast_body, (values,), "v", (shaped(*values.shape, dtype=bf16),), "v", 2, 12, after=after)[0]


def pack_body(*refs, count, bit_axis, rows):
    part_refs, (send_ref, keep_ref), refs = refs[:count], refs[count : count + 2], refs[count + 2 :]
    buffers, (in_sem, out_sem) = refs[:count], refs[count:]
    coming = [moving(ref, buf, in_sem.at[t]) for t, (ref, buf) in enumerate(zip(part_refs, buffers))]
    bit = lax.axis_index(bit_axis) % 2
    tall = send_ref.shape[1]
    base = rows * tall
    going, at = [], 0
    for copy, buf in zip(coming, buffers):
        copy.wait()
        wide = buf.shape[1]
        for block in range(buf.shape[0] // base):
            for pair in range(rows // 2):
                for out_ref, side in ((send_ref, 1 - bit), (keep_ref, bit)):
                    row = pl.multiple_of(block * base + (2 * pair + side) * tall, 16)
                    going.append(
                        moving(
                            buf.at[pl.ds(row, tall), :],
                            out_ref.at[pair, :, at : at + wide],
                            out_sem.at[len(going)],
                        )
                    )
            at += wide
    for copy in going:
        copy.wait()


def pack_split(parts, base, rows):
    count = len(parts)
    blocks_in = sum(p.shape[0] // base for p in parts)
    wide = sum(p.shape[0] // base * p.shape[1] for p in parts)
    half = shaped(rows // 2, base // rows, wide, dtype=bf16)
    return call(
        functools.partial(pack_body, count=count, bit_axis="rows", rows=rows),
        tuple(parts),
        "h" * count,
        (half, half),
        "hh",
        3,
        16,
        [VMEM(p.shape, bf16) for p in parts] + [DMA((count,)), DMA((blocks_in * rows,))],
    )


def step_body(got_ref, kept_ref, send_ref, keep_ref, sum_ref, *, step):
    bit = lax.axis_index("rows") // step % 2
    sum_ref[...] = (got_ref[...].astype(f32) + kept_ref[...].astype(f32)).astype(bf16)
    for pair in range(send_ref.shape[0]):
        send_ref[pair] = sum_ref[2 * pair + 1 - bit]
        keep_ref[pair] = sum_ref[2 * pair + bit]


def step_split(got, kept, step):
    half = shaped(got.shape[0] // 2, *got.shape[1:], dtype=bf16)
    return call(
        functools.partial(step_body, step=step),
        (got, kept),
        "vv",
        (half, half),
        "vv",
        2,
        12,
        [VMEM(got.shape, bf16)],
    )


def return_body(*refs, batch):
    ins, outs = refs[: 5 * batch], refs[5 * batch :]
    odd = lax.axis_index("rows") % 2 == 1
    for b in range(batch):
        far_up_ref, up_ref, down_ref, far_down_ref, got_ref = ins[5 * b : 5 * b + 5]
        below_ref, above_ref, partner_ref = outs[3 * b : 3 * b + 3]

        @pl.when(odd)
        def _():
            total = far_up_ref[...].astype(f32) + got_ref[...].astype(f32)
            below_ref[...] = total.astype(bf16)
            above_ref[...] = far_down_ref[...]
            partner_ref[...] = up_ref[...]

        @pl.when(jnp.logical_not(odd))
        def _():
            total = far_down_ref[...].astype(f32) + got_ref[...].astype(f32)
            below_ref[...] = far_up_ref[...]
            above_ref[...] = total.astype(bf16)
            partner_ref[...] = down_ref[...]


def return_step(tiles, got):
    far_up, up, _, down, far_down = tiles
    piece = shaped(*got.shape, dtype=bf16)
    return call(
        functools.partial(return_body, batch=1),
        (far_up, up, down, far_down, got),
        "vvvvv",
        (piece, piece, piece),
        "vvv",
        2,
        12,
    )


def shift_lanes(values, by, width):
    place = lax.broadcasted_iota(jnp.int32, values.shape, values.ndim - 1) % width
    moved = pltpu.roll(values, by % values.shape[-1], values.ndim - 1)
    return jnp.where((place >= by) & (place < width + by), moved, 0.0)


def shift_rows(values, by, width):
    place = lax.broadcasted_iota(jnp.int32, values.shape, 0) % width
    moved = pltpu.roll(values, by % values.shape[0], 0)
    return jnp.where((place >= by) & (place < width + by), moved, 0.0)


def offset_fraction(ext_ref, ow_ref, b, base, pixels, width):
    u = None
    for i in range(3):
        start = (base + 2 * i) * width
        term = dot(ow_ref[i], ext_ref[b, start : start + pixels, :], NT)
        u = term if u is None else u + term
    total = u[32:64]
    total = total + shift_lanes(u[0:32], 2, width) + shift_lanes(u[64:96], -2, width)
    return 1.0 / (1.0 + jnp.exp(-total))


def tiles_moving(tiles, ext_ref, pixels, sems):
    return [
        moving(ref, ext_ref.at[t // 5, t % 5 * pixels : (t % 5 + 1) * pixels, :], sems.at[t])
        for t, ref in enumerate(tiles)
    ]


def deform_forward_body(*refs, rows, width, deep, before):
    tile_refs, refs = refs[:5], refs[5:]
    if before:
        (before_ref, refs) = refs[0], refs[1:]
    ow_ref, disp_ref, m_ref, mask_ref, cols_out_ref, y_ref, frac_ref, stat_ref = refs[:8]
    ext_ref, par_ref, s_ref, cols_ref, m_buf, tile_sems, sems = refs[8:]
    pixels = rows * width
    batch = 1
    coming = tiles_moving(tile_refs, ext_ref, pixels, tile_sems)
    coming_m = moving(m_ref, m_buf, sems.at[0])
    for copy in coming:
        copy.wait()
    lane = lax.broadcasted_iota(jnp.int32, (32, 128), 1)
    column = lane % width
    upper = lane // width

    def image(b, carry):
        frac = offset_fraction(ext_ref, ow_ref, b, deep - 2, pixels, width)
        for i in range(4):
            frac_ref[b, i] = frac[i * 8 : i * 8 + 8]
        pix = lax.broadcasted_iota(jnp.int32, (1, pixels), 1)
        row_at, col_at = pix // width, pix % width
        tops, lefts, ys, xs = [], [], [], []
        for k in range(9):
            i, j = k // 3, k % 3
            tops.append(row_at + disp_ref[b, i, 2 * j : 2 * j + 1, :] + (deep - 2))
            lefts.append(col_at + 2 * (j - 1) + disp_ref[b, i, 2 * j + 1 : 2 * j + 2, :])
            at = i * 8 + 2 * j
            ys.append(frac[at : at + 1])
            xs.append(frac[at + 1 : at + 2])
        blank = jnp.zeros((23, pixels), f32)
        par = jnp.concatenate(
            [jnp.concatenate(g, axis=0).astype(f32) if g is not None else blank
             for g in (tops, None, lefts, None, ys, None, xs, None)], axis=0)
        par_ref[...] = par.T

        def row_of_taps(i, carry):
            for j in range(3):
                k = i * 3 + j
                for c in range(pixels // 32):
                    p = pltpu.roll(par_ref[c * 32 : c * 32 + 32, :], 128 - k, 1)
                    wide = (32, 128)
                    top = jnp.broadcast_to(p[:, 0:1], wide).astype(jnp.int32) - upper
                    left = jnp.broadcast_to(p[:, 32:33], wide).astype(jnp.int32)
                    fy = jnp.broadcast_to(p[:, 64:65], wide)
                    fx = jnp.broadcast_to(p[:, 96:97], wide)
                    cw = jnp.where(column == left, 1.0 - fx, jnp.where(column == left + 1, fx, 0.0))
                    ca, cb = (1.0 - fy) * cw, fy * cw
                    for q in range(8):
                        s = jnp.where(top == 2 * q, ca, jnp.where(top == 2 * q - 1, cb, 0.0))
                        s_ref[j * pixels + c * 32 : j * pixels + c * 32 + 32, q * 128 : q * 128 + 128] = s.astype(bf16)
            start = pl.multiple_of(i * 2 * width, 128)
            window = ext_ref[b, pl.ds(start, 16 * width), :]
            for j in range(3):
                got = dot(s_ref[j * pixels : (j + 1) * pixels, :], window).astype(bf16)
                cols_ref[pl.ds(pl.multiple_of(b * pixels, pixels), pixels), pl.ds(pl.multiple_of((i * 3 + j) * MID, MID), MID)] = got
            return carry

        return lax.fori_loop(0, 3, row_of_taps, carry)

    image(0, 0)
    going = moving(cols_ref, cols_out_ref, sems.at[1])
    coming_m.wait()
    y = dot(cols_ref[...], m_buf[...], NT)
    y_ref[...] = y
    block = sums_block(y * mask_ref[:, 0:1], y)
    if before:
        block = block + before_ref[...]
    stat_ref[...] = jnp.broadcast_to(block, stat_ref.shape)
    going.wait()


def deform_forward(tiles, offset_rows, disp, weight, mask_wide, rows, width, stat_shape, before=()):
    pixels = rows * width
    return call(
        functools.partial(deform_forward_body, rows=rows, width=width, deep=2 * rows, before=bool(before)),
        (*tiles, *before, offset_rows, disp, weight, mask_wide),
        "hhhhh" + "v" * len(before) + "vvhv",
        (shaped(pixels, 9 * MID, dtype=bf16), shaped(pixels, MID), shaped(1, 4, 8, pixels), shaped(*stat_shape)),
        "hvvv",
        8,
        24,
        [
            VMEM((1, 5 * pixels, MID), bf16),
            VMEM((pixels, 128), f32),
            VMEM((3 * pixels, 16 * width), bf16),
            VMEM((pixels, 9 * MID), bf16),
            VMEM(weight.shape, bf16),
            DMA((5,)),
            DMA((2,)),
        ],
    )


def deform_backward_body(*refs, rows, width, deep):
    tile_refs, refs = refs[:5], refs[5:]
    (ow_ref, disp_ref, frac_ref, m_ref, dy_ref), refs = refs[:5], refs[5:]
    out_refs, refs = refs[:5], refs[5:]
    dow_ref, ext_ref, dext_ref, dc_ref, g_ref, st_ref, df_ref, m_buf, tile_sems, m_sems = refs
    pixels = rows * width
    batch = 1
    coming = tiles_moving(tile_refs, ext_ref, pixels, tile_sems)
    coming_m = taps_moving(m_ref, m_buf, m_sems)
    window = 16 * width
    dow_ref[...] = jnp.zeros_like(dow_ref)
    dext_ref[...] = jnp.zeros_like(dext_ref)
    for copy in coming:
        copy.wait()

    def image(b, carry):
        def row_of_taps(i, carry):
            dy = dy_ref[...]
            for j in range(3):
                m = m_buf[:, (i * 3 + j) * MID : (i * 3 + j + 1) * MID]
                dc_ref[j * pixels : (j + 1) * pixels, :] = dot(dy, m).astype(bf16)
            start = i * 2 * width
            g_ref[...] = dot(ext_ref[b, pl.ds(start, window), :], dc_ref[...], NT)
            place = lax.broadcasted_iota(jnp.int32, (width, 128), 0)
            for j in range(3):
                for h in range(pixels // 128):
                    lanes = slice(h * 128, h * 128 + 128)
                    at_l = slice(j * pixels + h * 128, j * pixels + h * 128 + 128)
                    pix = lax.broadcasted_iota(jnp.int32, (1, 128), 1) + h * 128
                    by_y, by_x = slice(2 * j, 2 * j + 1), slice(2 * j + 1, 2 * j + 2)
                    top = pix // width + disp_ref[b, i, by_y, lanes] + (deep - 2)
                    left = pix % width + 2 * (j - 1) + disp_ref[b, i, by_x, lanes]
                    fy = frac_ref[b, i, by_y, lanes]
                    fx = frac_ref[b, i, by_x, lanes]
                    here, after = place == left, place == left + 1
                    cw = jnp.where(here, 1.0 - fx, jnp.where(after, fx, 0.0))
                    ca, cb = (1.0 - fy) * cw, fy * cw
                    low_sum = jnp.zeros((width, 128), f32)
                    high_sum = jnp.zeros((width, 128), f32)
                    for r in range(16):
                        part = slice(r * width, r * width + width)
                        g = g_ref[part, at_l]
                        m0, m1 = top == r, top == r - 1
                        low_sum = low_sum + jnp.where(m0, g, 0.0)
                        high_sum = high_sum + jnp.where(m1, g, 0.0)
                        st_ref[part, at_l] = jnp.where(m0, ca, jnp.where(m1, cb, 0.0)).astype(bf16)
                    d_fy = jnp.sum((high_sum - low_sum) * cw, axis=0, keepdims=True)
                    mixed = (1.0 - fy) * low_sum + fy * high_sum
                    d_fx = jnp.sum(
                        jnp.where(after, mixed, 0.0) - jnp.where(here, mixed, 0.0), axis=0, keepdims=True)
                    df_ref[i, by_y, lanes] = d_fy * fy * (1.0 - fy)
                    df_ref[i, by_x, lanes] = d_fx * fx * (1.0 - fx)
            dext_ref[b, pl.ds(start, window), :] += dot(st_ref[...], dc_ref[...])
            return carry

        df_ref[...] = jnp.zeros_like(df_ref)
        for i in range(3):
            coming_m[i].wait()
            row_of_taps(i, carry)
        d_off = df_ref[...].reshape(32, pixels).astype(bf16).astype(f32)
        stacked = jnp.concatenate(
            [shift_lanes(d_off, -2, width), d_off, shift_lanes(d_off, 2, width)], axis=0)
        across = jnp.concatenate([stacked, jnp.zeros((32, pixels), f32)], axis=0).T.astype(bf16)
        stacked = stacked.astype(bf16)
        for i in range(3):
            first = (deep - 2 + 2 * i) * width
            part = slice(first, first + pixels)
            dow_ref[i] += dot(stacked, ext_ref[b, part, :])
            dext_ref[b, part, :] += dot(across[:, :96], ow_ref[i])
        return carry

    image(0, 0)
    for t, ref in enumerate(out_refs):
        ref[...] = dext_ref[t // 5, t % 5 * pixels : (t % 5 + 1) * pixels, :].astype(ref.dtype)


def deform_backward(tiles, offset_rows, disp, frac, weight, dy, rows, width, after, through):
    pixels = rows * width
    return call(
        functools.partial(deform_backward_body, rows=rows, width=width, deep=2 * rows),
        (*tiles, offset_rows, disp, frac, weight, dy),
        "hhhhhvvvhv",
        tuple(shaped(pixels, MID, dtype=f32 if t == 2 else bf16) for t in range(5)) + (shaped(3, 96, MID),),
        "vvvvvv",
        10,
        32,
        [
            VMEM((1, 5 * pixels, MID), bf16),
            VMEM((1, 5 * pixels, MID), f32),
            VMEM((3 * pixels, MID), bf16),
            VMEM((16 * width, 3 * pixels), f32),
            VMEM((16 * width, 3 * pixels), bf16),
            VMEM((4, 8, pixels), f32),
            VMEM(weight.shape, bf16),
            DMA((5,)),
            DMA((3,)),
        ],
        after,
        through,
    )


def taps_moving(m_ref, m_buf, sems):
    wide = 3 * MID
    return columns_moving(m_ref, m_buf, sems, wide)


def conv_forward_body(rim_ref, m_ref, mask_ref, y_ref, stat_ref, m_buf, sems, *, batch, rows, width):
    pixels = rows * width
    coming = taps_moving(m_ref, m_buf, sems)
    sums = [[None] * 3 for _ in range(batch)]
    for i in range(3):
        coming[i].wait()
        for b in range(batch):
            for j in range(3):
                k = i * 3 + j
                start = 2 * i * width
                term = dot(rim_ref[b, start : start + pixels, :], m_buf[:, k * MID : (k + 1) * MID], NT)
                sums[b][j] = term if i == 0 else sums[b][j] + term
    for b in range(batch):
        total = sums[b][1] + shift_rows(sums[b][0], 2, width) + shift_rows(sums[b][2], -2, width)
        y_ref[b * pixels : (b + 1) * pixels, :] = total
    y = y_ref[...]
    write_stats(stat_ref, y * mask_ref[:, 0:1], y)


def conv_forward(rim, weight, mask_wide, rows, width, devices):
    batch = rim.shape[0]
    n = batch * rows * width
    return call(
        functools.partial(conv_forward_body, batch=batch, rows=rows, width=width),
        (rim, weight, mask_wide),
        "vhv",
        (shaped(n, MID), shaped(devices, 8, 128)),
        "vv",
        5,
        24,
        [VMEM(weight.shape, bf16), DMA((3,))],
    )


def conv_backward_body(
    rim_ref, m_ref, y_ref, par_ref, mask_ref, dt_ref, stat_ref, m_buf, sems, *, batch, rows, width
):
    pixels = rows * width
    coming = taps_moving(m_ref, m_buf, sems)
    sums = [[None] * 3 for _ in range(batch)]
    for i in range(3):
        coming[i].wait()
        for b in range(batch):
            for j in range(3):
                k = i * 3 + j
                start = (4 - 2 * i) * width
                term = dot(rim_ref[b, start : start + pixels, :], m_buf[:, k * MID : (k + 1) * MID])
                sums[b][j] = term if i == 0 else sums[b][j] + term
    for b in range(batch):
        total = sums[b][1] + shift_rows(sums[b][0], -2, width) + shift_rows(sums[b][2], 2, width)
        dt_ref[b * pixels : (b + 1) * pixels, :] = total
    y = y_ref[...]
    dt = gelu_slope(normed(y, par_ref)) * (dt_ref[...] * mask_ref[:, 0:1])
    dt_ref[...] = dt
    write_stats(stat_ref, dt, normal_of(y, par_ref))


def conv_backward(rim, weight, y, par, mask_wide, rows, width, devices, after):
    batch = rim.shape[0]
    n = batch * rows * width
    return call(
        functools.partial(conv_backward_body, batch=batch, rows=rows, width=width),
        (rim, weight, y, par, mask_wide),
        "vhvvv",
        (shaped(n, MID), shaped(devices, 8, 128)),
        "vv",
        6,
        24,
        [VMEM(weight.shape, bf16), DMA((3,))],
        after,
    )


def conv_weight_body(dy_ref, rim_ref, out_ref, dyt_ref, out_buf, sems, *, batch, rows, width):
    pixels = rows * width
    dy = dy_ref[...].astype(f32)
    going = []
    for j in range(3):
        moved = shift_rows(dy, 2 * (j - 1), width) if j != 1 else dy
        dyt_ref[j] = moved.T.astype(bf16)
        for i in range(3):
            part = slice((i * 3 + j) * MID, (i * 3 + j + 1) * MID)
            start = 2 * i * width
            total = None
            for b in range(batch):
                term = dot(dyt_ref[j, :, b * pixels : (b + 1) * pixels], rim_ref[b, start : start + pixels, :])
                total = term if total is None else total + term
            out_buf[:, part] = total.astype(bf16)
            going.append(moving(out_buf.at[:, part], out_ref.at[:, part], sems.at[i * 3 + j]))
    for copy in going:
        copy.wait()


def conv_weight_gradient(dy, rim, rows, width, after):
    batch = rim.shape[0]
    return call(
        functools.partial(conv_weight_body, batch=batch, rows=rows, width=width),
        (dy, rim),
        "vv",
        (shaped(MID, 9 * MID, dtype=bf16),),
        "h",
        6,
        20,
        [VMEM((3, MID, batch * rows * width), bf16), VMEM((MID, 9 * MID), bf16), DMA((9,))],
        after,
    )[0]


def columns_weight_body(dy_ref, *refs):
    *cols_refs, out_ref, dyt_ref, cols_buf, out_buf, sems = refs
    pixels = cols_refs[0].shape[0]
    coming = [
        columns_moving(ref, cols_buf.at[b * pixels : (b + 1) * pixels], sems.at[b])
        for b, ref in enumerate(cols_refs)
    ]
    dyt_ref[...] = dy_ref[...].astype(f32).T.astype(bf16)
    going = []
    for s, part in blocks(out_ref.shape[1]):
        for copies in coming:
            copies[s].wait()
        out_buf[:, part] = dot(dyt_ref[...], cols_buf[:, part]).astype(bf16)
        going.append(moving(out_buf.at[:, part], out_ref.at[:, part], sems.at[len(cols_refs), s]))
    for copy in going:
        copy.wait()


def columns_weight_gradient(dy, cols_parts, through):
    n, wide = dy.shape[0], cols_parts[0].shape[1]
    return call(
        columns_weight_body,
        (dy, *cols_parts),
        "v" + "h" * len(cols_parts),
        (shaped(MID, wide, dtype=bf16),),
        "h",
        6,
        20,
        [
            VMEM((MID, n), bf16),
            VMEM((n, wide), bf16),
            VMEM((MID, wide), bf16),
            DMA((len(cols_parts) + 1, wide // STEP)),
        ],
        through=through,
    )


TILES = 2
EPSILON = 1e-05


def swap_with(values, axis, step):
    return lax.ppermute(values, axis, [(i, i ^ step) for i in range(lax.axis_size(axis))])


def from_behind(block, axis, distance):
    devices = range(lax.axis_size(axis))
    route = [(i - distance, i) for i in devices if i - distance in devices]
    return lax.ppermute(block, axis, route)


def ladder_sum(values, axis):
    step = 1
    while step < lax.axis_size(axis):
        got = swap_with(values.astype(bf16), axis, step)
        values = values + got.astype(f32)
        step *= 2
    return values


def to_everyone(spread, groups=None):
    return lax.all_to_all(spread, ("rows", "ch"), 0, 0, axis_index_groups=groups, tiled=True)


def small_total(spread):
    return jnp.sum(to_everyone(spread), axis=0).reshape(2, -1)


def wide_total(block):
    devices = lax.axis_size("rows") * lax.axis_size("ch")
    core = lax.axis_index("ch") % 2
    above, below = block.reshape(2, -1, 128)
    half = jnp.where(core == 0, above, below) + swap_with(jnp.where(core == 0, below, above), "ch", 1)
    groups = [[i * 2 + k for i in range(devices // 2)] for k in range(2)]
    half = jnp.broadcast_to(half[None], (devices // 2,) + half.shape)
    half = jnp.sum(to_everyone(half, groups), axis=0)
    other = swap_with(half, "ch", 1)
    whole = jnp.stack([jnp.where(core == 0, half, other), jnp.where(core == 0, other, half)])
    whole = whole.reshape(-1, 2, STEP)
    return whole[:, 0].reshape(-1), whole[:, 1].reshape(-1)


def forward_rows(sums, gain, shift, count):
    mean = sums[0] / count
    scale = lax.rsqrt(sums[1] / count - mean * mean + EPSILON)
    return jnp.stack([scale * gain, shift - mean * scale * gain, scale, -mean * scale])


def backward_rows(sums, par, count):
    rows = jnp.stack([par[0], par[0] * sums[0] / count, par[0] * sums[1] / count])
    return rows, own_slice(sums[1]), own_slice(sums[0])


def own_slice(full):
    size = full.shape[0] // lax.axis_size("ch")
    return lax.dynamic_slice_in_dim(full, lax.axis_index("ch") * size, size)


def gather_weight(weight):
    return lax.all_gather(weight.astype(bf16), "ch", axis=0, tiled=True)


def gather_weight_after(weight, *after):
    return lax.all_gather(cast_after(weight, *after), "ch", axis=0, tiled=True)


def gather_by_swaps(weight):
    ch = lax.axis_size("ch")
    came = None
    held = weight.astype(bf16)[None]
    step = ch // 2
    while step >= 1:
        got = swap_with(held, "ch", step)
        came = got if came is None else came
        odd = lax.axis_index("ch") // step % 2 == 1
        held = jnp.stack([jnp.where(odd, got, held), jnp.where(odd, held, got)], axis=1)
        held = held.reshape((-1,) + held.shape[2:])
        step //= 2
    return held.reshape((-1,) + weight.shape[1:]), came


def pick(values, bit):
    return lax.dynamic_index_in_dim(values, bit, 1, keepdims=False)


def scatter_ch(gradient):
    return lax.psum_scatter(gradient, "ch", scatter_dimension=0, tiled=True)


def split(total, axis, step):
    bit = lax.axis_index(axis) // step % 2
    pairs = total.reshape((total.shape[0] // 2, 2) + total.shape[1:])
    return swap_with(pick(pairs, 1 - bit), axis, step), pick(pairs, bit)


def added(pair):
    got, kept = pair
    return (got.astype(f32) + kept.astype(f32)).astype(bf16)


def rest_of(total, axis, step=1):
    while step < lax.axis_size(axis):
        total = added(split(total, axis, step))
        step *= 2
    return total


def by_owner(gradient, axis="ch"):
    count = lax.axis_size(axis)
    return gradient.reshape((count, gradient.shape[0] // count) + gradient.shape[1:])


def first_step(parts, base):
    rows = lax.axis_size("rows")
    if base // rows % 16 == 0:
        send, keep = pack_split(parts, base, rows)
        return swap_with(send, "rows", 1), keep
    return split(by_owner(jnp.concatenate([blocks_to_lanes(p, base) for p in parts], axis=1), "rows"), "rows", 1)


def next_step(pair, step):
    send, keep = step_split(*pair, step)
    return swap_with(send, "rows", step), keep


def last_steps(pair, step):
    while step < lax.axis_size("rows"):
        pair = next_step(pair, step)
        step *= 2
    return added(pair)


def rows_reduce(parts, base):
    return last_steps(first_step(parts, base), 2)


def blocks_to_lanes(values, base):
    return jnp.concatenate([values[r : r + base] for r in range(0, values.shape[0], base)], axis=1)


def lanes_to_blocks(values, wide):
    return jnp.concatenate(
        [values[:, c : c + wide] for c in range(0, values.shape[1], wide)], axis=0
    )


def joined(got, kept, step):
    odd = lax.axis_index("rows") // step % 2 == 1
    total = jnp.stack([jnp.where(odd, got, kept), jnp.where(odd, kept, got)], axis=1)
    return total.reshape((-1,) + total.shape[2:])


def last_joins(total, step):
    while step >= 1:
        total = joined(swap_with(total, "rows", step), total, step)
        step //= 2
    return total


def cut(total, widths):
    total = total.reshape(-1, total.shape[2]).astype(f32)
    ends, at = [], 0
    for width in widths:
        ends.append(total[:, at : at + width])
        at += width
    return ends


def deep_rows(tile):
    odd = lax.axis_index("rows") % 2 == 1
    images = [tile[b] for b in range(tile.shape[0])]
    far = [(from_behind(own, "rows", 2), from_behind(own, "rows", -2)) for own in images]
    partner = [swap_with(own, "rows", 1) for own in images]
    passed = [swap_with(jnp.where(odd, up, down), "rows", 1) for up, down in far]
    tiles = []
    for own, (far_up, far_down), near, other in zip(images, far, partner, passed):
        tiles += [far_up, jnp.where(odd, near, other), own, jnp.where(odd, other, near), far_down]
    return tiles


def deep_return(tiles):
    odd = lax.axis_index("rows") % 2 == 1
    _, up, own, down, _ = tiles
    got = swap_with(jnp.where(odd, down, up), "rows", 1)
    below, above, partner = return_step(tiles, got)
    below = from_behind(below, "rows", -2)
    above = from_behind(above, "rows", 2)
    return [own, swap_with(partner, "rows", 1), below, above]


def near_rows(tile, width):
    size = 2 * width
    above = from_behind(tile[:, -size:], "rows", 1)
    below = from_behind(tile[:, :size], "rows", -1)
    return jnp.concatenate([above, tile, below], axis=1)


def per_device(
    inputs,
    heights,
    displacements,
    reduce_one,
    reduce_gain_one,
    reduce_bias_one,
    offset_weight,
    deform_weight,
    deform_gain,
    deform_bias,
    expand_one,
    expand_gain_one,
    expand_bias_one,
    reduce_two,
    reduce_gain_two,
    reduce_bias_two,
    conv_weight,
    conv_gain,
    conv_bias,
    expand_two,
    expand_gain_two,
    expand_bias_two,
    cotangent,
):
    batch, rows, width, channels = inputs.shape
    pixels = rows * width
    n = batch * pixels
    own_heights = lax.dynamic_slice_in_dim(heights, lax.axis_index("ch") * batch, batch)
    rows_here = lax.axis_index("rows") * rows + jnp.arange(rows, dtype=jnp.int32)
    mask = (rows_here[None, :] < own_heights[:, None]).astype(f32)
    mask = jnp.broadcast_to(mask[:, :, None], (batch, rows, width)).reshape(n, 1)
    mask_wide = jnp.broadcast_to(mask, (n, 128))
    count = jnp.sum(heights).astype(f32) * width

    offset_rows = offset_weight.astype(bf16).reshape(3, 6, 3, 3, MID).transpose(2, 3, 0, 1, 4)
    offset_rows = jnp.pad(offset_rows, ((0, 0), (0, 0), (0, 1), (0, 2), (0, 0))).reshape(3, 96, MID)
    disp = jnp.pad(displacements.reshape(3, 6, batch, pixels), ((0, 0), (0, 2), (0, 0), (0, 0)))
    disp = disp.transpose(2, 0, 1, 3)

    reduce_full, came = gather_by_swaps(reduce_one)
    deform_full = gather_weight_after(deform_weight, came)
    expand_full, reduce_full_two, conv_full, expand_full_two = [
        gather_weight(w) for w in (expand_one, reduce_two, conv_weight, expand_two)
    ]

    devices = lax.axis_size("rows") * lax.axis_size("ch")
    acts = inputs.reshape(n, channels)
    acts_low, y_a, spread = product_forward(acts, mask_wide, reduce_full, devices)
    par_a = forward_rows(small_total(spread), reduce_gain_one, reduce_bias_one, count)
    hidden = (gelu(y_a * par_a[0] + par_a[1]) * mask).astype(bf16)
    near_tiles = deep_rows(hidden.reshape(batch, pixels, MID))
    columns, y_parts, fractions, sums = [], [], [], ()
    for b in range(batch):
        part = slice(b * pixels, (b + 1) * pixels)
        stat_shape = (devices, 8, 128) if b == batch - 1 else (8, 128)
        cols, y, frac, total = deform_forward(
            near_tiles[5 * b : 5 * b + 5], offset_rows, disp[b : b + 1], deform_full, mask_wide[part],
            rows, width, stat_shape, sums,
        )
        sums = (total,)
        columns.append(cols)
        y_parts.append(y)
        fractions.append(frac)
    y_b = jnp.concatenate(y_parts, axis=0)
    par_b = forward_rows(small_total(sums[0]), deform_gain, deform_bias, count)
    middle, y_c, block = expand_forward(y_parts, par_b, mask_wide, expand_full)
    par_c = forward_rows(wide_total(block), expand_gain_one, expand_bias_one, count)

    first_low, y_d, spread = first_forward(y_c, par_c, acts, mask_wide, reduce_full_two, devices)
    par_d = forward_rows(small_total(spread), reduce_gain_two, reduce_bias_two, count)
    hidden_two = (gelu(y_d * par_d[0] + par_d[1]) * mask).astype(bf16)
    rimmed = near_rows(hidden_two.reshape(batch, pixels, MID), width)
    y_e, spread = conv_forward(rimmed, conv_full, mask_wide, rows, width, devices)
    par_e = forward_rows(small_total(spread), conv_gain, conv_bias, count)
    middle_two, y_f, block = expand_forward([y_e], par_e, mask_wide, expand_full_two)
    par_f = forward_rows(wide_total(block), expand_gain_two, expand_bias_two, count)

    output, dt_f, block = output_stage(y_f, par_f, first_low, cotangent.reshape(n, channels), mask_wide)
    back_f, expand_gain_two_grad, expand_bias_two_grad = backward_rows(wide_total(block), par_f, count)
    dy_f, dt_e, spread = expand_backward(
        dt_f, y_f, par_f, back_f, mask_wide, expand_full_two, y_e, par_e, devices
    )
    expand_two_local = dot(dy_f, middle_two, TN).astype(bf16)
    expand_two_part = scatter_ch(expand_two_local)
    back_e, conv_gain_grad, conv_bias_grad = backward_rows(small_total(spread), par_e, count)
    dy_e = norm_gradient(dt_e, y_e, par_e, back_e, mask).astype(bf16)
    dy_e_rim = near_rows(dy_e.reshape(batch, pixels, MID), width)
    conv_local = conv_weight_gradient(dy_e, rimmed, rows, width, (expand_two_local,))
    conv_part = scatter_ch(conv_local)
    dt_d, spread = conv_backward(
        dy_e_rim, conv_full, y_d, par_d, mask_wide, rows, width, devices, (conv_local,)
    )
    base = conv_part.shape[0]
    back_d, reduce_gain_two_grad, reduce_bias_two_grad = backward_rows(small_total(spread), par_d, count)
    dy_d, dt_c, block = residual_backward(
        dt_d, y_d, par_d, back_d, mask_wide, reduce_full_two, dt_f, y_c, par_c, acts_low
    )
    reduce_two_local = dot(dy_d, first_low, TN).astype(bf16)

    back_c, expand_gain_one_grad, expand_bias_one_grad = backward_rows(wide_total(block), par_c, count)
    dy_c, dt_b, spread, reduce_two_local = expand_backward(
        dt_c, y_c, par_c, back_c, mask_wide, expand_full, y_b, par_b, devices, (reduce_two_local,)
    )
    reduce_two_part = scatter_ch(reduce_two_local)
    expand_one_local = dot(dy_c, middle, TN).astype(bf16)
    back_b, deform_gain_grad, deform_bias_grad = backward_rows(small_total(spread), par_b, count)
    dy_b = norm_gradient(dt_b, y_b, par_b, back_b, mask).astype(bf16)
    batch_p = first_step([conv_part, expand_two_part], base)
    deform_local, kept_p, expand_one_local = columns_weight_gradient(
        dy_b, columns, (batch_p[1], expand_one_local)
    )
    expand_one_part = scatter_ch(expand_one_local)
    deform_part = scatter_ch(deform_local)
    batch_p = next_step((batch_p[0], kept_p), 2)
    pieces, offset_local, after, step = [], 0.0, (), 4
    for b in range(batch):
        part = slice(b * pixels, (b + 1) * pixels)
        *tiles, offset_term, kept_p = deform_backward(
            near_tiles[5 * b : 5 * b + 5], offset_rows, disp[b : b + 1], fractions[b], deform_full,
            dy_b[part], rows, width, after, (batch_p[1],),
        )
        batch_p = (batch_p[0], kept_p)
        if b < batch - 1:
            batch_p, step = next_step(batch_p, step), 2 * step
        after = (offset_term,)
        offset_local = offset_local + offset_term
        pieces += deep_return(tiles)
    share_p = last_steps(batch_p, step)
    step = lax.axis_size("rows") // 2
    got_p = swap_with(share_p, "rows", step)
    dt_a, spread, share_p, reduce_two_part, expand_one_part = hidden_backward(
        pieces, y_a, par_a, mask_wide, devices, (share_p, reduce_two_part, expand_one_part)
    )
    share_p = joined(got_p, share_p, step)
    got_p = swap_with(share_p, "rows", step // 2)
    batch_q = first_step([reduce_two_part, expand_one_part], base)
    back_a, reduce_gain_one_grad, reduce_bias_one_grad = backward_rows(small_total(spread), par_a, count)
    dy_a, share_p, kept_q, deform_part = mid_gradient(
        dt_a, y_a, par_a, back_a, mask_wide, (share_p, batch_q[1], deform_part)
    )
    share_p = joined(got_p, share_p, step // 2)
    got_p = swap_with(share_p, "rows", step // 4)
    batch_q = next_step((batch_q[0], kept_q), 2)
    batch_r = first_step([deform_part], base)
    reduce_one_local = dot(dy_a, acts_low, TN).astype(bf16)
    red_one = split(by_owner(reduce_one_local), "ch", 1)
    input_grad, kept, share_p, kept_q, kept_r = input_backward(
        dy_a, reduce_full, dt_c, (red_one[1], share_p, batch_q[1], batch_r[1])
    )
    reduce_one_part = rest_of(added((red_one[0], kept)), "ch", 2)[0]
    share_p = last_joins(joined(got_p, share_p, step // 4), step // 8)
    offset_part = ladder_sum(offset_local.reshape(-1, MID), "ch").astype(bf16)
    offset_part = jnp.pad(offset_part, ((0, -offset_part.shape[0] % base), (0, 0)))
    total_q = last_joins(last_steps((batch_q[0], kept_q), 4), step)
    total_r = last_joins(last_steps((batch_r[0], kept_r), 2), step)
    total_s = last_joins(rows_reduce([reduce_one_part, offset_part], base), step)
    conv_weight_grad, expand_two_grad = cut(share_p, (9 * MID, channels))
    reduce_two_grad, expand_one_grad = cut(total_q, (channels, channels))
    (deform_weight_grad,) = cut(total_r, (9 * MID,))
    reduce_one_grad, offset_grad = cut(total_s, (channels, offset_part.size // base))
    expand_two_grad = lanes_to_blocks(expand_two_grad, MID)
    expand_one_grad = lanes_to_blocks(expand_one_grad, MID)
    offset_grad = lanes_to_blocks(offset_grad, MID)[:288].reshape(3, 3, 4, 8, MID)[:, :, :3, :6]
    offset_weight_grad = offset_grad.transpose(2, 3, 0, 1, 4).reshape(18, 9 * MID)
    return (
        output.reshape(inputs.shape),
        input_grad.reshape(inputs.shape),
        reduce_one_grad,
        reduce_gain_one_grad,
        reduce_bias_one_grad,
        offset_weight_grad,
        deform_weight_grad,
        deform_gain_grad,
        deform_bias_grad,
        expand_one_grad,
        expand_gain_one_grad,
        expand_bias_one_grad,
        reduce_two_grad,
        reduce_gain_two_grad,
        reduce_bias_two_grad,
        conv_weight_grad,
        conv_gain_grad,
        conv_bias_grad,
        expand_two_grad,
        expand_gain_two_grad,
        expand_bias_two_grad,
    )


def solution(mesh):
    tiles = P("ch", "rows", None, None)
    owned = P("ch", None)
    block = (owned, P(), P())
    placed = (tiles, P(), P(None, "ch", "rows", None)) + block + (P(),) + 2 * block + 3 * block + (tiles,)
    grads = (owned, P("ch"), P("ch"))
    return jax.shard_map(
        per_device,
        mesh=mesh,
        in_specs=placed,
        out_specs=(tiles, tiles) + grads + (P(),) + 2 * grads + 3 * grads,
        check_vma=False,
    )
```

```python
import functools

import jax
import jax.numpy as jnp
from jax import lax
from jax.experimental import pallas as pl
from jax.experimental.pallas import tpu as pltpu
from jax.sharding import PartitionSpec as P

bf16 = jnp.bfloat16
f32 = jnp.float32
VMEM = pltpu.VMEM
HBM = pltpu.HBM
DMA = pltpu.SemaphoreType.DMA
MID = 512
STEP = 512
NT = (((1,), (1,)), ((), ()))
TN = (((0,), (0,)), ((), ()))
NN = (((1,), (0,)), ((), ()))
GELU_A = 0.7978845608028654
GELU_B = 0.044715


def dot(a, b, dims=NN):
    return lax.dot_general(a, b, dims, preferred_element_type=f32)


def shaped(*shape, dtype=f32):
    return jax.ShapeDtypeStruct(shape, dtype)


def without(body, n_in, n_after, n_out, n_through):
    first = n_in + n_after + n_through
    return lambda *refs: body(
        *refs[:n_in], *refs[first : first + n_out], *refs[first + n_out + n_through :]
    )


def cost(us):
    return pl.CostEstimate(flops=int(us * 0.4e9), bytes_accessed=int(us * 0.8e6), transcendentals=0)


def call(body, operands, places, outs, out_places, us, limit, scratch=(), after=(), through=()):
    def spec(place):
        return pl.BlockSpec(memory_space=HBM if place == "h" else VMEM)

    def pinned(value, place):
        if place == "v":
            return value
        return pltpu.with_memory_space_constraint(value, HBM if place == "h" else VMEM)

    def result(out, place):
        if place == "v":
            return out
        return (HBM if place == "h" else VMEM)(out.shape, out.dtype)

    n_in, n_out, n_after = len(operands), len(outs), len(after)
    kept = [pltpu.with_memory_space_constraint(v, HBM) for v in (*after, *through)]
    return pl.pallas_call(
        without(body, n_in, n_after, n_out, len(through)),
        in_specs=[spec(p) for p in places] + [spec("h")] * len(kept),
        out_specs=tuple(spec(p) for p in out_places) + (spec("h"),) * len(through),
        out_shape=tuple(result(o, p) for o, p in zip(outs, out_places))
        + tuple(HBM(v.shape, v.dtype) for v in through),
        input_output_aliases={n_in + n_after + t: n_out + t for t in range(len(through))},
        scratch_shapes=list(scratch),
        compiler_params=pltpu.CompilerParams(vmem_limit_bytes=limit * 2**20),
        cost_estimate=cost(us),
    )(*[pinned(v, p) for v, p in zip(operands, places)], *kept)


def moving(source, target, sem):
    copy = pltpu.make_async_copy(source, target, sem)
    copy.start()
    return copy


def columns_moving(source, target, sems, wide=STEP):
    return [
        moving(source.at[:, s * wide : (s + 1) * wide], target.at[:, s * wide : (s + 1) * wide], sems.at[s])
        for s in range(source.shape[1] // wide)
    ]


def rows_moving(source, target, sems, tall=STEP):
    return [
        moving(source.at[s * tall : (s + 1) * tall], target.at[s * tall : (s + 1) * tall], sems.at[s])
        for s in range(source.shape[0] // tall)
    ]


def blocks(wide):
    return [(s, slice(s * STEP, (s + 1) * STEP)) for s in range(wide // STEP)]


def gelu(v):
    return 0.5 * v * (1.0 + jnp.tanh(GELU_A * (v + GELU_B * v * v * v)))


def gelu_slope(v):
    t = jnp.tanh(GELU_A * (v + GELU_B * v * v * v))
    return 0.5 * (1.0 + t) + 0.5 * v * (1.0 - t * t) * (GELU_A * (1.0 + 3.0 * GELU_B * v * v))


def normed(values, par_ref, part=slice(None)):
    return values * par_ref[0:1, part] + par_ref[1:2, part]


def normal_of(values, par_ref, part=slice(None)):
    return values * par_ref[2:3, part] + par_ref[3:4, part]


def norm_gradient(upstream, values, par_ref, back_ref, mask, part=slice(None)):
    normal = normal_of(values, par_ref, part)
    return upstream * back_ref[0:1, part] - mask * (back_ref[1:2, part] + normal * back_ref[2:3, part])


def sums_block(weighted, values):
    n = weighted.shape[1] // 128
    sums = (
        jnp.sum(weighted, axis=0, keepdims=True),
        jnp.sum(weighted * values, axis=0, keepdims=True),
    )
    return jnp.concatenate([v[:, c * 128 : c * 128 + 128] for v in sums for c in range(n)], axis=0)


def write_stats(stat_ref, weighted, values):
    stat_ref[...] = jnp.broadcast_to(sums_block(weighted, values)[None], stat_ref.shape)


def product_forward_body(x_ref, mask_ref, w_ref, low_ref, out_ref, stat_ref, x_buf, low_buf, sems):
    wide = x_ref.shape[1]
    coming = columns_moving(x_ref, x_buf, sems.at[0])
    total, going = None, []
    for s, part in blocks(wide):
        coming[s].wait()
        low_buf[:, part] = x_buf[:, part].astype(bf16)
        going.append(moving(low_buf.at[:, part], low_ref.at[:, part], sems.at[1, s]))
        term = dot(low_buf[:, part], w_ref[:, part], NT)
        total = term if total is None else total + term
    out_ref[...] = total
    write_stats(stat_ref, total * mask_ref[:, 0:1], total)
    for copy in going:
        copy.wait()


def product_forward(x, mask_wide, weight, devices):
    n, wide = x.shape
    return call(
        product_forward_body,
        (x, mask_wide, weight),
        "hvv",
        (shaped(n, wide, dtype=bf16), shaped(n, MID), shaped(devices, 8, 128)),
        "hvv",
        5,
        20,
        [VMEM((n, wide), f32), VMEM((n, wide), bf16), DMA((2, wide // STEP))],
    )


def expand_forward_body(*refs):
    *y_refs, par_ref, mask_ref, e_ref, mid_ref, out_ref, stat_ref, e_buf, out_buf, sems = refs
    coming = rows_moving(e_ref, e_buf, sems.at[0])
    mask = mask_ref[:, 0:1]
    at = 0
    for y_ref in y_refs:
        part = slice(at, at + y_ref.shape[0])
        mid_ref[part, :] = (gelu(normed(y_ref[...], par_ref)) * mask_ref[part, 0:1]).astype(bf16)
        at += y_ref.shape[0]
    going = []
    for s, part in blocks(e_ref.shape[0]):
        coming[s].wait()
        out = dot(mid_ref[...], e_buf[part, :], NT)
        out_buf[:, part] = out.astype(bf16)
        going.append(moving(out_buf.at[:, part], out_ref.at[:, part], sems.at[1, s]))
        stat_ref[s * 8 : s * 8 + 8, :] = sums_block(out * mask, out)
    for copy in going:
        copy.wait()


def expand_forward(y_parts, par, mask_wide, weight):
    n, wide = mask_wide.shape[0], weight.shape[0]
    return call(
        expand_forward_body,
        (*y_parts, par, mask_wide, weight),
        "v" * (len(y_parts) + 2) + "h",
        (shaped(n, MID, dtype=bf16), shaped(n, wide, dtype=bf16), shaped(wide // 64, 128)),
        "vhv",
        4,
        16,
        [VMEM(weight.shape, bf16), VMEM((n, wide), bf16), DMA((2, wide // STEP))],
    )


def first_forward_body(
    y_ref, par_ref, x_ref, mask_ref, w_ref, low_ref, out_ref, stat_ref,
    y_buf, x_buf, w_buf, low_buf, sems
):
    wide = x_ref.shape[1]
    coming_y = columns_moving(y_ref, y_buf, sems.at[0])
    coming_x = columns_moving(x_ref, x_buf, sems.at[1])
    coming_w = columns_moving(w_ref, w_buf, sems.at[2])
    mask = mask_ref[:, 0:1]
    total, going = None, []
    for s, part in blocks(wide):
        coming_y[s].wait()
        coming_x[s].wait()
        first = gelu(normed(y_buf[:, part].astype(f32), par_ref, part) + x_buf[:, part]) * mask
        low_buf[:, part] = first.astype(bf16)
        going.append(moving(low_buf.at[:, part], low_ref.at[:, part], sems.at[3, s]))
        coming_w[s].wait()
        term = dot(low_buf[:, part], w_buf[:, part], NT)
        total = term if total is None else total + term
    out_ref[...] = total
    write_stats(stat_ref, total * mask, total)
    for copy in going:
        copy.wait()


def first_forward(y, par, x, mask_wide, weight, devices):
    n, wide = y.shape
    return call(
        first_forward_body,
        (y, par, x, mask_wide, weight),
        "hvhvh",
        (shaped(n, wide, dtype=bf16), shaped(n, MID), shaped(devices, 8, 128)),
        "hvv",
        6,
        24,
        [
            VMEM((n, wide), bf16),
            VMEM((n, wide), f32),
            VMEM(weight.shape, bf16),
            VMEM((n, wide), bf16),
            DMA((4, wide // STEP)),
        ],
    )


def output_stage_body(
    y_ref, par_ref, first_ref, cot_ref, mask_ref, out_ref, dt_ref, stat_ref,
    y_buf, first_buf, cot_buf, out_buf, dt_buf, sems
):
    wide = y_ref.shape[1]
    coming_y = columns_moving(y_ref, y_buf, sems.at[0])
    coming_f = columns_moving(first_ref, first_buf, sems.at[1])
    coming_c = columns_moving(cot_ref, cot_buf, sems.at[2])
    mask = mask_ref[:, 0:1]
    going = []
    for s, part in blocks(wide):
        coming_y[s].wait()
        coming_f[s].wait()
        y = y_buf[:, part].astype(f32)
        pre = normed(y, par_ref, part) + first_buf[:, part].astype(f32)
        t = jnp.tanh(GELU_A * (pre + GELU_B * pre * pre * pre))
        out_buf[:, part] = 0.5 * pre * (1.0 + t) * mask
        going.append(moving(out_buf.at[:, part], out_ref.at[:, part], sems.at[3, s]))
        slope = 0.5 * (1.0 + t) + 0.5 * pre * (1.0 - t * t) * (GELU_A * (1.0 + 3.0 * GELU_B * pre * pre))
        coming_c[s].wait()
        dt = slope * (cot_buf[:, part] * mask)
        dt_buf[:, part] = dt.astype(bf16)
        going.append(moving(dt_buf.at[:, part], dt_ref.at[:, part], sems.at[4, s]))
        stat_ref[s * 8 : s * 8 + 8, :] = sums_block(dt, normal_of(y, par_ref, part))
    for copy in going:
        copy.wait()


def output_stage(y, par, first, cot, mask_wide):
    n, wide = y.shape
    return call(
        output_stage_body,
        (y, par, first, cot, mask_wide),
        "hvhhv",
        (shaped(n, wide), shaped(n, wide, dtype=bf16), shaped(wide // 64, 128)),
        "hhv",
        8,
        28,
        [
            VMEM((n, wide), bf16),
            VMEM((n, wide), bf16),
            VMEM((n, wide), f32),
            VMEM((n, wide), f32),
            VMEM((n, wide), bf16),
            DMA((5, wide // STEP)),
        ],
    )


def expand_backward_body(
    dt_ref, y_ref, par_ref, back_ref, mask_ref, e_ref, mid_y_ref, mid_par_ref,
    dy_ref, mid_dt_ref, stat_ref, dt_buf, y_buf, e_buf, dy_buf, sems
):
    wide = dt_ref.shape[1]
    coming_dt = columns_moving(dt_ref, dt_buf, sems.at[0])
    coming_y = columns_moving(y_ref, y_buf, sems.at[1])
    coming_e = rows_moving(e_ref, e_buf, sems.at[2])
    mask = mask_ref[:, 0:1]
    total, going = None, []
    for s, part in blocks(wide):
        coming_dt[s].wait()
        coming_y[s].wait()
        dt, y = dt_buf[:, part].astype(f32), y_buf[:, part].astype(f32)
        dy = norm_gradient(dt, y, par_ref, back_ref, mask, part).astype(bf16)
        dy_buf[:, part] = dy
        going.append(moving(dy_buf.at[:, part], dy_ref.at[:, part], sems.at[3, s]))
        coming_e[s].wait()
        term = dot(dy, e_buf[part, :])
        total = term if total is None else total + term
    y = mid_y_ref[...]
    dt = gelu_slope(normed(y, mid_par_ref)) * (total * mask)
    mid_dt_ref[...] = dt
    write_stats(stat_ref, dt, normal_of(y, mid_par_ref))
    for copy in going:
        copy.wait()


def expand_backward(dt, y, par, back, mask_wide, weight, mid_y, mid_par, devices, through=()):
    n, wide = y.shape
    return call(
        expand_backward_body,
        (dt, y, par, back, mask_wide, weight, mid_y, mid_par),
        "hhvvvhvv",
        (shaped(n, wide, dtype=bf16), shaped(n, MID), shaped(devices, 8, 128)),
        "hvv",
        5,
        24,
        [
            VMEM((n, wide), bf16),
            VMEM((n, wide), bf16),
            VMEM(weight.shape, bf16),
            VMEM((n, wide), bf16),
            DMA((4, wide // STEP)),
        ],
        through=through,
    )


def residual_backward_body(
    dt_ref, y_ref, par_ref, back_ref, mask_ref, w_ref, add_ref, wide_y_ref, wide_par_ref, x_ref,
    dy_ref, out_ref, stat_ref, w_buf, add_buf, y_buf, x_buf, out_buf, sems
):
    wide = x_ref.shape[1]
    coming = [
        columns_moving(source, target, sems.at[t])
        for t, (source, target) in enumerate(
            ((w_ref, w_buf), (add_ref, add_buf), (wide_y_ref, y_buf), (x_ref, x_buf))
        )
    ]
    mask = mask_ref[:, 0:1]
    dy_ref[...] = norm_gradient(dt_ref[...], y_ref[...], par_ref, back_ref, mask).astype(bf16)
    going = []
    for s, part in blocks(wide):
        for copies in coming:
            copies[s].wait()
        grad = add_buf[:, part].astype(f32) + dot(dy_ref[...], w_buf[:, part])
        y = y_buf[:, part].astype(f32)
        pre = normed(y, wide_par_ref, part) + x_buf[:, part].astype(f32)
        dt = gelu_slope(pre) * (grad * mask)
        out_buf[:, part] = dt.astype(bf16)
        going.append(moving(out_buf.at[:, part], out_ref.at[:, part], sems.at[4, s]))
        stat_ref[s * 8 : s * 8 + 8, :] = sums_block(dt, normal_of(y, wide_par_ref, part))
    for copy in going:
        copy.wait()


def residual_backward(dt, y, par, back, mask_wide, weight, add, wide_y, wide_par, x):
    n, wide = x.shape
    return call(
        residual_backward_body,
        (dt, y, par, back, mask_wide, weight, add, wide_y, wide_par, x),
        "vvvvvhhhvh",
        (shaped(n, MID, dtype=bf16), shaped(n, wide, dtype=bf16), shaped(wide // 64, 128)),
        "vhv",
        6,
        24,
        [VMEM(weight.shape, bf16)] + [VMEM((n, wide), bf16)] * 4 + [DMA((5, wide // STEP))],
    )


def input_backward_body(dy_ref, w_ref, add_ref, out_ref, w_buf, add_buf, out_buf, sems):
    coming_w = columns_moving(w_ref, w_buf, sems.at[0])
    coming_a = columns_moving(add_ref, add_buf, sems.at[1])
    going = []
    for s, part in blocks(w_ref.shape[1]):
        coming_w[s].wait()
        coming_a[s].wait()
        out_buf[:, part] = add_buf[:, part].astype(f32) + dot(dy_ref[...], w_buf[:, part])
        going.append(moving(out_buf.at[:, part], out_ref.at[:, part], sems.at[2, s]))
    for copy in going:
        copy.wait()


def input_backward(dy, weight, add, through):
    n, wide = add.shape
    return call(
        input_backward_body,
        (dy, weight, add),
        "vhh",
        (shaped(n, wide),),
        "h",
        5,
        20,
        [VMEM(weight.shape, bf16), VMEM((n, wide), bf16), VMEM((n, wide), f32), DMA((3, wide // STEP))],
        through=through,
    )


def hidden_backward_body(*refs):
    *piece_refs, y_ref, par_ref, mask_ref, dt_ref, stat_ref = refs
    batch = len(piece_refs) // 4
    pixels = y_ref.shape[0] // batch
    for b in range(batch):
        own, near, up, down = [ref[...].astype(f32) for ref in piece_refs[4 * b : 4 * b + 4]]
        dt_ref[b * pixels : (b + 1) * pixels, :] = own + near + up + down
    grad = dt_ref[...]
    y = y_ref[...]
    dt = gelu_slope(normed(y, par_ref)) * (grad * mask_ref[:, 0:1])
    dt_ref[...] = dt
    write_stats(stat_ref, dt, normal_of(y, par_ref))


def hidden_backward(pieces, y, par, mask_wide, devices, through):
    n = y.shape[0]
    return call(
        hidden_backward_body,
        (*pieces, y, par, mask_wide),
        "v" * (len(pieces) + 3),
        (shaped(n, MID), shaped(devices, 8, 128)),
        "vv",
        3,
        16,
        through=through,
    )


def mid_gradient_body(dt_ref, y_ref, par_ref, back_ref, mask_ref, dy_ref):
    dy = norm_gradient(dt_ref[...], y_ref[...], par_ref, back_ref, mask_ref[:, 0:1])
    dy_ref[...] = dy.astype(bf16)


def mid_gradient(dt, y, par, back, mask_wide, through):
    return call(
        mid_gradient_body,
        (dt, y, par, back, mask_wide),
        "vvvvv",
        (shaped(*y.shape, dtype=bf16),),
        "v",
        2,
        12,
        through=through,
    )


def cast_body(v_ref, out_ref):
    out_ref[...] = v_ref[...].astype(bf16)


def cast_after(values, *after):
    return call(cast_body, (values,), "v", (shaped(*values.shape, dtype=bf16),), "v", 2, 12, after=after)[0]


def pack_body(*refs, count, bit_axis, rows):
    part_refs, (send_ref, keep_ref), refs = refs[:count], refs[count : count + 2], refs[count + 2 :]
    buffers, (in_sem, out_sem) = refs[:count], refs[count:]
    coming = [moving(ref, buf, in_sem.at[t]) for t, (ref, buf) in enumerate(zip(part_refs, buffers))]
    bit = lax.axis_index(bit_axis) % 2
    tall = send_ref.shape[1]
    base = rows * tall
    going, at = [], 0
    for copy, buf in zip(coming, buffers):
        copy.wait()
        wide = buf.shape[1]
        for block in range(buf.shape[0] // base):
            for pair in range(rows // 2):
                for out_ref, side in ((send_ref, 1 - bit), (keep_ref, bit)):
                    row = pl.multiple_of(block * base + (2 * pair + side) * tall, 16)
                    going.append(
                        moving(
                            buf.at[pl.ds(row, tall), :],
                            out_ref.at[pair, :, at : at + wide],
                            out_sem.at[len(going)],
                        )
                    )
            at += wide
    for copy in going:
        copy.wait()


def pack_split(parts, base, rows, after):
    count = len(parts)
    blocks_in = sum(p.shape[0] // base for p in parts)
    wide = sum(p.shape[0] // base * p.shape[1] for p in parts)
    half = shaped(rows // 2, base // rows, wide, dtype=bf16)
    return call(
        functools.partial(pack_body, count=count, bit_axis="rows", rows=rows),
        tuple(parts),
        "h" * count,
        (half, half),
        "hh",
        3,
        16,
        [VMEM(p.shape, bf16) for p in parts] + [DMA((count,)), DMA((blocks_in * rows,))],
        after,
    )


def step_body(got_ref, kept_ref, send_ref, keep_ref, sum_ref, *, step):
    bit = lax.axis_index("rows") // step % 2
    sum_ref[...] = (got_ref[...].astype(f32) + kept_ref[...].astype(f32)).astype(bf16)
    for pair in range(send_ref.shape[0]):
        send_ref[pair] = sum_ref[2 * pair + 1 - bit]
        keep_ref[pair] = sum_ref[2 * pair + bit]


def step_split(got, kept, step, after=()):
    half = shaped(got.shape[0] // 2, *got.shape[1:], dtype=bf16)
    return call(
        functools.partial(step_body, step=step),
        (got, kept),
        "vv",
        (half, half),
        "vv",
        2,
        12,
        [VMEM(got.shape, bf16)],
        after,
    )


def return_body(*refs, batch):
    ins, outs = refs[: 5 * batch], refs[5 * batch :]
    odd = lax.axis_index("rows") % 2 == 1
    for b in range(batch):
        far_up_ref, up_ref, down_ref, far_down_ref, got_ref = ins[5 * b : 5 * b + 5]
        below_ref, above_ref, partner_ref = outs[3 * b : 3 * b + 3]

        @pl.when(odd)
        def _():
            total = far_up_ref[...].astype(f32) + got_ref[...].astype(f32)
            below_ref[...] = total.astype(bf16)
            above_ref[...] = far_down_ref[...]
            partner_ref[...] = up_ref[...]

        @pl.when(jnp.logical_not(odd))
        def _():
            total = far_down_ref[...].astype(f32) + got_ref[...].astype(f32)
            below_ref[...] = far_up_ref[...]
            above_ref[...] = total.astype(bf16)
            partner_ref[...] = down_ref[...]


def return_step(tiles, got):
    far_up, up, _, down, far_down = tiles
    piece = shaped(*got.shape, dtype=bf16)
    return call(
        functools.partial(return_body, batch=1),
        (far_up, up, down, far_down, got),
        "vvvvv",
        (piece, piece, piece),
        "vvv",
        2,
        12,
    )


def shift_lanes(values, by, width):
    place = lax.broadcasted_iota(jnp.int32, values.shape, values.ndim - 1) % width
    moved = pltpu.roll(values, by % values.shape[-1], values.ndim - 1)
    return jnp.where((place >= by) & (place < width + by), moved, 0.0)


def shift_rows(values, by, width):
    place = lax.broadcasted_iota(jnp.int32, values.shape, 0) % width
    moved = pltpu.roll(values, by % values.shape[0], 0)
    return jnp.where((place >= by) & (place < width + by), moved, 0.0)


def offset_fraction(ext_ref, ow_ref, b, base, pixels, width):
    u = None
    for i in range(3):
        start = (base + 2 * i) * width
        term = dot(ow_ref[i], ext_ref[b, start : start + pixels, :], NT)
        u = term if u is None else u + term
    total = u[32:64]
    total = total + shift_lanes(u[0:32], 2, width) + shift_lanes(u[64:96], -2, width)
    return 1.0 / (1.0 + jnp.exp(-total))


def deform_forward_body(*refs, batch, rows, width, deep):
    tile_refs, refs = refs[:5], refs[5:]
    ow_ref, disp_ref, m_ref, mask_ref, cols_out_ref, y_ref, frac_ref, stat_ref = refs[:8]
    ext_ref, par_ref, s_ref, cols_ref, m_buf, tile_sems, sems = refs[8:]
    pixels = rows * width
    coming = [
        moving(ref, ext_ref.at[:, t * pixels : (t + 1) * pixels, :], tile_sems.at[t])
        for t, ref in enumerate(tile_refs)
    ]
    coming_m = moving(m_ref, m_buf, sems.at[0])
    for copy in coming:
        copy.wait()
    lane = lax.broadcasted_iota(jnp.int32, (32, 128), 1)
    column = lane % width
    upper = lane // width

    def image(b, carry):
        frac = offset_fraction(ext_ref, ow_ref, b, deep - 2, pixels, width)
        for i in range(4):
            frac_ref[b, i] = frac[i * 8 : i * 8 + 8]
        pix = lax.broadcasted_iota(jnp.int32, (1, pixels), 1)
        row_at, col_at = pix // width, pix % width
        tops, lefts, ys, xs = [], [], [], []
        for k in range(9):
            i, j = k // 3, k % 3
            tops.append(row_at + disp_ref[b, i, 2 * j : 2 * j + 1, :] + (deep - 2))
            lefts.append(col_at + 2 * (j - 1) + disp_ref[b, i, 2 * j + 1 : 2 * j + 2, :])
            at = i * 8 + 2 * j
            ys.append(frac[at : at + 1])
            xs.append(frac[at + 1 : at + 2])
        blank = jnp.zeros((23, pixels), f32)
        par = jnp.concatenate(
            [jnp.concatenate(g, axis=0).astype(f32) if g is not None else blank
             for g in (tops, None, lefts, None, ys, None, xs, None)], axis=0)
        par_ref[...] = par.T

        def row_of_taps(i, carry):
            for j in range(3):
                k = i * 3 + j
                for c in range(pixels // 32):
                    p = pltpu.roll(par_ref[c * 32 : c * 32 + 32, :], 128 - k, 1)
                    wide = (32, 128)
                    top = jnp.broadcast_to(p[:, 0:1], wide).astype(jnp.int32) - upper
                    left = jnp.broadcast_to(p[:, 32:33], wide).astype(jnp.int32)
                    fy = jnp.broadcast_to(p[:, 64:65], wide)
                    fx = jnp.broadcast_to(p[:, 96:97], wide)
                    cw = jnp.where(column == left, 1.0 - fx, jnp.where(column == left + 1, fx, 0.0))
                    ca, cb = (1.0 - fy) * cw, fy * cw
                    for q in range(8):
                        s = jnp.where(top == 2 * q, ca, jnp.where(top == 2 * q - 1, cb, 0.0))
                        s_ref[j * pixels + c * 32 : j * pixels + c * 32 + 32, q * 128 : q * 128 + 128] = s.astype(bf16)
            start = pl.multiple_of(i * 2 * width, 128)
            window = ext_ref[b, pl.ds(start, 16 * width), :]
            for j in range(3):
                got = dot(s_ref[j * pixels : (j + 1) * pixels, :], window).astype(bf16)
                cols_ref[pl.ds(pl.multiple_of(b * pixels, pixels), pixels), pl.ds(pl.multiple_of((i * 3 + j) * MID, MID), MID)] = got
            return carry

        return lax.fori_loop(0, 3, row_of_taps, carry)

    lax.fori_loop(0, batch, image, 0)
    going = moving(cols_ref, cols_out_ref, sems.at[1])
    coming_m.wait()
    y = dot(cols_ref[...], m_buf[...], NT)
    y_ref[...] = y
    write_stats(stat_ref, y * mask_ref[:, 0:1], y)
    going.wait()


def deform_forward(tiles, offset_rows, disp, weight, mask_wide, rows, width, devices):
    batch = tiles[0].shape[0]
    pixels = rows * width
    n = batch * pixels
    return call(
        functools.partial(deform_forward_body, batch=batch, rows=rows, width=width, deep=2 * rows),
        (*tiles, offset_rows, disp, weight, mask_wide),
        "hhhhhvvhv",
        (
            shaped(n, 9 * MID, dtype=bf16),
            shaped(n, MID),
            shaped(batch, 4, 8, pixels),
            shaped(devices, 8, 128),
        ),
        "hvvv",
        15,
        30,
        [
            VMEM((batch, 5 * pixels, MID), bf16),
            VMEM((pixels, 128), f32),
            VMEM((3 * pixels, 16 * width), bf16),
            VMEM((n, 9 * MID), bf16),
            VMEM(weight.shape, bf16),
            DMA((5,)),
            DMA((2,)),
        ],
    )


def deform_backward_body(*refs, rows, width, deep, which):
    tile_refs, refs = refs[:5], refs[5:]
    (ow_ref, disp_ref, frac_ref, m_ref, dy_ref), refs = refs[:5], refs[5:]
    out_refs, refs = refs[:5], refs[5:]
    dow_ref, ext_ref, dext_ref, dc_ref, g_ref, st_ref, df_ref, m_buf, tile_sems, m_sems = refs
    pixels = rows * width
    coming = [
        moving(ref.at[which], ext_ref.at[0, t * pixels : (t + 1) * pixels, :], tile_sems.at[t])
        for t, ref in enumerate(tile_refs)
    ]
    coming_m = taps_moving(m_ref, m_buf, m_sems)
    window = 16 * width
    dow_ref[...] = jnp.zeros_like(dow_ref)
    dext_ref[...] = jnp.zeros_like(dext_ref)
    for copy in coming:
        copy.wait()

    def image(b, carry):
        def row_of_taps(i, carry):
            dy = dy_ref[...]
            for j in range(3):
                m = m_buf[:, (i * 3 + j) * MID : (i * 3 + j + 1) * MID]
                dc_ref[j * pixels : (j + 1) * pixels, :] = dot(dy, m).astype(bf16)
            start = i * 2 * width
            g_ref[...] = dot(ext_ref[b, pl.ds(start, window), :], dc_ref[...], NT)
            place = lax.broadcasted_iota(jnp.int32, (width, 128), 0)
            for j in range(3):
                for h in range(pixels // 128):
                    lanes = slice(h * 128, h * 128 + 128)
                    at_l = slice(j * pixels + h * 128, j * pixels + h * 128 + 128)
                    pix = lax.broadcasted_iota(jnp.int32, (1, 128), 1) + h * 128
                    by_y, by_x = slice(2 * j, 2 * j + 1), slice(2 * j + 1, 2 * j + 2)
                    top = pix // width + disp_ref[b, i, by_y, lanes] + (deep - 2)
                    left = pix % width + 2 * (j - 1) + disp_ref[b, i, by_x, lanes]
                    fy = frac_ref[b, i, by_y, lanes]
                    fx = frac_ref[b, i, by_x, lanes]
                    here, after = place == left, place == left + 1
                    cw = jnp.where(here, 1.0 - fx, jnp.where(after, fx, 0.0))
                    ca, cb = (1.0 - fy) * cw, fy * cw
                    low_sum = jnp.zeros((width, 128), f32)
                    high_sum = jnp.zeros((width, 128), f32)
                    for r in range(16):
                        part = slice(r * width, r * width + width)
                        g = g_ref[part, at_l]
                        m0, m1 = top == r, top == r - 1
                        low_sum = low_sum + jnp.where(m0, g, 0.0)
                        high_sum = high_sum + jnp.where(m1, g, 0.0)
                        st_ref[part, at_l] = jnp.where(m0, ca, jnp.where(m1, cb, 0.0)).astype(bf16)
                    d_fy = jnp.sum((high_sum - low_sum) * cw, axis=0, keepdims=True)
                    mixed = (1.0 - fy) * low_sum + fy * high_sum
                    d_fx = jnp.sum(
                        jnp.where(after, mixed, 0.0) - jnp.where(here, mixed, 0.0), axis=0, keepdims=True)
                    df_ref[i, by_y, lanes] = d_fy * fy * (1.0 - fy)
                    df_ref[i, by_x, lanes] = d_fx * fx * (1.0 - fx)
            dext_ref[b, pl.ds(start, window), :] += dot(st_ref[...], dc_ref[...])
            return carry

        df_ref[...] = jnp.zeros_like(df_ref)
        for i in range(3):
            coming_m[i].wait()
            row_of_taps(i, carry)
        d_off = df_ref[...].reshape(32, pixels).astype(bf16).astype(f32)
        stacked = jnp.concatenate(
            [shift_lanes(d_off, -2, width), d_off, shift_lanes(d_off, 2, width)], axis=0)
        across = jnp.concatenate([stacked, jnp.zeros((32, pixels), f32)], axis=0).T.astype(bf16)
        stacked = stacked.astype(bf16)
        for i in range(3):
            first = (deep - 2 + 2 * i) * width
            part = slice(first, first + pixels)
            dow_ref[i] += dot(stacked, ext_ref[b, part, :])
            dext_ref[b, part, :] += dot(across[:, :96], ow_ref[i])
        return carry

    image(0, 0)
    for t, ref in enumerate(out_refs):
        ref[...] = dext_ref[t // 5, t % 5 * pixels : (t % 5 + 1) * pixels, :].astype(ref.dtype)


def deform_backward(which, tiles, offset_rows, disp, frac, weight, dy, rows, width, after, through):
    pixels = rows * width
    return call(
        functools.partial(deform_backward_body, rows=rows, width=width, deep=2 * rows, which=which),
        (*tiles, offset_rows, disp, frac, weight, dy),
        "hhhhhvvvhv",
        tuple(shaped(pixels, MID, dtype=f32 if t == 2 else bf16) for t in range(5)) + (shaped(3, 96, MID),),
        "vvvvvv",
        10,
        32,
        [
            VMEM((1, 5 * pixels, MID), bf16),
            VMEM((1, 5 * pixels, MID), f32),
            VMEM((3 * pixels, MID), bf16),
            VMEM((16 * width, 3 * pixels), f32),
            VMEM((16 * width, 3 * pixels), bf16),
            VMEM((4, 8, pixels), f32),
            VMEM(weight.shape, bf16),
            DMA((5,)),
            DMA((3,)),
        ],
        after,
        through,
    )


def taps_moving(m_ref, m_buf, sems):
    wide = 3 * MID
    return columns_moving(m_ref, m_buf, sems, wide)


def rim_moving(parts, rim_ref, sems):
    copies, at = [], 0
    for t, ref in enumerate(parts):
        copies.append(moving(ref, rim_ref.at[:, at : at + ref.shape[1], :], sems.at[t]))
        at += ref.shape[1]
    return copies


def conv_forward_body(
    above_ref, own_ref, below_ref, m_ref, mask_ref, y_ref, stat_ref, rim_ref, m_buf, rim_sems, sems,
    *, batch, rows, width
):
    pixels = rows * width
    coming = taps_moving(m_ref, m_buf, sems)
    for copy in rim_moving((above_ref, own_ref, below_ref), rim_ref, rim_sems):
        copy.wait()
    sums = [[None] * 3 for _ in range(batch)]
    for i in range(3):
        coming[i].wait()
        for b in range(batch):
            for j in range(3):
                k = i * 3 + j
                start = 2 * i * width
                term = dot(rim_ref[b, start : start + pixels, :], m_buf[:, k * MID : (k + 1) * MID], NT)
                sums[b][j] = term if i == 0 else sums[b][j] + term
    for b in range(batch):
        total = sums[b][1] + shift_rows(sums[b][0], 2, width) + shift_rows(sums[b][2], -2, width)
        y_ref[b * pixels : (b + 1) * pixels, :] = total
    y = y_ref[...]
    write_stats(stat_ref, y * mask_ref[:, 0:1], y)


def conv_forward(rim, weight, mask_wide, rows, width, devices):
    batch = rim[0].shape[0]
    n = batch * rows * width
    return call(
        functools.partial(conv_forward_body, batch=batch, rows=rows, width=width),
        (*rim, weight, mask_wide),
        "hhhhv",
        (shaped(n, MID), shaped(devices, 8, 128)),
        "vv",
        5,
        24,
        [VMEM((batch, (rows + 4) * width, MID), bf16), VMEM(weight.shape, bf16), DMA((3,)), DMA((3,))],
    )


def conv_backward_body(
    above_ref, own_ref, below_ref, m_ref, y_ref, par_ref, mask_ref, dt_ref, stat_ref,
    rim_ref, m_buf, rim_sems, sems, *, batch, rows, width
):
    pixels = rows * width
    coming = taps_moving(m_ref, m_buf, sems)
    for copy in rim_moving((above_ref, own_ref, below_ref), rim_ref, rim_sems):
        copy.wait()
    sums = [[None] * 3 for _ in range(batch)]
    for i in range(3):
        coming[i].wait()
        for b in range(batch):
            for j in range(3):
                k = i * 3 + j
                start = (4 - 2 * i) * width
                term = dot(rim_ref[b, start : start + pixels, :], m_buf[:, k * MID : (k + 1) * MID])
                sums[b][j] = term if i == 0 else sums[b][j] + term
    for b in range(batch):
        total = sums[b][1] + shift_rows(sums[b][0], -2, width) + shift_rows(sums[b][2], 2, width)
        dt_ref[b * pixels : (b + 1) * pixels, :] = total
    y = y_ref[...]
    dt = gelu_slope(normed(y, par_ref)) * (dt_ref[...] * mask_ref[:, 0:1])
    dt_ref[...] = dt
    write_stats(stat_ref, dt, normal_of(y, par_ref))


def conv_backward(rim, weight, y, par, mask_wide, rows, width, devices, after):
    batch = rim[0].shape[0]
    n = batch * rows * width
    return call(
        functools.partial(conv_backward_body, batch=batch, rows=rows, width=width),
        (*rim, weight, y, par, mask_wide),
        "hhhhvvv",
        (shaped(n, MID), shaped(devices, 8, 128)),
        "vv",
        6,
        24,
        [VMEM((batch, (rows + 4) * width, MID), bf16), VMEM(weight.shape, bf16), DMA((3,)), DMA((3,))],
        after,
    )


def conv_weight_body(
    dy_ref, above_ref, own_ref, below_ref, out_ref, rim_ref, dyt_ref, out_buf, rim_sems, sems,
    *, batch, rows, width
):
    pixels = rows * width
    coming = rim_moving((above_ref, own_ref, below_ref), rim_ref, rim_sems)
    dy = dy_ref[...].astype(f32)
    going = []
    for j in range(3):
        moved = shift_rows(dy, 2 * (j - 1), width) if j != 1 else dy
        dyt_ref[j] = moved.T.astype(bf16)
        if j == 0:
            for copy in coming:
                copy.wait()
        for i in range(3):
            part = slice((i * 3 + j) * MID, (i * 3 + j + 1) * MID)
            start = 2 * i * width
            total = None
            for b in range(batch):
                term = dot(dyt_ref[j, :, b * pixels : (b + 1) * pixels], rim_ref[b, start : start + pixels, :])
                total = term if total is None else total + term
            out_buf[:, part] = total.astype(bf16)
            going.append(moving(out_buf.at[:, part], out_ref.at[:, part], sems.at[i * 3 + j]))
    for copy in going:
        copy.wait()


def conv_weight_gradient(dy, rim, rows, width, after):
    batch = rim[0].shape[0]
    return call(
        functools.partial(conv_weight_body, batch=batch, rows=rows, width=width),
        (dy, *rim),
        "vhhh",
        (shaped(MID, 9 * MID, dtype=bf16),),
        "h",
        6,
        20,
        [
            VMEM((batch, (rows + 4) * width, MID), bf16),
            VMEM((3, MID, batch * rows * width), bf16),
            VMEM((MID, 9 * MID), bf16),
            DMA((3,)),
            DMA((9,)),
        ],
        after,
    )[0]


def columns_weight_body(dy_ref, cols_ref, out_ref, dyt_ref, cols_buf, out_buf, sems):
    coming = columns_moving(cols_ref, cols_buf, sems.at[0])
    dyt_ref[...] = dy_ref[...].astype(f32).T.astype(bf16)
    going = []
    for s, part in blocks(cols_ref.shape[1]):
        coming[s].wait()
        out_buf[:, part] = dot(dyt_ref[...], cols_buf[:, part]).astype(bf16)
        going.append(moving(out_buf.at[:, part], out_ref.at[:, part], sems.at[1, s]))
    for copy in going:
        copy.wait()


def columns_weight_gradient(dy, cols, through):
    n, wide = cols.shape
    return call(
        columns_weight_body,
        (dy, cols),
        "vh",
        (shaped(MID, wide, dtype=bf16),),
        "h",
        6,
        20,
        [VMEM((MID, n), bf16), VMEM((n, wide), bf16), VMEM((MID, wide), bf16), DMA((2, wide // STEP))],
        through=through,
    )


TILES = 2
EPSILON = 1e-05


def swap_with(values, axis, step):
    return lax.ppermute(values, axis, [(i, i ^ step) for i in range(lax.axis_size(axis))])


def from_behind(block, axis, distance):
    devices = range(lax.axis_size(axis))
    route = [(i - distance, i) for i in devices if i - distance in devices]
    return lax.ppermute(block, axis, route)


def ladder_sum(values, axis):
    step = 1
    while step < lax.axis_size(axis):
        got = swap_with(values.astype(bf16), axis, step)
        values = values + got.astype(f32)
        step *= 2
    return values


def to_everyone(spread, groups=None):
    return lax.all_to_all(spread, ("rows", "ch"), 0, 0, axis_index_groups=groups, tiled=True)


def small_total(spread):
    return jnp.sum(to_everyone(spread), axis=0).reshape(2, -1)


def wide_total(block):
    devices = lax.axis_size("rows") * lax.axis_size("ch")
    core = lax.axis_index("ch") % 2
    above, below = block.reshape(2, -1, 128)
    half = jnp.where(core == 0, above, below) + swap_with(jnp.where(core == 0, below, above), "ch", 1)
    groups = [[i * 2 + k for i in range(devices // 2)] for k in range(2)]
    half = jnp.broadcast_to(half[None], (devices // 2,) + half.shape)
    half = jnp.sum(to_everyone(half, groups), axis=0)
    other = swap_with(half, "ch", 1)
    whole = jnp.stack([jnp.where(core == 0, half, other), jnp.where(core == 0, other, half)])
    whole = whole.reshape(-1, 2, STEP)
    return whole[:, 0].reshape(-1), whole[:, 1].reshape(-1)


def forward_rows(sums, gain, shift, count):
    mean = sums[0] / count
    scale = lax.rsqrt(sums[1] / count - mean * mean + EPSILON)
    return jnp.stack([scale * gain, shift - mean * scale * gain, scale, -mean * scale])


def backward_rows(sums, par, count):
    rows = jnp.stack([par[0], par[0] * sums[0] / count, par[0] * sums[1] / count])
    return rows, own_slice(sums[1]), own_slice(sums[0])


def own_slice(full):
    size = full.shape[0] // lax.axis_size("ch")
    return lax.dynamic_slice_in_dim(full, lax.axis_index("ch") * size, size)


def gather_weight(weight):
    return lax.all_gather(weight.astype(bf16), "ch", axis=0, tiled=True)


def gather_weight_after(weight, *after):
    return lax.all_gather(cast_after(weight, *after), "ch", axis=0, tiled=True)


def gather_by_swaps(weight):
    ch = lax.axis_size("ch")
    came = None
    held = weight.astype(bf16)[None]
    step = ch // 2
    while step >= 1:
        got = swap_with(held, "ch", step)
        came = got if came is None else came
        odd = lax.axis_index("ch") // step % 2 == 1
        held = jnp.stack([jnp.where(odd, got, held), jnp.where(odd, held, got)], axis=1)
        held = held.reshape((-1,) + held.shape[2:])
        step //= 2
    return held.reshape((-1,) + weight.shape[1:]), came


def pick(values, bit):
    return lax.dynamic_index_in_dim(values, bit, 1, keepdims=False)


def scatter_ch(gradient):
    return lax.psum_scatter(gradient, "ch", scatter_dimension=0, tiled=True)


def split(total, axis, step):
    bit = lax.axis_index(axis) // step % 2
    pairs = total.reshape((total.shape[0] // 2, 2) + total.shape[1:])
    return swap_with(pick(pairs, 1 - bit), axis, step), pick(pairs, bit)


def added(pair):
    got, kept = pair
    return (got.astype(f32) + kept.astype(f32)).astype(bf16)


def rest_of(total, axis, step=1):
    while step < lax.axis_size(axis):
        total = added(split(total, axis, step))
        step *= 2
    return total


def by_owner(gradient, axis="ch"):
    count = lax.axis_size(axis)
    return gradient.reshape((count, gradient.shape[0] // count) + gradient.shape[1:])


def first_step(parts, base, after=()):
    rows = lax.axis_size("rows")
    if base // rows % 16 == 0:
        send, keep = pack_split(parts, base, rows, after)
        return swap_with(send, "rows", 1), keep
    return split(by_owner(jnp.concatenate([blocks_to_lanes(p, base) for p in parts], axis=1), "rows"), "rows", 1)


def next_step(pair, step, after=()):
    send, keep = step_split(*pair, step, after)
    return swap_with(send, "rows", step), keep


def last_steps(pair, step, after=()):
    while step < lax.axis_size("rows"):
        pair = next_step(pair, step, after)
        step, after = 2 * step, ()
    return added(pair)


def blocks_to_lanes(values, base):
    return jnp.concatenate([values[r : r + base] for r in range(0, values.shape[0], base)], axis=1)


def lanes_to_blocks(values, wide):
    return jnp.concatenate(
        [values[:, c : c + wide] for c in range(0, values.shape[1], wide)], axis=0
    )


def joined(got, kept, step):
    odd = lax.axis_index("rows") // step % 2 == 1
    total = jnp.stack([jnp.where(odd, got, kept), jnp.where(odd, kept, got)], axis=1)
    return total.reshape((-1,) + total.shape[2:])


def last_joins(total, step):
    while step >= 1:
        total = joined(swap_with(total, "rows", step), total, step)
        step //= 2
    return total


def cut(total, widths):
    total = total.reshape(-1, total.shape[2]).astype(f32)
    ends, at = [], 0
    for width in widths:
        ends.append(total[:, at : at + width])
        at += width
    return ends


def deep_rows(tile):
    odd = lax.axis_index("rows") % 2 == 1
    far_up = from_behind(tile, "rows", 2)
    far_down = from_behind(tile, "rows", -2)
    near = swap_with(tile, "rows", 1)
    other = swap_with(jnp.where(odd, far_up, far_down), "rows", 1)
    return far_up, jnp.where(odd, near, other), tile, jnp.where(odd, other, near), far_down


def deep_return(tiles):
    odd = lax.axis_index("rows") % 2 == 1
    _, up, own, down, _ = tiles
    got = swap_with(jnp.where(odd, down, up), "rows", 1)
    below, above, partner = return_step(tiles, got)
    below = from_behind(below, "rows", -2)
    above = from_behind(above, "rows", 2)
    return [own, swap_with(partner, "rows", 1), below, above]


def near_rows(tile, width):
    size = 2 * width
    above = from_behind(tile[:, -size:], "rows", 1)
    below = from_behind(tile[:, :size], "rows", -1)
    return above, tile, below


def per_device(
    inputs,
    heights,
    displacements,
    reduce_one,
    reduce_gain_one,
    reduce_bias_one,
    offset_weight,
    deform_weight,
    deform_gain,
    deform_bias,
    expand_one,
    expand_gain_one,
    expand_bias_one,
    reduce_two,
    reduce_gain_two,
    reduce_bias_two,
    conv_weight,
    conv_gain,
    conv_bias,
    expand_two,
    expand_gain_two,
    expand_bias_two,
    cotangent,
):
    batch, rows, width, channels = inputs.shape
    pixels = rows * width
    n = batch * pixels
    own_heights = lax.dynamic_slice_in_dim(heights, lax.axis_index("ch") * batch, batch)
    rows_here = lax.axis_index("rows") * rows + jnp.arange(rows, dtype=jnp.int32)
    mask = (rows_here[None, :] < own_heights[:, None]).astype(f32)
    mask = jnp.broadcast_to(mask[:, :, None], (batch, rows, width)).reshape(n, 1)
    mask_wide = jnp.broadcast_to(mask, (n, 128))
    count = jnp.sum(heights).astype(f32) * width

    offset_rows = offset_weight.astype(bf16).reshape(3, 6, 3, 3, MID).transpose(2, 3, 0, 1, 4)
    offset_rows = jnp.pad(offset_rows, ((0, 0), (0, 0), (0, 1), (0, 2), (0, 0))).reshape(3, 96, MID)
    disp = jnp.pad(displacements.reshape(3, 6, batch, pixels), ((0, 0), (0, 2), (0, 0), (0, 0)))
    disp = disp.transpose(2, 0, 1, 3)

    reduce_full, came = gather_by_swaps(reduce_one)
    deform_full = gather_weight_after(deform_weight, came)
    expand_full, reduce_full_two, conv_full, expand_full_two = [
        gather_weight(w) for w in (expand_one, reduce_two, conv_weight, expand_two)
    ]

    devices = lax.axis_size("rows") * lax.axis_size("ch")
    acts = inputs.reshape(n, channels)
    acts_low, y_a, spread = product_forward(acts, mask_wide, reduce_full, devices)
    par_a = forward_rows(small_total(spread), reduce_gain_one, reduce_bias_one, count)
    hidden = (gelu(y_a * par_a[0] + par_a[1]) * mask).astype(bf16)
    near_tiles = deep_rows(hidden.reshape(batch, pixels, MID))
    columns, y_b, fraction, spread = deform_forward(
        near_tiles, offset_rows, disp, deform_full, mask_wide, rows, width, devices
    )
    par_b = forward_rows(small_total(spread), deform_gain, deform_bias, count)
    middle, y_c, block = expand_forward([y_b], par_b, mask_wide, expand_full)
    par_c = forward_rows(wide_total(block), expand_gain_one, expand_bias_one, count)

    first_low, y_d, spread = first_forward(y_c, par_c, acts, mask_wide, reduce_full_two, devices)
    par_d = forward_rows(small_total(spread), reduce_gain_two, reduce_bias_two, count)
    hidden_two = (gelu(y_d * par_d[0] + par_d[1]) * mask).astype(bf16)
    rimmed = near_rows(hidden_two.reshape(batch, pixels, MID), width)
    y_e, spread = conv_forward(rimmed, conv_full, mask_wide, rows, width, devices)
    par_e = forward_rows(small_total(spread), conv_gain, conv_bias, count)
    middle_two, y_f, block = expand_forward([y_e], par_e, mask_wide, expand_full_two)
    par_f = forward_rows(wide_total(block), expand_gain_two, expand_bias_two, count)

    output, dt_f, block = output_stage(y_f, par_f, first_low, cotangent.reshape(n, channels), mask_wide)
    back_f, expand_gain_two_grad, expand_bias_two_grad = backward_rows(wide_total(block), par_f, count)
    dy_f, dt_e, spread = expand_backward(
        dt_f, y_f, par_f, back_f, mask_wide, expand_full_two, y_e, par_e, devices
    )
    expand_two_local = dot(dy_f, middle_two, TN).astype(bf16)
    expand_two_part = scatter_ch(expand_two_local)
    back_e, conv_gain_grad, conv_bias_grad = backward_rows(small_total(spread), par_e, count)
    dy_e = norm_gradient(dt_e, y_e, par_e, back_e, mask).astype(bf16)
    dy_e_rim = near_rows(dy_e.reshape(batch, pixels, MID), width)
    conv_local = conv_weight_gradient(dy_e, rimmed, rows, width, (expand_two_local,))
    conv_part = scatter_ch(conv_local)
    dt_d, spread = conv_backward(
        dy_e_rim, conv_full, y_d, par_d, mask_wide, rows, width, devices, (conv_local,)
    )
    base = conv_part.shape[0]
    back_d, reduce_gain_two_grad, reduce_bias_two_grad = backward_rows(small_total(spread), par_d, count)
    dy_d, dt_c, block = residual_backward(
        dt_d, y_d, par_d, back_d, mask_wide, reduce_full_two, dt_f, y_c, par_c, acts_low
    )
    reduce_two_local = dot(dy_d, first_low, TN).astype(bf16)

    back_c, expand_gain_one_grad, expand_bias_one_grad = backward_rows(wide_total(block), par_c, count)
    dy_c, dt_b, spread, reduce_two_local = expand_backward(
        dt_c, y_c, par_c, back_c, mask_wide, expand_full, y_b, par_b, devices, (reduce_two_local,)
    )
    reduce_two_part = scatter_ch(reduce_two_local)
    expand_one_local = dot(dy_c, middle, TN).astype(bf16)
    back_b, deform_gain_grad, deform_bias_grad = backward_rows(small_total(spread), par_b, count)
    dy_b = norm_gradient(dt_b, y_b, par_b, back_b, mask).astype(bf16)
    batch_p = first_step([conv_part, expand_two_part], base)
    deform_local, kept_p = columns_weight_gradient(dy_b, columns, (batch_p[1],))
    deform_part = scatter_ch(deform_local)
    batch_p = (batch_p[0], kept_p)
    pieces, offset_local, after, step = [], 0.0, (), 2
    for b in range(batch):
        part = slice(b * pixels, (b + 1) * pixels)
        results = deform_backward(
            b, near_tiles, offset_rows, disp[b : b + 1], fraction[b : b + 1], deform_full,
            dy_b[part], rows, width, after, (batch_p[1],) + ((expand_one_local,) if b == 0 else ()),
        )
        tiles, offset_term = results[:5], results[5]
        if b == 0:
            expand_one_part = scatter_ch(results[7])
        batch_p = (batch_p[0], results[6])
        if b < batch - 1:
            batch_p, step = next_step(batch_p, step), 2 * step
        after = (offset_term, reduce_two_part)
        offset_local = offset_local + offset_term
        pieces += deep_return(tiles)
    batch_p = next_step(batch_p, step)
    dt_a, spread, kept_p, reduce_two_part = hidden_backward(
        pieces, y_a, par_a, mask_wide, devices, (batch_p[1], reduce_two_part)
    )
    share_p = last_steps((batch_p[0], kept_p), 2 * step)
    step = lax.axis_size("rows") // 2
    got_p = swap_with(share_p, "rows", step)
    batch_q = first_step([reduce_two_part], base)
    back_a, reduce_gain_one_grad, reduce_bias_one_grad = backward_rows(small_total(spread), par_a, count)
    dy_a, share_p, kept_q, deform_part, offset_local = mid_gradient(
        dt_a, y_a, par_a, back_a, mask_wide, (share_p, batch_q[1], deform_part, offset_local)
    )
    share_p = joined(got_p, share_p, step)
    got_p = swap_with(share_p, "rows", step // 2)
    batch_q = next_step((batch_q[0], kept_q), 2)
    batch_r = first_step([deform_part], base)
    reduce_one_local = dot(dy_a, acts_low, TN).astype(bf16)
    red_one = split(by_owner(reduce_one_local), "ch", 1)
    input_grad, kept, share_p, kept_q, kept_r = input_backward(
        dy_a, reduce_full, dt_c, (red_one[1], share_p, batch_q[1], batch_r[1])
    )
    red_one = split(added((red_one[0], kept)), "ch", 2)
    reduce_one_part = rest_of(added(red_one), "ch", 4)[0]
    share_p = last_joins(joined(got_p, share_p, step // 2), step // 4)
    offset_local = offset_local.reshape(3, 3, 4, 8, MID)[:, :, :3, :6]
    offset_local = offset_local.transpose(2, 3, 0, 1, 4).reshape(-1, MID)
    offset_part = ladder_sum(offset_local, "ch").astype(bf16)
    offset_part = jnp.pad(offset_part, ((0, -offset_part.shape[0] % base), (0, 0)))
    total_q = last_joins(last_steps((batch_q[0], kept_q), 4, (red_one[1],)), step)
    total_r = last_joins(last_steps((batch_r[0], kept_r), 2, (red_one[1],)), step)
    batch_s = first_step([reduce_one_part, offset_part], base)
    batch_e = first_step([expand_one_part], base, (batch_s[1],))
    total_s = last_joins(last_steps(batch_s, 2), step)
    total_e = last_joins(last_steps(batch_e, 2), step)
    conv_weight_grad, expand_two_grad = cut(share_p, (9 * MID, channels))
    (reduce_two_grad,) = cut(total_q, (channels,))
    (expand_one_grad,) = cut(total_e, (channels,))
    (deform_weight_grad,) = cut(total_r, (9 * MID,))
    reduce_one_grad, offset_grad = cut(total_s, (channels, offset_part.size // base))
    expand_two_grad = lanes_to_blocks(expand_two_grad, MID)
    expand_one_grad = lanes_to_blocks(expand_one_grad, MID)
    offset_weight_grad = lanes_to_blocks(offset_grad, MID)[:162].reshape(18, 9 * MID)
    return (
        output.reshape(inputs.shape),
        input_grad.reshape(inputs.shape),
        reduce_one_grad,
        reduce_gain_one_grad,
        reduce_bias_one_grad,
        offset_weight_grad,
        deform_weight_grad,
        deform_gain_grad,
        deform_bias_grad,
        expand_one_grad,
        expand_gain_one_grad,
        expand_bias_one_grad,
        reduce_two_grad,
        reduce_gain_two_grad,
        reduce_bias_two_grad,
        conv_weight_grad,
        conv_gain_grad,
        conv_bias_grad,
        expand_two_grad,
        expand_gain_two_grad,
        expand_bias_two_grad,
    )


def solution(mesh):
    tiles = P("ch", "rows", None, None)
    owned = P("ch", None)
    block = (owned, P(), P())
    placed = (tiles, P(), P(None, "ch", "rows", None)) + block + (P(),) + 2 * block + 3 * block + (tiles,)
    grads = (owned, P("ch"), P("ch"))
    return jax.shard_map(
        per_device,
        mesh=mesh,
        in_specs=placed,
        out_specs=(tiles, tiles) + grads + (P(),) + 2 * grads + 3 * grads,
        check_vma=False,
    )
```

```python
import functools

import jax
import jax.numpy as jnp
from jax import lax
from jax.experimental import pallas as pl
from jax.experimental.pallas import tpu as pltpu
from jax.sharding import PartitionSpec as P

bf16 = jnp.bfloat16
f32 = jnp.float32
VMEM = pltpu.VMEM
HBM = pltpu.HBM
DMA = pltpu.SemaphoreType.DMA
MID = 512
STEP = 512
NT = (((1,), (1,)), ((), ()))
TN = (((0,), (0,)), ((), ()))
NN = (((1,), (0,)), ((), ()))
GELU_A = 0.7978845608028654
GELU_B = 0.044715


def dot(a, b, dims=NN):
    return lax.dot_general(a, b, dims, preferred_element_type=f32)


def shaped(*shape, dtype=f32):
    return jax.ShapeDtypeStruct(shape, dtype)


def without(body, n_in, n_order, n_out, n_through, token):
    first = n_in + n_order + n_through

    def inner(*refs):
        if token:
            refs[first + n_out + n_through][...] = jnp.zeros((8, 128), f32)
        body(*refs[:n_in], *refs[first : first + n_out], *refs[first + n_out + n_through + token :])

    return inner


def cost(us):
    return pl.CostEstimate(flops=int(us * 0.4e9), bytes_accessed=int(us * 0.8e6), transcendentals=0)


def call(body, operands, places, outs, out_places, us, limit, scratch=(), after=(), through=(), token=None):
    def spec(place):
        return pl.BlockSpec(memory_space=HBM if place == "h" else VMEM)

    def pinned(value, place):
        return pltpu.with_memory_space_constraint(value, HBM) if place == "h" else value

    def result(out, place):
        return HBM(out.shape, out.dtype) if place == "h" else out

    tokens = () if token is None else (token,)
    n_in, n_out, n_order = len(operands), len(outs), len(after) + len(tokens)
    return pl.pallas_call(
        without(body, n_in, n_order, n_out, len(through), len(tokens)),
        in_specs=[spec(p) for p in places] + [spec("h")] * len(after) + [spec("v")] * len(tokens)
        + [spec("h")] * len(through),
        out_specs=tuple(spec(p) for p in out_places) + (spec("h"),) * len(through)
        + (spec("v"),) * len(tokens),
        out_shape=tuple(result(o, p) for o, p in zip(outs, out_places))
        + tuple(HBM(v.shape, v.dtype) for v in through)
        + (shaped(8, 128),) * len(tokens),
        input_output_aliases={n_in + n_order + t: n_out + t for t in range(len(through))},
        scratch_shapes=list(scratch),
        compiler_params=pltpu.CompilerParams(vmem_limit_bytes=limit * 2**20),
        cost_estimate=cost(us),
    )(
        *[pinned(v, p) for v, p in zip(operands, places)],
        *[pinned(v, "h") for v in after],
        *tokens,
        *[pinned(v, "h") for v in through],
    )


def moving(source, target, sem):
    copy = pltpu.make_async_copy(source, target, sem)
    copy.start()
    return copy


def columns_moving(source, target, sems, wide=STEP):
    return [
        moving(source.at[:, s * wide : (s + 1) * wide], target.at[:, s * wide : (s + 1) * wide], sems.at[s])
        for s in range(source.shape[1] // wide)
    ]


def rows_moving(source, target, sems, tall=STEP):
    return [
        moving(source.at[s * tall : (s + 1) * tall], target.at[s * tall : (s + 1) * tall], sems.at[s])
        for s in range(source.shape[0] // tall)
    ]


def blocks(wide):
    return [(s, slice(s * STEP, (s + 1) * STEP)) for s in range(wide // STEP)]


def gelu(v):
    return 0.5 * v * (1.0 + jnp.tanh(GELU_A * (v + GELU_B * v * v * v)))


def gelu_slope(v):
    t = jnp.tanh(GELU_A * (v + GELU_B * v * v * v))
    return 0.5 * (1.0 + t) + 0.5 * v * (1.0 - t * t) * (GELU_A * (1.0 + 3.0 * GELU_B * v * v))


def normed(values, par_ref, part=slice(None)):
    return values * par_ref[0:1, part] + par_ref[1:2, part]


def normal_of(values, par_ref, part=slice(None)):
    return values * par_ref[2:3, part] + par_ref[3:4, part]


def norm_gradient(upstream, values, par_ref, back_ref, mask, part=slice(None)):
    normal = normal_of(values, par_ref, part)
    return upstream * back_ref[0:1, part] - mask * (back_ref[1:2, part] + normal * back_ref[2:3, part])


def sums_block(weighted, values):
    n = weighted.shape[1] // 128
    sums = (
        jnp.sum(weighted, axis=0, keepdims=True),
        jnp.sum(weighted * values, axis=0, keepdims=True),
    )
    return jnp.concatenate([v[:, c * 128 : c * 128 + 128] for v in sums for c in range(n)], axis=0)


def write_stats(stat_ref, weighted, values):
    stat_ref[...] = jnp.broadcast_to(sums_block(weighted, values)[None], stat_ref.shape)


def product_forward_body(x_ref, mask_ref, w_ref, low_ref, out_ref, stat_ref, x_buf, low_buf, sems):
    wide = x_ref.shape[1]
    coming = columns_moving(x_ref, x_buf, sems.at[0])
    total, going = None, []
    for s, part in blocks(wide):
        coming[s].wait()
        low_buf[:, part] = x_buf[:, part].astype(bf16)
        going.append(moving(low_buf.at[:, part], low_ref.at[:, part], sems.at[1, s]))
        term = dot(low_buf[:, part], w_ref[:, part], NT)
        total = term if total is None else total + term
    out_ref[...] = total
    write_stats(stat_ref, total * mask_ref[:, 0:1], total)
    for copy in going:
        copy.wait()


def product_forward(x, mask_wide, weight, devices):
    n, wide = x.shape
    return call(
        product_forward_body,
        (x, mask_wide, weight),
        "hvv",
        (shaped(n, wide, dtype=bf16), shaped(n, MID), shaped(devices, 8, 128)),
        "hvv",
        5,
        20,
        [VMEM((n, wide), f32), VMEM((n, wide), bf16), DMA((2, wide // STEP))],
    )


def expand_forward_body(*refs):
    *y_refs, par_ref, mask_ref, e_ref, mid_ref, out_ref, stat_ref, e_buf, out_buf, sems = refs
    coming = rows_moving(e_ref, e_buf, sems.at[0])
    mask = mask_ref[:, 0:1]
    at = 0
    for y_ref in y_refs:
        part = slice(at, at + y_ref.shape[0])
        mid_ref[part, :] = (gelu(normed(y_ref[...], par_ref)) * mask_ref[part, 0:1]).astype(bf16)
        at += y_ref.shape[0]
    going = []
    for s, part in blocks(e_ref.shape[0]):
        coming[s].wait()
        out = dot(mid_ref[...], e_buf[part, :], NT)
        out_buf[:, part] = out.astype(bf16)
        going.append(moving(out_buf.at[:, part], out_ref.at[:, part], sems.at[1, s]))
        stat_ref[s * 8 : s * 8 + 8, :] = sums_block(out * mask, out)
    for copy in going:
        copy.wait()


def expand_forward(y_parts, par, mask_wide, weight):
    n, wide = mask_wide.shape[0], weight.shape[0]
    return call(
        expand_forward_body,
        (*y_parts, par, mask_wide, weight),
        "v" * (len(y_parts) + 2) + "h",
        (shaped(n, MID, dtype=bf16), shaped(n, wide, dtype=bf16), shaped(wide // 64, 128)),
        "vhv",
        4,
        16,
        [VMEM(weight.shape, bf16), VMEM((n, wide), bf16), DMA((2, wide // STEP))],
    )


def first_forward_body(
    y_ref, par_ref, x_ref, mask_ref, w_ref, low_ref, out_ref, stat_ref,
    y_buf, x_buf, w_buf, low_buf, sems
):
    wide = x_ref.shape[1]
    coming_y = columns_moving(y_ref, y_buf, sems.at[0])
    coming_x = columns_moving(x_ref, x_buf, sems.at[1])
    coming_w = columns_moving(w_ref, w_buf, sems.at[2])
    mask = mask_ref[:, 0:1]
    total, going = None, []
    for s, part in blocks(wide):
        coming_y[s].wait()
        coming_x[s].wait()
        first = gelu(normed(y_buf[:, part].astype(f32), par_ref, part) + x_buf[:, part]) * mask
        low_buf[:, part] = first.astype(bf16)
        going.append(moving(low_buf.at[:, part], low_ref.at[:, part], sems.at[3, s]))
        coming_w[s].wait()
        term = dot(low_buf[:, part], w_buf[:, part], NT)
        total = term if total is None else total + term
    out_ref[...] = total
    write_stats(stat_ref, total * mask, total)
    for copy in going:
        copy.wait()


def first_forward(y, par, x, mask_wide, weight, devices):
    n, wide = y.shape
    return call(
        first_forward_body,
        (y, par, x, mask_wide, weight),
        "hvhvh",
        (shaped(n, wide, dtype=bf16), shaped(n, MID), shaped(devices, 8, 128)),
        "hvv",
        6,
        24,
        [
            VMEM((n, wide), bf16),
            VMEM((n, wide), f32),
            VMEM(weight.shape, bf16),
            VMEM((n, wide), bf16),
            DMA((4, wide // STEP)),
        ],
    )


def output_stage_body(
    y_ref, par_ref, first_ref, cot_ref, mask_ref, out_ref, dt_ref, stat_ref,
    y_buf, first_buf, cot_buf, out_buf, dt_buf, sems
):
    wide = y_ref.shape[1]
    coming_y = columns_moving(y_ref, y_buf, sems.at[0])
    coming_f = columns_moving(first_ref, first_buf, sems.at[1])
    coming_c = columns_moving(cot_ref, cot_buf, sems.at[2])
    mask = mask_ref[:, 0:1]
    going = []
    for s, part in blocks(wide):
        coming_y[s].wait()
        coming_f[s].wait()
        y = y_buf[:, part].astype(f32)
        pre = normed(y, par_ref, part) + first_buf[:, part].astype(f32)
        t = jnp.tanh(GELU_A * (pre + GELU_B * pre * pre * pre))
        out_buf[:, part] = 0.5 * pre * (1.0 + t) * mask
        going.append(moving(out_buf.at[:, part], out_ref.at[:, part], sems.at[3, s]))
        slope = 0.5 * (1.0 + t) + 0.5 * pre * (1.0 - t * t) * (GELU_A * (1.0 + 3.0 * GELU_B * pre * pre))
        coming_c[s].wait()
        dt = slope * (cot_buf[:, part] * mask)
        dt_buf[:, part] = dt.astype(bf16)
        going.append(moving(dt_buf.at[:, part], dt_ref.at[:, part], sems.at[4, s]))
        stat_ref[s * 8 : s * 8 + 8, :] = sums_block(dt, normal_of(y, par_ref, part))
    for copy in going:
        copy.wait()


def output_stage(y, par, first, cot, mask_wide):
    n, wide = y.shape
    return call(
        output_stage_body,
        (y, par, first, cot, mask_wide),
        "hvhhv",
        (shaped(n, wide), shaped(n, wide, dtype=bf16), shaped(wide // 64, 128)),
        "hhv",
        8,
        28,
        [
            VMEM((n, wide), bf16),
            VMEM((n, wide), bf16),
            VMEM((n, wide), f32),
            VMEM((n, wide), f32),
            VMEM((n, wide), bf16),
            DMA((5, wide // STEP)),
        ],
    )


def expand_backward_body(
    dt_ref, y_ref, par_ref, back_ref, mask_ref, e_ref, mid_y_ref, mid_par_ref,
    dy_ref, mid_dt_ref, stat_ref, dt_buf, y_buf, e_buf, dy_buf, sems
):
    wide = dt_ref.shape[1]
    coming_dt = columns_moving(dt_ref, dt_buf, sems.at[0])
    coming_y = columns_moving(y_ref, y_buf, sems.at[1])
    coming_e = rows_moving(e_ref, e_buf, sems.at[2])
    mask = mask_ref[:, 0:1]
    total, going = None, []
    for s, part in blocks(wide):
        coming_dt[s].wait()
        coming_y[s].wait()
        dt, y = dt_buf[:, part].astype(f32), y_buf[:, part].astype(f32)
        dy = norm_gradient(dt, y, par_ref, back_ref, mask, part).astype(bf16)
        dy_buf[:, part] = dy
        going.append(moving(dy_buf.at[:, part], dy_ref.at[:, part], sems.at[3, s]))
        coming_e[s].wait()
        term = dot(dy, e_buf[part, :])
        total = term if total is None else total + term
    y = mid_y_ref[...]
    dt = gelu_slope(normed(y, mid_par_ref)) * (total * mask)
    mid_dt_ref[...] = dt
    write_stats(stat_ref, dt, normal_of(y, mid_par_ref))
    for copy in going:
        copy.wait()


def expand_backward(dt, y, par, back, mask_wide, weight, mid_y, mid_par, devices, through=()):
    n, wide = y.shape
    return call(
        expand_backward_body,
        (dt, y, par, back, mask_wide, weight, mid_y, mid_par),
        "hhvvvhvv",
        (shaped(n, wide, dtype=bf16), shaped(n, MID), shaped(devices, 8, 128)),
        "hvv",
        5,
        24,
        [
            VMEM((n, wide), bf16),
            VMEM((n, wide), bf16),
            VMEM(weight.shape, bf16),
            VMEM((n, wide), bf16),
            DMA((4, wide // STEP)),
        ],
        through=through,
    )


def residual_backward_body(
    dt_ref, y_ref, par_ref, back_ref, mask_ref, w_ref, add_ref, wide_y_ref, wide_par_ref, x_ref,
    dy_ref, out_ref, stat_ref, w_buf, add_buf, y_buf, x_buf, out_buf, sems
):
    wide = x_ref.shape[1]
    coming = [
        columns_moving(source, target, sems.at[t])
        for t, (source, target) in enumerate(
            ((w_ref, w_buf), (add_ref, add_buf), (wide_y_ref, y_buf), (x_ref, x_buf))
        )
    ]
    mask = mask_ref[:, 0:1]
    dy_ref[...] = norm_gradient(dt_ref[...], y_ref[...], par_ref, back_ref, mask).astype(bf16)
    going = []
    for s, part in blocks(wide):
        for copies in coming:
            copies[s].wait()
        grad = add_buf[:, part].astype(f32) + dot(dy_ref[...], w_buf[:, part])
        y = y_buf[:, part].astype(f32)
        pre = normed(y, wide_par_ref, part) + x_buf[:, part].astype(f32)
        dt = gelu_slope(pre) * (grad * mask)
        out_buf[:, part] = dt.astype(bf16)
        going.append(moving(out_buf.at[:, part], out_ref.at[:, part], sems.at[4, s]))
        stat_ref[s * 8 : s * 8 + 8, :] = sums_block(dt, normal_of(y, wide_par_ref, part))
    for copy in going:
        copy.wait()


def residual_backward(dt, y, par, back, mask_wide, weight, add, wide_y, wide_par, x):
    n, wide = x.shape
    return call(
        residual_backward_body,
        (dt, y, par, back, mask_wide, weight, add, wide_y, wide_par, x),
        "vvvvvhhhvh",
        (shaped(n, MID, dtype=bf16), shaped(n, wide, dtype=bf16), shaped(wide // 64, 128)),
        "vhv",
        6,
        24,
        [VMEM(weight.shape, bf16)] + [VMEM((n, wide), bf16)] * 4 + [DMA((5, wide // STEP))],
    )


def input_backward_body(dy_ref, w_ref, add_ref, out_ref, w_buf, add_buf, out_buf, sems):
    coming_w = columns_moving(w_ref, w_buf, sems.at[0])
    coming_a = columns_moving(add_ref, add_buf, sems.at[1])
    going = []
    for s, part in blocks(w_ref.shape[1]):
        coming_w[s].wait()
        coming_a[s].wait()
        out_buf[:, part] = add_buf[:, part].astype(f32) + dot(dy_ref[...], w_buf[:, part])
        going.append(moving(out_buf.at[:, part], out_ref.at[:, part], sems.at[2, s]))
    for copy in going:
        copy.wait()


def input_backward(dy, weight, add, token):
    n, wide = add.shape
    return call(
        input_backward_body,
        (dy, weight, add),
        "vhh",
        (shaped(n, wide),),
        "h",
        5,
        20,
        [VMEM(weight.shape, bf16), VMEM((n, wide), bf16), VMEM((n, wide), f32), DMA((3, wide // STEP))],
        token=token,
    )


def hidden_backward_body(*refs):
    *piece_refs, y_ref, par_ref, mask_ref, dt_ref, stat_ref = refs
    batch = len(piece_refs) // 4
    pixels = y_ref.shape[0] // batch
    for b in range(batch):
        own, near, up, down = [ref[...].astype(f32) for ref in piece_refs[4 * b : 4 * b + 4]]
        dt_ref[b * pixels : (b + 1) * pixels, :] = own + near + up + down
    grad = dt_ref[...]
    y = y_ref[...]
    dt = gelu_slope(normed(y, par_ref)) * (grad * mask_ref[:, 0:1])
    dt_ref[...] = dt
    write_stats(stat_ref, dt, normal_of(y, par_ref))


def hidden_backward(pieces, y, par, mask_wide, devices, through):
    n = y.shape[0]
    return call(
        hidden_backward_body,
        (*pieces, y, par, mask_wide),
        "v" * (len(pieces) + 3),
        (shaped(n, MID), shaped(devices, 8, 128)),
        "vv",
        3,
        16,
        through=through,
    )


def last_gradient_body(
    dt_ref, y_ref, par_ref, back_ref, mask_ref, acts_ref, dy_ref, send_ref, keep_ref,
    dyt_ref, acts_buf, out_buf, in_sems, out_sems
):
    coming = columns_moving(acts_ref, acts_buf, in_sems)
    dy = norm_gradient(dt_ref[...], y_ref[...], par_ref, back_ref, mask_ref[:, 0:1]).astype(bf16)
    dy_ref[...] = dy
    dyt_ref[...] = dy.astype(f32).T.astype(bf16)
    core = lax.axis_index("ch") % 2
    half, base = send_ref.shape[0], send_ref.shape[1]
    going = []
    for s, part in blocks(acts_ref.shape[1]):
        coming[s].wait()
        out_buf[:, part] = dot(dyt_ref[...], acts_buf[:, part]).astype(bf16)
        for q in range(half):
            for t, (out_ref, side) in enumerate(((send_ref, 1 - core), (keep_ref, core))):
                row = pl.multiple_of((2 * q + side) * base, 16)
                going.append(
                    moving(
                        out_buf.at[pl.ds(row, base), part], out_ref.at[q, :, part], out_sems.at[s, q, t]
                    )
                )
    for copy in going:
        copy.wait()


def last_gradient(dt, y, par, back, mask_wide, acts, ch, through, token):
    n, wide = acts.shape
    half = shaped(ch // 2, MID // ch, wide, dtype=bf16)
    return call(
        last_gradient_body,
        (dt, y, par, back, mask_wide, acts),
        "vvvvvh",
        (shaped(n, MID, dtype=bf16), half, half),
        "vhh",
        6,
        20,
        [
            VMEM((MID, n), bf16),
            VMEM((n, wide), bf16),
            VMEM((MID, wide), bf16),
            DMA((wide // STEP,)),
            DMA((wide // STEP, ch // 2, 2)),
        ],
        through=through,
        token=token,
    )


def cast_body(v_ref, out_ref):
    out_ref[...] = v_ref[...].astype(bf16)


def cast_after(values, *after):
    return call(cast_body, (values,), "v", (shaped(*values.shape, dtype=bf16),), "v", 2, 12, after=after)[0]


def pack_body(*refs, count, bit_axis, rows):
    part_refs, (send_ref, keep_ref), refs = refs[:count], refs[count : count + 2], refs[count + 2 :]
    buffers, (in_sem, out_sem) = refs[:count], refs[count:]
    coming = [moving(ref, buf, in_sem.at[t]) for t, (ref, buf) in enumerate(zip(part_refs, buffers))]
    bit = lax.axis_index(bit_axis) % 2
    tall = send_ref.shape[1]
    base = rows * tall
    going, at = [], 0
    for copy, buf in zip(coming, buffers):
        copy.wait()
        wide = buf.shape[1]
        for block in range(buf.shape[0] // base):
            for pair in range(rows // 2):
                for out_ref, side in ((send_ref, 1 - bit), (keep_ref, bit)):
                    row = pl.multiple_of(block * base + (2 * pair + side) * tall, 16)
                    going.append(
                        moving(
                            buf.at[pl.ds(row, tall), :],
                            out_ref.at[pair, :, at : at + wide],
                            out_sem.at[len(going)],
                        )
                    )
            at += wide
    for copy in going:
        copy.wait()


def pack_split(parts, base, rows, token=None):
    count = len(parts)
    blocks_in = sum(p.shape[0] // base for p in parts)
    wide = sum(p.shape[0] // base * p.shape[1] for p in parts)
    half = shaped(rows // 2, base // rows, wide, dtype=bf16)
    return call(
        functools.partial(pack_body, count=count, bit_axis="rows", rows=rows),
        tuple(parts),
        "h" * count,
        (half, half),
        "hh",
        3,
        16,
        [VMEM(p.shape, bf16) for p in parts] + [DMA((count,)), DMA((blocks_in * rows,))],
        token=token,
    )


def step_body(got_ref, kept_ref, send_ref, keep_ref, sum_ref, *, axis, step):
    bit = lax.axis_index(axis) // step % 2
    sum_ref[...] = (got_ref[...].astype(f32) + kept_ref[...].astype(f32)).astype(bf16)
    for pair in range(send_ref.shape[0]):
        send_ref[pair] = sum_ref[2 * pair + 1 - bit]
        keep_ref[pair] = sum_ref[2 * pair + bit]


def step_split(got, kept, axis, step, token=None):
    half = shaped(got.shape[0] // 2, *got.shape[1:], dtype=bf16)
    return call(
        functools.partial(step_body, axis=axis, step=step),
        (got, kept),
        "vv",
        (half, half),
        "vv",
        2,
        12,
        [VMEM(got.shape, bf16)],
        token=token,
    )


def sum_body(got_ref, kept_ref, sum_ref):
    sum_ref[...] = (got_ref[...].astype(f32) + kept_ref[...].astype(f32)).astype(bf16)


def step_sum(got, kept, token):
    return call(sum_body, (got, kept), "vv", (shaped(*got.shape, dtype=bf16),), "v", 1, 12, token=token)


def join_body(got_ref, kept_ref, out_ref, *, step):
    bit = lax.axis_index("rows") // step % 2
    for a in range(got_ref.shape[0]):
        out_ref[2 * a + bit] = kept_ref[a]
        out_ref[2 * a + 1 - bit] = got_ref[a]


def join_step(got, kept, step, token):
    m, r, wide = got.shape
    return call(
        functools.partial(join_body, step=step),
        (got, kept),
        "vv",
        (shaped(2 * m, r, wide, dtype=bf16),),
        "v",
        1,
        12,
        token=token,
    )


def final_body(got_ref, kept_ref, *refs, cuts):
    out_refs, refs = refs[: len(cuts)], refs[len(cuts) :]
    buffers, sems = refs[: len(cuts)], refs[len(cuts)]
    bit = lax.axis_index("rows") % 2
    going, at = [], 0
    for out_ref, buf, (count, wide) in zip(out_refs, buffers, cuts):
        for k in range(count):
            part = slice(at, at + wide)
            for a in range(got_ref.shape[0]):
                buf[k, 2 * a + bit] = kept_ref[a, :, part].astype(f32)
                buf[k, 2 * a + 1 - bit] = got_ref[a, :, part].astype(f32)
            going.append(moving(buf.at[k], out_ref.at[k], sems.at[len(going)]))
            at += wide
    for copy in going:
        copy.wait()


def final_join(got, kept, cuts, token):
    m, r, _ = got.shape
    outs = [shaped(count, 2 * m, r, wide) for count, wide in cuts]
    *outs, token = call(
        functools.partial(final_body, cuts=cuts),
        (got, kept),
        "vv",
        outs,
        "h" * len(outs),
        2,
        20,
        [VMEM(o.shape, f32) for o in outs] + [DMA((sum(count for count, _ in cuts),))],
        token=token,
    )
    return [o.reshape(-1, o.shape[3]) for o in outs], token


def owned_body(*refs):
    n = len(refs) // 3
    for k in range(n):
        size = refs[n + 2 * k].shape[1]
        start = lax.axis_index("ch") * size
        turned = pltpu.roll(refs[k][...], refs[k].shape[1] - start, 1)
        refs[n + 2 * k][...] = turned[0:1, :size]
        refs[n + 2 * k + 1][...] = turned[1:2, :size]


def owned(sums, ch, token):
    outs = [shaped(1, s.shape[1] // ch) for s in sums for _ in range(2)]
    *outs, token = call(
        owned_body, tuple(sums), "v" * len(sums), outs, "v" * len(outs), 1, 12, token=token
    )
    return [o.reshape(-1) for o in outs], token


def return_body(*refs, batch):
    ins, outs = refs[: 5 * batch], refs[5 * batch :]
    odd = lax.axis_index("rows") % 2 == 1
    for b in range(batch):
        far_up_ref, up_ref, down_ref, far_down_ref, got_ref = ins[5 * b : 5 * b + 5]
        below_ref, above_ref, partner_ref = outs[3 * b : 3 * b + 3]

        @pl.when(odd)
        def _():
            total = far_up_ref[...].astype(f32) + got_ref[...].astype(f32)
            below_ref[...] = total.astype(bf16)
            above_ref[...] = far_down_ref[...]
            partner_ref[...] = up_ref[...]

        @pl.when(jnp.logical_not(odd))
        def _():
            total = far_down_ref[...].astype(f32) + got_ref[...].astype(f32)
            below_ref[...] = far_up_ref[...]
            above_ref[...] = total.astype(bf16)
            partner_ref[...] = down_ref[...]


def return_step(tiles, got):
    far_up, up, _, down, far_down = tiles
    piece = shaped(*got.shape, dtype=bf16)
    return call(
        functools.partial(return_body, batch=1),
        (far_up, up, down, far_down, got),
        "vvvvv",
        (piece, piece, piece),
        "vvv",
        2,
        12,
    )


def shift_lanes(values, by, width):
    place = lax.broadcasted_iota(jnp.int32, values.shape, values.ndim - 1) % width
    moved = pltpu.roll(values, by % values.shape[-1], values.ndim - 1)
    return jnp.where((place >= by) & (place < width + by), moved, 0.0)


def shift_rows(values, by, width):
    place = lax.broadcasted_iota(jnp.int32, values.shape, 0) % width
    moved = pltpu.roll(values, by % values.shape[0], 0)
    return jnp.where((place >= by) & (place < width + by), moved, 0.0)


def offset_fraction(ext_ref, ow_ref, b, base, pixels, width):
    u = None
    for i in range(3):
        start = (base + 2 * i) * width
        term = dot(ow_ref[i], ext_ref[b, start : start + pixels, :], NT)
        u = term if u is None else u + term
    total = u[32:64]
    total = total + shift_lanes(u[0:32], 2, width) + shift_lanes(u[64:96], -2, width)
    return 1.0 / (1.0 + jnp.exp(-total))


def deform_forward_body(*refs, batch, rows, width, deep):
    tile_refs, refs = refs[:5], refs[5:]
    ow_ref, disp_ref, m_ref, mask_ref, cols_out_ref, y_ref, frac_ref, stat_ref = refs[:8]
    ext_ref, par_ref, s_ref, cols_ref, m_buf, tile_sems, sems = refs[8:]
    pixels = rows * width
    coming = [
        moving(ref, ext_ref.at[:, t * pixels : (t + 1) * pixels, :], tile_sems.at[t])
        for t, ref in enumerate(tile_refs)
    ]
    coming_m = moving(m_ref, m_buf, sems.at[0])
    for copy in coming:
        copy.wait()
    lane = lax.broadcasted_iota(jnp.int32, (32, 128), 1)
    column = lane % width
    upper = lane // width

    def image(b, carry):
        frac = offset_fraction(ext_ref, ow_ref, b, deep - 2, pixels, width)
        for i in range(4):
            frac_ref[b, i] = frac[i * 8 : i * 8 + 8]
        pix = lax.broadcasted_iota(jnp.int32, (1, pixels), 1)
        row_at, col_at = pix // width, pix % width
        tops, lefts, ys, xs = [], [], [], []
        for k in range(9):
            i, j = k // 3, k % 3
            tops.append(row_at + disp_ref[b, i, 2 * j : 2 * j + 1, :] + (deep - 2))
            lefts.append(col_at + 2 * (j - 1) + disp_ref[b, i, 2 * j + 1 : 2 * j + 2, :])
            at = i * 8 + 2 * j
            ys.append(frac[at : at + 1])
            xs.append(frac[at + 1 : at + 2])
        blank = jnp.zeros((23, pixels), f32)
        par = jnp.concatenate(
            [jnp.concatenate(g, axis=0).astype(f32) if g is not None else blank
             for g in (tops, None, lefts, None, ys, None, xs, None)], axis=0)
        par_ref[...] = par.T

        def row_of_taps(i, carry):
            for j in range(3):
                k = i * 3 + j
                for c in range(pixels // 32):
                    p = pltpu.roll(par_ref[c * 32 : c * 32 + 32, :], 128 - k, 1)
                    wide = (32, 128)
                    top = jnp.broadcast_to(p[:, 0:1], wide).astype(jnp.int32) - upper
                    left = jnp.broadcast_to(p[:, 32:33], wide).astype(jnp.int32)
                    fy = jnp.broadcast_to(p[:, 64:65], wide)
                    fx = jnp.broadcast_to(p[:, 96:97], wide)
                    cw = jnp.where(column == left, 1.0 - fx, jnp.where(column == left + 1, fx, 0.0))
                    ca, cb = (1.0 - fy) * cw, fy * cw
                    for q in range(8):
                        s = jnp.where(top == 2 * q, ca, jnp.where(top == 2 * q - 1, cb, 0.0))
                        s_ref[j * pixels + c * 32 : j * pixels + c * 32 + 32, q * 128 : q * 128 + 128] = s.astype(bf16)
            start = pl.multiple_of(i * 2 * width, 128)
            window = ext_ref[b, pl.ds(start, 16 * width), :]
            for j in range(3):
                got = dot(s_ref[j * pixels : (j + 1) * pixels, :], window).astype(bf16)
                cols_ref[pl.ds(pl.multiple_of(b * pixels, pixels), pixels), pl.ds(pl.multiple_of((i * 3 + j) * MID, MID), MID)] = got
            return carry

        return lax.fori_loop(0, 3, row_of_taps, carry)

    lax.fori_loop(0, batch, image, 0)
    going = moving(cols_ref, cols_out_ref, sems.at[1])
    coming_m.wait()
    y = dot(cols_ref[...], m_buf[...], NT)
    y_ref[...] = y
    write_stats(stat_ref, y * mask_ref[:, 0:1], y)
    going.wait()


def deform_forward(tiles, offset_rows, disp, weight, mask_wide, rows, width, devices):
    batch = tiles[0].shape[0]
    pixels = rows * width
    n = batch * pixels
    return call(
        functools.partial(deform_forward_body, batch=batch, rows=rows, width=width, deep=2 * rows),
        (*tiles, offset_rows, disp, weight, mask_wide),
        "hhhhhvvhv",
        (
            shaped(n, 9 * MID, dtype=bf16),
            shaped(n, MID),
            shaped(batch, 4, 8, pixels),
            shaped(devices, 8, 128),
        ),
        "hvvv",
        15,
        30,
        [
            VMEM((batch, 5 * pixels, MID), bf16),
            VMEM((pixels, 128), f32),
            VMEM((3 * pixels, 16 * width), bf16),
            VMEM((n, 9 * MID), bf16),
            VMEM(weight.shape, bf16),
            DMA((5,)),
            DMA((2,)),
        ],
    )


def deform_backward_body(*refs, rows, width, deep, which):
    tile_refs, refs = refs[:5], refs[5:]
    (ow_ref, disp_ref, frac_ref, m_ref, dy_ref), refs = refs[:5], refs[5:]
    out_refs, refs = refs[:5], refs[5:]
    dow_ref, ext_ref, dext_ref, dc_ref, g_ref, st_ref, df_ref, m_buf, tile_sems, m_sems = refs
    pixels = rows * width
    coming = [
        moving(ref.at[which], ext_ref.at[0, t * pixels : (t + 1) * pixels, :], tile_sems.at[t])
        for t, ref in enumerate(tile_refs)
    ]
    coming_m = taps_moving(m_ref, m_buf, m_sems)
    window = 16 * width
    dow_ref[...] = jnp.zeros_like(dow_ref)
    dext_ref[...] = jnp.zeros_like(dext_ref)
    for copy in coming:
        copy.wait()

    def image(b, carry):
        def row_of_taps(i, carry):
            dy = dy_ref[which * pixels : (which + 1) * pixels, :]
            for j in range(3):
                m = m_buf[:, (i * 3 + j) * MID : (i * 3 + j + 1) * MID]
                dc_ref[j * pixels : (j + 1) * pixels, :] = dot(dy, m).astype(bf16)
            start = i * 2 * width
            g_ref[...] = dot(ext_ref[b, pl.ds(start, window), :], dc_ref[...], NT)
            place = lax.broadcasted_iota(jnp.int32, (width, 128), 0)
            for j in range(3):
                for h in range(pixels // 128):
                    lanes = slice(h * 128, h * 128 + 128)
                    at_l = slice(j * pixels + h * 128, j * pixels + h * 128 + 128)
                    pix = lax.broadcasted_iota(jnp.int32, (1, 128), 1) + h * 128
                    by_y, by_x = slice(2 * j, 2 * j + 1), slice(2 * j + 1, 2 * j + 2)
                    top = pix // width + disp_ref[which, i, by_y, lanes] + (deep - 2)
                    left = pix % width + 2 * (j - 1) + disp_ref[which, i, by_x, lanes]
                    fy = frac_ref[which, i, by_y, lanes]
                    fx = frac_ref[which, i, by_x, lanes]
                    here, after = place == left, place == left + 1
                    cw = jnp.where(here, 1.0 - fx, jnp.where(after, fx, 0.0))
                    ca, cb = (1.0 - fy) * cw, fy * cw
                    low_sum = jnp.zeros((width, 128), f32)
                    high_sum = jnp.zeros((width, 128), f32)
                    for r in range(16):
                        part = slice(r * width, r * width + width)
                        g = g_ref[part, at_l]
                        m0, m1 = top == r, top == r - 1
                        low_sum = low_sum + jnp.where(m0, g, 0.0)
                        high_sum = high_sum + jnp.where(m1, g, 0.0)
                        st_ref[part, at_l] = jnp.where(m0, ca, jnp.where(m1, cb, 0.0)).astype(bf16)
                    d_fy = jnp.sum((high_sum - low_sum) * cw, axis=0, keepdims=True)
                    mixed = (1.0 - fy) * low_sum + fy * high_sum
                    d_fx = jnp.sum(
                        jnp.where(after, mixed, 0.0) - jnp.where(here, mixed, 0.0), axis=0, keepdims=True)
                    df_ref[i, by_y, lanes] = d_fy * fy * (1.0 - fy)
                    df_ref[i, by_x, lanes] = d_fx * fx * (1.0 - fx)
            dext_ref[b, pl.ds(start, window), :] += dot(st_ref[...], dc_ref[...])
            return carry

        df_ref[...] = jnp.zeros_like(df_ref)
        for i in range(3):
            coming_m[i].wait()
            row_of_taps(i, carry)
        d_off = df_ref[...].reshape(32, pixels).astype(bf16).astype(f32)
        stacked = jnp.concatenate(
            [shift_lanes(d_off, -2, width), d_off, shift_lanes(d_off, 2, width)], axis=0)
        across = jnp.concatenate([stacked, jnp.zeros((32, pixels), f32)], axis=0).T.astype(bf16)
        stacked = stacked.astype(bf16)
        for i in range(3):
            first = (deep - 2 + 2 * i) * width
            part = slice(first, first + pixels)
            dow_ref[i] += dot(stacked, ext_ref[b, part, :])
            dext_ref[b, part, :] += dot(across[:, :96], ow_ref[i])
        return carry

    image(0, 0)
    for t, ref in enumerate(out_refs):
        ref[...] = dext_ref[t // 5, t % 5 * pixels : (t % 5 + 1) * pixels, :].astype(ref.dtype)


def deform_backward(which, tiles, offset_rows, disp, frac, weight, dy, rows, width, after, through):
    pixels = rows * width
    return call(
        functools.partial(deform_backward_body, rows=rows, width=width, deep=2 * rows, which=which),
        (*tiles, offset_rows, disp, frac, weight, dy),
        "hhhhhvvvhv",
        tuple(shaped(pixels, MID, dtype=f32 if t == 2 else bf16) for t in range(5)) + (shaped(3, 96, MID),),
        "vvvvvv",
        10,
        32,
        [
            VMEM((1, 5 * pixels, MID), bf16),
            VMEM((1, 5 * pixels, MID), f32),
            VMEM((3 * pixels, MID), bf16),
            VMEM((16 * width, 3 * pixels), f32),
            VMEM((16 * width, 3 * pixels), bf16),
            VMEM((4, 8, pixels), f32),
            VMEM(weight.shape, bf16),
            DMA((5,)),
            DMA((3,)),
        ],
        after,
        through,
    )


def taps_moving(m_ref, m_buf, sems):
    wide = 3 * MID
    return columns_moving(m_ref, m_buf, sems, wide)


def rim_moving(parts, rim_ref, sems):
    copies, at = [], 0
    for t, ref in enumerate(parts):
        copies.append(moving(ref, rim_ref.at[:, at : at + ref.shape[1], :], sems.at[t]))
        at += ref.shape[1]
    return copies


def conv_forward_body(
    above_ref, own_ref, below_ref, m_ref, mask_ref, y_ref, stat_ref, rim_ref, m_buf, rim_sems, sems,
    *, batch, rows, width
):
    pixels = rows * width
    coming = taps_moving(m_ref, m_buf, sems)
    for copy in rim_moving((above_ref, own_ref, below_ref), rim_ref, rim_sems):
        copy.wait()
    sums = [[None] * 3 for _ in range(batch)]
    for i in range(3):
        coming[i].wait()
        for b in range(batch):
            for j in range(3):
                k = i * 3 + j
                start = 2 * i * width
                term = dot(rim_ref[b, start : start + pixels, :], m_buf[:, k * MID : (k + 1) * MID], NT)
                sums[b][j] = term if i == 0 else sums[b][j] + term
    for b in range(batch):
        total = sums[b][1] + shift_rows(sums[b][0], 2, width) + shift_rows(sums[b][2], -2, width)
        y_ref[b * pixels : (b + 1) * pixels, :] = total
    y = y_ref[...]
    write_stats(stat_ref, y * mask_ref[:, 0:1], y)


def conv_forward(rim, weight, mask_wide, rows, width, devices):
    batch = rim[0].shape[0]
    n = batch * rows * width
    return call(
        functools.partial(conv_forward_body, batch=batch, rows=rows, width=width),
        (*rim, weight, mask_wide),
        "hhhhv",
        (shaped(n, MID), shaped(devices, 8, 128)),
        "vv",
        5,
        24,
        [VMEM((batch, (rows + 4) * width, MID), bf16), VMEM(weight.shape, bf16), DMA((3,)), DMA((3,))],
    )


def conv_backward_body(
    above_ref, own_ref, below_ref, m_ref, y_ref, par_ref, mask_ref, dt_ref, stat_ref,
    rim_ref, m_buf, rim_sems, sems, *, batch, rows, width
):
    pixels = rows * width
    coming = taps_moving(m_ref, m_buf, sems)
    for copy in rim_moving((above_ref, own_ref, below_ref), rim_ref, rim_sems):
        copy.wait()
    sums = [[None] * 3 for _ in range(batch)]
    for i in range(3):
        coming[i].wait()
        for b in range(batch):
            for j in range(3):
                k = i * 3 + j
                start = (4 - 2 * i) * width
                term = dot(rim_ref[b, start : start + pixels, :], m_buf[:, k * MID : (k + 1) * MID])
                sums[b][j] = term if i == 0 else sums[b][j] + term
    for b in range(batch):
        total = sums[b][1] + shift_rows(sums[b][0], -2, width) + shift_rows(sums[b][2], 2, width)
        dt_ref[b * pixels : (b + 1) * pixels, :] = total
    y = y_ref[...]
    dt = gelu_slope(normed(y, par_ref)) * (dt_ref[...] * mask_ref[:, 0:1])
    dt_ref[...] = dt
    write_stats(stat_ref, dt, normal_of(y, par_ref))


def conv_backward(rim, weight, y, par, mask_wide, rows, width, devices, after):
    batch = rim[0].shape[0]
    n = batch * rows * width
    return call(
        functools.partial(conv_backward_body, batch=batch, rows=rows, width=width),
        (*rim, weight, y, par, mask_wide),
        "hhhhvvv",
        (shaped(n, MID), shaped(devices, 8, 128)),
        "vv",
        6,
        24,
        [VMEM((batch, (rows + 4) * width, MID), bf16), VMEM(weight.shape, bf16), DMA((3,)), DMA((3,))],
        after,
    )


def conv_weight_body(
    dy_ref, above_ref, own_ref, below_ref, out_ref, rim_ref, dyt_ref, out_buf, rim_sems, sems,
    *, batch, rows, width
):
    pixels = rows * width
    coming = rim_moving((above_ref, own_ref, below_ref), rim_ref, rim_sems)
    dy = dy_ref[...].astype(f32)
    going = []
    for j in range(3):
        moved = shift_rows(dy, 2 * (j - 1), width) if j != 1 else dy
        dyt_ref[j] = moved.T.astype(bf16)
        if j == 0:
            for copy in coming:
                copy.wait()
        for i in range(3):
            part = slice((i * 3 + j) * MID, (i * 3 + j + 1) * MID)
            start = 2 * i * width
            total = None
            for b in range(batch):
                term = dot(dyt_ref[j, :, b * pixels : (b + 1) * pixels], rim_ref[b, start : start + pixels, :])
                total = term if total is None else total + term
            out_buf[:, part] = total.astype(bf16)
            going.append(moving(out_buf.at[:, part], out_ref.at[:, part], sems.at[i * 3 + j]))
    for copy in going:
        copy.wait()


def conv_weight_gradient(dy, rim, rows, width, after):
    batch = rim[0].shape[0]
    return call(
        functools.partial(conv_weight_body, batch=batch, rows=rows, width=width),
        (dy, *rim),
        "vhhh",
        (shaped(MID, 9 * MID, dtype=bf16),),
        "h",
        6,
        20,
        [
            VMEM((batch, (rows + 4) * width, MID), bf16),
            VMEM((3, MID, batch * rows * width), bf16),
            VMEM((MID, 9 * MID), bf16),
            DMA((3,)),
            DMA((9,)),
        ],
        after,
    )[0]


def columns_weight_body(dy_ref, cols_ref, out_ref, dyt_ref, cols_buf, out_buf, sems):
    coming = columns_moving(cols_ref, cols_buf, sems.at[0])
    dyt_ref[...] = dy_ref[...].astype(f32).T.astype(bf16)
    going = []
    for s, part in blocks(cols_ref.shape[1]):
        coming[s].wait()
        out_buf[:, part] = dot(dyt_ref[...], cols_buf[:, part]).astype(bf16)
        going.append(moving(out_buf.at[:, part], out_ref.at[:, part], sems.at[1, s]))
    for copy in going:
        copy.wait()


def columns_weight_gradient(dy, cols, through):
    n, wide = cols.shape
    return call(
        columns_weight_body,
        (dy, cols),
        "vh",
        (shaped(MID, wide, dtype=bf16),),
        "h",
        6,
        20,
        [VMEM((MID, n), bf16), VMEM((n, wide), bf16), VMEM((MID, wide), bf16), DMA((2, wide // STEP))],
        through=through,
    )


TILES = 2
EPSILON = 1e-05


def swap_with(values, axis, step):
    return lax.ppermute(values, axis, [(i, i ^ step) for i in range(lax.axis_size(axis))])


def from_behind(block, axis, distance):
    devices = range(lax.axis_size(axis))
    route = [(i - distance, i) for i in devices if i - distance in devices]
    return lax.ppermute(block, axis, route)


def ladder_sum(values, axis):
    step = 1
    while step < lax.axis_size(axis):
        got = swap_with(values.astype(bf16), axis, step)
        values = values + got.astype(f32)
        step *= 2
    return values


def to_everyone(spread, groups=None):
    return lax.all_to_all(spread, ("rows", "ch"), 0, 0, axis_index_groups=groups, tiled=True)


def small_total(spread):
    return jnp.sum(to_everyone(spread), axis=0).reshape(2, -1)


def wide_total(block):
    devices = lax.axis_size("rows") * lax.axis_size("ch")
    core = lax.axis_index("ch") % 2
    above, below = block.reshape(2, -1, 128)
    half = jnp.where(core == 0, above, below) + swap_with(jnp.where(core == 0, below, above), "ch", 1)
    groups = [[i * 2 + k for i in range(devices // 2)] for k in range(2)]
    half = jnp.broadcast_to(half[None], (devices // 2,) + half.shape)
    half = jnp.sum(to_everyone(half, groups), axis=0)
    other = swap_with(half, "ch", 1)
    whole = jnp.stack([jnp.where(core == 0, half, other), jnp.where(core == 0, other, half)])
    whole = whole.reshape(-1, 2, STEP)
    return whole[:, 0].reshape(-1), whole[:, 1].reshape(-1)


def forward_rows(sums, gain, shift, count):
    mean = sums[0] / count
    scale = lax.rsqrt(sums[1] / count - mean * mean + EPSILON)
    return jnp.stack([scale * gain, shift - mean * scale * gain, scale, -mean * scale])


def backward_rows(sums, par, count):
    rows = jnp.stack([par[0], par[0] * sums[0] / count, par[0] * sums[1] / count])
    return rows, jnp.stack([sums[1], sums[0]])


def gather_weight(weight):
    return lax.all_gather(weight.astype(bf16), "ch", axis=0, tiled=True)


def gather_weight_after(weight, *after):
    return lax.all_gather(cast_after(weight, *after), "ch", axis=0, tiled=True)


def gather_by_swaps(weight):
    ch = lax.axis_size("ch")
    came = None
    held = weight.astype(bf16)[None]
    step = ch // 2
    while step >= 1:
        got = swap_with(held, "ch", step)
        came = got if came is None else came
        odd = lax.axis_index("ch") // step % 2 == 1
        held = jnp.stack([jnp.where(odd, got, held), jnp.where(odd, held, got)], axis=1)
        held = held.reshape((-1,) + held.shape[2:])
        step //= 2
    return held.reshape((-1,) + weight.shape[1:]), came


def pick(values, bit):
    return lax.dynamic_index_in_dim(values, bit, 1, keepdims=False)


def scatter_ch(gradient):
    return lax.psum_scatter(gradient, "ch", scatter_dimension=0, tiled=True)


def split(total, axis, step):
    bit = lax.axis_index(axis) // step % 2
    pairs = total.reshape((total.shape[0] // 2, 2) + total.shape[1:])
    return swap_with(pick(pairs, 1 - bit), axis, step), pick(pairs, bit)


def added(pair):
    got, kept = pair
    return (got.astype(f32) + kept.astype(f32)).astype(bf16)


def rest_of(total, axis, step=1):
    while step < lax.axis_size(axis):
        total = added(split(total, axis, step))
        step *= 2
    return total


def by_owner(gradient, axis="ch"):
    count = lax.axis_size(axis)
    return gradient.reshape((count, gradient.shape[0] // count) + gradient.shape[1:])


def wide_enough(base):
    return base // lax.axis_size("rows") % 16 == 0


def first_step(parts, base, token=None):
    if wide_enough(base):
        send, keep, *token = pack_split(parts, base, lax.axis_size("rows"), token)
        return (swap_with(send, "rows", 1), keep, *token)
    laid = [jnp.concatenate([p[r : r + base] for r in range(0, p.shape[0], base)], axis=1) for p in parts]
    pair = split(by_owner(jnp.concatenate(laid, axis=1), "rows"), "rows", 1)
    return pair if token is None else (*pair, token)


class Ladder:
    def __init__(self, got, kept):
        self.got, self.kept, self.step, self.up = got, kept, 2, True

    def advance(self, token):
        last = lax.axis_size("rows") // 2
        if self.up and self.step <= last:
            send, self.kept, token = step_split(self.got, self.kept, "rows", self.step, token)
            self.got = swap_with(send, "rows", self.step)
            self.step *= 2
        elif self.up:
            self.kept, token = step_sum(self.got, self.kept, token)
            self.up, self.step = False, last
            self.got = swap_with(self.kept, "rows", self.step)
        else:
            self.kept, token = join_step(self.got, self.kept, self.step, token)
            self.step //= 2
            self.got = swap_with(self.kept, "rows", self.step)
        return token

    def ready(self):
        return not self.up and self.step == 1

    def finish(self, cuts, token):
        while not self.ready():
            token = self.advance(token)
        return final_join(self.got, self.kept, cuts, token)


def deep_rows(tile):
    odd = lax.axis_index("rows") % 2 == 1
    far_up = from_behind(tile, "rows", 2)
    far_down = from_behind(tile, "rows", -2)
    near = swap_with(tile, "rows", 1)
    other = swap_with(jnp.where(odd, far_up, far_down), "rows", 1)
    return far_up, jnp.where(odd, near, other), tile, jnp.where(odd, other, near), far_down


def deep_return(tiles):
    odd = lax.axis_index("rows") % 2 == 1
    _, up, own, down, _ = tiles
    got = swap_with(jnp.where(odd, down, up), "rows", 1)
    below, above, partner = return_step(tiles, got)
    below = from_behind(below, "rows", -2)
    above = from_behind(above, "rows", 2)
    return [own, swap_with(partner, "rows", 1), below, above]


def near_rows(tile, width):
    size = 2 * width
    above = from_behind(tile[:, -size:], "rows", 1)
    below = from_behind(tile[:, :size], "rows", -1)
    return above, tile, below


def per_device(
    inputs,
    heights,
    displacements,
    reduce_one,
    reduce_gain_one,
    reduce_bias_one,
    offset_weight,
    deform_weight,
    deform_gain,
    deform_bias,
    expand_one,
    expand_gain_one,
    expand_bias_one,
    reduce_two,
    reduce_gain_two,
    reduce_bias_two,
    conv_weight,
    conv_gain,
    conv_bias,
    expand_two,
    expand_gain_two,
    expand_bias_two,
    cotangent,
):
    batch, rows, width, channels = inputs.shape
    pixels = rows * width
    n = batch * pixels
    own_heights = lax.dynamic_slice_in_dim(heights, lax.axis_index("ch") * batch, batch)
    rows_here = lax.axis_index("rows") * rows + jnp.arange(rows, dtype=jnp.int32)
    mask = (rows_here[None, :] < own_heights[:, None]).astype(f32)
    mask = jnp.broadcast_to(mask[:, :, None], (batch, rows, width)).reshape(n, 1)
    mask_wide = jnp.broadcast_to(mask, (n, 128))
    count = jnp.sum(heights).astype(f32) * width

    offset_rows = offset_weight.astype(bf16).reshape(3, 6, 3, 3, MID).transpose(2, 3, 0, 1, 4)
    offset_rows = jnp.pad(offset_rows, ((0, 0), (0, 0), (0, 1), (0, 2), (0, 0))).reshape(3, 96, MID)
    disp = jnp.pad(displacements.reshape(3, 6, batch, pixels), ((0, 0), (0, 2), (0, 0), (0, 0)))
    disp = disp.transpose(2, 0, 1, 3)

    reduce_full, came = gather_by_swaps(reduce_one)
    deform_full = gather_weight_after(deform_weight, came)
    expand_full, reduce_full_two, conv_full, expand_full_two = [
        gather_weight(w) for w in (expand_one, reduce_two, conv_weight, expand_two)
    ]

    devices = lax.axis_size("rows") * lax.axis_size("ch")
    acts = inputs.reshape(n, channels)
    acts_low, y_a, spread = product_forward(acts, mask_wide, reduce_full, devices)
    par_a = forward_rows(small_total(spread), reduce_gain_one, reduce_bias_one, count)
    hidden = (gelu(y_a * par_a[0] + par_a[1]) * mask).astype(bf16)
    near_tiles = deep_rows(hidden.reshape(batch, pixels, MID))
    columns, y_b, fraction, spread = deform_forward(
        near_tiles, offset_rows, disp, deform_full, mask_wide, rows, width, devices
    )
    par_b = forward_rows(small_total(spread), deform_gain, deform_bias, count)
    middle, y_c, block = expand_forward([y_b], par_b, mask_wide, expand_full)
    par_c = forward_rows(wide_total(block), expand_gain_one, expand_bias_one, count)

    first_low, y_d, spread = first_forward(y_c, par_c, acts, mask_wide, reduce_full_two, devices)
    par_d = forward_rows(small_total(spread), reduce_gain_two, reduce_bias_two, count)
    hidden_two = (gelu(y_d * par_d[0] + par_d[1]) * mask).astype(bf16)
    rimmed = near_rows(hidden_two.reshape(batch, pixels, MID), width)
    y_e, spread = conv_forward(rimmed, conv_full, mask_wide, rows, width, devices)
    par_e = forward_rows(small_total(spread), conv_gain, conv_bias, count)
    middle_two, y_f, block = expand_forward([y_e], par_e, mask_wide, expand_full_two)
    par_f = forward_rows(wide_total(block), expand_gain_two, expand_bias_two, count)

    output, dt_f, block = output_stage(y_f, par_f, first_low, cotangent.reshape(n, channels), mask_wide)
    back_f, sums_f = backward_rows(wide_total(block), par_f, count)
    dy_f, dt_e, spread = expand_backward(
        dt_f, y_f, par_f, back_f, mask_wide, expand_full_two, y_e, par_e, devices
    )
    expand_two_local = dot(dy_f, middle_two, TN).astype(bf16)
    expand_two_part = scatter_ch(expand_two_local)
    back_e, sums_e = backward_rows(small_total(spread), par_e, count)
    dy_e = norm_gradient(dt_e, y_e, par_e, back_e, mask).astype(bf16)
    dy_e_rim = near_rows(dy_e.reshape(batch, pixels, MID), width)
    conv_local = conv_weight_gradient(dy_e, rimmed, rows, width, (expand_two_local,))
    conv_part = scatter_ch(conv_local)
    dt_d, spread = conv_backward(
        dy_e_rim, conv_full, y_d, par_d, mask_wide, rows, width, devices, (conv_local,)
    )
    base = conv_part.shape[0]
    back_d, sums_d = backward_rows(small_total(spread), par_d, count)
    dy_d, dt_c, block = residual_backward(
        dt_d, y_d, par_d, back_d, mask_wide, reduce_full_two, dt_f, y_c, par_c, acts_low
    )
    reduce_two_local = dot(dy_d, first_low, TN).astype(bf16)

    back_c, sums_c = backward_rows(wide_total(block), par_c, count)
    dy_c, dt_b, spread, reduce_two_local = expand_backward(
        dt_c, y_c, par_c, back_c, mask_wide, expand_full, y_b, par_b, devices, (reduce_two_local,)
    )
    reduce_two_part = scatter_ch(reduce_two_local)
    expand_one_local = dot(dy_c, middle, TN).astype(bf16)
    back_b, sums_b = backward_rows(small_total(spread), par_b, count)
    dy_b = norm_gradient(dt_b, y_b, par_b, back_b, mask).astype(bf16)
    got_p, kept_p = first_step([conv_part, expand_two_part], base)
    deform_local, kept_p = columns_weight_gradient(dy_b, columns, (kept_p,))
    deform_part = scatter_ch(deform_local)
    pieces, offset_local, after = [], 0.0, ()
    for b in range(batch):
        results = deform_backward(
            b, near_tiles, offset_rows, disp, fraction, deform_full,
            dy_b, rows, width, after, (kept_p,) + ((expand_one_local,) if b == 0 else ()),
        )
        tiles, offset_term, kept_p = results[:5], results[5], results[6]
        if b == 0:
            expand_one_part = scatter_ch(results[7])
        after = (offset_term, reduce_two_part)
        offset_local = offset_local + offset_term
        pieces += deep_return(tiles)
    token = jnp.zeros((8, 128), f32)
    sum_p = Ladder(got_p, kept_p)
    token = sum_p.advance(token)
    dt_a, spread, sum_p.kept, reduce_two_part = hidden_backward(
        pieces, y_a, par_a, mask_wide, devices, (sum_p.kept, reduce_two_part)
    )
    token = sum_p.advance(token)
    got_q, kept_q, token = first_step([reduce_two_part], base, token)
    back_a, sums_a = backward_rows(small_total(spread), par_a, count)
    dy_a, send_s, kept_s, sum_p.kept, kept_q, deform_part, offset_local, token = last_gradient(
        dt_a, y_a, par_a, back_a, mask_wide, acts_low, lax.axis_size("ch"),
        (sum_p.kept, kept_q, deform_part, offset_local), token
    )
    got_s = swap_with(send_s, "ch", 1)
    got_r, kept_r, token = first_step([deform_part], base, token)
    sum_q, sum_r = Ladder(got_q, kept_q), Ladder(got_r, kept_r)
    token = sum_p.advance(token)
    step = 2
    while step < lax.axis_size("ch"):
        send_s, kept_s, token = step_split(got_s, kept_s, "ch", step, token)
        got_s = swap_with(send_s, "ch", step)
        step *= 2
    token = sum_q.advance(token)
    token = sum_p.advance(token)
    input_grad, token = input_backward(dy_a, reduce_full, dt_c, token)
    token = sum_q.advance(token)
    got_e, kept_e, token = first_step([expand_one_part], base, token)
    sum_e = Ladder(got_e, kept_e)
    while not sum_p.ready():
        token = sum_p.advance(token)
    token = sum_r.advance(token)
    token = sum_q.advance(token)
    offset_local = offset_local.reshape(3, 3, 4, 8, MID)[:, :, :3, :6]
    offset_local = offset_local.transpose(2, 3, 0, 1, 4).reshape(-1, MID)
    offset_part = ladder_sum(offset_local, "ch").astype(bf16)
    offset_part = jnp.pad(offset_part, ((0, -offset_part.shape[0] % base), (0, 0)))
    reduce_one_part, token = step_sum(got_s, kept_s, token)
    got_s, kept_s, token = first_step([reduce_one_part[0], offset_part], base, token)
    sum_s = Ladder(got_s, kept_s)
    token = sum_e.advance(token)
    token = sum_r.advance(token)
    token = sum_q.advance(token)
    token = sum_s.advance(token)
    token = sum_e.advance(token)
    token = sum_r.advance(token)
    token = sum_s.advance(token)
    (conv_weight_grad, expand_two_grad), token = sum_p.finish(((1, 9 * MID), (channels // MID, MID)), token)
    token = sum_e.advance(token)
    token = sum_s.advance(token)
    token = sum_r.advance(token)
    (reduce_two_grad,), token = sum_q.finish(((1, channels),), token)
    token = sum_e.advance(token)
    token = sum_s.advance(token)
    (deform_weight_grad,), token = sum_r.finish(((1, 9 * MID),), token)
    (expand_one_grad,), token = sum_e.finish(((channels // MID, MID),), token)
    ends, token = owned((sums_a, sums_b, sums_c, sums_d, sums_e, sums_f), lax.axis_size("ch"), token)
    (reduce_one_grad, offset_grad), token = sum_s.finish(
        ((1, channels), (offset_part.shape[0] // base, MID)), token
    )
    offset_weight_grad = offset_grad[:162].reshape(18, 9 * MID)
    reduce_gain_one_grad, reduce_bias_one_grad, deform_gain_grad, deform_bias_grad = ends[:4]
    expand_gain_one_grad, expand_bias_one_grad, reduce_gain_two_grad, reduce_bias_two_grad = ends[4:8]
    conv_gain_grad, conv_bias_grad, expand_gain_two_grad, expand_bias_two_grad = ends[8:]
    return (
        output.reshape(inputs.shape),
        input_grad.reshape(inputs.shape),
        reduce_one_grad,
        reduce_gain_one_grad,
        reduce_bias_one_grad,
        offset_weight_grad,
        deform_weight_grad,
        deform_gain_grad,
        deform_bias_grad,
        expand_one_grad,
        expand_gain_one_grad,
        expand_bias_one_grad,
        reduce_two_grad,
        reduce_gain_two_grad,
        reduce_bias_two_grad,
        conv_weight_grad,
        conv_gain_grad,
        conv_bias_grad,
        expand_two_grad,
        expand_gain_two_grad,
        expand_bias_two_grad,
    )


def solution(mesh):
    tiles = P("ch", "rows", None, None)
    owned = P("ch", None)
    block = (owned, P(), P())
    placed = (tiles, P(), P(None, "ch", "rows", None)) + block + (P(),) + 2 * block + 3 * block + (tiles,)
    grads = (owned, P("ch"), P("ch"))
    return jax.shard_map(
        per_device,
        mesh=mesh,
        in_specs=placed,
        out_specs=(tiles, tiles) + grads + (P(),) + 2 * grads + 3 * grads,
        check_vma=False,
    )
```

```python
import functools

import jax
import jax.numpy as jnp
from jax import lax
from jax.experimental import pallas as pl
from jax.experimental.pallas import tpu as pltpu
from jax.sharding import PartitionSpec as P

bf16 = jnp.bfloat16
f32 = jnp.float32
VMEM = pltpu.VMEM
HBM = pltpu.HBM
DMA = pltpu.SemaphoreType.DMA
MID = 512
STEP = 512
NT = (((1,), (1,)), ((), ()))
TN = (((0,), (0,)), ((), ()))
NN = (((1,), (0,)), ((), ()))
GELU_A = 0.7978845608028654
GELU_B = 0.044715


def dot(a, b, dims=NN):
    return lax.dot_general(a, b, dims, preferred_element_type=f32)


def shaped(*shape, dtype=f32):
    return jax.ShapeDtypeStruct(shape, dtype)


def without(body, n_in, n_order, n_out, n_through, token):
    first = n_in + n_order + n_through

    def inner(*refs):
        if token:
            refs[first + n_out + n_through][...] = jnp.zeros((8, 128), f32)
        body(*refs[:n_in], *refs[first : first + n_out], *refs[first + n_out + n_through + token :])

    return inner


def cost(us):
    return pl.CostEstimate(flops=int(us), bytes_accessed=int(us), transcendentals=0)


def call(body, operands, places, outs, out_places, us, limit, scratch=(), after=(), through=(), token=None):
    def spec(place):
        return pl.BlockSpec(memory_space=HBM if place == "h" else VMEM)

    def pinned(value, place):
        return pltpu.with_memory_space_constraint(value, HBM) if place == "h" else value

    def result(out, place):
        return HBM(out.shape, out.dtype) if place == "h" else out

    tokens = () if token is None else (token,)
    n_in, n_out, n_order = len(operands), len(outs), len(after) + len(tokens)
    return pl.pallas_call(
        without(body, n_in, n_order, n_out, len(through), len(tokens)),
        in_specs=[spec(p) for p in places] + [spec("h")] * len(after) + [spec("v")] * len(tokens)
        + [spec("h")] * len(through),
        out_specs=tuple(spec(p) for p in out_places) + (spec("h"),) * len(through)
        + (spec("v"),) * len(tokens),
        out_shape=tuple(result(o, p) for o, p in zip(outs, out_places))
        + tuple(HBM(v.shape, v.dtype) for v in through)
        + (shaped(8, 128),) * len(tokens),
        input_output_aliases={n_in + n_order + t: n_out + t for t in range(len(through))},
        scratch_shapes=list(scratch),
        compiler_params=pltpu.CompilerParams(vmem_limit_bytes=limit * 2**20),
        cost_estimate=cost(us),
    )(
        *[pinned(v, p) for v, p in zip(operands, places)],
        *[pinned(v, "h") for v in after],
        *tokens,
        *[pinned(v, "h") for v in through],
    )


def moving(source, target, sem):
    copy = pltpu.make_async_copy(source, target, sem)
    copy.start()
    return copy


def columns_moving(source, target, sems, wide=STEP):
    return [
        moving(source.at[:, s * wide : (s + 1) * wide], target.at[:, s * wide : (s + 1) * wide], sems.at[s])
        for s in range(source.shape[1] // wide)
    ]


def rows_moving(source, target, sems, tall=STEP):
    return [
        moving(source.at[s * tall : (s + 1) * tall], target.at[s * tall : (s + 1) * tall], sems.at[s])
        for s in range(source.shape[0] // tall)
    ]


def blocks(wide):
    return [(s, slice(s * STEP, (s + 1) * STEP)) for s in range(wide // STEP)]


def gelu(v):
    return 0.5 * v * (1.0 + jnp.tanh(GELU_A * (v + GELU_B * v * v * v)))


def gelu_slope(v):
    t = jnp.tanh(GELU_A * (v + GELU_B * v * v * v))
    return 0.5 * (1.0 + t) + 0.5 * v * (1.0 - t * t) * (GELU_A * (1.0 + 3.0 * GELU_B * v * v))


def normed(values, par_ref, part=slice(None)):
    return values * par_ref[0:1, part] + par_ref[1:2, part]


def normal_of(values, par_ref, part=slice(None)):
    return values * par_ref[2:3, part] + par_ref[3:4, part]


def norm_gradient(upstream, values, par_ref, back_ref, mask, part=slice(None)):
    normal = normal_of(values, par_ref, part)
    return upstream * back_ref[0:1, part] - mask * (back_ref[1:2, part] + normal * back_ref[2:3, part])


def sums_block(weighted, values):
    n = weighted.shape[1] // 128
    sums = (
        jnp.sum(weighted, axis=0, keepdims=True),
        jnp.sum(weighted * values, axis=0, keepdims=True),
    )
    return jnp.concatenate([v[:, c * 128 : c * 128 + 128] for v in sums for c in range(n)], axis=0)


def write_stats(stat_ref, weighted, values):
    stat_ref[...] = jnp.broadcast_to(sums_block(weighted, values)[None], stat_ref.shape)


def product_forward_body(x_ref, mask_ref, w_ref, low_ref, out_ref, stat_ref, x_buf, low_buf, sems):
    wide = x_ref.shape[1]
    coming = columns_moving(x_ref, x_buf, sems.at[0])
    total, going = None, []
    for s, part in blocks(wide):
        coming[s].wait()
        low_buf[:, part] = x_buf[:, part].astype(bf16)
        going.append(moving(low_buf.at[:, part], low_ref.at[:, part], sems.at[1, s]))
        term = dot(low_buf[:, part], w_ref[:, part], NT)
        total = term if total is None else total + term
    out_ref[...] = total
    write_stats(stat_ref, total * mask_ref[:, 0:1], total)
    for copy in going:
        copy.wait()


def product_forward(x, mask_wide, weight, devices):
    n, wide = x.shape
    return call(
        product_forward_body,
        (x, mask_wide, weight),
        "hvv",
        (shaped(n, wide, dtype=bf16), shaped(n, MID), shaped(devices, 8, 128)),
        "hvv",
        5,
        20,
        [VMEM((n, wide), f32), VMEM((n, wide), bf16), DMA((2, wide // STEP))],
    )


def expand_forward_body(*refs):
    *y_refs, par_ref, mask_ref, e_ref, mid_ref, out_ref, stat_ref, e_buf, out_buf, sems = refs
    coming = rows_moving(e_ref, e_buf, sems.at[0])
    mask = mask_ref[:, 0:1]
    at = 0
    for y_ref in y_refs:
        part = slice(at, at + y_ref.shape[0])
        mid_ref[part, :] = (gelu(normed(y_ref[...], par_ref)) * mask_ref[part, 0:1]).astype(bf16)
        at += y_ref.shape[0]
    going = []
    for s, part in blocks(e_ref.shape[0]):
        coming[s].wait()
        out = dot(mid_ref[...], e_buf[part, :], NT)
        out_buf[:, part] = out.astype(bf16)
        going.append(moving(out_buf.at[:, part], out_ref.at[:, part], sems.at[1, s]))
        stat_ref[s * 8 : s * 8 + 8, :] = sums_block(out * mask, out)
    for copy in going:
        copy.wait()


def expand_forward(y_parts, par, mask_wide, weight):
    n, wide = mask_wide.shape[0], weight.shape[0]
    return call(
        expand_forward_body,
        (*y_parts, par, mask_wide, weight),
        "v" * (len(y_parts) + 2) + "h",
        (shaped(n, MID, dtype=bf16), shaped(n, wide, dtype=bf16), shaped(wide // 64, 128)),
        "vhv",
        4,
        16,
        [VMEM(weight.shape, bf16), VMEM((n, wide), bf16), DMA((2, wide // STEP))],
    )


def first_forward_body(
    y_ref, par_ref, x_ref, mask_ref, w_ref, low_ref, out_ref, stat_ref,
    y_buf, x_buf, w_buf, low_buf, sems
):
    wide = x_ref.shape[1]
    coming_y = columns_moving(y_ref, y_buf, sems.at[0])
    coming_x = columns_moving(x_ref, x_buf, sems.at[1])
    coming_w = columns_moving(w_ref, w_buf, sems.at[2])
    mask = mask_ref[:, 0:1]
    total, going = None, []
    for s, part in blocks(wide):
        coming_y[s].wait()
        coming_x[s].wait()
        first = gelu(normed(y_buf[:, part].astype(f32), par_ref, part) + x_buf[:, part]) * mask
        low_buf[:, part] = first.astype(bf16)
        going.append(moving(low_buf.at[:, part], low_ref.at[:, part], sems.at[3, s]))
        coming_w[s].wait()
        term = dot(low_buf[:, part], w_buf[:, part], NT)
        total = term if total is None else total + term
    out_ref[...] = total
    write_stats(stat_ref, total * mask, total)
    for copy in going:
        copy.wait()


def first_forward(y, par, x, mask_wide, weight, devices):
    n, wide = y.shape
    return call(
        first_forward_body,
        (y, par, x, mask_wide, weight),
        "hvhvh",
        (shaped(n, wide, dtype=bf16), shaped(n, MID), shaped(devices, 8, 128)),
        "hvv",
        6,
        24,
        [
            VMEM((n, wide), bf16),
            VMEM((n, wide), f32),
            VMEM(weight.shape, bf16),
            VMEM((n, wide), bf16),
            DMA((4, wide // STEP)),
        ],
    )


def output_stage_body(
    y_ref, par_ref, first_ref, cot_ref, mask_ref, out_ref, dt_ref, stat_ref,
    y_buf, first_buf, cot_buf, out_buf, dt_buf, sems
):
    wide = y_ref.shape[1]
    coming_y = columns_moving(y_ref, y_buf, sems.at[0])
    coming_f = columns_moving(first_ref, first_buf, sems.at[1])
    coming_c = columns_moving(cot_ref, cot_buf, sems.at[2])
    mask = mask_ref[:, 0:1]
    going = []
    for s, part in blocks(wide):
        coming_y[s].wait()
        coming_f[s].wait()
        y = y_buf[:, part].astype(f32)
        pre = normed(y, par_ref, part) + first_buf[:, part].astype(f32)
        t = jnp.tanh(GELU_A * (pre + GELU_B * pre * pre * pre))
        out_buf[:, part] = 0.5 * pre * (1.0 + t) * mask
        going.append(moving(out_buf.at[:, part], out_ref.at[:, part], sems.at[3, s]))
        slope = 0.5 * (1.0 + t) + 0.5 * pre * (1.0 - t * t) * (GELU_A * (1.0 + 3.0 * GELU_B * pre * pre))
        coming_c[s].wait()
        dt = slope * (cot_buf[:, part] * mask)
        dt_buf[:, part] = dt.astype(bf16)
        going.append(moving(dt_buf.at[:, part], dt_ref.at[:, part], sems.at[4, s]))
        stat_ref[s * 8 : s * 8 + 8, :] = sums_block(dt, normal_of(y, par_ref, part))
    for copy in going:
        copy.wait()


def output_stage(y, par, first, cot, mask_wide):
    n, wide = y.shape
    return call(
        output_stage_body,
        (y, par, first, cot, mask_wide),
        "hvhhv",
        (shaped(n, wide), shaped(n, wide, dtype=bf16), shaped(wide // 64, 128)),
        "hhv",
        8,
        28,
        [
            VMEM((n, wide), bf16),
            VMEM((n, wide), bf16),
            VMEM((n, wide), f32),
            VMEM((n, wide), f32),
            VMEM((n, wide), bf16),
            DMA((5, wide // STEP)),
        ],
    )


def expand_backward_body(
    dt_ref, y_ref, par_ref, back_ref, mask_ref, e_ref, mid_y_ref, mid_par_ref,
    dy_ref, mid_dt_ref, stat_ref, dt_buf, y_buf, e_buf, dy_buf, sems
):
    wide = dt_ref.shape[1]
    coming_dt = columns_moving(dt_ref, dt_buf, sems.at[0])
    coming_y = columns_moving(y_ref, y_buf, sems.at[1])
    coming_e = rows_moving(e_ref, e_buf, sems.at[2])
    mask = mask_ref[:, 0:1]
    total, going = None, []
    for s, part in blocks(wide):
        coming_dt[s].wait()
        coming_y[s].wait()
        dt, y = dt_buf[:, part].astype(f32), y_buf[:, part].astype(f32)
        dy = norm_gradient(dt, y, par_ref, back_ref, mask, part).astype(bf16)
        dy_buf[:, part] = dy
        going.append(moving(dy_buf.at[:, part], dy_ref.at[:, part], sems.at[3, s]))
        coming_e[s].wait()
        term = dot(dy, e_buf[part, :])
        total = term if total is None else total + term
    y = mid_y_ref[...]
    dt = gelu_slope(normed(y, mid_par_ref)) * (total * mask)
    mid_dt_ref[...] = dt
    write_stats(stat_ref, dt, normal_of(y, mid_par_ref))
    for copy in going:
        copy.wait()


def expand_backward(dt, y, par, back, mask_wide, weight, mid_y, mid_par, devices, through=()):
    n, wide = y.shape
    return call(
        expand_backward_body,
        (dt, y, par, back, mask_wide, weight, mid_y, mid_par),
        "hhvvvhvv",
        (shaped(n, wide, dtype=bf16), shaped(n, MID), shaped(devices, 8, 128)),
        "hvv",
        5,
        24,
        [
            VMEM((n, wide), bf16),
            VMEM((n, wide), bf16),
            VMEM(weight.shape, bf16),
            VMEM((n, wide), bf16),
            DMA((4, wide // STEP)),
        ],
        through=through,
    )


def residual_backward_body(
    dt_ref, y_ref, par_ref, back_ref, mask_ref, w_ref, add_ref, wide_y_ref, wide_par_ref, x_ref,
    dy_ref, out_ref, stat_ref, w_buf, add_buf, y_buf, x_buf, out_buf, sems
):
    wide = x_ref.shape[1]
    coming = [
        columns_moving(source, target, sems.at[t])
        for t, (source, target) in enumerate(
            ((w_ref, w_buf), (add_ref, add_buf), (wide_y_ref, y_buf), (x_ref, x_buf))
        )
    ]
    mask = mask_ref[:, 0:1]
    dy_ref[...] = norm_gradient(dt_ref[...], y_ref[...], par_ref, back_ref, mask).astype(bf16)
    going = []
    for s, part in blocks(wide):
        for copies in coming:
            copies[s].wait()
        grad = add_buf[:, part].astype(f32) + dot(dy_ref[...], w_buf[:, part])
        y = y_buf[:, part].astype(f32)
        pre = normed(y, wide_par_ref, part) + x_buf[:, part].astype(f32)
        dt = gelu_slope(pre) * (grad * mask)
        out_buf[:, part] = dt.astype(bf16)
        going.append(moving(out_buf.at[:, part], out_ref.at[:, part], sems.at[4, s]))
        stat_ref[s * 8 : s * 8 + 8, :] = sums_block(dt, normal_of(y, wide_par_ref, part))
    for copy in going:
        copy.wait()


def residual_backward(dt, y, par, back, mask_wide, weight, add, wide_y, wide_par, x):
    n, wide = x.shape
    return call(
        residual_backward_body,
        (dt, y, par, back, mask_wide, weight, add, wide_y, wide_par, x),
        "vvvvvhhhvh",
        (shaped(n, MID, dtype=bf16), shaped(n, wide, dtype=bf16), shaped(wide // 64, 128)),
        "vhv",
        6,
        24,
        [VMEM(weight.shape, bf16)] + [VMEM((n, wide), bf16)] * 4 + [DMA((5, wide // STEP))],
    )


def input_backward_body(dy_ref, w_ref, add_ref, out_ref, w_buf, add_buf, out_buf, sems):
    coming_w = columns_moving(w_ref, w_buf, sems.at[0])
    coming_a = columns_moving(add_ref, add_buf, sems.at[1])
    going = []
    for s, part in blocks(w_ref.shape[1]):
        coming_w[s].wait()
        coming_a[s].wait()
        out_buf[:, part] = add_buf[:, part].astype(f32) + dot(dy_ref[...], w_buf[:, part])
        going.append(moving(out_buf.at[:, part], out_ref.at[:, part], sems.at[2, s]))
    for copy in going:
        copy.wait()


def input_backward(dy, weight, add, token):
    n, wide = add.shape
    return call(
        input_backward_body,
        (dy, weight, add),
        "vhh",
        (shaped(n, wide),),
        "h",
        5,
        20,
        [VMEM(weight.shape, bf16), VMEM((n, wide), bf16), VMEM((n, wide), f32), DMA((3, wide // STEP))],
        token=token,
    )


def hidden_backward_body(*refs):
    *piece_refs, y_ref, par_ref, mask_ref, dt_ref, stat_ref = refs
    batch = len(piece_refs) // 4
    pixels = y_ref.shape[0] // batch
    for b in range(batch):
        own, near, up, down = [ref[...].astype(f32) for ref in piece_refs[4 * b : 4 * b + 4]]
        dt_ref[b * pixels : (b + 1) * pixels, :] = own + near + up + down
    grad = dt_ref[...]
    y = y_ref[...]
    dt = gelu_slope(normed(y, par_ref)) * (grad * mask_ref[:, 0:1])
    dt_ref[...] = dt
    write_stats(stat_ref, dt, normal_of(y, par_ref))


def hidden_backward(pieces, y, par, mask_wide, devices, through, token):
    n = y.shape[0]
    return call(
        hidden_backward_body,
        (*pieces, y, par, mask_wide),
        "v" * (len(pieces) + 3),
        (shaped(n, MID), shaped(devices, 8, 128)),
        "vv",
        3,
        16,
        through=through,
        token=token,
    )


def last_gradient_body(
    dt_ref, y_ref, par_ref, back_ref, mask_ref, acts_ref, dy_ref, send_ref, keep_ref,
    dyt_ref, acts_buf, out_buf, in_sems, out_sems
):
    coming = columns_moving(acts_ref, acts_buf, in_sems)
    dy = norm_gradient(dt_ref[...], y_ref[...], par_ref, back_ref, mask_ref[:, 0:1]).astype(bf16)
    dy_ref[...] = dy
    dyt_ref[...] = dy.astype(f32).T.astype(bf16)
    core = lax.axis_index("ch") % 2
    half, base = send_ref.shape[0], send_ref.shape[1]
    going = []
    for s, part in blocks(acts_ref.shape[1]):
        coming[s].wait()
        out_buf[:, part] = dot(dyt_ref[...], acts_buf[:, part]).astype(bf16)
        for q in range(half):
            for t, (out_ref, side) in enumerate(((send_ref, 1 - core), (keep_ref, core))):
                row = pl.multiple_of((2 * q + side) * base, 16)
                going.append(
                    moving(
                        out_buf.at[pl.ds(row, base), part], out_ref.at[q, :, part], out_sems.at[s, q, t]
                    )
                )
    for copy in going:
        copy.wait()


def last_gradient(dt, y, par, back, mask_wide, acts, ch, through, token):
    n, wide = acts.shape
    half = shaped(ch // 2, MID // ch, wide, dtype=bf16)
    return call(
        last_gradient_body,
        (dt, y, par, back, mask_wide, acts),
        "vvvvvh",
        (shaped(n, MID, dtype=bf16), half, half),
        "vhh",
        6,
        20,
        [
            VMEM((MID, n), bf16),
            VMEM((n, wide), bf16),
            VMEM((MID, wide), bf16),
            DMA((wide // STEP,)),
            DMA((wide // STEP, ch // 2, 2)),
        ],
        through=through,
        token=token,
    )


def cast_body(v_ref, out_ref):
    out_ref[...] = v_ref[...].astype(bf16)


def cast_after(values, *after):
    return call(cast_body, (values,), "v", (shaped(*values.shape, dtype=bf16),), "v", 2, 12, after=after)[0]


def pack_body(*refs, count, bit_axis, rows):
    part_refs, (send_ref, keep_ref), refs = refs[:count], refs[count : count + 2], refs[count + 2 :]
    buffers, (in_sem, out_sem) = refs[:count], refs[count:]
    coming = [moving(ref, buf, in_sem.at[t]) for t, (ref, buf) in enumerate(zip(part_refs, buffers))]
    bit = lax.axis_index(bit_axis) % 2
    tall = send_ref.shape[1]
    base = rows * tall
    going, at = [], 0
    for copy, buf in zip(coming, buffers):
        copy.wait()
        wide = buf.shape[1]
        for block in range(buf.shape[0] // base):
            for pair in range(rows // 2):
                for out_ref, side in ((send_ref, 1 - bit), (keep_ref, bit)):
                    row = pl.multiple_of(block * base + (2 * pair + side) * tall, 16)
                    going.append(
                        moving(
                            buf.at[pl.ds(row, tall), :],
                            out_ref.at[pair, :, at : at + wide],
                            out_sem.at[len(going)],
                        )
                    )
            at += wide
    for copy in going:
        copy.wait()


def pack_split(parts, base, rows, token=None):
    count = len(parts)
    blocks_in = sum(p.shape[0] // base for p in parts)
    wide = sum(p.shape[0] // base * p.shape[1] for p in parts)
    half = shaped(rows // 2, base // rows, wide, dtype=bf16)
    return call(
        functools.partial(pack_body, count=count, bit_axis="rows", rows=rows),
        tuple(parts),
        "h" * count,
        (half, half),
        "hh",
        3,
        16,
        [VMEM(p.shape, bf16) for p in parts] + [DMA((count,)), DMA((blocks_in * rows,))],
        token=token,
    )


def step_body(got_ref, kept_ref, send_ref, keep_ref, sum_ref, *, axis, step):
    bit = lax.axis_index(axis) // step % 2
    sum_ref[...] = (got_ref[...].astype(f32) + kept_ref[...].astype(f32)).astype(bf16)
    for pair in range(send_ref.shape[0]):
        send_ref[pair] = sum_ref[2 * pair + 1 - bit]
        keep_ref[pair] = sum_ref[2 * pair + bit]


def step_split(got, kept, axis, step, token=None):
    half = shaped(got.shape[0] // 2, *got.shape[1:], dtype=bf16)
    return call(
        functools.partial(step_body, axis=axis, step=step),
        (got, kept),
        "vv",
        (half, half),
        "vv",
        2,
        12,
        [VMEM(got.shape, bf16)],
        token=token,
    )


def sum_body(got_ref, kept_ref, sum_ref):
    sum_ref[...] = (got_ref[...].astype(f32) + kept_ref[...].astype(f32)).astype(bf16)


def step_sum(got, kept, token):
    return call(sum_body, (got, kept), "vv", (shaped(*got.shape, dtype=bf16),), "v", 1, 12, token=token)


def join_body(got_ref, kept_ref, out_ref, *, step):
    bit = lax.axis_index("rows") // step % 2
    for a in range(got_ref.shape[0]):
        out_ref[2 * a + bit] = kept_ref[a]
        out_ref[2 * a + 1 - bit] = got_ref[a]


def join_step(got, kept, step, token):
    m, r, wide = got.shape
    return call(
        functools.partial(join_body, step=step),
        (got, kept),
        "vv",
        (shaped(2 * m, r, wide, dtype=bf16),),
        "v",
        1,
        12,
        token=token,
    )


def final_body(got_ref, kept_ref, *refs, cuts):
    out_refs, refs = refs[: len(cuts)], refs[len(cuts) :]
    buffers, sems = refs[: len(cuts)], refs[len(cuts)]
    bit = lax.axis_index("rows") % 2
    going, at = [], 0
    for out_ref, buf, (count, wide) in zip(out_refs, buffers, cuts):
        for k in range(count):
            part = slice(at, at + wide)
            for a in range(got_ref.shape[0]):
                buf[k, 2 * a + bit] = kept_ref[a, :, part].astype(f32)
                buf[k, 2 * a + 1 - bit] = got_ref[a, :, part].astype(f32)
            going.append(moving(buf.at[k], out_ref.at[k], sems.at[len(going)]))
            at += wide
    for copy in going:
        copy.wait()


def final_join(got, kept, cuts, token):
    m, r, _ = got.shape
    outs = [shaped(count, 2 * m, r, wide) for count, wide in cuts]
    *outs, token = call(
        functools.partial(final_body, cuts=cuts),
        (got, kept),
        "vv",
        outs,
        "h" * len(outs),
        2,
        20,
        [VMEM(o.shape, f32) for o in outs] + [DMA((sum(count for count, _ in cuts),))],
        token=token,
    )
    return [o.reshape(-1, o.shape[3]) for o in outs], token


def owned_body(*refs):
    n = len(refs) // 3
    for k in range(n):
        size = refs[n + 2 * k].shape[1]
        start = lax.axis_index("ch") * size
        turned = pltpu.roll(refs[k][...], refs[k].shape[1] - start, 1)
        refs[n + 2 * k][...] = turned[0:1, :size]
        refs[n + 2 * k + 1][...] = turned[1:2, :size]


def owned(sums, ch, token):
    outs = [shaped(1, s.shape[1] // ch) for s in sums for _ in range(2)]
    *outs, token = call(
        owned_body, tuple(sums), "v" * len(sums), outs, "v" * len(outs), 1, 12, token=token
    )
    return [o.reshape(-1) for o in outs], token


def return_body(far_up_ref, up_ref, down_ref, far_down_ref, got_ref, *refs):
    count = (len(refs) - 2) // 3
    others, (below_ref, above_ref), partners = refs[: 2 * count], refs[2 * count : 2 * count + 2], refs[2 * count + 2 :]
    odd = lax.axis_index("rows") % 2 == 1

    @pl.when(odd)
    def _():
        total = far_up_ref[...].astype(f32) + got_ref[...].astype(f32)
        below_ref[...] = total.astype(bf16)
        above_ref[...] = far_down_ref[...]
        for b in range(count):
            partners[b][...] = others[2 * b][...]

    @pl.when(jnp.logical_not(odd))
    def _():
        total = far_down_ref[...].astype(f32) + got_ref[...].astype(f32)
        below_ref[...] = far_up_ref[...]
        above_ref[...] = total.astype(bf16)
        for b in range(count):
            partners[b][...] = others[2 * b + 1][...]


def return_step(tiles, got, pairs, token):
    far_up, up, _, down, far_down = tiles
    piece = shaped(*got.shape, dtype=bf16)
    others = [part for pair in pairs for part in pair]
    return call(
        return_body,
        (far_up, up, down, far_down, got, *others),
        "v" * (5 + len(others)),
        (piece,) * (2 + len(pairs)),
        "v" * (2 + len(pairs)),
        2,
        12,
        token=token,
    )


def shift_lanes(values, by, width):
    place = lax.broadcasted_iota(jnp.int32, values.shape, values.ndim - 1) % width
    moved = pltpu.roll(values, by % values.shape[-1], values.ndim - 1)
    return jnp.where((place >= by) & (place < width + by), moved, 0.0)


def shift_rows(values, by, width):
    place = lax.broadcasted_iota(jnp.int32, values.shape, 0) % width
    moved = pltpu.roll(values, by % values.shape[0], 0)
    return jnp.where((place >= by) & (place < width + by), moved, 0.0)


def offset_fraction(ext_ref, ow_ref, b, base, pixels, width):
    u = None
    for i in range(3):
        start = (base + 2 * i) * width
        term = dot(ow_ref[i], ext_ref[b, start : start + pixels, :], NT)
        u = term if u is None else u + term
    total = u[32:64]
    total = total + shift_lanes(u[0:32], 2, width) + shift_lanes(u[64:96], -2, width)
    return 1.0 / (1.0 + jnp.exp(-total))


def deform_forward_body(*refs, batch, rows, width, deep):
    tile_refs, refs = refs[:5], refs[5:]
    ow_ref, disp_ref, m_ref, mask_ref, cols_out_ref, y_ref, frac_ref, stat_ref = refs[:8]
    ext_ref, par_ref, s_ref, cols_ref, m_buf, tile_sems, sems = refs[8:]
    pixels = rows * width
    coming = [
        moving(ref, ext_ref.at[:, t * pixels : (t + 1) * pixels, :], tile_sems.at[t])
        for t, ref in enumerate(tile_refs)
    ]
    coming_m = moving(m_ref, m_buf, sems.at[0])
    for copy in coming:
        copy.wait()
    lane = lax.broadcasted_iota(jnp.int32, (32, 128), 1)
    column = lane % width
    upper = lane // width

    def image(b, carry):
        frac = offset_fraction(ext_ref, ow_ref, b, deep - 2, pixels, width)
        for i in range(4):
            frac_ref[b, i] = frac[i * 8 : i * 8 + 8]
        pix = lax.broadcasted_iota(jnp.int32, (1, pixels), 1)
        row_at, col_at = pix // width, pix % width
        tops, lefts, ys, xs = [], [], [], []
        for k in range(9):
            i, j = k // 3, k % 3
            tops.append(row_at + disp_ref[b, i, 2 * j : 2 * j + 1, :] + (deep - 2))
            lefts.append(col_at + 2 * (j - 1) + disp_ref[b, i, 2 * j + 1 : 2 * j + 2, :])
            at = i * 8 + 2 * j
            ys.append(frac[at : at + 1])
            xs.append(frac[at + 1 : at + 2])
        blank = jnp.zeros((23, pixels), f32)
        par = jnp.concatenate(
            [jnp.concatenate(g, axis=0).astype(f32) if g is not None else blank
             for g in (tops, None, lefts, None, ys, None, xs, None)], axis=0)
        par_ref[...] = par.T

        def row_of_taps(i, carry):
            for j in range(3):
                k = i * 3 + j
                for c in range(pixels // 32):
                    p = pltpu.roll(par_ref[c * 32 : c * 32 + 32, :], 128 - k, 1)
                    wide = (32, 128)
                    top = jnp.broadcast_to(p[:, 0:1], wide).astype(jnp.int32) - upper
                    left = jnp.broadcast_to(p[:, 32:33], wide).astype(jnp.int32)
                    fy = jnp.broadcast_to(p[:, 64:65], wide)
                    fx = jnp.broadcast_to(p[:, 96:97], wide)
                    cw = jnp.where(column == left, 1.0 - fx, jnp.where(column == left + 1, fx, 0.0))
                    ca, cb = (1.0 - fy) * cw, fy * cw
                    for q in range(8):
                        s = jnp.where(top == 2 * q, ca, jnp.where(top == 2 * q - 1, cb, 0.0))
                        s_ref[j * pixels + c * 32 : j * pixels + c * 32 + 32, q * 128 : q * 128 + 128] = s.astype(bf16)
            start = pl.multiple_of(i * 2 * width, 128)
            window = ext_ref[b, pl.ds(start, 16 * width), :]
            for j in range(3):
                got = dot(s_ref[j * pixels : (j + 1) * pixels, :], window).astype(bf16)
                cols_ref[pl.ds(pl.multiple_of(b * pixels, pixels), pixels), pl.ds(pl.multiple_of((i * 3 + j) * MID, MID), MID)] = got
            return carry

        return lax.fori_loop(0, 3, row_of_taps, carry)

    lax.fori_loop(0, batch, image, 0)
    going = moving(cols_ref, cols_out_ref, sems.at[1])
    coming_m.wait()
    y = dot(cols_ref[...], m_buf[...], NT)
    y_ref[...] = y
    write_stats(stat_ref, y * mask_ref[:, 0:1], y)
    going.wait()


def deform_forward(tiles, offset_rows, disp, weight, mask_wide, rows, width, devices):
    batch = tiles[0].shape[0]
    pixels = rows * width
    n = batch * pixels
    return call(
        functools.partial(deform_forward_body, batch=batch, rows=rows, width=width, deep=2 * rows),
        (*tiles, offset_rows, disp, weight, mask_wide),
        "hhhhhvvhv",
        (
            shaped(n, 9 * MID, dtype=bf16),
            shaped(n, MID),
            shaped(batch, 4, 8, pixels),
            shaped(devices, 8, 128),
        ),
        "hvvv",
        15,
        30,
        [
            VMEM((batch, 5 * pixels, MID), bf16),
            VMEM((pixels, 128), f32),
            VMEM((3 * pixels, 16 * width), bf16),
            VMEM((n, 9 * MID), bf16),
            VMEM(weight.shape, bf16),
            DMA((5,)),
            DMA((2,)),
        ],
    )


def deform_backward_body(*refs, rows, width, deep, which):
    tile_refs, refs = refs[:5], refs[5:]
    (ow_ref, disp_ref, frac_ref, m_ref, dy_ref), refs = refs[:5], refs[5:]
    out_refs, refs = refs[:5], refs[5:]
    dow_ref, ext_ref, dext_ref, dc_ref, g_ref, st_ref, df_ref, m_buf, tile_sems, m_sems = refs
    pixels = rows * width
    coming = [
        moving(ref.at[which], ext_ref.at[0, t * pixels : (t + 1) * pixels, :], tile_sems.at[t])
        for t, ref in enumerate(tile_refs)
    ]
    coming_m = taps_moving(m_ref, m_buf, m_sems)
    window = 16 * width
    dow_ref[...] = jnp.zeros_like(dow_ref)
    dext_ref[...] = jnp.zeros_like(dext_ref)
    for copy in coming:
        copy.wait()

    def image(b, carry):
        def row_of_taps(i, carry):
            dy = dy_ref[which * pixels : (which + 1) * pixels, :]
            for j in range(3):
                m = m_buf[:, (i * 3 + j) * MID : (i * 3 + j + 1) * MID]
                dc_ref[j * pixels : (j + 1) * pixels, :] = dot(dy, m).astype(bf16)
            start = i * 2 * width
            g_ref[...] = dot(ext_ref[b, pl.ds(start, window), :], dc_ref[...], NT)
            place = lax.broadcasted_iota(jnp.int32, (width, 128), 0)
            for j in range(3):
                for h in range(pixels // 128):
                    lanes = slice(h * 128, h * 128 + 128)
                    at_l = slice(j * pixels + h * 128, j * pixels + h * 128 + 128)
                    pix = lax.broadcasted_iota(jnp.int32, (1, 128), 1) + h * 128
                    by_y, by_x = slice(2 * j, 2 * j + 1), slice(2 * j + 1, 2 * j + 2)
                    top = pix // width + disp_ref[which, i, by_y, lanes] + (deep - 2)
                    left = pix % width + 2 * (j - 1) + disp_ref[which, i, by_x, lanes]
                    fy = frac_ref[which, i, by_y, lanes]
                    fx = frac_ref[which, i, by_x, lanes]
                    here, after = place == left, place == left + 1
                    cw = jnp.where(here, 1.0 - fx, jnp.where(after, fx, 0.0))
                    ca, cb = (1.0 - fy) * cw, fy * cw
                    low_sum = jnp.zeros((width, 128), f32)
                    high_sum = jnp.zeros((width, 128), f32)
                    for r in range(16):
                        part = slice(r * width, r * width + width)
                        g = g_ref[part, at_l]
                        m0, m1 = top == r, top == r - 1
                        low_sum = low_sum + jnp.where(m0, g, 0.0)
                        high_sum = high_sum + jnp.where(m1, g, 0.0)
                        st_ref[part, at_l] = jnp.where(m0, ca, jnp.where(m1, cb, 0.0)).astype(bf16)
                    d_fy = jnp.sum((high_sum - low_sum) * cw, axis=0, keepdims=True)
                    mixed = (1.0 - fy) * low_sum + fy * high_sum
                    d_fx = jnp.sum(
                        jnp.where(after, mixed, 0.0) - jnp.where(here, mixed, 0.0), axis=0, keepdims=True)
                    df_ref[i, by_y, lanes] = d_fy * fy * (1.0 - fy)
                    df_ref[i, by_x, lanes] = d_fx * fx * (1.0 - fx)
            dext_ref[b, pl.ds(start, window), :] += dot(st_ref[...], dc_ref[...])
            return carry

        df_ref[...] = jnp.zeros_like(df_ref)
        for i in range(3):
            coming_m[i].wait()
            row_of_taps(i, carry)
        d_off = df_ref[...].reshape(32, pixels).astype(bf16).astype(f32)
        stacked = jnp.concatenate(
            [shift_lanes(d_off, -2, width), d_off, shift_lanes(d_off, 2, width)], axis=0)
        across = jnp.concatenate([stacked, jnp.zeros((32, pixels), f32)], axis=0).T.astype(bf16)
        stacked = stacked.astype(bf16)
        for i in range(3):
            first = (deep - 2 + 2 * i) * width
            part = slice(first, first + pixels)
            dow_ref[i] += dot(stacked, ext_ref[b, part, :])
            dext_ref[b, part, :] += dot(across[:, :96], ow_ref[i])
        return carry

    image(0, 0)
    for t, ref in enumerate(out_refs):
        ref[...] = dext_ref[t // 5, t % 5 * pixels : (t % 5 + 1) * pixels, :].astype(ref.dtype)


def deform_backward(which, tiles, offset_rows, disp, frac, weight, dy, rows, width, after, through, token):
    pixels = rows * width
    return call(
        functools.partial(deform_backward_body, rows=rows, width=width, deep=2 * rows, which=which),
        (*tiles, offset_rows, disp, frac, weight, dy),
        "hhhhhvvvhv",
        tuple(shaped(pixels, MID, dtype=f32 if t == 2 else bf16) for t in range(5)) + (shaped(3, 96, MID),),
        "vvvvvv",
        10,
        32,
        [
            VMEM((1, 5 * pixels, MID), bf16),
            VMEM((1, 5 * pixels, MID), f32),
            VMEM((3 * pixels, MID), bf16),
            VMEM((16 * width, 3 * pixels), f32),
            VMEM((16 * width, 3 * pixels), bf16),
            VMEM((4, 8, pixels), f32),
            VMEM(weight.shape, bf16),
            DMA((5,)),
            DMA((3,)),
        ],
        after,
        through,
        token,
    )


def taps_moving(m_ref, m_buf, sems):
    wide = 3 * MID
    return columns_moving(m_ref, m_buf, sems, wide)


def rim_moving(parts, rim_ref, sems):
    copies, at = [], 0
    for t, ref in enumerate(parts):
        copies.append(moving(ref, rim_ref.at[:, at : at + ref.shape[1], :], sems.at[t]))
        at += ref.shape[1]
    return copies


def conv_forward_body(
    above_ref, own_ref, below_ref, m_ref, mask_ref, y_ref, stat_ref, rim_ref, m_buf, rim_sems, sems,
    *, batch, rows, width
):
    pixels = rows * width
    coming = taps_moving(m_ref, m_buf, sems)
    for copy in rim_moving((above_ref, own_ref, below_ref), rim_ref, rim_sems):
        copy.wait()
    sums = [[None] * 3 for _ in range(batch)]
    for i in range(3):
        coming[i].wait()
        for b in range(batch):
            for j in range(3):
                k = i * 3 + j
                start = 2 * i * width
                term = dot(rim_ref[b, start : start + pixels, :], m_buf[:, k * MID : (k + 1) * MID], NT)
                sums[b][j] = term if i == 0 else sums[b][j] + term
    for b in range(batch):
        total = sums[b][1] + shift_rows(sums[b][0], 2, width) + shift_rows(sums[b][2], -2, width)
        y_ref[b * pixels : (b + 1) * pixels, :] = total
    y = y_ref[...]
    write_stats(stat_ref, y * mask_ref[:, 0:1], y)


def conv_forward(rim, weight, mask_wide, rows, width, devices):
    batch = rim[0].shape[0]
    n = batch * rows * width
    return call(
        functools.partial(conv_forward_body, batch=batch, rows=rows, width=width),
        (*rim, weight, mask_wide),
        "hhhhv",
        (shaped(n, MID), shaped(devices, 8, 128)),
        "vv",
        5,
        24,
        [VMEM((batch, (rows + 4) * width, MID), bf16), VMEM(weight.shape, bf16), DMA((3,)), DMA((3,))],
    )


def conv_backward_body(
    above_ref, own_ref, below_ref, m_ref, y_ref, par_ref, mask_ref, dt_ref, stat_ref,
    rim_ref, m_buf, rim_sems, sems, *, batch, rows, width
):
    pixels = rows * width
    coming = taps_moving(m_ref, m_buf, sems)
    for copy in rim_moving((above_ref, own_ref, below_ref), rim_ref, rim_sems):
        copy.wait()
    sums = [[None] * 3 for _ in range(batch)]
    for i in range(3):
        coming[i].wait()
        for b in range(batch):
            for j in range(3):
                k = i * 3 + j
                start = (4 - 2 * i) * width
                term = dot(rim_ref[b, start : start + pixels, :], m_buf[:, k * MID : (k + 1) * MID])
                sums[b][j] = term if i == 0 else sums[b][j] + term
    for b in range(batch):
        total = sums[b][1] + shift_rows(sums[b][0], -2, width) + shift_rows(sums[b][2], 2, width)
        dt_ref[b * pixels : (b + 1) * pixels, :] = total
    y = y_ref[...]
    dt = gelu_slope(normed(y, par_ref)) * (dt_ref[...] * mask_ref[:, 0:1])
    dt_ref[...] = dt
    write_stats(stat_ref, dt, normal_of(y, par_ref))


def conv_backward(rim, weight, y, par, mask_wide, rows, width, devices, after):
    batch = rim[0].shape[0]
    n = batch * rows * width
    return call(
        functools.partial(conv_backward_body, batch=batch, rows=rows, width=width),
        (*rim, weight, y, par, mask_wide),
        "hhhhvvv",
        (shaped(n, MID), shaped(devices, 8, 128)),
        "vv",
        6,
        24,
        [VMEM((batch, (rows + 4) * width, MID), bf16), VMEM(weight.shape, bf16), DMA((3,)), DMA((3,))],
        after,
    )


def conv_weight_body(
    dy_ref, above_ref, own_ref, below_ref, out_ref, rim_ref, dyt_ref, out_buf, rim_sems, sems,
    *, batch, rows, width
):
    pixels = rows * width
    coming = rim_moving((above_ref, own_ref, below_ref), rim_ref, rim_sems)
    dy = dy_ref[...].astype(f32)
    going = []
    for j in range(3):
        moved = shift_rows(dy, 2 * (j - 1), width) if j != 1 else dy
        dyt_ref[j] = moved.T.astype(bf16)
        if j == 0:
            for copy in coming:
                copy.wait()
        for i in range(3):
            part = slice((i * 3 + j) * MID, (i * 3 + j + 1) * MID)
            start = 2 * i * width
            total = None
            for b in range(batch):
                term = dot(dyt_ref[j, :, b * pixels : (b + 1) * pixels], rim_ref[b, start : start + pixels, :])
                total = term if total is None else total + term
            out_buf[:, part] = total.astype(bf16)
            going.append(moving(out_buf.at[:, part], out_ref.at[:, part], sems.at[i * 3 + j]))
    for copy in going:
        copy.wait()


def conv_weight_gradient(dy, rim, rows, width, after):
    batch = rim[0].shape[0]
    return call(
        functools.partial(conv_weight_body, batch=batch, rows=rows, width=width),
        (dy, *rim),
        "vhhh",
        (shaped(MID, 9 * MID, dtype=bf16),),
        "h",
        6,
        20,
        [
            VMEM((batch, (rows + 4) * width, MID), bf16),
            VMEM((3, MID, batch * rows * width), bf16),
            VMEM((MID, 9 * MID), bf16),
            DMA((3,)),
            DMA((9,)),
        ],
        after,
    )[0]


def columns_weight_body(dy_ref, cols_ref, out_ref, dyt_ref, cols_buf, out_buf, sems):
    coming = columns_moving(cols_ref, cols_buf, sems.at[0])
    dyt_ref[...] = dy_ref[...].astype(f32).T.astype(bf16)
    going = []
    for s, part in blocks(cols_ref.shape[1]):
        coming[s].wait()
        out_buf[:, part] = dot(dyt_ref[...], cols_buf[:, part]).astype(bf16)
        going.append(moving(out_buf.at[:, part], out_ref.at[:, part], sems.at[1, s]))
    for copy in going:
        copy.wait()


def columns_weight_gradient(dy, cols, through):
    n, wide = cols.shape
    return call(
        columns_weight_body,
        (dy, cols),
        "vh",
        (shaped(MID, wide, dtype=bf16),),
        "h",
        6,
        20,
        [VMEM((MID, n), bf16), VMEM((n, wide), bf16), VMEM((MID, wide), bf16), DMA((2, wide // STEP))],
        through=through,
    )


TILES = 2
EPSILON = 1e-05


def swap_with(values, axis, step):
    return lax.ppermute(values, axis, [(i, i ^ step) for i in range(lax.axis_size(axis))])


def from_behind(block, axis, distance):
    devices = range(lax.axis_size(axis))
    route = [(i - distance, i) for i in devices if i - distance in devices]
    return lax.ppermute(block, axis, route)


def ladder_sum(values, axis):
    step = 1
    while step < lax.axis_size(axis):
        got = swap_with(values.astype(bf16), axis, step)
        values = values + got.astype(f32)
        step *= 2
    return values


def to_everyone(spread, groups=None):
    return lax.all_to_all(spread, ("rows", "ch"), 0, 0, axis_index_groups=groups, tiled=True)


def small_total(spread):
    return jnp.sum(to_everyone(spread), axis=0).reshape(2, -1)


def wide_total(block):
    devices = lax.axis_size("rows") * lax.axis_size("ch")
    core = lax.axis_index("ch") % 2
    above, below = block.reshape(2, -1, 128)
    half = jnp.where(core == 0, above, below) + swap_with(jnp.where(core == 0, below, above), "ch", 1)
    groups = [[i * 2 + k for i in range(devices // 2)] for k in range(2)]
    half = jnp.broadcast_to(half[None], (devices // 2,) + half.shape)
    half = jnp.sum(to_everyone(half, groups), axis=0)
    other = swap_with(half, "ch", 1)
    whole = jnp.stack([jnp.where(core == 0, half, other), jnp.where(core == 0, other, half)])
    whole = whole.reshape(-1, 2, STEP)
    return whole[:, 0].reshape(-1), whole[:, 1].reshape(-1)


def forward_rows(sums, gain, shift, count):
    mean = sums[0] / count
    scale = lax.rsqrt(sums[1] / count - mean * mean + EPSILON)
    return jnp.stack([scale * gain, shift - mean * scale * gain, scale, -mean * scale])


def backward_rows(sums, par, count):
    rows = jnp.stack([par[0], par[0] * sums[0] / count, par[0] * sums[1] / count])
    return rows, jnp.stack([sums[1], sums[0]])


def gather_weight(weight):
    return lax.all_gather(weight.astype(bf16), "ch", axis=0, tiled=True)


def gather_weight_after(weight, *after):
    return lax.all_gather(cast_after(weight, *after), "ch", axis=0, tiled=True)


def gather_by_swaps(weight):
    ch = lax.axis_size("ch")
    came = None
    held = weight.astype(bf16)[None]
    step = ch // 2
    while step >= 1:
        got = swap_with(held, "ch", step)
        came = got if came is None else came
        odd = lax.axis_index("ch") // step % 2 == 1
        held = jnp.stack([jnp.where(odd, got, held), jnp.where(odd, held, got)], axis=1)
        held = held.reshape((-1,) + held.shape[2:])
        step //= 2
    return held.reshape((-1,) + weight.shape[1:]), came


def pick(values, bit):
    return lax.dynamic_index_in_dim(values, bit, 1, keepdims=False)


def scatter_ch(gradient):
    return lax.psum_scatter(gradient, "ch", scatter_dimension=0, tiled=True)


def split(total, axis, step):
    bit = lax.axis_index(axis) // step % 2
    pairs = total.reshape((total.shape[0] // 2, 2) + total.shape[1:])
    return swap_with(pick(pairs, 1 - bit), axis, step), pick(pairs, bit)


def added(pair):
    got, kept = pair
    return (got.astype(f32) + kept.astype(f32)).astype(bf16)


def rest_of(total, axis, step=1):
    while step < lax.axis_size(axis):
        total = added(split(total, axis, step))
        step *= 2
    return total


def by_owner(gradient, axis="ch"):
    count = lax.axis_size(axis)
    return gradient.reshape((count, gradient.shape[0] // count) + gradient.shape[1:])


def wide_enough(base):
    return base // lax.axis_size("rows") % 16 == 0


def first_cut(parts, base, token):
    if wide_enough(base):
        return pack_split(parts, base, lax.axis_size("rows"), token)
    laid = [jnp.concatenate([p[r : r + base] for r in range(0, p.shape[0], base)], axis=1) for p in parts]
    pairs = by_owner(jnp.concatenate(laid, axis=1), "rows")
    pairs = pairs.reshape((pairs.shape[0] // 2, 2) + pairs.shape[1:])
    bit = lax.axis_index("rows") % 2
    return pick(pairs, 1 - bit), pick(pairs, bit), token


def first_step(parts, base, token):
    send, keep, token = first_cut(parts, base, token)
    return swap_with(send, "rows", 1), keep, token


class Ladder:
    def __init__(self, got, kept):
        self.got, self.kept, self.step, self.up = got, kept, 2, True

    def advance(self, token):
        last = lax.axis_size("rows") // 2
        if self.up and self.step <= last:
            send, self.kept, token = step_split(self.got, self.kept, "rows", self.step, token)
            self.got = swap_with(send, "rows", self.step)
            self.step *= 2
        elif self.up:
            self.kept, token = step_sum(self.got, self.kept, token)
            self.up, self.step = False, last
            self.got = swap_with(self.kept, "rows", self.step)
        else:
            self.kept, token = join_step(self.got, self.kept, self.step, token)
            self.step //= 2
            self.got = swap_with(self.kept, "rows", self.step)
        return token

    def ready(self):
        return not self.up and self.step == 1

    def finish(self, cuts, token):
        while not self.ready():
            token = self.advance(token)
        return final_join(self.got, self.kept, cuts, token)


def deep_rows(tile):
    odd = lax.axis_index("rows") % 2 == 1
    far_up = from_behind(tile, "rows", 2)
    far_down = from_behind(tile, "rows", -2)
    near = swap_with(tile, "rows", 1)
    other = swap_with(jnp.where(odd, far_up, far_down), "rows", 1)
    return far_up, jnp.where(odd, near, other), tile, jnp.where(odd, other, near), far_down


def near_rows(tile, width):
    size = 2 * width
    above = from_behind(tile[:, -size:], "rows", 1)
    below = from_behind(tile[:, :size], "rows", -1)
    return above, tile, below


def per_device(
    inputs,
    heights,
    displacements,
    reduce_one,
    reduce_gain_one,
    reduce_bias_one,
    offset_weight,
    deform_weight,
    deform_gain,
    deform_bias,
    expand_one,
    expand_gain_one,
    expand_bias_one,
    reduce_two,
    reduce_gain_two,
    reduce_bias_two,
    conv_weight,
    conv_gain,
    conv_bias,
    expand_two,
    expand_gain_two,
    expand_bias_two,
    cotangent,
):
    batch, rows, width, channels = inputs.shape
    pixels = rows * width
    n = batch * pixels
    own_heights = lax.dynamic_slice_in_dim(heights, lax.axis_index("ch") * batch, batch)
    rows_here = lax.axis_index("rows") * rows + jnp.arange(rows, dtype=jnp.int32)
    mask = (rows_here[None, :] < own_heights[:, None]).astype(f32)
    mask = jnp.broadcast_to(mask[:, :, None], (batch, rows, width)).reshape(n, 1)
    mask_wide = jnp.broadcast_to(mask, (n, 128))
    count = jnp.sum(heights).astype(f32) * width

    offset_rows = offset_weight.astype(bf16).reshape(3, 6, 3, 3, MID).transpose(2, 3, 0, 1, 4)
    offset_rows = jnp.pad(offset_rows, ((0, 0), (0, 0), (0, 1), (0, 2), (0, 0))).reshape(3, 96, MID)
    disp = jnp.pad(displacements.reshape(3, 6, batch, pixels), ((0, 0), (0, 2), (0, 0), (0, 0)))
    disp = disp.transpose(2, 0, 1, 3)

    reduce_full, came = gather_by_swaps(reduce_one)
    deform_full = gather_weight_after(deform_weight, came)
    expand_full, reduce_full_two, conv_full, expand_full_two = [
        gather_weight(w) for w in (expand_one, reduce_two, conv_weight, expand_two)
    ]

    devices = lax.axis_size("rows") * lax.axis_size("ch")
    acts = inputs.reshape(n, channels)
    acts_low, y_a, spread = product_forward(acts, mask_wide, reduce_full, devices)
    par_a = forward_rows(small_total(spread), reduce_gain_one, reduce_bias_one, count)
    hidden = (gelu(y_a * par_a[0] + par_a[1]) * mask).astype(bf16)
    near_tiles = deep_rows(hidden.reshape(batch, pixels, MID))
    columns, y_b, fraction, spread = deform_forward(
        near_tiles, offset_rows, disp, deform_full, mask_wide, rows, width, devices
    )
    par_b = forward_rows(small_total(spread), deform_gain, deform_bias, count)
    middle, y_c, block = expand_forward([y_b], par_b, mask_wide, expand_full)
    par_c = forward_rows(wide_total(block), expand_gain_one, expand_bias_one, count)

    first_low, y_d, spread = first_forward(y_c, par_c, acts, mask_wide, reduce_full_two, devices)
    par_d = forward_rows(small_total(spread), reduce_gain_two, reduce_bias_two, count)
    hidden_two = (gelu(y_d * par_d[0] + par_d[1]) * mask).astype(bf16)
    rimmed = near_rows(hidden_two.reshape(batch, pixels, MID), width)
    y_e, spread = conv_forward(rimmed, conv_full, mask_wide, rows, width, devices)
    par_e = forward_rows(small_total(spread), conv_gain, conv_bias, count)
    middle_two, y_f, block = expand_forward([y_e], par_e, mask_wide, expand_full_two)
    par_f = forward_rows(wide_total(block), expand_gain_two, expand_bias_two, count)

    output, dt_f, block = output_stage(y_f, par_f, first_low, cotangent.reshape(n, channels), mask_wide)
    back_f, sums_f = backward_rows(wide_total(block), par_f, count)
    dy_f, dt_e, spread = expand_backward(
        dt_f, y_f, par_f, back_f, mask_wide, expand_full_two, y_e, par_e, devices
    )
    expand_two_local = dot(dy_f, middle_two, TN).astype(bf16)
    expand_two_part = scatter_ch(expand_two_local)
    back_e, sums_e = backward_rows(small_total(spread), par_e, count)
    dy_e = norm_gradient(dt_e, y_e, par_e, back_e, mask).astype(bf16)
    dy_e_rim = near_rows(dy_e.reshape(batch, pixels, MID), width)
    conv_local = conv_weight_gradient(dy_e, rimmed, rows, width, (expand_two_local,))
    conv_part = scatter_ch(conv_local)
    dt_d, spread = conv_backward(
        dy_e_rim, conv_full, y_d, par_d, mask_wide, rows, width, devices, (conv_local,)
    )
    base = conv_part.shape[0]
    back_d, sums_d = backward_rows(small_total(spread), par_d, count)
    dy_d, dt_c, block = residual_backward(
        dt_d, y_d, par_d, back_d, mask_wide, reduce_full_two, dt_f, y_c, par_c, acts_low
    )
    reduce_two_local = dot(dy_d, first_low, TN).astype(bf16)

    back_c, sums_c = backward_rows(wide_total(block), par_c, count)
    dy_c, dt_b, spread, reduce_two_local = expand_backward(
        dt_c, y_c, par_c, back_c, mask_wide, expand_full, y_b, par_b, devices, (reduce_two_local,)
    )
    reduce_two_part = scatter_ch(reduce_two_local)
    expand_one_local = dot(dy_c, middle, TN).astype(bf16)
    back_b, sums_b = backward_rows(small_total(spread), par_b, count)
    dy_b = norm_gradient(dt_b, y_b, par_b, back_b, mask).astype(bf16)
    token = jnp.zeros((8, 128), f32)
    got_p, kept_p, token = first_step([conv_part, expand_two_part], base, token)
    deform_local, kept_p = columns_weight_gradient(dy_b, columns, (kept_p,))
    deform_part = scatter_ch(deform_local)
    sum_p = Ladder(got_p, kept_p)
    odd = lax.axis_index("rows") % 2 == 1
    images, passed, offset_local, after = [], [], 0.0, ()
    for b in range(batch):
        *tiles, offset_term, sum_p.kept, expand_one_local, token = deform_backward(
            b, near_tiles, offset_rows, disp, fraction, deform_full,
            dy_b, rows, width, after, (sum_p.kept, expand_one_local), token,
        )
        if b == 0:
            token = sum_p.advance(token)
        after = (reduce_two_part,)
        offset_local = offset_local + offset_term
        images.append(tiles)
        passed.append(swap_with(jnp.where(odd, tiles[3], tiles[1]), "rows", 1))
    expand_one_part = scatter_ch(expand_one_local)
    beyond = []
    for b in range(batch):
        pairs = [(t[1], t[3]) for t in images] if b == batch - 1 else []
        below, above, *partners, token = return_step(images[b], passed[b], pairs, token)
        beyond.append((from_behind(below, "rows", -2), from_behind(above, "rows", 2)))
    pieces = []
    for b in range(batch):
        pieces += [images[b][2], swap_with(partners[b], "rows", 1), *beyond[b]]
    token = sum_p.advance(token)
    send_q, kept_q, token = first_cut([reduce_two_part], base, token)
    send_r, kept_r, token = first_cut([deform_part], base, token)
    dt_a, spread, sum_p.kept, send_q, send_r, token = hidden_backward(
        pieces, y_a, par_a, mask_wide, devices, (sum_p.kept, send_q, send_r), token
    )
    got_q, got_r = swap_with(send_q, "rows", 1), swap_with(send_r, "rows", 1)
    back_a, sums_a = backward_rows(small_total(spread), par_a, count)
    dy_a, send_s, kept_s, sum_p.kept, kept_q, kept_r, offset_local, token = last_gradient(
        dt_a, y_a, par_a, back_a, mask_wide, acts_low, lax.axis_size("ch"),
        (sum_p.kept, kept_q, kept_r, offset_local), token
    )
    got_s = swap_with(send_s, "ch", 1)
    sum_q, sum_r = Ladder(got_q, kept_q), Ladder(got_r, kept_r)
    token = sum_p.advance(token)
    step = 2
    while step < lax.axis_size("ch"):
        send_s, kept_s, token = step_split(got_s, kept_s, "ch", step, token)
        got_s = swap_with(send_s, "ch", step)
        step *= 2
    token = sum_r.advance(token)
    token = sum_q.advance(token)
    token = sum_p.advance(token)
    input_grad, token = input_backward(dy_a, reduce_full, dt_c, token)
    token = sum_q.advance(token)
    got_e, kept_e, token = first_step([expand_one_part], base, token)
    sum_e = Ladder(got_e, kept_e)
    while not sum_p.ready():
        token = sum_p.advance(token)
    token = sum_q.advance(token)
    offset_local = offset_local.reshape(3, 3, 4, 8, MID)[:, :, :3, :6]
    offset_local = offset_local.transpose(2, 3, 0, 1, 4).reshape(-1, MID)
    offset_part = ladder_sum(offset_local, "ch").astype(bf16)
    offset_part = jnp.pad(offset_part, ((0, -offset_part.shape[0] % base), (0, 0)))
    reduce_one_part, token = step_sum(got_s, kept_s, token)
    got_s, kept_s, token = first_step([reduce_one_part[0], offset_part], base, token)
    sum_s = Ladder(got_s, kept_s)
    token = sum_e.advance(token)
    token = sum_r.advance(token)
    token = sum_q.advance(token)
    token = sum_s.advance(token)
    token = sum_e.advance(token)
    token = sum_r.advance(token)
    token = sum_s.advance(token)
    (conv_weight_grad, expand_two_grad), token = sum_p.finish(((1, 9 * MID), (channels // MID, MID)), token)
    token = sum_e.advance(token)
    token = sum_s.advance(token)
    token = sum_r.advance(token)
    (reduce_two_grad,), token = sum_q.finish(((1, channels),), token)
    token = sum_e.advance(token)
    token = sum_s.advance(token)
    (deform_weight_grad,), token = sum_r.finish(((1, 9 * MID),), token)
    (expand_one_grad,), token = sum_e.finish(((channels // MID, MID),), token)
    ends, token = owned((sums_a, sums_b, sums_c, sums_d, sums_e, sums_f), lax.axis_size("ch"), token)
    (reduce_one_grad, offset_grad), token = sum_s.finish(
        ((1, channels), (offset_part.shape[0] // base, MID)), token
    )
    offset_weight_grad = offset_grad[:162].reshape(18, 9 * MID)
    reduce_gain_one_grad, reduce_bias_one_grad, deform_gain_grad, deform_bias_grad = ends[:4]
    expand_gain_one_grad, expand_bias_one_grad, reduce_gain_two_grad, reduce_bias_two_grad = ends[4:8]
    conv_gain_grad, conv_bias_grad, expand_gain_two_grad, expand_bias_two_grad = ends[8:]
    return (
        output.reshape(inputs.shape),
        input_grad.reshape(inputs.shape),
        reduce_one_grad,
        reduce_gain_one_grad,
        reduce_bias_one_grad,
        offset_weight_grad,
        deform_weight_grad,
        deform_gain_grad,
        deform_bias_grad,
        expand_one_grad,
        expand_gain_one_grad,
        expand_bias_one_grad,
        reduce_two_grad,
        reduce_gain_two_grad,
        reduce_bias_two_grad,
        conv_weight_grad,
        conv_gain_grad,
        conv_bias_grad,
        expand_two_grad,
        expand_gain_two_grad,
        expand_bias_two_grad,
    )


def solution(mesh):
    tiles = P("ch", "rows", None, None)
    owned = P("ch", None)
    block = (owned, P(), P())
    placed = (tiles, P(), P(None, "ch", "rows", None)) + block + (P(),) + 2 * block + 3 * block + (tiles,)
    grads = (owned, P("ch"), P("ch"))
    return jax.shard_map(
        per_device,
        mesh=mesh,
        in_specs=placed,
        out_specs=(tiles, tiles) + grads + (P(),) + 2 * grads + 3 * grads,
        check_vma=False,
    )
```

```python
import functools

import jax
import jax.numpy as jnp
from jax import lax
from jax.experimental import pallas as pl
from jax.experimental.pallas import tpu as pltpu
from jax.sharding import PartitionSpec as P

bf16 = jnp.bfloat16
f32 = jnp.float32
VMEM = pltpu.VMEM
HBM = pltpu.HBM
DMA = pltpu.SemaphoreType.DMA
MID = 512
STEP = 512
NT = (((1,), (1,)), ((), ()))
TN = (((0,), (0,)), ((), ()))
NN = (((1,), (0,)), ((), ()))
GELU_A = 0.7978845608028654
GELU_B = 0.044715


def dot(a, b, dims=NN):
    return lax.dot_general(a, b, dims, preferred_element_type=f32)


def shaped(*shape, dtype=f32):
    return jax.ShapeDtypeStruct(shape, dtype)


def without(body, n_in, n_order, n_out, n_through, token):
    first = n_in + n_order + n_through

    def inner(*refs):
        if token:
            refs[first + n_out + n_through][...] = jnp.zeros((8, 128), f32)
        body(*refs[:n_in], *refs[first : first + n_out], *refs[first + n_out + n_through + token :])

    return inner


def cost(us):
    return pl.CostEstimate(flops=int(us * 1.1e9), bytes_accessed=int(us * 2.2e6), transcendentals=0)


def call(body, operands, places, outs, out_places, us, limit, scratch=(), after=(), through=(), token=None):
    def spec(place):
        return pl.BlockSpec(memory_space=HBM if place == "h" else VMEM)

    def pinned(value, place):
        return pltpu.with_memory_space_constraint(value, HBM) if place == "h" else value

    def result(out, place):
        return HBM(out.shape, out.dtype) if place == "h" else out

    tokens = () if token is None else (token,)
    n_in, n_out, n_order = len(operands), len(outs), len(after) + len(tokens)
    return pl.pallas_call(
        without(body, n_in, n_order, n_out, len(through), len(tokens)),
        in_specs=[spec(p) for p in places] + [spec("h")] * len(after) + [spec("v")] * len(tokens)
        + [spec("h")] * len(through),
        out_specs=tuple(spec(p) for p in out_places) + (spec("h"),) * len(through)
        + (spec("v"),) * len(tokens),
        out_shape=tuple(result(o, p) for o, p in zip(outs, out_places))
        + tuple(HBM(v.shape, v.dtype) for v in through)
        + (shaped(8, 128),) * len(tokens),
        input_output_aliases={n_in + n_order + t: n_out + t for t in range(len(through))},
        scratch_shapes=list(scratch),
        compiler_params=pltpu.CompilerParams(vmem_limit_bytes=limit * 2**20),
        cost_estimate=cost(us),
    )(
        *[pinned(v, p) for v, p in zip(operands, places)],
        *[pinned(v, "h") for v in after],
        *tokens,
        *[pinned(v, "h") for v in through],
    )


def moving(source, target, sem):
    copy = pltpu.make_async_copy(source, target, sem)
    copy.start()
    return copy


def columns_moving(source, target, sems, wide=STEP):
    return [
        moving(source.at[:, s * wide : (s + 1) * wide], target.at[:, s * wide : (s + 1) * wide], sems.at[s])
        for s in range(source.shape[1] // wide)
    ]


def rows_moving(source, target, sems, tall=STEP):
    return [
        moving(source.at[s * tall : (s + 1) * tall], target.at[s * tall : (s + 1) * tall], sems.at[s])
        for s in range(source.shape[0] // tall)
    ]


def blocks(wide):
    return [(s, slice(s * STEP, (s + 1) * STEP)) for s in range(wide // STEP)]


def gelu(v):
    return 0.5 * v * (1.0 + jnp.tanh(GELU_A * (v + GELU_B * v * v * v)))


def gelu_slope(v):
    t = jnp.tanh(GELU_A * (v + GELU_B * v * v * v))
    return 0.5 * (1.0 + t) + 0.5 * v * (1.0 - t * t) * (GELU_A * (1.0 + 3.0 * GELU_B * v * v))


def normed(values, par_ref, part=slice(None)):
    return values * par_ref[0:1, part] + par_ref[1:2, part]


def normal_of(values, par_ref, part=slice(None)):
    return values * par_ref[2:3, part] + par_ref[3:4, part]


def norm_gradient(upstream, values, par_ref, back_ref, mask, part=slice(None)):
    normal = normal_of(values, par_ref, part)
    return upstream * back_ref[0:1, part] - mask * (back_ref[1:2, part] + normal * back_ref[2:3, part])


def sums_block(weighted, values):
    n = weighted.shape[1] // 128
    sums = (
        jnp.sum(weighted, axis=0, keepdims=True),
        jnp.sum(weighted * values, axis=0, keepdims=True),
    )
    return jnp.concatenate([v[:, c * 128 : c * 128 + 128] for v in sums for c in range(n)], axis=0)


def write_stats(stat_ref, weighted, values):
    stat_ref[...] = jnp.broadcast_to(sums_block(weighted, values)[None], stat_ref.shape)


def product_forward_body(x_ref, mask_ref, w_ref, low_ref, out_ref, stat_ref, x_buf, low_buf, sems):
    wide = x_ref.shape[1]
    coming = columns_moving(x_ref, x_buf, sems.at[0])
    total, going = None, []
    for s, part in blocks(wide):
        coming[s].wait()
        low_buf[:, part] = x_buf[:, part].astype(bf16)
        going.append(moving(low_buf.at[:, part], low_ref.at[:, part], sems.at[1, s]))
        term = dot(low_buf[:, part], w_ref[:, part], NT)
        total = term if total is None else total + term
    out_ref[...] = total
    write_stats(stat_ref, total * mask_ref[:, 0:1], total)
    for copy in going:
        copy.wait()


def product_forward(x, mask_wide, weight, devices):
    n, wide = x.shape
    return call(
        product_forward_body,
        (x, mask_wide, weight),
        "hvv",
        (shaped(n, wide, dtype=bf16), shaped(n, MID), shaped(devices, 8, 128)),
        "hvv",
        5,
        20,
        [VMEM((n, wide), f32), VMEM((n, wide), bf16), DMA((2, wide // STEP))],
    )


def expand_forward_body(*refs):
    *y_refs, par_ref, mask_ref, e_ref, mid_ref, out_ref, stat_ref, e_buf, out_buf, sems = refs
    coming = rows_moving(e_ref, e_buf, sems.at[0])
    mask = mask_ref[:, 0:1]
    at = 0
    for y_ref in y_refs:
        part = slice(at, at + y_ref.shape[0])
        mid_ref[part, :] = (gelu(normed(y_ref[...], par_ref)) * mask_ref[part, 0:1]).astype(bf16)
        at += y_ref.shape[0]
    going = []
    for s, part in blocks(e_ref.shape[0]):
        coming[s].wait()
        out = dot(mid_ref[...], e_buf[part, :], NT)
        out_buf[:, part] = out.astype(bf16)
        going.append(moving(out_buf.at[:, part], out_ref.at[:, part], sems.at[1, s]))
        stat_ref[s * 8 : s * 8 + 8, :] = sums_block(out * mask, out)
    for copy in going:
        copy.wait()


def expand_forward(y_parts, par, mask_wide, weight):
    n, wide = mask_wide.shape[0], weight.shape[0]
    return call(
        expand_forward_body,
        (*y_parts, par, mask_wide, weight),
        "v" * (len(y_parts) + 2) + "h",
        (shaped(n, MID, dtype=bf16), shaped(n, wide, dtype=bf16), shaped(wide // 64, 128)),
        "vhv",
        4,
        16,
        [VMEM(weight.shape, bf16), VMEM((n, wide), bf16), DMA((2, wide // STEP))],
    )


def first_forward_body(
    y_ref, par_ref, x_ref, mask_ref, w_ref, low_ref, out_ref, stat_ref,
    y_buf, x_buf, w_buf, low_buf, sems
):
    wide = x_ref.shape[1]
    coming_y = columns_moving(y_ref, y_buf, sems.at[0])
    coming_x = columns_moving(x_ref, x_buf, sems.at[1])
    coming_w = columns_moving(w_ref, w_buf, sems.at[2])
    mask = mask_ref[:, 0:1]
    total, going = None, []
    for s, part in blocks(wide):
        coming_y[s].wait()
        coming_x[s].wait()
        first = gelu(normed(y_buf[:, part].astype(f32), par_ref, part) + x_buf[:, part]) * mask
        low_buf[:, part] = first.astype(bf16)
        going.append(moving(low_buf.at[:, part], low_ref.at[:, part], sems.at[3, s]))
        coming_w[s].wait()
        term = dot(low_buf[:, part], w_buf[:, part], NT)
        total = term if total is None else total + term
    out_ref[...] = total
    write_stats(stat_ref, total * mask, total)
    for copy in going:
        copy.wait()


def first_forward(y, par, x, mask_wide, weight, devices):
    n, wide = y.shape
    return call(
        first_forward_body,
        (y, par, x, mask_wide, weight),
        "hvhvh",
        (shaped(n, wide, dtype=bf16), shaped(n, MID), shaped(devices, 8, 128)),
        "hvv",
        6,
        24,
        [
            VMEM((n, wide), bf16),
            VMEM((n, wide), f32),
            VMEM(weight.shape, bf16),
            VMEM((n, wide), bf16),
            DMA((4, wide // STEP)),
        ],
    )


def output_stage_body(
    y_ref, par_ref, first_ref, cot_ref, mask_ref, out_ref, dt_ref, stat_ref,
    y_buf, first_buf, cot_buf, out_buf, dt_buf, sems
):
    wide = y_ref.shape[1]
    coming_y = columns_moving(y_ref, y_buf, sems.at[0])
    coming_f = columns_moving(first_ref, first_buf, sems.at[1])
    coming_c = columns_moving(cot_ref, cot_buf, sems.at[2])
    mask = mask_ref[:, 0:1]
    going = []
    for s, part in blocks(wide):
        coming_y[s].wait()
        coming_f[s].wait()
        y = y_buf[:, part].astype(f32)
        pre = normed(y, par_ref, part) + first_buf[:, part].astype(f32)
        t = jnp.tanh(GELU_A * (pre + GELU_B * pre * pre * pre))
        out_buf[:, part] = 0.5 * pre * (1.0 + t) * mask
        going.append(moving(out_buf.at[:, part], out_ref.at[:, part], sems.at[3, s]))
        slope = 0.5 * (1.0 + t) + 0.5 * pre * (1.0 - t * t) * (GELU_A * (1.0 + 3.0 * GELU_B * pre * pre))
        coming_c[s].wait()
        dt = slope * (cot_buf[:, part] * mask)
        dt_buf[:, part] = dt.astype(bf16)
        going.append(moving(dt_buf.at[:, part], dt_ref.at[:, part], sems.at[4, s]))
        stat_ref[s * 8 : s * 8 + 8, :] = sums_block(dt, normal_of(y, par_ref, part))
    for copy in going:
        copy.wait()


def output_stage(y, par, first, cot, mask_wide):
    n, wide = y.shape
    return call(
        output_stage_body,
        (y, par, first, cot, mask_wide),
        "hvhhv",
        (shaped(n, wide), shaped(n, wide, dtype=bf16), shaped(wide // 64, 128)),
        "hhv",
        8,
        28,
        [
            VMEM((n, wide), bf16),
            VMEM((n, wide), bf16),
            VMEM((n, wide), f32),
            VMEM((n, wide), f32),
            VMEM((n, wide), bf16),
            DMA((5, wide // STEP)),
        ],
    )


def expand_backward_body(
    dt_ref, y_ref, par_ref, back_ref, mask_ref, e_ref, mid_y_ref, mid_par_ref,
    dy_ref, mid_dt_ref, stat_ref, dt_buf, y_buf, e_buf, dy_buf, sems
):
    wide = dt_ref.shape[1]
    coming_dt = columns_moving(dt_ref, dt_buf, sems.at[0])
    coming_y = columns_moving(y_ref, y_buf, sems.at[1])
    coming_e = rows_moving(e_ref, e_buf, sems.at[2])
    mask = mask_ref[:, 0:1]
    total, going = None, []
    for s, part in blocks(wide):
        coming_dt[s].wait()
        coming_y[s].wait()
        dt, y = dt_buf[:, part].astype(f32), y_buf[:, part].astype(f32)
        dy = norm_gradient(dt, y, par_ref, back_ref, mask, part).astype(bf16)
        dy_buf[:, part] = dy
        going.append(moving(dy_buf.at[:, part], dy_ref.at[:, part], sems.at[3, s]))
        coming_e[s].wait()
        term = dot(dy, e_buf[part, :])
        total = term if total is None else total + term
    y = mid_y_ref[...]
    dt = gelu_slope(normed(y, mid_par_ref)) * (total * mask)
    mid_dt_ref[...] = dt
    write_stats(stat_ref, dt, normal_of(y, mid_par_ref))
    for copy in going:
        copy.wait()


def expand_backward(dt, y, par, back, mask_wide, weight, mid_y, mid_par, devices, through=()):
    n, wide = y.shape
    return call(
        expand_backward_body,
        (dt, y, par, back, mask_wide, weight, mid_y, mid_par),
        "hhvvvhvv",
        (shaped(n, wide, dtype=bf16), shaped(n, MID), shaped(devices, 8, 128)),
        "hvv",
        5,
        24,
        [
            VMEM((n, wide), bf16),
            VMEM((n, wide), bf16),
            VMEM(weight.shape, bf16),
            VMEM((n, wide), bf16),
            DMA((4, wide // STEP)),
        ],
        through=through,
    )


def residual_backward_body(
    dt_ref, y_ref, par_ref, back_ref, mask_ref, w_ref, add_ref, wide_y_ref, wide_par_ref, x_ref,
    dy_ref, out_ref, stat_ref, w_buf, add_buf, y_buf, x_buf, out_buf, sems
):
    wide = x_ref.shape[1]
    coming = [
        columns_moving(source, target, sems.at[t])
        for t, (source, target) in enumerate(
            ((w_ref, w_buf), (add_ref, add_buf), (wide_y_ref, y_buf), (x_ref, x_buf))
        )
    ]
    mask = mask_ref[:, 0:1]
    dy_ref[...] = norm_gradient(dt_ref[...], y_ref[...], par_ref, back_ref, mask).astype(bf16)
    going = []
    for s, part in blocks(wide):
        for copies in coming:
            copies[s].wait()
        grad = add_buf[:, part].astype(f32) + dot(dy_ref[...], w_buf[:, part])
        y = y_buf[:, part].astype(f32)
        pre = normed(y, wide_par_ref, part) + x_buf[:, part].astype(f32)
        dt = gelu_slope(pre) * (grad * mask)
        out_buf[:, part] = dt.astype(bf16)
        going.append(moving(out_buf.at[:, part], out_ref.at[:, part], sems.at[4, s]))
        stat_ref[s * 8 : s * 8 + 8, :] = sums_block(dt, normal_of(y, wide_par_ref, part))
    for copy in going:
        copy.wait()


def residual_backward(dt, y, par, back, mask_wide, weight, add, wide_y, wide_par, x):
    n, wide = x.shape
    return call(
        residual_backward_body,
        (dt, y, par, back, mask_wide, weight, add, wide_y, wide_par, x),
        "vvvvvhhhvh",
        (shaped(n, MID, dtype=bf16), shaped(n, wide, dtype=bf16), shaped(wide // 64, 128)),
        "vhv",
        6,
        24,
        [VMEM(weight.shape, bf16)] + [VMEM((n, wide), bf16)] * 4 + [DMA((5, wide // STEP))],
    )


def input_backward_body(dy_ref, w_ref, add_ref, out_ref, w_buf, add_buf, out_buf, sems):
    coming_w = columns_moving(w_ref, w_buf, sems.at[0])
    coming_a = columns_moving(add_ref, add_buf, sems.at[1])
    going = []
    for s, part in blocks(w_ref.shape[1]):
        coming_w[s].wait()
        coming_a[s].wait()
        out_buf[:, part] = add_buf[:, part].astype(f32) + dot(dy_ref[...], w_buf[:, part])
        going.append(moving(out_buf.at[:, part], out_ref.at[:, part], sems.at[2, s]))
    for copy in going:
        copy.wait()


def input_backward(dy, weight, add, through):
    n, wide = add.shape
    return call(
        input_backward_body,
        (dy, weight, add),
        "vhh",
        (shaped(n, wide),),
        "h",
        5,
        20,
        [VMEM(weight.shape, bf16), VMEM((n, wide), bf16), VMEM((n, wide), f32), DMA((3, wide // STEP))],
        through=through,
    )


def hidden_backward_body(*refs):
    *piece_refs, y_ref, par_ref, mask_ref, dt_ref, stat_ref = refs
    batch = len(piece_refs) // 4
    pixels = y_ref.shape[0] // batch
    for b in range(batch):
        own, near, up, down = [ref[...].astype(f32) for ref in piece_refs[4 * b : 4 * b + 4]]
        dt_ref[b * pixels : (b + 1) * pixels, :] = own + near + up + down
    grad = dt_ref[...]
    y = y_ref[...]
    dt = gelu_slope(normed(y, par_ref)) * (grad * mask_ref[:, 0:1])
    dt_ref[...] = dt
    write_stats(stat_ref, dt, normal_of(y, par_ref))


def hidden_backward(pieces, y, par, mask_wide, devices, through):
    n = y.shape[0]
    return call(
        hidden_backward_body,
        (*pieces, y, par, mask_wide),
        "v" * (len(pieces) + 3),
        (shaped(n, MID), shaped(devices, 8, 128)),
        "vv",
        3,
        16,
        through=through,
    )


def last_gradient_body(
    dt_ref, y_ref, par_ref, back_ref, mask_ref, acts_ref, dy_ref, send_ref, keep_ref,
    dyt_ref, acts_buf, out_buf, in_sems, out_sems
):
    coming = columns_moving(acts_ref, acts_buf, in_sems)
    dy = norm_gradient(dt_ref[...], y_ref[...], par_ref, back_ref, mask_ref[:, 0:1]).astype(bf16)
    dy_ref[...] = dy
    dyt_ref[...] = dy.astype(f32).T.astype(bf16)
    core = lax.axis_index("ch") % 2
    half, base = send_ref.shape[0], send_ref.shape[1]
    going = []
    for s, part in blocks(acts_ref.shape[1]):
        coming[s].wait()
        out_buf[:, part] = dot(dyt_ref[...], acts_buf[:, part]).astype(bf16)
        for q in range(half):
            for t, (out_ref, side) in enumerate(((send_ref, 1 - core), (keep_ref, core))):
                row = pl.multiple_of((2 * q + side) * base, 16)
                going.append(
                    moving(
                        out_buf.at[pl.ds(row, base), part], out_ref.at[q, :, part], out_sems.at[s, q, t]
                    )
                )
    for copy in going:
        copy.wait()


def last_gradient(dt, y, par, back, mask_wide, acts, ch, through):
    n, wide = acts.shape
    half = shaped(ch // 2, MID // ch, wide, dtype=bf16)
    return call(
        last_gradient_body,
        (dt, y, par, back, mask_wide, acts),
        "vvvvvh",
        (shaped(n, MID, dtype=bf16), half, half),
        "vhh",
        6,
        20,
        [
            VMEM((MID, n), bf16),
            VMEM((n, wide), bf16),
            VMEM((MID, wide), bf16),
            DMA((wide // STEP,)),
            DMA((wide // STEP, ch // 2, 2)),
        ],
        through=through,
    )


def cast_body(v_ref, out_ref):
    out_ref[...] = v_ref[...].astype(bf16)


def cast_after(values, *after):
    return call(cast_body, (values,), "v", (shaped(*values.shape, dtype=bf16),), "v", 2, 12, after=after)[0]


def pack_body(*refs, count, bit_axis, rows):
    part_refs, (send_ref, keep_ref), refs = refs[:count], refs[count : count + 2], refs[count + 2 :]
    buffers, (in_sem, out_sem) = refs[:count], refs[count:]
    coming = [moving(ref, buf, in_sem.at[t]) for t, (ref, buf) in enumerate(zip(part_refs, buffers))]
    bit = lax.axis_index(bit_axis) % 2
    tall = send_ref.shape[1]
    base = rows * tall
    going, at = [], 0
    for copy, buf in zip(coming, buffers):
        copy.wait()
        wide = buf.shape[1]
        for block in range(buf.shape[0] // base):
            for pair in range(rows // 2):
                for out_ref, side in ((send_ref, 1 - bit), (keep_ref, bit)):
                    row = pl.multiple_of(block * base + (2 * pair + side) * tall, 16)
                    going.append(
                        moving(
                            buf.at[pl.ds(row, tall), :],
                            out_ref.at[pair, :, at : at + wide],
                            out_sem.at[len(going)],
                        )
                    )
            at += wide
    for copy in going:
        copy.wait()


def pack_split(parts, base, rows, token=None):
    count = len(parts)
    blocks_in = sum(p.shape[0] // base for p in parts)
    wide = sum(p.shape[0] // base * p.shape[1] for p in parts)
    half = shaped(rows // 2, base // rows, wide, dtype=bf16)
    return call(
        functools.partial(pack_body, count=count, bit_axis="rows", rows=rows),
        tuple(parts),
        "h" * count,
        (half, half),
        "hh",
        3,
        16,
        [VMEM(p.shape, bf16) for p in parts] + [DMA((count,)), DMA((blocks_in * rows,))],
        token=token,
    )


def step_body(got_ref, kept_ref, send_ref, keep_ref, sum_ref, *, axis, step):
    bit = lax.axis_index(axis) // step % 2
    sum_ref[...] = (got_ref[...].astype(f32) + kept_ref[...].astype(f32)).astype(bf16)
    for pair in range(send_ref.shape[0]):
        send_ref[pair] = sum_ref[2 * pair + 1 - bit]
        keep_ref[pair] = sum_ref[2 * pair + bit]


def step_split(got, kept, axis, step, token=None):
    half = shaped(got.shape[0] // 2, *got.shape[1:], dtype=bf16)
    return call(
        functools.partial(step_body, axis=axis, step=step),
        (got, kept),
        "vv",
        (half, half),
        "vv",
        2,
        12,
        [VMEM(got.shape, bf16)],
        token=token,
    )


def sum_body(got_ref, kept_ref, sum_ref):
    sum_ref[...] = (got_ref[...].astype(f32) + kept_ref[...].astype(f32)).astype(bf16)


def step_sum(got, kept):
    return call(sum_body, (got, kept), "vv", (shaped(*got.shape, dtype=bf16),), "v", 1, 12)[0]


def join_body(got_ref, kept_ref, out_ref, *, step):
    bit = lax.axis_index("rows") // step % 2
    for a in range(got_ref.shape[0]):
        out_ref[2 * a + bit] = kept_ref[a]
        out_ref[2 * a + 1 - bit] = got_ref[a]


def join_step(got, kept, step):
    m, r, wide = got.shape
    return call(
        functools.partial(join_body, step=step),
        (got, kept),
        "vv",
        (shaped(2 * m, r, wide, dtype=bf16),),
        "v",
        1,
        12,
    )[0]


def final_body(got_ref, kept_ref, *refs, cuts):
    out_refs, refs = refs[: len(cuts)], refs[len(cuts) :]
    buffers, sems = refs[: len(cuts)], refs[len(cuts)]
    bit = lax.axis_index("rows") % 2
    going, at = [], 0
    for out_ref, buf, (count, wide) in zip(out_refs, buffers, cuts):
        for k in range(count):
            part = slice(at, at + wide)
            for a in range(got_ref.shape[0]):
                buf[k, 2 * a + bit] = kept_ref[a, :, part].astype(f32)
                buf[k, 2 * a + 1 - bit] = got_ref[a, :, part].astype(f32)
            going.append(moving(buf.at[k], out_ref.at[k], sems.at[len(going)]))
            at += wide
    for copy in going:
        copy.wait()


def final_join(got, kept, cuts):
    m, r, _ = got.shape
    outs = [shaped(count, 2 * m, r, wide) for count, wide in cuts]
    outs = call(
        functools.partial(final_body, cuts=cuts),
        (got, kept),
        "vv",
        outs,
        "h" * len(outs),
        2,
        20,
        [VMEM(o.shape, f32) for o in outs] + [DMA((sum(count for count, _ in cuts),))],
    )
    return [o.reshape(-1, o.shape[3]) for o in outs]


def owned_body(*refs):
    n = len(refs) // 3
    for k in range(n):
        size = refs[n + 2 * k].shape[1]
        start = lax.axis_index("ch") * size
        turned = pltpu.roll(refs[k][...], refs[k].shape[1] - start, 1)
        refs[n + 2 * k][...] = turned[0:1, :size]
        refs[n + 2 * k + 1][...] = turned[1:2, :size]


def owned(sums, ch):
    outs = [shaped(1, s.shape[1] // ch) for s in sums for _ in range(2)]
    outs = call(owned_body, tuple(sums), "v" * len(sums), outs, "v" * len(outs), 1, 12)
    return [o.reshape(-1) for o in outs]


def return_body(far_up_ref, up_ref, down_ref, far_down_ref, got_ref, *refs):
    count = (len(refs) - 2) // 3
    others, (below_ref, above_ref), partners = refs[: 2 * count], refs[2 * count : 2 * count + 2], refs[2 * count + 2 :]
    odd = lax.axis_index("rows") % 2 == 1

    @pl.when(odd)
    def _():
        total = far_up_ref[...].astype(f32) + got_ref[...].astype(f32)
        below_ref[...] = total.astype(bf16)
        above_ref[...] = far_down_ref[...]
        for b in range(count):
            partners[b][...] = others[2 * b][...]

    @pl.when(jnp.logical_not(odd))
    def _():
        total = far_down_ref[...].astype(f32) + got_ref[...].astype(f32)
        below_ref[...] = far_up_ref[...]
        above_ref[...] = total.astype(bf16)
        for b in range(count):
            partners[b][...] = others[2 * b + 1][...]


def return_step(tiles, got, pairs, through=()):
    far_up, up, _, down, far_down = tiles
    piece = shaped(*got.shape, dtype=bf16)
    others = [part for pair in pairs for part in pair]
    return call(
        return_body,
        (far_up, up, down, far_down, got, *others),
        "v" * (5 + len(others)),
        (piece,) * (2 + len(pairs)),
        "v" * (2 + len(pairs)),
        2,
        12,
        through=through,
    )


def gate_body(ref, out_ref):
    out_ref[...] = ref[...]


def gate(small, after, through):
    _, *through = call(gate_body, (small,), "v", (shaped(8, 128),), "v", 1, 8, after=after, through=through)
    return through


def shift_lanes(values, by, width):
    place = lax.broadcasted_iota(jnp.int32, values.shape, values.ndim - 1) % width
    moved = pltpu.roll(values, by % values.shape[-1], values.ndim - 1)
    return jnp.where((place >= by) & (place < width + by), moved, 0.0)


def shift_rows(values, by, width):
    place = lax.broadcasted_iota(jnp.int32, values.shape, 0) % width
    moved = pltpu.roll(values, by % values.shape[0], 0)
    return jnp.where((place >= by) & (place < width + by), moved, 0.0)


def offset_fraction(ext_ref, ow_ref, b, base, pixels, width):
    u = None
    for i in range(3):
        start = (base + 2 * i) * width
        term = dot(ow_ref[i], ext_ref[b, start : start + pixels, :], NT)
        u = term if u is None else u + term
    total = u[32:64]
    total = total + shift_lanes(u[0:32], 2, width) + shift_lanes(u[64:96], -2, width)
    return 1.0 / (1.0 + jnp.exp(-total))


def deform_forward_body(*refs, batch, rows, width, deep):
    tile_refs, refs = refs[:5], refs[5:]
    ow_ref, disp_ref, m_ref, mask_ref, cols_out_ref, y_ref, frac_ref, stat_ref = refs[:8]
    ext_ref, par_ref, s_ref, cols_ref, m_buf, tile_sems, sems = refs[8:]
    pixels = rows * width
    coming = [
        moving(ref, ext_ref.at[:, t * pixels : (t + 1) * pixels, :], tile_sems.at[t])
        for t, ref in enumerate(tile_refs)
    ]
    coming_m = moving(m_ref, m_buf, sems.at[0])
    for copy in coming:
        copy.wait()
    lane = lax.broadcasted_iota(jnp.int32, (32, 128), 1)
    column = lane % width
    upper = lane // width

    def image(b, carry):
        frac = offset_fraction(ext_ref, ow_ref, b, deep - 2, pixels, width)
        for i in range(4):
            frac_ref[b, i] = frac[i * 8 : i * 8 + 8]
        pix = lax.broadcasted_iota(jnp.int32, (1, pixels), 1)
        row_at, col_at = pix // width, pix % width
        tops, lefts, ys, xs = [], [], [], []
        for k in range(9):
            i, j = k // 3, k % 3
            tops.append(row_at + disp_ref[b, i, 2 * j : 2 * j + 1, :] + (deep - 2))
            lefts.append(col_at + 2 * (j - 1) + disp_ref[b, i, 2 * j + 1 : 2 * j + 2, :])
            at = i * 8 + 2 * j
            ys.append(frac[at : at + 1])
            xs.append(frac[at + 1 : at + 2])
        blank = jnp.zeros((23, pixels), f32)
        par = jnp.concatenate(
            [jnp.concatenate(g, axis=0).astype(f32) if g is not None else blank
             for g in (tops, None, lefts, None, ys, None, xs, None)], axis=0)
        par_ref[...] = par.T

        def row_of_taps(i, carry):
            for j in range(3):
                k = i * 3 + j
                for c in range(pixels // 32):
                    p = pltpu.roll(par_ref[c * 32 : c * 32 + 32, :], 128 - k, 1)
                    wide = (32, 128)
                    top = jnp.broadcast_to(p[:, 0:1], wide).astype(jnp.int32) - upper
                    left = jnp.broadcast_to(p[:, 32:33], wide).astype(jnp.int32)
                    fy = jnp.broadcast_to(p[:, 64:65], wide)
                    fx = jnp.broadcast_to(p[:, 96:97], wide)
                    cw = jnp.where(column == left, 1.0 - fx, jnp.where(column == left + 1, fx, 0.0))
                    ca, cb = (1.0 - fy) * cw, fy * cw
                    for q in range(8):
                        s = jnp.where(top == 2 * q, ca, jnp.where(top == 2 * q - 1, cb, 0.0))
                        s_ref[j * pixels + c * 32 : j * pixels + c * 32 + 32, q * 128 : q * 128 + 128] = s.astype(bf16)
            start = pl.multiple_of(i * 2 * width, 128)
            window = ext_ref[b, pl.ds(start, 16 * width), :]
            for j in range(3):
                got = dot(s_ref[j * pixels : (j + 1) * pixels, :], window).astype(bf16)
                cols_ref[pl.ds(pl.multiple_of(b * pixels, pixels), pixels), pl.ds(pl.multiple_of((i * 3 + j) * MID, MID), MID)] = got
            return carry

        return lax.fori_loop(0, 3, row_of_taps, carry)

    lax.fori_loop(0, batch, image, 0)
    going = moving(cols_ref, cols_out_ref, sems.at[1])
    coming_m.wait()
    y = dot(cols_ref[...], m_buf[...], NT)
    y_ref[...] = y
    write_stats(stat_ref, y * mask_ref[:, 0:1], y)
    going.wait()


def deform_forward(tiles, offset_rows, disp, weight, mask_wide, rows, width, devices):
    batch = tiles[0].shape[0]
    pixels = rows * width
    n = batch * pixels
    return call(
        functools.partial(deform_forward_body, batch=batch, rows=rows, width=width, deep=2 * rows),
        (*tiles, offset_rows, disp, weight, mask_wide),
        "hhhhhvvhv",
        (
            shaped(n, 9 * MID, dtype=bf16),
            shaped(n, MID),
            shaped(batch, 4, 8, pixels),
            shaped(devices, 8, 128),
        ),
        "hvvv",
        15,
        30,
        [
            VMEM((batch, 5 * pixels, MID), bf16),
            VMEM((pixels, 128), f32),
            VMEM((3 * pixels, 16 * width), bf16),
            VMEM((n, 9 * MID), bf16),
            VMEM(weight.shape, bf16),
            DMA((5,)),
            DMA((2,)),
        ],
    )


def deform_backward_body(*refs, batch, rows, width, deep):
    tile_refs, refs = refs[:5], refs[5:]
    (ow_ref, disp_ref, frac_ref, m_ref, dy_ref), refs = refs[:5], refs[5:]
    out_refs, refs = refs[: 5 * batch], refs[5 * batch :]
    dow_ref, ext_ref, dext_ref, dc_ref, g_ref, st_ref, df_ref, m_buf, tile_sems, m_sem = refs
    pixels = rows * width
    coming = [
        moving(ref, ext_ref.at[:, t * pixels : (t + 1) * pixels, :], tile_sems.at[t])
        for t, ref in enumerate(tile_refs)
    ]
    coming_m = moving(m_ref, m_buf, m_sem)
    window = 16 * width
    dow_ref[...] = jnp.zeros_like(dow_ref)
    dext_ref[...] = jnp.zeros_like(dext_ref)
    for copy in coming:
        copy.wait()
    coming_m.wait()

    def image(b, carry):
        at = pl.multiple_of(b * pixels, pixels)

        def row_of_taps(i, carry):
            dy = dy_ref[pl.ds(at, pixels), :]
            for j in range(3):
                m = m_buf[:, pl.ds(pl.multiple_of((i * 3 + j) * MID, MID), MID)]
                dc_ref[j * pixels : (j + 1) * pixels, :] = dot(dy, m).astype(bf16)
            start = pl.multiple_of(i * 2 * width, 128)
            g_ref[...] = dot(ext_ref[b, pl.ds(start, window), :], dc_ref[...], NT)
            place = lax.broadcasted_iota(jnp.int32, (width, 128), 0)
            for j in range(3):
                for h in range(pixels // 128):
                    lanes = slice(h * 128, h * 128 + 128)
                    at_l = slice(j * pixels + h * 128, j * pixels + h * 128 + 128)
                    pix = lax.broadcasted_iota(jnp.int32, (1, 128), 1) + h * 128
                    by_y, by_x = slice(2 * j, 2 * j + 1), slice(2 * j + 1, 2 * j + 2)
                    top = pix // width + disp_ref[b, i, by_y, lanes] + (deep - 2)
                    left = pix % width + 2 * (j - 1) + disp_ref[b, i, by_x, lanes]
                    fy = frac_ref[b, i, by_y, lanes]
                    fx = frac_ref[b, i, by_x, lanes]
                    here, after = place == left, place == left + 1
                    cw = jnp.where(here, 1.0 - fx, jnp.where(after, fx, 0.0))
                    ca, cb = (1.0 - fy) * cw, fy * cw
                    low_sum = jnp.zeros((width, 128), f32)
                    high_sum = jnp.zeros((width, 128), f32)
                    for r in range(16):
                        part = slice(r * width, r * width + width)
                        g = g_ref[part, at_l]
                        m0, m1 = top == r, top == r - 1
                        low_sum = low_sum + jnp.where(m0, g, 0.0)
                        high_sum = high_sum + jnp.where(m1, g, 0.0)
                        st_ref[part, at_l] = jnp.where(m0, ca, jnp.where(m1, cb, 0.0)).astype(bf16)
                    d_fy = jnp.sum((high_sum - low_sum) * cw, axis=0, keepdims=True)
                    mixed = (1.0 - fy) * low_sum + fy * high_sum
                    d_fx = jnp.sum(
                        jnp.where(after, mixed, 0.0) - jnp.where(here, mixed, 0.0), axis=0, keepdims=True)
                    df_ref[i, by_y, lanes] = d_fy * fy * (1.0 - fy)
                    df_ref[i, by_x, lanes] = d_fx * fx * (1.0 - fx)
            dext_ref[b, pl.ds(start, window), :] += dot(st_ref[...], dc_ref[...])
            return carry

        df_ref[...] = jnp.zeros_like(df_ref)
        carry = lax.fori_loop(0, 3, row_of_taps, carry)
        d_off = df_ref[...].reshape(32, pixels).astype(bf16).astype(f32)
        stacked = jnp.concatenate(
            [shift_lanes(d_off, -2, width), d_off, shift_lanes(d_off, 2, width)], axis=0)
        across = jnp.concatenate([stacked, jnp.zeros((32, pixels), f32)], axis=0).T.astype(bf16)
        stacked = stacked.astype(bf16)
        for i in range(3):
            first = (deep - 2 + 2 * i) * width
            part = slice(first, first + pixels)
            dow_ref[i] += dot(stacked, ext_ref[b, part, :])
            dext_ref[b, part, :] += dot(across[:, :96], ow_ref[i])
        return carry

    lax.fori_loop(0, batch, image, 0)
    for t, ref in enumerate(out_refs):
        ref[...] = dext_ref[t // 5, t % 5 * pixels : (t % 5 + 1) * pixels, :].astype(ref.dtype)


def deform_backward(tiles, offset_rows, disp, frac, weight, dy, rows, width, after, through):
    batch = tiles[0].shape[0]
    pixels = rows * width
    return call(
        functools.partial(deform_backward_body, batch=batch, rows=rows, width=width, deep=2 * rows),
        (*tiles, offset_rows, disp, frac, weight, dy),
        "hhhhhvvvhv",
        tuple(shaped(pixels, MID, dtype=f32 if t == 2 else bf16) for _ in range(batch) for t in range(5))
        + (shaped(3, 96, MID),),
        "v" * (5 * batch + 1),
        20,
        36,
        [
            VMEM((batch, 5 * pixels, MID), bf16),
            VMEM((batch, 5 * pixels, MID), f32),
            VMEM((3 * pixels, MID), bf16),
            VMEM((16 * width, 3 * pixels), f32),
            VMEM((16 * width, 3 * pixels), bf16),
            VMEM((4, 8, pixels), f32),
            VMEM(weight.shape, bf16),
            DMA((5,)),
            DMA,
        ],
        after,
        through,
    )


def taps_moving(m_ref, m_buf, sems):
    wide = 3 * MID
    return columns_moving(m_ref, m_buf, sems, wide)


def rim_moving(parts, rim_ref, sems):
    copies, at = [], 0
    for t, ref in enumerate(parts):
        copies.append(moving(ref, rim_ref.at[:, at : at + ref.shape[1], :], sems.at[t]))
        at += ref.shape[1]
    return copies


def conv_forward_body(
    above_ref, own_ref, below_ref, m_ref, mask_ref, y_ref, stat_ref, rim_ref, m_buf, rim_sems, sems,
    *, batch, rows, width
):
    pixels = rows * width
    coming = taps_moving(m_ref, m_buf, sems)
    for copy in rim_moving((above_ref, own_ref, below_ref), rim_ref, rim_sems):
        copy.wait()
    sums = [[None] * 3 for _ in range(batch)]
    for i in range(3):
        coming[i].wait()
        for b in range(batch):
            for j in range(3):
                k = i * 3 + j
                start = 2 * i * width
                term = dot(rim_ref[b, start : start + pixels, :], m_buf[:, k * MID : (k + 1) * MID], NT)
                sums[b][j] = term if i == 0 else sums[b][j] + term
    for b in range(batch):
        total = sums[b][1] + shift_rows(sums[b][0], 2, width) + shift_rows(sums[b][2], -2, width)
        y_ref[b * pixels : (b + 1) * pixels, :] = total
    y = y_ref[...]
    write_stats(stat_ref, y * mask_ref[:, 0:1], y)


def conv_forward(rim, weight, mask_wide, rows, width, devices):
    batch = rim[0].shape[0]
    n = batch * rows * width
    return call(
        functools.partial(conv_forward_body, batch=batch, rows=rows, width=width),
        (*rim, weight, mask_wide),
        "hhhhv",
        (shaped(n, MID), shaped(devices, 8, 128)),
        "vv",
        5,
        24,
        [VMEM((batch, (rows + 4) * width, MID), bf16), VMEM(weight.shape, bf16), DMA((3,)), DMA((3,))],
    )


def conv_backward_body(
    above_ref, own_ref, below_ref, m_ref, y_ref, par_ref, mask_ref, dt_ref, stat_ref,
    rim_ref, m_buf, rim_sems, sems, *, batch, rows, width
):
    pixels = rows * width
    coming = taps_moving(m_ref, m_buf, sems)
    for copy in rim_moving((above_ref, own_ref, below_ref), rim_ref, rim_sems):
        copy.wait()
    sums = [[None] * 3 for _ in range(batch)]
    for i in range(3):
        coming[i].wait()
        for b in range(batch):
            for j in range(3):
                k = i * 3 + j
                start = (4 - 2 * i) * width
                term = dot(rim_ref[b, start : start + pixels, :], m_buf[:, k * MID : (k + 1) * MID])
                sums[b][j] = term if i == 0 else sums[b][j] + term
    for b in range(batch):
        total = sums[b][1] + shift_rows(sums[b][0], -2, width) + shift_rows(sums[b][2], 2, width)
        dt_ref[b * pixels : (b + 1) * pixels, :] = total
    y = y_ref[...]
    dt = gelu_slope(normed(y, par_ref)) * (dt_ref[...] * mask_ref[:, 0:1])
    dt_ref[...] = dt
    write_stats(stat_ref, dt, normal_of(y, par_ref))


def conv_backward(rim, weight, y, par, mask_wide, rows, width, devices, after):
    batch = rim[0].shape[0]
    n = batch * rows * width
    return call(
        functools.partial(conv_backward_body, batch=batch, rows=rows, width=width),
        (*rim, weight, y, par, mask_wide),
        "hhhhvvv",
        (shaped(n, MID), shaped(devices, 8, 128)),
        "vv",
        6,
        24,
        [VMEM((batch, (rows + 4) * width, MID), bf16), VMEM(weight.shape, bf16), DMA((3,)), DMA((3,))],
        after,
    )


def conv_weight_body(
    dy_ref, above_ref, own_ref, below_ref, out_ref, rim_ref, dyt_ref, out_buf, rim_sems, sems,
    *, batch, rows, width
):
    pixels = rows * width
    coming = rim_moving((above_ref, own_ref, below_ref), rim_ref, rim_sems)
    dy = dy_ref[...].astype(f32)
    going = []
    for j in range(3):
        moved = shift_rows(dy, 2 * (j - 1), width) if j != 1 else dy
        dyt_ref[j] = moved.T.astype(bf16)
        if j == 0:
            for copy in coming:
                copy.wait()
        for i in range(3):
            part = slice((i * 3 + j) * MID, (i * 3 + j + 1) * MID)
            start = 2 * i * width
            total = None
            for b in range(batch):
                term = dot(dyt_ref[j, :, b * pixels : (b + 1) * pixels], rim_ref[b, start : start + pixels, :])
                total = term if total is None else total + term
            out_buf[:, part] = total.astype(bf16)
            going.append(moving(out_buf.at[:, part], out_ref.at[:, part], sems.at[i * 3 + j]))
    for copy in going:
        copy.wait()


def conv_weight_gradient(dy, rim, rows, width, after):
    batch = rim[0].shape[0]
    return call(
        functools.partial(conv_weight_body, batch=batch, rows=rows, width=width),
        (dy, *rim),
        "vhhh",
        (shaped(MID, 9 * MID, dtype=bf16),),
        "h",
        6,
        20,
        [
            VMEM((batch, (rows + 4) * width, MID), bf16),
            VMEM((3, MID, batch * rows * width), bf16),
            VMEM((MID, 9 * MID), bf16),
            DMA((3,)),
            DMA((9,)),
        ],
        after,
    )[0]


def columns_weight_body(dy_ref, cols_ref, out_ref, dyt_ref, cols_buf, out_buf, sems):
    coming = columns_moving(cols_ref, cols_buf, sems.at[0])
    dyt_ref[...] = dy_ref[...].astype(f32).T.astype(bf16)
    going = []
    for s, part in blocks(cols_ref.shape[1]):
        coming[s].wait()
        out_buf[:, part] = dot(dyt_ref[...], cols_buf[:, part]).astype(bf16)
        going.append(moving(out_buf.at[:, part], out_ref.at[:, part], sems.at[1, s]))
    for copy in going:
        copy.wait()


def columns_weight_gradient(dy, cols, through):
    n, wide = cols.shape
    return call(
        columns_weight_body,
        (dy, cols),
        "vh",
        (shaped(MID, wide, dtype=bf16),),
        "h",
        6,
        20,
        [VMEM((MID, n), bf16), VMEM((n, wide), bf16), VMEM((MID, wide), bf16), DMA((2, wide // STEP))],
        through=through,
    )


TILES = 2
EPSILON = 1e-05


def swap_with(values, axis, step):
    return lax.ppermute(values, axis, [(i, i ^ step) for i in range(lax.axis_size(axis))])


def from_behind(block, axis, distance):
    devices = range(lax.axis_size(axis))
    route = [(i - distance, i) for i in devices if i - distance in devices]
    return lax.ppermute(block, axis, route)


def ladder_sum(values, axis):
    step = 1
    while step < lax.axis_size(axis):
        got = swap_with(values.astype(bf16), axis, step)
        values = values + got.astype(f32)
        step *= 2
    return values


def to_everyone(spread, groups=None):
    return lax.all_to_all(spread, ("rows", "ch"), 0, 0, axis_index_groups=groups, tiled=True)


def small_total(spread):
    return jnp.sum(to_everyone(spread), axis=0).reshape(2, -1)


def wide_total(block):
    devices = lax.axis_size("rows") * lax.axis_size("ch")
    core = lax.axis_index("ch") % 2
    above, below = block.reshape(2, -1, 128)
    half = jnp.where(core == 0, above, below) + swap_with(jnp.where(core == 0, below, above), "ch", 1)
    groups = [[i * 2 + k for i in range(devices // 2)] for k in range(2)]
    half = jnp.broadcast_to(half[None], (devices // 2,) + half.shape)
    half = jnp.sum(to_everyone(half, groups), axis=0)
    other = swap_with(half, "ch", 1)
    whole = jnp.stack([jnp.where(core == 0, half, other), jnp.where(core == 0, other, half)])
    whole = whole.reshape(-1, 2, STEP)
    return whole[:, 0].reshape(-1), whole[:, 1].reshape(-1)


def forward_rows(sums, gain, shift, count):
    mean = sums[0] / count
    scale = lax.rsqrt(sums[1] / count - mean * mean + EPSILON)
    return jnp.stack([scale * gain, shift - mean * scale * gain, scale, -mean * scale])


def backward_rows(sums, par, count):
    rows = jnp.stack([par[0], par[0] * sums[0] / count, par[0] * sums[1] / count])
    return rows, jnp.stack([sums[1], sums[0]])


def gather_weight(weight):
    return lax.all_gather(weight.astype(bf16), "ch", axis=0, tiled=True)


def gather_weight_after(weight, *after):
    return lax.all_gather(cast_after(weight, *after), "ch", axis=0, tiled=True)


def gather_by_swaps(weight):
    ch = lax.axis_size("ch")
    came = None
    held = weight.astype(bf16)[None]
    step = ch // 2
    while step >= 1:
        got = swap_with(held, "ch", step)
        came = got if came is None else came
        odd = lax.axis_index("ch") // step % 2 == 1
        held = jnp.stack([jnp.where(odd, got, held), jnp.where(odd, held, got)], axis=1)
        held = held.reshape((-1,) + held.shape[2:])
        step //= 2
    return held.reshape((-1,) + weight.shape[1:]), came


def pick(values, bit):
    return lax.dynamic_index_in_dim(values, bit, 1, keepdims=False)


def scatter_ch(gradient):
    return lax.psum_scatter(gradient, "ch", scatter_dimension=0, tiled=True)


def split(total, axis, step):
    bit = lax.axis_index(axis) // step % 2
    pairs = total.reshape((total.shape[0] // 2, 2) + total.shape[1:])
    return swap_with(pick(pairs, 1 - bit), axis, step), pick(pairs, bit)


def added(pair):
    got, kept = pair
    return (got.astype(f32) + kept.astype(f32)).astype(bf16)


def rest_of(total, axis, step=1):
    while step < lax.axis_size(axis):
        total = added(split(total, axis, step))
        step *= 2
    return total


def by_owner(gradient, axis="ch"):
    count = lax.axis_size(axis)
    return gradient.reshape((count, gradient.shape[0] // count) + gradient.shape[1:])


def wide_enough(base):
    return base // lax.axis_size("rows") % 16 == 0


def first_step(parts, base):
    if wide_enough(base):
        send, keep = pack_split(parts, base, lax.axis_size("rows"))
        return swap_with(send, "rows", 1), keep
    laid = [jnp.concatenate([p[r : r + base] for r in range(0, p.shape[0], base)], axis=1) for p in parts]
    return split(by_owner(jnp.concatenate(laid, axis=1), "rows"), "rows", 1)


def next_step(got, kept, step, axis="rows"):
    send, keep = step_split(got, kept, axis, step)
    return swap_with(send, axis, step), keep


def last_steps(got, kept, step, axis="rows"):
    while step < lax.axis_size(axis):
        got, kept = next_step(got, kept, step, axis)
        step *= 2
    return step_sum(got, kept)


def gathered(share, cuts):
    step = lax.axis_size("rows") // 2
    while step > 1:
        share = join_step(swap_with(share, "rows", step), share, step)
        step //= 2
    return final_join(swap_with(share, "rows", 1), share, cuts)


def deep_rows(tile):
    odd = lax.axis_index("rows") % 2 == 1
    far_up = from_behind(tile, "rows", 2)
    far_down = from_behind(tile, "rows", -2)
    near = swap_with(tile, "rows", 1)
    other = swap_with(jnp.where(odd, far_up, far_down), "rows", 1)
    return far_up, jnp.where(odd, near, other), tile, jnp.where(odd, other, near), far_down


def near_rows(tile, width):
    size = 2 * width
    above = from_behind(tile[:, -size:], "rows", 1)
    below = from_behind(tile[:, :size], "rows", -1)
    return above, tile, below


def per_device(
    inputs,
    heights,
    displacements,
    reduce_one,
    reduce_gain_one,
    reduce_bias_one,
    offset_weight,
    deform_weight,
    deform_gain,
    deform_bias,
    expand_one,
    expand_gain_one,
    expand_bias_one,
    reduce_two,
    reduce_gain_two,
    reduce_bias_two,
    conv_weight,
    conv_gain,
    conv_bias,
    expand_two,
    expand_gain_two,
    expand_bias_two,
    cotangent,
):
    batch, rows, width, channels = inputs.shape
    pixels = rows * width
    n = batch * pixels
    own_heights = lax.dynamic_slice_in_dim(heights, lax.axis_index("ch") * batch, batch)
    rows_here = lax.axis_index("rows") * rows + jnp.arange(rows, dtype=jnp.int32)
    mask = (rows_here[None, :] < own_heights[:, None]).astype(f32)
    mask = jnp.broadcast_to(mask[:, :, None], (batch, rows, width)).reshape(n, 1)
    mask_wide = jnp.broadcast_to(mask, (n, 128))
    count = jnp.sum(heights).astype(f32) * width

    offset_rows = offset_weight.astype(bf16).reshape(3, 6, 3, 3, MID).transpose(2, 3, 0, 1, 4)
    offset_rows = jnp.pad(offset_rows, ((0, 0), (0, 0), (0, 1), (0, 2), (0, 0))).reshape(3, 96, MID)
    disp = jnp.pad(displacements.reshape(3, 6, batch, pixels), ((0, 0), (0, 2), (0, 0), (0, 0)))
    disp = disp.transpose(2, 0, 1, 3)

    reduce_full, came = gather_by_swaps(reduce_one)
    deform_full = gather_weight_after(deform_weight, came)
    expand_full, reduce_full_two, conv_full, expand_full_two = [
        gather_weight(w) for w in (expand_one, reduce_two, conv_weight, expand_two)
    ]

    devices = lax.axis_size("rows") * lax.axis_size("ch")
    acts = inputs.reshape(n, channels)
    acts_low, y_a, spread = product_forward(acts, mask_wide, reduce_full, devices)
    par_a = forward_rows(small_total(spread), reduce_gain_one, reduce_bias_one, count)
    hidden = (gelu(y_a * par_a[0] + par_a[1]) * mask).astype(bf16)
    near_tiles = deep_rows(hidden.reshape(batch, pixels, MID))
    columns, y_b, fraction, spread = deform_forward(
        near_tiles, offset_rows, disp, deform_full, mask_wide, rows, width, devices
    )
    par_b = forward_rows(small_total(spread), deform_gain, deform_bias, count)
    middle, y_c, block = expand_forward([y_b], par_b, mask_wide, expand_full)
    par_c = forward_rows(wide_total(block), expand_gain_one, expand_bias_one, count)

    first_low, y_d, spread = first_forward(y_c, par_c, acts, mask_wide, reduce_full_two, devices)
    par_d = forward_rows(small_total(spread), reduce_gain_two, reduce_bias_two, count)
    hidden_two = (gelu(y_d * par_d[0] + par_d[1]) * mask).astype(bf16)
    rimmed = near_rows(hidden_two.reshape(batch, pixels, MID), width)
    y_e, spread = conv_forward(rimmed, conv_full, mask_wide, rows, width, devices)
    par_e = forward_rows(small_total(spread), conv_gain, conv_bias, count)
    middle_two, y_f, block = expand_forward([y_e], par_e, mask_wide, expand_full_two)
    par_f = forward_rows(wide_total(block), expand_gain_two, expand_bias_two, count)

    output, dt_f, block = output_stage(y_f, par_f, first_low, cotangent.reshape(n, channels), mask_wide)
    back_f, sums_f = backward_rows(wide_total(block), par_f, count)
    dy_f, dt_e, spread = expand_backward(
        dt_f, y_f, par_f, back_f, mask_wide, expand_full_two, y_e, par_e, devices
    )
    expand_two_local = dot(dy_f, middle_two, TN).astype(bf16)
    expand_two_part = scatter_ch(expand_two_local)
    back_e, sums_e = backward_rows(small_total(spread), par_e, count)
    dy_e = norm_gradient(dt_e, y_e, par_e, back_e, mask).astype(bf16)
    dy_e_rim = near_rows(dy_e.reshape(batch, pixels, MID), width)
    conv_local = conv_weight_gradient(dy_e, rimmed, rows, width, (expand_two_local,))
    conv_part = scatter_ch(conv_local)
    dt_d, spread = conv_backward(
        dy_e_rim, conv_full, y_d, par_d, mask_wide, rows, width, devices, (conv_local,)
    )
    base = conv_part.shape[0]
    back_d, sums_d = backward_rows(small_total(spread), par_d, count)
    dy_d, dt_c, block = residual_backward(
        dt_d, y_d, par_d, back_d, mask_wide, reduce_full_two, dt_f, y_c, par_c, acts_low
    )
    reduce_two_local = dot(dy_d, first_low, TN).astype(bf16)

    back_c, sums_c = backward_rows(wide_total(block), par_c, count)
    red_two = split(by_owner(reduce_two_local), "ch", 1)
    dy_c, dt_b, spread, kept = expand_backward(
        dt_c, y_c, par_c, back_c, mask_wide, expand_full, y_b, par_b, devices, (red_two[1],)
    )
    red_two = next_step(red_two[0], kept, 2, "ch")
    expand_one_local = dot(dy_c, middle, TN).astype(bf16)
    exp_one = split(by_owner(expand_one_local), "ch", 1)
    back_b, sums_b = backward_rows(small_total(spread), par_b, count)
    dy_b = norm_gradient(dt_b, y_b, par_b, back_b, mask).astype(bf16)
    got_p, kept_p = first_step([conv_part, expand_two_part], base)
    deform_local, reduce_two_kept, expand_one_kept = columns_weight_gradient(
        dy_b, columns, (red_two[1], exp_one[1])
    )
    deform_part = scatter_ch(deform_local)
    reduce_two_part = last_steps(red_two[0], reduce_two_kept, 4, "ch")[0]
    exp_one = next_step(exp_one[0], expand_one_kept, 2, "ch")
    *tiles, offset_local, reduce_two_part, expand_one_kept, kept_p = deform_backward(
        near_tiles, offset_rows, disp, fraction, deform_full, dy_b, rows, width,
        (), (reduce_two_part, exp_one[1], kept_p),
    )
    odd = lax.axis_index("rows") % 2 == 1
    images = [tiles[t : t + 5] for t in range(0, 5 * batch, 5)]
    passed = [swap_with(jnp.where(odd, t[3], t[1]), "rows", 1) for t in images]
    got_p, kept_p = next_step(got_p, kept_p, 2)
    beyond = []
    for b in range(batch):
        pairs = [(t[1], t[3]) for t in images] if b == batch - 1 else []
        below, above, *partners, kept_p = return_step(images[b], passed[b], pairs, (kept_p,))
        beyond.append((from_behind(below, "rows", -2), from_behind(above, "rows", 2)))
    pieces = []
    for b in range(batch):
        pieces += [images[b][2], swap_with(partners[b], "rows", 1), *beyond[b]]
    expand_one_part = last_steps(exp_one[0], expand_one_kept, 4, "ch")[0]
    dt_a, spread, kept_p, expand_one_part = hidden_backward(
        pieces, y_a, par_a, mask_wide, devices, (kept_p, expand_one_part)
    )
    got_p, kept_p = next_step(got_p, kept_p, 4)
    got_q, kept_q = first_step([reduce_two_part, expand_one_part], base)
    back_a, sums_a = backward_rows(small_total(spread), par_a, count)
    dy_a, send_s, kept_s, kept_p, kept_q, offset_local, deform_part = last_gradient(
        dt_a, y_a, par_a, back_a, mask_wide, acts_low, lax.axis_size("ch"),
        (kept_p, kept_q, offset_local, deform_part),
    )
    got_s = swap_with(send_s, "ch", 1)
    got_r, kept_r = first_step([deform_part], base)
    input_grad, kept_s, kept_r = input_backward(dy_a, reduce_full, dt_c, (kept_s, kept_r))
    got_s, kept_s = next_step(got_s, kept_s, 2, "ch")
    offset_local = offset_local.reshape(3, 3, 4, 8, MID)[:, :, :3, :6]
    offset_local = offset_local.transpose(2, 3, 0, 1, 4).reshape(-1, MID)
    offset_part = ladder_sum(offset_local, "ch").astype(bf16)
    offset_part = jnp.pad(offset_part, ((0, -offset_part.shape[0] % base), (0, 0)))
    kept_q, kept_r, kept_p = gate(spread[0], (kept_s,), (kept_q, kept_r, kept_p))
    share_p = last_steps(got_p, kept_p, 8)
    share_q = last_steps(got_q, kept_q, 2)
    share_r = last_steps(got_r, kept_r, 2)
    reduce_one_part = last_steps(got_s, kept_s, 4, "ch")[0]
    got_s, kept_s = first_step([reduce_one_part, offset_part], base)
    share_q, share_r = gate(spread[0], (kept_s,), (share_q, share_r))
    conv_weight_grad, expand_two_grad = gathered(share_p, ((1, 9 * MID), (channels // MID, MID)))
    reduce_two_grad, expand_one_grad = gathered(share_q, ((1, channels), (channels // MID, MID)))
    (deform_weight_grad,) = gathered(share_r, ((1, 9 * MID),))
    reduce_one_grad, offset_grad = gathered(
        last_steps(got_s, kept_s, 2), ((1, channels), (offset_part.shape[0] // base, MID))
    )
    ends = owned((sums_a, sums_b, sums_c, sums_d, sums_e, sums_f), lax.axis_size("ch"))
    offset_weight_grad = offset_grad[:162].reshape(18, 9 * MID)
    reduce_gain_one_grad, reduce_bias_one_grad, deform_gain_grad, deform_bias_grad = ends[:4]
    expand_gain_one_grad, expand_bias_one_grad, reduce_gain_two_grad, reduce_bias_two_grad = ends[4:8]
    conv_gain_grad, conv_bias_grad, expand_gain_two_grad, expand_bias_two_grad = ends[8:]
    return (
        output.reshape(inputs.shape),
        input_grad.reshape(inputs.shape),
        reduce_one_grad,
        reduce_gain_one_grad,
        reduce_bias_one_grad,
        offset_weight_grad,
        deform_weight_grad,
        deform_gain_grad,
        deform_bias_grad,
        expand_one_grad,
        expand_gain_one_grad,
        expand_bias_one_grad,
        reduce_two_grad,
        reduce_gain_two_grad,
        reduce_bias_two_grad,
        conv_weight_grad,
        conv_gain_grad,
        conv_bias_grad,
        expand_two_grad,
        expand_gain_two_grad,
        expand_bias_two_grad,
    )


def solution(mesh):
    tiles = P("ch", "rows", None, None)
    owned = P("ch", None)
    block = (owned, P(), P())
    placed = (tiles, P(), P(None, "ch", "rows", None)) + block + (P(),) + 2 * block + 3 * block + (tiles,)
    grads = (owned, P("ch"), P("ch"))
    return jax.shard_map(
        per_device,
        mesh=mesh,
        in_specs=placed,
        out_specs=(tiles, tiles) + grads + (P(),) + 2 * grads + 3 * grads,
        check_vma=False,
    )
```

```python
import functools

import jax
import jax.numpy as jnp
from jax import lax
from jax.experimental import pallas as pl
from jax.experimental.pallas import tpu as pltpu
from jax.sharding import PartitionSpec as P

bf16 = jnp.bfloat16
f32 = jnp.float32
VMEM = pltpu.VMEM
HBM = pltpu.HBM
DMA = pltpu.SemaphoreType.DMA
MID = 512
STEP = 512
NT = (((1,), (1,)), ((), ()))
TN = (((0,), (0,)), ((), ()))
NN = (((1,), (0,)), ((), ()))
GELU_A = 0.7978845608028654
GELU_B = 0.044715


def dot(a, b, dims=NN):
    return lax.dot_general(a, b, dims, preferred_element_type=f32)


def shaped(*shape, dtype=f32):
    return jax.ShapeDtypeStruct(shape, dtype)


def without(body, n_in, n_order, n_out, n_through, token):
    first = n_in + n_order + n_through

    def inner(*refs):
        if token:
            refs[first + n_out + n_through][...] = jnp.zeros((8, 128), f32)
        body(*refs[:n_in], *refs[first : first + n_out], *refs[first + n_out + n_through + token :])

    return inner


def cost(us):
    return pl.CostEstimate(flops=int(us * 1.1e9), bytes_accessed=int(us * 2.2e6), transcendentals=0)


def call(body, operands, places, outs, out_places, us, limit, scratch=(), after=(), through=(), token=None):
    def spec(place):
        return pl.BlockSpec(memory_space=HBM if place == "h" else VMEM)

    def pinned(value, place):
        return pltpu.with_memory_space_constraint(value, HBM) if place == "h" else value

    def result(out, place):
        return HBM(out.shape, out.dtype) if place == "h" else out

    tokens = () if token is None else (token,)
    n_in, n_out, n_order = len(operands), len(outs), len(after) + len(tokens)
    return pl.pallas_call(
        without(body, n_in, n_order, n_out, len(through), len(tokens)),
        in_specs=[spec(p) for p in places] + [spec("h")] * len(after) + [spec("v")] * len(tokens)
        + [spec("h")] * len(through),
        out_specs=tuple(spec(p) for p in out_places) + (spec("h"),) * len(through)
        + (spec("v"),) * len(tokens),
        out_shape=tuple(result(o, p) for o, p in zip(outs, out_places))
        + tuple(HBM(v.shape, v.dtype) for v in through)
        + (shaped(8, 128),) * len(tokens),
        input_output_aliases={n_in + n_order + t: n_out + t for t in range(len(through))},
        scratch_shapes=list(scratch),
        compiler_params=pltpu.CompilerParams(vmem_limit_bytes=limit * 2**20),
        cost_estimate=cost(us),
    )(
        *[pinned(v, p) for v, p in zip(operands, places)],
        *[pinned(v, "h") for v in after],
        *tokens,
        *[pinned(v, "h") for v in through],
    )


def moving(source, target, sem):
    copy = pltpu.make_async_copy(source, target, sem)
    copy.start()
    return copy


def columns_moving(source, target, sems, wide=STEP):
    return [
        moving(source.at[:, s * wide : (s + 1) * wide], target.at[:, s * wide : (s + 1) * wide], sems.at[s])
        for s in range(source.shape[1] // wide)
    ]


def rows_moving(source, target, sems, tall=STEP):
    return [
        moving(source.at[s * tall : (s + 1) * tall], target.at[s * tall : (s + 1) * tall], sems.at[s])
        for s in range(source.shape[0] // tall)
    ]


def blocks(wide):
    return [(s, slice(s * STEP, (s + 1) * STEP)) for s in range(wide // STEP)]


def gelu(v):
    return 0.5 * v * (1.0 + jnp.tanh(GELU_A * (v + GELU_B * v * v * v)))


def gelu_slope(v):
    t = jnp.tanh(GELU_A * (v + GELU_B * v * v * v))
    return 0.5 * (1.0 + t) + 0.5 * v * (1.0 - t * t) * (GELU_A * (1.0 + 3.0 * GELU_B * v * v))


def normed(values, par_ref, part=slice(None)):
    return values * par_ref[0:1, part] + par_ref[1:2, part]


def normal_of(values, par_ref, part=slice(None)):
    return values * par_ref[2:3, part] + par_ref[3:4, part]


def norm_gradient(upstream, values, par_ref, back_ref, mask, part=slice(None)):
    normal = normal_of(values, par_ref, part)
    return upstream * back_ref[0:1, part] - mask * (back_ref[1:2, part] + normal * back_ref[2:3, part])


def sums_block(weighted, values):
    n = weighted.shape[1] // 128
    sums = (
        jnp.sum(weighted, axis=0, keepdims=True),
        jnp.sum(weighted * values, axis=0, keepdims=True),
    )
    return jnp.concatenate([v[:, c * 128 : c * 128 + 128] for v in sums for c in range(n)], axis=0)


def write_stats(stat_ref, weighted, values):
    stat_ref[...] = jnp.broadcast_to(sums_block(weighted, values)[None], stat_ref.shape)


def product_forward_body(x_ref, mask_ref, w_ref, low_ref, out_ref, stat_ref, x_buf, low_buf, sems):
    wide = x_ref.shape[1]
    coming = columns_moving(x_ref, x_buf, sems.at[0])
    total, going = None, []
    for s, part in blocks(wide):
        coming[s].wait()
        low_buf[:, part] = x_buf[:, part].astype(bf16)
        going.append(moving(low_buf.at[:, part], low_ref.at[:, part], sems.at[1, s]))
        term = dot(low_buf[:, part], w_ref[:, part], NT)
        total = term if total is None else total + term
    out_ref[...] = total
    write_stats(stat_ref, total * mask_ref[:, 0:1], total)
    for copy in going:
        copy.wait()


def product_forward(x, mask_wide, weight, devices):
    n, wide = x.shape
    return call(
        product_forward_body,
        (x, mask_wide, weight),
        "hvv",
        (shaped(n, wide, dtype=bf16), shaped(n, MID), shaped(devices, 8, 128)),
        "hvv",
        5,
        20,
        [VMEM((n, wide), f32), VMEM((n, wide), bf16), DMA((2, wide // STEP))],
    )


def expand_forward_body(*refs):
    *y_refs, par_ref, mask_ref, e_ref, mid_ref, out_ref, stat_ref, e_buf, out_buf, sems = refs
    coming = rows_moving(e_ref, e_buf, sems.at[0])
    mask = mask_ref[:, 0:1]
    at = 0
    for y_ref in y_refs:
        part = slice(at, at + y_ref.shape[0])
        mid_ref[part, :] = (gelu(normed(y_ref[...], par_ref)) * mask_ref[part, 0:1]).astype(bf16)
        at += y_ref.shape[0]
    going = []
    for s, part in blocks(e_ref.shape[0]):
        coming[s].wait()
        out = dot(mid_ref[...], e_buf[part, :], NT)
        out_buf[:, part] = out.astype(bf16)
        going.append(moving(out_buf.at[:, part], out_ref.at[:, part], sems.at[1, s]))
        stat_ref[s * 8 : s * 8 + 8, :] = sums_block(out * mask, out)
    for copy in going:
        copy.wait()


def expand_forward(y_parts, par, mask_wide, weight):
    n, wide = mask_wide.shape[0], weight.shape[0]
    return call(
        expand_forward_body,
        (*y_parts, par, mask_wide, weight),
        "v" * (len(y_parts) + 2) + "h",
        (shaped(n, MID, dtype=bf16), shaped(n, wide, dtype=bf16), shaped(wide // 64, 128)),
        "vhv",
        4,
        16,
        [VMEM(weight.shape, bf16), VMEM((n, wide), bf16), DMA((2, wide // STEP))],
    )


def first_forward_body(
    y_ref, par_ref, x_ref, mask_ref, w_ref, low_ref, out_ref, stat_ref,
    y_buf, x_buf, w_buf, low_buf, sems
):
    wide = x_ref.shape[1]
    coming_y = columns_moving(y_ref, y_buf, sems.at[0])
    coming_x = columns_moving(x_ref, x_buf, sems.at[1])
    coming_w = columns_moving(w_ref, w_buf, sems.at[2])
    mask = mask_ref[:, 0:1]
    total, going = None, []
    for s, part in blocks(wide):
        coming_y[s].wait()
        coming_x[s].wait()
        first = gelu(normed(y_buf[:, part].astype(f32), par_ref, part) + x_buf[:, part]) * mask
        low_buf[:, part] = first.astype(bf16)
        going.append(moving(low_buf.at[:, part], low_ref.at[:, part], sems.at[3, s]))
        coming_w[s].wait()
        term = dot(low_buf[:, part], w_buf[:, part], NT)
        total = term if total is None else total + term
    out_ref[...] = total
    write_stats(stat_ref, total * mask, total)
    for copy in going:
        copy.wait()


def first_forward(y, par, x, mask_wide, weight, devices):
    n, wide = y.shape
    return call(
        first_forward_body,
        (y, par, x, mask_wide, weight),
        "hvhvh",
        (shaped(n, wide, dtype=bf16), shaped(n, MID), shaped(devices, 8, 128)),
        "hvv",
        6,
        24,
        [
            VMEM((n, wide), bf16),
            VMEM((n, wide), f32),
            VMEM(weight.shape, bf16),
            VMEM((n, wide), bf16),
            DMA((4, wide // STEP)),
        ],
    )


def output_stage_body(
    y_ref, par_ref, first_ref, cot_ref, mask_ref, out_ref, dt_ref, stat_ref,
    y_buf, first_buf, cot_buf, out_buf, dt_buf, sems
):
    wide = y_ref.shape[1]
    coming_y = columns_moving(y_ref, y_buf, sems.at[0])
    coming_f = columns_moving(first_ref, first_buf, sems.at[1])
    coming_c = columns_moving(cot_ref, cot_buf, sems.at[2])
    mask = mask_ref[:, 0:1]
    going = []
    for s, part in blocks(wide):
        coming_y[s].wait()
        coming_f[s].wait()
        y = y_buf[:, part].astype(f32)
        pre = normed(y, par_ref, part) + first_buf[:, part].astype(f32)
        t = jnp.tanh(GELU_A * (pre + GELU_B * pre * pre * pre))
        out_buf[:, part] = 0.5 * pre * (1.0 + t) * mask
        going.append(moving(out_buf.at[:, part], out_ref.at[:, part], sems.at[3, s]))
        slope = 0.5 * (1.0 + t) + 0.5 * pre * (1.0 - t * t) * (GELU_A * (1.0 + 3.0 * GELU_B * pre * pre))
        coming_c[s].wait()
        dt = slope * (cot_buf[:, part] * mask)
        dt_buf[:, part] = dt.astype(bf16)
        going.append(moving(dt_buf.at[:, part], dt_ref.at[:, part], sems.at[4, s]))
        stat_ref[s * 8 : s * 8 + 8, :] = sums_block(dt, normal_of(y, par_ref, part))
    for copy in going:
        copy.wait()


def output_stage(y, par, first, cot, mask_wide):
    n, wide = y.shape
    return call(
        output_stage_body,
        (y, par, first, cot, mask_wide),
        "hvhhv",
        (shaped(n, wide), shaped(n, wide, dtype=bf16), shaped(wide // 64, 128)),
        "hhv",
        8,
        28,
        [
            VMEM((n, wide), bf16),
            VMEM((n, wide), bf16),
            VMEM((n, wide), f32),
            VMEM((n, wide), f32),
            VMEM((n, wide), bf16),
            DMA((5, wide // STEP)),
        ],
    )


def expand_backward_body(
    dt_ref, y_ref, par_ref, back_ref, mask_ref, e_ref, mid_y_ref, mid_par_ref,
    dy_ref, mid_dt_ref, stat_ref, dt_buf, y_buf, e_buf, dy_buf, sems
):
    wide = dt_ref.shape[1]
    coming_dt = columns_moving(dt_ref, dt_buf, sems.at[0])
    coming_y = columns_moving(y_ref, y_buf, sems.at[1])
    coming_e = rows_moving(e_ref, e_buf, sems.at[2])
    mask = mask_ref[:, 0:1]
    total, going = None, []
    for s, part in blocks(wide):
        coming_dt[s].wait()
        coming_y[s].wait()
        dt, y = dt_buf[:, part].astype(f32), y_buf[:, part].astype(f32)
        dy = norm_gradient(dt, y, par_ref, back_ref, mask, part).astype(bf16)
        dy_buf[:, part] = dy
        going.append(moving(dy_buf.at[:, part], dy_ref.at[:, part], sems.at[3, s]))
        coming_e[s].wait()
        term = dot(dy, e_buf[part, :])
        total = term if total is None else total + term
    y = mid_y_ref[...]
    dt = gelu_slope(normed(y, mid_par_ref)) * (total * mask)
    mid_dt_ref[...] = dt
    write_stats(stat_ref, dt, normal_of(y, mid_par_ref))
    for copy in going:
        copy.wait()


def expand_backward(dt, y, par, back, mask_wide, weight, mid_y, mid_par, devices, through=()):
    n, wide = y.shape
    return call(
        expand_backward_body,
        (dt, y, par, back, mask_wide, weight, mid_y, mid_par),
        "hhvvvhvv",
        (shaped(n, wide, dtype=bf16), shaped(n, MID), shaped(devices, 8, 128)),
        "hvv",
        5,
        24,
        [
            VMEM((n, wide), bf16),
            VMEM((n, wide), bf16),
            VMEM(weight.shape, bf16),
            VMEM((n, wide), bf16),
            DMA((4, wide // STEP)),
        ],
        through=through,
    )


def residual_backward_body(
    dt_ref, y_ref, par_ref, back_ref, mask_ref, w_ref, add_ref, wide_y_ref, wide_par_ref, x_ref,
    dy_ref, out_ref, stat_ref, w_buf, add_buf, y_buf, x_buf, out_buf, sems
):
    wide = x_ref.shape[1]
    coming = [
        columns_moving(source, target, sems.at[t])
        for t, (source, target) in enumerate(
            ((w_ref, w_buf), (add_ref, add_buf), (wide_y_ref, y_buf), (x_ref, x_buf))
        )
    ]
    mask = mask_ref[:, 0:1]
    dy_ref[...] = norm_gradient(dt_ref[...], y_ref[...], par_ref, back_ref, mask).astype(bf16)
    going = []
    for s, part in blocks(wide):
        for copies in coming:
            copies[s].wait()
        grad = add_buf[:, part].astype(f32) + dot(dy_ref[...], w_buf[:, part])
        y = y_buf[:, part].astype(f32)
        pre = normed(y, wide_par_ref, part) + x_buf[:, part].astype(f32)
        dt = gelu_slope(pre) * (grad * mask)
        out_buf[:, part] = dt.astype(bf16)
        going.append(moving(out_buf.at[:, part], out_ref.at[:, part], sems.at[4, s]))
        stat_ref[s * 8 : s * 8 + 8, :] = sums_block(dt, normal_of(y, wide_par_ref, part))
    for copy in going:
        copy.wait()


def residual_backward(dt, y, par, back, mask_wide, weight, add, wide_y, wide_par, x):
    n, wide = x.shape
    return call(
        residual_backward_body,
        (dt, y, par, back, mask_wide, weight, add, wide_y, wide_par, x),
        "vvvvvhhhvh",
        (shaped(n, MID, dtype=bf16), shaped(n, wide, dtype=bf16), shaped(wide // 64, 128)),
        "vhv",
        6,
        24,
        [VMEM(weight.shape, bf16)] + [VMEM((n, wide), bf16)] * 4 + [DMA((5, wide // STEP))],
    )


def input_backward_body(dy_ref, w_ref, add_ref, out_ref, w_buf, add_buf, out_buf, sems):
    coming_w = columns_moving(w_ref, w_buf, sems.at[0])
    coming_a = columns_moving(add_ref, add_buf, sems.at[1])
    going = []
    for s, part in blocks(w_ref.shape[1]):
        coming_w[s].wait()
        coming_a[s].wait()
        out_buf[:, part] = add_buf[:, part].astype(f32) + dot(dy_ref[...], w_buf[:, part])
        going.append(moving(out_buf.at[:, part], out_ref.at[:, part], sems.at[2, s]))
    for copy in going:
        copy.wait()


def input_backward(dy, weight, add, through):
    n, wide = add.shape
    return call(
        input_backward_body,
        (dy, weight, add),
        "vhh",
        (shaped(n, wide),),
        "h",
        5,
        20,
        [VMEM(weight.shape, bf16), VMEM((n, wide), bf16), VMEM((n, wide), f32), DMA((3, wide // STEP))],
        through=through,
    )


def hidden_backward_body(
    own_ref, near_ref, up_ref, down_ref, y_ref, par_ref, mask_ref, dt_ref, stat_ref
):
    batch, pixels, _ = own_ref.shape
    for b in range(batch):
        own, near, up, down = [ref[b].astype(f32) for ref in (own_ref, near_ref, up_ref, down_ref)]
        dt_ref[b * pixels : (b + 1) * pixels, :] = own + near + up + down
    grad = dt_ref[...]
    y = y_ref[...]
    dt = gelu_slope(normed(y, par_ref)) * (grad * mask_ref[:, 0:1])
    dt_ref[...] = dt
    write_stats(stat_ref, dt, normal_of(y, par_ref))


def hidden_backward(pieces, y, par, mask_wide, devices, through):
    n = y.shape[0]
    return call(
        hidden_backward_body,
        (*pieces, y, par, mask_wide),
        "v" * (len(pieces) + 3),
        (shaped(n, MID), shaped(devices, 8, 128)),
        "vv",
        3,
        16,
        through=through,
    )


def last_gradient_body(
    dt_ref, y_ref, par_ref, back_ref, mask_ref, acts_ref, dy_ref, send_ref, keep_ref,
    dyt_ref, acts_buf, out_buf, in_sems, out_sems
):
    coming = columns_moving(acts_ref, acts_buf, in_sems)
    dy = norm_gradient(dt_ref[...], y_ref[...], par_ref, back_ref, mask_ref[:, 0:1]).astype(bf16)
    dy_ref[...] = dy
    dyt_ref[...] = dy.astype(f32).T.astype(bf16)
    core = lax.axis_index("ch") % 2
    half, base = send_ref.shape[0], send_ref.shape[1]
    going = []
    for s, part in blocks(acts_ref.shape[1]):
        coming[s].wait()
        out_buf[:, part] = dot(dyt_ref[...], acts_buf[:, part]).astype(bf16)
        for q in range(half):
            for t, (out_ref, side) in enumerate(((send_ref, 1 - core), (keep_ref, core))):
                row = pl.multiple_of((2 * q + side) * base, 16)
                going.append(
                    moving(
                        out_buf.at[pl.ds(row, base), part], out_ref.at[q, :, part], out_sems.at[s, q, t]
                    )
                )
    for copy in going:
        copy.wait()


def last_gradient(dt, y, par, back, mask_wide, acts, ch, after, through):
    n, wide = acts.shape
    half = shaped(ch // 2, MID // ch, wide, dtype=bf16)
    return call(
        last_gradient_body,
        (dt, y, par, back, mask_wide, acts),
        "vvvvvh",
        (shaped(n, MID, dtype=bf16), half, half),
        "vhh",
        6,
        20,
        [
            VMEM((MID, n), bf16),
            VMEM((n, wide), bf16),
            VMEM((MID, wide), bf16),
            DMA((wide // STEP,)),
            DMA((wide // STEP, ch // 2, 2)),
        ],
        after=after,
        through=through,
    )


def cast_body(v_ref, out_ref):
    out_ref[...] = v_ref[...].astype(bf16)


def cast_after(values, *after):
    return call(cast_body, (values,), "v", (shaped(*values.shape, dtype=bf16),), "v", 2, 12, after=after)[0]


def pack_body(*refs, count, bit_axis, rows):
    part_refs, (send_ref, keep_ref), refs = refs[:count], refs[count : count + 2], refs[count + 2 :]
    buffers, (in_sem, out_sem) = refs[:count], refs[count:]
    coming = [moving(ref, buf, in_sem.at[t]) for t, (ref, buf) in enumerate(zip(part_refs, buffers))]
    bit = lax.axis_index(bit_axis) % 2
    tall = send_ref.shape[1]
    base = rows * tall
    going, at = [], 0
    for copy, buf in zip(coming, buffers):
        copy.wait()
        wide = buf.shape[1]
        for block in range(buf.shape[0] // base):
            for pair in range(rows // 2):
                for out_ref, side in ((send_ref, 1 - bit), (keep_ref, bit)):
                    row = pl.multiple_of(block * base + (2 * pair + side) * tall, 16)
                    going.append(
                        moving(
                            buf.at[pl.ds(row, tall), :],
                            out_ref.at[pair, :, at : at + wide],
                            out_sem.at[len(going)],
                        )
                    )
            at += wide
    for copy in going:
        copy.wait()


def pack_split(parts, base, rows, token=None):
    count = len(parts)
    blocks_in = sum(p.shape[0] // base for p in parts)
    wide = sum(p.shape[0] // base * p.shape[1] for p in parts)
    half = shaped(rows // 2, base // rows, wide, dtype=bf16)
    return call(
        functools.partial(pack_body, count=count, bit_axis="rows", rows=rows),
        tuple(parts),
        "h" * count,
        (half, half),
        "hh",
        3,
        16,
        [VMEM(p.shape, bf16) for p in parts] + [DMA((count,)), DMA((blocks_in * rows,))],
        token=token,
    )


def step_body(got_ref, kept_ref, send_ref, keep_ref, sum_ref, *, axis, step):
    bit = lax.axis_index(axis) // step % 2
    sum_ref[...] = (got_ref[...].astype(f32) + kept_ref[...].astype(f32)).astype(bf16)
    for pair in range(send_ref.shape[0]):
        send_ref[pair] = sum_ref[2 * pair + 1 - bit]
        keep_ref[pair] = sum_ref[2 * pair + bit]


def step_split(got, kept, axis, step, token=None):
    half = shaped(got.shape[0] // 2, *got.shape[1:], dtype=bf16)
    return call(
        functools.partial(step_body, axis=axis, step=step),
        (got, kept),
        "vv",
        (half, half),
        "vv",
        2,
        12,
        [VMEM(got.shape, bf16)],
        token=token,
    )


def sum_body(got_ref, kept_ref, sum_ref):
    sum_ref[...] = (got_ref[...].astype(f32) + kept_ref[...].astype(f32)).astype(bf16)


def step_sum(got, kept, token=None):
    return call(sum_body, (got, kept), "vv", (shaped(*got.shape, dtype=bf16),), "v", 1, 12, token=token)


def join_body(got_ref, kept_ref, out_ref, *, step):
    bit = lax.axis_index("rows") // step % 2
    for a in range(got_ref.shape[0]):
        out_ref[2 * a + bit] = kept_ref[a]
        out_ref[2 * a + 1 - bit] = got_ref[a]


def join_step(got, kept, step, token=None):
    m, r, wide = got.shape
    return call(
        functools.partial(join_body, step=step),
        (got, kept),
        "vv",
        (shaped(2 * m, r, wide, dtype=bf16),),
        "v",
        1,
        12,
        token=token,
    )


def final_body(got_ref, kept_ref, *refs, cuts):
    out_refs, refs = refs[: len(cuts)], refs[len(cuts) :]
    buffers, sems = refs[: len(cuts)], refs[len(cuts)]
    bit = lax.axis_index("rows") % 2
    going, at = [], 0
    for out_ref, buf, (count, wide) in zip(out_refs, buffers, cuts):
        for k in range(count):
            part = slice(at, at + wide)
            for a in range(got_ref.shape[0]):
                buf[k, 2 * a + bit] = kept_ref[a, :, part].astype(f32)
                buf[k, 2 * a + 1 - bit] = got_ref[a, :, part].astype(f32)
            going.append(moving(buf.at[k], out_ref.at[k], sems.at[len(going)]))
            at += wide
    for copy in going:
        copy.wait()


def final_join(got, kept, cuts):
    m, r, _ = got.shape
    outs = [shaped(count, 2 * m, r, wide) for count, wide in cuts]
    outs = call(
        functools.partial(final_body, cuts=cuts),
        (got, kept),
        "vv",
        outs,
        "h" * len(outs),
        2,
        20,
        [VMEM(o.shape, f32) for o in outs] + [DMA((sum(count for count, _ in cuts),))],
    )
    return [o.reshape(-1, o.shape[3]) for o in outs]


def owned_body(*refs):
    n = len(refs) // 3
    for k in range(n):
        size = refs[n + 2 * k].shape[1]
        start = lax.axis_index("ch") * size
        turned = pltpu.roll(refs[k][...], refs[k].shape[1] - start, 1)
        refs[n + 2 * k][...] = turned[0:1, :size]
        refs[n + 2 * k + 1][...] = turned[1:2, :size]


def owned(sums, ch):
    outs = [shaped(1, s.shape[1] // ch) for s in sums for _ in range(2)]
    outs = call(owned_body, tuple(sums), "v" * len(sums), outs, "v" * len(outs), 1, 12)
    return [o.reshape(-1) for o in outs]


def return_body(far_up_ref, up_ref, down_ref, far_down_ref, got_ref, below_ref, above_ref, partner_ref):
    odd = lax.axis_index("rows") % 2 == 1

    @pl.when(odd)
    def _():
        below_ref[...] = (far_up_ref[...].astype(f32) + got_ref[...].astype(f32)).astype(bf16)
        above_ref[...] = far_down_ref[...]
        partner_ref[...] = up_ref[...]

    @pl.when(jnp.logical_not(odd))
    def _():
        below_ref[...] = far_up_ref[...]
        above_ref[...] = (far_down_ref[...].astype(f32) + got_ref[...].astype(f32)).astype(bf16)
        partner_ref[...] = down_ref[...]


def return_step(far_up, up, down, far_down, got, through):
    piece = shaped(*got.shape, dtype=bf16)
    return call(
        return_body,
        (far_up, up, down, far_down, got),
        "vvvvv",
        (piece, piece, piece),
        "vvv",
        2,
        16,
        through=through,
    )


def shift_lanes(values, by, width):
    place = lax.broadcasted_iota(jnp.int32, values.shape, values.ndim - 1) % width
    moved = pltpu.roll(values, by % values.shape[-1], values.ndim - 1)
    return jnp.where((place >= by) & (place < width + by), moved, 0.0)


def shift_rows(values, by, width):
    place = lax.broadcasted_iota(jnp.int32, values.shape, 0) % width
    moved = pltpu.roll(values, by % values.shape[0], 0)
    return jnp.where((place >= by) & (place < width + by), moved, 0.0)


def offset_fraction(ext_ref, ow_ref, b, base, pixels, width):
    u = None
    for i in range(3):
        start = (base + 2 * i) * width
        term = dot(ow_ref[i], ext_ref[b, start : start + pixels, :], NT)
        u = term if u is None else u + term
    total = u[32:64]
    total = total + shift_lanes(u[0:32], 2, width) + shift_lanes(u[64:96], -2, width)
    return 1.0 / (1.0 + jnp.exp(-total))


def deform_forward_body(*refs, batch, rows, width, deep):
    tile_refs, refs = refs[:5], refs[5:]
    ow_ref, disp_ref, m_ref, mask_ref, cols_out_ref, y_ref, frac_ref, stat_ref = refs[:8]
    ext_ref, par_ref, s_ref, cols_ref, m_buf, tile_sems, sems = refs[8:]
    pixels = rows * width
    coming = [
        moving(ref, ext_ref.at[:, t * pixels : (t + 1) * pixels, :], tile_sems.at[t])
        for t, ref in enumerate(tile_refs)
    ]
    coming_m = moving(m_ref, m_buf, sems.at[0])
    for copy in coming:
        copy.wait()
    lane = lax.broadcasted_iota(jnp.int32, (32, 128), 1)
    column = lane % width
    upper = lane // width

    def image(b, carry):
        frac = offset_fraction(ext_ref, ow_ref, b, deep - 2, pixels, width)
        for i in range(4):
            frac_ref[b, i] = frac[i * 8 : i * 8 + 8]
        pix = lax.broadcasted_iota(jnp.int32, (1, pixels), 1)
        row_at, col_at = pix // width, pix % width
        tops, lefts, ys, xs = [], [], [], []
        for k in range(9):
            i, j = k // 3, k % 3
            tops.append(row_at + disp_ref[b, i, 2 * j : 2 * j + 1, :] + (deep - 2))
            lefts.append(col_at + 2 * (j - 1) + disp_ref[b, i, 2 * j + 1 : 2 * j + 2, :])
            at = i * 8 + 2 * j
            ys.append(frac[at : at + 1])
            xs.append(frac[at + 1 : at + 2])
        blank = jnp.zeros((23, pixels), f32)
        par = jnp.concatenate(
            [jnp.concatenate(g, axis=0).astype(f32) if g is not None else blank
             for g in (tops, None, lefts, None, ys, None, xs, None)], axis=0)
        par_ref[...] = par.T

        def row_of_taps(i, carry):
            for j in range(3):
                k = i * 3 + j
                for c in range(pixels // 32):
                    p = pltpu.roll(par_ref[c * 32 : c * 32 + 32, :], 128 - k, 1)
                    wide = (32, 128)
                    top = jnp.broadcast_to(p[:, 0:1], wide).astype(jnp.int32) - upper
                    left = jnp.broadcast_to(p[:, 32:33], wide).astype(jnp.int32)
                    fy = jnp.broadcast_to(p[:, 64:65], wide)
                    fx = jnp.broadcast_to(p[:, 96:97], wide)
                    cw = jnp.where(column == left, 1.0 - fx, jnp.where(column == left + 1, fx, 0.0))
                    ca, cb = (1.0 - fy) * cw, fy * cw
                    for q in range(8):
                        s = jnp.where(top == 2 * q, ca, jnp.where(top == 2 * q - 1, cb, 0.0))
                        s_ref[j * pixels + c * 32 : j * pixels + c * 32 + 32, q * 128 : q * 128 + 128] = s.astype(bf16)
            start = pl.multiple_of(i * 2 * width, 128)
            window = ext_ref[b, pl.ds(start, 16 * width), :]
            for j in range(3):
                got = dot(s_ref[j * pixels : (j + 1) * pixels, :], window).astype(bf16)
                cols_ref[pl.ds(pl.multiple_of(b * pixels, pixels), pixels), pl.ds(pl.multiple_of((i * 3 + j) * MID, MID), MID)] = got
            return carry

        return lax.fori_loop(0, 3, row_of_taps, carry)

    lax.fori_loop(0, batch, image, 0)
    going = moving(cols_ref, cols_out_ref, sems.at[1])
    coming_m.wait()
    y = dot(cols_ref[...], m_buf[...], NT)
    y_ref[...] = y
    write_stats(stat_ref, y * mask_ref[:, 0:1], y)
    going.wait()


def deform_forward(tiles, offset_rows, disp, weight, mask_wide, rows, width, devices):
    batch = tiles[0].shape[0]
    pixels = rows * width
    n = batch * pixels
    return call(
        functools.partial(deform_forward_body, batch=batch, rows=rows, width=width, deep=2 * rows),
        (*tiles, offset_rows, disp, weight, mask_wide),
        "hhhhhvvhv",
        (
            shaped(n, 9 * MID, dtype=bf16),
            shaped(n, MID),
            shaped(batch, 4, 8, pixels),
            shaped(devices, 8, 128),
        ),
        "hvvv",
        15,
        30,
        [
            VMEM((batch, 5 * pixels, MID), bf16),
            VMEM((pixels, 128), f32),
            VMEM((3 * pixels, 16 * width), bf16),
            VMEM((n, 9 * MID), bf16),
            VMEM(weight.shape, bf16),
            DMA((5,)),
            DMA((2,)),
        ],
    )


def deform_backward_body(*refs, batch, rows, width, deep):
    tile_refs, refs = refs[:5], refs[5:]
    (ow_ref, disp_ref, frac_ref, m_ref, dy_ref), refs = refs[:5], refs[5:]
    out_refs, refs = refs[:5], refs[5:]
    dow_ref, ext_ref, dext_ref, dc_ref, g_ref, st_ref, df_ref, m_buf, tile_sems, m_sem = refs
    pixels = rows * width
    coming = [
        moving(ref, ext_ref.at[:, t * pixels : (t + 1) * pixels, :], tile_sems.at[t])
        for t, ref in enumerate(tile_refs)
    ]
    coming_m = moving(m_ref, m_buf, m_sem)
    window = 16 * width
    dow_ref[...] = jnp.zeros_like(dow_ref)
    dext_ref[...] = jnp.zeros_like(dext_ref)
    for copy in coming:
        copy.wait()
    coming_m.wait()

    def image(b, carry):
        at = pl.multiple_of(b * pixels, pixels)

        def row_of_taps(i, carry):
            dy = dy_ref[pl.ds(at, pixels), :]
            for j in range(3):
                m = m_buf[:, pl.ds(pl.multiple_of((i * 3 + j) * MID, MID), MID)]
                dc_ref[j * pixels : (j + 1) * pixels, :] = dot(dy, m).astype(bf16)
            start = pl.multiple_of(i * 2 * width, 128)
            g_ref[...] = dot(ext_ref[b, pl.ds(start, window), :], dc_ref[...], NT)
            place = lax.broadcasted_iota(jnp.int32, (width, 128), 0)
            for j in range(3):
                for h in range(pixels // 128):
                    lanes = slice(h * 128, h * 128 + 128)
                    at_l = slice(j * pixels + h * 128, j * pixels + h * 128 + 128)
                    pix = lax.broadcasted_iota(jnp.int32, (1, 128), 1) + h * 128
                    by_y, by_x = slice(2 * j, 2 * j + 1), slice(2 * j + 1, 2 * j + 2)
                    top = pix // width + disp_ref[b, i, by_y, lanes] + (deep - 2)
                    left = pix % width + 2 * (j - 1) + disp_ref[b, i, by_x, lanes]
                    fy = frac_ref[b, i, by_y, lanes]
                    fx = frac_ref[b, i, by_x, lanes]
                    here, after = place == left, place == left + 1
                    cw = jnp.where(here, 1.0 - fx, jnp.where(after, fx, 0.0))
                    ca, cb = (1.0 - fy) * cw, fy * cw
                    low_sum = jnp.zeros((width, 128), f32)
                    high_sum = jnp.zeros((width, 128), f32)
                    for r in range(16):
                        part = slice(r * width, r * width + width)
                        g = g_ref[part, at_l]
                        m0, m1 = top == r, top == r - 1
                        low_sum = low_sum + jnp.where(m0, g, 0.0)
                        high_sum = high_sum + jnp.where(m1, g, 0.0)
                        st_ref[part, at_l] = jnp.where(m0, ca, jnp.where(m1, cb, 0.0)).astype(bf16)
                    d_fy = jnp.sum((high_sum - low_sum) * cw, axis=0, keepdims=True)
                    mixed = (1.0 - fy) * low_sum + fy * high_sum
                    d_fx = jnp.sum(
                        jnp.where(after, mixed, 0.0) - jnp.where(here, mixed, 0.0), axis=0, keepdims=True)
                    df_ref[i, by_y, lanes] = d_fy * fy * (1.0 - fy)
                    df_ref[i, by_x, lanes] = d_fx * fx * (1.0 - fx)
            dext_ref[b, pl.ds(start, window), :] += dot(st_ref[...], dc_ref[...])
            return carry

        df_ref[...] = jnp.zeros_like(df_ref)
        carry = lax.fori_loop(0, 3, row_of_taps, carry)
        d_off = df_ref[...].reshape(32, pixels).astype(bf16).astype(f32)
        stacked = jnp.concatenate(
            [shift_lanes(d_off, -2, width), d_off, shift_lanes(d_off, 2, width)], axis=0)
        across = jnp.concatenate([stacked, jnp.zeros((32, pixels), f32)], axis=0).T.astype(bf16)
        stacked = stacked.astype(bf16)
        for i in range(3):
            first = (deep - 2 + 2 * i) * width
            part = slice(first, first + pixels)
            dow_ref[i] += dot(stacked, ext_ref[b, part, :])
            dext_ref[b, part, :] += dot(across[:, :96], ow_ref[i])
        return carry

    lax.fori_loop(0, batch, image, 0)
    for t, ref in enumerate(out_refs):
        ref[...] = dext_ref[:, t * pixels : (t + 1) * pixels, :].astype(ref.dtype)


def deform_backward(tiles, offset_rows, disp, frac, weight, dy, rows, width, after, through):
    batch = tiles[0].shape[0]
    pixels = rows * width
    return call(
        functools.partial(deform_backward_body, batch=batch, rows=rows, width=width, deep=2 * rows),
        (*tiles, offset_rows, disp, frac, weight, dy),
        "hhhhhvvvhv",
        tuple(shaped(batch, pixels, MID, dtype=f32 if t == 2 else bf16) for t in range(5))
        + (shaped(3, 96, MID),),
        "vvvvvv",
        20,
        36,
        [
            VMEM((batch, 5 * pixels, MID), bf16),
            VMEM((batch, 5 * pixels, MID), f32),
            VMEM((3 * pixels, MID), bf16),
            VMEM((16 * width, 3 * pixels), f32),
            VMEM((16 * width, 3 * pixels), bf16),
            VMEM((4, 8, pixels), f32),
            VMEM(weight.shape, bf16),
            DMA((5,)),
            DMA,
        ],
        after,
        through,
    )


def taps_moving(m_ref, m_buf, sems):
    wide = 3 * MID
    return columns_moving(m_ref, m_buf, sems, wide)


def rim_moving(parts, rim_ref, sems):
    copies, at = [], 0
    for t, ref in enumerate(parts):
        copies.append(moving(ref, rim_ref.at[:, at : at + ref.shape[1], :], sems.at[t]))
        at += ref.shape[1]
    return copies


def conv_forward_body(
    above_ref, own_ref, below_ref, m_ref, mask_ref, y_ref, stat_ref, rim_ref, m_buf, rim_sems, sems,
    *, batch, rows, width
):
    pixels = rows * width
    coming = taps_moving(m_ref, m_buf, sems)
    for copy in rim_moving((above_ref, own_ref, below_ref), rim_ref, rim_sems):
        copy.wait()
    sums = [[None] * 3 for _ in range(batch)]
    for i in range(3):
        coming[i].wait()
        for b in range(batch):
            for j in range(3):
                k = i * 3 + j
                start = 2 * i * width
                term = dot(rim_ref[b, start : start + pixels, :], m_buf[:, k * MID : (k + 1) * MID], NT)
                sums[b][j] = term if i == 0 else sums[b][j] + term
    for b in range(batch):
        total = sums[b][1] + shift_rows(sums[b][0], 2, width) + shift_rows(sums[b][2], -2, width)
        y_ref[b * pixels : (b + 1) * pixels, :] = total
    y = y_ref[...]
    write_stats(stat_ref, y * mask_ref[:, 0:1], y)


def conv_forward(rim, weight, mask_wide, rows, width, devices):
    batch = rim[0].shape[0]
    n = batch * rows * width
    return call(
        functools.partial(conv_forward_body, batch=batch, rows=rows, width=width),
        (*rim, weight, mask_wide),
        "hhhhv",
        (shaped(n, MID), shaped(devices, 8, 128)),
        "vv",
        5,
        24,
        [VMEM((batch, (rows + 4) * width, MID), bf16), VMEM(weight.shape, bf16), DMA((3,)), DMA((3,))],
    )


def conv_backward_body(
    above_ref, own_ref, below_ref, m_ref, y_ref, par_ref, mask_ref, dt_ref, stat_ref,
    rim_ref, m_buf, rim_sems, sems, *, batch, rows, width
):
    pixels = rows * width
    coming = taps_moving(m_ref, m_buf, sems)
    for copy in rim_moving((above_ref, own_ref, below_ref), rim_ref, rim_sems):
        copy.wait()
    sums = [[None] * 3 for _ in range(batch)]
    for i in range(3):
        coming[i].wait()
        for b in range(batch):
            for j in range(3):
                k = i * 3 + j
                start = (4 - 2 * i) * width
                term = dot(rim_ref[b, start : start + pixels, :], m_buf[:, k * MID : (k + 1) * MID])
                sums[b][j] = term if i == 0 else sums[b][j] + term
    for b in range(batch):
        total = sums[b][1] + shift_rows(sums[b][0], -2, width) + shift_rows(sums[b][2], 2, width)
        dt_ref[b * pixels : (b + 1) * pixels, :] = total
    y = y_ref[...]
    dt = gelu_slope(normed(y, par_ref)) * (dt_ref[...] * mask_ref[:, 0:1])
    dt_ref[...] = dt
    write_stats(stat_ref, dt, normal_of(y, par_ref))


def conv_backward(rim, weight, y, par, mask_wide, rows, width, devices, after):
    batch = rim[0].shape[0]
    n = batch * rows * width
    return call(
        functools.partial(conv_backward_body, batch=batch, rows=rows, width=width),
        (*rim, weight, y, par, mask_wide),
        "hhhhvvv",
        (shaped(n, MID), shaped(devices, 8, 128)),
        "vv",
        6,
        24,
        [VMEM((batch, (rows + 4) * width, MID), bf16), VMEM(weight.shape, bf16), DMA((3,)), DMA((3,))],
        after,
    )


def conv_weight_body(
    dy_ref, above_ref, own_ref, below_ref, out_ref, rim_ref, dyt_ref, out_buf, rim_sems, sems,
    *, batch, rows, width
):
    pixels = rows * width
    coming = rim_moving((above_ref, own_ref, below_ref), rim_ref, rim_sems)
    dy = dy_ref[...].astype(f32)
    going = []
    for j in range(3):
        moved = shift_rows(dy, 2 * (j - 1), width) if j != 1 else dy
        dyt_ref[j] = moved.T.astype(bf16)
        if j == 0:
            for copy in coming:
                copy.wait()
        for i in range(3):
            part = slice((i * 3 + j) * MID, (i * 3 + j + 1) * MID)
            start = 2 * i * width
            total = None
            for b in range(batch):
                term = dot(dyt_ref[j, :, b * pixels : (b + 1) * pixels], rim_ref[b, start : start + pixels, :])
                total = term if total is None else total + term
            out_buf[:, part] = total.astype(bf16)
            going.append(moving(out_buf.at[:, part], out_ref.at[:, part], sems.at[i * 3 + j]))
    for copy in going:
        copy.wait()


def conv_weight_gradient(dy, rim, rows, width, after):
    batch = rim[0].shape[0]
    return call(
        functools.partial(conv_weight_body, batch=batch, rows=rows, width=width),
        (dy, *rim),
        "vhhh",
        (shaped(MID, 9 * MID, dtype=bf16),),
        "h",
        6,
        20,
        [
            VMEM((batch, (rows + 4) * width, MID), bf16),
            VMEM((3, MID, batch * rows * width), bf16),
            VMEM((MID, 9 * MID), bf16),
            DMA((3,)),
            DMA((9,)),
        ],
        after,
    )[0]


def columns_weight_body(dy_ref, cols_ref, out_ref, dyt_ref, cols_buf, out_buf, sems):
    coming = columns_moving(cols_ref, cols_buf, sems.at[0])
    dyt_ref[...] = dy_ref[...].astype(f32).T.astype(bf16)
    going = []
    for s, part in blocks(cols_ref.shape[1]):
        coming[s].wait()
        out_buf[:, part] = dot(dyt_ref[...], cols_buf[:, part]).astype(bf16)
        going.append(moving(out_buf.at[:, part], out_ref.at[:, part], sems.at[1, s]))
    for copy in going:
        copy.wait()


def columns_weight_gradient(dy, cols, through):
    n, wide = cols.shape
    return call(
        columns_weight_body,
        (dy, cols),
        "vh",
        (shaped(MID, wide, dtype=bf16),),
        "h",
        6,
        20,
        [VMEM((MID, n), bf16), VMEM((n, wide), bf16), VMEM((MID, wide), bf16), DMA((2, wide // STEP))],
        through=through,
    )


TILES = 2
EPSILON = 1e-05


def swap_with(values, axis, step):
    return lax.ppermute(values, axis, [(i, i ^ step) for i in range(lax.axis_size(axis))])


def from_behind(block, axis, distance):
    devices = range(lax.axis_size(axis))
    route = [(i - distance, i) for i in devices if i - distance in devices]
    return lax.ppermute(block, axis, route)


def ladder_sum(values, axis):
    step = 1
    while step < lax.axis_size(axis):
        got = swap_with(values.astype(bf16), axis, step)
        values = values + got.astype(f32)
        step *= 2
    return values


def to_everyone(spread, groups=None):
    return lax.all_to_all(spread, ("rows", "ch"), 0, 0, axis_index_groups=groups, tiled=True)


def small_total(spread):
    return jnp.sum(to_everyone(spread), axis=0).reshape(2, -1)


def wide_total(block):
    devices = lax.axis_size("rows") * lax.axis_size("ch")
    core = lax.axis_index("ch") % 2
    above, below = block.reshape(2, -1, 128)
    half = jnp.where(core == 0, above, below) + swap_with(jnp.where(core == 0, below, above), "ch", 1)
    groups = [[i * 2 + k for i in range(devices // 2)] for k in range(2)]
    half = jnp.broadcast_to(half[None], (devices // 2,) + half.shape)
    half = jnp.sum(to_everyone(half, groups), axis=0)
    other = swap_with(half, "ch", 1)
    whole = jnp.stack([jnp.where(core == 0, half, other), jnp.where(core == 0, other, half)])
    whole = whole.reshape(-1, 2, STEP)
    return whole[:, 0].reshape(-1), whole[:, 1].reshape(-1)


def forward_rows(sums, gain, shift, count):
    mean = sums[0] / count
    scale = lax.rsqrt(sums[1] / count - mean * mean + EPSILON)
    return jnp.stack([scale * gain, shift - mean * scale * gain, scale, -mean * scale])


def backward_rows(sums, par, count):
    rows = jnp.stack([par[0], par[0] * sums[0] / count, par[0] * sums[1] / count])
    return rows, jnp.stack([sums[1], sums[0]])


def gather_weight(weight):
    return lax.all_gather(weight.astype(bf16), "ch", axis=0, tiled=True)


def gather_weight_after(weight, *after):
    return lax.all_gather(cast_after(weight, *after), "ch", axis=0, tiled=True)


def gather_by_swaps(weight):
    ch = lax.axis_size("ch")
    came = None
    held = weight.astype(bf16)[None]
    step = ch // 2
    while step >= 1:
        got = swap_with(held, "ch", step)
        came = got if came is None else came
        odd = lax.axis_index("ch") // step % 2 == 1
        held = jnp.stack([jnp.where(odd, got, held), jnp.where(odd, held, got)], axis=1)
        held = held.reshape((-1,) + held.shape[2:])
        step //= 2
    return held.reshape((-1,) + weight.shape[1:]), came


def pick(values, bit):
    return lax.dynamic_index_in_dim(values, bit, 1, keepdims=False)


def scatter_ch(gradient):
    return lax.psum_scatter(gradient, "ch", scatter_dimension=0, tiled=True)


def split(total, axis, step):
    bit = lax.axis_index(axis) // step % 2
    pairs = total.reshape((total.shape[0] // 2, 2) + total.shape[1:])
    return swap_with(pick(pairs, 1 - bit), axis, step), pick(pairs, bit)


def added(pair):
    got, kept = pair
    return (got.astype(f32) + kept.astype(f32)).astype(bf16)


def rest_of(total, axis, step=1):
    while step < lax.axis_size(axis):
        total = added(split(total, axis, step))
        step *= 2
    return total


def by_owner(gradient, axis="ch"):
    count = lax.axis_size(axis)
    return gradient.reshape((count, gradient.shape[0] // count) + gradient.shape[1:])


def wide_enough(base):
    return base // lax.axis_size("rows") % 16 == 0


def first_step(parts, base, token=None):
    if wide_enough(base):
        send, keep, *token = pack_split(parts, base, lax.axis_size("rows"), token)
        return (swap_with(send, "rows", 1), keep, *token)
    laid = [jnp.concatenate([p[r : r + base] for r in range(0, p.shape[0], base)], axis=1) for p in parts]
    pair = split(by_owner(jnp.concatenate(laid, axis=1), "rows"), "rows", 1)
    return pair if token is None else (*pair, token)


def next_step(got, kept, step, axis="rows", token=None):
    send, keep, *token = step_split(got, kept, axis, step, token)
    return (swap_with(send, axis, step), keep, *token)


def last_steps(got, kept, step, axis):
    while step < lax.axis_size(axis):
        got, kept = next_step(got, kept, step, axis)
        step *= 2
    return step_sum(got, kept)[0]


class Ladder:
    def __init__(self, got, kept, step=2):
        self.got, self.kept, self.step, self.up = got, kept, step, True

    def advance(self, token=None):
        last = lax.axis_size("rows") // 2
        if self.up and self.step <= last:
            self.got, self.kept, *token = next_step(self.got, self.kept, self.step, "rows", token)
            self.step *= 2
            return token
        if self.up:
            self.kept, *token = step_sum(self.got, self.kept, token)
            self.up, self.step = False, last
        else:
            self.kept, *token = join_step(self.got, self.kept, self.step, token)
            self.step //= 2
        self.got = swap_with(self.kept, "rows", self.step)
        return token

    def ready(self):
        return not self.up and self.step == 1

    def finish(self, cuts):
        while not self.ready():
            self.advance()
        return final_join(self.got, self.kept, cuts)


def deep_rows(tile):
    odd = lax.axis_index("rows") % 2 == 1
    far_up = from_behind(tile, "rows", 2)
    far_down = from_behind(tile, "rows", -2)
    near = swap_with(tile, "rows", 1)
    other = swap_with(jnp.where(odd, far_up, far_down), "rows", 1)
    return far_up, jnp.where(odd, near, other), tile, jnp.where(odd, other, near), far_down


def near_rows(tile, width):
    size = 2 * width
    above = from_behind(tile[:, -size:], "rows", 1)
    below = from_behind(tile[:, :size], "rows", -1)
    return above, tile, below


def per_device(
    inputs,
    heights,
    displacements,
    reduce_one,
    reduce_gain_one,
    reduce_bias_one,
    offset_weight,
    deform_weight,
    deform_gain,
    deform_bias,
    expand_one,
    expand_gain_one,
    expand_bias_one,
    reduce_two,
    reduce_gain_two,
    reduce_bias_two,
    conv_weight,
    conv_gain,
    conv_bias,
    expand_two,
    expand_gain_two,
    expand_bias_two,
    cotangent,
):
    batch, rows, width, channels = inputs.shape
    pixels = rows * width
    n = batch * pixels
    own_heights = lax.dynamic_slice_in_dim(heights, lax.axis_index("ch") * batch, batch)
    rows_here = lax.axis_index("rows") * rows + jnp.arange(rows, dtype=jnp.int32)
    mask = (rows_here[None, :] < own_heights[:, None]).astype(f32)
    mask = jnp.broadcast_to(mask[:, :, None], (batch, rows, width)).reshape(n, 1)
    mask_wide = jnp.broadcast_to(mask, (n, 128))
    count = jnp.sum(heights).astype(f32) * width

    offset_rows = offset_weight.astype(bf16).reshape(3, 6, 3, 3, MID).transpose(2, 3, 0, 1, 4)
    offset_rows = jnp.pad(offset_rows, ((0, 0), (0, 0), (0, 1), (0, 2), (0, 0))).reshape(3, 96, MID)
    disp = jnp.pad(displacements.reshape(3, 6, batch, pixels), ((0, 0), (0, 2), (0, 0), (0, 0)))
    disp = disp.transpose(2, 0, 1, 3)

    reduce_full, came = gather_by_swaps(reduce_one)
    deform_full = gather_weight_after(deform_weight, came)
    expand_full, reduce_full_two, conv_full, expand_full_two = [
        gather_weight(w) for w in (expand_one, reduce_two, conv_weight, expand_two)
    ]

    devices = lax.axis_size("rows") * lax.axis_size("ch")
    acts = inputs.reshape(n, channels)
    acts_low, y_a, spread = product_forward(acts, mask_wide, reduce_full, devices)
    par_a = forward_rows(small_total(spread), reduce_gain_one, reduce_bias_one, count)
    hidden = (gelu(y_a * par_a[0] + par_a[1]) * mask).astype(bf16)
    near_tiles = deep_rows(hidden.reshape(batch, pixels, MID))
    columns, y_b, fraction, spread = deform_forward(
        near_tiles, offset_rows, disp, deform_full, mask_wide, rows, width, devices
    )
    par_b = forward_rows(small_total(spread), deform_gain, deform_bias, count)
    middle, y_c, block = expand_forward([y_b], par_b, mask_wide, expand_full)
    par_c = forward_rows(wide_total(block), expand_gain_one, expand_bias_one, count)

    first_low, y_d, spread = first_forward(y_c, par_c, acts, mask_wide, reduce_full_two, devices)
    par_d = forward_rows(small_total(spread), reduce_gain_two, reduce_bias_two, count)
    hidden_two = (gelu(y_d * par_d[0] + par_d[1]) * mask).astype(bf16)
    rimmed = near_rows(hidden_two.reshape(batch, pixels, MID), width)
    y_e, spread = conv_forward(rimmed, conv_full, mask_wide, rows, width, devices)
    par_e = forward_rows(small_total(spread), conv_gain, conv_bias, count)
    middle_two, y_f, block = expand_forward([y_e], par_e, mask_wide, expand_full_two)
    par_f = forward_rows(wide_total(block), expand_gain_two, expand_bias_two, count)

    output, dt_f, block = output_stage(y_f, par_f, first_low, cotangent.reshape(n, channels), mask_wide)
    back_f, sums_f = backward_rows(wide_total(block), par_f, count)
    dy_f, dt_e, spread = expand_backward(
        dt_f, y_f, par_f, back_f, mask_wide, expand_full_two, y_e, par_e, devices
    )
    expand_two_local = dot(dy_f, middle_two, TN).astype(bf16)
    expand_two_part = scatter_ch(expand_two_local)
    back_e, sums_e = backward_rows(small_total(spread), par_e, count)
    dy_e = norm_gradient(dt_e, y_e, par_e, back_e, mask).astype(bf16)
    dy_e_rim = near_rows(dy_e.reshape(batch, pixels, MID), width)
    conv_local = conv_weight_gradient(dy_e, rimmed, rows, width, (expand_two_local,))
    conv_part = scatter_ch(conv_local)
    dt_d, spread = conv_backward(
        dy_e_rim, conv_full, y_d, par_d, mask_wide, rows, width, devices, (conv_local,)
    )
    base = conv_part.shape[0]
    back_d, sums_d = backward_rows(small_total(spread), par_d, count)
    dy_d, dt_c, block = residual_backward(
        dt_d, y_d, par_d, back_d, mask_wide, reduce_full_two, dt_f, y_c, par_c, acts_low
    )
    reduce_two_local = dot(dy_d, first_low, TN).astype(bf16)

    back_c, sums_c = backward_rows(wide_total(block), par_c, count)
    red_two = split(by_owner(reduce_two_local), "ch", 1)
    dy_c, dt_b, spread, kept = expand_backward(
        dt_c, y_c, par_c, back_c, mask_wide, expand_full, y_b, par_b, devices, (red_two[1],)
    )
    red_two = next_step(red_two[0], kept, 2, "ch")
    expand_one_local = dot(dy_c, middle, TN).astype(bf16)
    exp_one = split(by_owner(expand_one_local), "ch", 1)
    back_b, sums_b = backward_rows(small_total(spread), par_b, count)
    dy_b = norm_gradient(dt_b, y_b, par_b, back_b, mask).astype(bf16)
    got_p, kept_p = first_step([conv_part, expand_two_part], base)
    deform_local, reduce_two_kept, expand_one_kept = columns_weight_gradient(
        dy_b, columns, (red_two[1], exp_one[1])
    )
    deform_part = scatter_ch(deform_local)
    exp_one = next_step(exp_one[0], expand_one_kept, 2, "ch")
    far_up, up, own, down, far_down, offset_local, reduce_two_kept, expand_one_kept, kept_p = deform_backward(
        near_tiles, offset_rows, disp, fraction, deform_full, dy_b, rows, width,
        (), (reduce_two_kept, exp_one[1], kept_p),
    )
    odd = lax.axis_index("rows") % 2 == 1
    passed = swap_with(jnp.where(odd, down, up), "rows", 1)
    got_p, kept_p = next_step(got_p, kept_p, 2)
    below, above, partner, kept_p = return_step(far_up, up, down, far_down, passed, (kept_p,))
    below, above = from_behind(below, "rows", -2), from_behind(above, "rows", 2)
    partner = swap_with(partner, "rows", 1)
    dt_a, spread, kept_p, reduce_two_kept, expand_one_kept = hidden_backward(
        (own, partner, below, above), y_a, par_a, mask_wide, devices,
        (kept_p, reduce_two_kept, expand_one_kept),
    )
    reduce_two_part = last_steps(red_two[0], reduce_two_kept, 4, "ch")[0]
    expand_one_part = last_steps(exp_one[0], expand_one_kept, 4, "ch")[0]
    got_p, kept_p = next_step(got_p, kept_p, 4)
    got_q, kept_q = first_step([reduce_two_part, expand_one_part], base)
    back_a, sums_a = backward_rows(small_total(spread), par_a, count)
    sum_p = Ladder(got_p, kept_p, 8)
    sum_p.advance()
    dy_a, send_s, kept_s, kept_q, deform_part = last_gradient(
        dt_a, y_a, par_a, back_a, mask_wide, acts_low, lax.axis_size("ch"), (sum_p.kept,), (kept_q, deform_part)
    )
    got_s = swap_with(send_s, "ch", 1)
    got_r, kept_r, token = first_step([deform_part], base, jnp.zeros((8, 128), f32))
    sum_q, sum_r = Ladder(got_q, kept_q), Ladder(got_r, kept_r)
    step = 2
    while step < lax.axis_size("ch"):
        got_s, kept_s, token = next_step(got_s, kept_s, step, "ch", token)
        step *= 2
    input_grad, kept_s, offset_local = input_backward(dy_a, reduce_full, dt_c, (kept_s, offset_local))
    offset_local = offset_local.reshape(3, 3, 4, 8, MID)[:, :, :3, :6]
    offset_local = offset_local.transpose(2, 3, 0, 1, 4).reshape(-1, MID)
    offset_part = ladder_sum(offset_local, "ch").astype(bf16)
    offset_part = jnp.pad(offset_part, ((0, -offset_part.shape[0] % base), (0, 0)))
    for ladder in (sum_p, sum_q, sum_r):
        ladder.advance(token)
    reduce_one_part = step_sum(got_s, kept_s)[0][0]
    got_s, kept_s, token = first_step([reduce_one_part, offset_part], base, token)
    sum_s = Ladder(got_s, kept_s)
    while not sum_s.ready():
        for ladder in (sum_p, sum_q, sum_r):
            if not ladder.ready():
                ladder.advance(token)
        (token,) = sum_s.advance(token)
    conv_weight_grad, expand_two_grad = sum_p.finish(((1, 9 * MID), (channels // MID, MID)))
    reduce_two_grad, expand_one_grad = sum_q.finish(((1, channels), (channels // MID, MID)))
    (deform_weight_grad,) = sum_r.finish(((1, 9 * MID),))
    reduce_one_grad, offset_grad = sum_s.finish(((1, channels), (offset_part.shape[0] // base, MID)))
    ends = owned((sums_a, sums_b, sums_c, sums_d, sums_e, sums_f), lax.axis_size("ch"))
    offset_weight_grad = offset_grad[:162].reshape(18, 9 * MID)
    reduce_gain_one_grad, reduce_bias_one_grad, deform_gain_grad, deform_bias_grad = ends[:4]
    expand_gain_one_grad, expand_bias_one_grad, reduce_gain_two_grad, reduce_bias_two_grad = ends[4:8]
    conv_gain_grad, conv_bias_grad, expand_gain_two_grad, expand_bias_two_grad = ends[8:]
    return (
        output.reshape(inputs.shape),
        input_grad.reshape(inputs.shape),
        reduce_one_grad,
        reduce_gain_one_grad,
        reduce_bias_one_grad,
        offset_weight_grad,
        deform_weight_grad,
        deform_gain_grad,
        deform_bias_grad,
        expand_one_grad,
        expand_gain_one_grad,
        expand_bias_one_grad,
        reduce_two_grad,
        reduce_gain_two_grad,
        reduce_bias_two_grad,
        conv_weight_grad,
        conv_gain_grad,
        conv_bias_grad,
        expand_two_grad,
        expand_gain_two_grad,
        expand_bias_two_grad,
    )


def solution(mesh):
    tiles = P("ch", "rows", None, None)
    owned = P("ch", None)
    block = (owned, P(), P())
    placed = (tiles, P(), P(None, "ch", "rows", None)) + block + (P(),) + 2 * block + 3 * block + (tiles,)
    grads = (owned, P("ch"), P("ch"))
    return jax.shard_map(
        per_device,
        mesh=mesh,
        in_specs=placed,
        out_specs=(tiles, tiles) + grads + (P(),) + 2 * grads + 3 * grads,
        check_vma=False,
    )
```

```python
import functools

import jax
import jax.numpy as jnp
from jax import lax
from jax.experimental import pallas as pl
from jax.experimental.pallas import tpu as pltpu
from jax.sharding import PartitionSpec as P

bf16 = jnp.bfloat16
f32 = jnp.float32
VMEM = pltpu.VMEM
HBM = pltpu.HBM
DMA = pltpu.SemaphoreType.DMA
MID = 512
STEP = 512
NT = (((1,), (1,)), ((), ()))
TN = (((0,), (0,)), ((), ()))
NN = (((1,), (0,)), ((), ()))
GELU_A = 0.7978845608028654
GELU_B = 0.044715


def dot(a, b, dims=NN):
    return lax.dot_general(a, b, dims, preferred_element_type=f32)


def shaped(*shape, dtype=f32):
    return jax.ShapeDtypeStruct(shape, dtype)


def without(body, n_in, n_order, n_out, n_through, token):
    first = n_in + n_order + n_through

    def inner(*refs):
        if token:
            refs[first + n_out + n_through][...] = jnp.zeros((8, 128), f32)
        body(*refs[:n_in], *refs[first : first + n_out], *refs[first + n_out + n_through + token :])

    return inner


def cost(us):
    return pl.CostEstimate(flops=int(us * 1.1e9), bytes_accessed=int(us * 2.2e6), transcendentals=0)


def call(body, operands, places, outs, out_places, us, limit, scratch=(), after=(), through=(), token=None):
    def spec(place):
        return pl.BlockSpec(memory_space=HBM if place == "h" else VMEM)

    def pinned(value, place):
        return pltpu.with_memory_space_constraint(value, HBM) if place == "h" else value

    def result(out, place):
        return HBM(out.shape, out.dtype) if place == "h" else out

    tokens = () if token is None else (token,)
    n_in, n_out, n_order = len(operands), len(outs), len(after) + len(tokens)
    return pl.pallas_call(
        without(body, n_in, n_order, n_out, len(through), len(tokens)),
        in_specs=[spec(p) for p in places] + [spec("h")] * len(after) + [spec("v")] * len(tokens)
        + [spec("h")] * len(through),
        out_specs=tuple(spec(p) for p in out_places) + (spec("h"),) * len(through)
        + (spec("v"),) * len(tokens),
        out_shape=tuple(result(o, p) for o, p in zip(outs, out_places))
        + tuple(HBM(v.shape, v.dtype) for v in through)
        + (shaped(8, 128),) * len(tokens),
        input_output_aliases={n_in + n_order + t: n_out + t for t in range(len(through))},
        scratch_shapes=list(scratch),
        compiler_params=pltpu.CompilerParams(vmem_limit_bytes=limit * 2**20),
        cost_estimate=cost(us),
    )(
        *[pinned(v, p) for v, p in zip(operands, places)],
        *[pinned(v, "h") for v in after],
        *tokens,
        *[pinned(v, "h") for v in through],
    )


def moving(source, target, sem):
    copy = pltpu.make_async_copy(source, target, sem)
    copy.start()
    return copy


def columns_moving(source, target, sems, wide=STEP):
    return [
        moving(source.at[:, s * wide : (s + 1) * wide], target.at[:, s * wide : (s + 1) * wide], sems.at[s])
        for s in range(source.shape[1] // wide)
    ]


def rows_moving(source, target, sems, tall=STEP):
    return [
        moving(source.at[s * tall : (s + 1) * tall], target.at[s * tall : (s + 1) * tall], sems.at[s])
        for s in range(source.shape[0] // tall)
    ]


def blocks(wide):
    return [(s, slice(s * STEP, (s + 1) * STEP)) for s in range(wide // STEP)]


def gelu(v):
    return 0.5 * v * (1.0 + jnp.tanh(GELU_A * (v + GELU_B * v * v * v)))


def gelu_slope(v):
    t = jnp.tanh(GELU_A * (v + GELU_B * v * v * v))
    return 0.5 * (1.0 + t) + 0.5 * v * (1.0 - t * t) * (GELU_A * (1.0 + 3.0 * GELU_B * v * v))


def normed(values, par_ref, part=slice(None)):
    return values * par_ref[0:1, part] + par_ref[1:2, part]


def normal_of(values, par_ref, part=slice(None)):
    return values * par_ref[2:3, part] + par_ref[3:4, part]


def norm_gradient(upstream, values, par_ref, back_ref, mask, part=slice(None)):
    normal = normal_of(values, par_ref, part)
    return upstream * back_ref[0:1, part] - mask * (back_ref[1:2, part] + normal * back_ref[2:3, part])


def sums_block(weighted, values):
    n = weighted.shape[1] // 128
    sums = (
        jnp.sum(weighted, axis=0, keepdims=True),
        jnp.sum(weighted * values, axis=0, keepdims=True),
    )
    return jnp.concatenate([v[:, c * 128 : c * 128 + 128] for v in sums for c in range(n)], axis=0)


def write_stats(stat_ref, weighted, values):
    stat_ref[...] = jnp.broadcast_to(sums_block(weighted, values)[None], stat_ref.shape)


def product_forward_body(x_ref, mask_ref, w_ref, low_ref, out_ref, stat_ref, x_buf, low_buf, sems):
    wide = x_ref.shape[1]
    coming = columns_moving(x_ref, x_buf, sems.at[0])
    total, going = None, []
    for s, part in blocks(wide):
        coming[s].wait()
        low_buf[:, part] = x_buf[:, part].astype(bf16)
        going.append(moving(low_buf.at[:, part], low_ref.at[:, part], sems.at[1, s]))
        term = dot(low_buf[:, part], w_ref[:, part], NT)
        total = term if total is None else total + term
    out_ref[...] = total
    write_stats(stat_ref, total * mask_ref[:, 0:1], total)
    for copy in going:
        copy.wait()


def product_forward(x, mask_wide, weight, devices):
    n, wide = x.shape
    return call(
        product_forward_body,
        (x, mask_wide, weight),
        "hvv",
        (shaped(n, wide, dtype=bf16), shaped(n, MID), shaped(devices, 8, 128)),
        "hvv",
        5,
        20,
        [VMEM((n, wide), f32), VMEM((n, wide), bf16), DMA((2, wide // STEP))],
    )


def expand_forward_body(*refs):
    *y_refs, par_ref, mask_ref, e_ref, mid_ref, out_ref, stat_ref, e_buf, out_buf, sems = refs
    coming = rows_moving(e_ref, e_buf, sems.at[0])
    mask = mask_ref[:, 0:1]
    at = 0
    for y_ref in y_refs:
        part = slice(at, at + y_ref.shape[0])
        mid_ref[part, :] = (gelu(normed(y_ref[...], par_ref)) * mask_ref[part, 0:1]).astype(bf16)
        at += y_ref.shape[0]
    going = []
    for s, part in blocks(e_ref.shape[0]):
        coming[s].wait()
        out = dot(mid_ref[...], e_buf[part, :], NT)
        out_buf[:, part] = out.astype(bf16)
        going.append(moving(out_buf.at[:, part], out_ref.at[:, part], sems.at[1, s]))
        stat_ref[s * 8 : s * 8 + 8, :] = sums_block(out * mask, out)
    for copy in going:
        copy.wait()


def expand_forward(y_parts, par, mask_wide, weight):
    n, wide = mask_wide.shape[0], weight.shape[0]
    return call(
        expand_forward_body,
        (*y_parts, par, mask_wide, weight),
        "v" * (len(y_parts) + 2) + "h",
        (shaped(n, MID, dtype=bf16), shaped(n, wide, dtype=bf16), shaped(wide // 64, 128)),
        "vhv",
        4,
        16,
        [VMEM(weight.shape, bf16), VMEM((n, wide), bf16), DMA((2, wide // STEP))],
    )


def first_forward_body(
    y_ref, par_ref, x_ref, mask_ref, w_ref, low_ref, out_ref, stat_ref,
    y_buf, x_buf, w_buf, low_buf, sems
):
    wide = x_ref.shape[1]
    coming_y = columns_moving(y_ref, y_buf, sems.at[0])
    coming_x = columns_moving(x_ref, x_buf, sems.at[1])
    coming_w = columns_moving(w_ref, w_buf, sems.at[2])
    mask = mask_ref[:, 0:1]
    total, going = None, []
    for s, part in blocks(wide):
        coming_y[s].wait()
        coming_x[s].wait()
        first = gelu(normed(y_buf[:, part].astype(f32), par_ref, part) + x_buf[:, part]) * mask
        low_buf[:, part] = first.astype(bf16)
        going.append(moving(low_buf.at[:, part], low_ref.at[:, part], sems.at[3, s]))
        coming_w[s].wait()
        term = dot(low_buf[:, part], w_buf[:, part], NT)
        total = term if total is None else total + term
    out_ref[...] = total
    write_stats(stat_ref, total * mask, total)
    for copy in going:
        copy.wait()


def first_forward(y, par, x, mask_wide, weight, devices):
    n, wide = y.shape
    return call(
        first_forward_body,
        (y, par, x, mask_wide, weight),
        "hvhvh",
        (shaped(n, wide, dtype=bf16), shaped(n, MID), shaped(devices, 8, 128)),
        "hvv",
        6,
        24,
        [
            VMEM((n, wide), bf16),
            VMEM((n, wide), f32),
            VMEM(weight.shape, bf16),
            VMEM((n, wide), bf16),
            DMA((4, wide // STEP)),
        ],
    )


def output_stage_body(
    y_ref, par_ref, first_ref, cot_ref, mask_ref, out_ref, dt_ref, stat_ref,
    y_buf, first_buf, cot_buf, out_buf, dt_buf, sems
):
    wide = y_ref.shape[1]
    coming_y = columns_moving(y_ref, y_buf, sems.at[0])
    coming_f = columns_moving(first_ref, first_buf, sems.at[1])
    coming_c = columns_moving(cot_ref, cot_buf, sems.at[2])
    mask = mask_ref[:, 0:1]
    going = []
    for s, part in blocks(wide):
        coming_y[s].wait()
        coming_f[s].wait()
        y = y_buf[:, part].astype(f32)
        pre = normed(y, par_ref, part) + first_buf[:, part].astype(f32)
        t = jnp.tanh(GELU_A * (pre + GELU_B * pre * pre * pre))
        out_buf[:, part] = 0.5 * pre * (1.0 + t) * mask
        going.append(moving(out_buf.at[:, part], out_ref.at[:, part], sems.at[3, s]))
        slope = 0.5 * (1.0 + t) + 0.5 * pre * (1.0 - t * t) * (GELU_A * (1.0 + 3.0 * GELU_B * pre * pre))
        coming_c[s].wait()
        dt = slope * (cot_buf[:, part] * mask)
        dt_buf[:, part] = dt.astype(bf16)
        going.append(moving(dt_buf.at[:, part], dt_ref.at[:, part], sems.at[4, s]))
        stat_ref[s * 8 : s * 8 + 8, :] = sums_block(dt, normal_of(y, par_ref, part))
    for copy in going:
        copy.wait()


def output_stage(y, par, first, cot, mask_wide):
    n, wide = y.shape
    return call(
        output_stage_body,
        (y, par, first, cot, mask_wide),
        "hvhhv",
        (shaped(n, wide), shaped(n, wide, dtype=bf16), shaped(wide // 64, 128)),
        "hhv",
        8,
        28,
        [
            VMEM((n, wide), bf16),
            VMEM((n, wide), bf16),
            VMEM((n, wide), f32),
            VMEM((n, wide), f32),
            VMEM((n, wide), bf16),
            DMA((5, wide // STEP)),
        ],
    )


def expand_backward_body(
    dt_ref, y_ref, par_ref, back_ref, mask_ref, e_ref, mid_y_ref, mid_par_ref,
    dy_ref, mid_dt_ref, stat_ref, dt_buf, y_buf, e_buf, dy_buf, sems
):
    wide = dt_ref.shape[1]
    coming_dt = columns_moving(dt_ref, dt_buf, sems.at[0])
    coming_y = columns_moving(y_ref, y_buf, sems.at[1])
    coming_e = rows_moving(e_ref, e_buf, sems.at[2])
    mask = mask_ref[:, 0:1]
    total, going = None, []
    for s, part in blocks(wide):
        coming_dt[s].wait()
        coming_y[s].wait()
        dt, y = dt_buf[:, part].astype(f32), y_buf[:, part].astype(f32)
        dy = norm_gradient(dt, y, par_ref, back_ref, mask, part).astype(bf16)
        dy_buf[:, part] = dy
        going.append(moving(dy_buf.at[:, part], dy_ref.at[:, part], sems.at[3, s]))
        coming_e[s].wait()
        term = dot(dy, e_buf[part, :])
        total = term if total is None else total + term
    y = mid_y_ref[...]
    dt = gelu_slope(normed(y, mid_par_ref)) * (total * mask)
    mid_dt_ref[...] = dt
    write_stats(stat_ref, dt, normal_of(y, mid_par_ref))
    for copy in going:
        copy.wait()


def expand_backward(dt, y, par, back, mask_wide, weight, mid_y, mid_par, devices, through=()):
    n, wide = y.shape
    return call(
        expand_backward_body,
        (dt, y, par, back, mask_wide, weight, mid_y, mid_par),
        "hhvvvhvv",
        (shaped(n, wide, dtype=bf16), shaped(n, MID), shaped(devices, 8, 128)),
        "hvv",
        5,
        24,
        [
            VMEM((n, wide), bf16),
            VMEM((n, wide), bf16),
            VMEM(weight.shape, bf16),
            VMEM((n, wide), bf16),
            DMA((4, wide // STEP)),
        ],
        through=through,
    )


def residual_backward_body(
    dt_ref, y_ref, par_ref, back_ref, mask_ref, w_ref, add_ref, wide_y_ref, wide_par_ref, x_ref,
    dy_ref, out_ref, stat_ref, w_buf, add_buf, y_buf, x_buf, out_buf, sems
):
    wide = x_ref.shape[1]
    coming = [
        columns_moving(source, target, sems.at[t])
        for t, (source, target) in enumerate(
            ((w_ref, w_buf), (add_ref, add_buf), (wide_y_ref, y_buf), (x_ref, x_buf))
        )
    ]
    mask = mask_ref[:, 0:1]
    dy_ref[...] = norm_gradient(dt_ref[...], y_ref[...], par_ref, back_ref, mask).astype(bf16)
    going = []
    for s, part in blocks(wide):
        for copies in coming:
            copies[s].wait()
        grad = add_buf[:, part].astype(f32) + dot(dy_ref[...], w_buf[:, part])
        y = y_buf[:, part].astype(f32)
        pre = normed(y, wide_par_ref, part) + x_buf[:, part].astype(f32)
        dt = gelu_slope(pre) * (grad * mask)
        out_buf[:, part] = dt.astype(bf16)
        going.append(moving(out_buf.at[:, part], out_ref.at[:, part], sems.at[4, s]))
        stat_ref[s * 8 : s * 8 + 8, :] = sums_block(dt, normal_of(y, wide_par_ref, part))
    for copy in going:
        copy.wait()


def residual_backward(dt, y, par, back, mask_wide, weight, add, wide_y, wide_par, x):
    n, wide = x.shape
    return call(
        residual_backward_body,
        (dt, y, par, back, mask_wide, weight, add, wide_y, wide_par, x),
        "vvvvvhhhvh",
        (shaped(n, MID, dtype=bf16), shaped(n, wide, dtype=bf16), shaped(wide // 64, 128)),
        "vhv",
        6,
        24,
        [VMEM(weight.shape, bf16)] + [VMEM((n, wide), bf16)] * 4 + [DMA((5, wide // STEP))],
    )


def input_backward_body(dy_ref, w_ref, add_ref, out_ref, w_buf, add_buf, out_buf, sems):
    coming_w = columns_moving(w_ref, w_buf, sems.at[0])
    coming_a = columns_moving(add_ref, add_buf, sems.at[1])
    going = []
    for s, part in blocks(w_ref.shape[1]):
        coming_w[s].wait()
        coming_a[s].wait()
        out_buf[:, part] = add_buf[:, part].astype(f32) + dot(dy_ref[...], w_buf[:, part])
        going.append(moving(out_buf.at[:, part], out_ref.at[:, part], sems.at[2, s]))
    for copy in going:
        copy.wait()


def input_backward(dy, weight, add, token):
    n, wide = add.shape
    return call(
        input_backward_body,
        (dy, weight, add),
        "vhh",
        (shaped(n, wide),),
        "h",
        5,
        20,
        [VMEM(weight.shape, bf16), VMEM((n, wide), bf16), VMEM((n, wide), f32), DMA((3, wide // STEP))],
        token=token,
    )


def hidden_backward_body(
    own_ref, near_ref, up_ref, down_ref, y_ref, par_ref, mask_ref, dt_ref, stat_ref
):
    batch, pixels, _ = own_ref.shape
    for b in range(batch):
        own, near, up, down = [ref[b].astype(f32) for ref in (own_ref, near_ref, up_ref, down_ref)]
        dt_ref[b * pixels : (b + 1) * pixels, :] = own + near + up + down
    grad = dt_ref[...]
    y = y_ref[...]
    dt = gelu_slope(normed(y, par_ref)) * (grad * mask_ref[:, 0:1])
    dt_ref[...] = dt
    write_stats(stat_ref, dt, normal_of(y, par_ref))


def hidden_backward(pieces, y, par, mask_wide, devices, through):
    n = y.shape[0]
    return call(
        hidden_backward_body,
        (*pieces, y, par, mask_wide),
        "v" * (len(pieces) + 3),
        (shaped(n, MID), shaped(devices, 8, 128)),
        "vv",
        3,
        16,
        through=through,
    )


def last_gradient_body(
    dt_ref, y_ref, par_ref, back_ref, mask_ref, acts_ref, dy_ref, send_ref, keep_ref,
    dyt_ref, acts_buf, out_buf, in_sems, out_sems
):
    coming = columns_moving(acts_ref, acts_buf, in_sems)
    dy = norm_gradient(dt_ref[...], y_ref[...], par_ref, back_ref, mask_ref[:, 0:1]).astype(bf16)
    dy_ref[...] = dy
    dyt_ref[...] = dy.astype(f32).T.astype(bf16)
    core = lax.axis_index("ch") % 2
    half, base = send_ref.shape[0], send_ref.shape[1]
    going = []
    for s, part in blocks(acts_ref.shape[1]):
        coming[s].wait()
        out_buf[:, part] = dot(dyt_ref[...], acts_buf[:, part]).astype(bf16)
        for q in range(half):
            for t, (out_ref, side) in enumerate(((send_ref, 1 - core), (keep_ref, core))):
                row = pl.multiple_of((2 * q + side) * base, 16)
                going.append(
                    moving(
                        out_buf.at[pl.ds(row, base), part], out_ref.at[q, :, part], out_sems.at[s, q, t]
                    )
                )
    for copy in going:
        copy.wait()


def last_gradient(dt, y, par, back, mask_wide, acts, ch, through):
    n, wide = acts.shape
    half = shaped(ch // 2, MID // ch, wide, dtype=bf16)
    return call(
        last_gradient_body,
        (dt, y, par, back, mask_wide, acts),
        "vvvvvh",
        (shaped(n, MID, dtype=bf16), half, half),
        "vhh",
        6,
        20,
        [
            VMEM((MID, n), bf16),
            VMEM((n, wide), bf16),
            VMEM((MID, wide), bf16),
            DMA((wide // STEP,)),
            DMA((wide // STEP, ch // 2, 2)),
        ],
        through=through,
    )


def cast_body(v_ref, out_ref):
    out_ref[...] = v_ref[...].astype(bf16)


def cast_after(values, *after):
    return call(cast_body, (values,), "v", (shaped(*values.shape, dtype=bf16),), "v", 2, 12, after=after)[0]


def pack_body(*refs, count, bit_axis, rows):
    part_refs, (send_ref, keep_ref), refs = refs[:count], refs[count : count + 2], refs[count + 2 :]
    buffers, (in_sem, out_sem) = refs[:count], refs[count:]
    coming = [moving(ref, buf, in_sem.at[t]) for t, (ref, buf) in enumerate(zip(part_refs, buffers))]
    bit = lax.axis_index(bit_axis) % 2
    tall = send_ref.shape[1]
    base = rows * tall
    going, at = [], 0
    for copy, buf in zip(coming, buffers):
        copy.wait()
        wide = buf.shape[1]
        for block in range(buf.shape[0] // base):
            for pair in range(rows // 2):
                for out_ref, side in ((send_ref, 1 - bit), (keep_ref, bit)):
                    row = pl.multiple_of(block * base + (2 * pair + side) * tall, 16)
                    going.append(
                        moving(
                            buf.at[pl.ds(row, tall), :],
                            out_ref.at[pair, :, at : at + wide],
                            out_sem.at[len(going)],
                        )
                    )
            at += wide
    for copy in going:
        copy.wait()


def pack_split(parts, base, rows, token=None):
    count = len(parts)
    blocks_in = sum(p.shape[0] // base for p in parts)
    wide = sum(p.shape[0] // base * p.shape[1] for p in parts)
    half = shaped(rows // 2, base // rows, wide, dtype=bf16)
    return call(
        functools.partial(pack_body, count=count, bit_axis="rows", rows=rows),
        tuple(parts),
        "h" * count,
        (half, half),
        "hh",
        3,
        16,
        [VMEM(p.shape, bf16) for p in parts] + [DMA((count,)), DMA((blocks_in * rows,))],
        token=token,
    )


def step_body(got_ref, kept_ref, send_ref, keep_ref, sum_ref, *, axis, step):
    bit = lax.axis_index(axis) // step % 2
    sum_ref[...] = (got_ref[...].astype(f32) + kept_ref[...].astype(f32)).astype(bf16)
    for pair in range(send_ref.shape[0]):
        send_ref[pair] = sum_ref[2 * pair + 1 - bit]
        keep_ref[pair] = sum_ref[2 * pair + bit]


def step_split(got, kept, axis, step, token=None):
    half = shaped(got.shape[0] // 2, *got.shape[1:], dtype=bf16)
    return call(
        functools.partial(step_body, axis=axis, step=step),
        (got, kept),
        "vv",
        (half, half),
        "vv",
        2,
        12,
        [VMEM(got.shape, bf16)],
        token=token,
    )


def sum_body(got_ref, kept_ref, sum_ref):
    sum_ref[...] = (got_ref[...].astype(f32) + kept_ref[...].astype(f32)).astype(bf16)


def step_sum(got, kept, token=None):
    return call(sum_body, (got, kept), "vv", (shaped(*got.shape, dtype=bf16),), "v", 1, 12, token=token)


def join_body(got_ref, kept_ref, out_ref, *, step):
    bit = lax.axis_index("rows") // step % 2
    for a in range(got_ref.shape[0]):
        out_ref[2 * a + bit] = kept_ref[a]
        out_ref[2 * a + 1 - bit] = got_ref[a]


def join_step(got, kept, step, token=None):
    m, r, wide = got.shape
    return call(
        functools.partial(join_body, step=step),
        (got, kept),
        "vv",
        (shaped(2 * m, r, wide, dtype=bf16),),
        "v",
        1,
        12,
        token=token,
    )


def final_body(got_ref, kept_ref, *refs, cuts):
    out_refs, refs = refs[: len(cuts)], refs[len(cuts) :]
    buffers, sems = refs[: len(cuts)], refs[len(cuts)]
    bit = lax.axis_index("rows") % 2
    going, at = [], 0
    for out_ref, buf, (count, wide) in zip(out_refs, buffers, cuts):
        for k in range(count):
            part = slice(at, at + wide)
            for a in range(got_ref.shape[0]):
                buf[k, 2 * a + bit] = kept_ref[a, :, part].astype(f32)
                buf[k, 2 * a + 1 - bit] = got_ref[a, :, part].astype(f32)
            going.append(moving(buf.at[k], out_ref.at[k], sems.at[len(going)]))
            at += wide
    for copy in going:
        copy.wait()


def final_join(got, kept, cuts, token):
    m, r, _ = got.shape
    outs = [shaped(count, 2 * m, r, wide) for count, wide in cuts]
    *outs, token = call(
        functools.partial(final_body, cuts=cuts),
        (got, kept),
        "vv",
        outs,
        "h" * len(outs),
        2,
        20,
        [VMEM(o.shape, f32) for o in outs] + [DMA((sum(count for count, _ in cuts),))],
        token=token,
    )
    return [o.reshape(-1, o.shape[3]) for o in outs], token


def owned_body(*refs):
    n = len(refs) // 3
    for k in range(n):
        size = refs[n + 2 * k].shape[1]
        start = lax.axis_index("ch") * size
        turned = pltpu.roll(refs[k][...], refs[k].shape[1] - start, 1)
        refs[n + 2 * k][...] = turned[0:1, :size]
        refs[n + 2 * k + 1][...] = turned[1:2, :size]


def owned(sums, ch):
    outs = [shaped(1, s.shape[1] // ch) for s in sums for _ in range(2)]
    outs = call(owned_body, tuple(sums), "v" * len(sums), outs, "v" * len(outs), 1, 12)
    return [o.reshape(-1) for o in outs]


def return_body(far_up_ref, up_ref, down_ref, far_down_ref, got_ref, below_ref, above_ref, partner_ref):
    odd = lax.axis_index("rows") % 2 == 1

    @pl.when(odd)
    def _():
        below_ref[...] = (far_up_ref[...].astype(f32) + got_ref[...].astype(f32)).astype(bf16)
        above_ref[...] = far_down_ref[...]
        partner_ref[...] = up_ref[...]

    @pl.when(jnp.logical_not(odd))
    def _():
        below_ref[...] = far_up_ref[...]
        above_ref[...] = (far_down_ref[...].astype(f32) + got_ref[...].astype(f32)).astype(bf16)
        partner_ref[...] = down_ref[...]


def return_step(far_up, up, down, far_down, got, through):
    piece = shaped(*got.shape, dtype=bf16)
    return call(
        return_body,
        (far_up, up, down, far_down, got),
        "vvvvv",
        (piece, piece, piece),
        "vvv",
        2,
        16,
        through=through,
    )


def shift_lanes(values, by, width):
    place = lax.broadcasted_iota(jnp.int32, values.shape, values.ndim - 1) % width
    moved = pltpu.roll(values, by % values.shape[-1], values.ndim - 1)
    return jnp.where((place >= by) & (place < width + by), moved, 0.0)


def shift_rows(values, by, width):
    place = lax.broadcasted_iota(jnp.int32, values.shape, 0) % width
    moved = pltpu.roll(values, by % values.shape[0], 0)
    return jnp.where((place >= by) & (place < width + by), moved, 0.0)


def offset_fraction(ext_ref, ow_ref, b, base, pixels, width):
    u = None
    for i in range(3):
        start = (base + 2 * i) * width
        term = dot(ow_ref[i], ext_ref[b, start : start + pixels, :], NT)
        u = term if u is None else u + term
    total = u[32:64]
    total = total + shift_lanes(u[0:32], 2, width) + shift_lanes(u[64:96], -2, width)
    return 1.0 / (1.0 + jnp.exp(-total))


def deform_forward_body(*refs, batch, rows, width, deep):
    tile_refs, refs = refs[:5], refs[5:]
    ow_ref, disp_ref, m_ref, mask_ref, cols_out_ref, y_ref, frac_ref, stat_ref = refs[:8]
    ext_ref, par_ref, s_ref, cols_ref, m_buf, tile_sems, sems = refs[8:]
    pixels = rows * width
    coming = [
        moving(ref, ext_ref.at[:, t * pixels : (t + 1) * pixels, :], tile_sems.at[t])
        for t, ref in enumerate(tile_refs)
    ]
    coming_m = moving(m_ref, m_buf, sems.at[0])
    for copy in coming:
        copy.wait()
    lane = lax.broadcasted_iota(jnp.int32, (32, 128), 1)
    column = lane % width
    upper = lane // width

    def image(b, carry):
        frac = offset_fraction(ext_ref, ow_ref, b, deep - 2, pixels, width)
        for i in range(4):
            frac_ref[b, i] = frac[i * 8 : i * 8 + 8]
        pix = lax.broadcasted_iota(jnp.int32, (1, pixels), 1)
        row_at, col_at = pix // width, pix % width
        tops, lefts, ys, xs = [], [], [], []
        for k in range(9):
            i, j = k // 3, k % 3
            tops.append(row_at + disp_ref[b, i, 2 * j : 2 * j + 1, :] + (deep - 2))
            lefts.append(col_at + 2 * (j - 1) + disp_ref[b, i, 2 * j + 1 : 2 * j + 2, :])
            at = i * 8 + 2 * j
            ys.append(frac[at : at + 1])
            xs.append(frac[at + 1 : at + 2])
        blank = jnp.zeros((23, pixels), f32)
        par = jnp.concatenate(
            [jnp.concatenate(g, axis=0).astype(f32) if g is not None else blank
             for g in (tops, None, lefts, None, ys, None, xs, None)], axis=0)
        par_ref[...] = par.T

        def row_of_taps(i, carry):
            for j in range(3):
                k = i * 3 + j
                for c in range(pixels // 32):
                    p = pltpu.roll(par_ref[c * 32 : c * 32 + 32, :], 128 - k, 1)
                    wide = (32, 128)
                    top = jnp.broadcast_to(p[:, 0:1], wide).astype(jnp.int32) - upper
                    left = jnp.broadcast_to(p[:, 32:33], wide).astype(jnp.int32)
                    fy = jnp.broadcast_to(p[:, 64:65], wide)
                    fx = jnp.broadcast_to(p[:, 96:97], wide)
                    cw = jnp.where(column == left, 1.0 - fx, jnp.where(column == left + 1, fx, 0.0))
                    ca, cb = (1.0 - fy) * cw, fy * cw
                    for q in range(8):
                        s = jnp.where(top == 2 * q, ca, jnp.where(top == 2 * q - 1, cb, 0.0))
                        s_ref[j * pixels + c * 32 : j * pixels + c * 32 + 32, q * 128 : q * 128 + 128] = s.astype(bf16)
            start = pl.multiple_of(i * 2 * width, 128)
            window = ext_ref[b, pl.ds(start, 16 * width), :]
            for j in range(3):
                got = dot(s_ref[j * pixels : (j + 1) * pixels, :], window).astype(bf16)
                cols_ref[pl.ds(pl.multiple_of(b * pixels, pixels), pixels), pl.ds(pl.multiple_of((i * 3 + j) * MID, MID), MID)] = got
            return carry

        return lax.fori_loop(0, 3, row_of_taps, carry)

    lax.fori_loop(0, batch, image, 0)
    going = moving(cols_ref, cols_out_ref, sems.at[1])
    coming_m.wait()
    y = dot(cols_ref[...], m_buf[...], NT)
    y_ref[...] = y
    write_stats(stat_ref, y * mask_ref[:, 0:1], y)
    going.wait()


def deform_forward(tiles, offset_rows, disp, weight, mask_wide, rows, width, devices):
    batch = tiles[0].shape[0]
    pixels = rows * width
    n = batch * pixels
    return call(
        functools.partial(deform_forward_body, batch=batch, rows=rows, width=width, deep=2 * rows),
        (*tiles, offset_rows, disp, weight, mask_wide),
        "hhhhhvvhv",
        (
            shaped(n, 9 * MID, dtype=bf16),
            shaped(n, MID),
            shaped(batch, 4, 8, pixels),
            shaped(devices, 8, 128),
        ),
        "hvvv",
        15,
        30,
        [
            VMEM((batch, 5 * pixels, MID), bf16),
            VMEM((pixels, 128), f32),
            VMEM((3 * pixels, 16 * width), bf16),
            VMEM((n, 9 * MID), bf16),
            VMEM(weight.shape, bf16),
            DMA((5,)),
            DMA((2,)),
        ],
    )


def deform_backward_body(*refs, batch, rows, width, deep):
    tile_refs, refs = refs[:5], refs[5:]
    (ow_ref, disp_ref, frac_ref, m_ref, dy_ref), refs = refs[:5], refs[5:]
    out_refs, refs = refs[:5], refs[5:]
    dow_ref, ext_ref, dext_ref, dc_ref, g_ref, st_ref, df_ref, m_buf, tile_sems, m_sem = refs
    pixels = rows * width
    coming = [
        moving(ref, ext_ref.at[:, t * pixels : (t + 1) * pixels, :], tile_sems.at[t])
        for t, ref in enumerate(tile_refs)
    ]
    coming_m = moving(m_ref, m_buf, m_sem)
    window = 16 * width
    dow_ref[...] = jnp.zeros_like(dow_ref)
    dext_ref[...] = jnp.zeros_like(dext_ref)
    for copy in coming:
        copy.wait()
    coming_m.wait()

    def image(b, carry):
        at = pl.multiple_of(b * pixels, pixels)

        def row_of_taps(i, carry):
            dy = dy_ref[pl.ds(at, pixels), :]
            for j in range(3):
                m = m_buf[:, pl.ds(pl.multiple_of((i * 3 + j) * MID, MID), MID)]
                dc_ref[j * pixels : (j + 1) * pixels, :] = dot(dy, m).astype(bf16)
            start = pl.multiple_of(i * 2 * width, 128)
            g_ref[...] = dot(ext_ref[b, pl.ds(start, window), :], dc_ref[...], NT)
            place = lax.broadcasted_iota(jnp.int32, (width, 128), 0)
            for j in range(3):
                for h in range(pixels // 128):
                    lanes = slice(h * 128, h * 128 + 128)
                    at_l = slice(j * pixels + h * 128, j * pixels + h * 128 + 128)
                    pix = lax.broadcasted_iota(jnp.int32, (1, 128), 1) + h * 128
                    by_y, by_x = slice(2 * j, 2 * j + 1), slice(2 * j + 1, 2 * j + 2)
                    top = pix // width + disp_ref[b, i, by_y, lanes] + (deep - 2)
                    left = pix % width + 2 * (j - 1) + disp_ref[b, i, by_x, lanes]
                    fy = frac_ref[b, i, by_y, lanes]
                    fx = frac_ref[b, i, by_x, lanes]
                    here, after = place == left, place == left + 1
                    cw = jnp.where(here, 1.0 - fx, jnp.where(after, fx, 0.0))
                    ca, cb = (1.0 - fy) * cw, fy * cw
                    low_sum = jnp.zeros((width, 128), f32)
                    high_sum = jnp.zeros((width, 128), f32)
                    for r in range(16):
                        part = slice(r * width, r * width + width)
                        g = g_ref[part, at_l]
                        m0, m1 = top == r, top == r - 1
                        low_sum = low_sum + jnp.where(m0, g, 0.0)
                        high_sum = high_sum + jnp.where(m1, g, 0.0)
                        st_ref[part, at_l] = jnp.where(m0, ca, jnp.where(m1, cb, 0.0)).astype(bf16)
                    d_fy = jnp.sum((high_sum - low_sum) * cw, axis=0, keepdims=True)
                    mixed = (1.0 - fy) * low_sum + fy * high_sum
                    d_fx = jnp.sum(
                        jnp.where(after, mixed, 0.0) - jnp.where(here, mixed, 0.0), axis=0, keepdims=True)
                    df_ref[i, by_y, lanes] = d_fy * fy * (1.0 - fy)
                    df_ref[i, by_x, lanes] = d_fx * fx * (1.0 - fx)
            dext_ref[b, pl.ds(start, window), :] += dot(st_ref[...], dc_ref[...])
            return carry

        df_ref[...] = jnp.zeros_like(df_ref)
        carry = lax.fori_loop(0, 3, row_of_taps, carry)
        d_off = df_ref[...].reshape(32, pixels).astype(bf16).astype(f32)
        stacked = jnp.concatenate(
            [shift_lanes(d_off, -2, width), d_off, shift_lanes(d_off, 2, width)], axis=0)
        across = jnp.concatenate([stacked, jnp.zeros((32, pixels), f32)], axis=0).T.astype(bf16)
        stacked = stacked.astype(bf16)
        for i in range(3):
            first = (deep - 2 + 2 * i) * width
            part = slice(first, first + pixels)
            dow_ref[i] += dot(stacked, ext_ref[b, part, :])
            dext_ref[b, part, :] += dot(across[:, :96], ow_ref[i])
        return carry

    lax.fori_loop(0, batch, image, 0)
    for t, ref in enumerate(out_refs):
        ref[...] = dext_ref[:, t * pixels : (t + 1) * pixels, :].astype(ref.dtype)


def deform_backward(tiles, offset_rows, disp, frac, weight, dy, rows, width, after, through):
    batch = tiles[0].shape[0]
    pixels = rows * width
    return call(
        functools.partial(deform_backward_body, batch=batch, rows=rows, width=width, deep=2 * rows),
        (*tiles, offset_rows, disp, frac, weight, dy),
        "hhhhhvvvhv",
        tuple(shaped(batch, pixels, MID, dtype=f32 if t == 2 else bf16) for t in range(5))
        + (shaped(3, 96, MID),),
        "vvvvvv",
        20,
        36,
        [
            VMEM((batch, 5 * pixels, MID), bf16),
            VMEM((batch, 5 * pixels, MID), f32),
            VMEM((3 * pixels, MID), bf16),
            VMEM((16 * width, 3 * pixels), f32),
            VMEM((16 * width, 3 * pixels), bf16),
            VMEM((4, 8, pixels), f32),
            VMEM(weight.shape, bf16),
            DMA((5,)),
            DMA,
        ],
        after,
        through,
    )


def taps_moving(m_ref, m_buf, sems):
    wide = 3 * MID
    return columns_moving(m_ref, m_buf, sems, wide)


def rim_moving(parts, rim_ref, sems):
    copies, at = [], 0
    for t, ref in enumerate(parts):
        copies.append(moving(ref, rim_ref.at[:, at : at + ref.shape[1], :], sems.at[t]))
        at += ref.shape[1]
    return copies


def conv_forward_body(
    above_ref, own_ref, below_ref, m_ref, mask_ref, y_ref, stat_ref, rim_ref, m_buf, rim_sems, sems,
    *, batch, rows, width
):
    pixels = rows * width
    coming = taps_moving(m_ref, m_buf, sems)
    for copy in rim_moving((above_ref, own_ref, below_ref), rim_ref, rim_sems):
        copy.wait()
    sums = [[None] * 3 for _ in range(batch)]
    for i in range(3):
        coming[i].wait()
        for b in range(batch):
            for j in range(3):
                k = i * 3 + j
                start = 2 * i * width
                term = dot(rim_ref[b, start : start + pixels, :], m_buf[:, k * MID : (k + 1) * MID], NT)
                sums[b][j] = term if i == 0 else sums[b][j] + term
    for b in range(batch):
        total = sums[b][1] + shift_rows(sums[b][0], 2, width) + shift_rows(sums[b][2], -2, width)
        y_ref[b * pixels : (b + 1) * pixels, :] = total
    y = y_ref[...]
    write_stats(stat_ref, y * mask_ref[:, 0:1], y)


def conv_forward(rim, weight, mask_wide, rows, width, devices):
    batch = rim[0].shape[0]
    n = batch * rows * width
    return call(
        functools.partial(conv_forward_body, batch=batch, rows=rows, width=width),
        (*rim, weight, mask_wide),
        "hhhhv",
        (shaped(n, MID), shaped(devices, 8, 128)),
        "vv",
        5,
        24,
        [VMEM((batch, (rows + 4) * width, MID), bf16), VMEM(weight.shape, bf16), DMA((3,)), DMA((3,))],
    )


def conv_backward_body(
    above_ref, own_ref, below_ref, m_ref, y_ref, par_ref, mask_ref, dt_ref, stat_ref,
    rim_ref, m_buf, rim_sems, sems, *, batch, rows, width
):
    pixels = rows * width
    coming = taps_moving(m_ref, m_buf, sems)
    for copy in rim_moving((above_ref, own_ref, below_ref), rim_ref, rim_sems):
        copy.wait()
    sums = [[None] * 3 for _ in range(batch)]
    for i in range(3):
        coming[i].wait()
        for b in range(batch):
            for j in range(3):
                k = i * 3 + j
                start = (4 - 2 * i) * width
                term = dot(rim_ref[b, start : start + pixels, :], m_buf[:, k * MID : (k + 1) * MID])
                sums[b][j] = term if i == 0 else sums[b][j] + term
    for b in range(batch):
        total = sums[b][1] + shift_rows(sums[b][0], -2, width) + shift_rows(sums[b][2], 2, width)
        dt_ref[b * pixels : (b + 1) * pixels, :] = total
    y = y_ref[...]
    dt = gelu_slope(normed(y, par_ref)) * (dt_ref[...] * mask_ref[:, 0:1])
    dt_ref[...] = dt
    write_stats(stat_ref, dt, normal_of(y, par_ref))


def conv_backward(rim, weight, y, par, mask_wide, rows, width, devices, after):
    batch = rim[0].shape[0]
    n = batch * rows * width
    return call(
        functools.partial(conv_backward_body, batch=batch, rows=rows, width=width),
        (*rim, weight, y, par, mask_wide),
        "hhhhvvv",
        (shaped(n, MID), shaped(devices, 8, 128)),
        "vv",
        6,
        24,
        [VMEM((batch, (rows + 4) * width, MID), bf16), VMEM(weight.shape, bf16), DMA((3,)), DMA((3,))],
        after,
    )


def conv_weight_body(
    dy_ref, above_ref, own_ref, below_ref, out_ref, rim_ref, dyt_ref, out_buf, rim_sems, sems,
    *, batch, rows, width
):
    pixels = rows * width
    coming = rim_moving((above_ref, own_ref, below_ref), rim_ref, rim_sems)
    dy = dy_ref[...].astype(f32)
    going = []
    for j in range(3):
        moved = shift_rows(dy, 2 * (j - 1), width) if j != 1 else dy
        dyt_ref[j] = moved.T.astype(bf16)
        if j == 0:
            for copy in coming:
                copy.wait()
        for i in range(3):
            part = slice((i * 3 + j) * MID, (i * 3 + j + 1) * MID)
            start = 2 * i * width
            total = None
            for b in range(batch):
                term = dot(dyt_ref[j, :, b * pixels : (b + 1) * pixels], rim_ref[b, start : start + pixels, :])
                total = term if total is None else total + term
            out_buf[:, part] = total.astype(bf16)
            going.append(moving(out_buf.at[:, part], out_ref.at[:, part], sems.at[i * 3 + j]))
    for copy in going:
        copy.wait()


def conv_weight_gradient(dy, rim, rows, width, after):
    batch = rim[0].shape[0]
    return call(
        functools.partial(conv_weight_body, batch=batch, rows=rows, width=width),
        (dy, *rim),
        "vhhh",
        (shaped(MID, 9 * MID, dtype=bf16),),
        "h",
        6,
        20,
        [
            VMEM((batch, (rows + 4) * width, MID), bf16),
            VMEM((3, MID, batch * rows * width), bf16),
            VMEM((MID, 9 * MID), bf16),
            DMA((3,)),
            DMA((9,)),
        ],
        after,
    )[0]


def columns_weight_body(dy_ref, cols_ref, out_ref, dyt_ref, cols_buf, out_buf, sems):
    coming = columns_moving(cols_ref, cols_buf, sems.at[0])
    dyt_ref[...] = dy_ref[...].astype(f32).T.astype(bf16)
    going = []
    for s, part in blocks(cols_ref.shape[1]):
        coming[s].wait()
        out_buf[:, part] = dot(dyt_ref[...], cols_buf[:, part]).astype(bf16)
        going.append(moving(out_buf.at[:, part], out_ref.at[:, part], sems.at[1, s]))
    for copy in going:
        copy.wait()


def columns_weight_gradient(dy, cols, through):
    n, wide = cols.shape
    return call(
        columns_weight_body,
        (dy, cols),
        "vh",
        (shaped(MID, wide, dtype=bf16),),
        "h",
        6,
        20,
        [VMEM((MID, n), bf16), VMEM((n, wide), bf16), VMEM((MID, wide), bf16), DMA((2, wide // STEP))],
        through=through,
    )


TILES = 2
EPSILON = 1e-05


def swap_with(values, axis, step):
    return lax.ppermute(values, axis, [(i, i ^ step) for i in range(lax.axis_size(axis))])


def from_behind(block, axis, distance):
    devices = range(lax.axis_size(axis))
    route = [(i - distance, i) for i in devices if i - distance in devices]
    return lax.ppermute(block, axis, route)


def ladder_sum(values, axis):
    step = 1
    while step < lax.axis_size(axis):
        got = swap_with(values.astype(bf16), axis, step)
        values = values + got.astype(f32)
        step *= 2
    return values


def to_everyone(spread, groups=None):
    return lax.all_to_all(spread, ("rows", "ch"), 0, 0, axis_index_groups=groups, tiled=True)


def small_total(spread):
    return jnp.sum(to_everyone(spread), axis=0).reshape(2, -1)


def wide_total(block):
    devices = lax.axis_size("rows") * lax.axis_size("ch")
    core = lax.axis_index("ch") % 2
    above, below = block.reshape(2, -1, 128)
    half = jnp.where(core == 0, above, below) + swap_with(jnp.where(core == 0, below, above), "ch", 1)
    groups = [[i * 2 + k for i in range(devices // 2)] for k in range(2)]
    half = jnp.broadcast_to(half[None], (devices // 2,) + half.shape)
    half = jnp.sum(to_everyone(half, groups), axis=0)
    other = swap_with(half, "ch", 1)
    whole = jnp.stack([jnp.where(core == 0, half, other), jnp.where(core == 0, other, half)])
    whole = whole.reshape(-1, 2, STEP)
    return whole[:, 0].reshape(-1), whole[:, 1].reshape(-1)


def forward_rows(sums, gain, shift, count):
    mean = sums[0] / count
    scale = lax.rsqrt(sums[1] / count - mean * mean + EPSILON)
    return jnp.stack([scale * gain, shift - mean * scale * gain, scale, -mean * scale])


def backward_rows(sums, par, count):
    rows = jnp.stack([par[0], par[0] * sums[0] / count, par[0] * sums[1] / count])
    return rows, jnp.stack([sums[1], sums[0]])


def gather_weight(weight):
    return lax.all_gather(weight.astype(bf16), "ch", axis=0, tiled=True)


def gather_weight_after(weight, *after):
    return lax.all_gather(cast_after(weight, *after), "ch", axis=0, tiled=True)


def gather_by_swaps(weight):
    ch = lax.axis_size("ch")
    came = None
    held = weight.astype(bf16)[None]
    step = ch // 2
    while step >= 1:
        got = swap_with(held, "ch", step)
        came = got if came is None else came
        odd = lax.axis_index("ch") // step % 2 == 1
        held = jnp.stack([jnp.where(odd, got, held), jnp.where(odd, held, got)], axis=1)
        held = held.reshape((-1,) + held.shape[2:])
        step //= 2
    return held.reshape((-1,) + weight.shape[1:]), came


def pick(values, bit):
    return lax.dynamic_index_in_dim(values, bit, 1, keepdims=False)


def scatter_ch(gradient):
    return lax.psum_scatter(gradient, "ch", scatter_dimension=0, tiled=True)


def split(total, axis, step):
    bit = lax.axis_index(axis) // step % 2
    pairs = total.reshape((total.shape[0] // 2, 2) + total.shape[1:])
    return swap_with(pick(pairs, 1 - bit), axis, step), pick(pairs, bit)


def added(pair):
    got, kept = pair
    return (got.astype(f32) + kept.astype(f32)).astype(bf16)


def rest_of(total, axis, step=1):
    while step < lax.axis_size(axis):
        total = added(split(total, axis, step))
        step *= 2
    return total


def by_owner(gradient, axis="ch"):
    count = lax.axis_size(axis)
    return gradient.reshape((count, gradient.shape[0] // count) + gradient.shape[1:])


def wide_enough(base):
    return base // lax.axis_size("rows") % 16 == 0


def first_step(parts, base, token=None):
    if wide_enough(base):
        send, keep, *token = pack_split(parts, base, lax.axis_size("rows"), token)
        return (swap_with(send, "rows", 1), keep, *token)
    laid = [jnp.concatenate([p[r : r + base] for r in range(0, p.shape[0], base)], axis=1) for p in parts]
    pair = split(by_owner(jnp.concatenate(laid, axis=1), "rows"), "rows", 1)
    return pair if token is None else (*pair, token)


def next_step(got, kept, step, axis="rows", token=None):
    send, keep, *token = step_split(got, kept, axis, step, token)
    return (swap_with(send, axis, step), keep, *token)


def last_steps(got, kept, step, axis):
    while step < lax.axis_size(axis):
        got, kept = next_step(got, kept, step, axis)
        step *= 2
    return step_sum(got, kept)[0]


class Ladder:
    def __init__(self, got, kept, step=2):
        self.got, self.kept, self.step, self.up = got, kept, step, True

    def advance(self, token=None):
        last = lax.axis_size("rows") // 2
        if self.up and self.step <= last:
            self.got, self.kept, *token = next_step(self.got, self.kept, self.step, "rows", token)
            self.step *= 2
            return token
        if self.up:
            self.kept, *token = step_sum(self.got, self.kept, token)
            self.up, self.step = False, last
        else:
            self.kept, *token = join_step(self.got, self.kept, self.step, token)
            self.step //= 2
        self.got = swap_with(self.kept, "rows", self.step)
        return token

    def ready(self):
        return not self.up and self.step == 1

    def finish(self, cuts, token):
        while not self.ready():
            (token,) = self.advance(token)
        return final_join(self.got, self.kept, cuts, token)


def deep_rows(tile):
    odd = lax.axis_index("rows") % 2 == 1
    far_up = from_behind(tile, "rows", 2)
    far_down = from_behind(tile, "rows", -2)
    near = swap_with(tile, "rows", 1)
    other = swap_with(jnp.where(odd, far_up, far_down), "rows", 1)
    return far_up, jnp.where(odd, near, other), tile, jnp.where(odd, other, near), far_down


def near_rows(tile, width):
    size = 2 * width
    above = from_behind(tile[:, -size:], "rows", 1)
    below = from_behind(tile[:, :size], "rows", -1)
    return above, tile, below


def per_device(
    inputs,
    heights,
    displacements,
    reduce_one,
    reduce_gain_one,
    reduce_bias_one,
    offset_weight,
    deform_weight,
    deform_gain,
    deform_bias,
    expand_one,
    expand_gain_one,
    expand_bias_one,
    reduce_two,
    reduce_gain_two,
    reduce_bias_two,
    conv_weight,
    conv_gain,
    conv_bias,
    expand_two,
    expand_gain_two,
    expand_bias_two,
    cotangent,
):
    batch, rows, width, channels = inputs.shape
    pixels = rows * width
    n = batch * pixels
    own_heights = lax.dynamic_slice_in_dim(heights, lax.axis_index("ch") * batch, batch)
    rows_here = lax.axis_index("rows") * rows + jnp.arange(rows, dtype=jnp.int32)
    mask = (rows_here[None, :] < own_heights[:, None]).astype(f32)
    mask = jnp.broadcast_to(mask[:, :, None], (batch, rows, width)).reshape(n, 1)
    mask_wide = jnp.broadcast_to(mask, (n, 128))
    count = jnp.sum(heights).astype(f32) * width

    offset_rows = offset_weight.astype(bf16).reshape(3, 6, 3, 3, MID).transpose(2, 3, 0, 1, 4)
    offset_rows = jnp.pad(offset_rows, ((0, 0), (0, 0), (0, 1), (0, 2), (0, 0))).reshape(3, 96, MID)
    disp = jnp.pad(displacements.reshape(3, 6, batch, pixels), ((0, 0), (0, 2), (0, 0), (0, 0)))
    disp = disp.transpose(2, 0, 1, 3)

    reduce_full, came = gather_by_swaps(reduce_one)
    deform_full = gather_weight_after(deform_weight, came)
    expand_full, reduce_full_two, conv_full, expand_full_two = [
        gather_weight(w) for w in (expand_one, reduce_two, conv_weight, expand_two)
    ]

    devices = lax.axis_size("rows") * lax.axis_size("ch")
    acts = inputs.reshape(n, channels)
    acts_low, y_a, spread = product_forward(acts, mask_wide, reduce_full, devices)
    par_a = forward_rows(small_total(spread), reduce_gain_one, reduce_bias_one, count)
    hidden = (gelu(y_a * par_a[0] + par_a[1]) * mask).astype(bf16)
    near_tiles = deep_rows(hidden.reshape(batch, pixels, MID))
    columns, y_b, fraction, spread = deform_forward(
        near_tiles, offset_rows, disp, deform_full, mask_wide, rows, width, devices
    )
    par_b = forward_rows(small_total(spread), deform_gain, deform_bias, count)
    middle, y_c, block = expand_forward([y_b], par_b, mask_wide, expand_full)
    par_c = forward_rows(wide_total(block), expand_gain_one, expand_bias_one, count)

    first_low, y_d, spread = first_forward(y_c, par_c, acts, mask_wide, reduce_full_two, devices)
    par_d = forward_rows(small_total(spread), reduce_gain_two, reduce_bias_two, count)
    hidden_two = (gelu(y_d * par_d[0] + par_d[1]) * mask).astype(bf16)
    rimmed = near_rows(hidden_two.reshape(batch, pixels, MID), width)
    y_e, spread = conv_forward(rimmed, conv_full, mask_wide, rows, width, devices)
    par_e = forward_rows(small_total(spread), conv_gain, conv_bias, count)
    middle_two, y_f, block = expand_forward([y_e], par_e, mask_wide, expand_full_two)
    par_f = forward_rows(wide_total(block), expand_gain_two, expand_bias_two, count)

    output, dt_f, block = output_stage(y_f, par_f, first_low, cotangent.reshape(n, channels), mask_wide)
    back_f, sums_f = backward_rows(wide_total(block), par_f, count)
    dy_f, dt_e, spread = expand_backward(
        dt_f, y_f, par_f, back_f, mask_wide, expand_full_two, y_e, par_e, devices
    )
    expand_two_local = dot(dy_f, middle_two, TN).astype(bf16)
    expand_two_part = scatter_ch(expand_two_local)
    back_e, sums_e = backward_rows(small_total(spread), par_e, count)
    dy_e = norm_gradient(dt_e, y_e, par_e, back_e, mask).astype(bf16)
    dy_e_rim = near_rows(dy_e.reshape(batch, pixels, MID), width)
    conv_local = conv_weight_gradient(dy_e, rimmed, rows, width, (expand_two_local,))
    conv_part = scatter_ch(conv_local)
    dt_d, spread = conv_backward(
        dy_e_rim, conv_full, y_d, par_d, mask_wide, rows, width, devices, (conv_local,)
    )
    base = conv_part.shape[0]
    back_d, sums_d = backward_rows(small_total(spread), par_d, count)
    dy_d, dt_c, block = residual_backward(
        dt_d, y_d, par_d, back_d, mask_wide, reduce_full_two, dt_f, y_c, par_c, acts_low
    )
    reduce_two_local = dot(dy_d, first_low, TN).astype(bf16)

    back_c, sums_c = backward_rows(wide_total(block), par_c, count)
    red_two = split(by_owner(reduce_two_local), "ch", 1)
    got_p, kept_p = first_step([conv_part, expand_two_part], base)
    dy_c, dt_b, spread, kept, kept_p = expand_backward(
        dt_c, y_c, par_c, back_c, mask_wide, expand_full, y_b, par_b, devices, (red_two[1], kept_p)
    )
    red_two = next_step(red_two[0], kept, 2, "ch")
    expand_one_local = dot(dy_c, middle, TN).astype(bf16)
    exp_one = split(by_owner(expand_one_local), "ch", 1)
    back_b, sums_b = backward_rows(small_total(spread), par_b, count)
    dy_b = norm_gradient(dt_b, y_b, par_b, back_b, mask).astype(bf16)
    sum_p = Ladder(got_p, kept_p)
    sum_p.advance()
    deform_local, reduce_two_kept, expand_one_kept, sum_p.kept = columns_weight_gradient(
        dy_b, columns, (red_two[1], exp_one[1], sum_p.kept)
    )
    sum_p.advance()
    deform_part = scatter_ch(deform_local)
    exp_one = next_step(exp_one[0], expand_one_kept, 2, "ch")
    far_up, up, own, down, far_down, offset_local, reduce_two_kept, expand_one_kept, sum_p.kept = deform_backward(
        near_tiles, offset_rows, disp, fraction, deform_full, dy_b, rows, width,
        (), (reduce_two_kept, exp_one[1], sum_p.kept),
    )
    odd = lax.axis_index("rows") % 2 == 1
    passed = swap_with(jnp.where(odd, down, up), "rows", 1)
    sum_p.advance()
    below, above, partner, sum_p.kept = return_step(far_up, up, down, far_down, passed, (sum_p.kept,))
    below, above = from_behind(below, "rows", -2), from_behind(above, "rows", 2)
    partner = swap_with(partner, "rows", 1)
    dt_a, spread, sum_p.kept, reduce_two_kept, expand_one_kept = hidden_backward(
        (own, partner, below, above), y_a, par_a, mask_wide, devices,
        (sum_p.kept, reduce_two_kept, expand_one_kept),
    )
    sum_p.advance()
    reduce_two_part = last_steps(red_two[0], reduce_two_kept, 4, "ch")[0]
    expand_one_part = last_steps(exp_one[0], expand_one_kept, 4, "ch")[0]
    got_q, kept_q = first_step([reduce_two_part, expand_one_part], base)
    back_a, sums_a = backward_rows(small_total(spread), par_a, count)
    dy_a, send_s, kept_s, sum_p.kept, kept_q, deform_part, offset_local = last_gradient(
        dt_a, y_a, par_a, back_a, mask_wide, acts_low, lax.axis_size("ch"),
        (sum_p.kept, kept_q, deform_part, offset_local),
    )
    got_s = swap_with(send_s, "ch", 1)
    got_r, kept_r, token = first_step([deform_part], base, jnp.zeros((8, 128), f32))
    sum_q, sum_r = Ladder(got_q, kept_q), Ladder(got_r, kept_r)
    (token,) = sum_p.advance(token)
    (token,) = sum_q.advance(token)
    step = 2
    while step < lax.axis_size("ch"):
        got_s, kept_s, token = next_step(got_s, kept_s, step, "ch", token)
        step *= 2
    (token,) = sum_r.advance(token)
    offset_local = offset_local.reshape(3, 3, 4, 8, MID)[:, :, :3, :6]
    offset_local = offset_local.transpose(2, 3, 0, 1, 4).reshape(-1, MID)
    offset_part = ladder_sum(offset_local, "ch").astype(bf16)
    offset_part = jnp.pad(offset_part, ((0, -offset_part.shape[0] % base), (0, 0)))
    reduce_one_part = step_sum(got_s, kept_s)[0][0]
    got_s, kept_s, token = first_step([reduce_one_part, offset_part], base, token)
    sum_s = Ladder(got_s, kept_s)
    input_grad, token = input_backward(dy_a, reduce_full, dt_c, token)
    (conv_weight_grad, expand_two_grad), token = sum_p.finish(((1, 9 * MID), (channels // MID, MID)), token)
    while not sum_s.ready():
        for ladder in (sum_q, sum_r):
            if not ladder.ready():
                ladder.advance(token)
        (token,) = sum_s.advance(token)
    (reduce_two_grad, expand_one_grad), token = sum_q.finish(((1, channels), (channels // MID, MID)), token)
    (deform_weight_grad,), token = sum_r.finish(((1, 9 * MID),), token)
    (reduce_one_grad, offset_grad), token = sum_s.finish(
        ((1, channels), (offset_part.shape[0] // base, MID)), token
    )
    ends = owned((sums_a, sums_b, sums_c, sums_d, sums_e, sums_f), lax.axis_size("ch"))
    offset_weight_grad = offset_grad[:162].reshape(18, 9 * MID)
    reduce_gain_one_grad, reduce_bias_one_grad, deform_gain_grad, deform_bias_grad = ends[:4]
    expand_gain_one_grad, expand_bias_one_grad, reduce_gain_two_grad, reduce_bias_two_grad = ends[4:8]
    conv_gain_grad, conv_bias_grad, expand_gain_two_grad, expand_bias_two_grad = ends[8:]
    return (
        output.reshape(inputs.shape),
        input_grad.reshape(inputs.shape),
        reduce_one_grad,
        reduce_gain_one_grad,
        reduce_bias_one_grad,
        offset_weight_grad,
        deform_weight_grad,
        deform_gain_grad,
        deform_bias_grad,
        expand_one_grad,
        expand_gain_one_grad,
        expand_bias_one_grad,
        reduce_two_grad,
        reduce_gain_two_grad,
        reduce_bias_two_grad,
        conv_weight_grad,
        conv_gain_grad,
        conv_bias_grad,
        expand_two_grad,
        expand_gain_two_grad,
        expand_bias_two_grad,
    )


def solution(mesh):
    tiles = P("ch", "rows", None, None)
    owned = P("ch", None)
    block = (owned, P(), P())
    placed = (tiles, P(), P(None, "ch", "rows", None)) + block + (P(),) + 2 * block + 3 * block + (tiles,)
    grads = (owned, P("ch"), P("ch"))
    return jax.shard_map(
        per_device,
        mesh=mesh,
        in_specs=placed,
        out_specs=(tiles, tiles) + grads + (P(),) + 2 * grads + 3 * grads,
        check_vma=False,
    )
```

```python
import functools

import jax
import jax.numpy as jnp
from jax import lax
from jax.experimental import pallas as pl
from jax.experimental.pallas import tpu as pltpu
from jax.sharding import PartitionSpec as P

bf16 = jnp.bfloat16
f32 = jnp.float32
VMEM = pltpu.VMEM
HBM = pltpu.HBM
DMA = pltpu.SemaphoreType.DMA
MID = 512
STEP = 512
NT = (((1,), (1,)), ((), ()))
TN = (((0,), (0,)), ((), ()))
NN = (((1,), (0,)), ((), ()))
GELU_A = 0.7978845608028654
GELU_B = 0.044715


def dot(a, b, dims=NN):
    return lax.dot_general(a, b, dims, preferred_element_type=f32)


def shaped(*shape, dtype=f32):
    return jax.ShapeDtypeStruct(shape, dtype)


def without(body, n_in, n_order, n_out, n_through, token):
    first = n_in + n_order + n_through

    def inner(*refs):
        if token:
            refs[first + n_out + n_through][...] = jnp.zeros((8, 128), f32)
        body(*refs[:n_in], *refs[first : first + n_out], *refs[first + n_out + n_through + token :])

    return inner


def cost(us):
    return pl.CostEstimate(flops=int(us * 1.1e9), bytes_accessed=int(us * 2.2e6), transcendentals=0)


def call(body, operands, places, outs, out_places, us, limit, scratch=(), after=(), through=(), token=None):
    def spec(place):
        return pl.BlockSpec(memory_space=HBM if place == "h" else VMEM)

    def pinned(value, place):
        return pltpu.with_memory_space_constraint(value, HBM) if place == "h" else value

    def result(out, place):
        return HBM(out.shape, out.dtype) if place == "h" else out

    tokens = () if token is None else (token,)
    n_in, n_out, n_order = len(operands), len(outs), len(after) + len(tokens)
    return pl.pallas_call(
        without(body, n_in, n_order, n_out, len(through), len(tokens)),
        in_specs=[spec(p) for p in places] + [spec("h")] * len(after) + [spec("v")] * len(tokens)
        + [spec("h")] * len(through),
        out_specs=tuple(spec(p) for p in out_places) + (spec("h"),) * len(through)
        + (spec("v"),) * len(tokens),
        out_shape=tuple(result(o, p) for o, p in zip(outs, out_places))
        + tuple(HBM(v.shape, v.dtype) for v in through)
        + (shaped(8, 128),) * len(tokens),
        input_output_aliases={n_in + n_order + t: n_out + t for t in range(len(through))},
        scratch_shapes=list(scratch),
        compiler_params=pltpu.CompilerParams(vmem_limit_bytes=limit * 2**20),
        cost_estimate=cost(us),
    )(
        *[pinned(v, p) for v, p in zip(operands, places)],
        *[pinned(v, "h") for v in after],
        *tokens,
        *[pinned(v, "h") for v in through],
    )


def moving(source, target, sem):
    copy = pltpu.make_async_copy(source, target, sem)
    copy.start()
    return copy


def columns_moving(source, target, sems, wide=STEP):
    return [
        moving(source.at[:, s * wide : (s + 1) * wide], target.at[:, s * wide : (s + 1) * wide], sems.at[s])
        for s in range(source.shape[1] // wide)
    ]


def rows_moving(source, target, sems, tall=STEP):
    return [
        moving(source.at[s * tall : (s + 1) * tall], target.at[s * tall : (s + 1) * tall], sems.at[s])
        for s in range(source.shape[0] // tall)
    ]


def blocks(wide):
    return [(s, slice(s * STEP, (s + 1) * STEP)) for s in range(wide // STEP)]


def gelu(v):
    return 0.5 * v * (1.0 + jnp.tanh(GELU_A * (v + GELU_B * v * v * v)))


def gelu_slope(v):
    t = jnp.tanh(GELU_A * (v + GELU_B * v * v * v))
    return 0.5 * (1.0 + t) + 0.5 * v * (1.0 - t * t) * (GELU_A * (1.0 + 3.0 * GELU_B * v * v))


def normed(values, par_ref, part=slice(None)):
    return values * par_ref[0:1, part] + par_ref[1:2, part]


def normal_of(values, par_ref, part=slice(None)):
    return values * par_ref[2:3, part] + par_ref[3:4, part]


def norm_gradient(upstream, values, par_ref, back_ref, mask, part=slice(None)):
    normal = normal_of(values, par_ref, part)
    return upstream * back_ref[0:1, part] - mask * (back_ref[1:2, part] + normal * back_ref[2:3, part])


def sums_block(weighted, values):
    n = weighted.shape[1] // 128
    sums = (
        jnp.sum(weighted, axis=0, keepdims=True),
        jnp.sum(weighted * values, axis=0, keepdims=True),
    )
    return jnp.concatenate([v[:, c * 128 : c * 128 + 128] for v in sums for c in range(n)], axis=0)


def write_stats(stat_ref, weighted, values):
    stat_ref[...] = jnp.broadcast_to(sums_block(weighted, values)[None], stat_ref.shape)


def product_forward_body(x_ref, mask_ref, w_ref, low_ref, out_ref, stat_ref, x_buf, low_buf, sems):
    wide = x_ref.shape[1]
    coming = columns_moving(x_ref, x_buf, sems.at[0])
    total, going = None, []
    for s, part in blocks(wide):
        coming[s].wait()
        low_buf[:, part] = x_buf[:, part].astype(bf16)
        going.append(moving(low_buf.at[:, part], low_ref.at[:, part], sems.at[1, s]))
        term = dot(low_buf[:, part], w_ref[:, part], NT)
        total = term if total is None else total + term
    out_ref[...] = total
    write_stats(stat_ref, total * mask_ref[:, 0:1], total)
    for copy in going:
        copy.wait()


def product_forward(x, mask_wide, weight, devices):
    n, wide = x.shape
    return call(
        product_forward_body,
        (x, mask_wide, weight),
        "hvv",
        (shaped(n, wide, dtype=bf16), shaped(n, MID), shaped(devices, 8, 128)),
        "hvv",
        5,
        20,
        [VMEM((n, wide), f32), VMEM((n, wide), bf16), DMA((2, wide // STEP))],
    )


def expand_forward_body(*refs):
    *y_refs, par_ref, mask_ref, e_ref, mid_ref, out_ref, stat_ref, e_buf, out_buf, sems = refs
    coming = rows_moving(e_ref, e_buf, sems.at[0])
    mask = mask_ref[:, 0:1]
    at = 0
    for y_ref in y_refs:
        part = slice(at, at + y_ref.shape[0])
        mid_ref[part, :] = (gelu(normed(y_ref[...], par_ref)) * mask_ref[part, 0:1]).astype(bf16)
        at += y_ref.shape[0]
    going = []
    for s, part in blocks(e_ref.shape[0]):
        coming[s].wait()
        out = dot(mid_ref[...], e_buf[part, :], NT)
        out_buf[:, part] = out.astype(bf16)
        going.append(moving(out_buf.at[:, part], out_ref.at[:, part], sems.at[1, s]))
        stat_ref[s * 8 : s * 8 + 8, :] = sums_block(out * mask, out)
    for copy in going:
        copy.wait()


def expand_forward(y_parts, par, mask_wide, weight):
    n, wide = mask_wide.shape[0], weight.shape[0]
    return call(
        expand_forward_body,
        (*y_parts, par, mask_wide, weight),
        "v" * (len(y_parts) + 2) + "h",
        (shaped(n, MID, dtype=bf16), shaped(n, wide, dtype=bf16), shaped(wide // 64, 128)),
        "vhv",
        4,
        16,
        [VMEM(weight.shape, bf16), VMEM((n, wide), bf16), DMA((2, wide // STEP))],
    )


def first_forward_body(
    y_ref, par_ref, x_ref, mask_ref, w_ref, low_ref, out_ref, stat_ref,
    y_buf, x_buf, w_buf, low_buf, sems
):
    wide = x_ref.shape[1]
    coming_y = columns_moving(y_ref, y_buf, sems.at[0])
    coming_x = columns_moving(x_ref, x_buf, sems.at[1])
    coming_w = columns_moving(w_ref, w_buf, sems.at[2])
    mask = mask_ref[:, 0:1]
    total, going = None, []
    for s, part in blocks(wide):
        coming_y[s].wait()
        coming_x[s].wait()
        first = gelu(normed(y_buf[:, part].astype(f32), par_ref, part) + x_buf[:, part]) * mask
        low_buf[:, part] = first.astype(bf16)
        going.append(moving(low_buf.at[:, part], low_ref.at[:, part], sems.at[3, s]))
        coming_w[s].wait()
        term = dot(low_buf[:, part], w_buf[:, part], NT)
        total = term if total is None else total + term
    out_ref[...] = total
    write_stats(stat_ref, total * mask, total)
    for copy in going:
        copy.wait()


def first_forward(y, par, x, mask_wide, weight, devices):
    n, wide = y.shape
    return call(
        first_forward_body,
        (y, par, x, mask_wide, weight),
        "hvhvh",
        (shaped(n, wide, dtype=bf16), shaped(n, MID), shaped(devices, 8, 128)),
        "hvv",
        6,
        24,
        [
            VMEM((n, wide), bf16),
            VMEM((n, wide), f32),
            VMEM(weight.shape, bf16),
            VMEM((n, wide), bf16),
            DMA((4, wide // STEP)),
        ],
    )


def output_stage_body(
    y_ref, par_ref, first_ref, cot_ref, mask_ref, out_ref, dt_ref, stat_ref,
    y_buf, first_buf, cot_buf, out_buf, dt_buf, sems
):
    wide = y_ref.shape[1]
    coming_y = columns_moving(y_ref, y_buf, sems.at[0])
    coming_f = columns_moving(first_ref, first_buf, sems.at[1])
    coming_c = columns_moving(cot_ref, cot_buf, sems.at[2])
    mask = mask_ref[:, 0:1]
    going = []
    for s, part in blocks(wide):
        coming_y[s].wait()
        coming_f[s].wait()
        y = y_buf[:, part].astype(f32)
        pre = normed(y, par_ref, part) + first_buf[:, part].astype(f32)
        t = jnp.tanh(GELU_A * (pre + GELU_B * pre * pre * pre))
        out_buf[:, part] = 0.5 * pre * (1.0 + t) * mask
        going.append(moving(out_buf.at[:, part], out_ref.at[:, part], sems.at[3, s]))
        slope = 0.5 * (1.0 + t) + 0.5 * pre * (1.0 - t * t) * (GELU_A * (1.0 + 3.0 * GELU_B * pre * pre))
        coming_c[s].wait()
        dt = slope * (cot_buf[:, part] * mask)
        dt_buf[:, part] = dt.astype(bf16)
        going.append(moving(dt_buf.at[:, part], dt_ref.at[:, part], sems.at[4, s]))
        stat_ref[s * 8 : s * 8 + 8, :] = sums_block(dt, normal_of(y, par_ref, part))
    for copy in going:
        copy.wait()


def output_stage(y, par, first, cot, mask_wide):
    n, wide = y.shape
    return call(
        output_stage_body,
        (y, par, first, cot, mask_wide),
        "hvhhv",
        (shaped(n, wide), shaped(n, wide, dtype=bf16), shaped(wide // 64, 128)),
        "hhv",
        8,
        28,
        [
            VMEM((n, wide), bf16),
            VMEM((n, wide), bf16),
            VMEM((n, wide), f32),
            VMEM((n, wide), f32),
            VMEM((n, wide), bf16),
            DMA((5, wide // STEP)),
        ],
    )


def expand_backward_body(
    dt_ref, y_ref, par_ref, back_ref, mask_ref, e_ref, mid_y_ref, mid_par_ref,
    dy_ref, mid_dt_ref, stat_ref, dt_buf, y_buf, e_buf, dy_buf, sems
):
    wide = dt_ref.shape[1]
    coming_dt = columns_moving(dt_ref, dt_buf, sems.at[0])
    coming_y = columns_moving(y_ref, y_buf, sems.at[1])
    coming_e = rows_moving(e_ref, e_buf, sems.at[2])
    mask = mask_ref[:, 0:1]
    total, going = None, []
    for s, part in blocks(wide):
        coming_dt[s].wait()
        coming_y[s].wait()
        dt, y = dt_buf[:, part].astype(f32), y_buf[:, part].astype(f32)
        dy = norm_gradient(dt, y, par_ref, back_ref, mask, part).astype(bf16)
        dy_buf[:, part] = dy
        going.append(moving(dy_buf.at[:, part], dy_ref.at[:, part], sems.at[3, s]))
        coming_e[s].wait()
        term = dot(dy, e_buf[part, :])
        total = term if total is None else total + term
    y = mid_y_ref[...]
    dt = gelu_slope(normed(y, mid_par_ref)) * (total * mask)
    mid_dt_ref[...] = dt
    write_stats(stat_ref, dt, normal_of(y, mid_par_ref))
    for copy in going:
        copy.wait()


def expand_backward(dt, y, par, back, mask_wide, weight, mid_y, mid_par, devices, through=()):
    n, wide = y.shape
    return call(
        expand_backward_body,
        (dt, y, par, back, mask_wide, weight, mid_y, mid_par),
        "hhvvvhvv",
        (shaped(n, wide, dtype=bf16), shaped(n, MID), shaped(devices, 8, 128)),
        "hvv",
        5,
        24,
        [
            VMEM((n, wide), bf16),
            VMEM((n, wide), bf16),
            VMEM(weight.shape, bf16),
            VMEM((n, wide), bf16),
            DMA((4, wide // STEP)),
        ],
        through=through,
    )


def residual_backward_body(
    dt_ref, y_ref, par_ref, back_ref, mask_ref, w_ref, add_ref, wide_y_ref, wide_par_ref, x_ref,
    dy_ref, out_ref, stat_ref, w_buf, add_buf, y_buf, x_buf, out_buf, sems
):
    wide = x_ref.shape[1]
    coming = [
        columns_moving(source, target, sems.at[t])
        for t, (source, target) in enumerate(
            ((w_ref, w_buf), (add_ref, add_buf), (wide_y_ref, y_buf), (x_ref, x_buf))
        )
    ]
    mask = mask_ref[:, 0:1]
    dy_ref[...] = norm_gradient(dt_ref[...], y_ref[...], par_ref, back_ref, mask).astype(bf16)
    going = []
    for s, part in blocks(wide):
        for copies in coming:
            copies[s].wait()
        grad = add_buf[:, part].astype(f32) + dot(dy_ref[...], w_buf[:, part])
        y = y_buf[:, part].astype(f32)
        pre = normed(y, wide_par_ref, part) + x_buf[:, part].astype(f32)
        dt = gelu_slope(pre) * (grad * mask)
        out_buf[:, part] = dt.astype(bf16)
        going.append(moving(out_buf.at[:, part], out_ref.at[:, part], sems.at[4, s]))
        stat_ref[s * 8 : s * 8 + 8, :] = sums_block(dt, normal_of(y, wide_par_ref, part))
    for copy in going:
        copy.wait()


def residual_backward(dt, y, par, back, mask_wide, weight, add, wide_y, wide_par, x):
    n, wide = x.shape
    return call(
        residual_backward_body,
        (dt, y, par, back, mask_wide, weight, add, wide_y, wide_par, x),
        "vvvvvhhhvh",
        (shaped(n, MID, dtype=bf16), shaped(n, wide, dtype=bf16), shaped(wide // 64, 128)),
        "vhv",
        6,
        24,
        [VMEM(weight.shape, bf16)] + [VMEM((n, wide), bf16)] * 4 + [DMA((5, wide // STEP))],
    )


def input_backward_body(dy_ref, w_ref, add_ref, out_ref, w_buf, add_buf, out_buf, sems):
    coming_w = columns_moving(w_ref, w_buf, sems.at[0])
    coming_a = columns_moving(add_ref, add_buf, sems.at[1])
    going = []
    for s, part in blocks(w_ref.shape[1]):
        coming_w[s].wait()
        coming_a[s].wait()
        out_buf[:, part] = add_buf[:, part].astype(f32) + dot(dy_ref[...], w_buf[:, part])
        going.append(moving(out_buf.at[:, part], out_ref.at[:, part], sems.at[2, s]))
    for copy in going:
        copy.wait()


def input_backward(dy, weight, add, token):
    n, wide = add.shape
    return call(
        input_backward_body,
        (dy, weight, add),
        "vhh",
        (shaped(n, wide),),
        "h",
        5,
        20,
        [VMEM(weight.shape, bf16), VMEM((n, wide), bf16), VMEM((n, wide), f32), DMA((3, wide // STEP))],
        token=token,
    )


def hidden_backward_body(
    own_ref, near_ref, up_ref, down_ref, y_ref, par_ref, mask_ref, dt_ref, stat_ref
):
    batch, pixels, _ = own_ref.shape
    for b in range(batch):
        own, near, up, down = [ref[b].astype(f32) for ref in (own_ref, near_ref, up_ref, down_ref)]
        dt_ref[b * pixels : (b + 1) * pixels, :] = own + near + up + down
    grad = dt_ref[...]
    y = y_ref[...]
    dt = gelu_slope(normed(y, par_ref)) * (grad * mask_ref[:, 0:1])
    dt_ref[...] = dt
    write_stats(stat_ref, dt, normal_of(y, par_ref))


def hidden_backward(pieces, y, par, mask_wide, devices, through):
    n = y.shape[0]
    return call(
        hidden_backward_body,
        (*pieces, y, par, mask_wide),
        "v" * (len(pieces) + 3),
        (shaped(n, MID), shaped(devices, 8, 128)),
        "vv",
        3,
        16,
        through=through,
    )


def last_gradient_body(
    dt_ref, y_ref, par_ref, back_ref, mask_ref, acts_ref, dy_ref, send_ref, keep_ref,
    dyt_ref, acts_buf, out_buf, in_sems, out_sems
):
    coming = columns_moving(acts_ref, acts_buf, in_sems)
    dy = norm_gradient(dt_ref[...], y_ref[...], par_ref, back_ref, mask_ref[:, 0:1]).astype(bf16)
    dy_ref[...] = dy
    dyt_ref[...] = dy.astype(f32).T.astype(bf16)
    core = lax.axis_index("ch") % 2
    half, base = send_ref.shape[0], send_ref.shape[1]
    going = []
    for s, part in blocks(acts_ref.shape[1]):
        coming[s].wait()
        out_buf[:, part] = dot(dyt_ref[...], acts_buf[:, part]).astype(bf16)
        for q in range(half):
            for t, (out_ref, side) in enumerate(((send_ref, 1 - core), (keep_ref, core))):
                row = pl.multiple_of((2 * q + side) * base, 16)
                going.append(
                    moving(
                        out_buf.at[pl.ds(row, base), part], out_ref.at[q, :, part], out_sems.at[s, q, t]
                    )
                )
    for copy in going:
        copy.wait()


def last_gradient(dt, y, par, back, mask_wide, acts, ch, through):
    n, wide = acts.shape
    half = shaped(ch // 2, MID // ch, wide, dtype=bf16)
    return call(
        last_gradient_body,
        (dt, y, par, back, mask_wide, acts),
        "vvvvvh",
        (shaped(n, MID, dtype=bf16), half, half),
        "vhh",
        6,
        20,
        [
            VMEM((MID, n), bf16),
            VMEM((n, wide), bf16),
            VMEM((MID, wide), bf16),
            DMA((wide // STEP,)),
            DMA((wide // STEP, ch // 2, 2)),
        ],
        through=through,
    )


def cast_body(v_ref, out_ref):
    out_ref[...] = v_ref[...].astype(bf16)


def cast_after(values, *after):
    return call(cast_body, (values,), "v", (shaped(*values.shape, dtype=bf16),), "v", 2, 12, after=after)[0]


def pack_body(*refs, count, bit_axis, rows):
    part_refs, (send_ref, keep_ref), refs = refs[:count], refs[count : count + 2], refs[count + 2 :]
    buffers, (in_sem, out_sem) = refs[:count], refs[count:]
    coming = [moving(ref, buf, in_sem.at[t]) for t, (ref, buf) in enumerate(zip(part_refs, buffers))]
    bit = lax.axis_index(bit_axis) % 2
    tall = send_ref.shape[1]
    base = rows * tall
    going, at = [], 0
    for copy, buf in zip(coming, buffers):
        copy.wait()
        wide = buf.shape[1]
        for block in range(buf.shape[0] // base):
            for pair in range(rows // 2):
                for out_ref, side in ((send_ref, 1 - bit), (keep_ref, bit)):
                    row = pl.multiple_of(block * base + (2 * pair + side) * tall, 16)
                    going.append(
                        moving(
                            buf.at[pl.ds(row, tall), :],
                            out_ref.at[pair, :, at : at + wide],
                            out_sem.at[len(going)],
                        )
                    )
            at += wide
    for copy in going:
        copy.wait()


def pack_split(parts, base, rows, token=None):
    count = len(parts)
    blocks_in = sum(p.shape[0] // base for p in parts)
    wide = sum(p.shape[0] // base * p.shape[1] for p in parts)
    half = shaped(rows // 2, base // rows, wide, dtype=bf16)
    return call(
        functools.partial(pack_body, count=count, bit_axis="rows", rows=rows),
        tuple(parts),
        "h" * count,
        (half, half),
        "hh",
        3,
        16,
        [VMEM(p.shape, bf16) for p in parts] + [DMA((count,)), DMA((blocks_in * rows,))],
        token=token,
    )


def step_body(got_ref, kept_ref, send_ref, keep_ref, sum_ref, *, axis, step):
    bit = lax.axis_index(axis) // step % 2
    sum_ref[...] = (got_ref[...].astype(f32) + kept_ref[...].astype(f32)).astype(bf16)
    for pair in range(send_ref.shape[0]):
        send_ref[pair] = sum_ref[2 * pair + 1 - bit]
        keep_ref[pair] = sum_ref[2 * pair + bit]


def step_split(got, kept, axis, step, token=None):
    half = shaped(got.shape[0] // 2, *got.shape[1:], dtype=bf16)
    return call(
        functools.partial(step_body, axis=axis, step=step),
        (got, kept),
        "vv",
        (half, half),
        "vv",
        2,
        12,
        [VMEM(got.shape, bf16)],
        token=token,
    )


def sum_body(got_ref, kept_ref, sum_ref):
    sum_ref[...] = (got_ref[...].astype(f32) + kept_ref[...].astype(f32)).astype(bf16)


def step_sum(got, kept, token=None):
    return call(sum_body, (got, kept), "vv", (shaped(*got.shape, dtype=bf16),), "v", 1, 12, token=token)


def join_body(got_ref, kept_ref, out_ref, *, step):
    bit = lax.axis_index("rows") // step % 2
    for a in range(got_ref.shape[0]):
        out_ref[2 * a + bit] = kept_ref[a]
        out_ref[2 * a + 1 - bit] = got_ref[a]


def join_step(got, kept, step, token=None):
    m, r, wide = got.shape
    return call(
        functools.partial(join_body, step=step),
        (got, kept),
        "vv",
        (shaped(2 * m, r, wide, dtype=bf16),),
        "v",
        1,
        12,
        token=token,
    )


def final_body(got_ref, kept_ref, *refs, cuts):
    out_refs, refs = refs[: len(cuts)], refs[len(cuts) :]
    buffers, sems = refs[: len(cuts)], refs[len(cuts)]
    bit = lax.axis_index("rows") % 2
    going, at = [], 0
    for out_ref, buf, (count, wide) in zip(out_refs, buffers, cuts):
        for k in range(count):
            part = slice(at, at + wide)
            for a in range(got_ref.shape[0]):
                buf[k, 2 * a + bit] = kept_ref[a, :, part].astype(f32)
                buf[k, 2 * a + 1 - bit] = got_ref[a, :, part].astype(f32)
            going.append(moving(buf.at[k], out_ref.at[k], sems.at[len(going)]))
            at += wide
    for copy in going:
        copy.wait()


def final_join(got, kept, cuts, token):
    m, r, _ = got.shape
    outs = [shaped(count, 2 * m, r, wide) for count, wide in cuts]
    *outs, token = call(
        functools.partial(final_body, cuts=cuts),
        (got, kept),
        "vv",
        outs,
        "h" * len(outs),
        2,
        20,
        [VMEM(o.shape, f32) for o in outs] + [DMA((sum(count for count, _ in cuts),))],
        token=token,
    )
    return [o.reshape(-1, o.shape[3]) for o in outs], token


def owned_body(*refs):
    n = len(refs) // 3
    for k in range(n):
        size = refs[n + 2 * k].shape[1]
        start = lax.axis_index("ch") * size
        turned = pltpu.roll(refs[k][...], refs[k].shape[1] - start, 1)
        refs[n + 2 * k][...] = turned[0:1, :size]
        refs[n + 2 * k + 1][...] = turned[1:2, :size]


def owned(sums, ch):
    outs = [shaped(1, s.shape[1] // ch) for s in sums for _ in range(2)]
    outs = call(owned_body, tuple(sums), "v" * len(sums), outs, "v" * len(outs), 1, 12)
    return [o.reshape(-1) for o in outs]


def return_body(far_up_ref, up_ref, down_ref, far_down_ref, got_ref, below_ref, above_ref, partner_ref):
    odd = lax.axis_index("rows") % 2 == 1

    @pl.when(odd)
    def _():
        below_ref[...] = (far_up_ref[...].astype(f32) + got_ref[...].astype(f32)).astype(bf16)
        above_ref[...] = far_down_ref[...]
        partner_ref[...] = up_ref[...]

    @pl.when(jnp.logical_not(odd))
    def _():
        below_ref[...] = far_up_ref[...]
        above_ref[...] = (far_down_ref[...].astype(f32) + got_ref[...].astype(f32)).astype(bf16)
        partner_ref[...] = down_ref[...]


def return_step(far_up, up, down, far_down, got, through):
    piece = shaped(*got.shape, dtype=bf16)
    return call(
        return_body,
        (far_up, up, down, far_down, got),
        "vvvvv",
        (piece, piece, piece),
        "vvv",
        2,
        16,
        through=through,
    )


def shift_lanes(values, by, width):
    place = lax.broadcasted_iota(jnp.int32, values.shape, values.ndim - 1) % width
    moved = pltpu.roll(values, by % values.shape[-1], values.ndim - 1)
    return jnp.where((place >= by) & (place < width + by), moved, 0.0)


def shift_rows(values, by, width):
    place = lax.broadcasted_iota(jnp.int32, values.shape, 0) % width
    moved = pltpu.roll(values, by % values.shape[0], 0)
    return jnp.where((place >= by) & (place < width + by), moved, 0.0)


def offset_fraction(ext_ref, ow_ref, b, base, pixels, width):
    u = None
    for i in range(3):
        start = (base + 2 * i) * width
        term = dot(ow_ref[i], ext_ref[b, start : start + pixels, :], NT)
        u = term if u is None else u + term
    total = u[32:64]
    total = total + shift_lanes(u[0:32], 2, width) + shift_lanes(u[64:96], -2, width)
    return 1.0 / (1.0 + jnp.exp(-total))


def deform_forward_body(*refs, batch, rows, width, deep):
    tile_refs, refs = refs[:5], refs[5:]
    ow_ref, disp_ref, m_ref, mask_ref, cols_out_ref, y_ref, frac_ref, stat_ref = refs[:8]
    ext_ref, par_ref, s_ref, cols_ref, m_buf, tile_sems, sems = refs[8:]
    pixels = rows * width
    coming = [
        moving(ref, ext_ref.at[:, t * pixels : (t + 1) * pixels, :], tile_sems.at[t])
        for t, ref in enumerate(tile_refs)
    ]
    coming_m = moving(m_ref, m_buf, sems.at[0])
    for copy in coming:
        copy.wait()
    lane = lax.broadcasted_iota(jnp.int32, (32, 128), 1)
    column = lane % width
    upper = lane // width

    def image(b, carry):
        frac = offset_fraction(ext_ref, ow_ref, b, deep - 2, pixels, width)
        for i in range(4):
            frac_ref[b, i] = frac[i * 8 : i * 8 + 8]
        pix = lax.broadcasted_iota(jnp.int32, (1, pixels), 1)
        row_at, col_at = pix // width, pix % width
        tops, lefts, ys, xs = [], [], [], []
        for k in range(9):
            i, j = k // 3, k % 3
            tops.append(row_at + disp_ref[b, i, 2 * j : 2 * j + 1, :] + (deep - 2))
            lefts.append(col_at + 2 * (j - 1) + disp_ref[b, i, 2 * j + 1 : 2 * j + 2, :])
            at = i * 8 + 2 * j
            ys.append(frac[at : at + 1])
            xs.append(frac[at + 1 : at + 2])
        blank = jnp.zeros((23, pixels), f32)
        par = jnp.concatenate(
            [jnp.concatenate(g, axis=0).astype(f32) if g is not None else blank
             for g in (tops, None, lefts, None, ys, None, xs, None)], axis=0)
        par_ref[...] = par.T

        def row_of_taps(i, carry):
            for j in range(3):
                k = i * 3 + j
                for c in range(pixels // 32):
                    p = pltpu.roll(par_ref[c * 32 : c * 32 + 32, :], 128 - k, 1)
                    wide = (32, 128)
                    top = jnp.broadcast_to(p[:, 0:1], wide).astype(jnp.int32) - upper
                    left = jnp.broadcast_to(p[:, 32:33], wide).astype(jnp.int32)
                    fy = jnp.broadcast_to(p[:, 64:65], wide)
                    fx = jnp.broadcast_to(p[:, 96:97], wide)
                    cw = jnp.where(column == left, 1.0 - fx, jnp.where(column == left + 1, fx, 0.0))
                    ca, cb = (1.0 - fy) * cw, fy * cw
                    for q in range(8):
                        s = jnp.where(top == 2 * q, ca, jnp.where(top == 2 * q - 1, cb, 0.0))
                        s_ref[j * pixels + c * 32 : j * pixels + c * 32 + 32, q * 128 : q * 128 + 128] = s.astype(bf16)
            start = pl.multiple_of(i * 2 * width, 128)
            window = ext_ref[b, pl.ds(start, 16 * width), :]
            for j in range(3):
                got = dot(s_ref[j * pixels : (j + 1) * pixels, :], window).astype(bf16)
                cols_ref[pl.ds(pl.multiple_of(b * pixels, pixels), pixels), pl.ds(pl.multiple_of((i * 3 + j) * MID, MID), MID)] = got
            return carry

        return lax.fori_loop(0, 3, row_of_taps, carry)

    lax.fori_loop(0, batch, image, 0)
    going = moving(cols_ref, cols_out_ref, sems.at[1])
    coming_m.wait()
    y = dot(cols_ref[...], m_buf[...], NT)
    y_ref[...] = y
    write_stats(stat_ref, y * mask_ref[:, 0:1], y)
    going.wait()


def deform_forward(tiles, offset_rows, disp, weight, mask_wide, rows, width, devices):
    batch = tiles[0].shape[0]
    pixels = rows * width
    n = batch * pixels
    return call(
        functools.partial(deform_forward_body, batch=batch, rows=rows, width=width, deep=2 * rows),
        (*tiles, offset_rows, disp, weight, mask_wide),
        "hhhhhvvhv",
        (
            shaped(n, 9 * MID, dtype=bf16),
            shaped(n, MID),
            shaped(batch, 4, 8, pixels),
            shaped(devices, 8, 128),
        ),
        "hvvv",
        15,
        30,
        [
            VMEM((batch, 5 * pixels, MID), bf16),
            VMEM((pixels, 128), f32),
            VMEM((3 * pixels, 16 * width), bf16),
            VMEM((n, 9 * MID), bf16),
            VMEM(weight.shape, bf16),
            DMA((5,)),
            DMA((2,)),
        ],
    )


def deform_backward_body(*refs, batch, rows, width, deep):
    tile_refs, refs = refs[:5], refs[5:]
    (ow_ref, disp_ref, frac_ref, m_ref, dy_ref), refs = refs[:5], refs[5:]
    out_refs, refs = refs[:5], refs[5:]
    dow_ref, ext_ref, dext_ref, dc_ref, g_ref, st_ref, df_ref, m_buf, tile_sems, m_sem = refs
    pixels = rows * width
    coming = [
        moving(ref, ext_ref.at[:, t * pixels : (t + 1) * pixels, :], tile_sems.at[t])
        for t, ref in enumerate(tile_refs)
    ]
    coming_m = moving(m_ref, m_buf, m_sem)
    window = 16 * width
    dow_ref[...] = jnp.zeros_like(dow_ref)
    dext_ref[...] = jnp.zeros_like(dext_ref)
    for copy in coming:
        copy.wait()
    coming_m.wait()

    def image(b, carry):
        at = pl.multiple_of(b * pixels, pixels)

        def row_of_taps(i, carry):
            dy = dy_ref[pl.ds(at, pixels), :]
            for j in range(3):
                m = m_buf[:, pl.ds(pl.multiple_of((i * 3 + j) * MID, MID), MID)]
                dc_ref[j * pixels : (j + 1) * pixels, :] = dot(dy, m).astype(bf16)
            start = pl.multiple_of(i * 2 * width, 128)
            g_ref[...] = dot(ext_ref[b, pl.ds(start, window), :], dc_ref[...], NT)
            place = lax.broadcasted_iota(jnp.int32, (width, 128), 0)
            for j in range(3):
                for h in range(pixels // 128):
                    lanes = slice(h * 128, h * 128 + 128)
                    at_l = slice(j * pixels + h * 128, j * pixels + h * 128 + 128)
                    pix = lax.broadcasted_iota(jnp.int32, (1, 128), 1) + h * 128
                    by_y, by_x = slice(2 * j, 2 * j + 1), slice(2 * j + 1, 2 * j + 2)
                    top = pix // width + disp_ref[b, i, by_y, lanes] + (deep - 2)
                    left = pix % width + 2 * (j - 1) + disp_ref[b, i, by_x, lanes]
                    fy = frac_ref[b, i, by_y, lanes]
                    fx = frac_ref[b, i, by_x, lanes]
                    here, after = place == left, place == left + 1
                    cw = jnp.where(here, 1.0 - fx, jnp.where(after, fx, 0.0))
                    ca, cb = (1.0 - fy) * cw, fy * cw
                    low_sum = jnp.zeros((width, 128), f32)
                    high_sum = jnp.zeros((width, 128), f32)
                    for r in range(16):
                        part = slice(r * width, r * width + width)
                        g = g_ref[part, at_l]
                        m0, m1 = top == r, top == r - 1
                        low_sum = low_sum + jnp.where(m0, g, 0.0)
                        high_sum = high_sum + jnp.where(m1, g, 0.0)
                        st_ref[part, at_l] = jnp.where(m0, ca, jnp.where(m1, cb, 0.0)).astype(bf16)
                    d_fy = jnp.sum((high_sum - low_sum) * cw, axis=0, keepdims=True)
                    mixed = (1.0 - fy) * low_sum + fy * high_sum
                    d_fx = jnp.sum(
                        jnp.where(after, mixed, 0.0) - jnp.where(here, mixed, 0.0), axis=0, keepdims=True)
                    df_ref[i, by_y, lanes] = d_fy * fy * (1.0 - fy)
                    df_ref[i, by_x, lanes] = d_fx * fx * (1.0 - fx)
            dext_ref[b, pl.ds(start, window), :] += dot(st_ref[...], dc_ref[...])
            return carry

        df_ref[...] = jnp.zeros_like(df_ref)
        carry = lax.fori_loop(0, 3, row_of_taps, carry)
        d_off = df_ref[...].reshape(32, pixels).astype(bf16).astype(f32)
        stacked = jnp.concatenate(
            [shift_lanes(d_off, -2, width), d_off, shift_lanes(d_off, 2, width)], axis=0)
        across = jnp.concatenate([stacked, jnp.zeros((32, pixels), f32)], axis=0).T.astype(bf16)
        stacked = stacked.astype(bf16)
        for i in range(3):
            first = (deep - 2 + 2 * i) * width
            part = slice(first, first + pixels)
            dow_ref[i] += dot(stacked, ext_ref[b, part, :])
            dext_ref[b, part, :] += dot(across[:, :96], ow_ref[i])
        return carry

    lax.fori_loop(0, batch, image, 0)
    for t, ref in enumerate(out_refs):
        ref[...] = dext_ref[:, t * pixels : (t + 1) * pixels, :].astype(ref.dtype)


def deform_backward(tiles, offset_rows, disp, frac, weight, dy, rows, width, after, through):
    batch = tiles[0].shape[0]
    pixels = rows * width
    return call(
        functools.partial(deform_backward_body, batch=batch, rows=rows, width=width, deep=2 * rows),
        (*tiles, offset_rows, disp, frac, weight, dy),
        "hhhhhvvvhv",
        tuple(shaped(batch, pixels, MID, dtype=f32 if t == 2 else bf16) for t in range(5))
        + (shaped(3, 96, MID),),
        "vvvvvv",
        20,
        36,
        [
            VMEM((batch, 5 * pixels, MID), bf16),
            VMEM((batch, 5 * pixels, MID), f32),
            VMEM((3 * pixels, MID), bf16),
            VMEM((16 * width, 3 * pixels), f32),
            VMEM((16 * width, 3 * pixels), bf16),
            VMEM((4, 8, pixels), f32),
            VMEM(weight.shape, bf16),
            DMA((5,)),
            DMA,
        ],
        after,
        through,
    )


def taps_moving(m_ref, m_buf, sems):
    wide = 3 * MID
    return columns_moving(m_ref, m_buf, sems, wide)


def rim_moving(parts, rim_ref, sems):
    copies, at = [], 0
    for t, ref in enumerate(parts):
        copies.append(moving(ref, rim_ref.at[:, at : at + ref.shape[1], :], sems.at[t]))
        at += ref.shape[1]
    return copies


def conv_forward_body(
    above_ref, own_ref, below_ref, m_ref, mask_ref, y_ref, stat_ref, rim_ref, m_buf, rim_sems, sems,
    *, batch, rows, width
):
    pixels = rows * width
    coming = taps_moving(m_ref, m_buf, sems)
    for copy in rim_moving((above_ref, own_ref, below_ref), rim_ref, rim_sems):
        copy.wait()
    sums = [[None] * 3 for _ in range(batch)]
    for i in range(3):
        coming[i].wait()
        for b in range(batch):
            for j in range(3):
                k = i * 3 + j
                start = 2 * i * width
                term = dot(rim_ref[b, start : start + pixels, :], m_buf[:, k * MID : (k + 1) * MID], NT)
                sums[b][j] = term if i == 0 else sums[b][j] + term
    for b in range(batch):
        total = sums[b][1] + shift_rows(sums[b][0], 2, width) + shift_rows(sums[b][2], -2, width)
        y_ref[b * pixels : (b + 1) * pixels, :] = total
    y = y_ref[...]
    write_stats(stat_ref, y * mask_ref[:, 0:1], y)


def conv_forward(rim, weight, mask_wide, rows, width, devices):
    batch = rim[0].shape[0]
    n = batch * rows * width
    return call(
        functools.partial(conv_forward_body, batch=batch, rows=rows, width=width),
        (*rim, weight, mask_wide),
        "hhhhv",
        (shaped(n, MID), shaped(devices, 8, 128)),
        "vv",
        5,
        24,
        [VMEM((batch, (rows + 4) * width, MID), bf16), VMEM(weight.shape, bf16), DMA((3,)), DMA((3,))],
    )


def conv_backward_body(
    above_ref, own_ref, below_ref, m_ref, y_ref, par_ref, mask_ref, dt_ref, stat_ref,
    rim_ref, m_buf, rim_sems, sems, *, batch, rows, width
):
    pixels = rows * width
    coming = taps_moving(m_ref, m_buf, sems)
    for copy in rim_moving((above_ref, own_ref, below_ref), rim_ref, rim_sems):
        copy.wait()
    sums = [[None] * 3 for _ in range(batch)]
    for i in range(3):
        coming[i].wait()
        for b in range(batch):
            for j in range(3):
                k = i * 3 + j
                start = (4 - 2 * i) * width
                term = dot(rim_ref[b, start : start + pixels, :], m_buf[:, k * MID : (k + 1) * MID])
                sums[b][j] = term if i == 0 else sums[b][j] + term
    for b in range(batch):
        total = sums[b][1] + shift_rows(sums[b][0], -2, width) + shift_rows(sums[b][2], 2, width)
        dt_ref[b * pixels : (b + 1) * pixels, :] = total
    y = y_ref[...]
    dt = gelu_slope(normed(y, par_ref)) * (dt_ref[...] * mask_ref[:, 0:1])
    dt_ref[...] = dt
    write_stats(stat_ref, dt, normal_of(y, par_ref))


def conv_backward(rim, weight, y, par, mask_wide, rows, width, devices, after):
    batch = rim[0].shape[0]
    n = batch * rows * width
    return call(
        functools.partial(conv_backward_body, batch=batch, rows=rows, width=width),
        (*rim, weight, y, par, mask_wide),
        "hhhhvvv",
        (shaped(n, MID), shaped(devices, 8, 128)),
        "vv",
        6,
        24,
        [VMEM((batch, (rows + 4) * width, MID), bf16), VMEM(weight.shape, bf16), DMA((3,)), DMA((3,))],
        after,
    )


def conv_weight_body(
    dy_ref, above_ref, own_ref, below_ref, out_ref, rim_ref, dyt_ref, out_buf, rim_sems, sems,
    *, batch, rows, width
):
    pixels = rows * width
    coming = rim_moving((above_ref, own_ref, below_ref), rim_ref, rim_sems)
    dy = dy_ref[...].astype(f32)
    going = []
    for j in range(3):
        moved = shift_rows(dy, 2 * (j - 1), width) if j != 1 else dy
        dyt_ref[j] = moved.T.astype(bf16)
        if j == 0:
            for copy in coming:
                copy.wait()
        for i in range(3):
            part = slice((i * 3 + j) * MID, (i * 3 + j + 1) * MID)
            start = 2 * i * width
            total = None
            for b in range(batch):
                term = dot(dyt_ref[j, :, b * pixels : (b + 1) * pixels], rim_ref[b, start : start + pixels, :])
                total = term if total is None else total + term
            out_buf[:, part] = total.astype(bf16)
            going.append(moving(out_buf.at[:, part], out_ref.at[:, part], sems.at[i * 3 + j]))
    for copy in going:
        copy.wait()


def conv_weight_gradient(dy, rim, rows, width, after):
    batch = rim[0].shape[0]
    return call(
        functools.partial(conv_weight_body, batch=batch, rows=rows, width=width),
        (dy, *rim),
        "vhhh",
        (shaped(MID, 9 * MID, dtype=bf16),),
        "h",
        6,
        20,
        [
            VMEM((batch, (rows + 4) * width, MID), bf16),
            VMEM((3, MID, batch * rows * width), bf16),
            VMEM((MID, 9 * MID), bf16),
            DMA((3,)),
            DMA((9,)),
        ],
        after,
    )[0]


def columns_weight_body(dy_ref, cols_ref, out_ref, dyt_ref, cols_buf, out_buf, sems):
    coming = columns_moving(cols_ref, cols_buf, sems.at[0])
    dyt_ref[...] = dy_ref[...].astype(f32).T.astype(bf16)
    going = []
    for s, part in blocks(cols_ref.shape[1]):
        coming[s].wait()
        out_buf[:, part] = dot(dyt_ref[...], cols_buf[:, part]).astype(bf16)
        going.append(moving(out_buf.at[:, part], out_ref.at[:, part], sems.at[1, s]))
    for copy in going:
        copy.wait()


def columns_weight_gradient(dy, cols, through):
    n, wide = cols.shape
    return call(
        columns_weight_body,
        (dy, cols),
        "vh",
        (shaped(MID, wide, dtype=bf16),),
        "h",
        6,
        20,
        [VMEM((MID, n), bf16), VMEM((n, wide), bf16), VMEM((MID, wide), bf16), DMA((2, wide // STEP))],
        through=through,
    )


TILES = 2
EPSILON = 1e-05


def swap_with(values, axis, step):
    return lax.ppermute(values, axis, [(i, i ^ step) for i in range(lax.axis_size(axis))])


def from_behind(block, axis, distance):
    devices = range(lax.axis_size(axis))
    route = [(i - distance, i) for i in devices if i - distance in devices]
    return lax.ppermute(block, axis, route)


def ladder_sum(values, axis):
    step = 1
    while step < lax.axis_size(axis):
        got = swap_with(values.astype(bf16), axis, step)
        values = values + got.astype(f32)
        step *= 2
    return values


def to_everyone(spread, groups=None):
    return lax.all_to_all(spread, ("rows", "ch"), 0, 0, axis_index_groups=groups, tiled=True)


def small_total(spread):
    return jnp.sum(to_everyone(spread), axis=0).reshape(2, -1)


def wide_total(block):
    devices = lax.axis_size("rows") * lax.axis_size("ch")
    core = lax.axis_index("ch") % 2
    above, below = block.reshape(2, -1, 128)
    half = jnp.where(core == 0, above, below) + swap_with(jnp.where(core == 0, below, above), "ch", 1)
    groups = [[i * 2 + k for i in range(devices // 2)] for k in range(2)]
    half = jnp.broadcast_to(half[None], (devices // 2,) + half.shape)
    half = jnp.sum(to_everyone(half, groups), axis=0)
    other = swap_with(half, "ch", 1)
    whole = jnp.stack([jnp.where(core == 0, half, other), jnp.where(core == 0, other, half)])
    whole = whole.reshape(-1, 2, STEP)
    return whole[:, 0].reshape(-1), whole[:, 1].reshape(-1)


def forward_rows(sums, gain, shift, count):
    mean = sums[0] / count
    scale = lax.rsqrt(sums[1] / count - mean * mean + EPSILON)
    return jnp.stack([scale * gain, shift - mean * scale * gain, scale, -mean * scale])


def backward_rows(sums, par, count):
    rows = jnp.stack([par[0], par[0] * sums[0] / count, par[0] * sums[1] / count])
    return rows, jnp.stack([sums[1], sums[0]])


def gather_weight(weight):
    return lax.all_gather(weight.astype(bf16), "ch", axis=0, tiled=True)


def gather_weight_after(weight, *after):
    return lax.all_gather(cast_after(weight, *after), "ch", axis=0, tiled=True)


def gather_by_swaps(weight):
    ch = lax.axis_size("ch")
    came = None
    held = weight.astype(bf16)[None]
    step = ch // 2
    while step >= 1:
        got = swap_with(held, "ch", step)
        came = got if came is None else came
        odd = lax.axis_index("ch") // step % 2 == 1
        held = jnp.stack([jnp.where(odd, got, held), jnp.where(odd, held, got)], axis=1)
        held = held.reshape((-1,) + held.shape[2:])
        step //= 2
    return held.reshape((-1,) + weight.shape[1:]), came


def pick(values, bit):
    return lax.dynamic_index_in_dim(values, bit, 1, keepdims=False)


def scatter_ch(gradient):
    return lax.psum_scatter(gradient, "ch", scatter_dimension=0, tiled=True)


def split(total, axis, step):
    bit = lax.axis_index(axis) // step % 2
    pairs = total.reshape((total.shape[0] // 2, 2) + total.shape[1:])
    return swap_with(pick(pairs, 1 - bit), axis, step), pick(pairs, bit)


def added(pair):
    got, kept = pair
    return (got.astype(f32) + kept.astype(f32)).astype(bf16)


def rest_of(total, axis, step=1):
    while step < lax.axis_size(axis):
        total = added(split(total, axis, step))
        step *= 2
    return total


def by_owner(gradient, axis="ch"):
    count = lax.axis_size(axis)
    return gradient.reshape((count, gradient.shape[0] // count) + gradient.shape[1:])


def wide_enough(base):
    return base // lax.axis_size("rows") % 16 == 0


def first_step(parts, base, token=None):
    if wide_enough(base):
        send, keep, *token = pack_split(parts, base, lax.axis_size("rows"), token)
        return (swap_with(send, "rows", 1), keep, *token)
    laid = [jnp.concatenate([p[r : r + base] for r in range(0, p.shape[0], base)], axis=1) for p in parts]
    pair = split(by_owner(jnp.concatenate(laid, axis=1), "rows"), "rows", 1)
    return pair if token is None else (*pair, token)


def next_step(got, kept, step, axis="rows", token=None):
    send, keep, *token = step_split(got, kept, axis, step, token)
    return (swap_with(send, axis, step), keep, *token)


def last_steps(got, kept, step, axis):
    while step < lax.axis_size(axis):
        got, kept = next_step(got, kept, step, axis)
        step *= 2
    return step_sum(got, kept)[0]


class Ladder:
    def __init__(self, got, kept, step=2):
        self.got, self.kept, self.step, self.up = got, kept, step, True

    def advance(self, token=None):
        if self.ready():
            return (token,)
        last = lax.axis_size("rows") // 2
        if self.up and self.step <= last:
            self.got, self.kept, *token = next_step(self.got, self.kept, self.step, "rows", token)
            self.step *= 2
            return token
        if self.up:
            self.kept, *token = step_sum(self.got, self.kept, token)
            self.up, self.step = False, last
        else:
            self.kept, *token = join_step(self.got, self.kept, self.step, token)
            self.step //= 2
        self.got = swap_with(self.kept, "rows", self.step)
        return token

    def ready(self):
        return not self.up and self.step == 1

    def finish(self, cuts, token):
        while not self.ready():
            (token,) = self.advance(token)
        return final_join(self.got, self.kept, cuts, token)


def deep_rows(tile):
    odd = lax.axis_index("rows") % 2 == 1
    far_up = from_behind(tile, "rows", 2)
    far_down = from_behind(tile, "rows", -2)
    near = swap_with(tile, "rows", 1)
    other = swap_with(jnp.where(odd, far_up, far_down), "rows", 1)
    return far_up, jnp.where(odd, near, other), tile, jnp.where(odd, other, near), far_down


def near_rows(tile, width):
    size = 2 * width
    above = from_behind(tile[:, -size:], "rows", 1)
    below = from_behind(tile[:, :size], "rows", -1)
    return above, tile, below


def per_device(
    inputs,
    heights,
    displacements,
    reduce_one,
    reduce_gain_one,
    reduce_bias_one,
    offset_weight,
    deform_weight,
    deform_gain,
    deform_bias,
    expand_one,
    expand_gain_one,
    expand_bias_one,
    reduce_two,
    reduce_gain_two,
    reduce_bias_two,
    conv_weight,
    conv_gain,
    conv_bias,
    expand_two,
    expand_gain_two,
    expand_bias_two,
    cotangent,
):
    batch, rows, width, channels = inputs.shape
    pixels = rows * width
    n = batch * pixels
    own_heights = lax.dynamic_slice_in_dim(heights, lax.axis_index("ch") * batch, batch)
    rows_here = lax.axis_index("rows") * rows + jnp.arange(rows, dtype=jnp.int32)
    mask = (rows_here[None, :] < own_heights[:, None]).astype(f32)
    mask = jnp.broadcast_to(mask[:, :, None], (batch, rows, width)).reshape(n, 1)
    mask_wide = jnp.broadcast_to(mask, (n, 128))
    count = jnp.sum(heights).astype(f32) * width

    offset_rows = offset_weight.astype(bf16).reshape(3, 6, 3, 3, MID).transpose(2, 3, 0, 1, 4)
    offset_rows = jnp.pad(offset_rows, ((0, 0), (0, 0), (0, 1), (0, 2), (0, 0))).reshape(3, 96, MID)
    disp = jnp.pad(displacements.reshape(3, 6, batch, pixels), ((0, 0), (0, 2), (0, 0), (0, 0)))
    disp = disp.transpose(2, 0, 1, 3)

    reduce_full, came = gather_by_swaps(reduce_one)
    deform_full = gather_weight_after(deform_weight, came)
    expand_full, reduce_full_two, conv_full, expand_full_two = [
        gather_weight(w) for w in (expand_one, reduce_two, conv_weight, expand_two)
    ]

    devices = lax.axis_size("rows") * lax.axis_size("ch")
    acts = inputs.reshape(n, channels)
    acts_low, y_a, spread = product_forward(acts, mask_wide, reduce_full, devices)
    par_a = forward_rows(small_total(spread), reduce_gain_one, reduce_bias_one, count)
    hidden = (gelu(y_a * par_a[0] + par_a[1]) * mask).astype(bf16)
    near_tiles = deep_rows(hidden.reshape(batch, pixels, MID))
    columns, y_b, fraction, spread = deform_forward(
        near_tiles, offset_rows, disp, deform_full, mask_wide, rows, width, devices
    )
    par_b = forward_rows(small_total(spread), deform_gain, deform_bias, count)
    middle, y_c, block = expand_forward([y_b], par_b, mask_wide, expand_full)
    par_c = forward_rows(wide_total(block), expand_gain_one, expand_bias_one, count)

    first_low, y_d, spread = first_forward(y_c, par_c, acts, mask_wide, reduce_full_two, devices)
    par_d = forward_rows(small_total(spread), reduce_gain_two, reduce_bias_two, count)
    hidden_two = (gelu(y_d * par_d[0] + par_d[1]) * mask).astype(bf16)
    rimmed = near_rows(hidden_two.reshape(batch, pixels, MID), width)
    y_e, spread = conv_forward(rimmed, conv_full, mask_wide, rows, width, devices)
    par_e = forward_rows(small_total(spread), conv_gain, conv_bias, count)
    middle_two, y_f, block = expand_forward([y_e], par_e, mask_wide, expand_full_two)
    par_f = forward_rows(wide_total(block), expand_gain_two, expand_bias_two, count)

    output, dt_f, block = output_stage(y_f, par_f, first_low, cotangent.reshape(n, channels), mask_wide)
    back_f, sums_f = backward_rows(wide_total(block), par_f, count)
    dy_f, dt_e, spread = expand_backward(
        dt_f, y_f, par_f, back_f, mask_wide, expand_full_two, y_e, par_e, devices
    )
    expand_two_local = dot(dy_f, middle_two, TN).astype(bf16)
    expand_two_part = scatter_ch(expand_two_local)
    back_e, sums_e = backward_rows(small_total(spread), par_e, count)
    dy_e = norm_gradient(dt_e, y_e, par_e, back_e, mask).astype(bf16)
    dy_e_rim = near_rows(dy_e.reshape(batch, pixels, MID), width)
    conv_local = conv_weight_gradient(dy_e, rimmed, rows, width, (expand_two_local,))
    conv_part = scatter_ch(conv_local)
    dt_d, spread = conv_backward(
        dy_e_rim, conv_full, y_d, par_d, mask_wide, rows, width, devices, (conv_local,)
    )
    base = conv_part.shape[0]
    back_d, sums_d = backward_rows(small_total(spread), par_d, count)
    dy_d, dt_c, block = residual_backward(
        dt_d, y_d, par_d, back_d, mask_wide, reduce_full_two, dt_f, y_c, par_c, acts_low
    )
    reduce_two_local = dot(dy_d, first_low, TN).astype(bf16)

    back_c, sums_c = backward_rows(wide_total(block), par_c, count)
    red_two = split(by_owner(reduce_two_local), "ch", 1)
    dy_c, dt_b, spread, kept = expand_backward(
        dt_c, y_c, par_c, back_c, mask_wide, expand_full, y_b, par_b, devices, (red_two[1],)
    )
    red_two = next_step(red_two[0], kept, 2, "ch")
    expand_one_local = dot(dy_c, middle, TN).astype(bf16)
    exp_one = split(by_owner(expand_one_local), "ch", 1)
    back_b, sums_b = backward_rows(small_total(spread), par_b, count)
    dy_b = norm_gradient(dt_b, y_b, par_b, back_b, mask).astype(bf16)
    sum_p = Ladder(*first_step([conv_part, expand_two_part], base))
    deform_local, reduce_two_kept, expand_one_kept = columns_weight_gradient(
        dy_b, columns, (red_two[1], exp_one[1])
    )
    deform_part = scatter_ch(deform_local)
    exp_one = next_step(exp_one[0], expand_one_kept, 2, "ch")
    far_up, up, own, down, far_down, offset_local, reduce_two_kept, expand_one_kept, sum_p.kept = deform_backward(
        near_tiles, offset_rows, disp, fraction, deform_full, dy_b, rows, width,
        (), (reduce_two_kept, exp_one[1], sum_p.kept),
    )
    odd = lax.axis_index("rows") % 2 == 1
    passed = swap_with(jnp.where(odd, down, up), "rows", 1)
    sum_p.advance()
    below, above, partner, sum_p.kept = return_step(far_up, up, down, far_down, passed, (sum_p.kept,))
    below, above = from_behind(below, "rows", -2), from_behind(above, "rows", 2)
    partner = swap_with(partner, "rows", 1)
    dt_a, spread, sum_p.kept, reduce_two_kept, expand_one_kept = hidden_backward(
        (own, partner, below, above), y_a, par_a, mask_wide, devices,
        (sum_p.kept, reduce_two_kept, expand_one_kept),
    )
    sum_p.advance()
    reduce_two_part = last_steps(red_two[0], reduce_two_kept, 4, "ch")[0]
    expand_one_part = last_steps(exp_one[0], expand_one_kept, 4, "ch")[0]
    got_q, kept_q = first_step([reduce_two_part, expand_one_part], base)
    back_a, sums_a = backward_rows(small_total(spread), par_a, count)
    dy_a, send_s, kept_s, sum_p.kept, kept_q, deform_part, offset_local = last_gradient(
        dt_a, y_a, par_a, back_a, mask_wide, acts_low, lax.axis_size("ch"),
        (sum_p.kept, kept_q, deform_part, offset_local),
    )
    got_s = swap_with(send_s, "ch", 1)
    got_r, kept_r, token = first_step([deform_part], base, jnp.zeros((8, 128), f32))
    sum_q, sum_r = Ladder(got_q, kept_q), Ladder(got_r, kept_r)
    step = 2
    while step < lax.axis_size("ch"):
        got_s, kept_s, token = next_step(got_s, kept_s, step, "ch", token)
        step *= 2
    for ladder in (sum_p, sum_q):
        (token,) = ladder.advance(token)
    input_grad, token = input_backward(dy_a, reduce_full, dt_c, token)
    for ladder in (sum_q, sum_p, sum_r):
        (token,) = ladder.advance(token)
    offset_local = offset_local.reshape(3, 3, 4, 8, MID)[:, :, :3, :6]
    offset_local = offset_local.transpose(2, 3, 0, 1, 4).reshape(-1, MID)
    offset_part = ladder_sum(offset_local, "ch").astype(bf16)
    offset_part = jnp.pad(offset_part, ((0, -offset_part.shape[0] % base), (0, 0)))
    reduce_one_part = step_sum(got_s, kept_s)[0][0]
    got_s, kept_s, token = first_step([reduce_one_part, offset_part], base, token)
    sum_s = Ladder(got_s, kept_s)
    for ladder in (sum_q, sum_p, sum_q, sum_r, sum_s, sum_r, sum_q, sum_s, sum_r, sum_s):
        (token,) = ladder.advance(token)
    (conv_weight_grad, expand_two_grad), token = sum_p.finish(((1, 9 * MID), (channels // MID, MID)), token)
    for ladder in (sum_r, sum_s):
        (token,) = ladder.advance(token)
    (reduce_two_grad, expand_one_grad), token = sum_q.finish(((1, channels), (channels // MID, MID)), token)
    (token,) = sum_s.advance(token)
    (deform_weight_grad,), token = sum_r.finish(((1, 9 * MID),), token)
    (reduce_one_grad, offset_grad), token = sum_s.finish(
        ((1, channels), (offset_part.shape[0] // base, MID)), token
    )
    ends = owned((sums_a, sums_b, sums_c, sums_d, sums_e, sums_f), lax.axis_size("ch"))
    offset_weight_grad = offset_grad[:162].reshape(18, 9 * MID)
    reduce_gain_one_grad, reduce_bias_one_grad, deform_gain_grad, deform_bias_grad = ends[:4]
    expand_gain_one_grad, expand_bias_one_grad, reduce_gain_two_grad, reduce_bias_two_grad = ends[4:8]
    conv_gain_grad, conv_bias_grad, expand_gain_two_grad, expand_bias_two_grad = ends[8:]
    return (
        output.reshape(inputs.shape),
        input_grad.reshape(inputs.shape),
        reduce_one_grad,
        reduce_gain_one_grad,
        reduce_bias_one_grad,
        offset_weight_grad,
        deform_weight_grad,
        deform_gain_grad,
        deform_bias_grad,
        expand_one_grad,
        expand_gain_one_grad,
        expand_bias_one_grad,
        reduce_two_grad,
        reduce_gain_two_grad,
        reduce_bias_two_grad,
        conv_weight_grad,
        conv_gain_grad,
        conv_bias_grad,
        expand_two_grad,
        expand_gain_two_grad,
        expand_bias_two_grad,
    )


def solution(mesh):
    tiles = P("ch", "rows", None, None)
    owned = P("ch", None)
    block = (owned, P(), P())
    placed = (tiles, P(), P(None, "ch", "rows", None)) + block + (P(),) + 2 * block + 3 * block + (tiles,)
    grads = (owned, P("ch"), P("ch"))
    return jax.shard_map(
        per_device,
        mesh=mesh,
        in_specs=placed,
        out_specs=(tiles, tiles) + grads + (P(),) + 2 * grads + 3 * grads,
        check_vma=False,
    )
```

```python
import functools

import jax
import jax.numpy as jnp
from jax import lax
from jax.experimental import pallas as pl
from jax.experimental.pallas import tpu as pltpu
from jax.sharding import PartitionSpec as P

bf16 = jnp.bfloat16
f32 = jnp.float32
VMEM = pltpu.VMEM
HBM = pltpu.HBM
DMA = pltpu.SemaphoreType.DMA
MID = 512
STEP = 512
NT = (((1,), (1,)), ((), ()))
TN = (((0,), (0,)), ((), ()))
NN = (((1,), (0,)), ((), ()))
GELU_A = 0.7978845608028654
GELU_B = 0.044715


def dot(a, b, dims=NN):
    return lax.dot_general(a, b, dims, preferred_element_type=f32)


def shaped(*shape, dtype=f32):
    return jax.ShapeDtypeStruct(shape, dtype)


def without(body, n_in, n_order, n_out, n_through, token):
    first = n_in + n_order + n_through

    def inner(*refs):
        if token:
            refs[first + n_out + n_through][...] = jnp.zeros((8, 128), f32)
        body(*refs[:n_in], *refs[first : first + n_out], *refs[first + n_out + n_through + token :])

    return inner


def cost(us):
    return pl.CostEstimate(flops=int(us * 1.1e9), bytes_accessed=int(us * 2.2e6), transcendentals=0)


def call(body, operands, places, outs, out_places, us, limit, scratch=(), after=(), through=(), token=None):
    def spec(place):
        return pl.BlockSpec(memory_space=HBM if place == "h" else VMEM)

    def pinned(value, place):
        return pltpu.with_memory_space_constraint(value, HBM) if place == "h" else value

    def result(out, place):
        return HBM(out.shape, out.dtype) if place == "h" else out

    tokens = () if token is None else (token,)
    n_in, n_out, n_order = len(operands), len(outs), len(after) + len(tokens)
    return pl.pallas_call(
        without(body, n_in, n_order, n_out, len(through), len(tokens)),
        in_specs=[spec(p) for p in places] + [spec("h")] * len(after) + [spec("v")] * len(tokens)
        + [spec("h")] * len(through),
        out_specs=tuple(spec(p) for p in out_places) + (spec("h"),) * len(through)
        + (spec("v"),) * len(tokens),
        out_shape=tuple(result(o, p) for o, p in zip(outs, out_places))
        + tuple(HBM(v.shape, v.dtype) for v in through)
        + (shaped(8, 128),) * len(tokens),
        input_output_aliases={n_in + n_order + t: n_out + t for t in range(len(through))},
        scratch_shapes=list(scratch),
        compiler_params=pltpu.CompilerParams(vmem_limit_bytes=limit * 2**20),
        cost_estimate=cost(us),
    )(
        *[pinned(v, p) for v, p in zip(operands, places)],
        *[pinned(v, "h") for v in after],
        *tokens,
        *[pinned(v, "h") for v in through],
    )


def moving(source, target, sem):
    copy = pltpu.make_async_copy(source, target, sem)
    copy.start()
    return copy


def columns_moving(source, target, sems, wide=STEP):
    return [
        moving(source.at[:, s * wide : (s + 1) * wide], target.at[:, s * wide : (s + 1) * wide], sems.at[s])
        for s in range(source.shape[1] // wide)
    ]


def rows_moving(source, target, sems, tall=STEP):
    return [
        moving(source.at[s * tall : (s + 1) * tall], target.at[s * tall : (s + 1) * tall], sems.at[s])
        for s in range(source.shape[0] // tall)
    ]


def blocks(wide):
    return [(s, slice(s * STEP, (s + 1) * STEP)) for s in range(wide // STEP)]


def gelu(v):
    return 0.5 * v * (1.0 + jnp.tanh(GELU_A * (v + GELU_B * v * v * v)))


def gelu_slope(v):
    t = jnp.tanh(GELU_A * (v + GELU_B * v * v * v))
    return 0.5 * (1.0 + t) + 0.5 * v * (1.0 - t * t) * (GELU_A * (1.0 + 3.0 * GELU_B * v * v))


def normed(values, par_ref, part=slice(None)):
    return values * par_ref[0:1, part] + par_ref[1:2, part]


def normal_of(values, par_ref, part=slice(None)):
    return values * par_ref[2:3, part] + par_ref[3:4, part]


def norm_gradient(upstream, values, par_ref, back_ref, mask, part=slice(None)):
    normal = normal_of(values, par_ref, part)
    return upstream * back_ref[0:1, part] - mask * (back_ref[1:2, part] + normal * back_ref[2:3, part])


def sums_block(weighted, values):
    n = weighted.shape[1] // 128
    sums = (
        jnp.sum(weighted, axis=0, keepdims=True),
        jnp.sum(weighted * values, axis=0, keepdims=True),
    )
    return jnp.concatenate([v[:, c * 128 : c * 128 + 128] for v in sums for c in range(n)], axis=0)


def write_stats(stat_ref, weighted, values):
    stat_ref[...] = jnp.broadcast_to(sums_block(weighted, values)[None], stat_ref.shape)


def product_forward_body(x_ref, mask_ref, w_ref, low_ref, out_ref, stat_ref, x_buf, low_buf, sems):
    wide = x_ref.shape[1]
    coming = columns_moving(x_ref, x_buf, sems.at[0])
    total, going = None, []
    for s, part in blocks(wide):
        coming[s].wait()
        low_buf[:, part] = x_buf[:, part].astype(bf16)
        going.append(moving(low_buf.at[:, part], low_ref.at[:, part], sems.at[1, s]))
        term = dot(low_buf[:, part], w_ref[:, part], NT)
        total = term if total is None else total + term
    out_ref[...] = total
    write_stats(stat_ref, total * mask_ref[:, 0:1], total)
    for copy in going:
        copy.wait()


def product_forward(x, mask_wide, weight, devices):
    n, wide = x.shape
    return call(
        product_forward_body,
        (x, mask_wide, weight),
        "hvv",
        (shaped(n, wide, dtype=bf16), shaped(n, MID), shaped(devices, 8, 128)),
        "hvv",
        5,
        20,
        [VMEM((n, wide), f32), VMEM((n, wide), bf16), DMA((2, wide // STEP))],
    )


def expand_forward_body(*refs):
    *y_refs, par_ref, mask_ref, e_ref, mid_ref, out_ref, stat_ref, e_buf, out_buf, sems = refs
    coming = rows_moving(e_ref, e_buf, sems.at[0])
    mask = mask_ref[:, 0:1]
    at = 0
    for y_ref in y_refs:
        part = slice(at, at + y_ref.shape[0])
        mid_ref[part, :] = (gelu(normed(y_ref[...], par_ref)) * mask_ref[part, 0:1]).astype(bf16)
        at += y_ref.shape[0]
    going = []
    for s, part in blocks(e_ref.shape[0]):
        coming[s].wait()
        out = dot(mid_ref[...], e_buf[part, :], NT)
        out_buf[:, part] = out.astype(bf16)
        going.append(moving(out_buf.at[:, part], out_ref.at[:, part], sems.at[1, s]))
        stat_ref[s * 8 : s * 8 + 8, :] = sums_block(out * mask, out)
    for copy in going:
        copy.wait()


def expand_forward(y_parts, par, mask_wide, weight):
    n, wide = mask_wide.shape[0], weight.shape[0]
    return call(
        expand_forward_body,
        (*y_parts, par, mask_wide, weight),
        "v" * (len(y_parts) + 2) + "h",
        (shaped(n, MID, dtype=bf16), shaped(n, wide, dtype=bf16), shaped(wide // 64, 128)),
        "vhv",
        4,
        16,
        [VMEM(weight.shape, bf16), VMEM((n, wide), bf16), DMA((2, wide // STEP))],
    )


def first_forward_body(
    y_ref, par_ref, x_ref, mask_ref, w_ref, low_ref, out_ref, stat_ref,
    y_buf, x_buf, w_buf, low_buf, sems
):
    wide = x_ref.shape[1]
    coming_y = columns_moving(y_ref, y_buf, sems.at[0])
    coming_x = columns_moving(x_ref, x_buf, sems.at[1])
    coming_w = columns_moving(w_ref, w_buf, sems.at[2])
    mask = mask_ref[:, 0:1]
    total, going = None, []
    for s, part in blocks(wide):
        coming_y[s].wait()
        coming_x[s].wait()
        first = gelu(normed(y_buf[:, part].astype(f32), par_ref, part) + x_buf[:, part]) * mask
        low_buf[:, part] = first.astype(bf16)
        going.append(moving(low_buf.at[:, part], low_ref.at[:, part], sems.at[3, s]))
        coming_w[s].wait()
        term = dot(low_buf[:, part], w_buf[:, part], NT)
        total = term if total is None else total + term
    out_ref[...] = total
    write_stats(stat_ref, total * mask, total)
    for copy in going:
        copy.wait()


def first_forward(y, par, x, mask_wide, weight, devices):
    n, wide = y.shape
    return call(
        first_forward_body,
        (y, par, x, mask_wide, weight),
        "hvhvh",
        (shaped(n, wide, dtype=bf16), shaped(n, MID), shaped(devices, 8, 128)),
        "hvv",
        6,
        24,
        [
            VMEM((n, wide), bf16),
            VMEM((n, wide), f32),
            VMEM(weight.shape, bf16),
            VMEM((n, wide), bf16),
            DMA((4, wide // STEP)),
        ],
    )


def output_stage_body(
    y_ref, par_ref, first_ref, cot_ref, mask_ref, out_ref, dt_ref, stat_ref,
    y_buf, first_buf, cot_buf, out_buf, dt_buf, sems
):
    wide = y_ref.shape[1]
    coming_y = columns_moving(y_ref, y_buf, sems.at[0])
    coming_f = columns_moving(first_ref, first_buf, sems.at[1])
    coming_c = columns_moving(cot_ref, cot_buf, sems.at[2])
    mask = mask_ref[:, 0:1]
    going = []
    for s, part in blocks(wide):
        coming_y[s].wait()
        coming_f[s].wait()
        y = y_buf[:, part].astype(f32)
        pre = normed(y, par_ref, part) + first_buf[:, part].astype(f32)
        t = jnp.tanh(GELU_A * (pre + GELU_B * pre * pre * pre))
        out_buf[:, part] = 0.5 * pre * (1.0 + t) * mask
        going.append(moving(out_buf.at[:, part], out_ref.at[:, part], sems.at[3, s]))
        slope = 0.5 * (1.0 + t) + 0.5 * pre * (1.0 - t * t) * (GELU_A * (1.0 + 3.0 * GELU_B * pre * pre))
        coming_c[s].wait()
        dt = slope * (cot_buf[:, part] * mask)
        dt_buf[:, part] = dt.astype(bf16)
        going.append(moving(dt_buf.at[:, part], dt_ref.at[:, part], sems.at[4, s]))
        stat_ref[s * 8 : s * 8 + 8, :] = sums_block(dt, normal_of(y, par_ref, part))
    for copy in going:
        copy.wait()


def output_stage(y, par, first, cot, mask_wide):
    n, wide = y.shape
    return call(
        output_stage_body,
        (y, par, first, cot, mask_wide),
        "hvhhv",
        (shaped(n, wide), shaped(n, wide, dtype=bf16), shaped(wide // 64, 128)),
        "hhv",
        8,
        28,
        [
            VMEM((n, wide), bf16),
            VMEM((n, wide), bf16),
            VMEM((n, wide), f32),
            VMEM((n, wide), f32),
            VMEM((n, wide), bf16),
            DMA((5, wide // STEP)),
        ],
    )


def expand_backward_body(
    dt_ref, y_ref, par_ref, back_ref, mask_ref, e_ref, mid_y_ref, mid_par_ref,
    dy_ref, mid_dt_ref, stat_ref, dt_buf, y_buf, e_buf, dy_buf, sems
):
    wide = dt_ref.shape[1]
    coming_dt = columns_moving(dt_ref, dt_buf, sems.at[0])
    coming_y = columns_moving(y_ref, y_buf, sems.at[1])
    coming_e = rows_moving(e_ref, e_buf, sems.at[2])
    mask = mask_ref[:, 0:1]
    total, going = None, []
    for s, part in blocks(wide):
        coming_dt[s].wait()
        coming_y[s].wait()
        dt, y = dt_buf[:, part].astype(f32), y_buf[:, part].astype(f32)
        dy = norm_gradient(dt, y, par_ref, back_ref, mask, part).astype(bf16)
        dy_buf[:, part] = dy
        going.append(moving(dy_buf.at[:, part], dy_ref.at[:, part], sems.at[3, s]))
        coming_e[s].wait()
        term = dot(dy, e_buf[part, :])
        total = term if total is None else total + term
    y = mid_y_ref[...]
    dt = gelu_slope(normed(y, mid_par_ref)) * (total * mask)
    mid_dt_ref[...] = dt
    write_stats(stat_ref, dt, normal_of(y, mid_par_ref))
    for copy in going:
        copy.wait()


def expand_backward(dt, y, par, back, mask_wide, weight, mid_y, mid_par, devices, through=()):
    n, wide = y.shape
    return call(
        expand_backward_body,
        (dt, y, par, back, mask_wide, weight, mid_y, mid_par),
        "hhvvvhvv",
        (shaped(n, wide, dtype=bf16), shaped(n, MID), shaped(devices, 8, 128)),
        "hvv",
        5,
        24,
        [
            VMEM((n, wide), bf16),
            VMEM((n, wide), bf16),
            VMEM(weight.shape, bf16),
            VMEM((n, wide), bf16),
            DMA((4, wide // STEP)),
        ],
        through=through,
    )


def residual_backward_body(
    dt_ref, y_ref, par_ref, back_ref, mask_ref, w_ref, add_ref, wide_y_ref, wide_par_ref, x_ref,
    dy_ref, out_ref, stat_ref, w_buf, add_buf, y_buf, x_buf, out_buf, sems
):
    wide = x_ref.shape[1]
    coming = [
        columns_moving(source, target, sems.at[t])
        for t, (source, target) in enumerate(
            ((w_ref, w_buf), (add_ref, add_buf), (wide_y_ref, y_buf), (x_ref, x_buf))
        )
    ]
    mask = mask_ref[:, 0:1]
    dy_ref[...] = norm_gradient(dt_ref[...], y_ref[...], par_ref, back_ref, mask).astype(bf16)
    going = []
    for s, part in blocks(wide):
        for copies in coming:
            copies[s].wait()
        grad = add_buf[:, part].astype(f32) + dot(dy_ref[...], w_buf[:, part])
        y = y_buf[:, part].astype(f32)
        pre = normed(y, wide_par_ref, part) + x_buf[:, part].astype(f32)
        dt = gelu_slope(pre) * (grad * mask)
        out_buf[:, part] = dt.astype(bf16)
        going.append(moving(out_buf.at[:, part], out_ref.at[:, part], sems.at[4, s]))
        stat_ref[s * 8 : s * 8 + 8, :] = sums_block(dt, normal_of(y, wide_par_ref, part))
    for copy in going:
        copy.wait()


def residual_backward(dt, y, par, back, mask_wide, weight, add, wide_y, wide_par, x):
    n, wide = x.shape
    return call(
        residual_backward_body,
        (dt, y, par, back, mask_wide, weight, add, wide_y, wide_par, x),
        "vvvvvhhhvh",
        (shaped(n, MID, dtype=bf16), shaped(n, wide, dtype=bf16), shaped(wide // 64, 128)),
        "vhv",
        6,
        24,
        [VMEM(weight.shape, bf16)] + [VMEM((n, wide), bf16)] * 4 + [DMA((5, wide // STEP))],
    )


def input_backward_body(dy_ref, w_ref, add_ref, out_ref, w_buf, add_buf, out_buf, sems):
    coming_w = columns_moving(w_ref, w_buf, sems.at[0])
    coming_a = columns_moving(add_ref, add_buf, sems.at[1])
    going = []
    for s, part in blocks(w_ref.shape[1]):
        coming_w[s].wait()
        coming_a[s].wait()
        out_buf[:, part] = add_buf[:, part].astype(f32) + dot(dy_ref[...], w_buf[:, part])
        going.append(moving(out_buf.at[:, part], out_ref.at[:, part], sems.at[2, s]))
    for copy in going:
        copy.wait()


def input_backward(dy, weight, add, token):
    n, wide = add.shape
    return call(
        input_backward_body,
        (dy, weight, add),
        "vhh",
        (shaped(n, wide),),
        "h",
        5,
        20,
        [VMEM(weight.shape, bf16), VMEM((n, wide), bf16), VMEM((n, wide), f32), DMA((3, wide // STEP))],
        token=token,
    )


def hidden_backward_body(
    own_ref, near_ref, up_ref, down_ref, y_ref, par_ref, mask_ref, dt_ref, stat_ref
):
    batch, pixels, _ = own_ref.shape
    for b in range(batch):
        own, near, up, down = [ref[b].astype(f32) for ref in (own_ref, near_ref, up_ref, down_ref)]
        dt_ref[b * pixels : (b + 1) * pixels, :] = own + near + up + down
    grad = dt_ref[...]
    y = y_ref[...]
    dt = gelu_slope(normed(y, par_ref)) * (grad * mask_ref[:, 0:1])
    dt_ref[...] = dt
    write_stats(stat_ref, dt, normal_of(y, par_ref))


def hidden_backward(pieces, y, par, mask_wide, devices, through):
    n = y.shape[0]
    return call(
        hidden_backward_body,
        (*pieces, y, par, mask_wide),
        "v" * (len(pieces) + 3),
        (shaped(n, MID), shaped(devices, 8, 128)),
        "vv",
        3,
        16,
        through=through,
    )


def last_gradient_body(
    dt_ref, y_ref, par_ref, back_ref, mask_ref, acts_ref, dy_ref, send_ref, keep_ref,
    dyt_ref, acts_buf, out_buf, in_sems, out_sems
):
    coming = columns_moving(acts_ref, acts_buf, in_sems)
    dy = norm_gradient(dt_ref[...], y_ref[...], par_ref, back_ref, mask_ref[:, 0:1]).astype(bf16)
    dy_ref[...] = dy
    dyt_ref[...] = dy.astype(f32).T.astype(bf16)
    core = lax.axis_index("ch") % 2
    half, base = send_ref.shape[0], send_ref.shape[1]
    going = []
    for s, part in blocks(acts_ref.shape[1]):
        coming[s].wait()
        out_buf[:, part] = dot(dyt_ref[...], acts_buf[:, part]).astype(bf16)
        for q in range(half):
            for t, (out_ref, side) in enumerate(((send_ref, 1 - core), (keep_ref, core))):
                row = pl.multiple_of((2 * q + side) * base, 16)
                going.append(
                    moving(
                        out_buf.at[pl.ds(row, base), part], out_ref.at[q, :, part], out_sems.at[s, q, t]
                    )
                )
    for copy in going:
        copy.wait()


def last_gradient(dt, y, par, back, mask_wide, acts, ch, through):
    n, wide = acts.shape
    half = shaped(ch // 2, MID // ch, wide, dtype=bf16)
    return call(
        last_gradient_body,
        (dt, y, par, back, mask_wide, acts),
        "vvvvvh",
        (shaped(n, MID, dtype=bf16), half, half),
        "vhh",
        6,
        20,
        [
            VMEM((MID, n), bf16),
            VMEM((n, wide), bf16),
            VMEM((MID, wide), bf16),
            DMA((wide // STEP,)),
            DMA((wide // STEP, ch // 2, 2)),
        ],
        through=through,
    )


def cast_body(v_ref, out_ref):
    out_ref[...] = v_ref[...].astype(bf16)


def cast_after(values, *after):
    return call(cast_body, (values,), "v", (shaped(*values.shape, dtype=bf16),), "v", 2, 12, after=after)[0]


def pack_body(*refs, count, bit_axis, rows):
    part_refs, (send_ref, keep_ref), refs = refs[:count], refs[count : count + 2], refs[count + 2 :]
    buffers, (in_sem, out_sem) = refs[:count], refs[count:]
    coming = [moving(ref, buf, in_sem.at[t]) for t, (ref, buf) in enumerate(zip(part_refs, buffers))]
    bit = lax.axis_index(bit_axis) % 2
    tall = send_ref.shape[1]
    base = rows * tall
    going, at = [], 0
    for copy, buf in zip(coming, buffers):
        copy.wait()
        wide = buf.shape[1]
        for block in range(buf.shape[0] // base):
            for pair in range(rows // 2):
                for out_ref, side in ((send_ref, 1 - bit), (keep_ref, bit)):
                    row = pl.multiple_of(block * base + (2 * pair + side) * tall, 16)
                    going.append(
                        moving(
                            buf.at[pl.ds(row, tall), :],
                            out_ref.at[pair, :, at : at + wide],
                            out_sem.at[len(going)],
                        )
                    )
            at += wide
    for copy in going:
        copy.wait()


def pack_split(parts, base, rows, token=None):
    count = len(parts)
    blocks_in = sum(p.shape[0] // base for p in parts)
    wide = sum(p.shape[0] // base * p.shape[1] for p in parts)
    half = shaped(rows // 2, base // rows, wide, dtype=bf16)
    return call(
        functools.partial(pack_body, count=count, bit_axis="rows", rows=rows),
        tuple(parts),
        "h" * count,
        (half, half),
        "hh",
        3,
        16,
        [VMEM(p.shape, bf16) for p in parts] + [DMA((count,)), DMA((blocks_in * rows,))],
        token=token,
    )


def step_body(got_ref, kept_ref, send_ref, keep_ref, sum_ref, *, axis, step):
    bit = lax.axis_index(axis) // step % 2
    sum_ref[...] = (got_ref[...].astype(f32) + kept_ref[...].astype(f32)).astype(bf16)
    for pair in range(send_ref.shape[0]):
        send_ref[pair] = sum_ref[2 * pair + 1 - bit]
        keep_ref[pair] = sum_ref[2 * pair + bit]


def step_split(got, kept, axis, step, token=None):
    half = shaped(got.shape[0] // 2, *got.shape[1:], dtype=bf16)
    return call(
        functools.partial(step_body, axis=axis, step=step),
        (got, kept),
        "vv",
        (half, half),
        "vv",
        2,
        12,
        [VMEM(got.shape, bf16)],
        token=token,
    )


def sum_body(got_ref, kept_ref, sum_ref):
    sum_ref[...] = (got_ref[...].astype(f32) + kept_ref[...].astype(f32)).astype(bf16)


def step_sum(got, kept, token=None):
    return call(sum_body, (got, kept), "vv", (shaped(*got.shape, dtype=bf16),), "v", 1, 12, token=token)


def join_body(got_ref, kept_ref, out_ref, *, step):
    bit = lax.axis_index("rows") // step % 2
    for a in range(got_ref.shape[0]):
        out_ref[2 * a + bit] = kept_ref[a]
        out_ref[2 * a + 1 - bit] = got_ref[a]


def join_step(got, kept, step, token=None):
    m, r, wide = got.shape
    return call(
        functools.partial(join_body, step=step),
        (got, kept),
        "vv",
        (shaped(2 * m, r, wide, dtype=bf16),),
        "v",
        1,
        12,
        token=token,
    )


def final_body(got_ref, kept_ref, *refs, cuts):
    out_refs, refs = refs[: len(cuts)], refs[len(cuts) :]
    buffers, sems = refs[: len(cuts)], refs[len(cuts)]
    bit = lax.axis_index("rows") % 2
    going, at = [], 0
    for out_ref, buf, (count, wide) in zip(out_refs, buffers, cuts):
        for k in range(count):
            part = slice(at, at + wide)
            for a in range(got_ref.shape[0]):
                buf[k, 2 * a + bit] = kept_ref[a, :, part].astype(f32)
                buf[k, 2 * a + 1 - bit] = got_ref[a, :, part].astype(f32)
            going.append(moving(buf.at[k], out_ref.at[k], sems.at[len(going)]))
            at += wide
    for copy in going:
        copy.wait()


def final_join(got, kept, cuts, token):
    m, r, _ = got.shape
    outs = [shaped(count, 2 * m, r, wide) for count, wide in cuts]
    *outs, token = call(
        functools.partial(final_body, cuts=cuts),
        (got, kept),
        "vv",
        outs,
        "h" * len(outs),
        2,
        20,
        [VMEM(o.shape, f32) for o in outs] + [DMA((sum(count for count, _ in cuts),))],
        token=token,
    )
    return [o.reshape(-1, o.shape[3]) for o in outs], token


def owned_body(*refs):
    n = len(refs) // 3
    for k in range(n):
        size = refs[n + 2 * k].shape[1]
        start = lax.axis_index("ch") * size
        turned = pltpu.roll(refs[k][...], refs[k].shape[1] - start, 1)
        refs[n + 2 * k][...] = turned[0:1, :size]
        refs[n + 2 * k + 1][...] = turned[1:2, :size]


def owned(sums, ch):
    outs = [shaped(1, s.shape[1] // ch) for s in sums for _ in range(2)]
    outs = call(owned_body, tuple(sums), "v" * len(sums), outs, "v" * len(outs), 1, 12)
    return [o.reshape(-1) for o in outs]


def return_body(far_up_ref, up_ref, down_ref, far_down_ref, got_ref, below_ref, above_ref, partner_ref):
    odd = lax.axis_index("rows") % 2 == 1

    @pl.when(odd)
    def _():
        below_ref[...] = (far_up_ref[...].astype(f32) + got_ref[...].astype(f32)).astype(bf16)
        above_ref[...] = far_down_ref[...]
        partner_ref[...] = up_ref[...]

    @pl.when(jnp.logical_not(odd))
    def _():
        below_ref[...] = far_up_ref[...]
        above_ref[...] = (far_down_ref[...].astype(f32) + got_ref[...].astype(f32)).astype(bf16)
        partner_ref[...] = down_ref[...]


def return_step(far_up, up, down, far_down, got, through):
    piece = shaped(*got.shape, dtype=bf16)
    return call(
        return_body,
        (far_up, up, down, far_down, got),
        "vvvvv",
        (piece, piece, piece),
        "vvv",
        2,
        16,
        through=through,
    )


def shift_lanes(values, by, width):
    place = lax.broadcasted_iota(jnp.int32, values.shape, values.ndim - 1) % width
    moved = pltpu.roll(values, by % values.shape[-1], values.ndim - 1)
    return jnp.where((place >= by) & (place < width + by), moved, 0.0)


def shift_rows(values, by, width):
    place = lax.broadcasted_iota(jnp.int32, values.shape, 0) % width
    moved = pltpu.roll(values, by % values.shape[0], 0)
    return jnp.where((place >= by) & (place < width + by), moved, 0.0)


def offset_fraction(ext_ref, ow_ref, b, base, pixels, width):
    u = None
    for i in range(3):
        start = (base + 2 * i) * width
        term = dot(ow_ref[i], ext_ref[b, start : start + pixels, :], NT)
        u = term if u is None else u + term
    total = u[32:64]
    total = total + shift_lanes(u[0:32], 2, width) + shift_lanes(u[64:96], -2, width)
    return 1.0 / (1.0 + jnp.exp(-total))


def deform_forward_body(*refs, batch, rows, width, deep):
    tile_refs, refs = refs[:5], refs[5:]
    ow_ref, disp_ref, m_ref, mask_ref, cols_out_ref, y_ref, frac_ref, stat_ref = refs[:8]
    ext_ref, par_ref, s_ref, cols_ref, m_buf, tile_sems, sems = refs[8:]
    pixels = rows * width
    coming = [
        moving(ref, ext_ref.at[:, t * pixels : (t + 1) * pixels, :], tile_sems.at[t])
        for t, ref in enumerate(tile_refs)
    ]
    coming_m = moving(m_ref, m_buf, sems.at[0])
    for copy in coming:
        copy.wait()
    lane = lax.broadcasted_iota(jnp.int32, (32, 128), 1)
    column = lane % width
    upper = lane // width

    def image(b, carry):
        frac = offset_fraction(ext_ref, ow_ref, b, deep - 2, pixels, width)
        for i in range(4):
            frac_ref[b, i] = frac[i * 8 : i * 8 + 8]
        pix = lax.broadcasted_iota(jnp.int32, (1, pixels), 1)
        row_at, col_at = pix // width, pix % width
        tops, lefts, ys, xs = [], [], [], []
        for k in range(9):
            i, j = k // 3, k % 3
            tops.append(row_at + disp_ref[b, i, 2 * j : 2 * j + 1, :] + (deep - 2))
            lefts.append(col_at + 2 * (j - 1) + disp_ref[b, i, 2 * j + 1 : 2 * j + 2, :])
            at = i * 8 + 2 * j
            ys.append(frac[at : at + 1])
            xs.append(frac[at + 1 : at + 2])
        blank = jnp.zeros((23, pixels), f32)
        par = jnp.concatenate(
            [jnp.concatenate(g, axis=0).astype(f32) if g is not None else blank
             for g in (tops, None, lefts, None, ys, None, xs, None)], axis=0)
        par_ref[...] = par.T

        def row_of_taps(i, carry):
            for j in range(3):
                k = i * 3 + j
                for c in range(pixels // 32):
                    p = pltpu.roll(par_ref[c * 32 : c * 32 + 32, :], 128 - k, 1)
                    wide = (32, 128)
                    top = jnp.broadcast_to(p[:, 0:1], wide).astype(jnp.int32) - upper
                    left = jnp.broadcast_to(p[:, 32:33], wide).astype(jnp.int32)
                    fy = jnp.broadcast_to(p[:, 64:65], wide)
                    fx = jnp.broadcast_to(p[:, 96:97], wide)
                    cw = jnp.where(column == left, 1.0 - fx, jnp.where(column == left + 1, fx, 0.0))
                    ca, cb = (1.0 - fy) * cw, fy * cw
                    for q in range(8):
                        s = jnp.where(top == 2 * q, ca, jnp.where(top == 2 * q - 1, cb, 0.0))
                        s_ref[j * pixels + c * 32 : j * pixels + c * 32 + 32, q * 128 : q * 128 + 128] = s.astype(bf16)
            start = pl.multiple_of(i * 2 * width, 128)
            window = ext_ref[b, pl.ds(start, 16 * width), :]
            for j in range(3):
                got = dot(s_ref[j * pixels : (j + 1) * pixels, :], window).astype(bf16)
                cols_ref[pl.ds(pl.multiple_of(b * pixels, pixels), pixels), pl.ds(pl.multiple_of((i * 3 + j) * MID, MID), MID)] = got
            return carry

        return lax.fori_loop(0, 3, row_of_taps, carry)

    lax.fori_loop(0, batch, image, 0)
    going = moving(cols_ref, cols_out_ref, sems.at[1])
    coming_m.wait()
    y = dot(cols_ref[...], m_buf[...], NT)
    y_ref[...] = y
    write_stats(stat_ref, y * mask_ref[:, 0:1], y)
    going.wait()


def deform_forward(tiles, offset_rows, disp, weight, mask_wide, rows, width, devices):
    batch = tiles[0].shape[0]
    pixels = rows * width
    n = batch * pixels
    return call(
        functools.partial(deform_forward_body, batch=batch, rows=rows, width=width, deep=2 * rows),
        (*tiles, offset_rows, disp, weight, mask_wide),
        "hhhhhvvhv",
        (
            shaped(n, 9 * MID, dtype=bf16),
            shaped(n, MID),
            shaped(batch, 4, 8, pixels),
            shaped(devices, 8, 128),
        ),
        "hvvv",
        15,
        30,
        [
            VMEM((batch, 5 * pixels, MID), bf16),
            VMEM((pixels, 128), f32),
            VMEM((3 * pixels, 16 * width), bf16),
            VMEM((n, 9 * MID), bf16),
            VMEM(weight.shape, bf16),
            DMA((5,)),
            DMA((2,)),
        ],
    )


def deform_backward_body(*refs, batch, rows, width, deep):
    tile_refs, refs = refs[:5], refs[5:]
    (ow_ref, disp_ref, frac_ref, m_ref, dy_ref), refs = refs[:5], refs[5:]
    out_refs, refs = refs[:5], refs[5:]
    dow_ref, ext_ref, dext_ref, dc_ref, g_ref, st_ref, df_ref, m_buf, tile_sems, m_sem = refs
    pixels = rows * width
    coming = [
        moving(ref, ext_ref.at[:, t * pixels : (t + 1) * pixels, :], tile_sems.at[t])
        for t, ref in enumerate(tile_refs)
    ]
    coming_m = moving(m_ref, m_buf, m_sem)
    window = 16 * width
    dow_ref[...] = jnp.zeros_like(dow_ref)
    dext_ref[...] = jnp.zeros_like(dext_ref)
    for copy in coming:
        copy.wait()
    coming_m.wait()

    def image(b, carry):
        at = pl.multiple_of(b * pixels, pixels)

        def row_of_taps(i, carry):
            dy = dy_ref[pl.ds(at, pixels), :]
            for j in range(3):
                m = m_buf[:, pl.ds(pl.multiple_of((i * 3 + j) * MID, MID), MID)]
                dc_ref[j * pixels : (j + 1) * pixels, :] = dot(dy, m).astype(bf16)
            start = pl.multiple_of(i * 2 * width, 128)
            g_ref[...] = dot(ext_ref[b, pl.ds(start, window), :], dc_ref[...], NT)
            place = lax.broadcasted_iota(jnp.int32, (width, 128), 0)
            for j in range(3):
                for h in range(pixels // 128):
                    lanes = slice(h * 128, h * 128 + 128)
                    at_l = slice(j * pixels + h * 128, j * pixels + h * 128 + 128)
                    pix = lax.broadcasted_iota(jnp.int32, (1, 128), 1) + h * 128
                    by_y, by_x = slice(2 * j, 2 * j + 1), slice(2 * j + 1, 2 * j + 2)
                    top = pix // width + disp_ref[b, i, by_y, lanes] + (deep - 2)
                    left = pix % width + 2 * (j - 1) + disp_ref[b, i, by_x, lanes]
                    fy = frac_ref[b, i, by_y, lanes]
                    fx = frac_ref[b, i, by_x, lanes]
                    here, after = place == left, place == left + 1
                    cw = jnp.where(here, 1.0 - fx, jnp.where(after, fx, 0.0))
                    ca, cb = (1.0 - fy) * cw, fy * cw
                    low_sum = jnp.zeros((width, 128), f32)
                    high_sum = jnp.zeros((width, 128), f32)
                    for r in range(16):
                        part = slice(r * width, r * width + width)
                        g = g_ref[part, at_l]
                        m0, m1 = top == r, top == r - 1
                        low_sum = low_sum + jnp.where(m0, g, 0.0)
                        high_sum = high_sum + jnp.where(m1, g, 0.0)
                        st_ref[part, at_l] = jnp.where(m0, ca, jnp.where(m1, cb, 0.0)).astype(bf16)
                    d_fy = jnp.sum((high_sum - low_sum) * cw, axis=0, keepdims=True)
                    mixed = (1.0 - fy) * low_sum + fy * high_sum
                    d_fx = jnp.sum(
                        jnp.where(after, mixed, 0.0) - jnp.where(here, mixed, 0.0), axis=0, keepdims=True)
                    df_ref[i, by_y, lanes] = d_fy * fy * (1.0 - fy)
                    df_ref[i, by_x, lanes] = d_fx * fx * (1.0 - fx)
            dext_ref[b, pl.ds(start, window), :] += dot(st_ref[...], dc_ref[...])
            return carry

        df_ref[...] = jnp.zeros_like(df_ref)
        carry = lax.fori_loop(0, 3, row_of_taps, carry)
        d_off = df_ref[...].reshape(32, pixels).astype(bf16).astype(f32)
        stacked = jnp.concatenate(
            [shift_lanes(d_off, -2, width), d_off, shift_lanes(d_off, 2, width)], axis=0)
        across = jnp.concatenate([stacked, jnp.zeros((32, pixels), f32)], axis=0).T.astype(bf16)
        stacked = stacked.astype(bf16)
        for i in range(3):
            first = (deep - 2 + 2 * i) * width
            part = slice(first, first + pixels)
            dow_ref[i] += dot(stacked, ext_ref[b, part, :])
            dext_ref[b, part, :] += dot(across[:, :96], ow_ref[i])
        return carry

    lax.fori_loop(0, batch, image, 0)
    for t, ref in enumerate(out_refs):
        ref[...] = dext_ref[:, t * pixels : (t + 1) * pixels, :].astype(ref.dtype)


def deform_backward(tiles, offset_rows, disp, frac, weight, dy, rows, width, after, through):
    batch = tiles[0].shape[0]
    pixels = rows * width
    return call(
        functools.partial(deform_backward_body, batch=batch, rows=rows, width=width, deep=2 * rows),
        (*tiles, offset_rows, disp, frac, weight, dy),
        "hhhhhvvvhv",
        tuple(shaped(batch, pixels, MID, dtype=f32 if t == 2 else bf16) for t in range(5))
        + (shaped(3, 96, MID),),
        "vvvvvv",
        20,
        36,
        [
            VMEM((batch, 5 * pixels, MID), bf16),
            VMEM((batch, 5 * pixels, MID), f32),
            VMEM((3 * pixels, MID), bf16),
            VMEM((16 * width, 3 * pixels), f32),
            VMEM((16 * width, 3 * pixels), bf16),
            VMEM((4, 8, pixels), f32),
            VMEM(weight.shape, bf16),
            DMA((5,)),
            DMA,
        ],
        after,
        through,
    )


def taps_moving(m_ref, m_buf, sems):
    wide = 3 * MID
    return columns_moving(m_ref, m_buf, sems, wide)


def rim_moving(parts, rim_ref, sems):
    copies, at = [], 0
    for t, ref in enumerate(parts):
        copies.append(moving(ref, rim_ref.at[:, at : at + ref.shape[1], :], sems.at[t]))
        at += ref.shape[1]
    return copies


def conv_forward_body(
    above_ref, own_ref, below_ref, m_ref, mask_ref, y_ref, stat_ref, rim_ref, m_buf, rim_sems, sems,
    *, batch, rows, width
):
    pixels = rows * width
    coming = taps_moving(m_ref, m_buf, sems)
    for copy in rim_moving((above_ref, own_ref, below_ref), rim_ref, rim_sems):
        copy.wait()
    sums = [[None] * 3 for _ in range(batch)]
    for i in range(3):
        coming[i].wait()
        for b in range(batch):
            for j in range(3):
                k = i * 3 + j
                start = 2 * i * width
                term = dot(rim_ref[b, start : start + pixels, :], m_buf[:, k * MID : (k + 1) * MID], NT)
                sums[b][j] = term if i == 0 else sums[b][j] + term
    for b in range(batch):
        total = sums[b][1] + shift_rows(sums[b][0], 2, width) + shift_rows(sums[b][2], -2, width)
        y_ref[b * pixels : (b + 1) * pixels, :] = total
    y = y_ref[...]
    write_stats(stat_ref, y * mask_ref[:, 0:1], y)


def conv_forward(rim, weight, mask_wide, rows, width, devices):
    batch = rim[0].shape[0]
    n = batch * rows * width
    return call(
        functools.partial(conv_forward_body, batch=batch, rows=rows, width=width),
        (*rim, weight, mask_wide),
        "hhhhv",
        (shaped(n, MID), shaped(devices, 8, 128)),
        "vv",
        5,
        24,
        [VMEM((batch, (rows + 4) * width, MID), bf16), VMEM(weight.shape, bf16), DMA((3,)), DMA((3,))],
    )


def conv_backward_body(
    above_ref, own_ref, below_ref, m_ref, y_ref, par_ref, mask_ref, dt_ref, stat_ref,
    rim_ref, m_buf, rim_sems, sems, *, batch, rows, width
):
    pixels = rows * width
    coming = taps_moving(m_ref, m_buf, sems)
    for copy in rim_moving((above_ref, own_ref, below_ref), rim_ref, rim_sems):
        copy.wait()
    sums = [[None] * 3 for _ in range(batch)]
    for i in range(3):
        coming[i].wait()
        for b in range(batch):
            for j in range(3):
                k = i * 3 + j
                start = (4 - 2 * i) * width
                term = dot(rim_ref[b, start : start + pixels, :], m_buf[:, k * MID : (k + 1) * MID])
                sums[b][j] = term if i == 0 else sums[b][j] + term
    for b in range(batch):
        total = sums[b][1] + shift_rows(sums[b][0], -2, width) + shift_rows(sums[b][2], 2, width)
        dt_ref[b * pixels : (b + 1) * pixels, :] = total
    y = y_ref[...]
    dt = gelu_slope(normed(y, par_ref)) * (dt_ref[...] * mask_ref[:, 0:1])
    dt_ref[...] = dt
    write_stats(stat_ref, dt, normal_of(y, par_ref))


def conv_backward(rim, weight, y, par, mask_wide, rows, width, devices, after):
    batch = rim[0].shape[0]
    n = batch * rows * width
    return call(
        functools.partial(conv_backward_body, batch=batch, rows=rows, width=width),
        (*rim, weight, y, par, mask_wide),
        "hhhhvvv",
        (shaped(n, MID), shaped(devices, 8, 128)),
        "vv",
        6,
        24,
        [VMEM((batch, (rows + 4) * width, MID), bf16), VMEM(weight.shape, bf16), DMA((3,)), DMA((3,))],
        after,
    )


def conv_weight_body(
    dy_ref, above_ref, own_ref, below_ref, out_ref, rim_ref, dyt_ref, out_buf, rim_sems, sems,
    *, batch, rows, width
):
    pixels = rows * width
    coming = rim_moving((above_ref, own_ref, below_ref), rim_ref, rim_sems)
    dy = dy_ref[...].astype(f32)
    going = []
    for j in range(3):
        moved = shift_rows(dy, 2 * (j - 1), width) if j != 1 else dy
        dyt_ref[j] = moved.T.astype(bf16)
        if j == 0:
            for copy in coming:
                copy.wait()
        for i in range(3):
            part = slice((i * 3 + j) * MID, (i * 3 + j + 1) * MID)
            start = 2 * i * width
            total = None
            for b in range(batch):
                term = dot(dyt_ref[j, :, b * pixels : (b + 1) * pixels], rim_ref[b, start : start + pixels, :])
                total = term if total is None else total + term
            out_buf[:, part] = total.astype(bf16)
            going.append(moving(out_buf.at[:, part], out_ref.at[:, part], sems.at[i * 3 + j]))
    for copy in going:
        copy.wait()


def conv_weight_gradient(dy, rim, rows, width, after):
    batch = rim[0].shape[0]
    return call(
        functools.partial(conv_weight_body, batch=batch, rows=rows, width=width),
        (dy, *rim),
        "vhhh",
        (shaped(MID, 9 * MID, dtype=bf16),),
        "h",
        6,
        20,
        [
            VMEM((batch, (rows + 4) * width, MID), bf16),
            VMEM((3, MID, batch * rows * width), bf16),
            VMEM((MID, 9 * MID), bf16),
            DMA((3,)),
            DMA((9,)),
        ],
        after,
    )[0]


def columns_weight_body(dy_ref, cols_ref, out_ref, dyt_ref, cols_buf, out_buf, sems):
    coming = columns_moving(cols_ref, cols_buf, sems.at[0])
    dyt_ref[...] = dy_ref[...].astype(f32).T.astype(bf16)
    going = []
    for s, part in blocks(cols_ref.shape[1]):
        coming[s].wait()
        out_buf[:, part] = dot(dyt_ref[...], cols_buf[:, part]).astype(bf16)
        going.append(moving(out_buf.at[:, part], out_ref.at[:, part], sems.at[1, s]))
    for copy in going:
        copy.wait()


def columns_weight_gradient(dy, cols, through):
    n, wide = cols.shape
    return call(
        columns_weight_body,
        (dy, cols),
        "vh",
        (shaped(MID, wide, dtype=bf16),),
        "h",
        6,
        20,
        [VMEM((MID, n), bf16), VMEM((n, wide), bf16), VMEM((MID, wide), bf16), DMA((2, wide // STEP))],
        through=through,
    )


TILES = 2
EPSILON = 1e-05


def swap_with(values, axis, step):
    return lax.ppermute(values, axis, [(i, i ^ step) for i in range(lax.axis_size(axis))])


def from_behind(block, axis, distance):
    devices = range(lax.axis_size(axis))
    route = [(i - distance, i) for i in devices if i - distance in devices]
    return lax.ppermute(block, axis, route)


def ladder_sum(values, axis):
    step = 1
    while step < lax.axis_size(axis):
        got = swap_with(values.astype(bf16), axis, step)
        values = values + got.astype(f32)
        step *= 2
    return values


def to_everyone(spread, groups=None):
    return lax.all_to_all(spread, ("rows", "ch"), 0, 0, axis_index_groups=groups, tiled=True)


def small_total(spread):
    return jnp.sum(to_everyone(spread), axis=0).reshape(2, -1)


def wide_total(block):
    devices = lax.axis_size("rows") * lax.axis_size("ch")
    core = lax.axis_index("ch") % 2
    above, below = block.reshape(2, -1, 128)
    half = jnp.where(core == 0, above, below) + swap_with(jnp.where(core == 0, below, above), "ch", 1)
    groups = [[i * 2 + k for i in range(devices // 2)] for k in range(2)]
    half = jnp.broadcast_to(half[None], (devices // 2,) + half.shape)
    half = jnp.sum(to_everyone(half, groups), axis=0)
    other = swap_with(half, "ch", 1)
    whole = jnp.stack([jnp.where(core == 0, half, other), jnp.where(core == 0, other, half)])
    whole = whole.reshape(-1, 2, STEP)
    return whole[:, 0].reshape(-1), whole[:, 1].reshape(-1)


def forward_rows(sums, gain, shift, count):
    mean = sums[0] / count
    scale = lax.rsqrt(sums[1] / count - mean * mean + EPSILON)
    return jnp.stack([scale * gain, shift - mean * scale * gain, scale, -mean * scale])


def backward_rows(sums, par, count):
    rows = jnp.stack([par[0], par[0] * sums[0] / count, par[0] * sums[1] / count])
    return rows, jnp.stack([sums[1], sums[0]])


def gather_weight(weight):
    return lax.all_gather(weight.astype(bf16), "ch", axis=0, tiled=True)


def gather_weight_after(weight, *after):
    return lax.all_gather(cast_after(weight, *after), "ch", axis=0, tiled=True)


def gather_by_swaps(weight):
    ch = lax.axis_size("ch")
    came = None
    held = weight.astype(bf16)[None]
    step = ch // 2
    while step >= 1:
        got = swap_with(held, "ch", step)
        came = got if came is None else came
        odd = lax.axis_index("ch") // step % 2 == 1
        held = jnp.stack([jnp.where(odd, got, held), jnp.where(odd, held, got)], axis=1)
        held = held.reshape((-1,) + held.shape[2:])
        step //= 2
    return held.reshape((-1,) + weight.shape[1:]), came


def pick(values, bit):
    return lax.dynamic_index_in_dim(values, bit, 1, keepdims=False)


def scatter_ch(gradient):
    return lax.psum_scatter(gradient, "ch", scatter_dimension=0, tiled=True)


def split(total, axis, step):
    bit = lax.axis_index(axis) // step % 2
    pairs = total.reshape((total.shape[0] // 2, 2) + total.shape[1:])
    return swap_with(pick(pairs, 1 - bit), axis, step), pick(pairs, bit)


def added(pair):
    got, kept = pair
    return (got.astype(f32) + kept.astype(f32)).astype(bf16)


def rest_of(total, axis, step=1):
    while step < lax.axis_size(axis):
        total = added(split(total, axis, step))
        step *= 2
    return total


def by_owner(gradient, axis="ch"):
    count = lax.axis_size(axis)
    return gradient.reshape((count, gradient.shape[0] // count) + gradient.shape[1:])


def wide_enough(base):
    return base // lax.axis_size("rows") % 16 == 0


def first_step(parts, base, token=None):
    if wide_enough(base):
        send, keep, *token = pack_split(parts, base, lax.axis_size("rows"), token)
        return (swap_with(send, "rows", 1), keep, *token)
    laid = [jnp.concatenate([p[r : r + base] for r in range(0, p.shape[0], base)], axis=1) for p in parts]
    pair = split(by_owner(jnp.concatenate(laid, axis=1), "rows"), "rows", 1)
    return pair if token is None else (*pair, token)


def next_step(got, kept, step, axis="rows", token=None):
    send, keep, *token = step_split(got, kept, axis, step, token)
    return (swap_with(send, axis, step), keep, *token)


def last_steps(got, kept, step, axis):
    while step < lax.axis_size(axis):
        got, kept = next_step(got, kept, step, axis)
        step *= 2
    return step_sum(got, kept)[0]


class Ladder:
    def __init__(self, got, kept, step=2):
        self.got, self.kept, self.step, self.up = got, kept, step, True

    def advance(self, token=None):
        if self.ready():
            return (token,)
        last = lax.axis_size("rows") // 2
        if self.up and self.step <= last:
            self.got, self.kept, *token = next_step(self.got, self.kept, self.step, "rows", token)
            self.step *= 2
            return token
        if self.up:
            self.kept, *token = step_sum(self.got, self.kept, token)
            self.up, self.step = False, last
        else:
            self.kept, *token = join_step(self.got, self.kept, self.step, token)
            self.step //= 2
        self.got = swap_with(self.kept, "rows", self.step)
        return token

    def ready(self):
        return not self.up and self.step == 1

    def finish(self, cuts, token):
        while not self.ready():
            (token,) = self.advance(token)
        return final_join(self.got, self.kept, cuts, token)


def deep_rows(tile):
    odd = lax.axis_index("rows") % 2 == 1
    far_up = from_behind(tile, "rows", 2)
    far_down = from_behind(tile, "rows", -2)
    near = swap_with(tile, "rows", 1)
    other = swap_with(jnp.where(odd, far_up, far_down), "rows", 1)
    return far_up, jnp.where(odd, near, other), tile, jnp.where(odd, other, near), far_down


def near_rows(tile, width):
    size = 2 * width
    above = from_behind(tile[:, -size:], "rows", 1)
    below = from_behind(tile[:, :size], "rows", -1)
    return above, tile, below


def per_device(
    inputs,
    heights,
    displacements,
    reduce_one,
    reduce_gain_one,
    reduce_bias_one,
    offset_weight,
    deform_weight,
    deform_gain,
    deform_bias,
    expand_one,
    expand_gain_one,
    expand_bias_one,
    reduce_two,
    reduce_gain_two,
    reduce_bias_two,
    conv_weight,
    conv_gain,
    conv_bias,
    expand_two,
    expand_gain_two,
    expand_bias_two,
    cotangent,
):
    batch, rows, width, channels = inputs.shape
    pixels = rows * width
    n = batch * pixels
    own_heights = lax.dynamic_slice_in_dim(heights, lax.axis_index("ch") * batch, batch)
    rows_here = lax.axis_index("rows") * rows + jnp.arange(rows, dtype=jnp.int32)
    mask = (rows_here[None, :] < own_heights[:, None]).astype(f32)
    mask = jnp.broadcast_to(mask[:, :, None], (batch, rows, width)).reshape(n, 1)
    mask_wide = jnp.broadcast_to(mask, (n, 128))
    count = jnp.sum(heights).astype(f32) * width

    offset_rows = offset_weight.astype(bf16).reshape(3, 6, 3, 3, MID).transpose(2, 3, 0, 1, 4)
    offset_rows = jnp.pad(offset_rows, ((0, 0), (0, 0), (0, 1), (0, 2), (0, 0))).reshape(3, 96, MID)
    disp = jnp.pad(displacements.reshape(3, 6, batch, pixels), ((0, 0), (0, 2), (0, 0), (0, 0)))
    disp = disp.transpose(2, 0, 1, 3)

    reduce_full, came = gather_by_swaps(reduce_one)
    deform_full = gather_weight_after(deform_weight, came)
    expand_full, reduce_full_two, conv_full, expand_full_two = [
        gather_weight(w) for w in (expand_one, reduce_two, conv_weight, expand_two)
    ]

    devices = lax.axis_size("rows") * lax.axis_size("ch")
    acts = inputs.reshape(n, channels)
    acts_low, y_a, spread = product_forward(acts, mask_wide, reduce_full, devices)
    par_a = forward_rows(small_total(spread), reduce_gain_one, reduce_bias_one, count)
    hidden = (gelu(y_a * par_a[0] + par_a[1]) * mask).astype(bf16)
    near_tiles = deep_rows(hidden.reshape(batch, pixels, MID))
    columns, y_b, fraction, spread = deform_forward(
        near_tiles, offset_rows, disp, deform_full, mask_wide, rows, width, devices
    )
    par_b = forward_rows(small_total(spread), deform_gain, deform_bias, count)
    middle, y_c, block = expand_forward([y_b], par_b, mask_wide, expand_full)
    par_c = forward_rows(wide_total(block), expand_gain_one, expand_bias_one, count)

    first_low, y_d, spread = first_forward(y_c, par_c, acts, mask_wide, reduce_full_two, devices)
    par_d = forward_rows(small_total(spread), reduce_gain_two, reduce_bias_two, count)
    hidden_two = (gelu(y_d * par_d[0] + par_d[1]) * mask).astype(bf16)
    rimmed = near_rows(hidden_two.reshape(batch, pixels, MID), width)
    y_e, spread = conv_forward(rimmed, conv_full, mask_wide, rows, width, devices)
    par_e = forward_rows(small_total(spread), conv_gain, conv_bias, count)
    middle_two, y_f, block = expand_forward([y_e], par_e, mask_wide, expand_full_two)
    par_f = forward_rows(wide_total(block), expand_gain_two, expand_bias_two, count)

    output, dt_f, block = output_stage(y_f, par_f, first_low, cotangent.reshape(n, channels), mask_wide)
    back_f, sums_f = backward_rows(wide_total(block), par_f, count)
    dy_f, dt_e, spread = expand_backward(
        dt_f, y_f, par_f, back_f, mask_wide, expand_full_two, y_e, par_e, devices
    )
    expand_two_local = dot(dy_f, middle_two, TN).astype(bf16)
    expand_two_part = scatter_ch(expand_two_local)
    back_e, sums_e = backward_rows(small_total(spread), par_e, count)
    dy_e = norm_gradient(dt_e, y_e, par_e, back_e, mask).astype(bf16)
    dy_e_rim = near_rows(dy_e.reshape(batch, pixels, MID), width)
    conv_local = conv_weight_gradient(dy_e, rimmed, rows, width, (expand_two_local,))
    conv_part = scatter_ch(conv_local)
    dt_d, spread = conv_backward(
        dy_e_rim, conv_full, y_d, par_d, mask_wide, rows, width, devices, (conv_local,)
    )
    base = conv_part.shape[0]
    back_d, sums_d = backward_rows(small_total(spread), par_d, count)
    dy_d, dt_c, block = residual_backward(
        dt_d, y_d, par_d, back_d, mask_wide, reduce_full_two, dt_f, y_c, par_c, acts_low
    )
    reduce_two_local = dot(dy_d, first_low, TN).astype(bf16)

    back_c, sums_c = backward_rows(wide_total(block), par_c, count)
    red_two = split(by_owner(reduce_two_local), "ch", 1)
    dy_c, dt_b, spread, kept = expand_backward(
        dt_c, y_c, par_c, back_c, mask_wide, expand_full, y_b, par_b, devices, (red_two[1],)
    )
    red_two = next_step(red_two[0], kept, 2, "ch")
    expand_one_local = dot(dy_c, middle, TN).astype(bf16)
    exp_one = split(by_owner(expand_one_local), "ch", 1)
    back_b, sums_b = backward_rows(small_total(spread), par_b, count)
    dy_b = norm_gradient(dt_b, y_b, par_b, back_b, mask).astype(bf16)
    sum_p = Ladder(*first_step([conv_part, expand_two_part], base))
    deform_local, reduce_two_kept, expand_one_kept = columns_weight_gradient(
        dy_b, columns, (red_two[1], exp_one[1])
    )
    deform_part = scatter_ch(deform_local)
    exp_one = next_step(exp_one[0], expand_one_kept, 2, "ch")
    far_up, up, own, down, far_down, offset_local, reduce_two_kept, expand_one_kept, sum_p.kept = deform_backward(
        near_tiles, offset_rows, disp, fraction, deform_full, dy_b, rows, width,
        (), (reduce_two_kept, exp_one[1], sum_p.kept),
    )
    odd = lax.axis_index("rows") % 2 == 1
    passed = swap_with(jnp.where(odd, down, up), "rows", 1)
    sum_p.advance()
    below, above, partner, sum_p.kept = return_step(far_up, up, down, far_down, passed, (sum_p.kept,))
    below, above = from_behind(below, "rows", -2), from_behind(above, "rows", 2)
    partner = swap_with(partner, "rows", 1)
    dt_a, spread, sum_p.kept, reduce_two_kept, expand_one_kept = hidden_backward(
        (own, partner, below, above), y_a, par_a, mask_wide, devices,
        (sum_p.kept, reduce_two_kept, expand_one_kept),
    )
    sum_p.advance()
    reduce_two_part = last_steps(red_two[0], reduce_two_kept, 4, "ch")[0]
    expand_one_part = last_steps(exp_one[0], expand_one_kept, 4, "ch")[0]
    got_q, kept_q = first_step([reduce_two_part, expand_one_part], base)
    back_a, sums_a = backward_rows(small_total(spread), par_a, count)
    dy_a, send_s, kept_s, sum_p.kept, kept_q, deform_part, offset_local = last_gradient(
        dt_a, y_a, par_a, back_a, mask_wide, acts_low, lax.axis_size("ch"),
        (sum_p.kept, kept_q, deform_part, offset_local),
    )
    got_s = swap_with(send_s, "ch", 1)
    got_r, kept_r, token = first_step([deform_part], base, jnp.zeros((8, 128), f32))
    sum_q, sum_r = Ladder(got_q, kept_q), Ladder(got_r, kept_r)
    step = 2
    while step < lax.axis_size("ch"):
        got_s, kept_s, token = next_step(got_s, kept_s, step, "ch", token)
        step *= 2
    for ladder in (sum_p, sum_q):
        (token,) = ladder.advance(token)
    input_grad, token = input_backward(dy_a, reduce_full, dt_c, token)
    (token,) = sum_q.advance(token)
    offset_local = offset_local.reshape(3, 3, 4, 8, MID)[:, :, :3, :6]
    offset_local = offset_local.transpose(2, 3, 0, 1, 4).reshape(-1, MID)
    offset_part = ladder_sum(offset_local, "ch").astype(bf16)
    offset_part = jnp.pad(offset_part, ((0, -offset_part.shape[0] % base), (0, 0)))
    reduce_one_part = step_sum(got_s, kept_s)[0][0]
    got_s, kept_s, token = first_step([reduce_one_part, offset_part], base, token)
    sum_s = Ladder(got_s, kept_s)
    for ladder in (sum_p, sum_r, sum_q, sum_s, sum_p, sum_r, sum_q, sum_s, sum_r, sum_s, sum_q, sum_r, sum_s):
        (token,) = ladder.advance(token)
    (conv_weight_grad, expand_two_grad), token = sum_p.finish(((1, 9 * MID), (channels // MID, MID)), token)
    for ladder in (sum_r, sum_s):
        (token,) = ladder.advance(token)
    (reduce_two_grad, expand_one_grad), token = sum_q.finish(((1, channels), (channels // MID, MID)), token)
    (token,) = sum_s.advance(token)
    (deform_weight_grad,), token = sum_r.finish(((1, 9 * MID),), token)
    (reduce_one_grad, offset_grad), token = sum_s.finish(
        ((1, channels), (offset_part.shape[0] // base, MID)), token
    )
    ends = owned((sums_a, sums_b, sums_c, sums_d, sums_e, sums_f), lax.axis_size("ch"))
    offset_weight_grad = offset_grad[:162].reshape(18, 9 * MID)
    reduce_gain_one_grad, reduce_bias_one_grad, deform_gain_grad, deform_bias_grad = ends[:4]
    expand_gain_one_grad, expand_bias_one_grad, reduce_gain_two_grad, reduce_bias_two_grad = ends[4:8]
    conv_gain_grad, conv_bias_grad, expand_gain_two_grad, expand_bias_two_grad = ends[8:]
    return (
        output.reshape(inputs.shape),
        input_grad.reshape(inputs.shape),
        reduce_one_grad,
        reduce_gain_one_grad,
        reduce_bias_one_grad,
        offset_weight_grad,
        deform_weight_grad,
        deform_gain_grad,
        deform_bias_grad,
        expand_one_grad,
        expand_gain_one_grad,
        expand_bias_one_grad,
        reduce_two_grad,
        reduce_gain_two_grad,
        reduce_bias_two_grad,
        conv_weight_grad,
        conv_gain_grad,
        conv_bias_grad,
        expand_two_grad,
        expand_gain_two_grad,
        expand_bias_two_grad,
    )


def solution(mesh):
    tiles = P("ch", "rows", None, None)
    owned = P("ch", None)
    block = (owned, P(), P())
    placed = (tiles, P(), P(None, "ch", "rows", None)) + block + (P(),) + 2 * block + 3 * block + (tiles,)
    grads = (owned, P("ch"), P("ch"))
    return jax.shard_map(
        per_device,
        mesh=mesh,
        in_specs=placed,
        out_specs=(tiles, tiles) + grads + (P(),) + 2 * grads + 3 * grads,
        check_vma=False,
    )
```
